32 devices in a mesh: dp: 16 (over z, y, x), mp: 2 (over core).
Axes of the slice: x: 2, y: 2, z: 4, core: 2. Of those that a mesh axis runs over, the one named last changes fastest.
Arguments:
- features: bfloat16 [12288, 768], P('dp'), may hold values from -6 to 6
- lap_vectors: bfloat16 [12288, 16], P('dp'), may hold values from -5 to 5
- node_counts: int32 [96], P('dp'), may hold values from 2 to 51, as said below
- edge_counts: int32 [96], P('dp'), may hold values from 1 to 77, as said below
- endpoints: int32 [12288, 2], P('dp'), may hold values from 0 to 50, as said below
- w_ident: bfloat16 [32, 768], replicated, may hold values from -1 to 1
- type_table: bfloat16 [2, 768], replicated, may hold values from -3 to 3
- gain_one: bfloat16 [768], replicated, may hold values from 0.5 to 1.5
- shift_one: bfloat16 [768], replicated, may hold values from -2 to 2
- w_query: bfloat16 [768, 768], P(None, 'mp'), may hold values from -0.21875 to 0.21875
- w_key: bfloat16 [768, 768], P(None, 'mp'), may hold values from -0.21875 to 0.21875
- w_value: bfloat16 [768, 768], P(None, 'mp'), may hold values from -0.21875 to 0.21875
- bias_query: bfloat16 [768], P('mp'), may hold values from -3 to 3
- bias_value: bfloat16 [768], P('mp'), may hold values from -3 to 3
- w_out: bfloat16 [768, 768], P('mp'), may hold values from -0.875 to 0.875
- bias_out: bfloat16 [768], replicated, may hold values from -2 to 2
- gain_two: bfloat16 [768], replicated, may hold values from 0.5 to 1.5
- shift_two: bfloat16 [768], replicated, may hold values from -2 to 2
- w_up: bfloat16 [768, 768], P(None, 'mp'), may hold values from -0.21875 to 0.21875
- bias_up: bfloat16 [768], P('mp'), may hold values from -3 to 3
- w_down: bfloat16 [768, 768], P('mp'), may hold values from -0.21875 to 0.21875
- bias_down: bfloat16 [768], replicated, may hold values from -2 to 2
- cotangent: bfloat16 [12288, 768], P('dp'), may hold values from -6 to 6
Outputs:
- result: bfloat16 [12288, 768], P(('dp', 'mp'))
- grad_features: float32 [12288, 768], P(('dp', 'mp'))
- grad_w_ident: float32 [32, 768], replicated
- grad_type_table: float32 [2, 768], replicated
- grad_gain_one: float32 [768], replicated
- grad_shift_one: float32 [768], replicated
- grad_w_query: float32 [768, 768], P(None, 'mp')
- grad_w_key: float32 [768, 768], P(None, 'mp')
- grad_w_value: float32 [768, 768], P(None, 'mp')
- grad_bias_query: float32 [768], P('mp')
- grad_bias_value: float32 [768], P('mp')
- grad_w_out: float32 [768, 768], P('mp')
- grad_bias_out: float32 [768], replicated
- grad_gain_two: float32 [768], replicated
- grad_shift_two: float32 [768], replicated
- grad_w_up: float32 [768, 768], P(None, 'mp')
- grad_bias_up: float32 [768], P('mp')
- grad_w_down: float32 [768, 768], P('mp')
- grad_bias_down: float32 [768], replicated
The draws below stay inside these ranges and needn't reach their ends.
Inputs may be any that keep to these rules, and one draw needn't show every extreme that they name: `node_counts`: some molecule has exactly 51 nodes and some has 2. edge_counts >= node_counts - 1 and node_counts + edge_counts <= 128 for every molecule; some molecule fills all 128 token slots. `endpoints`: in a molecule with n nodes and e edges, slot p < n holds (p, p), slots n to n + e - 1 hold two node indices below n, later slots hold (0, 0).
All inputs are finite; a program needn't handle non-finite values.
Results may differ from the reference program's by a relative error of at most 0.015.
Values may be sent and summed in bfloat16 or wider, within the bound.
No kernel may reach another device: no remote copies, remote signals or barrier semaphores. Data moves between devices by JAX's collectives and lax.ppermute only.
A program may use at most 128 MiB of HBM per device.

```python
import math
import jax
import jax.numpy as jnp
from jax import lax

D = 768
HEADS = 32
HDIM = 24
FF = 768
LAPK = 16
SEQ = 128
NMAX = 51
HH = 768
IDW = 32
MOLS = 96
TOKENS = 12288


def molecule_shapes(key):
    nodes_key, edges_key, pick_key = jax.random.split(key, 3)
    node_total = jax.random.randint(nodes_key, (MOLS,), 2, NMAX + 1)
    edge_total = jax.random.randint(edges_key, (MOLS,), node_total - 1, SEQ - NMAX + 1)
    full_pick = jax.random.randint(pick_key, (), 0, MOLS)
    small_pick = (full_pick + 1 + jax.random.randint(jax.random.fold_in(pick_key, 1), (), 0, MOLS - 1)) % MOLS
    molecule_ids = jnp.arange(MOLS)
    node_total = jnp.where(molecule_ids == full_pick, NMAX, jnp.where(molecule_ids == small_pick, 2, node_total))
    edge_total = jnp.where(molecule_ids == full_pick, SEQ - NMAX, jnp.where(molecule_ids == small_pick, 1, edge_total))
    return (node_total.astype(jnp.int32), edge_total.astype(jnp.int32))


def draw_node_counts(key, part):
    node_total, edge_total = molecule_shapes(key)
    return node_total


def draw_edge_counts(key, part):
    node_total, edge_total = molecule_shapes(key)
    return edge_total


def draw_endpoints(key, part):
    node_total, edge_total = molecule_shapes(key)
    key = jax.random.fold_in(key, 7)
    tree_key, first_key, second_key = jax.random.split(key, 3)
    position = jnp.arange(SEQ, dtype=jnp.int32)[None, :]
    node_col = node_total[:, None]
    edge_pos = position - node_col
    parent = jax.random.randint(tree_key, (MOLS, SEQ), 0, jnp.maximum(edge_pos + 1, 1))
    first_any = jax.random.randint(first_key, (MOLS, SEQ), 0, node_col)
    second_any = jax.random.randint(second_key, (MOLS, SEQ), 0, node_col)
    in_tree = (edge_pos >= 0) & (edge_pos < node_col - 1)
    in_rest = (edge_pos >= node_col - 1) & (edge_pos < edge_total[:, None])
    is_node = position < node_col
    first_end = jnp.where(is_node, position, jnp.where(in_tree, parent, jnp.where(in_rest, first_any, 0)))
    second_end = jnp.where(is_node, position, jnp.where(in_tree, edge_pos + 1, jnp.where(in_rest, second_any, 0)))
    return jnp.stack([first_end, second_end], axis=-1).reshape(MOLS * SEQ, 2).astype(jnp.int32)


def levels(rng, extent, shards, low, top_value):
    def one(dim, shards_of):
        steps = jax.random.uniform(jax.random.fold_in(jax.random.fold_in(rng, 6), dim), (shards_of,), jnp.float32, low / len(shards), top_value / len(shards))
        return jnp.repeat(jnp.exp(steps), extent[dim] // shards_of).reshape((-1,) + (1,) * (len(extent) - dim - 1))

    loudness = one(*shards[0])
    for cut in shards[1:]:
        loudness = loudness * one(*cut)
    return loudness


def bell_draw(rng, shape, deviation, reach, pieces=(), kind=jnp.bfloat16):
    drawn = jax.random.normal(rng, shape, jnp.float32) * deviation
    if len(pieces) > 0:
        drawn = levels(rng, shape, pieces, -0.22, 0.18) * drawn
    return jnp.clip(drawn, min=-reach, max=reach).astype(kind)


def setup_inputs(seed: int = 0) -> dict:
    streams_of = jax.random.split(jax.random.key(seed), 24)
    features = bell_draw(streams_of[0], (TOKENS, D), 1.0, 6.0, ((0, 16),))
    lap_vectors = bell_draw(streams_of[1], (TOKENS, LAPK), 1.0, 5.0, ((0, 16),))
    node_counts = draw_node_counts(jax.random.fold_in(streams_of[23], 71), 0)
    edge_counts = draw_edge_counts(jax.random.fold_in(streams_of[23], 71), 0)
    endpoints = draw_endpoints(jax.random.fold_in(streams_of[23], 71), 0)
    w_ident = bell_draw(streams_of[5], (IDW, D), IDW ** -0.5, 1.0)
    type_table = bell_draw(streams_of[6], (2, D), 0.5, 3.0)
    gain_one = jnp.clip(1.0 + 0.1 * jax.random.normal(streams_of[7], (D,), jnp.float32), 0.5, 1.5).astype(jnp.bfloat16)
    shift_one = bell_draw(streams_of[8], (D,), 0.3, 2.0)
    w_query = bell_draw(streams_of[9], (D, HH), D ** -0.5, 0.21875, ((1, 2),))
    w_key = bell_draw(streams_of[10], (D, HH), D ** -0.5, 0.21875, ((1, 2),))
    w_value = bell_draw(streams_of[11], (D, HH), D ** -0.5, 0.21875, ((1, 2),))
    bias_query = bell_draw(streams_of[12], (HH,), 0.5, 3.0, ((0, 2),))
    bias_value = bell_draw(streams_of[13], (HH,), 0.5, 3.0, ((0, 2),))
    w_out = bell_draw(streams_of[14], (HH, D), (HH // 16) ** -0.5, 0.875, ((0, 2),))
    bias_out = bell_draw(streams_of[15], (D,), 0.3, 2.0)
    gain_two = jnp.clip(1.0 + 0.1 * jax.random.normal(streams_of[16], (D,), jnp.float32), 0.5, 1.5).astype(jnp.bfloat16)
    shift_two = bell_draw(streams_of[17], (D,), 0.3, 2.0)
    w_up = bell_draw(streams_of[18], (D, FF), D ** -0.5, 0.21875, ((1, 2),))
    bias_up = bell_draw(streams_of[19], (FF,), 0.5, 3.0, ((0, 2),))
    w_down = bell_draw(streams_of[20], (FF, D), FF ** -0.5, 0.21875, ((0, 2),))
    bias_down = bell_draw(streams_of[21], (D,), 0.3, 2.0)
    cotangent = bell_draw(streams_of[22], (TOKENS, D), 1.0, 6.0, ((0, 16),))
    return dict(features=features, lap_vectors=lap_vectors, node_counts=node_counts, edge_counts=edge_counts, endpoints=endpoints, w_ident=w_ident, type_table=type_table, gain_one=gain_one, shift_one=shift_one, w_query=w_query, w_key=w_key, w_value=w_value, bias_query=bias_query, bias_value=bias_value, w_out=w_out, bias_out=bias_out, gain_two=gain_two, shift_two=shift_two, w_up=w_up, bias_up=bias_up, w_down=w_down, bias_down=bias_down, cotangent=cotangent)


@jax.custom_vjp
def low(v):
    return lax.optimization_barrier(v.astype(jnp.bfloat16)).astype(jnp.float32)

@jax.custom_vjp
def low_back(v):
    return v

def low_keep(v):
    return (low(v), None)

def low_pass(kept, grad):
    return (grad,)

def back_keep(v):
    return (v, None)

def back_low(kept, grad):
    return (low(grad),)
low.defvjp(low_keep, low_pass)
low_back.defvjp(back_keep, back_low)

def exact_dot(left_side, right_side):
    return jnp.dot(left_side, right_side, precision=lax.Precision.HIGHEST, preferred_element_type=jnp.float32)

def layer_norm(hidden, gain, shift):
    average = lax.optimization_barrier(jnp.mean(hidden, axis=-1, keepdims=True))
    centred = hidden - average
    variance = lax.optimization_barrier(jnp.mean(centred * centred, axis=-1, keepdims=True))
    return centred * lax.rsqrt(variance + 1e-05) * gain + shift

def forward_block(params, features, ident_rows, is_edge, keep_rows):
    w_ident, type_table, gain_one, shift_one, w_query, w_key, w_value, bias_query, bias_value, w_out, bias_out, gain_two, shift_two, w_up, bias_up, w_down, bias_down = params
    row_count = features.shape[0]
    molecules = row_count // SEQ
    score_scale = 1.0 / math.sqrt(HDIM)
    hidden = features + exact_dot(ident_rows, w_ident) + type_table[0] * (1.0 - is_edge)[:, None] + type_table[1] * is_edge[:, None]
    normed = low(layer_norm(hidden, gain_one, shift_one))
    queries = low_back(low(exact_dot(normed, w_query) + bias_query))
    key_rows = low_back(low(exact_dot(normed, w_key)))
    values = low_back(low(exact_dot(normed, w_value) + bias_value))
    head_shape = (molecules, SEQ, HEADS, HDIM)
    scores = jnp.einsum('mqhd,mkhd->mhqk', queries.reshape(head_shape), key_rows.reshape(head_shape), precision=lax.Precision.HIGHEST) * score_scale
    scores = low_back(scores)
    keep_grid = keep_rows.reshape(molecules, 1, 1, SEQ)
    masked = jnp.where(keep_grid > 0.5, scores, -1e+30)
    prob_low = low(jax.nn.softmax(masked, axis=-1))
    mixed_out = jnp.einsum('mhqk,mkhd->mqhd', prob_low, values.reshape(head_shape), precision=lax.Precision.HIGHEST).reshape(row_count, HEADS * HDIM)
    attended = low_back(low(mixed_out * keep_rows[:, None]))
    middle = hidden + low_back(exact_dot(attended, w_out)) + bias_out
    normed_two = low(layer_norm(middle, gain_two, shift_two))
    before = low_back(exact_dot(normed_two, w_up) + bias_up)
    active = low(jax.nn.gelu(before, approximate=False))
    return middle + low_back(exact_dot(active, w_down)) + bias_down

def take_rows(table_rows, indices):
    return table_rows[indices]

def to_float(weight):
    return weight.astype(jnp.float32)

def reference(features, lap_vectors, node_counts, edge_counts, endpoints, w_ident, type_table, gain_one, shift_one, w_query, w_key, w_value, bias_query, bias_value, w_out, bias_out, gain_two, shift_two, w_up, bias_up, w_down, bias_down, cotangent):
    params = jax.tree.map(to_float, (w_ident, type_table, gain_one, shift_one, w_query, w_key, w_value, bias_query, bias_value, w_out, bias_out, gain_two, shift_two, w_up, bias_up, w_down, bias_down))
    position = jnp.arange(SEQ, dtype=jnp.int32)[None, :]
    keep_rows = (position < (node_counts + edge_counts)[:, None]).astype(jnp.float32)
    is_edge = (position >= node_counts[:, None]).astype(jnp.float32)
    lap_table = lap_vectors.astype(jnp.float32).reshape(MOLS, SEQ, LAPK)
    end_pairs = endpoints.reshape(MOLS, SEQ, 2)
    first_rows = jax.vmap(take_rows)(lap_table, end_pairs[:, :, 0])
    second_rows = jax.vmap(take_rows)(lap_table, end_pairs[:, :, 1])
    ident_rows = jnp.concatenate([first_rows, second_rows], axis=-1)
    group_size = 32
    blocks = MOLS // group_size
    block_rows = group_size * SEQ
    stacked = (features.astype(jnp.float32).reshape(blocks, block_rows, D), ident_rows.reshape(blocks, block_rows, IDW), is_edge.reshape(blocks, block_rows), keep_rows.reshape(blocks, block_rows), cotangent.astype(jnp.float32).reshape(blocks, block_rows, D))

    def one_block(totals, block_data):
        feat_blk, ident_blk, edge_blk, keep_blk, cot_blk = block_data

        def run_layer(weights, feat_in):
            return forward_block(weights, feat_in, ident_blk, edge_blk, keep_blk)
        layer_out, pullback = jax.vjp(run_layer, params, feat_blk)
        grad_params, grad_feat = pullback(cot_blk * keep_blk[:, None])
        totals = jax.tree.map(jnp.add, totals, grad_params)
        return (totals, (layer_out.astype(jnp.bfloat16), grad_feat))
    zero_grads = jax.tree.map(jnp.zeros_like, params)
    totals, outputs = lax.scan(one_block, zero_grads, stacked)
    result = outputs[0].reshape(TOKENS, D)
    grad_features = outputs[1].reshape(TOKENS, D)
    return (result, grad_features, totals[0], totals[1], totals[2], totals[3], totals[4], totals[5], totals[6], totals[7], totals[8], totals[9], totals[10], totals[11], totals[12], totals[13], totals[14], totals[15], totals[16])
```

```python
from functools import partial
import math

import jax
import jax.numpy as jnp
from jax import lax
from jax.sharding import PartitionSpec as P

HDIM = 24
SEQ = 128


EPSILON = 1e-05


def norm_parts(hidden):
    average = jnp.mean(hidden, axis=-1, keepdims=True)
    centred = hidden - average
    inverse = lax.rsqrt(jnp.mean(centred * centred, axis=-1, keepdims=True) + EPSILON)
    return (centred * inverse, inverse)


def norm_back(unit_rows, inverse, grad_normed, gain):
    grad_hat = grad_normed * gain
    return inverse * (
        grad_hat
        - jnp.mean(grad_hat, axis=-1, keepdims=True)
        - unit_rows * jnp.mean(grad_hat * unit_rows, axis=-1, keepdims=True)
    )


def row_tables(node_counts, edge_counts, seq_len):
    position = lax.broadcasted_iota(jnp.int32, (node_counts.shape[0], seq_len), 1)
    keep_rows = (position < (node_counts + edge_counts)[:, None]).astype(jnp.float32).reshape(-1)
    is_edge = (position >= node_counts[:, None]).astype(jnp.float32).reshape(-1)
    return (keep_rows, is_edge)


def identifiers(lap_vectors, endpoints, seq_len):
    molecules = lap_vectors.shape[0] // seq_len
    lap_table = lap_vectors.reshape(molecules, seq_len, lap_vectors.shape[1])
    slot_ids = lax.broadcasted_iota(jnp.int32, (1, 1, seq_len), 2)
    end_pairs = endpoints.reshape(molecules, seq_len, 2)
    pick_first = (end_pairs[:, :, 0:1] == slot_ids).astype(jnp.bfloat16)
    pick_second = (end_pairs[:, :, 1:2] == slot_ids).astype(jnp.bfloat16)
    first_rows = jnp.einsum(
        "mts,msk->mtk", pick_first, lap_table, preferred_element_type=jnp.float32
    )
    second_rows = jnp.einsum(
        "mts,msk->mtk", pick_second, lap_table, preferred_element_type=jnp.float32
    )
    joined = jnp.concatenate([first_rows, second_rows], axis=-1)
    return joined.reshape(molecules * seq_len, joined.shape[-1])


def group_count(molecules, seq_len):
    group_size = max(1, min(molecules, 2048 // seq_len))
    return group_size


def attend(queries, key_rows, values, keep_rows, head_count, seq_len):
    row_count = queries.shape[0]
    molecules = row_count // seq_len
    group_size = group_count(molecules, seq_len)
    grid_shape = (molecules // group_size, group_size, seq_len, head_count, HDIM)
    score_scale = 1.0 / math.sqrt(HDIM)

    def one_group(group_block):
        query_blk, key_blk, value_blk, keep_blk = group_block
        scores = (
            jnp.einsum("mqhd,mkhd->mhqk", query_blk, key_blk, preferred_element_type=jnp.float32)
            * score_scale
        )
        masked = jnp.where(keep_blk[:, None, None, :] > 0.5, scores, -1e30)
        row_max = jnp.max(masked, axis=-1, keepdims=True)
        raised = jnp.exp(masked - row_max)
        row_sum = jnp.sum(raised, axis=-1, keepdims=True)
        prob_low = (raised / row_sum).astype(jnp.bfloat16)
        mixed_out = jnp.einsum(
            "mhqk,mkhd->mqhd", prob_low, value_blk, preferred_element_type=jnp.float32
        )
        return (mixed_out, row_max + jnp.log(row_sum))

    mixed_out, log_total = lax.map(
        one_group,
        (
            queries.reshape(grid_shape),
            key_rows.reshape(grid_shape),
            values.reshape(grid_shape),
            keep_rows.reshape(grid_shape[:3]),
        ),
    )
    return (mixed_out.reshape(row_count, head_count * HDIM), log_total)


def attend_back(
    queries, key_rows, values, log_total, grad_attended, keep_rows, head_count, seq_len
):
    row_count = queries.shape[0]
    molecules = row_count // seq_len
    group_size = group_count(molecules, seq_len)
    grid_shape = (molecules // group_size, group_size, seq_len, head_count, HDIM)
    score_scale = 1.0 / math.sqrt(HDIM)

    def one_group(group_block):
        query_blk, key_blk, value_blk, keep_blk, total_blk, grad_blk = group_block
        scores = (
            jnp.einsum("mqhd,mkhd->mhqk", query_blk, key_blk, preferred_element_type=jnp.float32)
            * score_scale
        )
        masked = jnp.where(keep_blk[:, None, None, :] > 0.5, scores, -1e30)
        weights = jnp.exp(masked - total_blk)
        prob_low = weights.astype(jnp.bfloat16)
        grad_probs = jnp.einsum(
            "mqhd,mkhd->mhqk", grad_blk, value_blk, preferred_element_type=jnp.float32
        )
        grad_values = jnp.einsum(
            "mhqk,mqhd->mkhd", prob_low, grad_blk, preferred_element_type=jnp.float32
        )
        inner_sum = jnp.sum(weights * grad_probs, axis=-1, keepdims=True)
        grad_scores = (weights * (grad_probs - inner_sum)).astype(jnp.bfloat16)
        grad_queries = (
            jnp.einsum("mhqk,mkhd->mqhd", grad_scores, key_blk, preferred_element_type=jnp.float32)
            * score_scale
        )
        grad_keys = (
            jnp.einsum(
                "mhqk,mqhd->mkhd", grad_scores, query_blk, preferred_element_type=jnp.float32
            )
            * score_scale
        )
        return (
            grad_queries.astype(jnp.bfloat16),
            grad_keys.astype(jnp.bfloat16),
            grad_values.astype(jnp.bfloat16),
        )

    grad_parts = lax.map(
        one_group,
        (
            queries.reshape(grid_shape),
            key_rows.reshape(grid_shape),
            values.reshape(grid_shape),
            keep_rows.reshape(grid_shape[:3]),
            log_total,
            grad_attended.reshape(grid_shape),
        ),
    )
    flat_shape = (row_count, head_count * HDIM)
    return (
        grad_parts[0].reshape(flat_shape),
        grad_parts[1].reshape(flat_shape),
        grad_parts[2].reshape(flat_shape),
    )


def col_sum(matrix):
    return jnp.sum(matrix.astype(jnp.float32), axis=0)


def layer_core(
    features,
    ident_rows,
    is_edge,
    keep_rows,
    cotangent,
    weights,
    small,
    mix_attn,
    mix_ffn,
    back_ffn,
    back_attn,
    row_start,
    row_total,
    seq_len,
):
    w_query, w_key, w_value, bias_query, bias_value, w_out, w_up, bias_up, w_down = weights
    small_f = jax.tree.map(lambda weight: weight.astype(jnp.float32), small)
    w_ident, type_table, gain_one, shift_one, bias_out, gain_two, shift_two, bias_down = small_f
    head_count = w_query.shape[1] // HDIM
    hidden = (
        features.astype(jnp.float32)
        + jnp.dot(
            ident_rows, w_ident, precision=lax.Precision.HIGHEST, preferred_element_type=jnp.float32
        )
        + type_table[0] * (1.0 - is_edge)[:, None]
        + type_table[1] * is_edge[:, None]
    )
    unit_one, inverse_one = norm_parts(hidden)
    normed = (unit_one * gain_one + shift_one).astype(jnp.bfloat16)
    queries = (
        jnp.dot(normed, w_query, preferred_element_type=jnp.float32)
        + bias_query.astype(jnp.float32)
    ).astype(jnp.bfloat16)
    key_rows = jnp.dot(normed, w_key, preferred_element_type=jnp.float32).astype(jnp.bfloat16)
    values = (
        jnp.dot(normed, w_value, preferred_element_type=jnp.float32)
        + bias_value.astype(jnp.float32)
    ).astype(jnp.bfloat16)
    mixed_out, log_total = attend(queries, key_rows, values, keep_rows, head_count, seq_len)
    attended = (mixed_out * keep_rows[:, None]).astype(jnp.bfloat16)
    middle = (
        hidden + mix_attn(jnp.dot(attended, w_out, preferred_element_type=jnp.float32)) + bias_out
    )
    unit_two, inverse_two = norm_parts(middle)
    normed_two = (unit_two * gain_two + shift_two).astype(jnp.bfloat16)
    before = jnp.dot(normed_two, w_up, preferred_element_type=jnp.float32) + bias_up.astype(
        jnp.float32
    )
    gelu_out, gelu_pull = jax.vjp(partial(jax.nn.gelu, approximate=False), before)
    active = gelu_out.astype(jnp.bfloat16)
    result = (
        middle + mix_ffn(jnp.dot(active, w_down, preferred_element_type=jnp.float32)) + bias_down
    )
    grad_result = cotangent.astype(jnp.float32) * keep_rows[:, None]
    grad_ffn = grad_result.astype(jnp.bfloat16)
    grad_w_down = jnp.einsum("tf,td->fd", active, grad_ffn, preferred_element_type=jnp.float32)
    grad_active = jnp.einsum("td,fd->tf", grad_ffn, w_down, preferred_element_type=jnp.float32)
    grad_before = gelu_pull(grad_active)[0].astype(jnp.bfloat16)
    grad_w_up = jnp.einsum("td,tf->df", normed_two, grad_before, preferred_element_type=jnp.float32)
    grad_bias_up = col_sum(grad_before)
    grad_normed_two = back_ffn(
        jnp.einsum("tf,df->td", grad_before, w_up, preferred_element_type=jnp.float32)
    )
    grad_middle = grad_result + norm_back(unit_two, inverse_two, grad_normed_two, gain_two)
    grad_branch = grad_middle.astype(jnp.bfloat16)
    grad_w_out = jnp.einsum("th,td->hd", attended, grad_branch, preferred_element_type=jnp.float32)
    grad_attended = jnp.einsum(
        "td,hd->th", grad_branch, w_out, preferred_element_type=jnp.float32
    ).astype(jnp.bfloat16) * keep_rows[:, None].astype(jnp.bfloat16)
    grad_queries, grad_keys, grad_values = attend_back(
        queries, key_rows, values, log_total, grad_attended, keep_rows, head_count, seq_len
    )
    grad_w_query = jnp.einsum("td,th->dh", normed, grad_queries, preferred_element_type=jnp.float32)
    grad_w_key = jnp.einsum("td,th->dh", normed, grad_keys, preferred_element_type=jnp.float32)
    grad_w_value = jnp.einsum("td,th->dh", normed, grad_values, preferred_element_type=jnp.float32)
    grad_bias_query = col_sum(grad_queries)
    grad_bias_value = col_sum(grad_values)
    grad_normed = back_attn(
        jnp.einsum("th,dh->td", grad_queries, w_query, preferred_element_type=jnp.float32)
        + jnp.einsum("th,dh->td", grad_keys, w_key, preferred_element_type=jnp.float32)
        + jnp.einsum("th,dh->td", grad_values, w_value, preferred_element_type=jnp.float32)
    )
    grad_hidden = grad_middle + norm_back(unit_one, inverse_one, grad_normed, gain_one)

    def own_rows(matrix):
        return lax.dynamic_slice_in_dim(matrix, row_start, row_total, 0)

    own_grad_hidden = own_rows(grad_hidden)
    own_edge = own_rows(is_edge)
    own_normed = own_rows(grad_normed)
    own_normed_two = own_rows(grad_normed_two)
    small_grads = (
        jnp.dot(
            own_rows(ident_rows).T,
            own_grad_hidden,
            precision=lax.Precision.HIGHEST,
            preferred_element_type=jnp.float32,
        ),
        jnp.stack(
            [
                jnp.sum(own_grad_hidden * (1.0 - own_edge)[:, None], axis=0),
                jnp.sum(own_grad_hidden * own_edge[:, None], axis=0),
            ]
        ),
        jnp.sum(own_normed * own_rows(unit_one), axis=0),
        jnp.sum(own_normed, axis=0),
        jnp.sum(own_rows(grad_middle), axis=0),
        jnp.sum(own_normed_two * own_rows(unit_two), axis=0),
        jnp.sum(own_normed_two, axis=0),
        jnp.sum(own_rows(grad_result), axis=0),
    )
    weight_grads = (
        grad_w_query,
        grad_w_key,
        grad_w_value,
        grad_bias_query,
        grad_bias_value,
        grad_w_out,
        grad_w_up,
        grad_bias_up,
        grad_w_down,
    )
    return (result, grad_hidden, weight_grads, small_grads)


def per_device(
    features,
    lap_vectors,
    node_counts,
    edge_counts,
    endpoints,
    w_ident,
    type_table,
    gain_one,
    shift_one,
    w_query,
    w_key,
    w_value,
    bias_query,
    bias_value,
    w_out,
    bias_out,
    gain_two,
    shift_two,
    w_up,
    bias_up,
    w_down,
    bias_down,
    cotangent,
):
    seq_len = SEQ
    mp_count = lax.axis_size("mp")
    mp_index = lax.axis_index("mp")
    row_count = features.shape[0]
    half_rows = row_count // mp_count
    sharded = (w_query, w_key, w_value, bias_query, bias_value, w_out, w_up, bias_up, w_down)
    small = (w_ident, type_table, gain_one, shift_one, bias_out, gain_two, shift_two, bias_down)

    def mix_attn(partial_sum):
        return lax.psum(partial_sum.astype(jnp.bfloat16), "mp").astype(jnp.float32)

    def mix_ffn(partial_sum):
        return lax.psum(partial_sum.astype(jnp.bfloat16), "mp").astype(jnp.float32)

    def back_ffn(partial_sum):
        return lax.psum(partial_sum.astype(jnp.bfloat16), "mp").astype(jnp.float32)

    def back_attn(partial_sum):
        return lax.psum(partial_sum.astype(jnp.bfloat16), "mp").astype(jnp.float32)

    own_features, own_lap, own_ends, own_cot = (features, lap_vectors, endpoints, cotangent)
    own_nodes, own_edges = (node_counts, edge_counts)
    row_start = mp_index * half_rows
    keep_rows, is_edge = row_tables(own_nodes, own_edges, seq_len)
    ident_rows = identifiers(own_lap, own_ends, seq_len)
    result, grad_hidden, weight_grads, small_grads = layer_core(
        own_features,
        ident_rows,
        is_edge,
        keep_rows,
        own_cot,
        sharded,
        small,
        mix_attn,
        mix_ffn,
        back_ffn,
        back_attn,
        row_start,
        half_rows,
        seq_len,
    )
    result = lax.dynamic_slice_in_dim(result, row_start, half_rows, 0)
    grad_hidden = lax.dynamic_slice_in_dim(grad_hidden, row_start, half_rows, 0)
    flat = jnp.concatenate(
        [part.astype(jnp.bfloat16).reshape(-1) for part in weight_grads]
    ).reshape(-1, 128)
    flat = lax.psum(flat, "dp").reshape(-1)
    summed, start = [], 0
    for part in weight_grads:
        summed.append(flat[start : start + part.size].reshape(part.shape).astype(jnp.float32))
        start += part.size
    weight_grads = summed
    packed = jnp.concatenate([part.reshape(-1, part.shape[-1]) for part in small_grads])
    packed = lax.psum(packed, ("dp", "mp"))
    small_grads = (
        packed[:32], packed[32:34], packed[34], packed[35], packed[36], packed[37], packed[38], packed[39],
    )
    return (
        result.astype(jnp.bfloat16),
        grad_hidden,
        small_grads[0],
        small_grads[1],
        small_grads[2],
        small_grads[3],
        weight_grads[0],
        weight_grads[1],
        weight_grads[2],
        weight_grads[3],
        weight_grads[4],
        weight_grads[5],
        small_grads[4],
        small_grads[5],
        small_grads[6],
        weight_grads[6],
        weight_grads[7],
        weight_grads[8],
        small_grads[7],
    )


def solution(mesh):
    return jax.shard_map(
        per_device,
        mesh=mesh,
        in_specs=(
            P("dp", None),
            P("dp", None),
            P("dp"),
            P("dp"),
            P("dp", None),
            P(),
            P(),
            P(),
            P(),
            P(None, "mp"),
            P(None, "mp"),
            P(None, "mp"),
            P("mp"),
            P("mp"),
            P("mp", None),
            P(),
            P(),
            P(),
            P(None, "mp"),
            P("mp"),
            P("mp", None),
            P(),
            P("dp", None),
        ),
        out_specs=(
            P(("dp", "mp"), None),
            P(("dp", "mp"), None),
            P(),
            P(),
            P(),
            P(),
            P(None, "mp"),
            P(None, "mp"),
            P(None, "mp"),
            P("mp"),
            P("mp"),
            P("mp", None),
            P(),
            P(),
            P(),
            P(None, "mp"),
            P("mp"),
            P("mp", None),
            P(),
        ),
        check_vma=False,
    )
```

```python
from functools import partial
import math

import jax
import jax.numpy as jnp
from jax import lax
from jax.sharding import PartitionSpec as P

HDIM = 24
SEQ = 128
INNER = 4


EPSILON = 1e-05


def norm_parts(hidden):
    average = jnp.mean(hidden, axis=-1, keepdims=True)
    centred = hidden - average
    inverse = lax.rsqrt(jnp.mean(centred * centred, axis=-1, keepdims=True) + EPSILON)
    return (centred * inverse, inverse)


def norm_back(unit_rows, inverse, grad_normed, gain):
    grad_hat = grad_normed * gain
    return inverse * (
        grad_hat
        - jnp.mean(grad_hat, axis=-1, keepdims=True)
        - unit_rows * jnp.mean(grad_hat * unit_rows, axis=-1, keepdims=True)
    )


def row_tables(node_counts, edge_counts, seq_len):
    position = lax.broadcasted_iota(jnp.int32, (node_counts.shape[0], seq_len), 1)
    keep_rows = (position < (node_counts + edge_counts)[:, None]).astype(jnp.float32).reshape(-1)
    is_edge = (position >= node_counts[:, None]).astype(jnp.float32).reshape(-1)
    return (keep_rows, is_edge)


def identifiers(lap_vectors, endpoints, seq_len):
    molecules = lap_vectors.shape[0] // seq_len
    lap_table = lap_vectors.reshape(molecules, seq_len, lap_vectors.shape[1])
    slot_ids = lax.broadcasted_iota(jnp.int32, (1, 1, seq_len), 2)
    end_pairs = endpoints.reshape(molecules, seq_len, 2)
    pick_first = (end_pairs[:, :, 0:1] == slot_ids).astype(jnp.bfloat16)
    pick_second = (end_pairs[:, :, 1:2] == slot_ids).astype(jnp.bfloat16)
    first_rows = jnp.einsum(
        "mts,msk->mtk", pick_first, lap_table, preferred_element_type=jnp.float32
    )
    second_rows = jnp.einsum(
        "mts,msk->mtk", pick_second, lap_table, preferred_element_type=jnp.float32
    )
    joined = jnp.concatenate([first_rows, second_rows], axis=-1)
    return joined.reshape(molecules * seq_len, joined.shape[-1])


def group_count(molecules, seq_len):
    group_size = max(1, min(molecules, 2048 // seq_len))
    return group_size


def attend(queries, key_rows, values, keep_rows, head_count, seq_len):
    row_count = queries.shape[0]
    molecules = row_count // seq_len
    group_size = group_count(molecules, seq_len)
    grid_shape = (molecules // group_size, group_size, seq_len, head_count, HDIM)
    score_scale = 1.0 / math.sqrt(HDIM)

    def one_group(group_block):
        query_blk, key_blk, value_blk, keep_blk = group_block
        scores = (
            jnp.einsum("mqhd,mkhd->mhqk", query_blk, key_blk, preferred_element_type=jnp.float32)
            * score_scale
        )
        masked = jnp.where(keep_blk[:, None, None, :] > 0.5, scores, -1e30)
        row_max = jnp.max(masked, axis=-1, keepdims=True)
        raised = jnp.exp(masked - row_max)
        row_sum = jnp.sum(raised, axis=-1, keepdims=True)
        prob_low = (raised / row_sum).astype(jnp.bfloat16)
        mixed_out = jnp.einsum(
            "mhqk,mkhd->mqhd", prob_low, value_blk, preferred_element_type=jnp.float32
        )
        return (mixed_out, row_max + jnp.log(row_sum))

    mixed_out, log_total = lax.map(
        one_group,
        (
            queries.reshape(grid_shape),
            key_rows.reshape(grid_shape),
            values.reshape(grid_shape),
            keep_rows.reshape(grid_shape[:3]),
        ),
    )
    return (mixed_out.reshape(row_count, head_count * HDIM), log_total)


def attend_back(
    queries, key_rows, values, log_total, grad_attended, keep_rows, head_count, seq_len
):
    row_count = queries.shape[0]
    molecules = row_count // seq_len
    group_size = group_count(molecules, seq_len)
    grid_shape = (molecules // group_size, group_size, seq_len, head_count, HDIM)
    score_scale = 1.0 / math.sqrt(HDIM)

    def one_group(group_block):
        query_blk, key_blk, value_blk, keep_blk, total_blk, grad_blk = group_block
        scores = (
            jnp.einsum("mqhd,mkhd->mhqk", query_blk, key_blk, preferred_element_type=jnp.float32)
            * score_scale
        )
        masked = jnp.where(keep_blk[:, None, None, :] > 0.5, scores, -1e30)
        weights = jnp.exp(masked - total_blk)
        prob_low = weights.astype(jnp.bfloat16)
        grad_probs = jnp.einsum(
            "mqhd,mkhd->mhqk", grad_blk, value_blk, preferred_element_type=jnp.float32
        )
        grad_values = jnp.einsum(
            "mhqk,mqhd->mkhd", prob_low, grad_blk, preferred_element_type=jnp.float32
        )
        inner_sum = jnp.sum(weights * grad_probs, axis=-1, keepdims=True)
        grad_scores = (weights * (grad_probs - inner_sum)).astype(jnp.bfloat16)
        grad_queries = (
            jnp.einsum("mhqk,mkhd->mqhd", grad_scores, key_blk, preferred_element_type=jnp.float32)
            * score_scale
        )
        grad_keys = (
            jnp.einsum(
                "mhqk,mqhd->mkhd", grad_scores, query_blk, preferred_element_type=jnp.float32
            )
            * score_scale
        )
        return (
            grad_queries.astype(jnp.bfloat16),
            grad_keys.astype(jnp.bfloat16),
            grad_values.astype(jnp.bfloat16),
        )

    grad_parts = lax.map(
        one_group,
        (
            queries.reshape(grid_shape),
            key_rows.reshape(grid_shape),
            values.reshape(grid_shape),
            keep_rows.reshape(grid_shape[:3]),
            log_total,
            grad_attended.reshape(grid_shape),
        ),
    )
    flat_shape = (row_count, head_count * HDIM)
    return (
        grad_parts[0].reshape(flat_shape),
        grad_parts[1].reshape(flat_shape),
        grad_parts[2].reshape(flat_shape),
    )


def col_sum(matrix):
    return jnp.sum(matrix.astype(jnp.float32), axis=0)


def per_device(
    features, lap_vectors, node_counts, edge_counts, endpoints, w_ident, type_table,
    gain_one, shift_one, w_query, w_key, w_value, bias_query, bias_value, w_out, bias_out,
    gain_two, shift_two, w_up, bias_up, w_down, bias_down, cotangent,
):
    f32, bf16 = jnp.float32, jnp.bfloat16
    dp_count = lax.axis_size("dp")
    dp_index = lax.axis_index("dp")
    mp_index = lax.axis_index("mp")
    outer_count = dp_count // INNER
    inner_at, outer_at = dp_index % INNER, dp_index // INNER

    def swap(block):
        return lax.ppermute(block, "mp", [(0, 1), (1, 0)])

    def inner_move(block, step):
        pairs = [(s, s // INNER * INNER + (s % INNER ^ step)) for s in range(dp_count)]
        return lax.ppermute(block, "dp", pairs)

    def outer_move(block, step):
        pairs = [(s, (s // INNER ^ step) * INNER + s % INNER) for s in range(dp_count)]
        return lax.ppermute(block, "dp", pairs)

    def dot(left, right):
        return jnp.dot(left, right, preferred_element_type=f32)

    def dot_t(left, right):
        return lax.dot_general(left, right, (((0,), (0,)), ((), ())), preferred_element_type=f32)

    def dot_nt(left, right):
        return lax.dot_general(left, right, (((1,), (1,)), ((), ())), preferred_element_type=f32)

    rows_all = features.shape[0]
    rows = rows_all // 2
    mols = node_counts.shape[0] // 2
    own = lambda block, size: lax.dynamic_slice_in_dim(block, mp_index * size, size, 0)
    feats, cots = own(features, rows), own(cotangent, rows)
    lap, ends = own(lap_vectors, rows), own(endpoints, rows)
    nodes, edges = own(node_counts, mols), own(edge_counts, mols)
    width = w_query.shape[1]

    wq = jnp.concatenate([w_query, swap(w_query)], axis=1)
    wk = jnp.concatenate([w_key, swap(w_key)], axis=1)
    wv = jnp.concatenate([w_value, swap(w_value)], axis=1)
    bq = jnp.concatenate([bias_query, swap(bias_query)])
    bv = jnp.concatenate([bias_value, swap(bias_value)])
    wo = jnp.concatenate([w_out, swap(w_out)], axis=0)
    wu = jnp.concatenate([w_up, swap(w_up)], axis=1)
    bu = jnp.concatenate([bias_up, swap(bias_up)])
    wd = jnp.concatenate([w_down, swap(w_down)], axis=0)

    keep_rows, is_edge = row_tables(nodes, edges, SEQ)
    ident_rows = identifiers(lap, ends, SEQ)
    g1, s1, g2, s2, bo, bd, wi, tt = (
        v.astype(f32)
        for v in (gain_one, shift_one, gain_two, shift_two, bias_out, bias_down, w_ident, type_table)
    )
    hidden = (
        feats.astype(f32)
        + jnp.dot(ident_rows, wi, precision=lax.Precision.HIGHEST, preferred_element_type=f32)
        + tt[0] * (1.0 - is_edge)[:, None]
        + tt[1] * is_edge[:, None]
    )
    unit_one, inverse_one = norm_parts(hidden)
    normed = (unit_one * g1 + s1).astype(bf16)
    normed_peer = swap(normed)
    queries = (dot(normed, wq) + bq.astype(f32)).astype(bf16)
    key_rows = dot(normed, wk).astype(bf16)
    values = (dot(normed, wv) + bv.astype(f32)).astype(bf16)
    head_count = wq.shape[1] // HDIM
    mixed_out, log_total = attend(queries, key_rows, values, keep_rows, head_count, SEQ)
    attended = (mixed_out * keep_rows[:, None]).astype(bf16)
    middle = hidden + dot(attended, wo) + bo
    unit_two, inverse_two = norm_parts(middle)
    normed_two = (unit_two * g2 + s2).astype(bf16)
    before = dot(normed_two, wu) + bu.astype(f32)
    gelu_out, gelu_pull = jax.vjp(partial(jax.nn.gelu, approximate=False), before)
    active = gelu_out.astype(bf16)
    result = (middle + dot(active, wd) + bd).astype(bf16)

    grad_result = cots.astype(f32) * keep_rows[:, None]
    grad_ffn = grad_result.astype(bf16)
    grad_before = gelu_pull(dot_nt(grad_ffn, wd))[0].astype(bf16)
    grad_normed_two = dot_nt(grad_before, wu)
    grad_middle = grad_result + norm_back(unit_two, inverse_two, grad_normed_two, g2)
    grad_branch = grad_middle.astype(bf16)
    small_a = jnp.stack(
        [
            col_sum(grad_middle),
            col_sum(grad_normed_two * unit_two),
            col_sum(grad_normed_two),
            col_sum(grad_result),
        ]
    )

    def both(block, axis):
        mine, other = jnp.split(block, 2, axis=axis)
        return mine, swap(other)

    def columns(block):
        first, second = jnp.split(block, 2, axis=1)
        mine = jnp.where(mp_index == 0, first, second)
        other = jnp.where(mp_index == 0, second, first)
        return mine + swap(other.astype(bf16)).astype(f32)

    def col_half(block):
        return dot(block[:, :width], block[:, width:])

    def stacked(block):
        return jnp.concatenate(both(block, 1), axis=0)

    nt_all = jnp.concatenate([normed_two, swap(normed_two)], axis=0)
    gb_all = stacked(grad_before)
    at_all = stacked(attended)
    ac_all = stacked(active)
    gm_all = jnp.concatenate([grad_branch, swap(grad_branch)], axis=0)
    gf_all = jnp.concatenate([grad_ffn, swap(grad_ffn)], axis=0)
    small_a = columns(small_a)
    grad_w_up = dot_t(nt_all, gb_all).astype(bf16)
    grad_w_out = dot_t(at_all, gm_all).astype(bf16)
    grad_w_down = dot_t(ac_all, gf_all).astype(bf16)
    grad_bias_up = col_sum(gb_all)

    def reduced(blocks, small_rows):
        small_rows = small_rows.astype(bf16)
        size = sum(block.size for block in blocks) // (INNER * outer_count * width)
        per = [block.reshape(INNER, -1, width) for block in blocks]
        packed = jnp.concatenate(per, axis=1).reshape(INNER, outer_count, size, width)
        parts = [
            lax.dynamic_index_in_dim(packed, inner_at ^ step, 0, keepdims=False)
            for step in range(INNER)
        ]
        got = [inner_move(parts[step], step) for step in range(1, INNER)]
        got_small = [inner_move(small_rows, step) for step in range(1, INNER)]
        total = sum([block.astype(f32) for block in [parts[0]] + got]).astype(bf16)
        small_total = sum([block.astype(f32) for block in [small_rows] + got_small]).astype(bf16)
        picks = [
            lax.dynamic_index_in_dim(total, outer_at ^ step, 0, keepdims=False)
            for step in range(outer_count)
        ]
        got = [outer_move(picks[step], step) for step in range(1, outer_count)]
        got_small = [outer_move(small_total, step) for step in range(1, outer_count)]
        mine = sum([block.astype(f32) for block in [picks[0]] + got]).astype(bf16)
        small_total = sum([block.astype(f32) for block in [small_total] + got_small])
        line = jnp.stack([mine] + [outer_move(mine, step) for step in range(1, outer_count)])
        plane = jnp.stack([line] + [inner_move(line, step) for step in range(1, INNER)])
        order_in = jnp.arange(INNER) ^ inner_at
        order_out = jnp.arange(outer_count) ^ outer_at
        whole = plane[order_in][:, order_out].reshape(INNER, outer_count * size, width)
        outs, start = [], 0
        for block in blocks:
            count = block.size // (INNER * width)
            outs.append(
                whole[:, start : start + count].reshape(block.shape).astype(f32)
            )
            start += count
        return outs, small_total

    (grad_w_up, grad_w_out, grad_w_down), small_a = reduced(
        [grad_w_up, grad_w_out, grad_w_down], jnp.concatenate([small_a, grad_bias_up[None]])
    )

    grad_attended = (dot_nt(grad_branch, wo) * keep_rows[:, None]).astype(bf16)
    grad_queries, grad_keys, grad_values = attend_back(
        queries, key_rows, values, log_total, grad_attended, keep_rows, head_count, SEQ
    )
    grad_normed = dot_nt(grad_queries, wq) + dot_nt(grad_keys, wk) + dot_nt(grad_values, wv)
    grad_hidden = grad_middle + norm_back(unit_one, inverse_one, grad_normed, g1)
    small_b = jnp.concatenate(
        [
            lax.dot_general(
                ident_rows, grad_hidden, (((0,), (0,)), ((), ())),
                precision=lax.Precision.HIGHEST, preferred_element_type=f32,
            ),
            jnp.stack(
                [
                    jnp.sum(grad_hidden * (1.0 - is_edge)[:, None], axis=0),
                    jnp.sum(grad_hidden * is_edge[:, None], axis=0),
                    col_sum(grad_normed * unit_one),
                    col_sum(grad_normed),
                ]
            ),
        ]
    )
    nm_all = jnp.concatenate([normed, normed_peer], axis=0)
    gq_all, gk_all, gv_all = stacked(grad_queries), stacked(grad_keys), stacked(grad_values)
    small_b = columns(small_b)
    (grad_w_query, grad_w_key, grad_w_value), small_b = reduced(
        [dot_t(nm_all, g).astype(bf16) for g in (gq_all, gk_all, gv_all)],
        jnp.concatenate([small_b, col_sum(gq_all)[None], col_sum(gv_all)[None]]),
    )

    def widened(block):
        other = swap(block.astype(bf16)).astype(f32)
        first = jnp.where(mp_index == 0, block, other)
        second = jnp.where(mp_index == 0, other, block)
        return jnp.concatenate([first, second], axis=1)

    wide_a, wide_b = widened(small_a[:4]), widened(small_b[:36])
    return (
        result,
        grad_hidden,
        wide_b[:32],
        wide_b[32:34],
        wide_b[34],
        wide_b[35],
        grad_w_query,
        grad_w_key,
        grad_w_value,
        small_b[36],
        small_b[37],
        grad_w_out,
        wide_a[0],
        wide_a[1],
        wide_a[2],
        grad_w_up,
        small_a[4],
        grad_w_down,
        wide_a[3],
    )


def solution(mesh):
    return jax.shard_map(
        per_device,
        mesh=mesh,
        in_specs=(
            P("dp", None),
            P("dp", None),
            P("dp"),
            P("dp"),
            P("dp", None),
            P(),
            P(),
            P(),
            P(),
            P(None, "mp"),
            P(None, "mp"),
            P(None, "mp"),
            P("mp"),
            P("mp"),
            P("mp", None),
            P(),
            P(),
            P(),
            P(None, "mp"),
            P("mp"),
            P("mp", None),
            P(),
            P("dp", None),
        ),
        out_specs=(
            P(("dp", "mp"), None),
            P(("dp", "mp"), None),
            P(),
            P(),
            P(),
            P(),
            P(None, "mp"),
            P(None, "mp"),
            P(None, "mp"),
            P("mp"),
            P("mp"),
            P("mp", None),
            P(),
            P(),
            P(),
            P(None, "mp"),
            P("mp"),
            P("mp", None),
            P(),
        ),
        check_vma=False,
    )
```

```python
import math

import jax
import jax.numpy as jnp
from jax import lax
from jax.experimental import pallas as pl
from jax.experimental.pallas import tpu as pltpu
from jax.sharding import PartitionSpec as P

HDIM = 24
SEQ = 128
LANES = 128
INNER = 4
OUTER = 4
EPSILON = 1e-05
SCALE = 1.0 / math.sqrt(HDIM)
F32, BF16 = jnp.float32, jnp.bfloat16
VMEM_BYTES = 58 * 1024 * 1024


def dot(left, right):
    return jnp.dot(left, right, preferred_element_type=F32)


def dot_nt(left, right):
    return lax.dot_general(left, right, (((1,), (1,)), ((), ())), preferred_element_type=F32)


def dot_tn(left, right):
    return lax.dot_general(left, right, (((0,), (0,)), ((), ())), preferred_element_type=F32)


def norm_parts(hidden):
    average = jnp.mean(hidden, axis=-1, keepdims=True)
    centred = hidden - average
    inverse = lax.rsqrt(jnp.mean(centred * centred, axis=-1, keepdims=True) + EPSILON)
    return centred * inverse, inverse


def norm_back(unit, inverse, grad_hat):
    return inverse * (
        grad_hat
        - jnp.mean(grad_hat, axis=-1, keepdims=True)
        - unit * jnp.mean(grad_hat * unit, axis=-1, keepdims=True)
    )


def row_sum(block):
    return jnp.sum(block, axis=0, keepdims=True)


def positions(length):
    return lax.broadcasted_iota(jnp.int32, (length, 1), 0)


def whole():
    return pl.BlockSpec(memory_space=pltpu.VMEM)


def call(kernel, scalars, args, specs, outs, scratch=(), flops=0, moved=0):
    return pl.pallas_call(
        kernel,
        out_shape=[jax.ShapeDtypeStruct(shape, kind) for shape, kind in outs],
        grid_spec=pltpu.PrefetchScalarGridSpec(
            num_scalar_prefetch=len(scalars),
            grid=(1,),
            in_specs=specs,
            out_specs=[whole() for _ in outs],
            scratch_shapes=list(scratch),
        ),
        compiler_params=pltpu.CompilerParams(vmem_limit_bytes=VMEM_BYTES),
        cost_estimate=pl.CostEstimate(flops=flops, bytes_accessed=moved, transcendentals=0),
    )(*scalars, *args)


def head_windows(width):
    windows = []
    for pair in range(width // (2 * HDIM)):
        low = pair * 2 * HDIM // LANES * LANES
        high = -(-(pair + 1) * 2 * HDIM // LANES) * LANES
        windows.append((low, high))
    return windows


def split_heads(block, mask_ref, pair, window):
    low, high = window
    tiles = block.shape[0] // mask_ref.shape[1]
    part = block[:, low:high]
    sides = []
    for head in (2 * pair, 2 * pair + 1):
        mask = mask_ref[head][:, low:high]
        sides.append(part * jnp.concatenate([mask] * tiles, axis=0))
    return jnp.concatenate(sides, axis=0)


def embed_kernel(
    info, nodes, edges, feats, lap, ends, w_ident, vecs, biases, w_q, w_k, w_v,
    hidden_out, ident_out, normed_out, normed_t_out, q_out, k_out, v_out,
):
    rows = feats.shape[0]
    mols = rows // SEQ
    lapk = lap.shape[1]

    def molecule(m, carry):
        at = pl.ds(pl.multiple_of(m * SEQ, SEQ), SEQ)
        count = nodes[info[0] * mols + m]
        table = lap[at, :]
        pair = ends[at, :]
        slot = lax.broadcasted_iota(jnp.int32, (SEQ, SEQ), 1)
        hidden = feats[at, :].astype(F32)
        for end in (0, 1):
            pick = (pair[:, end : end + 1] == slot).astype(F32).astype(BF16)
            picked = dot(pick, table).astype(BF16)
            ident_out[at, end * lapk : (end + 1) * lapk] = picked
            hidden = hidden + dot(picked, w_ident[end * lapk : (end + 1) * lapk, :])
        hidden = hidden + jnp.where(positions(SEQ) >= count, vecs[1:2, :], vecs[0:1, :])
        hidden_out[at, :] = hidden
        unit, _ = norm_parts(hidden)
        normed = unit * vecs[2:3, :] + vecs[3:4, :]
        normed_out[at, :] = normed.astype(BF16)
        normed_t_out[:, at] = normed.T.astype(BF16)
        return carry

    lax.fori_loop(0, mols, molecule, 0)
    normed = normed_out[...]
    q_out[...] = (dot(normed, w_q[...]) + biases[0:1, :].astype(F32)).astype(BF16)
    k_out[...] = dot(normed, w_k[...]).astype(BF16)
    v_out[...] = (dot(normed, w_v[...]) + biases[1:2, :].astype(F32)).astype(BF16)


def forward_kernel(
    info, nodes, edges, hidden, normed, q_own, k_own, v_own, w_q, w_k, w_v, biases_own, biases,
    wo_own, wo, wu_own, wu, wd_own, wd, vecs, cots, masks,
    result_out, q_out, k_out, v_out, lse_out, keep_out, send_out, ga_own_out, ga_out, gm_out,
    mixed, attended, middle, unit, normed_two, active, slope, grad_ffn, grad_branch,
):
    rows, dim = hidden.shape
    width = q_own.shape[1]
    mols = rows // SEQ
    pairs = width // (2 * HDIM)
    windows = head_windows(width)
    own_core = info[0]

    q_out[...] = (dot(normed[...], w_q[...]) + biases[0:1, :].astype(F32)).astype(BF16)
    k_out[...] = dot(normed[...], w_k[...]).astype(BF16)
    v_out[...] = (dot(normed[...], w_v[...]) + biases[1:2, :].astype(F32)).astype(BF16)

    def attend(m, carry):
        at = pl.ds(pl.multiple_of(m * SEQ, SEQ), SEQ)
        place = own_core * mols + m
        count = nodes[place] + edges[place]
        key_keep = positions(SEQ) < count
        query_keep = lax.broadcasted_iota(jnp.int32, (1, SEQ), 1) < count
        sides = ((q_own, k_own, v_own, keep_out), (q_out, k_out, v_out, send_out))
        for side, (q_ref, k_ref, v_ref, part_out) in enumerate(sides):
            queries, key_rows = q_ref[at, :], k_ref[at, :]
            values_t = v_ref[at, :].astype(F32).T.astype(BF16)
            for pair in range(pairs):
                low, high = windows[pair]
                both = split_heads(queries, masks, pair, windows[pair])
                scores = dot_nt(key_rows[:, low:high], both) * SCALE
                scores = jnp.where(key_keep, scores, -1e30)
                top = jnp.max(scores, axis=0, keepdims=True)
                raised = jnp.exp(scores - top)
                total = row_sum(raised)
                probs = (raised * (1.0 / total)).astype(BF16)
                lse_out[m, pl.ds(side * pairs + pair, 1), :] = top + jnp.log(total)
                first = pair * 2 * HDIM
                out = dot(values_t[first : first + 2 * HDIM], probs)
                mixed[first : first + HDIM, :] = out[:HDIM, :SEQ]
                mixed[first + HDIM : first + 2 * HDIM, :] = out[HDIM:, SEQ:]
            kept = jnp.where(query_keep, mixed[...], 0.0)
            part_out[dim : dim + width, at] = kept.astype(BF16)
            attended[at, side * width : (side + 1) * width] = kept.T.astype(BF16)
        return carry

    lax.fori_loop(0, mols, attend, 0)
    middle[...] = (
        hidden[...] + dot(attended[:, :width], wo_own[...]) + dot(attended[:, width:], wo[...])
    )

    def second_norm(m, carry):
        at = pl.ds(pl.multiple_of(m * SEQ, SEQ), SEQ)
        place = own_core * mols + m
        keep = positions(SEQ) < nodes[place] + edges[place]
        total = middle[at, :] + vecs[4:5, :]
        middle[at, :] = total
        unit_rows, _ = norm_parts(total)
        unit[at, :] = unit_rows
        rows_two = unit_rows * vecs[5:6, :] + vecs[6:7, :]
        normed_two[at, :] = rows_two.astype(BF16)
        turned = rows_two.T.astype(BF16)
        keep_out[:dim, at] = turned
        send_out[:dim, at] = turned
        grad_ffn[at, :] = jnp.where(keep, cots[at, :].astype(F32), 0.0).astype(BF16)
        return carry

    lax.fori_loop(0, mols, second_norm, 0)

    for side, (w_ref, b_ref, part_out) in enumerate(
        ((wu_own, biases_own, keep_out), (wu, biases, send_out))
    ):
        columns = slice(side * width, (side + 1) * width)
        slope[:, columns] = dot(normed_two[...], w_ref[...]) + b_ref[2:3, :].astype(F32)

        def activate(m, carry):
            at = pl.ds(pl.multiple_of(m * SEQ, SEQ), SEQ)
            before = slope[at, columns]
            phi = 0.5 * (1.0 + lax.erf(before * math.sqrt(0.5)))
            out = before * phi
            slope[at, columns] = phi + before * jnp.exp(before * before * -0.5) * (
                1.0 / math.sqrt(2.0 * math.pi)
            )
            active[at, columns] = out.astype(BF16)
            part_out[dim + width : dim + 2 * width, at] = out.T.astype(BF16)
            return carry

        lax.fori_loop(0, mols, activate, 0)

    result_out[...] = (
        middle[...]
        + dot(active[:, :width], wd_own[...])
        + dot(active[:, width:], wd[...])
        + vecs[7:8, :]
    ).astype(BF16)

    place_b = dim + 2 * width
    for side, (w_ref, part_out) in enumerate(((wd_own, keep_out), (wd, send_out))):
        columns = slice(side * width, (side + 1) * width)
        grad_before = slope[:, columns] * dot_nt(grad_ffn[...], w_ref[...])
        part_out[place_b : place_b + rows, :] = grad_before.astype(BF16)

    back = pl.ds(place_b, rows)
    gm_out[...] = dot_nt(keep_out[back, :], wu_own[...]) + dot_nt(send_out[back, :], wu[...])

    def second_back(m, sums):
        at = pl.ds(pl.multiple_of(m * SEQ, SEQ), SEQ)
        place = own_core * mols + m
        keep = positions(SEQ) < nodes[place] + edges[place]
        grad_normed = gm_out[at, :]
        unit_rows = unit[at, :]
        _, inverse = norm_parts(middle[at, :])
        grad_result = jnp.where(keep, cots[at, :].astype(F32), 0.0)
        grad = grad_result + norm_back(unit_rows, inverse, grad_normed * vecs[5:6, :])
        gm_out[at, :] = grad
        grad_branch[at, :] = grad.astype(BF16)
        return (
            sums[0] + row_sum(grad),
            sums[1] + row_sum(grad_normed * unit_rows),
            sums[2] + row_sum(grad_normed),
            sums[3] + row_sum(grad_result),
        )

    nothing = jnp.zeros((1, dim), F32)
    sums = lax.fori_loop(0, mols, second_back, (nothing,) * 4)
    place_m = place_b + rows
    for part_out in (keep_out, send_out):
        part_out[place_m : place_m + rows, :] = grad_branch[:, :width]
        part_out[place_m + rows : place_m + 2 * rows, :] = grad_branch[:, width:]
    small = jnp.concatenate(list(sums) + [nothing] * 12, axis=0)
    left, right = small[:, :width], small[:, width:]
    place_s = place_m + 2 * rows
    keep_out[place_s:, :] = jnp.where(own_core == 0, left, right).astype(BF16)
    send_out[place_s:, :] = jnp.where(own_core == 0, right, left).astype(BF16)

    ga_own_out[...] = dot_nt(grad_branch[...], wo_own[...]).astype(BF16)
    ga_out[...] = dot_nt(grad_branch[...], wo[...]).astype(BF16)

    def mask_rows(m, carry):
        at = pl.ds(pl.multiple_of(m * SEQ, SEQ), SEQ)
        place = own_core * mols + m
        keep = positions(SEQ) < nodes[place] + edges[place]
        for ref in (ga_own_out, ga_out):
            ref[at, :] = jnp.where(keep, ref[at, :].astype(F32), 0.0).astype(BF16)
        return carry

    lax.fori_loop(0, mols, mask_rows, 0)


def attend_back_kernel(
    info, nodes, edges, q_own, k_own, v_own, ga_own, q_ref2, k_ref2, v_ref2, ga_ref2, lse, masks,
    keep_out, send_out, dq_t, dk, dv,
):
    rows, width = q_own.shape
    mols = rows // SEQ
    pairs = width // (2 * HDIM)
    windows = head_windows(width)
    own_core = info[0]

    def molecule(m, carry):
        base = pl.multiple_of(m * SEQ, SEQ)
        at = pl.ds(base, SEQ)
        place = own_core * mols + m
        key_keep = positions(SEQ) < nodes[place] + edges[place]
        sides = (
            (q_own, k_own, v_own, ga_own, keep_out),
            (q_ref2, k_ref2, v_ref2, ga_ref2, send_out),
        )
        for side, (q_ref, k_ref, v_ref, g_ref, part_out) in enumerate(sides):
            queries, key_rows, values, grads = q_ref[at, :], k_ref[at, :], v_ref[at, :], g_ref[at, :]
            keys_t = key_rows.astype(F32).T.astype(BF16)
            dk[...] = jnp.zeros_like(dk)
            dv[...] = jnp.zeros_like(dv)
            for pair in range(pairs):
                low, high = windows[pair]
                both_q = split_heads(queries, masks, pair, windows[pair])
                both_g = split_heads(grads, masks, pair, windows[pair])
                scores = dot_nt(key_rows[:, low:high], both_q) * SCALE
                total = lse[m, pl.ds(side * pairs + pair, 1), :]
                probs = jnp.where(key_keep, jnp.exp(scores - total), 0.0)
                grad_probs = dot_nt(values[:, low:high], both_g)
                inner = row_sum(probs * grad_probs)
                grad_scores = (probs * (grad_probs - inner)).astype(BF16)
                dv[:, low:high] += dot(probs.astype(BF16), both_g)
                dk[:, low:high] += dot(grad_scores, both_q)
                first = pair * 2 * HDIM
                out = dot(keys_t[first : first + 2 * HDIM], grad_scores)
                dq_t[first : first + HDIM, :] = out[:HDIM, :SEQ]
                dq_t[first + HDIM : first + 2 * HDIM, :] = out[HDIM:, SEQ:]
            part_out[at, :] = (dq_t[...].T * SCALE).astype(BF16)
            part_out[pl.ds(base + rows, SEQ), :] = (dk[...] * SCALE).astype(BF16)
            part_out[pl.ds(base + 2 * rows, SEQ), :] = dv[...].astype(BF16)
        return carry

    lax.fori_loop(0, mols, molecule, 0)


def embed_back_kernel(
    info, nodes, edges, grads_own, grads, wq_own, wk_own, wv_own, w_q, w_k, w_v, hidden, ident,
    grad_middle, vecs, features_out, keep_out, send_out, grad_normed, small,
):
    rows, dim = hidden.shape
    width = wq_own.shape[1]
    mols = rows // SEQ
    own_core = info[0]
    idw = ident.shape[1]
    total = None
    for part, weights in ((grads_own, (wq_own, wk_own, wv_own)), (grads, (w_q, w_k, w_v))):
        for place, weight in enumerate(weights):
            term = dot_nt(part[place * rows : (place + 1) * rows, :], weight[...])
            total = term if total is None else total + term
    grad_normed[...] = total
    small[...] = jnp.zeros_like(small)

    def molecule(m, carry):
        at = pl.ds(pl.multiple_of(m * SEQ, SEQ), SEQ)
        is_edge = positions(SEQ) >= nodes[own_core * mols + m]
        unit, inverse = norm_parts(hidden[at, :])
        grad_rows = grad_normed[at, :]
        grad = grad_middle[at, :] + norm_back(unit, inverse, grad_rows * vecs[2:3, :])
        features_out[at, :] = grad
        high = grad.astype(BF16)
        rest = (grad - high.astype(F32)).astype(BF16)
        picked = ident[at, :]
        small[:idw, :] += dot_tn(picked, high) + dot_tn(picked, rest)
        edge_rows = jnp.where(is_edge, grad, 0.0)
        small[idw : idw + 1, :] += row_sum(grad - edge_rows)
        small[idw + 1 : idw + 2, :] += row_sum(edge_rows)
        small[idw + 2 : idw + 3, :] += row_sum(grad_rows * unit)
        small[idw + 3 : idw + 4, :] += row_sum(grad_rows)
        return carry

    lax.fori_loop(0, mols, molecule, 0)
    left, right = small[:, :width], small[:, width:]
    keep_out[...] = jnp.where(own_core == 0, left, right).astype(BF16)
    send_out[...] = jnp.where(own_core == 0, right, left).astype(BF16)


def ffn_grads_kernel(info, nodes, edges, kept, got, cots, *rest):
    outs, (grad_ffn,) = rest[:INNER], rest[INNER:]
    rows_all, dim = cots.shape
    rows, width = rows_all // 2, kept.shape[1]
    mols = rows // SEQ
    own_core, inner = info[0], info[1]
    for m in range(2 * mols):
        keep = positions(SEQ) < nodes[m] + edges[m]
        at = slice(m * SEQ, (m + 1) * SEQ)
        grad_ffn[at, :] = jnp.where(keep, cots[at, :].astype(F32), 0.0).astype(BF16)
    own_rows = pl.ds(pl.multiple_of(own_core * rows, SEQ), rows)
    other_rows = pl.ds(pl.multiple_of((1 - own_core) * rows, SEQ), rows)
    place_b = dim + 2 * width
    place_m = place_b + rows
    place_s = place_m + 2 * rows
    small_rows = kept.shape[0] - place_s
    back = slice(place_b, place_m)
    bias = row_sum(kept[back, :].astype(F32)) + row_sum(got[back, :].astype(F32))
    small = kept[place_s:, :].astype(F32) + got[place_s:, :].astype(F32)
    spot = lax.broadcasted_iota(jnp.int32, (small_rows, width), 0)
    small = jnp.where(spot == 4, bias, small).astype(BF16)
    unit = dim // (INNER * OUTER)
    for step in range(INNER):
        dest = inner ^ step
        out = outs[step]
        size = dim // INNER
        at = pl.ds(pl.multiple_of(dest * size, 64), size)
        up = dot(kept[at, :], kept[back, :]) + dot(got[at, :], got[back, :])
        for z in range(OUTER):
            out[z, :unit, :] = up[z * unit : (z + 1) * unit].astype(BF16)
            out[z, 3 * unit :, :] = small
        size = width // INNER
        at = pl.ds(pl.multiple_of(dim + dest * size, 32), size)
        for half in (0, 1):
            mid = slice(place_m + half * rows, place_m + (half + 1) * rows)
            proj = dot(kept[at, :], kept[mid, :]) + dot(got[at, :], got[mid, :])
            for block in range(OUTER // 2):
                out[2 * block + half, unit : 2 * unit, :] = proj[
                    block * unit : (block + 1) * unit
                ].astype(BF16)
        at = pl.ds(pl.multiple_of(dim + width + dest * size, 32), size)
        for half in (0, 1):
            columns = slice(half * width, (half + 1) * width)
            proj = dot(kept[at, :], grad_ffn[own_rows, columns])
            proj = proj + dot(got[at, :], grad_ffn[other_rows, columns])
            for block in range(OUTER // 2):
                out[2 * block + half, 2 * unit : 3 * unit, :] = proj[
                    block * unit : (block + 1) * unit
                ].astype(BF16)


def qkv_grads_kernel(info, nodes, edges, normed_t, normed_t_got, kept, got, small_kept, small_got, *outs):
    dim, rows = normed_t.shape
    width = kept.shape[1]
    inner = info[1]
    unit = dim // (INNER * OUTER)
    small_rows = small_kept.shape[0]
    small = small_kept[...].astype(F32) + small_got[...].astype(F32)
    spot = lax.broadcasted_iota(jnp.int32, (small_rows, width), 0)
    for row, place in ((36, 0), (37, 2)):
        part = slice(place * rows, (place + 1) * rows)
        bias = row_sum(kept[part, :].astype(F32)) + row_sum(got[part, :].astype(F32))
        small = jnp.where(spot == row, bias, small)
    small = small.astype(BF16)
    for step in range(INNER):
        dest = inner ^ step
        out = outs[step]
        size = dim // INNER
        at = pl.ds(pl.multiple_of(dest * size, 64), size)
        for place in range(3):
            part = slice(place * rows, (place + 1) * rows)
            grad = dot(normed_t[at, :], kept[part, :]) + dot(normed_t_got[at, :], got[part, :])
            for z in range(OUTER):
                out[z, place * unit : (place + 1) * unit, :] = grad[
                    z * unit : (z + 1) * unit
                ].astype(BF16)
        for z in range(OUTER):
            out[z, 3 * unit :, :] = small


def plane_sum_kernel(info, first, second, third, fourth, *outs):
    outer = info[2]
    for step in range(OUTER):
        place = outer ^ step
        total = first[place].astype(F32) + second[place].astype(F32)
        total = total + third[place].astype(F32) + fourth[place].astype(F32)
        outs[step][...] = total.astype(BF16)


def line_sum_kernel(info, first, second, third, fourth, out, small_out):
    total = first[...].astype(F32) + second[...].astype(F32)
    total = total + third[...].astype(F32) + fourth[...].astype(F32)
    size = out.shape[0]
    out[...] = total[:size].astype(BF16)
    small_out[...] = total[size:]


def place_kernel(split_second, wide_rows, info, *refs):
    lines, (small, small_got), outs = refs[:INNER], refs[INNER : INNER + 2], refs[INNER + 2 :]
    own_core, inner, outer = info[0], info[1], info[2]
    unit = lines[0].shape[1] // 3
    width = lines[0].shape[2]
    for step in range(INNER):
        dest = inner ^ step
        for z in range(OUTER):
            block = lines[step][outer ^ z].astype(F32)
            tall = pl.ds(pl.multiple_of((dest * OUTER + z) * unit, 16), unit)
            flat = pl.ds(pl.multiple_of((dest * (OUTER // 2) + z // 2) * unit, 16), unit)
            columns = slice(z % 2 * width, (z % 2 + 1) * width)
            for place in range(3):
                part = block[place * unit : (place + 1) * unit]
                if split_second and place > 0:
                    outs[place][flat, columns] = part
                else:
                    outs[place][tall, :] = part
    mine, other = small[...], small_got[...]
    left = jnp.where(own_core == 0, mine, other)
    right = jnp.where(own_core == 0, other, mine)
    wide_out, narrow_out = outs[3], outs[4]
    wide_out[:, :width] = left[:wide_rows]
    wide_out[:, width:] = right[:wide_rows]
    narrow_out[...] = mine[wide_rows:]


def per_device(
    features, lap_vectors, node_counts, edge_counts, endpoints, w_ident, type_table,
    gain_one, shift_one, w_query, w_key, w_value, bias_query, bias_value, w_out, bias_out,
    gain_two, shift_two, w_up, bias_up, w_down, bias_down, cotangent,
):
    dp_count = lax.axis_size("dp")
    dp_index = lax.axis_index("dp")
    mp_index = lax.axis_index("mp")
    block = INNER * OUTER
    rest_count = dp_count // block
    info = jnp.stack([mp_index, dp_index % INNER, dp_index // INNER % OUTER]).astype(jnp.int32)

    def swap(part):
        return lax.ppermute(part, "mp", [(0, 1), (1, 0)])

    def inner_move(part, step):
        return lax.ppermute(part, "dp", [(s, s ^ step) for s in range(dp_count)])

    def outer_move(part, step):
        return lax.ppermute(part, "dp", [(s, s ^ (step * INNER)) for s in range(dp_count)])

    rows_all, dim = features.shape
    rows = rows_all // 2
    mols = rows // SEQ
    width = w_query.shape[1]
    heads = width // HDIM
    lapk = lap_vectors.shape[1]
    idw = w_ident.shape[0]
    scalars = (info, node_counts, edge_counts)
    half_rows = lambda columns: pl.BlockSpec((rows, columns), lambda g, info, n, e: (info[0], 0))

    biases = jnp.stack([bias_query, bias_value, bias_up])
    vecs = jnp.concatenate(
        [type_table]
        + [v[None] for v in (gain_one, shift_one, bias_out, gain_two, shift_two, bias_down)]
    ).astype(F32)
    masks = (
        lax.broadcasted_iota(jnp.int32, (heads, 16, width), 2) // HDIM
        == lax.broadcasted_iota(jnp.int32, (heads, 16, width), 0)
    ).astype(BF16)

    wq_got, wk_got, wv_got = swap(w_query), swap(w_key), swap(w_value)
    biases_got = swap(biases)
    wo_got, wu_got, wd_got = swap(w_out), swap(w_up), swap(w_down)

    square = dim * dim * rows * 2
    hidden, ident, normed, normed_t, q_own, k_own, v_own = call(
        embed_kernel,
        scalars,
        (features, lap_vectors, endpoints, w_ident, vecs, biases, w_query, w_key, w_value),
        [half_rows(dim), half_rows(lapk), half_rows(2)] + [whole()] * 6,
        [
            ((rows, dim), F32),
            ((rows, idw), BF16),
            ((rows, dim), BF16),
            ((dim, rows), BF16),
            ((rows, width), BF16),
            ((rows, width), BF16),
            ((rows, width), BF16),
        ],
        flops=2 * square,
        moved=8_000_000,
    )
    normed_t_got = swap(normed_t)
    sent_rows = dim + 2 * width + 3 * rows + 16
    result, q_got, k_got, v_got, lse, kept_a, sent_a, ga_own, ga_got, grad_middle = call(
        forward_kernel,
        scalars,
        (
            hidden, normed, q_own, k_own, v_own, wq_got, wk_got, wv_got, biases, biases_got,
            w_out, wo_got, w_up, wu_got, w_down, wd_got, vecs, cotangent, masks,
        ),
        [whole()] * 17 + [half_rows(dim), whole()],
        [
            ((rows, dim), BF16),
            ((rows, width), BF16),
            ((rows, width), BF16),
            ((rows, width), BF16),
            ((mols, heads, 2 * SEQ), F32),
            ((sent_rows, width), BF16),
            ((sent_rows, width), BF16),
            ((rows, width), BF16),
            ((rows, width), BF16),
            ((rows, dim), F32),
        ],
        scratch=[
            pltpu.VMEM((width, SEQ), F32),
            pltpu.VMEM((rows, dim), BF16),
            pltpu.VMEM((rows, dim), F32),
            pltpu.VMEM((rows, dim), F32),
            pltpu.VMEM((rows, dim), BF16),
            pltpu.VMEM((rows, dim), BF16),
            pltpu.VMEM((rows, dim), F32),
            pltpu.VMEM((rows, dim), BF16),
            pltpu.VMEM((rows, dim), BF16),
        ],
        flops=12 * square,
        moved=25_000_000,
    )
    got_a = swap(sent_a)

    unit = dim // block
    small_a, small_b = 16, 48

    def rest_sum(part):
        if rest_count == 1:
            return part
        groups = [[r * block + s for r in range(rest_count)] for s in range(block)]
        return lax.psum(part.astype(F32), "dp", axis_index_groups=groups).astype(part.dtype)

    def reduced(parts, small_rows):
        got = [inner_move(parts[step], step) for step in range(1, INNER)]
        lines = call(
            plane_sum_kernel,
            (info,),
            (parts[0], *got),
            [whole()] * INNER,
            [((3 * unit + small_rows, width), BF16)] * OUTER,
            flops=1_000_000,
            moved=3_000_000,
        )
        got = [outer_move(lines[step], step) for step in range(1, OUTER)]
        mine, small = call(
            line_sum_kernel,
            (info,),
            (lines[0], *got),
            [whole()] * OUTER,
            [((3 * unit, width), BF16), ((small_rows, width), F32)],
            flops=1_000_000,
            moved=1_000_000,
        )
        mine, small = rest_sum(mine), rest_sum(small)
        small_got = swap(small)
        line = jnp.stack([mine] + [outer_move(mine, step) for step in range(1, OUTER)])
        planes = [line] + [inner_move(line, step) for step in range(1, INNER)]
        return planes, small, small_got

    def placed(planes, small, small_got, split_second, wide_rows):
        tall, flat = ((dim, width), F32), ((width, dim), F32)
        shapes = [tall, flat, flat] if split_second else [tall] * 3
        return call(
            lambda *refs: place_kernel(split_second, wide_rows, *refs),
            (info,),
            (*planes, small, small_got),
            [whole()] * (INNER + 2),
            shapes
            + [((wide_rows, dim), F32), ((small.shape[0] - wide_rows, width), F32)],
            flops=1_000_000,
            moved=6_000_000,
        )

    parts_a = call(
        ffn_grads_kernel,
        scalars,
        (kept_a, got_a, cotangent),
        [whole()] * 3,
        [((OUTER, 3 * unit + small_a, width), BF16)] * INNER,
        scratch=[pltpu.VMEM((rows_all, dim), BF16)],
        flops=3 * square,
        moved=7_000_000,
    )
    planes_a, sums_a, sums_a_got = reduced(parts_a, small_a)

    kept_b, sent_b = call(
        attend_back_kernel,
        scalars,
        (q_own, k_own, v_own, ga_own, q_got, k_got, v_got, ga_got, lse, masks),
        [whole()] * 10,
        [((3 * rows, width), BF16)] * 2,
        scratch=[
            pltpu.VMEM((width, SEQ), F32),
            pltpu.VMEM((SEQ, width), F32),
            pltpu.VMEM((SEQ, width), F32),
        ],
        flops=20 * square,
        moved=10_000_000,
    )
    got_b = swap(sent_b)
    grad_features, small_kept, small_sent = call(
        embed_back_kernel,
        scalars,
        (
            kept_b, sent_b, w_query, w_key, w_value, wq_got, wk_got, wv_got, hidden, ident,
            grad_middle, vecs,
        ),
        [whole()] * 12,
        [((rows, dim), F32), ((small_b, width), BF16), ((small_b, width), BF16)],
        scratch=[pltpu.VMEM((rows, dim), F32), pltpu.VMEM((small_b, dim), F32)],
        flops=4 * square,
        moved=9_000_000,
    )
    small_got = swap(small_sent)
    parts_b = call(
        qkv_grads_kernel,
        scalars,
        (normed_t, normed_t_got, kept_b, got_b, small_kept, small_got),
        [whole()] * 6,
        [((OUTER, 3 * unit + small_b, width), BF16)] * INNER,
        flops=3 * square,
        moved=6_000_000,
    )
    planes_b, sums_b, sums_b_got = reduced(parts_b, small_b)

    grad_w_up, grad_w_out, grad_w_down, wide_a, narrow_a = placed(
        planes_a, sums_a, sums_a_got, True, 4
    )
    wide_b_rows = idw + 4
    grad_w_query, grad_w_key, grad_w_value, wide_b, narrow_b = placed(
        planes_b, sums_b, sums_b_got, False, wide_b_rows
    )
    return (
        result,
        grad_features,
        wide_b[:idw],
        wide_b[idw : idw + 2],
        wide_b[idw + 2],
        wide_b[idw + 3],
        grad_w_query,
        grad_w_key,
        grad_w_value,
        narrow_b[0],
        narrow_b[1],
        grad_w_out,
        wide_a[0],
        wide_a[1],
        wide_a[2],
        grad_w_up,
        narrow_a[0],
        grad_w_down,
        wide_a[3],
    )


def solution(mesh):
    token, split = P("dp", None), P(("dp", "mp"), None)
    columns, lines, cut, copy = P(None, "mp"), P("mp", None), P("mp"), P()
    return jax.shard_map(
        per_device,
        mesh=mesh,
        in_specs=(
            token, token, P("dp"), P("dp"), token, copy, copy, copy, copy, columns, columns,
            columns, cut, cut, lines, copy, copy, copy, columns, cut, lines, copy, token,
        ),
        out_specs=(
            split, split, copy, copy, copy, copy, columns, columns, columns, cut, cut, lines,
            copy, copy, copy, columns, cut, lines, copy,
        ),
        check_vma=False,
    )
```

```python
import math

import jax
import jax.numpy as jnp
from jax import lax
from jax.experimental import pallas as pl
from jax.experimental.pallas import tpu as pltpu
from jax.sharding import PartitionSpec as P

HDIM = 24
SEQ = 128
LANES = 128
INNER = 4
OUTER = 4
EPSILON = 1e-05
SCALE = 1.0 / math.sqrt(HDIM)
F32, BF16 = jnp.float32, jnp.bfloat16
MIB = 1024 * 1024


def dot(left, right):
    return jnp.dot(left, right, preferred_element_type=F32)


def dot_nt(left, right):
    return lax.dot_general(left, right, (((1,), (1,)), ((), ())), preferred_element_type=F32)


def dot_tn(left, right):
    return lax.dot_general(left, right, (((0,), (0,)), ((), ())), preferred_element_type=F32)


def norm_parts(hidden):
    average = jnp.mean(hidden, axis=-1, keepdims=True)
    centred = hidden - average
    inverse = lax.rsqrt(jnp.mean(centred * centred, axis=-1, keepdims=True) + EPSILON)
    return centred * inverse, inverse


def norm_back(unit, inverse, grad_hat):
    return inverse * (
        grad_hat
        - jnp.mean(grad_hat, axis=-1, keepdims=True)
        - unit * jnp.mean(grad_hat * unit, axis=-1, keepdims=True)
    )


def row_sum(block):
    return jnp.sum(block, axis=0, keepdims=True)


def positions(length):
    return lax.broadcasted_iota(jnp.int32, (length, 1), 0)


def whole():
    return pl.BlockSpec(memory_space=pltpu.VMEM)


def call(kernel, scalars, args, specs, outs, scratch=(), micros=5, limit=24):
    return pl.pallas_call(
        kernel,
        out_shape=[jax.ShapeDtypeStruct(shape, kind) for shape, kind in outs],
        grid_spec=pltpu.PrefetchScalarGridSpec(
            num_scalar_prefetch=len(scalars),
            grid=(1,),
            in_specs=specs,
            out_specs=[whole() for _ in outs],
            scratch_shapes=list(scratch),
        ),
        compiler_params=pltpu.CompilerParams(vmem_limit_bytes=limit * MIB),
        cost_estimate=pl.CostEstimate(
            flops=0, bytes_accessed=micros * 3_000_000, transcendentals=0
        ),
    )(*scalars, *args)


def head_windows(width):
    windows = []
    for pair in range(width // (2 * HDIM)):
        low = pair * 2 * HDIM // LANES * LANES
        high = -(-(pair + 1) * 2 * HDIM // LANES) * LANES
        windows.append((low, high))
    return windows


def split_heads(block, pair, window):
    low, high = window
    part = block[:, low:high]
    column = low + lax.broadcasted_iota(jnp.int32, (16, high - low), 1)
    sides = []
    for head in (2 * pair, 2 * pair + 1):
        inside = (column >= head * HDIM) & (column < (head + 1) * HDIM)
        mask = jnp.where(inside, 1.0, 0.0).astype(BF16)
        sides.append(part * jnp.concatenate([mask] * (block.shape[0] // 16), axis=0))
    return jnp.concatenate(sides, axis=0)


def embed_kernel(
    info, nodes, edges, feats, lap, ends, w_ident, vecs, biases, w_q, w_k, w_v,
    hidden_out, ident_out, normed_out, normed_t_out, q_out, k_out, v_out,
):
    rows = feats.shape[0]
    mols = rows // SEQ

    def molecule(m, carry):
        at = pl.ds(pl.multiple_of(m * SEQ, SEQ), SEQ)
        count = nodes[info[0] * mols + m]
        table = lap[:, at]
        slot = lax.broadcasted_iota(jnp.int32, (SEQ, SEQ), 0)
        picked = []
        for end in (0, 1):
            pick = jnp.where(ends[end : end + 1, at] == slot, 1.0, 0.0).astype(BF16)
            picked.append(dot(table, pick))
        ident = jnp.concatenate(picked, axis=0).astype(BF16)
        ident_out[:, at] = ident
        hidden = feats[at, :].astype(F32) + dot_tn(ident, w_ident[...])
        hidden = hidden + jnp.where(positions(SEQ) >= count, vecs[1:2, :], vecs[0:1, :])
        hidden_out[at, :] = hidden
        unit, _ = norm_parts(hidden)
        normed = (unit * vecs[2:3, :] + vecs[3:4, :]).astype(BF16)
        normed_out[at, :] = normed
        normed_t_out[:, at] = normed.T
        return carry

    lax.fori_loop(0, mols, molecule, 0)
    normed = normed_out[...]
    q_out[...] = (dot(normed, w_q[...]) + biases[0:1, :].astype(F32)).astype(BF16)
    k_out[...] = dot(normed, w_k[...]).astype(BF16)
    v_out[...] = (dot(normed, w_v[...]) + biases[1:2, :].astype(F32)).astype(BF16)


def forward_kernel(
    info, nodes, edges, hidden, normed, q_own, k_own, v_own, w_q, w_k, w_v, biases_own, biases,
    wo_own, wo, wu_own, wu, wd_own, wd, vecs, cots,
    q_out, k_out, v_out, probs_out, keep_out, send_out, middle, active, gm_out, grad_branch,
    mixed, attended, unit, normed_two, slope, grad_ffn,
):
    rows, dim = hidden.shape
    width = q_own.shape[1]
    mols = rows // SEQ
    pairs = width // (2 * HDIM)
    windows = head_windows(width)
    own_core = info[0]

    q_out[...] = (dot(normed[...], w_q[...]) + biases[0:1, :].astype(F32)).astype(BF16)
    k_out[...] = dot(normed[...], w_k[...]).astype(BF16)
    v_out[...] = (dot(normed[...], w_v[...]) + biases[1:2, :].astype(F32)).astype(BF16)

    def attend(m, carry):
        at = pl.ds(pl.multiple_of(m * SEQ, SEQ), SEQ)
        place = own_core * mols + m
        count = nodes[place] + edges[place]
        key_keep = positions(SEQ) < count
        query_keep = lax.broadcasted_iota(jnp.int32, (1, SEQ), 1) < count
        sides = ((q_own, k_own, v_own, keep_out), (q_out, k_out, v_out, send_out))
        for side, (q_ref, k_ref, v_ref, part_out) in enumerate(sides):
            queries, key_rows = q_ref[at, :], k_ref[at, :]
            values_t = v_ref[at, :].T
            for pair in range(pairs):
                low, high = windows[pair]
                both = split_heads(queries, pair, windows[pair])
                scores = dot_nt(key_rows[:, low:high], both) * SCALE
                scores = jnp.where(key_keep, scores, -1e30)
                top = jnp.max(scores, axis=0, keepdims=True)
                raised = jnp.exp(scores - top)
                total = row_sum(raised)
                probs = (raised * (1.0 / total)).astype(BF16)
                probs_out[m, side * pairs + pair] = probs
                first = pair * 2 * HDIM
                out = dot(values_t[first : first + 2 * HDIM], probs)
                mixed[first : first + HDIM, :] = out[:HDIM, :SEQ]
                mixed[first + HDIM : first + 2 * HDIM, :] = out[HDIM:, SEQ:]
            kept = jnp.where(query_keep, mixed[...], 0.0).astype(BF16)
            part_out[dim : dim + width, at] = kept
            attended[at, side * width : (side + 1) * width] = kept.T
        return carry

    lax.fori_loop(0, mols, attend, 0)
    middle[...] = (
        hidden[...] + dot(attended[:, :width], wo_own[...]) + dot(attended[:, width:], wo[...])
    )

    def second_norm(m, carry):
        at = pl.ds(pl.multiple_of(m * SEQ, SEQ), SEQ)
        place = own_core * mols + m
        keep = positions(SEQ) < nodes[place] + edges[place]
        total = middle[at, :] + vecs[4:5, :]
        middle[at, :] = total
        unit_rows, _ = norm_parts(total)
        unit[at, :] = unit_rows
        rows_two = (unit_rows * vecs[5:6, :] + vecs[6:7, :]).astype(BF16)
        normed_two[at, :] = rows_two
        turned = rows_two.T
        keep_out[:dim, at] = turned
        send_out[:dim, at] = turned
        grad_ffn[at, :] = jnp.where(keep, cots[at, :].astype(F32), 0.0).astype(BF16)
        return carry

    lax.fori_loop(0, mols, second_norm, 0)

    for side, (w_ref, b_ref, part_out) in enumerate(
        ((wu_own, biases_own, keep_out), (wu, biases, send_out))
    ):
        columns = slice(side * width, (side + 1) * width)
        slope[:, columns] = dot(normed_two[...], w_ref[...]) + b_ref[2:3, :].astype(F32)

        def activate(m, carry):
            at = pl.ds(pl.multiple_of(m * SEQ, SEQ), SEQ)
            before = slope[at, columns]
            phi = 0.5 * (1.0 + lax.erf(before * math.sqrt(0.5)))
            out = (before * phi).astype(BF16)
            slope[at, columns] = phi + before * jnp.exp(before * before * -0.5) * (
                1.0 / math.sqrt(2.0 * math.pi)
            )
            active[at, columns] = out
            part_out[dim + width : dim + 2 * width, at] = out.T
            return carry

        lax.fori_loop(0, mols, activate, 0)

    place_b = dim + 2 * width
    for side, (w_ref, part_out) in enumerate(((wd_own, keep_out), (wd, send_out))):
        columns = slice(side * width, (side + 1) * width)
        grad_before = slope[:, columns] * dot_nt(grad_ffn[...], w_ref[...])
        part_out[place_b : place_b + rows, :] = grad_before.astype(BF16)

    back = pl.ds(place_b, rows)
    gm_out[...] = dot_nt(keep_out[back, :], wu_own[...]) + dot_nt(send_out[back, :], wu[...])

    def second_back(m, sums):
        at = pl.ds(pl.multiple_of(m * SEQ, SEQ), SEQ)
        place = own_core * mols + m
        keep = positions(SEQ) < nodes[place] + edges[place]
        grad_normed = gm_out[at, :]
        unit_rows = unit[at, :]
        _, inverse = norm_parts(middle[at, :])
        grad_result = jnp.where(keep, cots[at, :].astype(F32), 0.0)
        grad = grad_result + norm_back(unit_rows, inverse, grad_normed * vecs[5:6, :])
        gm_out[at, :] = grad
        grad_branch[at, :] = grad.astype(BF16)
        return (
            sums[0] + row_sum(grad),
            sums[1] + row_sum(grad_normed * unit_rows),
            sums[2] + row_sum(grad_normed),
            sums[3] + row_sum(grad_result),
        )

    nothing = jnp.zeros((1, dim), F32)
    sums = lax.fori_loop(0, mols, second_back, (nothing,) * 4)
    place_m = place_b + rows
    for part_out in (keep_out, send_out):
        part_out[place_m : place_m + rows, :] = grad_branch[:, :width]
        part_out[place_m + rows : place_m + 2 * rows, :] = grad_branch[:, width:]
    small = jnp.concatenate(list(sums) + [nothing] * 12, axis=0)
    left, right = small[:, :width], small[:, width:]
    place_s = place_m + 2 * rows
    keep_out[place_s:, :] = jnp.where(own_core == 0, left, right).astype(BF16)
    send_out[place_s:, :] = jnp.where(own_core == 0, right, left).astype(BF16)


def result_kernel(
    info, nodes, edges, middle, active, grad_branch, wd_own, wd, wo_own, wo, vecs,
    result_out, ga_own_out, ga_out,
):
    rows = middle.shape[0]
    width = wd.shape[0]
    mols = rows // SEQ
    result_out[...] = (
        middle[...]
        + dot(active[:, :width], wd_own[...])
        + dot(active[:, width:], wd[...])
        + vecs[7:8, :]
    ).astype(BF16)
    for ref, weight in ((ga_own_out, wo_own), (ga_out, wo)):
        product = dot_nt(grad_branch[...], weight[...])
        for m in range(mols):
            place = info[0] * mols + m
            keep = positions(SEQ) < nodes[place] + edges[place]
            at = slice(m * SEQ, (m + 1) * SEQ)
            ref[at, :] = jnp.where(keep, product[at], 0.0).astype(BF16)


def attend_back_kernel(
    info, nodes, edges, q_own, k_own, v_own, ga_own, q_ref2, k_ref2, v_ref2, ga_ref2, probs_all,
    keep_out, send_out, dq_t, dk, dv,
):
    rows, width = q_own.shape
    mols = rows // SEQ
    pairs = width // (2 * HDIM)
    windows = head_windows(width)

    def molecule(m, carry):
        base = pl.multiple_of(m * SEQ, SEQ)
        at = pl.ds(base, SEQ)
        sides = (
            (q_own, k_own, v_own, ga_own, keep_out),
            (q_ref2, k_ref2, v_ref2, ga_ref2, send_out),
        )
        for side, (q_ref, k_ref, v_ref, g_ref, part_out) in enumerate(sides):
            queries, key_rows, values, grads = q_ref[at, :], k_ref[at, :], v_ref[at, :], g_ref[at, :]
            keys_t = key_rows.T
            dk[...] = jnp.zeros_like(dk)
            dv[...] = jnp.zeros_like(dv)
            for pair in range(pairs):
                low, high = windows[pair]
                both_q = split_heads(queries, pair, windows[pair])
                both_g = split_heads(grads, pair, windows[pair])
                probs_low = probs_all[m, side * pairs + pair]
                probs = probs_low.astype(F32)
                grad_probs = dot_nt(values[:, low:high], both_g)
                inner = row_sum(probs * grad_probs)
                grad_scores = (probs * (grad_probs - inner)).astype(BF16)
                dv[:, low:high] += dot(probs_low, both_g)
                dk[:, low:high] += dot(grad_scores, both_q)
                first = pair * 2 * HDIM
                out = dot(keys_t[first : first + 2 * HDIM], grad_scores)
                dq_t[first : first + HDIM, :] = out[:HDIM, :SEQ]
                dq_t[first + HDIM : first + 2 * HDIM, :] = out[HDIM:, SEQ:]
            part_out[at, :] = (dq_t[...] * SCALE).astype(BF16).T
            part_out[pl.ds(base + rows, SEQ), :] = (dk[...] * SCALE).astype(BF16)
            part_out[pl.ds(base + 2 * rows, SEQ), :] = dv[...].astype(BF16)
        return carry

    lax.fori_loop(0, mols, molecule, 0)


def embed_back_kernel(
    info, nodes, edges, grads_own, grads, wq_own, wk_own, wv_own, w_q, w_k, w_v, hidden, ident,
    grad_middle, vecs, features_out, keep_out, send_out, grad_normed, small,
):
    rows, dim = hidden.shape
    width = wq_own.shape[1]
    mols = rows // SEQ
    own_core = info[0]
    idw = ident.shape[0]
    total = None
    for part, weights in ((grads_own, (wq_own, wk_own, wv_own)), (grads, (w_q, w_k, w_v))):
        for place, weight in enumerate(weights):
            term = dot_nt(part[place * rows : (place + 1) * rows, :], weight[...])
            total = term if total is None else total + term
    grad_normed[...] = total
    small[...] = jnp.zeros_like(small)

    def molecule(m, carry):
        at = pl.ds(pl.multiple_of(m * SEQ, SEQ), SEQ)
        is_edge = positions(SEQ) >= nodes[own_core * mols + m]
        unit, inverse = norm_parts(hidden[at, :])
        grad_rows = grad_normed[at, :]
        grad = grad_middle[at, :] + norm_back(unit, inverse, grad_rows * vecs[2:3, :])
        features_out[at, :] = grad
        high = grad.astype(BF16)
        rest = (grad - high.astype(F32)).astype(BF16)
        picked = ident[:, at]
        small[:idw, :] += dot(picked, high) + dot(picked, rest)
        edge_rows = jnp.where(is_edge, grad, 0.0)
        small[idw : idw + 1, :] += row_sum(grad - edge_rows)
        small[idw + 1 : idw + 2, :] += row_sum(edge_rows)
        small[idw + 2 : idw + 3, :] += row_sum(grad_rows * unit)
        small[idw + 3 : idw + 4, :] += row_sum(grad_rows)
        return carry

    lax.fori_loop(0, mols, molecule, 0)
    left, right = small[:, :width], small[:, width:]
    keep_out[...] = jnp.where(own_core == 0, left, right).astype(BF16)
    send_out[...] = jnp.where(own_core == 0, right, left).astype(BF16)


def deal(info, unit, outs, block_at, small):
    inner, outer = info[1], info[2]
    first_kept, first_sent, second_kept, second_sent = outs
    for step in range(INNER):
        for turn in range(OUTER):
            if turn < 2:
                out, slot = (first_sent if step % 2 else first_kept), step // 2
            else:
                out, slot = (second_sent if step // 2 else second_kept), step % 2
            start = (slot * 2 + turn % 2) * 3 * unit
            for place in range(3):
                out[start + place * unit : start + (place + 1) * unit, :] = block_at(
                    inner ^ step, outer ^ turn, place
                )
    for out in (first_kept, first_sent):
        out[INNER * 3 * unit :, :] = small


def ffn_grads_kernel(info, nodes, edges, kept, got, cots, *rest):
    outs, (tall, flat, grad_ffn) = rest[:4], rest[4:]
    rows_all, dim = cots.shape
    rows, width = rows_all // 2, kept.shape[1]
    mols = rows // SEQ
    own_core = info[0]
    for m in range(2 * mols):
        keep = positions(SEQ) < nodes[m] + edges[m]
        at = slice(m * SEQ, (m + 1) * SEQ)
        grad_ffn[at, :] = jnp.where(keep, cots[at, :].astype(F32), 0.0).astype(BF16)
    own_rows = pl.ds(pl.multiple_of(own_core * rows, SEQ), rows)
    other_rows = pl.ds(pl.multiple_of((1 - own_core) * rows, SEQ), rows)
    place_b = dim + 2 * width
    place_m = place_b + rows
    place_s = place_m + 2 * rows
    back = slice(place_b, place_m)
    tall[...] = (dot(kept[:dim, :], kept[back, :]) + dot(got[:dim, :], got[back, :])).astype(BF16)
    turned = slice(dim, dim + width)
    for half in (0, 1):
        mid = slice(place_m + half * rows, place_m + (half + 1) * rows)
        flat[half] = (
            dot(kept[turned, :], kept[mid, :]) + dot(got[turned, :], got[mid, :])
        ).astype(BF16)
    turned = slice(dim + width, dim + 2 * width)
    for half in (0, 1):
        columns = slice(half * width, (half + 1) * width)
        product = dot(kept[turned, :], grad_ffn[own_rows, columns])
        product = product + dot(got[turned, :], grad_ffn[other_rows, columns])
        flat[2 + half] = product.astype(BF16)
    bias = row_sum(kept[back, :].astype(F32)) + row_sum(got[back, :].astype(F32))
    small = kept[place_s:, :].astype(F32) + got[place_s:, :].astype(F32)
    spot = lax.broadcasted_iota(jnp.int32, small.shape, 0)
    small = jnp.where(spot == 4, bias, small).astype(BF16)
    unit = dim // (INNER * OUTER)

    def block_at(dest, z, place):
        if place == 0:
            return tall[pl.ds(pl.multiple_of((dest * OUTER + z) * unit, 16), unit), :]
        row = pl.multiple_of((dest * (OUTER // 2) + z // 2) * unit, 16)
        return flat[2 * (place - 1) + z % 2, pl.ds(row, unit), :]

    deal(info, unit, outs, block_at, small)


def qkv_grads_kernel(info, normed_t, normed_t_got, kept, got, small_kept, small_got, *rest):
    outs, (tall,) = rest[:4], rest[4:]
    dim, rows = normed_t.shape
    unit = dim // (INNER * OUTER)
    small = small_kept[...].astype(F32) + small_got[...].astype(F32)
    spot = lax.broadcasted_iota(jnp.int32, small.shape, 0)
    for place in range(3):
        part = slice(place * rows, (place + 1) * rows)
        tall[place] = (
            dot(normed_t[...], kept[part, :]) + dot(normed_t_got[...], got[part, :])
        ).astype(BF16)
        if place != 1:
            bias = row_sum(kept[part, :].astype(F32)) + row_sum(got[part, :].astype(F32))
            small = jnp.where(spot == 36 + place // 2, bias, small)

    def block_at(dest, z, place):
        return tall[place, pl.ds(pl.multiple_of((dest * OUTER + z) * unit, 16), unit), :]

    deal(info, unit, outs, block_at, small.astype(BF16))


def place_kernel(split_second, info, own, side_x, side_y, far_first, far_second, *outs):
    inner, outer = info[1], info[2]
    unit = own.shape[0] // (3 * OUTER)
    width = own.shape[1]
    for step in range(INNER):
        for turn in range(OUTER):
            ref, start = (own, side_x, side_y, far_first)[step], turn * 3 * unit
            if step == 3 and turn >= 2:
                ref, start = far_second, (turn - 2) * 3 * unit
            dest, z = inner ^ step, outer ^ turn
            tall = pl.ds(pl.multiple_of((dest * OUTER + z) * unit, 16), unit)
            flat = pl.ds(pl.multiple_of((dest * (OUTER // 2) + z // 2) * unit, 16), unit)
            columns = pl.ds(pl.multiple_of(z % 2 * width, LANES), width)
            for place in range(3):
                part = ref[start + place * unit : start + (place + 1) * unit, :].astype(F32)
                if split_second and place > 0:
                    outs[place][flat, columns] = part
                else:
                    outs[place][tall, :] = part


def per_device(
    features, lap_vectors, node_counts, edge_counts, endpoints, w_ident, type_table,
    gain_one, shift_one, w_query, w_key, w_value, bias_query, bias_value, w_out, bias_out,
    gain_two, shift_two, w_up, bias_up, w_down, bias_down, cotangent,
):
    dp_count = lax.axis_size("dp")
    dp_index = lax.axis_index("dp")
    mp_index = lax.axis_index("mp")
    block = INNER * OUTER
    rest_count = dp_count // block
    info = jnp.stack([mp_index, dp_index % INNER, dp_index // INNER % OUTER]).astype(jnp.int32)

    def swap(part):
        return lax.ppermute(part, "mp", [(0, 1), (1, 0)])

    def inner_move(part, step):
        return lax.ppermute(part, "dp", [(s, s ^ step) for s in range(dp_count)])

    def outer_move(part, step):
        return lax.ppermute(part, "dp", [(s, s ^ (step * INNER)) for s in range(dp_count)])

    rows_all, dim = features.shape
    rows = rows_all // 2
    mols = rows // SEQ
    width = w_query.shape[1]
    heads = width // HDIM
    lapk = lap_vectors.shape[1]
    idw = w_ident.shape[0]
    scalars = (info, node_counts, edge_counts)
    half_rows = lambda columns: pl.BlockSpec((rows, columns), lambda g, info, n, e: (info[0], 0))

    def gathered(rows_of):
        spot = lax.broadcasted_iota(jnp.int32, (len(rows_of), 1), 0)
        table = rows_of[-1][None]
        for place in range(len(rows_of) - 1):
            table = jnp.where(spot == place, rows_of[place][None], table)
        return table

    biases = gathered([bias_query, bias_value, bias_up])
    vecs = gathered(
        [
            type_table[0], type_table[1], gain_one, shift_one,
            bias_out, gain_two, shift_two, bias_down,
        ]
    ).astype(F32)

    wq_got, wk_got, wv_got = swap(w_query), swap(w_key), swap(w_value)
    biases_got = swap(biases)
    wo_got, wu_got, wd_got = swap(w_out), swap(w_up), swap(w_down)

    half_columns = lambda count: pl.BlockSpec((count, rows), lambda g, info, n, e: (0, info[0]))
    hidden, ident, normed, normed_t, q_own, k_own, v_own = call(
        embed_kernel,
        scalars,
        (features, lap_vectors.T, endpoints.T, w_ident, vecs, biases, w_query, w_key, w_value),
        [half_rows(dim), half_columns(lapk), half_columns(2)] + [whole()] * 6,
        [
            ((rows, dim), F32),
            ((idw, rows), BF16),
            ((rows, dim), BF16),
            ((dim, rows), BF16),
            ((rows, width), BF16),
            ((rows, width), BF16),
            ((rows, width), BF16),
        ],
        micros=6,
    )
    normed_t_got = swap(normed_t)
    sent_rows = dim + 2 * width + 3 * rows + 16
    (
        q_got, k_got, v_got, probs, kept_a, sent_a, middle, active, grad_middle, grad_branch,
    ) = call(
        forward_kernel,
        scalars,
        (
            hidden, normed, q_own, k_own, v_own, wq_got, wk_got, wv_got, biases, biases_got,
            w_out, wo_got, w_up, wu_got, w_down, wd_got, vecs, cotangent,
        ),
        [whole()] * 17 + [half_rows(dim)],
        [
            ((rows, width), BF16),
            ((rows, width), BF16),
            ((rows, width), BF16),
            ((mols, heads, SEQ, 2 * SEQ), BF16),
            ((sent_rows, width), BF16),
            ((sent_rows, width), BF16),
            ((rows, dim), F32),
            ((rows, dim), BF16),
            ((rows, dim), F32),
            ((rows, dim), BF16),
        ],
        scratch=[
            pltpu.VMEM((width, SEQ), F32),
            pltpu.VMEM((rows, dim), BF16),
            pltpu.VMEM((rows, dim), F32),
            pltpu.VMEM((rows, dim), BF16),
            pltpu.VMEM((rows, dim), F32),
            pltpu.VMEM((rows, dim), BF16),
        ],
        micros=20,
        limit=44,
    )
    got_a = swap(sent_a)
    result, ga_own, ga_got = call(
        result_kernel,
        scalars,
        (middle, active, grad_branch, w_down, wd_got, w_out, wo_got, vecs),
        [whole()] * 8,
        [((rows, dim), BF16), ((rows, width), BF16), ((rows, width), BF16)],
        micros=4,
    )

    unit = dim // block
    chunk = 3 * unit
    small_a, small_b = 16, 48

    def rest_sum(part):
        if rest_count == 1:
            return part
        groups = [[r * block + s for r in range(rest_count)] for s in range(block)]
        return lax.psum(part.astype(F32), "dp", axis_index_groups=groups).astype(part.dtype)

    def added(*parts):
        return sum(part.astype(F32) for part in parts)

    def reduced(parts, small_rows):
        first_kept, first_sent, second_kept, second_sent = parts
        first = added(first_kept, inner_move(first_sent, 1)).astype(BF16)
        second = added(second_kept, inner_move(second_sent, 2)).astype(BF16)
        pair = 2 * chunk
        first = added(
            jnp.concatenate([first[:pair], first[2 * pair :]]), inner_move(first[pair:], 2)
        ).astype(BF16)
        second = added(second[:pair], inner_move(second[pair:], 1)).astype(BF16)
        small = first[pair:]
        lines = [first[chunk:], *(
            jnp.concatenate([second[turn * chunk : (turn + 1) * chunk], small]) for turn in (0, 1)
        )]
        got = [outer_move(lines[turn - 1], turn) for turn in range(1, OUTER)]
        mine = rest_sum(added(first[:chunk], *(part[:chunk] for part in got)).astype(BF16))
        small = rest_sum(added(small, *(part[chunk:] for part in got)))
        small_got = swap(small)
        line = jnp.concatenate([mine] + [outer_move(mine, turn) for turn in range(1, OUTER)])
        side_x, side_y = inner_move(line, 1), inner_move(line, 2)
        far_first, far_second = inner_move(side_y[:pair], 1), inner_move(side_x[pair:], 2)
        both = jnp.where(
            mp_index == 0,
            jnp.concatenate([small, small_got], axis=1),
            jnp.concatenate([small_got, small], axis=1),
        )
        return (line, side_x, side_y, far_first, far_second), small, both

    def placed(planes, split_second):
        tall, flat = ((dim, width), F32), ((width, dim), F32)
        return call(
            lambda *refs: place_kernel(split_second, *refs),
            (info,),
            planes,
            [whole()] * 5,
            [tall, flat, flat] if split_second else [tall] * 3,
            micros=3,
        )

    kept_a, result, ga_own = lax.optimization_barrier((kept_a, result, ga_own))
    parts_a = call(
        ffn_grads_kernel,
        scalars,
        (kept_a, got_a, cotangent),
        [whole()] * 3,
        [
            ((INNER * chunk + small_a, width), BF16),
            ((INNER * chunk + small_a, width), BF16),
            ((INNER * chunk, width), BF16),
            ((INNER * chunk, width), BF16),
        ],
        scratch=[
            pltpu.VMEM((dim, width), BF16),
            pltpu.VMEM((4, width, width), BF16),
            pltpu.VMEM((rows_all, dim), BF16),
        ],
        micros=6,
    )
    planes_a, narrow_a, wide_a = reduced(parts_a, small_a)
    ga_own, ga_got, _ = lax.optimization_barrier((ga_own, ga_got, parts_a[0]))

    kept_b, sent_b = call(
        attend_back_kernel,
        scalars,
        (q_own, k_own, v_own, ga_own, q_got, k_got, v_got, ga_got, probs),
        [whole()] * 9,
        [((3 * rows, width), BF16)] * 2,
        scratch=[
            pltpu.VMEM((width, SEQ), F32),
            pltpu.VMEM((SEQ, width), F32),
            pltpu.VMEM((SEQ, width), F32),
        ],
        micros=12,
    )
    got_b = swap(sent_b)
    grad_features, small_kept, small_sent = call(
        embed_back_kernel,
        scalars,
        (
            kept_b, sent_b, w_query, w_key, w_value, wq_got, wk_got, wv_got, hidden, ident,
            grad_middle, vecs,
        ),
        [whole()] * 12,
        [((rows, dim), F32), ((small_b, width), BF16), ((small_b, width), BF16)],
        scratch=[pltpu.VMEM((rows, dim), F32), pltpu.VMEM((small_b, dim), F32)],
        micros=7,
    )
    small_got = swap(small_sent)
    parts_b = call(
        qkv_grads_kernel,
        (info,),
        (normed_t, normed_t_got, kept_b, got_b, small_kept, small_got),
        [whole()] * 6,
        [
            ((INNER * chunk + small_b, width), BF16),
            ((INNER * chunk + small_b, width), BF16),
            ((INNER * chunk, width), BF16),
            ((INNER * chunk, width), BF16),
        ],
        scratch=[pltpu.VMEM((3, dim, width), BF16)],
        micros=6,
    )
    planes_b, narrow_b, wide_b = reduced(parts_b, small_b)

    grad_w_up, grad_w_out, grad_w_down = placed(planes_a, True)
    grad_w_query, grad_w_key, grad_w_value = placed(planes_b, False)
    return (
        result,
        grad_features,
        wide_b[:idw],
        wide_b[idw : idw + 2],
        wide_b[idw + 2],
        wide_b[idw + 3],
        grad_w_query,
        grad_w_key,
        grad_w_value,
        narrow_b[idw + 4],
        narrow_b[idw + 5],
        grad_w_out,
        wide_a[0],
        wide_a[1],
        wide_a[2],
        grad_w_up,
        narrow_a[4],
        grad_w_down,
        wide_a[3],
    )


def solution(mesh):
    token, split = P("dp", None), P(("dp", "mp"), None)
    columns, lines, cut, copy = P(None, "mp"), P("mp", None), P("mp"), P()
    return jax.shard_map(
        per_device,
        mesh=mesh,
        in_specs=(
            token, token, P("dp"), P("dp"), token, copy, copy, copy, copy, columns, columns,
            columns, cut, cut, lines, copy, copy, copy, columns, cut, lines, copy, token,
        ),
        out_specs=(
            split, split, copy, copy, copy, copy, columns, columns, columns, cut, cut, lines,
            copy, copy, copy, columns, cut, lines, copy,
        ),
        check_vma=False,
    )
```

```python
import math

import jax
import jax.numpy as jnp
from jax import lax
from jax.experimental import pallas as pl
from jax.experimental.pallas import tpu as pltpu
from jax.sharding import PartitionSpec as P

HDIM = 24
SEQ = 128
LANES = 128
INNER = 4
OUTER = 4
EPSILON = 1e-05
SCALE = 1.0 / math.sqrt(HDIM)
F32, BF16 = jnp.float32, jnp.bfloat16
MIB = 1024 * 1024


def dot(left, right):
    return jnp.dot(left, right, preferred_element_type=F32)


def dot_nt(left, right):
    return lax.dot_general(left, right, (((1,), (1,)), ((), ())), preferred_element_type=F32)


def dot_tn(left, right):
    return lax.dot_general(left, right, (((0,), (0,)), ((), ())), preferred_element_type=F32)


def norm_parts(hidden):
    average = jnp.mean(hidden, axis=-1, keepdims=True)
    centred = hidden - average
    inverse = lax.rsqrt(jnp.mean(centred * centred, axis=-1, keepdims=True) + EPSILON)
    return centred * inverse, inverse


def norm_back(unit, inverse, grad_hat):
    return inverse * (
        grad_hat
        - jnp.mean(grad_hat, axis=-1, keepdims=True)
        - unit * jnp.mean(grad_hat * unit, axis=-1, keepdims=True)
    )


def row_sum(block):
    return jnp.sum(block, axis=0, keepdims=True)


def positions(length):
    return lax.broadcasted_iota(jnp.int32, (length, 1), 0)


def whole():
    return pl.BlockSpec(memory_space=pltpu.VMEM)


def outside():
    return pl.BlockSpec(memory_space=pltpu.HBM)


def node_count(info, m):
    return info[3 + m]


def slot_count(info, m):
    return info[3 + m] + info[3 + (info.shape[0] - 3) // 2 + m]


def call(kernel, scalars, args, specs, outs, scratch=(), micros=5, limit=24, local=True):
    return pl.pallas_call(
        kernel,
        out_shape=[jax.ShapeDtypeStruct(shape, kind) for shape, kind in outs],
        grid_spec=pltpu.PrefetchScalarGridSpec(
            num_scalar_prefetch=len(scalars),
            grid=(1,),
            in_specs=specs,
            out_specs=[whole() for _ in outs],
            scratch_shapes=list(scratch),
        ),
        compiler_params=pltpu.CompilerParams(vmem_limit_bytes=limit * MIB),
        cost_estimate=pl.CostEstimate(
            flops=1 if local else micros * 1_000_000_000,
            bytes_accessed=1 if local else 0,
            transcendentals=0,
        ),
    )(*scalars, *args)


def head_windows(width):
    windows = []
    for pair in range(width // (2 * HDIM)):
        low = pair * 2 * HDIM // LANES * LANES
        high = -(-(pair + 1) * 2 * HDIM // LANES) * LANES
        windows.append((low, high))
    return windows


def split_heads(block, pair, window):
    low, high = window
    part = block[:, low:high]
    column = low + lax.broadcasted_iota(jnp.int32, (16, high - low), 1)
    sides = []
    for head in (2 * pair, 2 * pair + 1):
        inside = (column >= head * HDIM) & (column < (head + 1) * HDIM)
        mask = jnp.where(inside, 1.0, 0.0).astype(BF16)
        sides.append(part * jnp.concatenate([mask] * (block.shape[0] // 16), axis=0))
    return jnp.concatenate(sides, axis=0)


def embed_kernel(
    info, feats_in, lap_in, ends_in, w_ident_in, vecs, wq_in, wk_in, wv_in,
    hidden_out, ident_out, normed_out, normed_t_out, q_out, k_out, v_out,
    feats, lap, ends, w_ident, w_q, w_k, w_v, sems,
):
    rows, dim = feats.shape
    width = w_q.shape[1]
    mols = rows // SEQ
    own_rows = pl.ds(pl.multiple_of(info[0] * rows, SEQ), rows)
    moves = (
        (ends_in.at[:, own_rows], ends),
        (lap_in.at[:, own_rows], lap),
        (w_ident_in, w_ident),
        (feats_in.at[own_rows, :], feats),
        (wq_in, w_q),
        (wk_in, w_k),
        (wv_in, w_v),
    )
    copies = [
        pltpu.make_async_copy(source, target, sems.at[place])
        for place, (source, target) in enumerate(moves)
    ]
    for copy in copies:
        copy.start()
    for copy in copies[:4]:
        copy.wait()

    def molecule(m, carry):
        at = pl.ds(pl.multiple_of(m * SEQ, SEQ), SEQ)
        count = node_count(info, info[0] * mols + m)
        table = lap[:, at]
        slot = lax.broadcasted_iota(jnp.int32, (SEQ, SEQ), 0)
        picked = []
        for end in (0, 1):
            pick = jnp.where(ends[end : end + 1, at] == slot, 1.0, 0.0).astype(BF16)
            picked.append(dot(table, pick))
        ident = jnp.concatenate(picked, axis=0).astype(BF16)
        ident_out[:, at] = ident
        hidden = feats[at, :].astype(F32) + dot_tn(ident, w_ident[...])
        hidden = hidden + jnp.where(positions(SEQ) >= count, vecs[1:2, :], vecs[0:1, :])
        hidden_out[at, :] = hidden
        unit, _ = norm_parts(hidden)
        normed = (unit * vecs[2:3, :] + vecs[3:4, :]).astype(BF16)
        normed_out[at, :] = normed
        normed_t_out[:, at] = normed.T
        return carry

    lax.fori_loop(0, mols, molecule, 0)
    normed = normed_out[...]
    copies[4].wait()
    q_out[...] = (dot(normed, w_q[...]) + vecs[8:9, :width]).astype(BF16)
    copies[5].wait()
    k_out[...] = dot(normed, w_k[...]).astype(BF16)
    copies[6].wait()
    v_out[...] = (dot(normed, w_v[...]) + vecs[9:10, :width]).astype(BF16)


def forward_kernel(
    info, hidden, normed, q_own, k_own, v_own, w_q, w_k, w_v,
    wo_own, wo, wu_own, wu, wd_own, wd, vecs, vecs_got, cots,
    q_out, k_out, v_out, probs_out, keep_out, send_out, middle, active, gm_out, grad_branch,
    mixed, attended, unit, normed_two, slope, grad_ffn,
):
    rows, dim = hidden.shape
    width = q_own.shape[1]
    mols = rows // SEQ
    pairs = width // (2 * HDIM)
    windows = head_windows(width)
    own_core = info[0]

    q_out[...] = (dot(normed[...], w_q[...]) + vecs_got[8:9, :width]).astype(BF16)
    k_out[...] = dot(normed[...], w_k[...]).astype(BF16)
    v_out[...] = (dot(normed[...], w_v[...]) + vecs_got[9:10, :width]).astype(BF16)

    def attend(m, carry):
        at = pl.ds(pl.multiple_of(m * SEQ, SEQ), SEQ)
        place = own_core * mols + m
        count = slot_count(info, place)
        key_keep = positions(SEQ) < count
        query_keep = lax.broadcasted_iota(jnp.int32, (1, SEQ), 1) < count
        sides = ((q_own, k_own, v_own, keep_out), (q_out, k_out, v_out, send_out))
        for side, (q_ref, k_ref, v_ref, part_out) in enumerate(sides):
            queries, key_rows = q_ref[at, :], k_ref[at, :]
            values_t = v_ref[at, :].T
            for pair in range(pairs):
                low, high = windows[pair]
                both = split_heads(queries, pair, windows[pair])
                scores = dot_nt(key_rows[:, low:high], both) * SCALE
                scores = jnp.where(key_keep, scores, -1e30)
                top = jnp.max(scores, axis=0, keepdims=True)
                raised = jnp.exp(scores - top)
                total = row_sum(raised)
                probs = (raised * (1.0 / total)).astype(BF16)
                probs_out[m, side * pairs + pair] = probs
                first = pair * 2 * HDIM
                out = dot(values_t[first : first + 2 * HDIM], probs)
                mixed[first : first + HDIM, :] = out[:HDIM, :SEQ]
                mixed[first + HDIM : first + 2 * HDIM, :] = out[HDIM:, SEQ:]
            kept = jnp.where(query_keep, mixed[...], 0.0).astype(BF16)
            part_out[dim : dim + width, at] = kept
            attended[at, side * width : (side + 1) * width] = kept.T
        return carry

    lax.fori_loop(0, mols, attend, 0)
    middle[...] = (
        hidden[...] + dot(attended[:, :width], wo_own[...]) + dot(attended[:, width:], wo[...])
    )

    def second_norm(m, carry):
        at = pl.ds(pl.multiple_of(m * SEQ, SEQ), SEQ)
        place = own_core * mols + m
        keep = positions(SEQ) < slot_count(info, place)
        total = middle[at, :] + vecs[4:5, :]
        middle[at, :] = total
        unit_rows, _ = norm_parts(total)
        unit[at, :] = unit_rows
        rows_two = (unit_rows * vecs[5:6, :] + vecs[6:7, :]).astype(BF16)
        normed_two[at, :] = rows_two
        turned = rows_two.T
        keep_out[:dim, at] = turned
        send_out[:dim, at] = turned
        grad_ffn[at, :] = jnp.where(keep, cots[at, :].astype(F32), 0.0).astype(BF16)
        return carry

    lax.fori_loop(0, mols, second_norm, 0)

    for side, (w_ref, b_ref, part_out) in enumerate(
        ((wu_own, vecs, keep_out), (wu, vecs_got, send_out))
    ):
        columns = slice(side * width, (side + 1) * width)
        slope[:, columns] = dot(normed_two[...], w_ref[...]) + b_ref[10:11, :width]

        def activate(m, carry):
            at = pl.ds(pl.multiple_of(m * SEQ, SEQ), SEQ)
            before = slope[at, columns]
            phi = 0.5 * (1.0 + lax.erf(before * math.sqrt(0.5)))
            out = (before * phi).astype(BF16)
            slope[at, columns] = phi + before * jnp.exp(before * before * -0.5) * (
                1.0 / math.sqrt(2.0 * math.pi)
            )
            active[at, columns] = out
            part_out[dim + width : dim + 2 * width, at] = out.T
            return carry

        lax.fori_loop(0, mols, activate, 0)

    place_b = dim + 2 * width
    for side, (w_ref, part_out) in enumerate(((wd_own, keep_out), (wd, send_out))):
        columns = slice(side * width, (side + 1) * width)
        grad_before = slope[:, columns] * dot_nt(grad_ffn[...], w_ref[...])
        part_out[place_b : place_b + rows, :] = grad_before.astype(BF16)

    back = pl.ds(place_b, rows)
    gm_out[...] = dot_nt(keep_out[back, :], wu_own[...]) + dot_nt(send_out[back, :], wu[...])

    def second_back(m, sums):
        at = pl.ds(pl.multiple_of(m * SEQ, SEQ), SEQ)
        place = own_core * mols + m
        keep = positions(SEQ) < slot_count(info, place)
        grad_normed = gm_out[at, :]
        unit_rows = unit[at, :]
        _, inverse = norm_parts(middle[at, :])
        grad_result = jnp.where(keep, cots[at, :].astype(F32), 0.0)
        grad = grad_result + norm_back(unit_rows, inverse, grad_normed * vecs[5:6, :])
        gm_out[at, :] = grad
        grad_branch[at, :] = grad.astype(BF16)
        return (
            sums[0] + row_sum(grad),
            sums[1] + row_sum(grad_normed * unit_rows),
            sums[2] + row_sum(grad_normed),
            sums[3] + row_sum(grad_result),
        )

    nothing = jnp.zeros((1, dim), F32)
    sums = lax.fori_loop(0, mols, second_back, (nothing,) * 4)
    place_m = place_b + rows
    for part_out in (keep_out, send_out):
        part_out[place_m : place_m + rows, :] = grad_branch[:, :width]
        part_out[place_m + rows : place_m + 2 * rows, :] = grad_branch[:, width:]
    small = jnp.concatenate(list(sums) + [nothing] * 12, axis=0)
    left, right = small[:, :width], small[:, width:]
    place_s = place_m + 2 * rows
    keep_out[place_s:, :] = jnp.where(own_core == 0, left, right).astype(BF16)
    send_out[place_s:, :] = jnp.where(own_core == 0, right, left).astype(BF16)


def result_kernel(
    info, middle, active, grad_branch, wd_own, wd, wo_own, wo, vecs,
    result_out, ga_own_out, ga_out,
):
    rows = middle.shape[0]
    width = wd.shape[0]
    mols = rows // SEQ
    result_out[...] = (
        middle[...]
        + dot(active[:, :width], wd_own[...])
        + dot(active[:, width:], wd[...])
        + vecs[7:8, :]
    ).astype(BF16)
    for ref, weight in ((ga_own_out, wo_own), (ga_out, wo)):
        product = dot_nt(grad_branch[...], weight[...])
        for m in range(mols):
            place = info[0] * mols + m
            keep = positions(SEQ) < slot_count(info, place)
            at = slice(m * SEQ, (m + 1) * SEQ)
            ref[at, :] = jnp.where(keep, product[at], 0.0).astype(BF16)


def attend_back_kernel(
    m, info, q_own, k_own, v_own, ga_own, q_got, k_got, v_got, ga_got, probs_all,
    keep_out, send_out, dq_t, dk, dv,
):
    width = q_own.shape[1]
    pairs = width // (2 * HDIM)
    windows = head_windows(width)
    at = slice(m * SEQ, (m + 1) * SEQ)
    sides = (
        (q_own, k_own, v_own, ga_own, keep_out),
        (q_got, k_got, v_got, ga_got, send_out),
    )
    for side, (q_ref, k_ref, v_ref, g_ref, part_out) in enumerate(sides):
        queries, key_rows, values, grads = q_ref[at, :], k_ref[at, :], v_ref[at, :], g_ref[at, :]
        keys_t = key_rows.T
        dk[side] = jnp.zeros_like(dk[side])
        dv[side] = jnp.zeros_like(dv[side])
        for pair in range(pairs):
            low, high = windows[pair]
            both_q = split_heads(queries, pair, windows[pair])
            both_g = split_heads(grads, pair, windows[pair])
            probs_low = probs_all[m, side * pairs + pair]
            probs = probs_low.astype(F32)
            grad_probs = dot_nt(values[:, low:high], both_g)
            inner = row_sum(probs * grad_probs)
            grad_scores = (probs * (grad_probs - inner)).astype(BF16)
            dv[side, :, low:high] += dot(probs_low, both_g)
            dk[side, :, low:high] += dot(grad_scores, both_q)
            first = pair * 2 * HDIM
            out = dot(keys_t[first : first + 2 * HDIM], grad_scores)
            dq_t[side, first : first + HDIM, :] = out[:HDIM, :SEQ]
            dq_t[side, first + HDIM : first + 2 * HDIM, :] = out[HDIM:, SEQ:]
        part_out[:SEQ, :] = (dq_t[side] * SCALE).astype(BF16).T
        part_out[SEQ : 2 * SEQ, :] = (dk[side] * SCALE).astype(BF16)
        part_out[2 * SEQ :, :] = dv[side].astype(BF16)


def embed_back_kernel(
    info, *refs,
):
    mols = len(refs[:-16]) // 2
    grads_own, grads = refs[:mols], refs[mols : 2 * mols]
    (
        wq_own, wk_own, wv_own, w_q, w_k, w_v, hidden, ident, grad_middle, vecs,
        features_out, keep_out, send_out, grad_normed, small, stacked,
    ) = refs[2 * mols :]
    rows, dim = hidden.shape
    width = wq_own.shape[1]
    own_core = info[0]
    idw = ident.shape[0]
    total = None
    for part, weights in ((grads_own, (wq_own, wk_own, wv_own)), (grads, (w_q, w_k, w_v))):
        for place, weight in enumerate(weights):
            for m in range(mols):
                stacked[m * SEQ : (m + 1) * SEQ, :] = part[m][place * SEQ : (place + 1) * SEQ, :]
            term = dot_nt(stacked[...], weight[...])
            total = term if total is None else total + term
    grad_normed[...] = total
    small[...] = jnp.zeros_like(small)

    def molecule(m, carry):
        at = pl.ds(pl.multiple_of(m * SEQ, SEQ), SEQ)
        is_edge = positions(SEQ) >= node_count(info, own_core * mols + m)
        unit, inverse = norm_parts(hidden[at, :])
        grad_rows = grad_normed[at, :]
        grad = grad_middle[at, :] + norm_back(unit, inverse, grad_rows * vecs[2:3, :])
        features_out[at, :] = grad
        high = grad.astype(BF16)
        rest = (grad - high.astype(F32)).astype(BF16)
        picked = ident[:, at]
        small[:idw, :] += dot(picked, high) + dot(picked, rest)
        edge_rows = jnp.where(is_edge, grad, 0.0)
        small[idw : idw + 1, :] += row_sum(grad - edge_rows)
        small[idw + 1 : idw + 2, :] += row_sum(edge_rows)
        small[idw + 2 : idw + 3, :] += row_sum(grad_rows * unit)
        small[idw + 3 : idw + 4, :] += row_sum(grad_rows)
        return carry

    lax.fori_loop(0, mols, molecule, 0)
    left, right = small[:, :width], small[:, width:]
    keep_out[...] = jnp.where(own_core == 0, left, right)
    send_out[...] = jnp.where(own_core == 0, right, left).astype(BF16)


def deal(info, unit, outs, block_at, small):
    inner, outer = info[1], info[2]
    first_kept, first_sent, second_kept, second_sent = outs
    for step in range(INNER):
        for turn in range(OUTER):
            if turn < 2:
                out, slot = (first_sent if step % 2 else first_kept), step // 2
            else:
                out, slot = (second_sent if step // 2 else second_kept), step % 2
            start = (slot * 2 + turn % 2) * 3 * unit
            for place in range(3):
                out[start + place * unit : start + (place + 1) * unit, :] = block_at(
                    inner ^ step, outer ^ turn, place
                )
    if small is not None:
        for out in (first_kept, first_sent):
            out[INNER * 3 * unit :, :] = small


def ffn_grads_kernel(info, kept, got, cots, *rest):
    outs, (tall, flat, grad_ffn) = rest[:4], rest[4:]
    rows_all, dim = cots.shape
    rows, width = rows_all // 2, kept.shape[1]
    mols = rows // SEQ
    own_core = info[0]
    for m in range(2 * mols):
        keep = positions(SEQ) < slot_count(info, m)
        at = slice(m * SEQ, (m + 1) * SEQ)
        grad_ffn[at, :] = jnp.where(keep, cots[at, :].astype(F32), 0.0).astype(BF16)
    own_rows = pl.ds(pl.multiple_of(own_core * rows, SEQ), rows)
    other_rows = pl.ds(pl.multiple_of((1 - own_core) * rows, SEQ), rows)
    place_b = dim + 2 * width
    place_m = place_b + rows
    place_s = place_m + 2 * rows
    back = slice(place_b, place_m)
    tall[...] = (dot(kept[:dim, :], kept[back, :]) + dot(got[:dim, :], got[back, :])).astype(BF16)
    turned = slice(dim, dim + width)
    for half in (0, 1):
        mid = slice(place_m + half * rows, place_m + (half + 1) * rows)
        flat[half] = (
            dot(kept[turned, :], kept[mid, :]) + dot(got[turned, :], got[mid, :])
        ).astype(BF16)
    turned = slice(dim + width, dim + 2 * width)
    for half in (0, 1):
        columns = slice(half * width, (half + 1) * width)
        product = dot(kept[turned, :], grad_ffn[own_rows, columns])
        product = product + dot(got[turned, :], grad_ffn[other_rows, columns])
        flat[2 + half] = product.astype(BF16)
    bias = row_sum(kept[back, :].astype(F32)) + row_sum(got[back, :].astype(F32))
    small = kept[place_s:, :].astype(F32) + got[place_s:, :].astype(F32)
    spot = lax.broadcasted_iota(jnp.int32, small.shape, 0)
    small = jnp.where(spot == 4, bias, small).astype(BF16)
    unit = dim // (INNER * OUTER)

    def block_at(dest, z, place):
        if place == 0:
            return tall[pl.ds(pl.multiple_of((dest * OUTER + z) * unit, 16), unit), :]
        row = pl.multiple_of((dest * (OUTER // 2) + z // 2) * unit, 16)
        return flat[2 * (place - 1) + z % 2, pl.ds(row, unit), :]

    deal(info, unit, outs, block_at, small)


def qkv_grads_kernel(info, normed_t, normed_t_got, *refs):
    mols = normed_t.shape[1] // SEQ
    kept, got = refs[:mols], refs[mols : 2 * mols]
    outs, small_out = refs[2 * mols : 2 * mols + 4], refs[2 * mols + 4]
    tall, normed, stacked = refs[2 * mols + 5 :]
    dim, rows = normed_t.shape
    unit = dim // (INNER * OUTER)
    normed[:, :rows] = normed_t[...]
    normed[:, rows:] = normed_t_got[...]
    spot = lax.broadcasted_iota(jnp.int32, small_out.shape, 0)
    small = jnp.zeros(small_out.shape, F32)
    for place in range(3):
        for m, part in enumerate(kept + got):
            stacked[m * SEQ : (m + 1) * SEQ, :] = part[place * SEQ : (place + 1) * SEQ, :]
        tall[place] = dot(normed[...], stacked[...]).astype(BF16)
        if place != 1:
            small = jnp.where(spot == 36 + place // 2, row_sum(stacked[...].astype(F32)), small)
    small_out[...] = small

    def block_at(dest, z, place):
        return tall[place, pl.ds(pl.multiple_of((dest * OUTER + z) * unit, 16), unit), :]

    deal(info, unit, outs, block_at, None)


def place_kernel(split_second, info, own, side_x, side_y, far_first, far_second, *outs):
    inner, outer = info[1], info[2]
    unit = own.shape[0] // (3 * OUTER)
    width = own.shape[1]
    for step in range(INNER):
        for turn in range(OUTER):
            ref, start = (own, side_x, side_y, far_first)[step], turn * 3 * unit
            if step == 3 and turn >= 2:
                ref, start = far_second, (turn - 2) * 3 * unit
            dest, z = inner ^ step, outer ^ turn
            tall = pl.ds(pl.multiple_of((dest * OUTER + z) * unit, 16), unit)
            flat = pl.ds(pl.multiple_of((dest * (OUTER // 2) + z // 2) * unit, 16), unit)
            columns = pl.ds(pl.multiple_of(z % 2 * width, LANES), width)
            for place in range(3):
                part = ref[start + place * unit : start + (place + 1) * unit, :].astype(F32)
                if split_second and place > 0:
                    outs[place][flat, columns] = part
                else:
                    outs[place][tall, :] = part


def per_device(
    features, lap_vectors, node_counts, edge_counts, endpoints, w_ident, type_table,
    gain_one, shift_one, w_query, w_key, w_value, bias_query, bias_value, w_out, bias_out,
    gain_two, shift_two, w_up, bias_up, w_down, bias_down, cotangent,
):
    dp_count = lax.axis_size("dp")
    dp_index = lax.axis_index("dp")
    mp_index = lax.axis_index("mp")
    block = INNER * OUTER
    rest_count = dp_count // block
    place = jnp.stack([mp_index, dp_index % INNER, dp_index // INNER % OUTER]).astype(jnp.int32)
    info = jnp.concatenate([place, node_counts, edge_counts])

    def swap(part):
        return lax.ppermute(part, "mp", [(0, 1), (1, 0)])

    def inner_move(part, step):
        return lax.ppermute(part, "dp", [(s, s ^ step) for s in range(dp_count)])

    def outer_move(part, step):
        return lax.ppermute(part, "dp", [(s, s ^ (step * INNER)) for s in range(dp_count)])

    rows_all, dim = features.shape
    rows = rows_all // 2
    mols = rows // SEQ
    width = w_query.shape[1]
    heads = width // HDIM
    lapk = lap_vectors.shape[1]
    idw = w_ident.shape[0]
    scalars = (info,)
    half_rows = lambda columns: pl.BlockSpec((rows, columns), lambda g, info: (info[0], 0))

    rows_of = [
        None, None, gain_one, shift_one, bias_out, gain_two, shift_two, bias_down,
        bias_query, bias_value, bias_up,
    ]
    spot = lax.broadcasted_iota(jnp.int32, (16, 1), 0)
    vecs = jnp.pad(type_table, ((0, 14), (0, 0)))
    for place, row in enumerate(rows_of):
        if row is not None:
            vecs = jnp.where(spot == place, jnp.pad(row, (0, dim - row.shape[0]))[None], vecs)
    vecs = vecs.astype(F32)

    wq_got, wk_got, wv_got = swap(w_query), swap(w_key), swap(w_value)
    vecs_got = swap(vecs)
    wo_got, wu_got, wd_got = swap(w_out), swap(w_up), swap(w_down)

    hidden, ident, normed, normed_t, q_own, k_own, v_own = call(
        embed_kernel,
        scalars,
        (
            pltpu.with_memory_space_constraint(features, pltpu.HBM),
            pltpu.with_memory_space_constraint(lap_vectors.T, pltpu.HBM),
            pltpu.with_memory_space_constraint(endpoints.T, pltpu.HBM),
            pltpu.with_memory_space_constraint(w_ident, pltpu.HBM),
            vecs,
            *(pltpu.with_memory_space_constraint(w, pltpu.HBM) for w in (w_query, w_key, w_value)),
        ),
        [outside()] * 4 + [whole()] + [outside()] * 3,
        [
            ((rows, dim), F32),
            ((idw, rows), BF16),
            ((rows, dim), BF16),
            ((dim, rows), BF16),
            ((rows, width), BF16),
            ((rows, width), BF16),
            ((rows, width), BF16),
        ],
        scratch=[
            pltpu.VMEM((rows, dim), BF16),
            pltpu.VMEM((lapk, rows), BF16),
            pltpu.VMEM((2, rows), jnp.int32),
            pltpu.VMEM((idw, dim), BF16),
            pltpu.VMEM((dim, width), BF16),
            pltpu.VMEM((dim, width), BF16),
            pltpu.VMEM((dim, width), BF16),
            pltpu.SemaphoreType.DMA((7,)),
        ],
        micros=6,
        local=False,
    )
    normed_t_got = swap(normed_t)
    sent_rows = dim + 2 * width + 3 * rows + 16
    (
        q_got, k_got, v_got, probs, kept_a, sent_a, middle, active, grad_middle, grad_branch,
    ) = call(
        forward_kernel,
        scalars,
        (
            hidden, normed, q_own, k_own, v_own, wq_got, wk_got, wv_got,
            w_out, wo_got, w_up, wu_got, w_down, wd_got, vecs, vecs_got, cotangent,
        ),
        [whole()] * 16 + [half_rows(dim)],
        [
            ((rows, width), BF16),
            ((rows, width), BF16),
            ((rows, width), BF16),
            ((mols, heads, SEQ, 2 * SEQ), BF16),
            ((sent_rows, width), BF16),
            ((sent_rows, width), BF16),
            ((rows, dim), F32),
            ((rows, dim), BF16),
            ((rows, dim), F32),
            ((rows, dim), BF16),
        ],
        scratch=[
            pltpu.VMEM((width, SEQ), F32),
            pltpu.VMEM((rows, dim), BF16),
            pltpu.VMEM((rows, dim), F32),
            pltpu.VMEM((rows, dim), BF16),
            pltpu.VMEM((rows, dim), F32),
            pltpu.VMEM((rows, dim), BF16),
        ],
        micros=20,
        limit=44,
    )
    got_a = swap(sent_a)
    result, ga_own, ga_got = call(
        result_kernel,
        scalars,
        (middle, active, grad_branch, w_down, wd_got, w_out, wo_got, vecs),
        [whole()] * 8,
        [((rows, dim), BF16), ((rows, width), BF16), ((rows, width), BF16)],
        micros=4,
    )

    unit = dim // block
    chunk = 3 * unit
    small_a, small_b = 16, 48

    def rest_sum(part):
        if rest_count == 1:
            return part
        groups = [[r * block + s for r in range(rest_count)] for s in range(block)]
        return lax.psum(part.astype(F32), "dp", axis_index_groups=groups).astype(part.dtype)

    def added(*parts):
        return sum(part.astype(F32) for part in parts)

    pair = 2 * chunk

    def after(part, *others):
        return lax.optimization_barrier((part, *others))[0]

    def plane_step(parts):
        first_kept, first_sent, second_kept, second_sent = parts
        first = added(first_kept, inner_move(first_sent, 1)).astype(BF16)
        second = added(second_kept, inner_move(second_sent, 2)).astype(BF16)
        return first, second

    def plane_turn(first, second, small):
        sent = jnp.concatenate([first[pair : 2 * pair], small])
        first = added(jnp.concatenate([first[:pair], small]), inner_move(sent, 2)).astype(BF16)
        second = added(second[:pair], inner_move(second[pair : 2 * pair], 1)).astype(BF16)
        return first, second

    def line_step(first, second):
        small = first[pair:]
        lines = [first[chunk:], *(
            jnp.concatenate([second[turn * chunk : (turn + 1) * chunk], small]) for turn in (0, 1)
        )]
        got = [outer_move(lines[turn - 1], turn) for turn in range(1, OUTER)]
        mine = rest_sum(added(first[:chunk], *(part[:chunk] for part in got)).astype(BF16))
        small = rest_sum(added(small, *(part[chunk:] for part in got)))
        return mine, small

    def line_back(mine):
        return jnp.concatenate([mine] + [outer_move(mine, turn) for turn in range(1, OUTER)])

    def plane_back(line, small=None):
        if small is None:
            side_x = inner_move(line, 1)
        else:
            side_x = inner_move(jnp.concatenate([line, small.astype(BF16)]), 1)
            small = added(small.astype(BF16), side_x[2 * pair :])
            side_x = side_x[: 2 * pair]
        return side_x, inner_move(line, 2), small

    def plane_back_turn(side_x, side_y):
        return inner_move(side_y[:pair], 1), inner_move(side_x[pair:], 2)

    def widened(small):
        small_got = swap(small)
        return jnp.where(
            mp_index == 0,
            jnp.concatenate([small, small_got], axis=1),
            jnp.concatenate([small_got, small], axis=1),
        )

    def placed(planes, split_second):
        tall, flat = ((dim, width), F32), ((width, dim), F32)
        return call(
            lambda *refs: place_kernel(split_second, *refs),
            (info,),
            planes,
            [whole()] * 5,
            [tall, flat, flat] if split_second else [tall] * 3,
            micros=3,
        )

    kept_a, result, ga_own = lax.optimization_barrier((kept_a, result, ga_own))
    parts_a = call(
        ffn_grads_kernel,
        scalars,
        (kept_a, got_a, cotangent),
        [whole()] * 3,
        [
            ((INNER * chunk + small_a, width), BF16),
            ((INNER * chunk + small_a, width), BF16),
            ((INNER * chunk, width), BF16),
            ((INNER * chunk, width), BF16),
        ],
        scratch=[
            pltpu.VMEM((dim, width), BF16),
            pltpu.VMEM((4, width, width), BF16),
            pltpu.VMEM((rows_all, dim), BF16),
        ],
        micros=6,
    )
    q_own = after(q_own, parts_a[0])
    steps_a = plane_step(parts_a)
    kept_b, got_b, sent_b = [], [], []
    for m in range(mols):
        if m == 2:
            q_own, steps_a = lax.optimization_barrier((q_own, steps_a))
            turned_a = plane_turn(*steps_a, steps_a[0][2 * pair :])
        kept, sent = call(
            lambda *refs, m=m: attend_back_kernel(m, *refs),
            scalars,
            (q_own, k_own, v_own, ga_own, q_got, k_got, v_got, ga_got, probs),
            [whole()] * 9,
            [((3 * SEQ, width), BF16)] * 2,
            scratch=[
                pltpu.VMEM((2, width, SEQ), F32),
                pltpu.VMEM((2, SEQ, width), F32),
                pltpu.VMEM((2, SEQ, width), F32),
            ],
            micros=4,
        )
        kept_b.append(kept)
        sent_b.append(sent)
        got_b.append(swap(sent))
        q_own, q_got, _ = lax.optimization_barrier((q_own, q_got, kept))

    normed_t, turned_a = lax.optimization_barrier((normed_t, turned_a))
    mine_a, narrow_a = line_step(*turned_a)
    parts_b = call(
        qkv_grads_kernel,
        scalars,
        (normed_t, normed_t_got, *kept_b, *got_b),
        [whole()] * (2 + 2 * mols),
        [((INNER * chunk, width), BF16)] * 4 + [((small_b, width), F32)],
        scratch=[
            pltpu.VMEM((3, dim, width), BF16),
            pltpu.VMEM((dim, 2 * rows), BF16),
            pltpu.VMEM((2 * rows, width), BF16),
        ],
        micros=4,
    )
    steps_b = plane_step(parts_b[:4])
    hidden, mine_a = lax.optimization_barrier((after(hidden, parts_b[0]), mine_a))
    line_a = line_back(mine_a)
    wide_a = widened(narrow_a)
    grad_features, small_kept, small_sent = call(
        embed_back_kernel,
        scalars,
        (
            *kept_b, *sent_b, w_query, w_key, w_value, wq_got, wk_got, wv_got, hidden, ident,
            grad_middle, vecs,
        ),
        [whole()] * (10 + 2 * mols),
        [((rows, dim), F32), ((small_b, width), F32), ((small_b, width), BF16)],
        scratch=[
            pltpu.VMEM((rows, dim), F32),
            pltpu.VMEM((small_b, dim), F32),
            pltpu.VMEM((rows, width), BF16),
        ],
        micros=7,
        local=False,
    )
    small_got, steps_b = lax.optimization_barrier((swap(small_sent), steps_b))
    late = added(small_kept, small_got, parts_b[4]).astype(BF16)
    turned_b = plane_turn(*steps_b, late)
    turned_b, line_a = lax.optimization_barrier((turned_b, line_a))
    mine_b, small_b_sum = line_step(*turned_b)
    side_ax, side_ay, _ = plane_back(line_a)
    mine_b, side_ax, side_ay = lax.optimization_barrier((mine_b, side_ax, side_ay))
    line_b = line_back(mine_b)
    far_a = plane_back_turn(side_ax, side_ay)
    planes_a = (line_a, side_ax, side_ay, *far_a)
    line_b, far_a = lax.optimization_barrier((line_b, far_a))
    side_bx, side_by, narrow_b = plane_back(line_b, small_b_sum)
    far_b = plane_back_turn(side_bx, side_by)
    wide_b = widened(narrow_b)
    planes_b = (line_b, side_bx, side_by, *far_b)

    grad_w_up, grad_w_out, grad_w_down = placed(planes_a, True)
    grad_w_query, grad_w_key, grad_w_value = placed(planes_b, False)
    return (
        result,
        grad_features,
        wide_b[:idw],
        wide_b[idw : idw + 2],
        wide_b[idw + 2],
        wide_b[idw + 3],
        grad_w_query,
        grad_w_key,
        grad_w_value,
        narrow_b[idw + 4],
        narrow_b[idw + 5],
        grad_w_out,
        wide_a[0],
        wide_a[1],
        wide_a[2],
        grad_w_up,
        narrow_a[4],
        grad_w_down,
        wide_a[3],
    )


def solution(mesh):
    token, split = P("dp", None), P(("dp", "mp"), None)
    columns, lines, cut, copy = P(None, "mp"), P("mp", None), P("mp"), P()
    return jax.shard_map(
        per_device,
        mesh=mesh,
        in_specs=(
            token, token, P("dp"), P("dp"), token, copy, copy, copy, copy, columns, columns,
            columns, cut, cut, lines, copy, copy, copy, columns, cut, lines, copy, token,
        ),
        out_specs=(
            split, split, copy, copy, copy, copy, columns, columns, columns, cut, cut, lines,
            copy, copy, copy, columns, cut, lines, copy,
        ),
        check_vma=False,
    )
```

```python
import math

import jax
import jax.numpy as jnp
from jax import lax
from jax.experimental import pallas as pl
from jax.experimental.pallas import tpu as pltpu
from jax.sharding import PartitionSpec as P

HDIM = 24
SEQ = 128
LANES = 128
INNER = 4
OUTER = 4
EPSILON = 1e-05
SCALE = 1.0 / math.sqrt(HDIM)
F32, BF16 = jnp.float32, jnp.bfloat16
MIB = 1024 * 1024


def dot(left, right):
    return jnp.dot(left, right, preferred_element_type=F32)


def dot_nt(left, right):
    return lax.dot_general(left, right, (((1,), (1,)), ((), ())), preferred_element_type=F32)


def dot_tn(left, right):
    return lax.dot_general(left, right, (((0,), (0,)), ((), ())), preferred_element_type=F32)


def norm_parts(hidden):
    average = jnp.mean(hidden, axis=-1, keepdims=True)
    centred = hidden - average
    inverse = lax.rsqrt(jnp.mean(centred * centred, axis=-1, keepdims=True) + EPSILON)
    return centred * inverse, inverse


def norm_back(unit, inverse, grad_hat):
    return inverse * (
        grad_hat
        - jnp.mean(grad_hat, axis=-1, keepdims=True)
        - unit * jnp.mean(grad_hat * unit, axis=-1, keepdims=True)
    )


def row_sum(block):
    return jnp.sum(block, axis=0, keepdims=True)


def positions(length):
    return lax.broadcasted_iota(jnp.int32, (length, 1), 0)


def whole():
    return pl.BlockSpec(memory_space=pltpu.VMEM)


def outside():
    return pl.BlockSpec(memory_space=pltpu.HBM)


def node_count(info, m):
    return info[3 + m]


def slot_count(info, m):
    return info[3 + m] + info[3 + (info.shape[0] - 3) // 2 + m]


def call(kernel, scalars, args, specs, outs, scratch=(), micros=5, limit=24, local=True):
    return pl.pallas_call(
        kernel,
        out_shape=[jax.ShapeDtypeStruct(shape, kind) for shape, kind in outs],
        grid_spec=pltpu.PrefetchScalarGridSpec(
            num_scalar_prefetch=len(scalars),
            grid=(1,),
            in_specs=specs,
            out_specs=[whole() for _ in outs],
            scratch_shapes=list(scratch),
        ),
        compiler_params=pltpu.CompilerParams(vmem_limit_bytes=limit * MIB),
        cost_estimate=pl.CostEstimate(
            flops=1 if local else micros * 1_000_000_000,
            bytes_accessed=1 if local else 0,
            transcendentals=0,
        ),
    )(*scalars, *args)


def head_windows(width):
    windows = []
    for pair in range(width // (2 * HDIM)):
        low = pair * 2 * HDIM // LANES * LANES
        high = -(-(pair + 1) * 2 * HDIM // LANES) * LANES
        windows.append((low, high))
    return windows


def split_heads(block, pair, window):
    low, high = window
    part = block[:, low:high]
    column = low + lax.broadcasted_iota(jnp.int32, (16, high - low), 1)
    sides = []
    for head in (2 * pair, 2 * pair + 1):
        inside = (column >= head * HDIM) & (column < (head + 1) * HDIM)
        mask = jnp.where(inside, 1.0, 0.0).astype(BF16)
        sides.append(part * jnp.concatenate([mask] * (block.shape[0] // 16), axis=0))
    return jnp.concatenate(sides, axis=0)


def embed_kernel(
    info, feats_in, lap_in, ends_in, w_ident_in, vecs_in, biases_in, wq_in, wk_in, wv_in,
    hidden_out, ident_out, normed_out, normed_t_out, q_out, k_out, v_out,
    feats, lap, ends, w_ident, vecs, biases, w_q, w_k, w_v, sems,
):
    rows, dim = feats.shape
    mols = rows // SEQ
    own_rows = pl.ds(pl.multiple_of(info[0] * rows, SEQ), rows)
    moves = (
        (ends_in.at[:, own_rows], ends),
        (lap_in.at[:, own_rows], lap),
        (w_ident_in, w_ident),
        (vecs_in, vecs),
        (feats_in.at[own_rows, :], feats),
        (biases_in, biases),
        (wq_in, w_q),
        (wk_in, w_k),
        (wv_in, w_v),
    )
    copies = [
        pltpu.make_async_copy(source, target, sems.at[place])
        for place, (source, target) in enumerate(moves)
    ]
    for copy in copies:
        copy.start()
    for copy in copies[:6]:
        copy.wait()

    def molecule(m, carry):
        at = pl.ds(pl.multiple_of(m * SEQ, SEQ), SEQ)
        count = node_count(info, info[0] * mols + m)
        table = lap[:, at]
        slot = lax.broadcasted_iota(jnp.int32, (SEQ, SEQ), 0)
        picked = []
        for end in (0, 1):
            pick = jnp.where(ends[end : end + 1, at] == slot, 1.0, 0.0).astype(BF16)
            picked.append(dot(table, pick))
        ident = jnp.concatenate(picked, axis=0).astype(BF16)
        ident_out[:, at] = ident
        hidden = feats[at, :].astype(F32) + dot_tn(ident, w_ident[...])
        hidden = hidden + jnp.where(positions(SEQ) >= count, vecs[1:2, :], vecs[0:1, :])
        hidden_out[at, :] = hidden
        unit, _ = norm_parts(hidden)
        normed = (unit * vecs[2:3, :] + vecs[3:4, :]).astype(BF16)
        normed_out[at, :] = normed
        normed_t_out[:, at] = normed.T
        return carry

    lax.fori_loop(0, mols, molecule, 0)
    normed = normed_out[...]
    copies[6].wait()
    q_out[...] = (dot(normed, w_q[...]) + biases[0:1, :]).astype(BF16)
    copies[7].wait()
    k_out[...] = dot(normed, w_k[...]).astype(BF16)
    copies[8].wait()
    v_out[...] = (dot(normed, w_v[...]) + biases[1:2, :]).astype(BF16)


def forward_kernel(
    info, hidden, normed, q_own, k_own, v_own, w_q, w_k, w_v,
    wo_own, wo, wu_own, wu, wd_own, wd, vecs, biases_own, biases, cots,
    q_out, k_out, v_out, probs_out, keep_out, send_out, middle, active, gm_out, grad_branch,
    mixed, attended, unit, normed_two, slope, grad_ffn,
):
    rows, dim = hidden.shape
    width = q_own.shape[1]
    mols = rows // SEQ
    pairs = width // (2 * HDIM)
    windows = head_windows(width)
    own_core = info[0]

    q_out[...] = (dot(normed[...], w_q[...]) + biases[0:1, :]).astype(BF16)
    k_out[...] = dot(normed[...], w_k[...]).astype(BF16)
    v_out[...] = (dot(normed[...], w_v[...]) + biases[1:2, :]).astype(BF16)

    def attend(m, carry):
        at = pl.ds(pl.multiple_of(m * SEQ, SEQ), SEQ)
        place = own_core * mols + m
        count = slot_count(info, place)
        key_keep = positions(SEQ) < count
        query_keep = lax.broadcasted_iota(jnp.int32, (1, SEQ), 1) < count
        sides = ((q_own, k_own, v_own, keep_out), (q_out, k_out, v_out, send_out))
        for side, (q_ref, k_ref, v_ref, part_out) in enumerate(sides):
            queries, key_rows = q_ref[at, :], k_ref[at, :]
            values_t = v_ref[at, :].T
            for pair in range(pairs):
                low, high = windows[pair]
                both = split_heads(queries, pair, windows[pair])
                scores = dot_nt(key_rows[:, low:high], both) * SCALE
                scores = jnp.where(key_keep, scores, -1e30)
                top = jnp.max(scores, axis=0, keepdims=True)
                raised = jnp.exp(scores - top)
                total = row_sum(raised)
                probs = (raised * (1.0 / total)).astype(BF16)
                probs_out[m, side * pairs + pair] = probs
                first = pair * 2 * HDIM
                out = dot(values_t[first : first + 2 * HDIM], probs)
                mixed[first : first + HDIM, :] = out[:HDIM, :SEQ]
                mixed[first + HDIM : first + 2 * HDIM, :] = out[HDIM:, SEQ:]
            kept = jnp.where(query_keep, mixed[...], 0.0).astype(BF16)
            part_out[dim : dim + width, at] = kept
            attended[at, side * width : (side + 1) * width] = kept.T
        return carry

    lax.fori_loop(0, mols, attend, 0)
    middle[...] = (
        hidden[...] + dot(attended[:, :width], wo_own[...]) + dot(attended[:, width:], wo[...])
    )

    def second_norm(m, carry):
        at = pl.ds(pl.multiple_of(m * SEQ, SEQ), SEQ)
        place = own_core * mols + m
        keep = positions(SEQ) < slot_count(info, place)
        total = middle[at, :] + vecs[4:5, :]
        middle[at, :] = total
        unit_rows, _ = norm_parts(total)
        unit[at, :] = unit_rows
        rows_two = (unit_rows * vecs[5:6, :] + vecs[6:7, :]).astype(BF16)
        normed_two[at, :] = rows_two
        turned = rows_two.T
        keep_out[:dim, at] = turned
        send_out[:dim, at] = turned
        grad_ffn[at, :] = jnp.where(keep, cots[at, :].astype(F32), 0.0).astype(BF16)
        return carry

    lax.fori_loop(0, mols, second_norm, 0)

    for side, (w_ref, b_ref, part_out) in enumerate(
        ((wu_own, biases_own, keep_out), (wu, biases, send_out))
    ):
        columns = slice(side * width, (side + 1) * width)
        slope[:, columns] = dot(normed_two[...], w_ref[...]) + b_ref[2:3, :]

        def activate(m, carry):
            at = pl.ds(pl.multiple_of(m * SEQ, SEQ), SEQ)
            before = slope[at, columns]
            phi = 0.5 * (1.0 + lax.erf(before * math.sqrt(0.5)))
            out = (before * phi).astype(BF16)
            slope[at, columns] = phi + before * jnp.exp(before * before * -0.5) * (
                1.0 / math.sqrt(2.0 * math.pi)
            )
            active[at, columns] = out
            part_out[dim + width : dim + 2 * width, at] = out.T
            return carry

        lax.fori_loop(0, mols, activate, 0)

    place_b = dim + 2 * width
    for side, (w_ref, part_out) in enumerate(((wd_own, keep_out), (wd, send_out))):
        columns = slice(side * width, (side + 1) * width)
        grad_before = slope[:, columns] * dot_nt(grad_ffn[...], w_ref[...])
        part_out[place_b : place_b + rows, :] = grad_before.astype(BF16)

    back = pl.ds(place_b, rows)
    gm_out[...] = dot_nt(keep_out[back, :], wu_own[...]) + dot_nt(send_out[back, :], wu[...])

    def second_back(m, sums):
        at = pl.ds(pl.multiple_of(m * SEQ, SEQ), SEQ)
        place = own_core * mols + m
        keep = positions(SEQ) < slot_count(info, place)
        grad_normed = gm_out[at, :]
        unit_rows = unit[at, :]
        _, inverse = norm_parts(middle[at, :])
        grad_result = jnp.where(keep, cots[at, :].astype(F32), 0.0)
        grad = grad_result + norm_back(unit_rows, inverse, grad_normed * vecs[5:6, :])
        gm_out[at, :] = grad
        grad_branch[at, :] = grad.astype(BF16)
        return (
            sums[0] + row_sum(grad),
            sums[1] + row_sum(grad_normed * unit_rows),
            sums[2] + row_sum(grad_normed),
            sums[3] + row_sum(grad_result),
        )

    nothing = jnp.zeros((1, dim), F32)
    sums = lax.fori_loop(0, mols, second_back, (nothing,) * 4)
    place_m = place_b + rows
    for part_out in (keep_out, send_out):
        part_out[place_m : place_m + rows, :] = grad_branch[:, :width]
        part_out[place_m + rows : place_m + 2 * rows, :] = grad_branch[:, width:]
    small = jnp.concatenate(list(sums) + [nothing] * 12, axis=0)
    left, right = small[:, :width], small[:, width:]
    place_s = place_m + 2 * rows
    keep_out[place_s:, :] = jnp.where(own_core == 0, left, right).astype(BF16)
    send_out[place_s:, :] = jnp.where(own_core == 0, right, left).astype(BF16)


def result_kernel(
    info, middle, active, grad_branch, wd_own, wd, wo_own, wo, vecs,
    result_out, ga_own_out, ga_out,
):
    rows = middle.shape[0]
    width = wd.shape[0]
    mols = rows // SEQ
    result_out[...] = (
        middle[...]
        + dot(active[:, :width], wd_own[...])
        + dot(active[:, width:], wd[...])
        + vecs[7:8, :]
    ).astype(BF16)
    for ref, weight in ((ga_own_out, wo_own), (ga_out, wo)):
        product = dot_nt(grad_branch[...], weight[...])
        for m in range(mols):
            place = info[0] * mols + m
            keep = positions(SEQ) < slot_count(info, place)
            at = slice(m * SEQ, (m + 1) * SEQ)
            ref[at, :] = jnp.where(keep, product[at], 0.0).astype(BF16)


def attend_back_kernel(
    m, info, q_own, k_own, v_own, ga_own, q_got, k_got, v_got, ga_got, probs_all,
    keep_out, send_out, dq_t, dk, dv,
):
    width = q_own.shape[1]
    pairs = width // (2 * HDIM)
    windows = head_windows(width)
    at = slice(m * SEQ, (m + 1) * SEQ)
    sides = (
        (q_own, k_own, v_own, ga_own, keep_out),
        (q_got, k_got, v_got, ga_got, send_out),
    )
    for side, (q_ref, k_ref, v_ref, g_ref, part_out) in enumerate(sides):
        queries, key_rows, values, grads = q_ref[at, :], k_ref[at, :], v_ref[at, :], g_ref[at, :]
        keys_t = key_rows.T
        dk[side] = jnp.zeros_like(dk[side])
        dv[side] = jnp.zeros_like(dv[side])
        for pair in range(pairs):
            low, high = windows[pair]
            both_q = split_heads(queries, pair, windows[pair])
            both_g = split_heads(grads, pair, windows[pair])
            probs_low = probs_all[m, side * pairs + pair]
            probs = probs_low.astype(F32)
            grad_probs = dot_nt(values[:, low:high], both_g)
            inner = row_sum(probs * grad_probs)
            grad_scores = (probs * (grad_probs - inner)).astype(BF16)
            dv[side, :, low:high] += dot(probs_low, both_g)
            dk[side, :, low:high] += dot(grad_scores, both_q)
            first = pair * 2 * HDIM
            out = dot(keys_t[first : first + 2 * HDIM], grad_scores)
            dq_t[side, first : first + HDIM, :] = out[:HDIM, :SEQ]
            dq_t[side, first + HDIM : first + 2 * HDIM, :] = out[HDIM:, SEQ:]
        part_out[:SEQ, :] = (dq_t[side] * SCALE).astype(BF16).T
        part_out[SEQ : 2 * SEQ, :] = (dk[side] * SCALE).astype(BF16)
        part_out[2 * SEQ :, :] = dv[side].astype(BF16)


def embed_back_kernel(
    info, *refs,
):
    mols = len(refs[:-17]) // 2
    grads_own, grads = refs[:mols], refs[mols : 2 * mols]
    (
        wq_own, wk_own, wv_own, w_q, w_k, w_v, ident, w_ident, grad_middle, vecs, feats,
        features_out, keep_out, send_out, grad_normed, small, stacked,
    ) = refs[2 * mols :]
    rows, dim = feats.shape
    width = wq_own.shape[1]
    own_core = info[0]
    idw = ident.shape[0]
    total = None
    for part, weights in ((grads_own, (wq_own, wk_own, wv_own)), (grads, (w_q, w_k, w_v))):
        for place, weight in enumerate(weights):
            for m in range(mols):
                stacked[m * SEQ : (m + 1) * SEQ, :] = part[m][place * SEQ : (place + 1) * SEQ, :]
            term = dot_nt(stacked[...], weight[...])
            total = term if total is None else total + term
    grad_normed[...] = total
    small[...] = jnp.zeros_like(small)

    def molecule(m, carry):
        at = pl.ds(pl.multiple_of(m * SEQ, SEQ), SEQ)
        is_edge = positions(SEQ) >= node_count(info, own_core * mols + m)
        hidden = feats[at, :].astype(F32) + dot_tn(ident[:, at], w_ident[...])
        hidden = hidden + jnp.where(is_edge, vecs[1:2, :], vecs[0:1, :])
        unit, inverse = norm_parts(hidden)
        grad_rows = grad_normed[at, :]
        grad = grad_middle[at, :] + norm_back(unit, inverse, grad_rows * vecs[2:3, :])
        features_out[at, :] = grad
        high = grad.astype(BF16)
        rest = (grad - high.astype(F32)).astype(BF16)
        picked = ident[:, at]
        small[:idw, :] += dot(picked, high) + dot(picked, rest)
        edge_rows = jnp.where(is_edge, grad, 0.0)
        small[idw : idw + 1, :] += row_sum(grad - edge_rows)
        small[idw + 1 : idw + 2, :] += row_sum(edge_rows)
        small[idw + 2 : idw + 3, :] += row_sum(grad_rows * unit)
        small[idw + 3 : idw + 4, :] += row_sum(grad_rows)
        return carry

    lax.fori_loop(0, mols, molecule, 0)
    left, right = small[:, :width], small[:, width:]
    keep_out[...] = jnp.where(own_core == 0, left, right)
    send_out[...] = jnp.where(own_core == 0, right, left).astype(BF16)


def deal(info, unit, outs, block_at, small):
    inner, outer = info[1], info[2]
    first_kept, first_sent, second_kept, second_sent = outs
    for step in range(INNER):
        for turn in range(OUTER):
            if turn < 2:
                out, slot = (first_sent if step % 2 else first_kept), step // 2
            else:
                out, slot = (second_sent if step // 2 else second_kept), step % 2
            start = (slot * 2 + turn % 2) * 3 * unit
            for place in range(3):
                out[start + place * unit : start + (place + 1) * unit, :] = block_at(
                    inner ^ step, outer ^ turn, place
                )
    if small is not None:
        for out in (first_kept, first_sent):
            out[INNER * 3 * unit :, :] = small


def ffn_grads_kernel(info, kept, got, cots, *rest):
    outs, (tall, flat, grad_ffn) = rest[:4], rest[4:]
    rows_all, dim = cots.shape
    rows, width = rows_all // 2, kept.shape[1]
    mols = rows // SEQ
    own_core = info[0]
    for m in range(2 * mols):
        keep = positions(SEQ) < slot_count(info, m)
        at = slice(m * SEQ, (m + 1) * SEQ)
        grad_ffn[at, :] = jnp.where(keep, cots[at, :].astype(F32), 0.0).astype(BF16)
    own_rows = pl.ds(pl.multiple_of(own_core * rows, SEQ), rows)
    other_rows = pl.ds(pl.multiple_of((1 - own_core) * rows, SEQ), rows)
    place_b = dim + 2 * width
    place_m = place_b + rows
    place_s = place_m + 2 * rows
    back = slice(place_b, place_m)
    tall[...] = (dot(kept[:dim, :], kept[back, :]) + dot(got[:dim, :], got[back, :])).astype(BF16)
    turned = slice(dim, dim + width)
    for half in (0, 1):
        mid = slice(place_m + half * rows, place_m + (half + 1) * rows)
        flat[half] = (
            dot(kept[turned, :], kept[mid, :]) + dot(got[turned, :], got[mid, :])
        ).astype(BF16)
    turned = slice(dim + width, dim + 2 * width)
    for half in (0, 1):
        columns = slice(half * width, (half + 1) * width)
        product = dot(kept[turned, :], grad_ffn[own_rows, columns])
        product = product + dot(got[turned, :], grad_ffn[other_rows, columns])
        flat[2 + half] = product.astype(BF16)
    bias = row_sum(kept[back, :].astype(F32)) + row_sum(got[back, :].astype(F32))
    small = kept[place_s:, :].astype(F32) + got[place_s:, :].astype(F32)
    spot = lax.broadcasted_iota(jnp.int32, small.shape, 0)
    small = jnp.where(spot == 4, bias, small).astype(BF16)
    unit = dim // (INNER * OUTER)

    def block_at(dest, z, place):
        if place == 0:
            return tall[pl.ds(pl.multiple_of((dest * OUTER + z) * unit, 16), unit), :]
        row = pl.multiple_of((dest * (OUTER // 2) + z // 2) * unit, 16)
        return flat[2 * (place - 1) + z % 2, pl.ds(row, unit), :]

    deal(info, unit, outs, block_at, small)


def qkv_grads_kernel(info, normed_t, normed_t_got, *refs):
    mols = normed_t.shape[1] // SEQ
    kept, got = refs[:mols], refs[mols : 2 * mols]
    outs, small_out = refs[2 * mols : 2 * mols + 4], refs[2 * mols + 4]
    tall, normed, stacked = refs[2 * mols + 5 :]
    dim, rows = normed_t.shape
    unit = dim // (INNER * OUTER)
    normed[:, :rows] = normed_t[...]
    normed[:, rows:] = normed_t_got[...]
    spot = lax.broadcasted_iota(jnp.int32, small_out.shape, 0)
    small = jnp.zeros(small_out.shape, F32)
    for place in range(3):
        for m, part in enumerate(kept + got):
            stacked[m * SEQ : (m + 1) * SEQ, :] = part[place * SEQ : (place + 1) * SEQ, :]
        tall[place] = dot(normed[...], stacked[...]).astype(BF16)
        if place != 1:
            small = jnp.where(spot == 36 + place // 2, row_sum(stacked[...].astype(F32)), small)
    small_out[...] = small

    def block_at(dest, z, place):
        return tall[place, pl.ds(pl.multiple_of((dest * OUTER + z) * unit, 16), unit), :]

    deal(info, unit, outs, block_at, None)


def place_kernel(split_second, info, own, side_x, side_y, far_first, far_second, *outs):
    inner, outer = info[1], info[2]
    unit = own.shape[0] // (3 * OUTER)
    width = own.shape[1]
    for step in range(INNER):
        for turn in range(OUTER):
            ref, start = (own, side_x, side_y, far_first)[step], turn * 3 * unit
            if step == 3 and turn >= 2:
                ref, start = far_second, (turn - 2) * 3 * unit
            dest, z = inner ^ step, outer ^ turn
            tall = pl.ds(pl.multiple_of((dest * OUTER + z) * unit, 16), unit)
            flat = pl.ds(pl.multiple_of((dest * (OUTER // 2) + z // 2) * unit, 16), unit)
            columns = pl.ds(pl.multiple_of(z % 2 * width, LANES), width)
            for place in range(3):
                part = ref[start + place * unit : start + (place + 1) * unit, :].astype(F32)
                if split_second and place > 0:
                    outs[place][flat, columns] = part
                else:
                    outs[place][tall, :] = part


def per_device(
    features, lap_vectors, node_counts, edge_counts, endpoints, w_ident, type_table,
    gain_one, shift_one, w_query, w_key, w_value, bias_query, bias_value, w_out, bias_out,
    gain_two, shift_two, w_up, bias_up, w_down, bias_down, cotangent,
):
    dp_count = lax.axis_size("dp")
    dp_index = lax.axis_index("dp")
    mp_index = lax.axis_index("mp")
    block = INNER * OUTER
    rest_count = dp_count // block
    place = jnp.stack([mp_index, dp_index % INNER, dp_index // INNER % OUTER]).astype(jnp.int32)
    info = jnp.concatenate([place, node_counts, edge_counts])

    def swap(part):
        return lax.ppermute(part, "mp", [(0, 1), (1, 0)])

    def inner_move(part, step):
        return lax.ppermute(part, "dp", [(s, s ^ step) for s in range(dp_count)])

    def outer_move(part, step):
        return lax.ppermute(part, "dp", [(s, s ^ (step * INNER)) for s in range(dp_count)])

    rows_all, dim = features.shape
    rows = rows_all // 2
    mols = rows // SEQ
    width = w_query.shape[1]
    heads = width // HDIM
    lapk = lap_vectors.shape[1]
    idw = w_ident.shape[0]
    scalars = (info,)
    half_rows = lambda columns: pl.BlockSpec((rows, columns), lambda g, info: (info[0], 0))

    def table_of(rows_of, start):
        spot = lax.broadcasted_iota(jnp.int32, (8, 1), 0)
        for place, row in enumerate(rows_of):
            start = jnp.where(spot == place, row[None], start) if row is not None else start
        return start.astype(F32)

    def pinned(part):
        return pltpu.with_memory_space_constraint(part, pltpu.HBM)

    biases = table_of([bias_query, bias_value, bias_up], jnp.zeros((8, width), BF16))
    vecs = table_of(
        [None, None, gain_one, shift_one, bias_out, gain_two, shift_two, bias_down],
        jnp.pad(type_table, ((0, 6), (0, 0))),
    )

    wq_got, wk_got, wv_got = swap(w_query), swap(w_key), swap(w_value)
    biases_got = swap(biases)
    wo_got, wu_got, wd_got = swap(w_out), swap(w_up), swap(w_down)

    hidden, ident, normed, normed_t, q_own, k_own, v_own = call(
        embed_kernel,
        scalars,
        tuple(
            pinned(part)
            for part in (
                features, lap_vectors.T, endpoints.T, w_ident, vecs, biases,
                w_query, w_key, w_value,
            )
        ),
        [outside()] * 9,
        [
            ((rows, dim), F32),
            ((idw, rows), BF16),
            ((rows, dim), BF16),
            ((dim, rows), BF16),
            ((rows, width), BF16),
            ((rows, width), BF16),
            ((rows, width), BF16),
        ],
        scratch=[
            pltpu.VMEM((rows, dim), BF16),
            pltpu.VMEM((lapk, rows), BF16),
            pltpu.VMEM((2, rows), jnp.int32),
            pltpu.VMEM((idw, dim), BF16),
            pltpu.VMEM((8, dim), F32),
            pltpu.VMEM((8, width), F32),
            pltpu.VMEM((dim, width), BF16),
            pltpu.VMEM((dim, width), BF16),
            pltpu.VMEM((dim, width), BF16),
            pltpu.SemaphoreType.DMA((9,)),
        ],
        micros=6,
        local=False,
    )
    normed_t_got = swap(normed_t)
    sent_rows = dim + 2 * width + 3 * rows + 16
    (
        q_got, k_got, v_got, probs, kept_a, sent_a, middle, active, grad_middle, grad_branch,
    ) = call(
        forward_kernel,
        scalars,
        (
            hidden, normed, q_own, k_own, v_own, wq_got, wk_got, wv_got,
            w_out, wo_got, w_up, wu_got, w_down, wd_got, pinned(vecs), pinned(biases),
            biases_got, cotangent,
        ),
        [whole()] * 17 + [half_rows(dim)],
        [
            ((rows, width), BF16),
            ((rows, width), BF16),
            ((rows, width), BF16),
            ((mols, heads, SEQ, 2 * SEQ), BF16),
            ((sent_rows, width), BF16),
            ((sent_rows, width), BF16),
            ((rows, dim), F32),
            ((rows, dim), BF16),
            ((rows, dim), F32),
            ((rows, dim), BF16),
        ],
        scratch=[
            pltpu.VMEM((width, SEQ), F32),
            pltpu.VMEM((rows, dim), BF16),
            pltpu.VMEM((rows, dim), F32),
            pltpu.VMEM((rows, dim), BF16),
            pltpu.VMEM((rows, dim), F32),
            pltpu.VMEM((rows, dim), BF16),
        ],
        micros=20,
        limit=30,
    )
    got_a = swap(sent_a)
    middle, normed_t_got = lax.optimization_barrier((middle, normed_t_got))
    result, ga_own, ga_got = call(
        result_kernel,
        scalars,
        (middle, active, grad_branch, w_down, wd_got, w_out, wo_got, pinned(vecs)),
        [whole()] * 8,
        [((rows, dim), BF16), ((rows, width), BF16), ((rows, width), BF16)],
        micros=4,
    )

    unit = dim // block
    chunk = 3 * unit
    small_a, small_b = 16, 48

    def rest_sum(part):
        if rest_count == 1:
            return part
        groups = [[r * block + s for r in range(rest_count)] for s in range(block)]
        return lax.psum(part.astype(F32), "dp", axis_index_groups=groups).astype(part.dtype)

    def added(*parts):
        return sum(part.astype(F32) for part in parts)

    pair = 2 * chunk

    def after(part, *others):
        return lax.optimization_barrier((part, *others))[0]

    def plane_step(parts):
        first_kept, first_sent, second_kept, second_sent = parts
        first = added(first_kept, inner_move(first_sent, 1)).astype(BF16)
        second = added(second_kept, inner_move(second_sent, 2)).astype(BF16)
        return first, second

    def plane_turn(first, second, small, *others):
        sent = jnp.concatenate([first[pair : 2 * pair], small])
        got = after(inner_move(sent, 2), *others)
        first = added(jnp.concatenate([first[:pair], small]), got).astype(BF16)
        got = after(inner_move(second[pair : 2 * pair], 1), *others)
        return first, added(second[:pair], got).astype(BF16)

    def line_step(first, second, *others):
        small = first[pair:]
        lines = [first[chunk:], *(
            jnp.concatenate([second[turn * chunk : (turn + 1) * chunk], small]) for turn in (0, 1)
        )]
        got = [after(outer_move(lines[turn - 1], turn), *others) for turn in range(1, OUTER)]
        mine = rest_sum(added(first[:chunk], *(part[:chunk] for part in got)).astype(BF16))
        small = rest_sum(added(small, *(part[chunk:] for part in got)))
        return mine, small

    def line_back(mine, *others):
        got = [after(outer_move(mine, turn), *others) for turn in range(1, OUTER)]
        return jnp.concatenate([mine] + got)

    def plane_back(line, small=None):
        if small is None:
            side_x = inner_move(line, 1)
        else:
            side_x = inner_move(jnp.concatenate([line, small.astype(BF16)]), 1)
            small = added(small.astype(BF16), side_x[2 * pair :])
            side_x = side_x[: 2 * pair]
        return side_x, inner_move(line, 2), small

    def plane_back_turn(side_x, side_y):
        return inner_move(side_y[:pair], 1), inner_move(side_x[pair:], 2)

    def widened(small):
        small_got = swap(small)
        return jnp.where(
            mp_index == 0,
            jnp.concatenate([small, small_got], axis=1),
            jnp.concatenate([small_got, small], axis=1),
        )

    def placed(planes, split_second):
        tall, flat = ((dim, width), F32), ((width, dim), F32)
        return call(
            lambda *refs: place_kernel(split_second, *refs),
            (info,),
            planes,
            [whole()] * 5,
            [tall, flat, flat] if split_second else [tall] * 3,
            micros=3,
        )

    kept_a, result, ga_own = lax.optimization_barrier((kept_a, result, ga_own))
    parts_a = call(
        ffn_grads_kernel,
        scalars,
        (kept_a, got_a, cotangent),
        [whole()] * 3,
        [
            ((INNER * chunk + small_a, width), BF16),
            ((INNER * chunk + small_a, width), BF16),
            ((INNER * chunk, width), BF16),
            ((INNER * chunk, width), BF16),
        ],
        scratch=[
            pltpu.VMEM((dim, width), BF16),
            pltpu.VMEM((4, width, width), BF16),
            pltpu.VMEM((rows_all, dim), BF16),
        ],
        micros=6,
    )
    q_own = after(q_own, parts_a[0])
    steps_a = plane_step(parts_a)
    kept_b, got_b, sent_b = [], [], []
    for m in range(mols):
        if m == 2:
            q_own, steps_a = lax.optimization_barrier((q_own, steps_a))
        kept, sent = call(
            lambda *refs, m=m: attend_back_kernel(m, *refs),
            scalars,
            (q_own, k_own, v_own, ga_own, q_got, k_got, v_got, ga_got, probs),
            [whole()] * 9,
            [((3 * SEQ, width), BF16)] * 2,
            scratch=[
                pltpu.VMEM((2, width, SEQ), F32),
                pltpu.VMEM((2, SEQ, width), F32),
                pltpu.VMEM((2, SEQ, width), F32),
            ],
            micros=4,
        )
        kept_b.append(kept)
        sent_b.append(sent)
        got_b.append(swap(sent))
        q_own, q_got, _ = lax.optimization_barrier((q_own, q_got, kept))

    turned_a = plane_turn(*steps_a, steps_a[0][2 * pair :])
    normed_t, turned_a = lax.optimization_barrier((normed_t, turned_a))
    parts_b = call(
        qkv_grads_kernel,
        scalars,
        (normed_t, normed_t_got, *kept_b, *got_b),
        [whole()] * (2 + 2 * mols),
        [((INNER * chunk, width), BF16)] * 4 + [((small_b, width), F32)],
        scratch=[
            pltpu.VMEM((3, dim, width), BF16),
            pltpu.VMEM((dim, 2 * rows), BF16),
            pltpu.VMEM((2 * rows, width), BF16),
        ],
        micros=4,
    )
    steps_b = plane_step(parts_b[:4])
    mine_a, narrow_a = line_step(*turned_a, *steps_b)
    grad_middle = after(grad_middle, parts_b[0])
    grad_features, small_kept, small_sent = call(
        embed_back_kernel,
        scalars,
        (
            *kept_b, *sent_b, w_query, w_key, w_value, wq_got, wk_got, wv_got, ident, w_ident,
            grad_middle, pinned(vecs), features,
        ),
        [whole()] * (10 + 2 * mols) + [half_rows(dim)],
        [((rows, dim), F32), ((small_b, width), F32), ((small_b, width), BF16)],
        scratch=[
            pltpu.VMEM((rows, dim), F32),
            pltpu.VMEM((small_b, dim), F32),
            pltpu.VMEM((rows, width), BF16),
        ],
        micros=7,
        local=False,
    )
    small_got, steps_b = lax.optimization_barrier((swap(small_sent), steps_b))
    late = added(small_kept, small_got, parts_b[4]).astype(BF16)
    turned_b = plane_turn(*steps_b, late)
    line_a = line_back(mine_a, *turned_b)
    wide_a = widened(narrow_a)
    mine_b, small_b_sum = line_step(*turned_b)
    side_ax, side_ay, _ = plane_back(line_a)
    line_b = line_back(mine_b)
    far_a = plane_back_turn(side_ax, side_ay)
    planes_a = (line_a, side_ax, side_ay, *far_a)
    line_b, far_a = lax.optimization_barrier((line_b, far_a))
    side_bx, side_by, narrow_b = plane_back(line_b, small_b_sum)
    far_b = plane_back_turn(side_bx, side_by)
    wide_b = widened(narrow_b)
    planes_b = (line_b, side_bx, side_by, *far_b)

    grad_w_up, grad_w_out, grad_w_down = placed(planes_a, True)
    grad_w_query, grad_w_key, grad_w_value = placed(planes_b, False)
    return (
        result,
        grad_features,
        wide_b[:idw],
        wide_b[idw : idw + 2],
        wide_b[idw + 2],
        wide_b[idw + 3],
        grad_w_query,
        grad_w_key,
        grad_w_value,
        narrow_b[idw + 4],
        narrow_b[idw + 5],
        grad_w_out,
        wide_a[0],
        wide_a[1],
        wide_a[2],
        grad_w_up,
        narrow_a[4],
        grad_w_down,
        wide_a[3],
    )


def solution(mesh):
    token, split = P("dp", None), P(("dp", "mp"), None)
    columns, lines, cut, copy = P(None, "mp"), P("mp", None), P("mp"), P()
    return jax.shard_map(
        per_device,
        mesh=mesh,
        in_specs=(
            token, token, P("dp"), P("dp"), token, copy, copy, copy, copy, columns, columns,
            columns, cut, cut, lines, copy, copy, copy, columns, cut, lines, copy, token,
        ),
        out_specs=(
            split, split, copy, copy, copy, copy, columns, columns, columns, cut, cut, lines,
            copy, copy, copy, columns, cut, lines, copy,
        ),
        check_vma=False,
    )
```

```python
import math

import jax
import jax.numpy as jnp
from jax import lax
from jax.experimental import pallas as pl
from jax.experimental.pallas import tpu as pltpu
from jax.sharding import PartitionSpec as P

HDIM = 24
SEQ = 128
LANES = 128
INNER = 4
OUTER = 4
EPSILON = 1e-05
SCALE = 1.0 / math.sqrt(HDIM)
F32, BF16 = jnp.float32, jnp.bfloat16
MIB = 1024 * 1024


def dot(left, right):
    return jnp.dot(left, right, preferred_element_type=F32)


def dot_nt(left, right):
    return lax.dot_general(left, right, (((1,), (1,)), ((), ())), preferred_element_type=F32)


def dot_tn(left, right):
    return lax.dot_general(left, right, (((0,), (0,)), ((), ())), preferred_element_type=F32)


def norm_parts(hidden):
    average = jnp.mean(hidden, axis=-1, keepdims=True)
    centred = hidden - average
    inverse = lax.rsqrt(jnp.mean(centred * centred, axis=-1, keepdims=True) + EPSILON)
    return centred * inverse, inverse


def norm_back(unit, inverse, grad_hat):
    return inverse * (
        grad_hat
        - jnp.mean(grad_hat, axis=-1, keepdims=True)
        - unit * jnp.mean(grad_hat * unit, axis=-1, keepdims=True)
    )


def row_sum(block):
    return jnp.sum(block, axis=0, keepdims=True)


def positions(length):
    return lax.broadcasted_iota(jnp.int32, (length, 1), 0)


def whole():
    return pl.BlockSpec(memory_space=pltpu.VMEM)


def outside():
    return pl.BlockSpec(memory_space=pltpu.HBM)


def node_count(info, m):
    return info[3 + m]


def slot_count(info, m):
    return info[3 + m] + info[3 + (info.shape[0] - 3) // 2 + m]


def call(kernel, scalars, args, specs, outs, scratch=(), micros=5, limit=24, local=True):
    return pl.pallas_call(
        kernel,
        out_shape=[jax.ShapeDtypeStruct(shape, kind) for shape, kind in outs],
        grid_spec=pltpu.PrefetchScalarGridSpec(
            num_scalar_prefetch=len(scalars),
            grid=(1,),
            in_specs=specs,
            out_specs=[whole() for _ in outs],
            scratch_shapes=list(scratch),
        ),
        compiler_params=pltpu.CompilerParams(vmem_limit_bytes=limit * MIB),
        cost_estimate=pl.CostEstimate(
            flops=1 if local else micros * 1_000_000_000,
            bytes_accessed=1 if local else 0,
            transcendentals=0,
        ),
    )(*scalars, *args)


def head_windows(width):
    windows = []
    for pair in range(width // (2 * HDIM)):
        low = pair * 2 * HDIM // LANES * LANES
        high = -(-(pair + 1) * 2 * HDIM // LANES) * LANES
        windows.append((low, high))
    return windows


def split_heads(block, pair, window):
    low, high = window
    part = block[:, low:high]
    column = low + lax.broadcasted_iota(jnp.int32, (16, high - low), 1)
    sides = []
    for head in (2 * pair, 2 * pair + 1):
        inside = (column >= head * HDIM) & (column < (head + 1) * HDIM)
        mask = jnp.where(inside, 1.0, 0.0).astype(BF16)
        sides.append(part * jnp.concatenate([mask] * (block.shape[0] // 16), axis=0))
    return jnp.concatenate(sides, axis=0)


def embed_rows(feats, lap, ends, w_ident, vecs, at, count):
    table = lap[:, at]
    slot = lax.broadcasted_iota(jnp.int32, (SEQ, SEQ), 0)
    picked = []
    for end in (0, 1):
        pick = jnp.where(ends[end : end + 1, at] == slot, 1.0, 0.0).astype(BF16)
        picked.append(dot(table, pick))
    ident = jnp.concatenate(picked, axis=0).astype(BF16)
    hidden = feats[at, :].astype(F32) + dot_tn(ident, w_ident[...])
    hidden = hidden + jnp.where(positions(SEQ) >= count, vecs[1:2, :], vecs[0:1, :])
    unit, _ = norm_parts(hidden)
    return hidden, ident, (unit * vecs[2:3, :] + vecs[3:4, :]).astype(BF16)


def embed_kernel(
    info, feats_in, lap_in, ends_in, w_ident_in, vecs_in, biases_in, wq_in, wk_in, wv_in,
    hidden_out, ident_out, normed_out, normed_t_out, q_out, k_out, v_out,
    feats, lap, ends, w_ident, vecs, biases, w_q, w_k, w_v, sems,
):
    rows, dim = feats.shape
    mols = rows // SEQ
    own_rows = pl.ds(pl.multiple_of(info[0] * rows, SEQ), rows)
    moves = (
        (ends_in.at[:, own_rows], ends),
        (lap_in.at[:, own_rows], lap),
        (w_ident_in, w_ident),
        (vecs_in, vecs),
        (feats_in.at[own_rows, :], feats),
        (biases_in, biases),
        (wq_in, w_q),
        (wk_in, w_k),
        (wv_in, w_v),
    )
    copies = [
        pltpu.make_async_copy(source, target, sems.at[place])
        for place, (source, target) in enumerate(moves)
    ]
    for copy in copies:
        copy.start()
    for copy in copies[:6]:
        copy.wait()

    def molecule(m, carry):
        at = pl.ds(pl.multiple_of(m * SEQ, SEQ), SEQ)
        count = node_count(info, info[0] * mols + m)
        hidden, ident, normed = embed_rows(feats, lap, ends, w_ident, vecs, at, count)
        ident_out[:, at] = ident
        hidden_out[at, :] = hidden
        normed_out[at, :] = normed
        normed_t_out[:, at] = normed.T
        return carry

    lax.fori_loop(0, mols, molecule, 0)
    normed = normed_out[...]
    copies[6].wait()
    q_out[...] = (dot(normed, w_q[...]) + biases[0:1, :]).astype(BF16)
    copies[7].wait()
    k_out[...] = dot(normed, w_k[...]).astype(BF16)
    copies[8].wait()
    v_out[...] = (dot(normed, w_v[...]) + biases[1:2, :]).astype(BF16)


def forward_kernel(
    info, hidden, normed, q_own, k_own, v_own, w_q, w_k, w_v,
    wo_own, wo, wu_own, wu, wd_own, wd, vecs, biases_own, biases, cots,
    q_out, k_out, v_out, probs_out, keep_out, send_out, middle, active, gm_out,
    ga_own_out, ga_out, dv_own_out, dv_out,
    mixed, attended, unit, normed_two, slope, grad_ffn, grad_branch, dv,
):
    rows, dim = hidden.shape
    width = q_own.shape[1]
    mols = rows // SEQ
    pairs = width // (2 * HDIM)
    windows = head_windows(width)
    own_core = info[0]

    q_out[...] = (dot(normed[...], w_q[...]) + biases[0:1, :]).astype(BF16)
    k_out[...] = dot(normed[...], w_k[...]).astype(BF16)
    v_out[...] = (dot(normed[...], w_v[...]) + biases[1:2, :]).astype(BF16)

    def attend(m, carry):
        at = pl.ds(pl.multiple_of(m * SEQ, SEQ), SEQ)
        place = own_core * mols + m
        count = slot_count(info, place)
        key_keep = positions(SEQ) < count
        query_keep = lax.broadcasted_iota(jnp.int32, (1, SEQ), 1) < count
        sides = ((q_own, k_own, v_own, keep_out), (q_out, k_out, v_out, send_out))
        for side, (q_ref, k_ref, v_ref, part_out) in enumerate(sides):
            queries, key_rows = q_ref[at, :], k_ref[at, :]
            values_t = v_ref[at, :].T
            for pair in range(pairs):
                low, high = windows[pair]
                both = split_heads(queries, pair, windows[pair])
                scores = dot_nt(key_rows[:, low:high], both) * SCALE
                scores = jnp.where(key_keep, scores, -1e30)
                top = jnp.max(scores, axis=0, keepdims=True)
                raised = jnp.exp(scores - top)
                total = row_sum(raised)
                probs = (raised * (1.0 / total)).astype(BF16)
                probs_out[m, side * pairs + pair] = probs
                first = pair * 2 * HDIM
                out = dot(values_t[first : first + 2 * HDIM], probs)
                mixed[first : first + HDIM, :] = out[:HDIM, :SEQ]
                mixed[first + HDIM : first + 2 * HDIM, :] = out[HDIM:, SEQ:]
            kept = jnp.where(query_keep, mixed[...], 0.0).astype(BF16)
            part_out[dim : dim + width, at] = kept
            attended[at, side * width : (side + 1) * width] = kept.T
        return carry

    lax.fori_loop(0, mols, attend, 0)
    middle[...] = (
        hidden[...] + dot(attended[:, :width], wo_own[...]) + dot(attended[:, width:], wo[...])
    )

    def second_norm(m, carry):
        at = pl.ds(pl.multiple_of(m * SEQ, SEQ), SEQ)
        place = own_core * mols + m
        keep = positions(SEQ) < slot_count(info, place)
        total = middle[at, :] + vecs[4:5, :]
        middle[at, :] = total
        unit_rows, _ = norm_parts(total)
        unit[at, :] = unit_rows
        rows_two = (unit_rows * vecs[5:6, :] + vecs[6:7, :]).astype(BF16)
        normed_two[at, :] = rows_two
        turned = rows_two.T
        keep_out[:dim, at] = turned
        send_out[:dim, at] = turned
        grad_ffn[at, :] = jnp.where(keep, cots[at, :].astype(F32), 0.0).astype(BF16)
        return carry

    lax.fori_loop(0, mols, second_norm, 0)

    for side, (w_ref, b_ref, part_out) in enumerate(
        ((wu_own, biases_own, keep_out), (wu, biases, send_out))
    ):
        columns = slice(side * width, (side + 1) * width)
        slope[:, columns] = dot(normed_two[...], w_ref[...]) + b_ref[2:3, :]

        def activate(m, carry):
            at = pl.ds(pl.multiple_of(m * SEQ, SEQ), SEQ)
            before = slope[at, columns]
            phi = 0.5 * (1.0 + lax.erf(before * math.sqrt(0.5)))
            out = (before * phi).astype(BF16)
            slope[at, columns] = phi + before * jnp.exp(before * before * -0.5) * (
                1.0 / math.sqrt(2.0 * math.pi)
            )
            active[at, columns] = out
            part_out[dim + width : dim + 2 * width, at] = out.T
            return carry

        lax.fori_loop(0, mols, activate, 0)

    place_b = dim + 2 * width
    for side, (w_ref, part_out) in enumerate(((wd_own, keep_out), (wd, send_out))):
        columns = slice(side * width, (side + 1) * width)
        grad_before = slope[:, columns] * dot_nt(grad_ffn[...], w_ref[...])
        part_out[place_b : place_b + rows, :] = grad_before.astype(BF16)

    back = pl.ds(place_b, rows)
    gm_out[...] = dot_nt(keep_out[back, :], wu_own[...]) + dot_nt(send_out[back, :], wu[...])

    def second_back(m, sums):
        at = pl.ds(pl.multiple_of(m * SEQ, SEQ), SEQ)
        place = own_core * mols + m
        keep = positions(SEQ) < slot_count(info, place)
        grad_normed = gm_out[at, :]
        unit_rows = unit[at, :]
        _, inverse = norm_parts(middle[at, :])
        grad_result = jnp.where(keep, cots[at, :].astype(F32), 0.0)
        grad = grad_result + norm_back(unit_rows, inverse, grad_normed * vecs[5:6, :])
        gm_out[at, :] = grad
        grad_branch[at, :] = grad.astype(BF16)
        return (
            sums[0] + row_sum(grad),
            sums[1] + row_sum(grad_normed * unit_rows),
            sums[2] + row_sum(grad_normed),
            sums[3] + row_sum(grad_result),
        )

    nothing = jnp.zeros((1, dim), F32)
    sums = lax.fori_loop(0, mols, second_back, (nothing,) * 4)
    place_m = place_b + rows
    for part_out in (keep_out, send_out):
        part_out[place_m : place_m + rows, :] = grad_branch[:, :width]
        part_out[place_m + rows : place_m + 2 * rows, :] = grad_branch[:, width:]
    small = jnp.concatenate(list(sums) + [nothing] * 12, axis=0)
    left, right = small[:, :width], small[:, width:]
    place_v = place_m + 2 * rows
    place_s = place_v + rows
    keep_out[place_s:, :] = jnp.where(own_core == 0, left, right).astype(BF16)
    send_out[place_s:, :] = jnp.where(own_core == 0, right, left).astype(BF16)

    sides = ((ga_own_out, wo_own, dv_own_out, keep_out), (ga_out, wo, dv_out, send_out))
    for ref, weight, _, _ in sides:
        product = dot_nt(grad_branch[...], weight[...])
        for m in range(mols):
            place = own_core * mols + m
            keep = positions(SEQ) < slot_count(info, place)
            at = slice(m * SEQ, (m + 1) * SEQ)
            ref[at, :] = jnp.where(keep, product[at], 0.0).astype(BF16)

    def value_back(m, carry):
        base = pl.multiple_of(m * SEQ, SEQ)
        at = pl.ds(base, SEQ)
        for side, (ref, _, out, part_out) in enumerate(sides):
            grads = ref[at, :]
            dv[side] = jnp.zeros_like(dv[side])
            for pair in range(pairs):
                low, high = windows[pair]
                both = split_heads(grads, pair, windows[pair])
                dv[side, :, low:high] += dot(probs_out[m, side * pairs + pair], both)
            total = dv[side].astype(BF16)
            out[at, :] = total
            part_out[pl.ds(base + place_v, SEQ), :] = total
        return carry

    lax.fori_loop(0, mols, value_back, 0)


def result_kernel(
    info, middle, active, wd_own, wd, w_ident, vecs, feats, lap, ends, result_out, normed_t_out
):
    width = wd.shape[0]
    mols = middle.shape[0] // SEQ
    result_out[...] = (
        middle[...]
        + dot(active[:, :width], wd_own[...])
        + dot(active[:, width:], wd[...])
        + vecs[7:8, :]
    ).astype(BF16)

    def molecule(m, carry):
        at = pl.ds(pl.multiple_of(m * SEQ, SEQ), SEQ)
        count = node_count(info, (1 - info[0]) * mols + m)
        normed_t_out[:, at] = embed_rows(feats, lap, ends, w_ident, vecs, at, count)[2].T
        return carry

    lax.fori_loop(0, mols, molecule, 0)


def attend_back_kernel(
    m, info, q_own, k_own, v_own, ga_own, q_got, k_got, v_got, ga_got, probs_all,
    keep_out, send_out, dq_t, dk,
):
    width = q_own.shape[1]
    pairs = width // (2 * HDIM)
    windows = head_windows(width)
    at = slice(m * SEQ, (m + 1) * SEQ)
    sides = (
        (q_own, k_own, v_own, ga_own, keep_out),
        (q_got, k_got, v_got, ga_got, send_out),
    )
    for side, (q_ref, k_ref, v_ref, g_ref, part_out) in enumerate(sides):
        queries, key_rows, values, grads = q_ref[at, :], k_ref[at, :], v_ref[at, :], g_ref[at, :]
        keys_t = key_rows.T
        dk[side] = jnp.zeros_like(dk[side])
        for pair in range(pairs):
            low, high = windows[pair]
            both_q = split_heads(queries, pair, windows[pair])
            both_g = split_heads(grads, pair, windows[pair])
            probs = probs_all[m, side * pairs + pair].astype(F32)
            grad_probs = dot_nt(values[:, low:high], both_g)
            inner = row_sum(probs * grad_probs)
            grad_scores = (probs * (grad_probs - inner)).astype(BF16)
            dk[side, :, low:high] += dot(grad_scores, both_q)
            first = pair * 2 * HDIM
            out = dot(keys_t[first : first + 2 * HDIM], grad_scores)
            dq_t[side, first : first + HDIM, :] = out[:HDIM, :SEQ]
            dq_t[side, first + HDIM : first + 2 * HDIM, :] = out[HDIM:, SEQ:]
        part_out[:SEQ, :] = (dq_t[side] * SCALE).astype(BF16).T
        part_out[SEQ:, :] = (dk[side] * SCALE).astype(BF16)


def embed_back_kernel(
    info, *refs,
):
    mols = len(refs[:-18]) // 2
    grads_own, grads = refs[:mols], refs[mols : 2 * mols]
    (
        dv_own, dv,
        wq_own, wk_own, wv_own, w_q, w_k, w_v, ident, w_ident, grad_middle, vecs, feats,
        features_out, small_out, grad_normed, small, stacked,
    ) = refs[2 * mols :]
    rows, dim = feats.shape
    width = wq_own.shape[1]
    own_core = info[0]
    idw = ident.shape[0]
    total = None
    for part, values, weights in (
        (grads_own, dv_own, (wq_own, wk_own, wv_own)),
        (grads, dv, (w_q, w_k, w_v)),
    ):
        term = dot_nt(values[...], weights[2][...])
        total = term if total is None else total + term
        for place, weight in enumerate(weights[:2]):
            for m in range(mols):
                stacked[m * SEQ : (m + 1) * SEQ, :] = part[m][place * SEQ : (place + 1) * SEQ, :]
            total = total + dot_nt(stacked[...], weight[...])
    grad_normed[...] = total
    small[...] = jnp.zeros_like(small)

    def molecule(m, carry):
        at = pl.ds(pl.multiple_of(m * SEQ, SEQ), SEQ)
        is_edge = positions(SEQ) >= node_count(info, own_core * mols + m)
        hidden = feats[at, :].astype(F32) + dot_tn(ident[:, at], w_ident[...])
        hidden = hidden + jnp.where(is_edge, vecs[1:2, :], vecs[0:1, :])
        unit, inverse = norm_parts(hidden)
        grad_rows = grad_normed[at, :]
        grad = grad_middle[at, :] + norm_back(unit, inverse, grad_rows * vecs[2:3, :])
        features_out[at, :] = grad
        high = grad.astype(BF16)
        rest = (grad - high.astype(F32)).astype(BF16)
        picked = ident[:, at]
        small[:idw, :] += dot(picked, high) + dot(picked, rest)
        edge_rows = jnp.where(is_edge, grad, 0.0)
        small[idw : idw + 1, :] += row_sum(grad - edge_rows)
        small[idw + 1 : idw + 2, :] += row_sum(edge_rows)
        small[idw + 2 : idw + 3, :] += row_sum(grad_rows * unit)
        small[idw + 3 : idw + 4, :] += row_sum(grad_rows)
        return carry

    lax.fori_loop(0, mols, molecule, 0)
    count = idw + 4
    small_out[...] = jnp.zeros_like(small_out)
    small_out[:count, :] = small[:count, :width]
    small_out[count : 2 * count, :] = small[:count, width:]


def deal(info, unit, places, outs, block_at, small):
    inner, outer = info[1], info[2]
    first_kept, first_sent, second_kept, second_sent = outs
    for step in range(INNER):
        for turn in range(OUTER):
            if turn < 2:
                out, slot = (first_sent if step % 2 else first_kept), step // 2
            else:
                out, slot = (second_sent if step // 2 else second_kept), step % 2
            start = (slot * 2 + turn % 2) * places * unit
            for place in range(places):
                out[start + place * unit : start + (place + 1) * unit, :] = block_at(
                    inner ^ step, outer ^ turn, place
                )
    if small is not None:
        for out in (first_kept, first_sent):
            out[INNER * places * unit :, :] = small


def ffn_grads_kernel(info, kept, got, cots, normed_t, normed_t_got, *rest):
    outs, (tall, flat, grad_ffn) = rest[:4], rest[4:]
    rows_all, dim = cots.shape
    rows, width = rows_all // 2, kept.shape[1]
    mols = rows // SEQ
    own_core = info[0]
    for m in range(2 * mols):
        keep = positions(SEQ) < slot_count(info, m)
        at = slice(m * SEQ, (m + 1) * SEQ)
        grad_ffn[at, :] = jnp.where(keep, cots[at, :].astype(F32), 0.0).astype(BF16)
    own_rows = pl.ds(pl.multiple_of(own_core * rows, SEQ), rows)
    other_rows = pl.ds(pl.multiple_of((1 - own_core) * rows, SEQ), rows)
    place_b = dim + 2 * width
    place_m = place_b + rows
    place_v = place_m + 2 * rows
    place_s = place_v + rows
    back, value = slice(place_b, place_m), slice(place_v, place_s)
    tall[1] = (
        dot(normed_t[...], kept[value, :]) + dot(normed_t_got[...], got[value, :])
    ).astype(BF16)
    tall[0] = (dot(kept[:dim, :], kept[back, :]) + dot(got[:dim, :], got[back, :])).astype(BF16)
    turned = slice(dim, dim + width)
    for half in (0, 1):
        mid = slice(place_m + half * rows, place_m + (half + 1) * rows)
        flat[half] = (
            dot(kept[turned, :], kept[mid, :]) + dot(got[turned, :], got[mid, :])
        ).astype(BF16)
    turned = slice(dim + width, dim + 2 * width)
    for half in (0, 1):
        columns = slice(half * width, (half + 1) * width)
        product = dot(kept[turned, :], grad_ffn[own_rows, columns])
        product = product + dot(got[turned, :], grad_ffn[other_rows, columns])
        flat[2 + half] = product.astype(BF16)
    small = kept[place_s:, :].astype(F32) + got[place_s:, :].astype(F32)
    spot = lax.broadcasted_iota(jnp.int32, small.shape, 0)
    for row, part in ((4, back), (5, value)):
        bias = row_sum(kept[part, :].astype(F32)) + row_sum(got[part, :].astype(F32))
        small = jnp.where(spot == row, bias, small)
    small = small.astype(BF16)
    unit = dim // (INNER * OUTER)

    def block_at(dest, z, place):
        if place < 2:
            return tall[place, pl.ds(pl.multiple_of((dest * OUTER + z) * unit, 16), unit), :]
        row = pl.multiple_of((dest * (OUTER // 2) + z // 2) * unit, 16)
        return flat[2 * (place - 2) + z % 2, pl.ds(row, unit), :]

    deal(info, unit, 4, outs, block_at, small)


def qkv_grads_kernel(info, normed_t, normed_t_got, *refs):
    mols = normed_t.shape[1] // SEQ
    kept, got = refs[:mols], refs[mols : 2 * mols]
    outs, small_out = refs[2 * mols : 2 * mols + 4], refs[2 * mols + 4]
    tall, normed, stacked = refs[2 * mols + 5 :]
    dim, rows = normed_t.shape
    unit = dim // (INNER * OUTER)
    normed[:, :rows] = normed_t[...]
    normed[:, rows:] = normed_t_got[...]
    spot = lax.broadcasted_iota(jnp.int32, small_out.shape, 0)
    small = jnp.zeros(small_out.shape, F32)
    for place in range(2):
        for m, part in enumerate(kept + got):
            stacked[m * SEQ : (m + 1) * SEQ, :] = part[place * SEQ : (place + 1) * SEQ, :]
        tall[place] = dot(normed[...], stacked[...]).astype(BF16)
        if place == 0:
            small = jnp.where(spot == 72, row_sum(stacked[...].astype(F32)), small)
    small_out[...] = small

    def block_at(dest, z, place):
        return tall[place, pl.ds(pl.multiple_of((dest * OUTER + z) * unit, 16), unit), :]

    deal(info, unit, 2, outs, block_at, None)


def place_kernel(flat_from, info, own, side_x, side_y, far_first, far_second, *outs):
    inner, outer = info[1], info[2]
    places = len(outs)
    unit = own.shape[0] // (places * OUTER)
    width = own.shape[1]
    for step in range(INNER):
        for turn in range(OUTER):
            ref, start = (own, side_x, side_y, far_first)[step], turn * places * unit
            if step == 3 and turn >= 2:
                ref, start = far_second, (turn - 2) * places * unit
            dest, z = inner ^ step, outer ^ turn
            tall = pl.ds(pl.multiple_of((dest * OUTER + z) * unit, 16), unit)
            flat = pl.ds(pl.multiple_of((dest * (OUTER // 2) + z // 2) * unit, 16), unit)
            columns = pl.ds(pl.multiple_of(z % 2 * width, LANES), width)
            for place in range(places):
                part = ref[start + place * unit : start + (place + 1) * unit, :].astype(F32)
                if place >= flat_from:
                    outs[place][flat, columns] = part
                else:
                    outs[place][tall, :] = part


def per_device(
    features, lap_vectors, node_counts, edge_counts, endpoints, w_ident, type_table,
    gain_one, shift_one, w_query, w_key, w_value, bias_query, bias_value, w_out, bias_out,
    gain_two, shift_two, w_up, bias_up, w_down, bias_down, cotangent,
):
    dp_count = lax.axis_size("dp")
    dp_index = lax.axis_index("dp")
    mp_index = lax.axis_index("mp")
    block = INNER * OUTER
    rest_count = dp_count // block
    place = jnp.stack([mp_index, dp_index % INNER, dp_index // INNER % OUTER]).astype(jnp.int32)
    info = jnp.concatenate([place, node_counts, edge_counts])

    def swap(part):
        return lax.ppermute(part, "mp", [(0, 1), (1, 0)])

    def inner_move(part, step):
        return lax.ppermute(part, "dp", [(s, s ^ step) for s in range(dp_count)])

    def outer_move(part, step):
        return lax.ppermute(part, "dp", [(s, s ^ (step * INNER)) for s in range(dp_count)])

    rows_all, dim = features.shape
    rows = rows_all // 2
    mols = rows // SEQ
    width = w_query.shape[1]
    heads = width // HDIM
    lapk = lap_vectors.shape[1]
    idw = w_ident.shape[0]
    scalars = (info,)
    half_rows = lambda columns: pl.BlockSpec((rows, columns), lambda g, info: (info[0], 0))

    def table_of(rows_of, start):
        spot = lax.broadcasted_iota(jnp.int32, (8, 1), 0)
        for place, row in enumerate(rows_of):
            start = jnp.where(spot == place, row[None], start) if row is not None else start
        return start.astype(F32)

    def pinned(part):
        return pltpu.with_memory_space_constraint(part, pltpu.HBM)

    biases = table_of([bias_query, bias_value, bias_up], jnp.zeros((8, width), BF16))
    vecs = table_of(
        [None, None, gain_one, shift_one, bias_out, gain_two, shift_two, bias_down],
        jnp.pad(type_table, ((0, 6), (0, 0))),
    )

    wq_got, wk_got, wv_got = swap(w_query), swap(w_key), swap(w_value)
    biases_got = swap(biases)
    wo_got, wu_got, wd_got = swap(w_out), swap(w_up), swap(w_down)

    hidden, ident, normed, normed_t, q_own, k_own, v_own = call(
        embed_kernel,
        scalars,
        tuple(
            pinned(part)
            for part in (
                features, lap_vectors.T, endpoints.T, w_ident, vecs, biases,
                w_query, w_key, w_value,
            )
        ),
        [outside()] * 9,
        [
            ((rows, dim), F32),
            ((idw, rows), BF16),
            ((rows, dim), BF16),
            ((dim, rows), BF16),
            ((rows, width), BF16),
            ((rows, width), BF16),
            ((rows, width), BF16),
        ],
        scratch=[
            pltpu.VMEM((rows, dim), BF16),
            pltpu.VMEM((lapk, rows), BF16),
            pltpu.VMEM((2, rows), jnp.int32),
            pltpu.VMEM((idw, dim), BF16),
            pltpu.VMEM((8, dim), F32),
            pltpu.VMEM((8, width), F32),
            pltpu.VMEM((dim, width), BF16),
            pltpu.VMEM((dim, width), BF16),
            pltpu.VMEM((dim, width), BF16),
            pltpu.SemaphoreType.DMA((9,)),
        ],
        micros=6,
        local=False,
    )
    sent_rows = dim + 2 * width + 4 * rows + 16
    (
        q_got, k_got, v_got, probs, kept_a, sent_a, middle, active, grad_middle,
        ga_own, ga_got, dv_own, dv_got,
    ) = call(
        forward_kernel,
        scalars,
        (
            hidden, normed, q_own, k_own, v_own, wq_got, wk_got, wv_got,
            w_out, wo_got, w_up, wu_got, w_down, wd_got, pinned(vecs), pinned(biases),
            biases_got, cotangent,
        ),
        [whole()] * 17 + [half_rows(dim)],
        [
            ((rows, width), BF16),
            ((rows, width), BF16),
            ((rows, width), BF16),
            ((mols, heads, SEQ, 2 * SEQ), BF16),
            ((sent_rows, width), BF16),
            ((sent_rows, width), BF16),
            ((rows, dim), F32),
            ((rows, dim), BF16),
            ((rows, dim), F32),
            ((rows, width), BF16),
            ((rows, width), BF16),
            ((rows, width), BF16),
            ((rows, width), BF16),
        ],
        scratch=[
            pltpu.VMEM((width, SEQ), F32),
            pltpu.VMEM((rows, dim), BF16),
            pltpu.VMEM((rows, dim), F32),
            pltpu.VMEM((rows, dim), BF16),
            pltpu.VMEM((rows, dim), F32),
            pltpu.VMEM((rows, dim), BF16),
            pltpu.VMEM((rows, dim), BF16),
            pltpu.VMEM((2, SEQ, width), F32),
        ],
        micros=20,
        limit=30,
    )
    got_a = swap(sent_a)
    other_rows = lambda columns: pl.BlockSpec((rows, columns), lambda g, info: (1 - info[0], 0))
    other_columns = lambda count: pl.BlockSpec((count, rows), lambda g, info: (0, 1 - info[0]))
    result, normed_t_got = call(
        result_kernel,
        scalars,
        (
            middle, active, w_down, wd_got, w_ident, pinned(vecs),
            features, lap_vectors.T, endpoints.T,
        ),
        [whole()] * 6 + [other_rows(dim), other_columns(lapk), other_columns(2)],
        [((rows, dim), BF16), ((dim, rows), BF16)],
        micros=4,
    )

    unit = dim // block
    chunk_a, chunk_b = 4 * unit, 2 * unit
    small_a, small_b = 16, 80

    def rest_sum(part):
        if rest_count == 1:
            return part
        groups = [[r * block + s for r in range(rest_count)] for s in range(block)]
        return lax.psum(part.astype(F32), "dp", axis_index_groups=groups).astype(part.dtype)

    def added(*parts):
        return sum(part.astype(F32) for part in parts)

    def after(part, *others):
        return lax.optimization_barrier((part, *others))[0]

    def plane_step(parts):
        first_kept, first_sent, second_kept, second_sent = parts
        first = added(first_kept, inner_move(first_sent, 1)).astype(BF16)
        second = added(second_kept, inner_move(second_sent, 2)).astype(BF16)
        return first, second

    def plane_turn(first, second, small, *others):
        pair = second.shape[0] // 2
        sent = jnp.concatenate([first[pair : 2 * pair], small])
        got = after(inner_move(sent, 2), *others)
        first = added(jnp.concatenate([first[:pair], small]), got).astype(BF16)
        got = after(inner_move(second[pair : 2 * pair], 1), *others)
        return first, added(second[:pair], got).astype(BF16)

    def line_step(first, second, *others):
        pair, chunk = second.shape[0], second.shape[0] // 2
        small = first[pair:]
        lines = [first[chunk:], *(
            jnp.concatenate([second[turn * chunk : (turn + 1) * chunk], small]) for turn in (0, 1)
        )]
        got = [after(outer_move(lines[turn - 1], turn), *others) for turn in range(1, OUTER)]
        mine = rest_sum(added(first[:chunk], *(part[:chunk] for part in got)).astype(BF16))
        small = rest_sum(added(small, *(part[chunk:] for part in got)))
        return mine, small

    def line_back(mine, *others):
        got = [after(outer_move(mine, turn), *others) for turn in range(1, OUTER)]
        return jnp.concatenate([mine] + got)

    def plane_back(line, small=None):
        if small is None:
            side_x = inner_move(line, 1)
        else:
            side_x = inner_move(jnp.concatenate([line, small.astype(BF16)]), 1)
            small = added(small.astype(BF16), side_x[line.shape[0] :])
            side_x = side_x[: line.shape[0]]
        return side_x, inner_move(line, 2), small

    def plane_back_turn(side_x, side_y):
        pair = side_x.shape[0] // 2
        return inner_move(side_y[:pair], 1), inner_move(side_x[pair:], 2)

    def widened(small):
        small_got = swap(small)
        return jnp.where(
            mp_index == 0,
            jnp.concatenate([small, small_got], axis=1),
            jnp.concatenate([small_got, small], axis=1),
        )

    def placed(planes, tall, flat):
        return call(
            lambda *refs: place_kernel(tall, *refs),
            (info,),
            planes,
            [whole()] * 5,
            [((dim, width), F32)] * tall + [((width, dim), F32)] * flat,
            micros=3,
        )

    kept_a, result, normed_t_got = lax.optimization_barrier((kept_a, result, normed_t_got))
    parts_a = call(
        ffn_grads_kernel,
        scalars,
        (kept_a, got_a, cotangent, normed_t, normed_t_got),
        [whole()] * 5,
        [
            ((INNER * chunk_a + small_a, width), BF16),
            ((INNER * chunk_a + small_a, width), BF16),
            ((INNER * chunk_a, width), BF16),
            ((INNER * chunk_a, width), BF16),
        ],
        scratch=[
            pltpu.VMEM((2, dim, width), BF16),
            pltpu.VMEM((4, width, width), BF16),
            pltpu.VMEM((rows_all, dim), BF16),
        ],
        micros=6,
    )
    q_own = after(q_own, parts_a[0])
    steps_a = plane_step(parts_a)
    kept_b, got_b, sent_b = [], [], []
    for m in range(mols):
        if m == 2:
            q_own, steps_a = lax.optimization_barrier((q_own, steps_a))
        kept, sent = call(
            lambda *refs, m=m: attend_back_kernel(m, *refs),
            scalars,
            (q_own, k_own, v_own, ga_own, q_got, k_got, v_got, ga_got, probs),
            [whole()] * 9,
            [((2 * SEQ, width), BF16)] * 2,
            scratch=[
                pltpu.VMEM((2, width, SEQ), F32),
                pltpu.VMEM((2, SEQ, width), F32),
            ],
            micros=4,
        )
        kept_b.append(kept)
        sent_b.append(sent)
        got_b.append(swap(sent))
        q_own, q_got, _ = lax.optimization_barrier((q_own, q_got, kept))

    turned_a = plane_turn(*steps_a, steps_a[0][INNER * chunk_a :])
    normed_t, turned_a = lax.optimization_barrier((normed_t, turned_a))
    parts_b = call(
        qkv_grads_kernel,
        scalars,
        (normed_t, normed_t_got, *kept_b, *got_b),
        [whole()] * (2 + 2 * mols),
        [((INNER * chunk_b, width), BF16)] * 4 + [((small_b, width), F32)],
        scratch=[
            pltpu.VMEM((2, dim, width), BF16),
            pltpu.VMEM((dim, 2 * rows), BF16),
            pltpu.VMEM((2 * rows, width), BF16),
        ],
        micros=4,
    )
    steps_b = plane_step(parts_b[:4])
    mine_a, narrow_a = line_step(*turned_a, *steps_b)
    grad_middle = after(grad_middle, parts_b[0])
    grad_features, small_own = call(
        embed_back_kernel,
        scalars,
        (
            *kept_b, *sent_b, dv_own, dv_got, w_query, w_key, w_value, wq_got, wk_got, wv_got, ident, w_ident,
            grad_middle, pinned(vecs), features,
        ),
        [whole()] * (12 + 2 * mols) + [half_rows(dim)],
        [((rows, dim), F32), ((small_b, width), F32)],
        scratch=[
            pltpu.VMEM((rows, dim), F32),
            pltpu.VMEM((idw + 8, dim), F32),
            pltpu.VMEM((rows, width), BF16),
        ],
        micros=7,
        local=False,
    )
    late = added(small_own, parts_b[4]).astype(BF16)
    turned_b = plane_turn(*steps_b, late)
    line_a = line_back(mine_a, *turned_b)
    wide_a = widened(narrow_a)
    mine_b, small_b_sum = line_step(*turned_b)
    side_ax, side_ay, _ = plane_back(line_a)
    line_b = line_back(mine_b)
    far_a = plane_back_turn(side_ax, side_ay)
    planes_a = (line_a, side_ax, side_ay, *far_a)
    line_b, far_a = lax.optimization_barrier((line_b, far_a))
    side_bx, side_by, narrow_b = plane_back(line_b, small_b_sum)
    far_b = plane_back_turn(side_bx, side_by)
    wide_b_rows = idw + 4
    both_b = narrow_b[: 2 * wide_b_rows]
    both_b = both_b + swap(both_b)
    wide_b = jnp.concatenate([both_b[:wide_b_rows], both_b[wide_b_rows:]], axis=1)
    planes_b = (line_b, side_bx, side_by, *far_b)

    grad_w_up, grad_w_value, grad_w_out, grad_w_down = placed(planes_a, 2, 2)
    grad_w_query, grad_w_key = placed(planes_b, 2, 0)
    return (
        result,
        grad_features,
        wide_b[:idw],
        wide_b[idw : idw + 2],
        wide_b[idw + 2],
        wide_b[idw + 3],
        grad_w_query,
        grad_w_key,
        grad_w_value,
        narrow_b[2 * wide_b_rows],
        narrow_a[5],
        grad_w_out,
        wide_a[0],
        wide_a[1],
        wide_a[2],
        grad_w_up,
        narrow_a[4],
        grad_w_down,
        wide_a[3],
    )


def solution(mesh):
    token, split = P("dp", None), P(("dp", "mp"), None)
    columns, lines, cut, copy = P(None, "mp"), P("mp", None), P("mp"), P()
    return jax.shard_map(
        per_device,
        mesh=mesh,
        in_specs=(
            token, token, P("dp"), P("dp"), token, copy, copy, copy, copy, columns, columns,
            columns, cut, cut, lines, copy, copy, copy, columns, cut, lines, copy, token,
        ),
        out_specs=(
            split, split, copy, copy, copy, copy, columns, columns, columns, cut, cut, lines,
            copy, copy, copy, columns, cut, lines, copy,
        ),
        check_vma=False,
    )
```

```python
import math

import jax
import jax.numpy as jnp
from jax import lax
from jax.experimental import pallas as pl
from jax.experimental.pallas import tpu as pltpu
from jax.sharding import PartitionSpec as P

HDIM = 24
SEQ = 128
LANES = 128
INNER = 4
OUTER = 4
EPSILON = 1e-05
SCALE = 1.0 / math.sqrt(HDIM)
F32, BF16 = jnp.float32, jnp.bfloat16
MIB = 1024 * 1024


def dot(left, right):
    return jnp.dot(left, right, preferred_element_type=F32)


def dot_nt(left, right):
    return lax.dot_general(left, right, (((1,), (1,)), ((), ())), preferred_element_type=F32)


def dot_tn(left, right):
    return lax.dot_general(left, right, (((0,), (0,)), ((), ())), preferred_element_type=F32)


def norm_parts(hidden):
    average = jnp.mean(hidden, axis=-1, keepdims=True)
    centred = hidden - average
    inverse = lax.rsqrt(jnp.mean(centred * centred, axis=-1, keepdims=True) + EPSILON)
    return centred * inverse, inverse


def norm_back(unit, inverse, grad_hat):
    return inverse * (
        grad_hat
        - jnp.mean(grad_hat, axis=-1, keepdims=True)
        - unit * jnp.mean(grad_hat * unit, axis=-1, keepdims=True)
    )


def row_sum(block):
    return jnp.sum(block, axis=0, keepdims=True)


def positions(length):
    return lax.broadcasted_iota(jnp.int32, (length, 1), 0)


def whole():
    return pl.BlockSpec(memory_space=pltpu.VMEM)


def outside():
    return pl.BlockSpec(memory_space=pltpu.HBM)


def node_count(info, m):
    return info[3 + m]


def slot_count(info, m):
    return info[3 + m] + info[3 + (info.shape[0] - 3) // 2 + m]


def call(kernel, scalars, args, specs, outs, scratch=(), micros=5, limit=24, local=True):
    return pl.pallas_call(
        kernel,
        out_shape=[jax.ShapeDtypeStruct(shape, kind) for shape, kind in outs],
        grid_spec=pltpu.PrefetchScalarGridSpec(
            num_scalar_prefetch=len(scalars),
            grid=(1,),
            in_specs=specs,
            out_specs=[whole() for _ in outs],
            scratch_shapes=list(scratch),
        ),
        compiler_params=pltpu.CompilerParams(vmem_limit_bytes=limit * MIB),
        cost_estimate=pl.CostEstimate(
            flops=1 if local else micros * 1_000_000_000,
            bytes_accessed=1 if local else 0,
            transcendentals=0,
        ),
    )(*scalars, *args)


def head_windows(width):
    windows = []
    for pair in range(width // (2 * HDIM)):
        low = pair * 2 * HDIM // LANES * LANES
        high = -(-(pair + 1) * 2 * HDIM // LANES) * LANES
        windows.append((low, high))
    return windows


def split_heads(block, pair, window):
    low, high = window
    part = block[:, low:high]
    column = low + lax.broadcasted_iota(jnp.int32, (16, high - low), 1)
    sides = []
    for head in (2 * pair, 2 * pair + 1):
        inside = (column >= head * HDIM) & (column < (head + 1) * HDIM)
        mask = jnp.where(inside, 1.0, 0.0).astype(BF16)
        sides.append(part * jnp.concatenate([mask] * (block.shape[0] // 16), axis=0))
    return jnp.concatenate(sides, axis=0)


def embed_rows(feats, lap, ends, w_ident, vecs, at, count):
    table = lap[:, at]
    slot = lax.broadcasted_iota(jnp.int32, (SEQ, SEQ), 0)
    picked = []
    for end in (0, 1):
        pick = jnp.where(ends[end : end + 1, at] == slot, 1.0, 0.0).astype(BF16)
        picked.append(dot(table, pick))
    ident = jnp.concatenate(picked, axis=0).astype(BF16)
    hidden = feats[at, :].astype(F32) + dot_tn(ident, w_ident[...])
    hidden = hidden + jnp.where(positions(SEQ) >= count, vecs[1:2, :], vecs[0:1, :])
    unit, _ = norm_parts(hidden)
    return hidden, ident, (unit * vecs[2:3, :] + vecs[3:4, :]).astype(BF16)


def embed_kernel(
    info, feats_in, lap_in, ends_in, w_ident_in, vecs_in, biases_in, wq_in, wk_in, wv_in,
    hidden_out, ident_out, normed_out, normed_t_out, q_out, k_out, v_out,
    feats, lap, ends, w_ident, vecs, biases, w_q, w_k, w_v, sems,
):
    rows, dim = feats.shape
    mols = rows // SEQ
    own_rows = pl.ds(pl.multiple_of(info[0] * rows, SEQ), rows)
    moves = (
        (ends_in.at[:, own_rows], ends),
        (lap_in.at[:, own_rows], lap),
        (w_ident_in, w_ident),
        (vecs_in, vecs),
        (feats_in.at[own_rows, :], feats),
        (biases_in, biases),
        (wq_in, w_q),
        (wk_in, w_k),
        (wv_in, w_v),
    )
    copies = [
        pltpu.make_async_copy(source, target, sems.at[place])
        for place, (source, target) in enumerate(moves)
    ]
    for copy in copies:
        copy.start()
    for copy in copies[:6]:
        copy.wait()

    def molecule(m, carry):
        at = pl.ds(pl.multiple_of(m * SEQ, SEQ), SEQ)
        count = node_count(info, info[0] * mols + m)
        hidden, ident, normed = embed_rows(feats, lap, ends, w_ident, vecs, at, count)
        ident_out[:, at] = ident
        hidden_out[at, :] = hidden
        normed_out[at, :] = normed
        normed_t_out[:, at] = normed.T
        return carry

    lax.fori_loop(0, mols, molecule, 0)
    normed = normed_out[...]
    copies[6].wait()
    q_out[...] = (dot(normed, w_q[...]) + biases[0:1, :]).astype(BF16)
    copies[7].wait()
    k_out[...] = dot(normed, w_k[...]).astype(BF16)
    copies[8].wait()
    v_out[...] = (dot(normed, w_v[...]) + biases[1:2, :]).astype(BF16)


def forward_kernel(
    info, hidden, normed, q_own, k_own, v_own, w_q, w_k, w_v,
    wo_own, wo, wu_own, wu, wd_own, wd, vecs, biases_own, biases, cots,
    q_out, k_out, v_out, probs_out, keep_out, send_out, middle, active, gm_out,
    ga_own_out, ga_out, dv_own_out, dv_out,
    mixed, attended, unit, normed_two, slope, grad_ffn, grad_branch, dv,
):
    rows, dim = hidden.shape
    width = q_own.shape[1]
    mols = rows // SEQ
    pairs = width // (2 * HDIM)
    windows = head_windows(width)
    own_core = info[0]

    q_out[...] = (dot(normed[...], w_q[...]) + biases[0:1, :]).astype(BF16)
    k_out[...] = dot(normed[...], w_k[...]).astype(BF16)
    v_out[...] = (dot(normed[...], w_v[...]) + biases[1:2, :]).astype(BF16)

    def attend(m, carry):
        at = pl.ds(pl.multiple_of(m * SEQ, SEQ), SEQ)
        place = own_core * mols + m
        count = slot_count(info, place)
        key_keep = positions(SEQ) < count
        query_keep = lax.broadcasted_iota(jnp.int32, (1, SEQ), 1) < count
        sides = ((q_own, k_own, v_own, keep_out), (q_out, k_out, v_out, send_out))
        for side, (q_ref, k_ref, v_ref, part_out) in enumerate(sides):
            queries, key_rows = q_ref[at, :], k_ref[at, :]
            values_t = v_ref[at, :].T
            for pair in range(pairs):
                low, high = windows[pair]
                both = split_heads(queries, pair, windows[pair])
                scores = dot_nt(key_rows[:, low:high], both) * SCALE
                scores = jnp.where(key_keep, scores, -1e30)
                top = jnp.max(scores, axis=0, keepdims=True)
                raised = jnp.exp(scores - top)
                total = row_sum(raised)
                probs = (raised * (1.0 / total)).astype(BF16)
                probs_out[m, side * pairs + pair] = probs
                first = pair * 2 * HDIM
                out = dot(values_t[first : first + 2 * HDIM], probs)
                mixed[first : first + HDIM, :] = out[:HDIM, :SEQ]
                mixed[first + HDIM : first + 2 * HDIM, :] = out[HDIM:, SEQ:]
            kept = jnp.where(query_keep, mixed[...], 0.0).astype(BF16)
            part_out[dim : dim + width, at] = kept
            attended[at, side * width : (side + 1) * width] = kept.T
        return carry

    lax.fori_loop(0, mols, attend, 0)
    middle[...] = (
        hidden[...] + dot(attended[:, :width], wo_own[...]) + dot(attended[:, width:], wo[...])
    )

    def second_norm(m, carry):
        at = pl.ds(pl.multiple_of(m * SEQ, SEQ), SEQ)
        place = own_core * mols + m
        keep = positions(SEQ) < slot_count(info, place)
        total = middle[at, :] + vecs[4:5, :]
        middle[at, :] = total
        unit_rows, _ = norm_parts(total)
        unit[at, :] = unit_rows
        rows_two = (unit_rows * vecs[5:6, :] + vecs[6:7, :]).astype(BF16)
        normed_two[at, :] = rows_two
        turned = rows_two.T
        keep_out[:dim, at] = turned
        send_out[:dim, at] = turned
        grad_ffn[at, :] = jnp.where(keep, cots[at, :].astype(F32), 0.0).astype(BF16)
        return carry

    lax.fori_loop(0, mols, second_norm, 0)

    for side, (w_ref, b_ref, part_out) in enumerate(
        ((wu_own, biases_own, keep_out), (wu, biases, send_out))
    ):
        columns = slice(side * width, (side + 1) * width)
        slope[:, columns] = dot(normed_two[...], w_ref[...]) + b_ref[2:3, :]

        def activate(m, carry):
            at = pl.ds(pl.multiple_of(m * SEQ, SEQ), SEQ)
            before = slope[at, columns]
            phi = 0.5 * (1.0 + lax.erf(before * math.sqrt(0.5)))
            out = (before * phi).astype(BF16)
            slope[at, columns] = phi + before * jnp.exp(before * before * -0.5) * (
                1.0 / math.sqrt(2.0 * math.pi)
            )
            active[at, columns] = out
            part_out[dim + width : dim + 2 * width, at] = out.T
            return carry

        lax.fori_loop(0, mols, activate, 0)

    place_b = dim + 2 * width
    for side, (w_ref, part_out) in enumerate(((wd_own, keep_out), (wd, send_out))):
        columns = slice(side * width, (side + 1) * width)
        grad_before = slope[:, columns] * dot_nt(grad_ffn[...], w_ref[...])
        part_out[place_b : place_b + rows, :] = grad_before.astype(BF16)

    back = pl.ds(place_b, rows)
    gm_out[...] = dot_nt(keep_out[back, :], wu_own[...]) + dot_nt(send_out[back, :], wu[...])

    def second_back(m, sums):
        at = pl.ds(pl.multiple_of(m * SEQ, SEQ), SEQ)
        place = own_core * mols + m
        keep = positions(SEQ) < slot_count(info, place)
        grad_normed = gm_out[at, :]
        unit_rows = unit[at, :]
        _, inverse = norm_parts(middle[at, :])
        grad_result = jnp.where(keep, cots[at, :].astype(F32), 0.0)
        grad = grad_result + norm_back(unit_rows, inverse, grad_normed * vecs[5:6, :])
        gm_out[at, :] = grad
        grad_branch[at, :] = grad.astype(BF16)
        return (
            sums[0] + row_sum(grad),
            sums[1] + row_sum(grad_normed * unit_rows),
            sums[2] + row_sum(grad_normed),
            sums[3] + row_sum(grad_result),
        )

    nothing = jnp.zeros((1, dim), F32)
    sums = lax.fori_loop(0, mols, second_back, (nothing,) * 4)
    place_m = place_b + rows
    for part_out in (keep_out, send_out):
        part_out[place_m : place_m + rows, :] = grad_branch[:, :width]
        part_out[place_m + rows : place_m + 2 * rows, :] = grad_branch[:, width:]
    small = jnp.concatenate(list(sums) + [nothing] * 12, axis=0)
    left, right = small[:, :width], small[:, width:]
    place_v = place_m + 2 * rows
    place_s = place_v + rows
    keep_out[place_s:, :] = jnp.where(own_core == 0, left, right).astype(BF16)
    send_out[place_s:, :] = jnp.where(own_core == 0, right, left).astype(BF16)

    sides = ((ga_own_out, wo_own, dv_own_out, keep_out), (ga_out, wo, dv_out, send_out))
    for ref, weight, _, _ in sides:
        product = dot_nt(grad_branch[...], weight[...])
        for m in range(mols):
            place = own_core * mols + m
            keep = positions(SEQ) < slot_count(info, place)
            at = slice(m * SEQ, (m + 1) * SEQ)
            ref[at, :] = jnp.where(keep, product[at], 0.0).astype(BF16)

    def value_back(m, carry):
        base = pl.multiple_of(m * SEQ, SEQ)
        at = pl.ds(base, SEQ)
        for side, (ref, _, out, part_out) in enumerate(sides):
            grads = ref[at, :]
            dv[side] = jnp.zeros_like(dv[side])
            for pair in range(pairs):
                low, high = windows[pair]
                both = split_heads(grads, pair, windows[pair])
                dv[side, :, low:high] += dot(probs_out[m, side * pairs + pair], both)
            total = dv[side].astype(BF16)
            out[at, :] = total
            part_out[pl.ds(base + place_v, SEQ), :] = total
        return carry

    lax.fori_loop(0, mols, value_back, 0)


def result_kernel(
    info, middle, active, wd_own, wd, w_ident, vecs, feats, lap, ends, result_out, normed_t_out
):
    width = wd.shape[0]
    mols = middle.shape[0] // SEQ
    result_out[...] = (
        middle[...]
        + dot(active[:, :width], wd_own[...])
        + dot(active[:, width:], wd[...])
        + vecs[7:8, :]
    ).astype(BF16)

    def molecule(m, carry):
        at = pl.ds(pl.multiple_of(m * SEQ, SEQ), SEQ)
        count = node_count(info, (1 - info[0]) * mols + m)
        normed_t_out[:, at] = embed_rows(feats, lap, ends, w_ident, vecs, at, count)[2].T
        return carry

    lax.fori_loop(0, mols, molecule, 0)


def attend_back_kernel(
    m, info, q_own, k_own, v_own, ga_own, q_got, k_got, v_got, ga_got, probs_all,
    keep_out, send_out, dq_t, dk,
):
    width = q_own.shape[1]
    pairs = width // (2 * HDIM)
    windows = head_windows(width)
    at = slice(m * SEQ, (m + 1) * SEQ)
    sides = (
        (q_own, k_own, v_own, ga_own, keep_out),
        (q_got, k_got, v_got, ga_got, send_out),
    )
    for side, (q_ref, k_ref, v_ref, g_ref, part_out) in enumerate(sides):
        queries, key_rows, values, grads = q_ref[at, :], k_ref[at, :], v_ref[at, :], g_ref[at, :]
        keys_t = key_rows.T
        dk[side] = jnp.zeros_like(dk[side])
        for pair in range(pairs):
            low, high = windows[pair]
            both_q = split_heads(queries, pair, windows[pair])
            both_g = split_heads(grads, pair, windows[pair])
            probs = probs_all[m, side * pairs + pair].astype(F32)
            grad_probs = dot_nt(values[:, low:high], both_g)
            inner = row_sum(probs * grad_probs)
            grad_scores = (probs * (grad_probs - inner)).astype(BF16)
            dk[side, :, low:high] += dot(grad_scores, both_q)
            first = pair * 2 * HDIM
            out = dot(keys_t[first : first + 2 * HDIM], grad_scores)
            dq_t[side, first : first + HDIM, :] = out[:HDIM, :SEQ]
            dq_t[side, first + HDIM : first + 2 * HDIM, :] = out[HDIM:, SEQ:]
        part_out[:SEQ, :] = (dq_t[side] * SCALE).astype(BF16).T
        part_out[SEQ:, :] = (dk[side] * SCALE).astype(BF16)


def embed_back_kernel(
    info, *refs,
):
    mols = len(refs[:-18]) // 2
    grads_own, grads = refs[:mols], refs[mols : 2 * mols]
    (
        dv_own, dv,
        wq_own, wk_own, wv_own, w_q, w_k, w_v, ident, w_ident, grad_middle, vecs, feats,
        features_out, small_out, grad_normed, small, stacked,
    ) = refs[2 * mols :]
    rows, dim = feats.shape
    width = wq_own.shape[1]
    own_core = info[0]
    idw = ident.shape[0]
    total = None
    for part, values, weights in (
        (grads_own, dv_own, (wq_own, wk_own, wv_own)),
        (grads, dv, (w_q, w_k, w_v)),
    ):
        term = dot_nt(values[...], weights[2][...])
        total = term if total is None else total + term
        for place, weight in enumerate(weights[:2]):
            for m in range(mols):
                stacked[m * SEQ : (m + 1) * SEQ, :] = part[m][place * SEQ : (place + 1) * SEQ, :]
            total = total + dot_nt(stacked[...], weight[...])
    grad_normed[...] = total
    small[...] = jnp.zeros_like(small)

    def molecule(m, carry):
        at = pl.ds(pl.multiple_of(m * SEQ, SEQ), SEQ)
        is_edge = positions(SEQ) >= node_count(info, own_core * mols + m)
        hidden = feats[at, :].astype(F32) + dot_tn(ident[:, at], w_ident[...])
        hidden = hidden + jnp.where(is_edge, vecs[1:2, :], vecs[0:1, :])
        unit, inverse = norm_parts(hidden)
        grad_rows = grad_normed[at, :]
        grad = grad_middle[at, :] + norm_back(unit, inverse, grad_rows * vecs[2:3, :])
        features_out[at, :] = grad
        high = grad.astype(BF16)
        rest = (grad - high.astype(F32)).astype(BF16)
        picked = ident[:, at]
        small[:idw, :] += dot(picked, high) + dot(picked, rest)
        edge_rows = jnp.where(is_edge, grad, 0.0)
        small[idw : idw + 1, :] += row_sum(grad - edge_rows)
        small[idw + 1 : idw + 2, :] += row_sum(edge_rows)
        small[idw + 2 : idw + 3, :] += row_sum(grad_rows * unit)
        small[idw + 3 : idw + 4, :] += row_sum(grad_rows)
        return carry

    lax.fori_loop(0, mols, molecule, 0)
    count = idw + 4
    small_out[...] = jnp.zeros_like(small_out)
    small_out[:count, :] = small[:count, :width]
    small_out[count : 2 * count, :] = small[:count, width:]


def deal(info, unit, places, outs, block_at, small):
    inner = info[1]
    first_kept, first_sent, second_kept, second_sent = outs
    for step in range(INNER):
        for z in range(OUTER):
            if z < 2:
                out, slot = (first_sent if step % 2 else first_kept), step // 2
            else:
                out, slot = (second_sent if step // 2 else second_kept), step % 2
            start = (slot * 2 + z % 2) * places * unit
            for place in range(places):
                out[start + place * unit : start + (place + 1) * unit, :] = block_at(
                    inner ^ step, z, place
                )
    if small is not None:
        for out in (first_kept, first_sent):
            out[INNER * places * unit :, :] = small


def ffn_grads_kernel(info, kept, got, cots, normed_t, normed_t_got, *rest):
    outs, (tall, flat, grad_ffn) = rest[:4], rest[4:]
    rows_all, dim = cots.shape
    rows, width = rows_all // 2, kept.shape[1]
    mols = rows // SEQ
    own_core = info[0]
    for m in range(2 * mols):
        keep = positions(SEQ) < slot_count(info, m)
        at = slice(m * SEQ, (m + 1) * SEQ)
        grad_ffn[at, :] = jnp.where(keep, cots[at, :].astype(F32), 0.0).astype(BF16)
    own_rows = pl.ds(pl.multiple_of(own_core * rows, SEQ), rows)
    other_rows = pl.ds(pl.multiple_of((1 - own_core) * rows, SEQ), rows)
    place_b = dim + 2 * width
    place_m = place_b + rows
    place_v = place_m + 2 * rows
    place_s = place_v + rows
    back, value = slice(place_b, place_m), slice(place_v, place_s)
    tall[1] = (
        dot(normed_t[...], kept[value, :]) + dot(normed_t_got[...], got[value, :])
    ).astype(BF16)
    tall[0] = (dot(kept[:dim, :], kept[back, :]) + dot(got[:dim, :], got[back, :])).astype(BF16)
    turned = slice(dim, dim + width)
    for half in (0, 1):
        mid = slice(place_m + half * rows, place_m + (half + 1) * rows)
        flat[half] = (
            dot(kept[turned, :], kept[mid, :]) + dot(got[turned, :], got[mid, :])
        ).astype(BF16)
    turned = slice(dim + width, dim + 2 * width)
    for half in (0, 1):
        columns = slice(half * width, (half + 1) * width)
        product = dot(kept[turned, :], grad_ffn[own_rows, columns])
        product = product + dot(got[turned, :], grad_ffn[other_rows, columns])
        flat[2 + half] = product.astype(BF16)
    small = kept[place_s:, :].astype(F32) + got[place_s:, :].astype(F32)
    spot = lax.broadcasted_iota(jnp.int32, small.shape, 0)
    for row, part in ((4, back), (5, value)):
        bias = row_sum(kept[part, :].astype(F32)) + row_sum(got[part, :].astype(F32))
        small = jnp.where(spot == row, bias, small)
    small = small.astype(BF16)
    unit = dim // (INNER * OUTER)

    def block_at(dest, z, place):
        if place < 2:
            return tall[place, pl.ds(pl.multiple_of((dest * OUTER + z) * unit, 16), unit), :]
        row = pl.multiple_of((dest * (OUTER // 2) + z // 2) * unit, 16)
        return flat[2 * (place - 2) + z % 2, pl.ds(row, unit), :]

    deal(info, unit, 4, outs, block_at, small)


def qkv_grads_kernel(info, normed_t, normed_t_got, *refs):
    mols = normed_t.shape[1] // SEQ
    kept, got = refs[:mols], refs[mols : 2 * mols]
    outs, small_out = refs[2 * mols : 2 * mols + 4], refs[2 * mols + 4]
    tall, normed, stacked = refs[2 * mols + 5 :]
    dim, rows = normed_t.shape
    unit = dim // (INNER * OUTER)
    normed[:, :rows] = normed_t[...]
    normed[:, rows:] = normed_t_got[...]
    spot = lax.broadcasted_iota(jnp.int32, small_out.shape, 0)
    small = jnp.zeros(small_out.shape, F32)
    for place in range(2):
        for m, part in enumerate(kept + got):
            stacked[m * SEQ : (m + 1) * SEQ, :] = part[place * SEQ : (place + 1) * SEQ, :]
        tall[place] = dot(normed[...], stacked[...]).astype(BF16)
        if place == 0:
            small = jnp.where(spot == 72, row_sum(stacked[...].astype(F32)), small)
    small_out[...] = small

    def block_at(dest, z, place):
        return tall[place, pl.ds(pl.multiple_of((dest * OUTER + z) * unit, 16), unit), :]

    deal(info, unit, 2, outs, block_at, None)


def place_kernel(flat_from, info, own, side_x, side_y, far_first, far_second, *outs):
    inner = info[1]
    places = len(outs)
    unit = own.shape[0] // (places * OUTER)
    width = own.shape[1]
    for step in range(INNER):
        for z in range(OUTER):
            ref, start = (own, side_x, side_y, far_first)[step], z * places * unit
            if step == 3 and z >= 2:
                ref, start = far_second, (z - 2) * places * unit
            dest = inner ^ step
            tall = pl.ds(pl.multiple_of((dest * OUTER + z) * unit, 16), unit)
            flat = pl.ds(pl.multiple_of((dest * (OUTER // 2) + z // 2) * unit, 16), unit)
            columns = slice(z % 2 * width, (z % 2 + 1) * width)
            for place in range(places):
                part = ref[start + place * unit : start + (place + 1) * unit, :].astype(F32)
                if place >= flat_from:
                    outs[place][flat, columns] = part
                else:
                    outs[place][tall, :] = part


def per_device(
    features, lap_vectors, node_counts, edge_counts, endpoints, w_ident, type_table,
    gain_one, shift_one, w_query, w_key, w_value, bias_query, bias_value, w_out, bias_out,
    gain_two, shift_two, w_up, bias_up, w_down, bias_down, cotangent,
):
    dp_count = lax.axis_size("dp")
    dp_index = lax.axis_index("dp")
    mp_index = lax.axis_index("mp")
    block = INNER * OUTER
    rest_count = dp_count // block
    place = jnp.stack([mp_index, dp_index % INNER, dp_index // INNER % OUTER]).astype(jnp.int32)
    info = jnp.concatenate([place, node_counts, edge_counts])

    def swap(part):
        return lax.ppermute(part, "mp", [(0, 1), (1, 0)])

    def inner_move(part, step):
        return lax.ppermute(part, "dp", [(s, s ^ step) for s in range(dp_count)])

    lines = [
        [r * block + z * INNER + i for z in range(OUTER)]
        for r in range(rest_count) for i in range(INNER)
    ]

    def line_move(part):
        return lax.all_to_all(part, "dp", 0, 0, axis_index_groups=lines)

    rows_all, dim = features.shape
    rows = rows_all // 2
    mols = rows // SEQ
    width = w_query.shape[1]
    heads = width // HDIM
    lapk = lap_vectors.shape[1]
    idw = w_ident.shape[0]
    scalars = (info,)
    half_rows = lambda columns: pl.BlockSpec((rows, columns), lambda g, info: (info[0], 0))

    def table_of(rows_of, start):
        spot = lax.broadcasted_iota(jnp.int32, (8, 1), 0)
        for place, row in enumerate(rows_of):
            start = jnp.where(spot == place, row[None], start) if row is not None else start
        return start.astype(F32)

    def pinned(part):
        return pltpu.with_memory_space_constraint(part, pltpu.HBM)

    biases = table_of([bias_query, bias_value, bias_up], jnp.zeros((8, width), BF16))
    vecs = table_of(
        [None, None, gain_one, shift_one, bias_out, gain_two, shift_two, bias_down],
        jnp.pad(type_table, ((0, 6), (0, 0))),
    )

    wq_got, wk_got, wv_got = swap(w_query), swap(w_key), swap(w_value)
    biases_got = swap(biases)
    wo_got, wu_got, wd_got = swap(w_out), swap(w_up), swap(w_down)

    hidden, ident, normed, normed_t, q_own, k_own, v_own = call(
        embed_kernel,
        scalars,
        tuple(
            pinned(part)
            for part in (
                features, lap_vectors.T, endpoints.T, w_ident, vecs, biases,
                w_query, w_key, w_value,
            )
        ),
        [outside()] * 9,
        [
            ((rows, dim), F32),
            ((idw, rows), BF16),
            ((rows, dim), BF16),
            ((dim, rows), BF16),
            ((rows, width), BF16),
            ((rows, width), BF16),
            ((rows, width), BF16),
        ],
        scratch=[
            pltpu.VMEM((rows, dim), BF16),
            pltpu.VMEM((lapk, rows), BF16),
            pltpu.VMEM((2, rows), jnp.int32),
            pltpu.VMEM((idw, dim), BF16),
            pltpu.VMEM((8, dim), F32),
            pltpu.VMEM((8, width), F32),
            pltpu.VMEM((dim, width), BF16),
            pltpu.VMEM((dim, width), BF16),
            pltpu.VMEM((dim, width), BF16),
            pltpu.SemaphoreType.DMA((9,)),
        ],
        micros=6,
        local=False,
    )
    sent_rows = dim + 2 * width + 4 * rows + 16
    (
        q_got, k_got, v_got, probs, kept_a, sent_a, middle, active, grad_middle,
        ga_own, ga_got, dv_own, dv_got,
    ) = call(
        forward_kernel,
        scalars,
        (
            hidden, normed, q_own, k_own, v_own, wq_got, wk_got, wv_got,
            w_out, wo_got, w_up, wu_got, w_down, wd_got, pinned(vecs), pinned(biases),
            biases_got, cotangent,
        ),
        [whole()] * 17 + [half_rows(dim)],
        [
            ((rows, width), BF16),
            ((rows, width), BF16),
            ((rows, width), BF16),
            ((mols, heads, SEQ, 2 * SEQ), BF16),
            ((sent_rows, width), BF16),
            ((sent_rows, width), BF16),
            ((rows, dim), F32),
            ((rows, dim), BF16),
            ((rows, dim), F32),
            ((rows, width), BF16),
            ((rows, width), BF16),
            ((rows, width), BF16),
            ((rows, width), BF16),
        ],
        scratch=[
            pltpu.VMEM((width, SEQ), F32),
            pltpu.VMEM((rows, dim), BF16),
            pltpu.VMEM((rows, dim), F32),
            pltpu.VMEM((rows, dim), BF16),
            pltpu.VMEM((rows, dim), F32),
            pltpu.VMEM((rows, dim), BF16),
            pltpu.VMEM((rows, dim), BF16),
            pltpu.VMEM((2, SEQ, width), F32),
        ],
        micros=20,
        limit=30,
    )
    got_a = swap(sent_a)
    other_rows = lambda columns: pl.BlockSpec((rows, columns), lambda g, info: (1 - info[0], 0))
    other_columns = lambda count: pl.BlockSpec((count, rows), lambda g, info: (0, 1 - info[0]))
    result, normed_t_got = call(
        result_kernel,
        scalars,
        (
            middle, active, w_down, wd_got, w_ident, pinned(vecs),
            features, lap_vectors.T, endpoints.T,
        ),
        [whole()] * 6 + [other_rows(dim), other_columns(lapk), other_columns(2)],
        [((rows, dim), BF16), ((dim, rows), BF16)],
        micros=4,
    )

    unit = dim // block
    chunk_a, chunk_b = 4 * unit, 2 * unit
    small_a, small_b = 16, 80

    def rest_sum(part):
        if rest_count == 1:
            return part
        groups = [[r * block + s for r in range(rest_count)] for s in range(block)]
        return lax.psum(part.astype(F32), "dp", axis_index_groups=groups).astype(part.dtype)

    def added(*parts):
        return sum(part.astype(F32) for part in parts)

    def after(part, *others):
        return lax.optimization_barrier((part, *others))[0]

    def plane_step(parts):
        first_kept, first_sent, second_kept, second_sent = parts
        first = added(first_kept, inner_move(first_sent, 1)).astype(BF16)
        second = added(second_kept, inner_move(second_sent, 2)).astype(BF16)
        return first, second

    def plane_turn(first, second, small, *others):
        pair = second.shape[0] // 2
        sent = jnp.concatenate([first[pair : 2 * pair], small])
        got = after(inner_move(sent, 2), *others)
        first = added(jnp.concatenate([first[:pair], small]), got).astype(BF16)
        got = after(inner_move(second[pair : 2 * pair], 1), *others)
        return first, added(second[:pair], got).astype(BF16)

    def line_step(first, second, *others):
        chunk = second.shape[0] // 2
        small = first[2 * chunk :]
        sent = jnp.stack(
            [
                jnp.concatenate([half[z * chunk : (z + 1) * chunk], small])
                for half in (first, second) for z in (0, 1)
            ]
        )
        got = after(line_move(sent), *others)
        total = jnp.sum(got.astype(F32), axis=0)
        return rest_sum(total[:chunk].astype(BF16)), rest_sum(total[chunk:])

    def line_back(mine, *others):
        got = line_move(jnp.broadcast_to(mine[None], (OUTER, *mine.shape)))
        return after(got, *others).reshape(OUTER * mine.shape[0], width)

    def plane_back(line, small=None):
        if small is None:
            side_x = inner_move(line, 1)
        else:
            side_x = inner_move(jnp.concatenate([line, small.astype(BF16)]), 1)
            small = added(small.astype(BF16), side_x[line.shape[0] :])
            side_x = side_x[: line.shape[0]]
        return side_x, inner_move(line, 2), small

    def plane_back_turn(side_x, side_y):
        pair = side_x.shape[0] // 2
        return inner_move(side_y[:pair], 1), inner_move(side_x[pair:], 2)

    def widened(small):
        small_got = swap(small)
        return jnp.where(
            mp_index == 0,
            jnp.concatenate([small, small_got], axis=1),
            jnp.concatenate([small_got, small], axis=1),
        )

    def placed(planes, tall, flat):
        return call(
            lambda *refs: place_kernel(tall, *refs),
            (info,),
            planes,
            [whole()] * 5,
            [((dim, width), F32)] * tall + [((width, dim), F32)] * flat,
            micros=3,
        )

    kept_a, result, normed_t_got = lax.optimization_barrier((kept_a, result, normed_t_got))
    parts_a = call(
        ffn_grads_kernel,
        scalars,
        (kept_a, got_a, cotangent, normed_t, normed_t_got),
        [whole()] * 5,
        [
            ((INNER * chunk_a + small_a, width), BF16),
            ((INNER * chunk_a + small_a, width), BF16),
            ((INNER * chunk_a, width), BF16),
            ((INNER * chunk_a, width), BF16),
        ],
        scratch=[
            pltpu.VMEM((2, dim, width), BF16),
            pltpu.VMEM((4, width, width), BF16),
            pltpu.VMEM((rows_all, dim), BF16),
        ],
        micros=6,
    )
    q_own = after(q_own, parts_a[0])
    steps_a = plane_step(parts_a)
    kept_b, got_b, sent_b = [], [], []
    for m in range(mols):
        if m == 2:
            q_own, steps_a = lax.optimization_barrier((q_own, steps_a))
        kept, sent = call(
            lambda *refs, m=m: attend_back_kernel(m, *refs),
            scalars,
            (q_own, k_own, v_own, ga_own, q_got, k_got, v_got, ga_got, probs),
            [whole()] * 9,
            [((2 * SEQ, width), BF16)] * 2,
            scratch=[
                pltpu.VMEM((2, width, SEQ), F32),
                pltpu.VMEM((2, SEQ, width), F32),
            ],
            micros=4,
        )
        kept_b.append(kept)
        sent_b.append(sent)
        got_b.append(swap(sent))
        q_own, q_got, _ = lax.optimization_barrier((q_own, q_got, kept))

    turned_a = plane_turn(*steps_a, steps_a[0][INNER * chunk_a :])
    normed_t, turned_a = lax.optimization_barrier((normed_t, turned_a))
    parts_b = call(
        qkv_grads_kernel,
        scalars,
        (normed_t, normed_t_got, *kept_b, *got_b),
        [whole()] * (2 + 2 * mols),
        [((INNER * chunk_b, width), BF16)] * 4 + [((small_b, width), F32)],
        scratch=[
            pltpu.VMEM((2, dim, width), BF16),
            pltpu.VMEM((dim, 2 * rows), BF16),
            pltpu.VMEM((2 * rows, width), BF16),
        ],
        micros=4,
    )
    steps_b = plane_step(parts_b[:4])
    mine_a, narrow_a = line_step(*turned_a, *steps_b)
    grad_middle = after(grad_middle, parts_b[0])
    grad_features, small_own = call(
        embed_back_kernel,
        scalars,
        (
            *kept_b, *sent_b, dv_own, dv_got, w_query, w_key, w_value, wq_got, wk_got, wv_got, ident, w_ident,
            grad_middle, pinned(vecs), features,
        ),
        [whole()] * (12 + 2 * mols) + [half_rows(dim)],
        [((rows, dim), F32), ((small_b, width), F32)],
        scratch=[
            pltpu.VMEM((rows, dim), F32),
            pltpu.VMEM((idw + 8, dim), F32),
            pltpu.VMEM((rows, width), BF16),
        ],
        micros=7,
        local=False,
    )
    late = added(small_own, parts_b[4]).astype(BF16)
    turned_b = plane_turn(*steps_b, late)
    line_a = line_back(mine_a, *turned_b)
    wide_a = widened(narrow_a)
    mine_b, small_b_sum = line_step(*turned_b)
    side_ax, side_ay, _ = plane_back(line_a)
    line_b = line_back(mine_b)
    far_a = plane_back_turn(side_ax, side_ay)
    planes_a = (line_a, side_ax, side_ay, *far_a)
    line_b, far_a = lax.optimization_barrier((line_b, far_a))
    side_bx, side_by, narrow_b = plane_back(line_b, small_b_sum)
    far_b = plane_back_turn(side_bx, side_by)
    wide_b_rows = idw + 4
    both_b = narrow_b[: 2 * wide_b_rows]
    both_b = both_b + swap(both_b)
    wide_b = jnp.concatenate([both_b[:wide_b_rows], both_b[wide_b_rows:]], axis=1)
    planes_b = (line_b, side_bx, side_by, *far_b)

    grad_w_up, grad_w_value, grad_w_out, grad_w_down = placed(planes_a, 2, 2)
    grad_w_query, grad_w_key = placed(planes_b, 2, 0)
    return (
        result,
        grad_features,
        wide_b[:idw],
        wide_b[idw : idw + 2],
        wide_b[idw + 2],
        wide_b[idw + 3],
        grad_w_query,
        grad_w_key,
        grad_w_value,
        narrow_b[2 * wide_b_rows],
        narrow_a[5],
        grad_w_out,
        wide_a[0],
        wide_a[1],
        wide_a[2],
        grad_w_up,
        narrow_a[4],
        grad_w_down,
        wide_a[3],
    )


def solution(mesh):
    token, split = P("dp", None), P(("dp", "mp"), None)
    columns, lines, cut, copy = P(None, "mp"), P("mp", None), P("mp"), P()
    return jax.shard_map(
        per_device,
        mesh=mesh,
        in_specs=(
            token, token, P("dp"), P("dp"), token, copy, copy, copy, copy, columns, columns,
            columns, cut, cut, lines, copy, copy, copy, columns, cut, lines, copy, token,
        ),
        out_specs=(
            split, split, copy, copy, copy, copy, columns, columns, columns, cut, cut, lines,
            copy, copy, copy, columns, cut, lines, copy,
        ),
        check_vma=False,
    )
```

```python
import math

import jax
import jax.numpy as jnp
from jax import lax
from jax.experimental import pallas as pl
from jax.experimental.pallas import tpu as pltpu
from jax.sharding import PartitionSpec as P

HDIM = 24
SEQ = 128
LANES = 128
INNER = 4
OUTER = 4
EPSILON = 1e-05
SCALE = 1.0 / math.sqrt(HDIM)
F32, BF16 = jnp.float32, jnp.bfloat16
MIB = 1024 * 1024


def dot(left, right):
    return jnp.dot(left, right, preferred_element_type=F32)


def dot_nt(left, right):
    return lax.dot_general(left, right, (((1,), (1,)), ((), ())), preferred_element_type=F32)


def dot_tn(left, right):
    return lax.dot_general(left, right, (((0,), (0,)), ((), ())), preferred_element_type=F32)


def norm_parts(hidden):
    average = jnp.mean(hidden, axis=-1, keepdims=True)
    centred = hidden - average
    inverse = lax.rsqrt(jnp.mean(centred * centred, axis=-1, keepdims=True) + EPSILON)
    return centred * inverse, inverse


def norm_back(unit, inverse, grad_hat):
    return inverse * (
        grad_hat
        - jnp.mean(grad_hat, axis=-1, keepdims=True)
        - unit * jnp.mean(grad_hat * unit, axis=-1, keepdims=True)
    )


def row_sum(block):
    return jnp.sum(block, axis=0, keepdims=True)


def positions(length):
    return lax.broadcasted_iota(jnp.int32, (length, 1), 0)


def whole():
    return pl.BlockSpec(memory_space=pltpu.VMEM)


def outside():
    return pl.BlockSpec(memory_space=pltpu.HBM)


def node_count(info, m):
    return info[3 + m]


def slot_count(info, m):
    return info[3 + m] + info[3 + (info.shape[0] - 3) // 2 + m]


def call(kernel, scalars, args, specs, outs, scratch=(), micros=5, limit=24, local=True):
    return pl.pallas_call(
        kernel,
        out_shape=[jax.ShapeDtypeStruct(shape, kind) for shape, kind in outs],
        grid_spec=pltpu.PrefetchScalarGridSpec(
            num_scalar_prefetch=len(scalars),
            grid=(1,),
            in_specs=specs,
            out_specs=[whole() for _ in outs],
            scratch_shapes=list(scratch),
        ),
        compiler_params=pltpu.CompilerParams(vmem_limit_bytes=limit * MIB),
        cost_estimate=pl.CostEstimate(
            flops=1 if local else micros * 1_000_000_000,
            bytes_accessed=1 if local else 0,
            transcendentals=0,
        ),
    )(*scalars, *args)


def head_windows(width):
    windows = []
    for pair in range(width // (2 * HDIM)):
        low = pair * 2 * HDIM // LANES * LANES
        high = -(-(pair + 1) * 2 * HDIM // LANES) * LANES
        windows.append((low, high))
    return windows


def split_heads(block, pair, window):
    low, high = window
    part = block[:, low:high]
    column = low + lax.broadcasted_iota(jnp.int32, (16, high - low), 1)
    sides = []
    for head in (2 * pair, 2 * pair + 1):
        inside = (column >= head * HDIM) & (column < (head + 1) * HDIM)
        mask = jnp.where(inside, 1.0, 0.0).astype(BF16)
        sides.append(part * jnp.concatenate([mask] * (block.shape[0] // 16), axis=0))
    return jnp.concatenate(sides, axis=0)


def embed_rows(feats, lap, ends, w_ident, vecs, at, count):
    table = lap[:, at]
    slot = lax.broadcasted_iota(jnp.int32, (SEQ, SEQ), 0)
    picked = []
    for end in (0, 1):
        pick = jnp.where(ends[end : end + 1, at] == slot, 1.0, 0.0).astype(BF16)
        picked.append(dot(table, pick))
    ident = jnp.concatenate(picked, axis=0).astype(BF16)
    hidden = feats[at, :].astype(F32) + dot_tn(ident, w_ident[...])
    hidden = hidden + jnp.where(positions(SEQ) >= count, vecs[1:2, :], vecs[0:1, :])
    unit, _ = norm_parts(hidden)
    return hidden, ident, (unit * vecs[2:3, :] + vecs[3:4, :]).astype(BF16)


def embed_kernel(
    info, feats_in, lap_in, ends_in, w_ident_in, vecs_in, biases_in, wq_in, wk_in, wv_in,
    hidden_out, ident_out, normed_out, normed_t_out, q_out, k_out, v_out,
    feats, lap, ends, w_ident, vecs, biases, w_q, w_k, w_v, sems,
):
    rows, dim = feats.shape
    mols = rows // SEQ
    own_rows = pl.ds(pl.multiple_of(info[0] * rows, SEQ), rows)
    moves = (
        (ends_in.at[:, own_rows], ends),
        (lap_in.at[:, own_rows], lap),
        (w_ident_in, w_ident),
        (vecs_in, vecs),
        (feats_in.at[own_rows, :], feats),
        (biases_in, biases),
        (wq_in, w_q),
        (wk_in, w_k),
        (wv_in, w_v),
    )
    copies = [
        pltpu.make_async_copy(source, target, sems.at[place])
        for place, (source, target) in enumerate(moves)
    ]
    for copy in copies:
        copy.start()
    for copy in copies[:6]:
        copy.wait()

    def molecule(m, carry):
        at = pl.ds(pl.multiple_of(m * SEQ, SEQ), SEQ)
        count = node_count(info, info[0] * mols + m)
        hidden, ident, normed = embed_rows(feats, lap, ends, w_ident, vecs, at, count)
        ident_out[:, at] = ident
        hidden_out[at, :] = hidden
        normed_out[at, :] = normed
        normed_t_out[:, at] = normed.T
        return carry

    lax.fori_loop(0, mols, molecule, 0)
    normed = normed_out[...]
    copies[6].wait()
    q_out[...] = (dot(normed, w_q[...]) + biases[0:1, :]).astype(BF16)
    copies[7].wait()
    k_out[...] = dot(normed, w_k[...]).astype(BF16)
    copies[8].wait()
    v_out[...] = (dot(normed, w_v[...]) + biases[1:2, :]).astype(BF16)


def forward_kernel(
    info, hidden, normed, q_own, k_own, v_own, w_q, w_k, w_v,
    wo_own, wo, wu_own, wu, wd_own, wd, vecs, biases_own, biases, cots,
    q_out, k_out, v_out, probs_out, keep_out, send_out, middle, active, gm_out, grad_branch,
    mixed, attended, unit, normed_two, slope, grad_ffn,
):
    rows, dim = hidden.shape
    width = q_own.shape[1]
    mols = rows // SEQ
    pairs = width // (2 * HDIM)
    windows = head_windows(width)
    own_core = info[0]

    q_out[...] = (dot(normed[...], w_q[...]) + biases[0:1, :]).astype(BF16)
    k_out[...] = dot(normed[...], w_k[...]).astype(BF16)
    v_out[...] = (dot(normed[...], w_v[...]) + biases[1:2, :]).astype(BF16)

    def attend(m, carry):
        at = pl.ds(pl.multiple_of(m * SEQ, SEQ), SEQ)
        place = own_core * mols + m
        count = slot_count(info, place)
        key_keep = positions(SEQ) < count
        query_keep = lax.broadcasted_iota(jnp.int32, (1, SEQ), 1) < count
        sides = ((q_own, k_own, v_own, keep_out), (q_out, k_out, v_out, send_out))
        for side, (q_ref, k_ref, v_ref, part_out) in enumerate(sides):
            queries, key_rows = q_ref[at, :], k_ref[at, :]
            values_t = v_ref[at, :].T
            for pair in range(pairs):
                low, high = windows[pair]
                both = split_heads(queries, pair, windows[pair])
                scores = dot_nt(key_rows[:, low:high], both) * SCALE
                scores = jnp.where(key_keep, scores, -1e30)
                top = jnp.max(scores, axis=0, keepdims=True)
                raised = jnp.exp(scores - top)
                total = row_sum(raised)
                probs = (raised * (1.0 / total)).astype(BF16)
                probs_out[m, side * pairs + pair] = probs
                first = pair * 2 * HDIM
                out = dot(values_t[first : first + 2 * HDIM], probs)
                mixed[first : first + HDIM, :] = out[:HDIM, :SEQ]
                mixed[first + HDIM : first + 2 * HDIM, :] = out[HDIM:, SEQ:]
            kept = jnp.where(query_keep, mixed[...], 0.0).astype(BF16)
            part_out[dim : dim + width, at] = kept
            attended[at, side * width : (side + 1) * width] = kept.T
        return carry

    lax.fori_loop(0, mols, attend, 0)
    middle[...] = (
        hidden[...] + dot(attended[:, :width], wo_own[...]) + dot(attended[:, width:], wo[...])
    )

    def second_norm(m, carry):
        at = pl.ds(pl.multiple_of(m * SEQ, SEQ), SEQ)
        place = own_core * mols + m
        keep = positions(SEQ) < slot_count(info, place)
        total = middle[at, :] + vecs[4:5, :]
        middle[at, :] = total
        unit_rows, _ = norm_parts(total)
        unit[at, :] = unit_rows
        rows_two = (unit_rows * vecs[5:6, :] + vecs[6:7, :]).astype(BF16)
        normed_two[at, :] = rows_two
        turned = rows_two.T
        keep_out[:dim, at] = turned
        send_out[:dim, at] = turned
        grad_ffn[at, :] = jnp.where(keep, cots[at, :].astype(F32), 0.0).astype(BF16)
        return carry

    lax.fori_loop(0, mols, second_norm, 0)

    for side, (w_ref, b_ref, part_out) in enumerate(
        ((wu_own, biases_own, keep_out), (wu, biases, send_out))
    ):
        columns = slice(side * width, (side + 1) * width)
        slope[:, columns] = dot(normed_two[...], w_ref[...]) + b_ref[2:3, :]

        def activate(m, carry):
            at = pl.ds(pl.multiple_of(m * SEQ, SEQ), SEQ)
            before = slope[at, columns]
            phi = 0.5 * (1.0 + lax.erf(before * math.sqrt(0.5)))
            out = (before * phi).astype(BF16)
            slope[at, columns] = phi + before * jnp.exp(before * before * -0.5) * (
                1.0 / math.sqrt(2.0 * math.pi)
            )
            active[at, columns] = out
            part_out[dim + width : dim + 2 * width, at] = out.T
            return carry

        lax.fori_loop(0, mols, activate, 0)

    place_b = dim + 2 * width
    for side, (w_ref, part_out) in enumerate(((wd_own, keep_out), (wd, send_out))):
        columns = slice(side * width, (side + 1) * width)
        grad_before = slope[:, columns] * dot_nt(grad_ffn[...], w_ref[...])
        part_out[place_b : place_b + rows, :] = grad_before.astype(BF16)

    back = pl.ds(place_b, rows)
    gm_out[...] = dot_nt(keep_out[back, :], wu_own[...]) + dot_nt(send_out[back, :], wu[...])

    def second_back(m, sums):
        at = pl.ds(pl.multiple_of(m * SEQ, SEQ), SEQ)
        place = own_core * mols + m
        keep = positions(SEQ) < slot_count(info, place)
        grad_normed = gm_out[at, :]
        unit_rows = unit[at, :]
        _, inverse = norm_parts(middle[at, :])
        grad_result = jnp.where(keep, cots[at, :].astype(F32), 0.0)
        grad = grad_result + norm_back(unit_rows, inverse, grad_normed * vecs[5:6, :])
        gm_out[at, :] = grad
        grad_branch[at, :] = grad.astype(BF16)
        return (
            sums[0] + row_sum(grad),
            sums[1] + row_sum(grad_normed * unit_rows),
            sums[2] + row_sum(grad_normed),
            sums[3] + row_sum(grad_result),
        )

    nothing = jnp.zeros((1, dim), F32)
    sums = lax.fori_loop(0, mols, second_back, (nothing,) * 4)
    place_m = place_b + rows
    for part_out in (keep_out, send_out):
        part_out[place_m : place_m + rows, :] = grad_branch[:, :width]
        part_out[place_m + rows : place_m + 2 * rows, :] = grad_branch[:, width:]
    small = jnp.concatenate(list(sums) + [nothing] * 12, axis=0)
    left, right = small[:, :width], small[:, width:]
    place_s = place_m + 2 * rows
    keep_out[place_s:, :] = jnp.where(own_core == 0, left, right).astype(BF16)
    send_out[place_s:, :] = jnp.where(own_core == 0, right, left).astype(BF16)


def result_kernel(
    info, middle, active, grad_branch, wd_own, wd, wo_own, wo, w_ident, vecs, feats, lap, ends,
    result_out, ga_own_out, ga_out, normed_t_out,
):
    rows = middle.shape[0]
    width = wd.shape[0]
    mols = rows // SEQ
    result_out[...] = (
        middle[...]
        + dot(active[:, :width], wd_own[...])
        + dot(active[:, width:], wd[...])
        + vecs[7:8, :]
    ).astype(BF16)
    for ref, weight in ((ga_own_out, wo_own), (ga_out, wo)):
        product = dot_nt(grad_branch[...], weight[...])
        for m in range(mols):
            place = info[0] * mols + m
            keep = positions(SEQ) < slot_count(info, place)
            at = slice(m * SEQ, (m + 1) * SEQ)
            ref[at, :] = jnp.where(keep, product[at], 0.0).astype(BF16)

    def molecule(m, carry):
        at = pl.ds(pl.multiple_of(m * SEQ, SEQ), SEQ)
        count = node_count(info, (1 - info[0]) * mols + m)
        normed_t_out[:, at] = embed_rows(feats, lap, ends, w_ident, vecs, at, count)[2].T
        return carry

    lax.fori_loop(0, mols, molecule, 0)


def attend_back_kernel(
    m, info, q_own, k_own, v_own, ga_own, q_got, k_got, v_got, ga_got, probs_all,
    keep_out, send_out, dq_t, dk, dv,
):
    width = q_own.shape[1]
    pairs = width // (2 * HDIM)
    windows = head_windows(width)
    at = slice(m * SEQ, (m + 1) * SEQ)
    sides = (
        (q_own, k_own, v_own, ga_own, keep_out),
        (q_got, k_got, v_got, ga_got, send_out),
    )
    for side, (q_ref, k_ref, v_ref, g_ref, part_out) in enumerate(sides):
        queries, key_rows, values, grads = q_ref[at, :], k_ref[at, :], v_ref[at, :], g_ref[at, :]
        keys_t = key_rows.T
        dk[side] = jnp.zeros_like(dk[side])
        dv[side] = jnp.zeros_like(dv[side])
        for pair in range(pairs):
            low, high = windows[pair]
            both_q = split_heads(queries, pair, windows[pair])
            both_g = split_heads(grads, pair, windows[pair])
            probs_low = probs_all[m, side * pairs + pair]
            probs = probs_low.astype(F32)
            grad_probs = dot_nt(values[:, low:high], both_g)
            inner = row_sum(probs * grad_probs)
            grad_scores = (probs * (grad_probs - inner)).astype(BF16)
            dv[side, :, low:high] += dot(probs_low, both_g)
            dk[side, :, low:high] += dot(grad_scores, both_q)
            first = pair * 2 * HDIM
            out = dot(keys_t[first : first + 2 * HDIM], grad_scores)
            dq_t[side, first : first + HDIM, :] = out[:HDIM, :SEQ]
            dq_t[side, first + HDIM : first + 2 * HDIM, :] = out[HDIM:, SEQ:]
        part_out[:SEQ, :] = (dq_t[side] * SCALE).astype(BF16).T
        part_out[SEQ : 2 * SEQ, :] = (dk[side] * SCALE).astype(BF16)
        part_out[2 * SEQ :, :] = dv[side].astype(BF16)


def embed_back_kernel(
    info, *refs,
):
    mols = len(refs[:-16]) // 2
    grads_own, grads = refs[:mols], refs[mols : 2 * mols]
    (
        wq_own, wk_own, wv_own, w_q, w_k, w_v, ident, w_ident, grad_middle, vecs, feats,
        features_out, small_out, grad_normed, small, stacked,
    ) = refs[2 * mols :]
    rows, dim = feats.shape
    width = wq_own.shape[1]
    own_core = info[0]
    idw = ident.shape[0]
    total = None
    for part, weights in ((grads_own, (wq_own, wk_own, wv_own)), (grads, (w_q, w_k, w_v))):
        for place, weight in enumerate(weights):
            for m in range(mols):
                stacked[m * SEQ : (m + 1) * SEQ, :] = part[m][place * SEQ : (place + 1) * SEQ, :]
            term = dot_nt(stacked[...], weight[...])
            total = term if total is None else total + term
    grad_normed[...] = total
    small[...] = jnp.zeros_like(small)

    def molecule(m, carry):
        at = pl.ds(pl.multiple_of(m * SEQ, SEQ), SEQ)
        is_edge = positions(SEQ) >= node_count(info, own_core * mols + m)
        hidden = feats[at, :].astype(F32) + dot_tn(ident[:, at], w_ident[...])
        hidden = hidden + jnp.where(is_edge, vecs[1:2, :], vecs[0:1, :])
        unit, inverse = norm_parts(hidden)
        grad_rows = grad_normed[at, :]
        grad = grad_middle[at, :] + norm_back(unit, inverse, grad_rows * vecs[2:3, :])
        features_out[at, :] = grad
        high = grad.astype(BF16)
        rest = (grad - high.astype(F32)).astype(BF16)
        picked = ident[:, at]
        small[:idw, :] += dot(picked, high) + dot(picked, rest)
        edge_rows = jnp.where(is_edge, grad, 0.0)
        small[idw : idw + 1, :] += row_sum(grad - edge_rows)
        small[idw + 1 : idw + 2, :] += row_sum(edge_rows)
        small[idw + 2 : idw + 3, :] += row_sum(grad_rows * unit)
        small[idw + 3 : idw + 4, :] += row_sum(grad_rows)
        return carry

    lax.fori_loop(0, mols, molecule, 0)
    count = idw + 4
    small_out[...] = jnp.zeros_like(small_out)
    small_out[:count, :] = small[:count, :width]
    small_out[count : 2 * count, :] = small[:count, width:]


def deal(info, unit, outs, block_at, small):
    inner, outer = info[1], info[2]
    first_kept, first_sent, second_kept, second_sent = outs
    for step in range(INNER):
        for turn in range(OUTER):
            if turn < 2:
                out, slot = (first_sent if step % 2 else first_kept), step // 2
            else:
                out, slot = (second_sent if step // 2 else second_kept), step % 2
            start = (slot * 2 + turn % 2) * 3 * unit
            for place in range(3):
                out[start + place * unit : start + (place + 1) * unit, :] = block_at(
                    inner ^ step, outer ^ turn, place
                )
    if small is not None:
        for out in (first_kept, first_sent):
            out[INNER * 3 * unit :, :] = small


def ffn_grads_kernel(info, kept, got, cots, *rest):
    outs, (tall, flat, grad_ffn) = rest[:4], rest[4:]
    rows_all, dim = cots.shape
    rows, width = rows_all // 2, kept.shape[1]
    mols = rows // SEQ
    own_core = info[0]
    for m in range(2 * mols):
        keep = positions(SEQ) < slot_count(info, m)
        at = slice(m * SEQ, (m + 1) * SEQ)
        grad_ffn[at, :] = jnp.where(keep, cots[at, :].astype(F32), 0.0).astype(BF16)
    own_rows = pl.ds(pl.multiple_of(own_core * rows, SEQ), rows)
    other_rows = pl.ds(pl.multiple_of((1 - own_core) * rows, SEQ), rows)
    place_b = dim + 2 * width
    place_m = place_b + rows
    place_s = place_m + 2 * rows
    back = slice(place_b, place_m)
    tall[...] = (dot(kept[:dim, :], kept[back, :]) + dot(got[:dim, :], got[back, :])).astype(BF16)
    turned = slice(dim, dim + width)
    for half in (0, 1):
        mid = slice(place_m + half * rows, place_m + (half + 1) * rows)
        flat[half] = (
            dot(kept[turned, :], kept[mid, :]) + dot(got[turned, :], got[mid, :])
        ).astype(BF16)
    turned = slice(dim + width, dim + 2 * width)
    for half in (0, 1):
        columns = slice(half * width, (half + 1) * width)
        product = dot(kept[turned, :], grad_ffn[own_rows, columns])
        product = product + dot(got[turned, :], grad_ffn[other_rows, columns])
        flat[2 + half] = product.astype(BF16)
    bias = row_sum(kept[back, :].astype(F32)) + row_sum(got[back, :].astype(F32))
    small = kept[place_s:, :].astype(F32) + got[place_s:, :].astype(F32)
    spot = lax.broadcasted_iota(jnp.int32, small.shape, 0)
    small = jnp.where(spot == 4, bias, small).astype(BF16)
    unit = dim // (INNER * OUTER)

    def block_at(dest, z, place):
        if place == 0:
            return tall[pl.ds(pl.multiple_of((dest * OUTER + z) * unit, 16), unit), :]
        row = pl.multiple_of((dest * (OUTER // 2) + z // 2) * unit, 16)
        return flat[2 * (place - 1) + z % 2, pl.ds(row, unit), :]

    deal(info, unit, outs, block_at, small)


def qkv_grads_kernel(info, normed_t, normed_t_got, *refs):
    mols = normed_t.shape[1] // SEQ
    kept, got = refs[:mols], refs[mols : 2 * mols]
    outs, small_out = refs[2 * mols : 2 * mols + 4], refs[2 * mols + 4]
    tall, normed, stacked = refs[2 * mols + 5 :]
    dim, rows = normed_t.shape
    unit = dim // (INNER * OUTER)
    normed[:, :rows] = normed_t[...]
    normed[:, rows:] = normed_t_got[...]
    spot = lax.broadcasted_iota(jnp.int32, small_out.shape, 0)
    small = jnp.zeros(small_out.shape, F32)
    for place in range(3):
        for m, part in enumerate(kept + got):
            stacked[m * SEQ : (m + 1) * SEQ, :] = part[place * SEQ : (place + 1) * SEQ, :]
        tall[place] = dot(normed[...], stacked[...]).astype(BF16)
        if place != 1:
            small = jnp.where(spot == 72 + place // 2, row_sum(stacked[...].astype(F32)), small)
    small_out[...] = small

    def block_at(dest, z, place):
        return tall[place, pl.ds(pl.multiple_of((dest * OUTER + z) * unit, 16), unit), :]

    deal(info, unit, outs, block_at, None)


def add(first, second):
    return (first.astype(F32) + second.astype(F32)).astype(BF16)


def plane_sum_kernel(late, first, first_got, second, second_got, *refs):
    extra, (first_kept, first_sent, second_kept, second_sent) = refs[:-4], refs[-4:]
    pair = second_kept.shape[0]
    total = add(first[...], first_got[...])
    first_kept[:pair, :] = total[:pair]
    first_sent[:pair, :] = total[pair : 2 * pair]
    if late:
        small = (extra[0][...] + extra[1][...]).astype(BF16)
    else:
        small = total[2 * pair :]
    first_kept[pair:, :] = small
    first_sent[pair:, :] = small
    total = add(second[...], second_got[...])
    second_kept[...] = total[:pair]
    second_sent[...] = total[pair:]


def line_cut_kernel(first, first_got, second, second_got, *outs):
    chunk = second.shape[0] // 2
    total = add(first[...], first_got[...])
    small = total[2 * chunk :]
    other = add(second[...], second_got[...])
    blocks = (total[:chunk], total[chunk : 2 * chunk], other[:chunk], other[chunk:])
    for out, block in zip(outs, blocks):
        out[:chunk, :] = block
        out[chunk:, :] = small


def line_sum_kernel(first, second, third, fourth, out, small_out):
    total = first[...].astype(F32) + second[...].astype(F32)
    total = total + third[...].astype(F32) + fourth[...].astype(F32)
    size = out.shape[0]
    out[...] = total[:size].astype(BF16)
    small_out[...] = total[size:]


def line_join_kernel(*refs):
    parts, extra, outs = refs[:OUTER], refs[OUTER:-2], refs[-2:]
    size = parts[0].shape[0]
    for out in outs:
        for turn, part in enumerate(parts):
            out[turn * size : (turn + 1) * size, :] = part[...]
    for ref in extra:
        outs[0][OUTER * size :, :] = ref[...].astype(BF16)


def place_kernel(split_second, info, own, side_x, side_y, far_first, far_second, *outs):
    inner, outer = info[1], info[2]
    unit = own.shape[0] // (3 * OUTER)
    width = own.shape[1]
    for step in range(INNER):
        for turn in range(OUTER):
            ref, start = (own, side_x, side_y, far_first)[step], turn * 3 * unit
            if step == 3 and turn >= 2:
                ref, start = far_second, (turn - 2) * 3 * unit
            dest, z = inner ^ step, outer ^ turn
            tall = pl.ds(pl.multiple_of((dest * OUTER + z) * unit, 16), unit)
            flat = pl.ds(pl.multiple_of((dest * (OUTER // 2) + z // 2) * unit, 16), unit)
            columns = pl.ds(pl.multiple_of(z % 2 * width, LANES), width)
            for place in range(3):
                part = ref[start + place * unit : start + (place + 1) * unit, :].astype(F32)
                if split_second and place > 0:
                    outs[place][flat, columns] = part
                else:
                    outs[place][tall, :] = part


def per_device(
    features, lap_vectors, node_counts, edge_counts, endpoints, w_ident, type_table,
    gain_one, shift_one, w_query, w_key, w_value, bias_query, bias_value, w_out, bias_out,
    gain_two, shift_two, w_up, bias_up, w_down, bias_down, cotangent,
):
    dp_count = lax.axis_size("dp")
    dp_index = lax.axis_index("dp")
    mp_index = lax.axis_index("mp")
    block = INNER * OUTER
    rest_count = dp_count // block
    place = jnp.stack([mp_index, dp_index % INNER, dp_index // INNER % OUTER]).astype(jnp.int32)
    info = jnp.concatenate([place, node_counts, edge_counts])

    def swap(part):
        return lax.ppermute(part, "mp", [(0, 1), (1, 0)])

    def inner_move(part, step):
        return lax.ppermute(part, "dp", [(s, s ^ step) for s in range(dp_count)])

    def outer_move(part, step):
        return lax.ppermute(part, "dp", [(s, s ^ (step * INNER)) for s in range(dp_count)])

    rows_all, dim = features.shape
    rows = rows_all // 2
    mols = rows // SEQ
    width = w_query.shape[1]
    heads = width // HDIM
    lapk = lap_vectors.shape[1]
    idw = w_ident.shape[0]
    scalars = (info,)
    half_rows = lambda columns: pl.BlockSpec((rows, columns), lambda g, info: (info[0], 0))

    def table_of(rows_of, start):
        spot = lax.broadcasted_iota(jnp.int32, (8, 1), 0)
        for place, row in enumerate(rows_of):
            start = jnp.where(spot == place, row[None], start) if row is not None else start
        return start.astype(F32)

    def pinned(part):
        return pltpu.with_memory_space_constraint(part, pltpu.HBM)

    biases = table_of([bias_query, bias_value, bias_up], jnp.zeros((8, width), BF16))
    vecs = table_of(
        [None, None, gain_one, shift_one, bias_out, gain_two, shift_two, bias_down],
        jnp.pad(type_table, ((0, 6), (0, 0))),
    )

    wq_got, wk_got, wv_got = swap(w_query), swap(w_key), swap(w_value)
    biases_got = swap(biases)
    wo_got, wu_got, wd_got = swap(w_out), swap(w_up), swap(w_down)

    hidden, ident, normed, normed_t, q_own, k_own, v_own = call(
        embed_kernel,
        scalars,
        tuple(
            pinned(part)
            for part in (
                features, lap_vectors.T, endpoints.T, w_ident, vecs, biases,
                w_query, w_key, w_value,
            )
        ),
        [outside()] * 9,
        [
            ((rows, dim), F32),
            ((idw, rows), BF16),
            ((rows, dim), BF16),
            ((dim, rows), BF16),
            ((rows, width), BF16),
            ((rows, width), BF16),
            ((rows, width), BF16),
        ],
        scratch=[
            pltpu.VMEM((rows, dim), BF16),
            pltpu.VMEM((lapk, rows), BF16),
            pltpu.VMEM((2, rows), jnp.int32),
            pltpu.VMEM((idw, dim), BF16),
            pltpu.VMEM((8, dim), F32),
            pltpu.VMEM((8, width), F32),
            pltpu.VMEM((dim, width), BF16),
            pltpu.VMEM((dim, width), BF16),
            pltpu.VMEM((dim, width), BF16),
            pltpu.SemaphoreType.DMA((9,)),
        ],
        micros=6,
        local=False,
    )
    sent_rows = dim + 2 * width + 3 * rows + 16
    (
        q_got, k_got, v_got, probs, kept_a, sent_a, middle, active, grad_middle, grad_branch,
    ) = call(
        forward_kernel,
        scalars,
        (
            hidden, normed, q_own, k_own, v_own, wq_got, wk_got, wv_got,
            w_out, wo_got, w_up, wu_got, w_down, wd_got, pinned(vecs), pinned(biases),
            biases_got, cotangent,
        ),
        [whole()] * 17 + [half_rows(dim)],
        [
            ((rows, width), BF16),
            ((rows, width), BF16),
            ((rows, width), BF16),
            ((mols, heads, SEQ, 2 * SEQ), BF16),
            ((sent_rows, width), BF16),
            ((sent_rows, width), BF16),
            ((rows, dim), F32),
            ((rows, dim), BF16),
            ((rows, dim), F32),
            ((rows, dim), BF16),
        ],
        scratch=[
            pltpu.VMEM((width, SEQ), F32),
            pltpu.VMEM((rows, dim), BF16),
            pltpu.VMEM((rows, dim), F32),
            pltpu.VMEM((rows, dim), BF16),
            pltpu.VMEM((rows, dim), F32),
            pltpu.VMEM((rows, dim), BF16),
        ],
        micros=20,
        limit=30,
    )
    got_a = swap(sent_a)
    other_rows = lambda columns: pl.BlockSpec((rows, columns), lambda g, info: (1 - info[0], 0))
    other_columns = lambda count: pl.BlockSpec((count, rows), lambda g, info: (0, 1 - info[0]))
    result, ga_own, ga_got, normed_t_got = call(
        result_kernel,
        scalars,
        (
            middle, active, grad_branch, w_down, wd_got, w_out, wo_got, w_ident, pinned(vecs),
            features, lap_vectors.T, endpoints.T,
        ),
        [whole()] * 9 + [other_rows(dim), other_columns(lapk), other_columns(2)],
        [((rows, dim), BF16), ((rows, width), BF16), ((rows, width), BF16), ((dim, rows), BF16)],
        micros=4,
    )

    unit = dim // block
    chunk = 3 * unit
    small_a, small_b = 16, 80

    def rest_sum(part):
        if rest_count == 1:
            return part
        groups = [[r * block + s for r in range(rest_count)] for s in range(block)]
        return lax.psum(part.astype(F32), "dp", axis_index_groups=groups).astype(part.dtype)

    pair = 2 * chunk

    def after(part, *others):
        return lax.optimization_barrier((part, *others))[0]

    def plane_step(parts, others=(), extra=(), small_rows=0, micros=0):
        first, first_sent, second, second_sent = parts
        first_got = after(inner_move(first_sent, 1), *others)
        second_got = after(inner_move(second_sent, 2), *others)
        return call(
            lambda *refs: plane_sum_kernel(bool(extra), *refs),
            (),
            (first, first_got, second, second_got, *extra),
            [whole()] * (4 + len(extra)),
            [((pair + small_rows, width), BF16)] * 2 + [((pair, width), BF16)] * 2,
            micros=micros,
            local=False,
        )

    def plane_turn(parts, others=(), micros=0):
        first, first_sent, second, second_sent = parts
        first_got = after(inner_move(first_sent, 2), *others)
        second_got = after(inner_move(second_sent, 1), *others)
        rows_out = first.shape[0] - chunk
        return call(
            line_cut_kernel,
            (),
            (first, first_got, second, second_got),
            [whole()] * 4,
            [((rows_out, width), BF16)] * OUTER,
            micros=micros,
            local=False,
        )

    def line_step(parts, others=(), micros=0):
        got = [after(outer_move(parts[turn], turn), *others) for turn in range(1, OUTER)]
        mine, small = call(
            line_sum_kernel,
            (),
            (parts[0], *got),
            [whole()] * OUTER,
            [((chunk, width), BF16), ((parts[0].shape[0] - chunk, width), F32)],
            micros=micros,
            local=False,
        )
        return rest_sum(mine), rest_sum(small)

    def line_back(mine, others=(), extra=(), micros=0):
        got = [after(outer_move(mine, turn), *others) for turn in range(1, OUTER)]
        more = sum(part.shape[0] for part in extra)
        return call(
            line_join_kernel,
            (),
            (mine, *got, *extra),
            [whole()] * (OUTER + len(extra)),
            [((OUTER * chunk + more, width), BF16), ((OUTER * chunk, width), BF16)],
            micros=micros,
            local=False,
        )

    def plane_back(lines):
        return inner_move(lines[0], 1), inner_move(lines[1], 2)

    def plane_back_turn(side_x, side_y):
        return inner_move(side_y[:pair], 1), inner_move(side_x[pair : 2 * pair], 2)

    def widened(small):
        small_got = swap(small)
        return jnp.where(
            mp_index == 0,
            jnp.concatenate([small, small_got], axis=1),
            jnp.concatenate([small_got, small], axis=1),
        )

    def placed(planes, split_second):
        tall, flat = ((dim, width), F32), ((width, dim), F32)
        return call(
            lambda *refs: place_kernel(split_second, *refs),
            (info,),
            planes,
            [whole()] * 5,
            [tall, flat, flat] if split_second else [tall] * 3,
            micros=0,
            local=False,
        )

    kept_a, result, ga_own = lax.optimization_barrier((kept_a, result, ga_own))
    parts_a = call(
        ffn_grads_kernel,
        scalars,
        (kept_a, got_a, cotangent),
        [whole()] * 3,
        [
            ((INNER * chunk + small_a, width), BF16),
            ((INNER * chunk + small_a, width), BF16),
            ((INNER * chunk, width), BF16),
            ((INNER * chunk, width), BF16),
        ],
        scratch=[
            pltpu.VMEM((dim, width), BF16),
            pltpu.VMEM((4, width, width), BF16),
            pltpu.VMEM((rows_all, dim), BF16),
        ],
        micros=6,
    )
    q_own = after(q_own, parts_a[0])
    kept_b, got_b, sent_b = [], [], []
    for m in range(mols):
        kept, sent = call(
            lambda *refs, m=m: attend_back_kernel(m, *refs),
            scalars,
            (q_own, k_own, v_own, ga_own, q_got, k_got, v_got, ga_got, probs),
            [whole()] * 9,
            [((3 * SEQ, width), BF16)] * 2,
            scratch=[
                pltpu.VMEM((2, width, SEQ), F32),
                pltpu.VMEM((2, SEQ, width), F32),
                pltpu.VMEM((2, SEQ, width), F32),
            ],
            micros=4,
        )
        kept_b.append(kept)
        sent_b.append(sent)
        got_b.append(swap(sent))
        q_own, q_got, _ = lax.optimization_barrier((q_own, q_got, kept))

    steps_a = plane_step(parts_a, others=(kept_b[-1],), small_rows=small_a)
    normed_t = after(normed_t, *steps_a)
    parts_b = call(
        qkv_grads_kernel,
        scalars,
        (normed_t, normed_t_got, *kept_b, *got_b),
        [whole()] * (2 + 2 * mols),
        [((INNER * chunk, width), BF16)] * 4 + [((small_b, width), F32)],
        scratch=[
            pltpu.VMEM((3, dim, width), BF16),
            pltpu.VMEM((dim, 2 * rows), BF16),
            pltpu.VMEM((2 * rows, width), BF16),
        ],
        micros=4,
    )
    turned_a = plane_turn(steps_a, others=(parts_b[0],))
    grad_middle = after(grad_middle, parts_b[0], *turned_a)
    grad_features, small_own = call(
        embed_back_kernel,
        scalars,
        (
            *kept_b, *sent_b, w_query, w_key, w_value, wq_got, wk_got, wv_got, ident, w_ident,
            grad_middle, pinned(vecs), features,
        ),
        [whole()] * (10 + 2 * mols) + [half_rows(dim)],
        [((rows, dim), F32), ((small_b, width), F32)],
        scratch=[
            pltpu.VMEM((rows, dim), F32),
            pltpu.VMEM((idw + 8, dim), F32),
            pltpu.VMEM((rows, width), BF16),
        ],
        micros=7,
        local=False,
    )
    steps_b = plane_step(
        parts_b[:4], extra=(small_own, parts_b[4]), small_rows=small_b
    )
    mine_a, narrow_a = line_step(turned_a, others=steps_b, micros=3)
    turned_b = plane_turn(steps_b)
    lines_a = line_back(mine_a, others=turned_b, micros=3)
    mine_b, late_b = line_step(turned_b)
    sides_a = plane_back(lines_a)
    lines_b = line_back(mine_b, extra=(late_b,))
    far_a = plane_back_turn(*sides_a)
    planes_a = (lines_a[1], *sides_a, *far_a)
    wide_a = widened(narrow_a)
    sides_b = plane_back(lines_b)
    far_b = plane_back_turn(*sides_b)
    narrow_b = late_b + sides_b[0][OUTER * chunk :].astype(F32)
    planes_b = (lines_b[1], sides_b[0], sides_b[1], *far_b)
    wide_b_rows = idw + 4
    both_b = narrow_b[: 2 * wide_b_rows]
    both_b = both_b + swap(both_b)
    wide_b = jnp.concatenate([both_b[:wide_b_rows], both_b[wide_b_rows:]], axis=1)

    grad_w_up, grad_w_out, grad_w_down = placed(planes_a, True)
    grad_w_query, grad_w_key, grad_w_value = placed(planes_b, False)
    return (
        result,
        grad_features,
        wide_b[:idw],
        wide_b[idw : idw + 2],
        wide_b[idw + 2],
        wide_b[idw + 3],
        grad_w_query,
        grad_w_key,
        grad_w_value,
        narrow_b[2 * wide_b_rows],
        narrow_b[2 * wide_b_rows + 1],
        grad_w_out,
        wide_a[0],
        wide_a[1],
        wide_a[2],
        grad_w_up,
        narrow_a[4],
        grad_w_down,
        wide_a[3],
    )


def solution(mesh):
    token, split = P("dp", None), P(("dp", "mp"), None)
    columns, lines, cut, copy = P(None, "mp"), P("mp", None), P("mp"), P()
    return jax.shard_map(
        per_device,
        mesh=mesh,
        in_specs=(
            token, token, P("dp"), P("dp"), token, copy, copy, copy, copy, columns, columns,
            columns, cut, cut, lines, copy, copy, copy, columns, cut, lines, copy, token,
        ),
        out_specs=(
            split, split, copy, copy, copy, copy, columns, columns, columns, cut, cut, lines,
            copy, copy, copy, columns, cut, lines, copy,
        ),
        check_vma=False,
    )
```

```python
import math

import jax
import jax.numpy as jnp
from jax import lax
from jax.experimental import pallas as pl
from jax.experimental.pallas import tpu as pltpu
from jax.sharding import PartitionSpec as P

HDIM = 24
SEQ = 128
LANES = 128
INNER = 4
OUTER = 4
EPSILON = 1e-05
SCALE = 1.0 / math.sqrt(HDIM)
F32, BF16 = jnp.float32, jnp.bfloat16
MIB = 1024 * 1024


def dot(left, right):
    return jnp.dot(left, right, preferred_element_type=F32)


def dot_nt(left, right):
    return lax.dot_general(left, right, (((1,), (1,)), ((), ())), preferred_element_type=F32)


def dot_tn(left, right):
    return lax.dot_general(left, right, (((0,), (0,)), ((), ())), preferred_element_type=F32)


def norm_parts(hidden):
    average = jnp.mean(hidden, axis=-1, keepdims=True)
    centred = hidden - average
    inverse = lax.rsqrt(jnp.mean(centred * centred, axis=-1, keepdims=True) + EPSILON)
    return centred * inverse, inverse


def norm_back(unit, inverse, grad_hat):
    return inverse * (
        grad_hat
        - jnp.mean(grad_hat, axis=-1, keepdims=True)
        - unit * jnp.mean(grad_hat * unit, axis=-1, keepdims=True)
    )


def row_sum(block):
    return jnp.sum(block, axis=0, keepdims=True)


def positions(length):
    return lax.broadcasted_iota(jnp.int32, (length, 1), 0)


def whole():
    return pl.BlockSpec(memory_space=pltpu.VMEM)


def outside():
    return pl.BlockSpec(memory_space=pltpu.HBM)


def places():
    index = lax.axis_index("dp")
    return lax.axis_index("mp"), index % INNER, index // INNER % OUTER


def copy_in(sources, targets, sems):
    copies = [
        pltpu.make_async_copy(source, target, sems.at[place])
        for place, (source, target) in enumerate(zip(sources, targets))
    ]
    for copy in copies:
        copy.start()
    return copies


def row_of(ref):
    block = ref[...].astype(F32)
    return jnp.concatenate([block[r : r + 1, :] for r in range(block.shape[0])], axis=1)


def put_row(ref, row):
    for r in range(ref.shape[0]):
        ref[r : r + 1, :] = row[:, r * LANES : (r + 1) * LANES]


def call(kernel, args, specs, outs, scratch=(), micros=0, limit=24):
    return pl.pallas_call(
        kernel,
        out_shape=[jax.ShapeDtypeStruct(shape, kind) for shape, kind in outs],
        in_specs=specs,
        out_specs=[whole() for _ in outs],
        scratch_shapes=list(scratch),
        compiler_params=pltpu.CompilerParams(vmem_limit_bytes=limit * MIB),
        cost_estimate=pl.CostEstimate(
            flops=micros * 1_000_000_000, bytes_accessed=0, transcendentals=0
        ),
    )(*args)


def head_windows(width):
    windows = []
    for pair in range(width // (2 * HDIM)):
        low = pair * 2 * HDIM // LANES * LANES
        high = -(-(pair + 1) * 2 * HDIM // LANES) * LANES
        windows.append((low, high))
    return windows


def split_heads(block, pair, window):
    low, high = window
    part = block[:, low:high]
    column = low + lax.broadcasted_iota(jnp.int32, (16, high - low), 1)
    sides = []
    for head in (2 * pair, 2 * pair + 1):
        inside = (column >= head * HDIM) & (column < (head + 1) * HDIM)
        mask = jnp.where(inside, 1.0, 0.0).astype(BF16)
        sides.append(part * jnp.concatenate([mask] * (block.shape[0] // 16), axis=0))
    return jnp.concatenate(sides, axis=0)


def embed_rows(feats, lap, ends, w_ident, types, gain, shift, at, count):
    table = lap[:, at]
    slot = lax.broadcasted_iota(jnp.int32, (SEQ, SEQ), 0)
    picked = []
    for end in (0, 1):
        pick = jnp.where(ends[end : end + 1, at] == slot, 1.0, 0.0).astype(BF16)
        picked.append(dot(table, pick))
    ident = jnp.concatenate(picked, axis=0).astype(BF16)
    hidden = feats[at, :].astype(F32) + dot_tn(ident, w_ident[...])
    kinds = types[...].astype(F32)
    hidden = hidden + jnp.where(positions(SEQ) >= count, kinds[1:2, :], kinds[0:1, :])
    unit, _ = norm_parts(hidden)
    return hidden, ident, (unit * gain + shift).astype(BF16)


def embed_kernel(
    feats_in, lap_in, ends_in, nodes_in, w_ident_in, types_in, gain_in, shift_in,
    bias_q_in, bias_v_in, wq_in, wk_in, wv_in,
    hidden_out, ident_out, normed_out, normed_t_out, q_out, k_out, v_out,
    feats, lap, ends, nodes, w_ident, types, gain_rows, shift_rows, bias_q, bias_v,
    w_q, w_k, w_v, sems,
):
    rows, dim = feats.shape
    mols = rows // SEQ
    core = places()[0]
    own_rows = pl.ds(pl.multiple_of(core * rows, SEQ), rows)
    copies = copy_in(
        (
            feats_in.at[own_rows, :], lap_in.at[:, own_rows], ends_in.at[:, own_rows], nodes_in,
            w_ident_in, types_in, gain_in, shift_in, bias_q_in, bias_v_in, wq_in, wk_in, wv_in,
        ),
        (
            feats, lap, ends, nodes, w_ident, types, gain_rows, shift_rows, bias_q, bias_v,
            w_q, w_k, w_v,
        ),
        sems,
    )
    for copy in copies[:10]:
        copy.wait()
    gain, shift = row_of(gain_rows), row_of(shift_rows)

    def molecule(m, carry):
        at = pl.ds(pl.multiple_of(m * SEQ, SEQ), SEQ)
        count = nodes[core * mols + m]
        hidden, ident, normed = embed_rows(
            feats, lap, ends, w_ident, types, gain, shift, at, count
        )
        ident_out[:, at] = ident
        hidden_out[at, :] = hidden
        normed_out[at, :] = normed
        normed_t_out[:, at] = normed.T
        return carry

    lax.fori_loop(0, mols, molecule, 0)
    normed = normed_out[...]
    copies[10].wait()
    q_out[...] = (dot(normed, w_q[...]) + row_of(bias_q)).astype(BF16)
    copies[11].wait()
    k_out[...] = dot(normed, w_k[...]).astype(BF16)
    copies[12].wait()
    v_out[...] = (dot(normed, w_v[...]) + row_of(bias_v)).astype(BF16)


def forward_kernel(
    hidden, normed, q_own, k_own, v_own, w_q, w_k, w_v, wo_own, wo, wu_own, wu, wd_own, wd,
    bias_q, bias_v, bias_u,
    nodes_in, edges_in, cots_in, bias_u_own_in, bias_o_in, gain_in, shift_in,
    q_out, k_out, v_out, probs_out, keep_out, send_out, middle, active, gm_out, grad_branch,
    nodes, edges, cots, bias_u_own, bias_o, gain_rows, shift_rows, sems,
    mixed, attended, unit, normed_two, slope, grad_ffn,
):
    rows, dim = hidden.shape
    width = q_own.shape[1]
    mols = rows // SEQ
    pairs = width // (2 * HDIM)
    windows = head_windows(width)
    core = places()[0]
    copies = copy_in(
        (
            nodes_in, edges_in, cots_in.at[pl.ds(pl.multiple_of(core * rows, SEQ), rows), :],
            bias_u_own_in, bias_o_in, gain_in, shift_in,
        ),
        (nodes, edges, cots, bias_u_own, bias_o, gain_rows, shift_rows),
        sems,
    )

    q_out[...] = (dot(normed[...], w_q[...]) + row_of(bias_q)).astype(BF16)
    k_out[...] = dot(normed[...], w_k[...]).astype(BF16)
    v_out[...] = (dot(normed[...], w_v[...]) + row_of(bias_v)).astype(BF16)

    for copy in copies:
        copy.wait()
    gain, shift, bias_out = row_of(gain_rows), row_of(shift_rows), row_of(bias_o)

    def attend(m, carry):
        at = pl.ds(pl.multiple_of(m * SEQ, SEQ), SEQ)
        place = core * mols + m
        count = nodes[place] + edges[place]
        key_keep = positions(SEQ) < count
        query_keep = lax.broadcasted_iota(jnp.int32, (1, SEQ), 1) < count
        sides = ((q_own, k_own, v_own, keep_out), (q_out, k_out, v_out, send_out))
        for side, (q_ref, k_ref, v_ref, part_out) in enumerate(sides):
            queries, key_rows = q_ref[at, :], k_ref[at, :]
            values_t = v_ref[at, :].T
            for pair in range(pairs):
                low, high = windows[pair]
                both = split_heads(queries, pair, windows[pair])
                scores = dot_nt(key_rows[:, low:high], both) * SCALE
                scores = jnp.where(key_keep, scores, -1e30)
                top = jnp.max(scores, axis=0, keepdims=True)
                raised = jnp.exp(scores - top)
                total = row_sum(raised)
                probs = (raised * (1.0 / total)).astype(BF16)
                probs_out[m, side * pairs + pair] = probs
                first = pair * 2 * HDIM
                out = dot(values_t[first : first + 2 * HDIM], probs)
                mixed[first : first + HDIM, :] = out[:HDIM, :SEQ]
                mixed[first + HDIM : first + 2 * HDIM, :] = out[HDIM:, SEQ:]
            kept = jnp.where(query_keep, mixed[...], 0.0).astype(BF16)
            part_out[dim : dim + width, at] = kept
            attended[at, side * width : (side + 1) * width] = kept.T
        return carry

    lax.fori_loop(0, mols, attend, 0)
    middle[...] = (
        hidden[...] + dot(attended[:, :width], wo_own[...]) + dot(attended[:, width:], wo[...])
    )

    def second_norm(m, carry):
        at = pl.ds(pl.multiple_of(m * SEQ, SEQ), SEQ)
        place = core * mols + m
        keep = positions(SEQ) < nodes[place] + edges[place]
        total = middle[at, :] + bias_out
        middle[at, :] = total
        unit_rows, _ = norm_parts(total)
        unit[at, :] = unit_rows
        rows_two = (unit_rows * gain + shift).astype(BF16)
        normed_two[at, :] = rows_two
        turned = rows_two.T
        keep_out[:dim, at] = turned
        send_out[:dim, at] = turned
        grad_ffn[at, :] = jnp.where(keep, cots[at, :].astype(F32), 0.0).astype(BF16)
        return carry

    lax.fori_loop(0, mols, second_norm, 0)

    for side, (w_ref, b_ref, part_out) in enumerate(
        ((wu_own, bias_u_own, keep_out), (wu, bias_u, send_out))
    ):
        columns = slice(side * width, (side + 1) * width)
        slope[:, columns] = dot(normed_two[...], w_ref[...]) + row_of(b_ref)

        def activate(m, carry):
            at = pl.ds(pl.multiple_of(m * SEQ, SEQ), SEQ)
            before = slope[at, columns]
            phi = 0.5 * (1.0 + lax.erf(before * math.sqrt(0.5)))
            out = (before * phi).astype(BF16)
            slope[at, columns] = phi + before * jnp.exp(before * before * -0.5) * (
                1.0 / math.sqrt(2.0 * math.pi)
            )
            active[at, columns] = out
            part_out[dim + width : dim + 2 * width, at] = out.T
            return carry

        lax.fori_loop(0, mols, activate, 0)

    place_b = dim + 2 * width
    for side, (w_ref, part_out) in enumerate(((wd_own, keep_out), (wd, send_out))):
        columns = slice(side * width, (side + 1) * width)
        grad_before = slope[:, columns] * dot_nt(grad_ffn[...], w_ref[...])
        part_out[place_b : place_b + rows, :] = grad_before.astype(BF16)

    back = pl.ds(place_b, rows)
    gm_out[...] = dot_nt(keep_out[back, :], wu_own[...]) + dot_nt(send_out[back, :], wu[...])

    def second_back(m, sums):
        at = pl.ds(pl.multiple_of(m * SEQ, SEQ), SEQ)
        place = core * mols + m
        keep = positions(SEQ) < nodes[place] + edges[place]
        grad_normed = gm_out[at, :]
        unit_rows = unit[at, :]
        _, inverse = norm_parts(middle[at, :])
        grad_result = jnp.where(keep, cots[at, :].astype(F32), 0.0)
        grad = grad_result + norm_back(unit_rows, inverse, grad_normed * gain)
        gm_out[at, :] = grad
        grad_branch[at, :] = grad.astype(BF16)
        return (
            sums[0] + row_sum(grad),
            sums[1] + row_sum(grad_normed * unit_rows),
            sums[2] + row_sum(grad_normed),
            sums[3] + row_sum(grad_result),
        )

    nothing = jnp.zeros((1, dim), F32)
    sums = lax.fori_loop(0, mols, second_back, (nothing,) * 4)
    place_m = place_b + rows
    for part_out in (keep_out, send_out):
        part_out[place_m : place_m + rows, :] = grad_branch[:, :width]
        part_out[place_m + rows : place_m + 2 * rows, :] = grad_branch[:, width:]
    small = jnp.concatenate(list(sums) + [nothing] * 12, axis=0)
    left, right = small[:, :width], small[:, width:]
    place_s = place_m + 2 * rows
    keep_out[place_s:, :] = jnp.where(core == 0, left, right).astype(BF16)
    send_out[place_s:, :] = jnp.where(core == 0, right, left).astype(BF16)


def result_kernel(middle, active, wd_own, wd, bias, result_out):
    width = wd.shape[0]
    result_out[...] = (
        middle[...]
        + dot(active[:, :width], wd_own[...])
        + dot(active[:, width:], wd[...])
        + row_of(bias)
    ).astype(BF16)


def branch_kernel(
    grad_branch, wo_own, wo, nodes_in, edges_in, ga_own_out, ga_out, nodes, edges, sems
):
    mols = grad_branch.shape[0] // SEQ
    core = places()[0]
    copies = copy_in((nodes_in, edges_in), (nodes, edges), sems)
    products = [dot_nt(grad_branch[...], weight[...]) for weight in (wo_own, wo)]
    for copy in copies:
        copy.wait()
    for ref, product in zip((ga_own_out, ga_out), products):
        for m in range(mols):
            place = core * mols + m
            keep = positions(SEQ) < nodes[place] + edges[place]
            at = slice(m * SEQ, (m + 1) * SEQ)
            ref[at, :] = jnp.where(keep, product[at], 0.0).astype(BF16)


def partner_kernel(
    feats_in, lap_in, ends_in, nodes_in, w_ident_in, types_in, gain_in, shift_in, normed_t_out,
    feats, lap, ends, nodes, w_ident, types, gain_rows, shift_rows, sems,
):
    rows = feats.shape[0]
    mols = rows // SEQ
    core = places()[0]
    other = pl.ds(pl.multiple_of((1 - core) * rows, SEQ), rows)
    copies = copy_in(
        (
            feats_in.at[other, :], lap_in.at[:, other], ends_in.at[:, other], nodes_in,
            w_ident_in, types_in, gain_in, shift_in,
        ),
        (feats, lap, ends, nodes, w_ident, types, gain_rows, shift_rows),
        sems,
    )
    for copy in copies:
        copy.wait()
    gain, shift = row_of(gain_rows), row_of(shift_rows)

    def molecule(m, carry):
        at = pl.ds(pl.multiple_of(m * SEQ, SEQ), SEQ)
        count = nodes[(1 - core) * mols + m]
        rows_of = embed_rows(feats, lap, ends, w_ident, types, gain, shift, at, count)
        normed_t_out[:, at] = rows_of[2].T
        return carry

    lax.fori_loop(0, mols, molecule, 0)


def attend_back_kernel(
    m, q_own, k_own, v_own, ga_own, q_got, k_got, v_got, ga_got, probs_all,
    keep_out, send_out, dq_t, dk, dv,
):
    width = q_own.shape[1]
    pairs = width // (2 * HDIM)
    windows = head_windows(width)
    at = slice(m * SEQ, (m + 1) * SEQ)
    sides = (
        (q_own, k_own, v_own, ga_own, keep_out),
        (q_got, k_got, v_got, ga_got, send_out),
    )
    for side, (q_ref, k_ref, v_ref, g_ref, part_out) in enumerate(sides):
        queries, key_rows, values, grads = q_ref[at, :], k_ref[at, :], v_ref[at, :], g_ref[at, :]
        keys_t = key_rows.T
        dk[side] = jnp.zeros_like(dk[side])
        dv[side] = jnp.zeros_like(dv[side])
        for pair in range(pairs):
            low, high = windows[pair]
            both_q = split_heads(queries, pair, windows[pair])
            both_g = split_heads(grads, pair, windows[pair])
            probs_low = probs_all[m, side * pairs + pair]
            probs = probs_low.astype(F32)
            grad_probs = dot_nt(values[:, low:high], both_g)
            inner = row_sum(probs * grad_probs)
            grad_scores = (probs * (grad_probs - inner)).astype(BF16)
            dv[side, :, low:high] += dot(probs_low, both_g)
            dk[side, :, low:high] += dot(grad_scores, both_q)
            first = pair * 2 * HDIM
            out = dot(keys_t[first : first + 2 * HDIM], grad_scores)
            dq_t[side, first : first + HDIM, :] = out[:HDIM, :SEQ]
            dq_t[side, first + HDIM : first + 2 * HDIM, :] = out[HDIM:, SEQ:]
        part_out[:SEQ, :] = (dq_t[side] * SCALE).astype(BF16).T
        part_out[SEQ : 2 * SEQ, :] = (dk[side] * SCALE).astype(BF16)
        part_out[2 * SEQ :, :] = dv[side].astype(BF16)


def embed_back_kernel(*refs):
    mols = (len(refs) - 24) // 2
    grads_own, grads = refs[:mols], refs[mols : 2 * mols]
    (
        wq_own, wk_own, wv_own, w_q, w_k, w_v, ident, grad_middle,
        feats_in, nodes_in, w_ident_in, types_in, gain_in,
        features_out, small_out,
        feats, nodes, w_ident, types, gain_rows, sems, grad_normed, small, stacked,
    ) = refs[2 * mols :]
    core = places()[0]
    rows = feats.shape[0]
    copies = copy_in(
        (
            feats_in.at[pl.ds(pl.multiple_of(core * rows, SEQ), rows), :], nodes_in,
            w_ident_in, types_in, gain_in,
        ),
        (feats, nodes, w_ident, types, gain_rows),
        sems,
    )
    rows, dim = feats.shape
    width = wq_own.shape[1]
    idw = ident.shape[0]
    total = None
    for part, weights in ((grads_own, (wq_own, wk_own, wv_own)), (grads, (w_q, w_k, w_v))):
        for place, weight in enumerate(weights):
            for m in range(mols):
                stacked[m * SEQ : (m + 1) * SEQ, :] = part[m][place * SEQ : (place + 1) * SEQ, :]
            term = dot_nt(stacked[...], weight[...])
            total = term if total is None else total + term
    grad_normed[...] = total
    small[...] = jnp.zeros_like(small)
    for copy in copies:
        copy.wait()
    gain = row_of(gain_rows)
    kinds = types[...].astype(F32)

    def molecule(m, carry):
        at = pl.ds(pl.multiple_of(m * SEQ, SEQ), SEQ)
        is_edge = positions(SEQ) >= nodes[core * mols + m]
        hidden = feats[at, :].astype(F32) + dot_tn(ident[:, at], w_ident[...])
        hidden = hidden + jnp.where(is_edge, kinds[1:2, :], kinds[0:1, :])
        unit, inverse = norm_parts(hidden)
        grad_rows = grad_normed[at, :]
        grad = grad_middle[at, :] + norm_back(unit, inverse, grad_rows * gain)
        features_out[at, :] = grad
        high = grad.astype(BF16)
        rest = (grad - high.astype(F32)).astype(BF16)
        picked = ident[:, at]
        small[:idw, :] += dot(picked, high) + dot(picked, rest)
        edge_rows = jnp.where(is_edge, grad, 0.0)
        small[idw : idw + 1, :] += row_sum(grad - edge_rows)
        small[idw + 1 : idw + 2, :] += row_sum(edge_rows)
        small[idw + 2 : idw + 3, :] += row_sum(grad_rows * unit)
        small[idw + 3 : idw + 4, :] += row_sum(grad_rows)
        return carry

    lax.fori_loop(0, mols, molecule, 0)
    count = idw + 4
    small_out[...] = jnp.zeros_like(small_out)
    small_out[:count, :] = small[:count, :width]
    small_out[count : 2 * count, :] = small[:count, width:]


def deal_direct(unit, outs, block_at, small):
    _, inner, outer = places()
    for step, out in enumerate(outs):
        for turn in range(OUTER):
            start = turn * 3 * unit
            for place in range(3):
                out[start + place * unit : start + (place + 1) * unit, :] = block_at(
                    inner ^ step, outer ^ turn, place
                )
        out[OUTER * 3 * unit :, :] = small


def deal(unit, outs, block_at):
    _, inner, outer = places()
    first_kept, first_sent, second_kept, second_sent = outs
    for step in range(INNER):
        for turn in range(OUTER):
            if turn < 2:
                out, slot = (first_sent if step % 2 else first_kept), step // 2
            else:
                out, slot = (second_sent if step // 2 else second_kept), step % 2
            start = (slot * 2 + turn % 2) * 3 * unit
            for place in range(3):
                out[start + place * unit : start + (place + 1) * unit, :] = block_at(
                    inner ^ step, outer ^ turn, place
                )


def ffn_grads_kernel(kept, got, cots_in, nodes_in, edges_in, *rest):
    outs, (cots, nodes, edges, sems, tall, flat, grad_ffn) = rest[:4], rest[4:]
    copies = copy_in((nodes_in, edges_in, cots_in), (nodes, edges, cots), sems)
    rows_all, dim = cots.shape
    rows, width = rows_all // 2, kept.shape[1]
    mols = rows // SEQ
    core = places()[0]
    own_rows = pl.ds(pl.multiple_of(core * rows, SEQ), rows)
    other_rows = pl.ds(pl.multiple_of((1 - core) * rows, SEQ), rows)
    place_b = dim + 2 * width
    place_m = place_b + rows
    place_s = place_m + 2 * rows
    back = slice(place_b, place_m)
    tall[...] = (dot(kept[:dim, :], kept[back, :]) + dot(got[:dim, :], got[back, :])).astype(BF16)
    turned = slice(dim, dim + width)
    for half in (0, 1):
        mid = slice(place_m + half * rows, place_m + (half + 1) * rows)
        flat[half] = (
            dot(kept[turned, :], kept[mid, :]) + dot(got[turned, :], got[mid, :])
        ).astype(BF16)
    for copy in copies:
        copy.wait()
    for m in range(2 * mols):
        keep = positions(SEQ) < nodes[m] + edges[m]
        at = slice(m * SEQ, (m + 1) * SEQ)
        grad_ffn[at, :] = jnp.where(keep, cots[at, :].astype(F32), 0.0).astype(BF16)
    turned = slice(dim + width, dim + 2 * width)
    for half in (0, 1):
        columns = slice(half * width, (half + 1) * width)
        product = dot(kept[turned, :], grad_ffn[own_rows, columns])
        product = product + dot(got[turned, :], grad_ffn[other_rows, columns])
        flat[2 + half] = product.astype(BF16)
    bias = row_sum(kept[back, :].astype(F32)) + row_sum(got[back, :].astype(F32))
    small = kept[place_s:, :].astype(F32) + got[place_s:, :].astype(F32)
    spot = lax.broadcasted_iota(jnp.int32, small.shape, 0)
    small = jnp.where(spot == 4, bias, small).astype(BF16)
    unit = dim // (INNER * OUTER)

    def block_at(dest, z, place):
        if place == 0:
            return tall[pl.ds(pl.multiple_of((dest * OUTER + z) * unit, 16), unit), :]
        row = pl.multiple_of((dest * (OUTER // 2) + z // 2) * unit, 16)
        return flat[2 * (place - 1) + z % 2, pl.ds(row, unit), :]

    deal_direct(unit, outs, block_at, small)


def qkv_grads_kernel(normed_t, normed_t_got, *refs):
    mols = normed_t.shape[1] // SEQ
    kept, got = refs[:mols], refs[mols : 2 * mols]
    outs, small_out = refs[2 * mols : 2 * mols + 4], refs[2 * mols + 4]
    tall, normed, stacked = refs[2 * mols + 5 :]
    dim, rows = normed_t.shape
    unit = dim // (INNER * OUTER)
    normed[:, :rows] = normed_t[...]
    normed[:, rows:] = normed_t_got[...]
    spot = lax.broadcasted_iota(jnp.int32, small_out.shape, 0)
    small = jnp.zeros(small_out.shape, F32)
    for place in range(3):
        for m, part in enumerate(kept + got):
            stacked[m * SEQ : (m + 1) * SEQ, :] = part[place * SEQ : (place + 1) * SEQ, :]
        tall[place] = dot(normed[...], stacked[...]).astype(BF16)
        if place != 1:
            small = jnp.where(spot == 72 + place // 2, row_sum(stacked[...].astype(F32)), small)
    small_out[...] = small

    def block_at(dest, z, place):
        return tall[place, pl.ds(pl.multiple_of((dest * OUTER + z) * unit, 16), unit), :]

    deal(unit, outs, block_at)


def add(first, second):
    return (first.astype(F32) + second.astype(F32)).astype(BF16)


def plane_all_kernel(first, second, third, fourth, own, near, middle, far):
    chunk = own.shape[0]
    total = first[...].astype(F32) + second[...].astype(F32)
    total = (total + third[...].astype(F32) + fourth[...].astype(F32)).astype(BF16)
    own[...] = total[:chunk]
    near[:chunk, :] = total[chunk : 2 * chunk]
    near[chunk:, :] = total[OUTER * chunk :]
    middle[...] = total[2 * chunk : 3 * chunk]
    far[...] = total[3 * chunk : 4 * chunk]


def plane_sum_kernel(
    first, first_got, second, second_got, small_first, small_second,
    first_kept, first_sent, second_kept, second_sent,
):
    pair = second_kept.shape[0]
    total = add(first[...], first_got[...])
    first_kept[:pair, :] = total[:pair]
    first_sent[:pair, :] = total[pair:]
    small = (small_first[...] + small_second[...]).astype(BF16)
    first_kept[pair:, :] = small
    first_sent[pair:, :] = small
    total = add(second[...], second_got[...])
    second_kept[...] = total[:pair]
    second_sent[...] = total[pair:]


def line_cut_kernel(first, first_got, second, second_got, own, near, middle, far):
    chunk = own.shape[0]
    total = add(first[...], first_got[...])
    own[...] = total[:chunk]
    near[...] = total[chunk:]
    total = add(second[...], second_got[...])
    middle[...] = total[:chunk]
    far[...] = total[chunk:]


def line_sum_kernel(own, near, near_got, middle_got, far_got, out, out_small):
    chunk = own.shape[0]
    total = own[...].astype(F32) + near_got[:chunk, :].astype(F32)
    total = total + middle_got[...].astype(F32) + far_got[...].astype(F32)
    out[...] = total.astype(BF16)
    out_small[:chunk, :] = total.astype(BF16)
    out_small[chunk:, :] = add(near[chunk:, :], near_got[chunk:, :])


def line_join_kernel(own, near, middle, far, line_x, line_y, small_out):
    chunk = near.shape[0]
    small = own[chunk:, :].astype(F32) + middle[chunk:, :].astype(F32)
    small_out[...] = small
    for out in (line_x, line_y):
        for turn, part in enumerate((own, near, middle, far)):
            out[turn * chunk : (turn + 1) * chunk, :] = part[:chunk, :]
    line_x[OUTER * chunk :, :] = small.astype(BF16)


def place_kernel(split_second, *refs):
    outs, parts = refs[-3:], refs[:-3]
    own = parts[0]
    _, inner, outer = places()
    unit = own.shape[0] // (3 * OUTER)
    width = own.shape[1]
    for step in range(INNER):
        for turn in range(OUTER):
            ref, start = parts[step], turn * 3 * unit
            if len(parts) == 5 and step == 3 and turn >= 2:
                ref, start = parts[4], (turn - 2) * 3 * unit
            dest, z = inner ^ step, outer ^ turn
            tall = pl.ds(pl.multiple_of((dest * OUTER + z) * unit, 16), unit)
            flat = pl.ds(pl.multiple_of((dest * (OUTER // 2) + z // 2) * unit, 16), unit)
            columns = pl.ds(pl.multiple_of(z % 2 * width, LANES), width)
            for place in range(3):
                part = ref[start + place * unit : start + (place + 1) * unit, :].astype(F32)
                if split_second and place > 0:
                    outs[place][flat, columns] = part
                else:
                    outs[place][tall, :] = part


def finish_first_kernel(small, got, bias_out, gain, shift, bias_down, bias_up):
    core = places()[0]
    for place, ref in enumerate((bias_out, gain, shift, bias_down)):
        mine, other = small[place : place + 1, :], got[place : place + 1, :]
        left = jnp.where(core == 0, mine, other)
        put_row(ref, jnp.concatenate([left, jnp.where(core == 0, other, mine)], axis=1))
    put_row(bias_up, small[4:5, :])


def finish_second_kernel(small, extra, got, w_ident, types, gain, shift, bias_q, bias_v):
    idw = w_ident.shape[0]
    count = idw + 4
    width = small.shape[1]
    mine = small[...] + extra[...].astype(F32)
    total = mine[: 2 * count] + got[: 2 * count, :]
    for out, first, size in ((w_ident, 0, idw), (types, idw, 2)):
        out[:, :width] = total[first : first + size]
        out[:, width:] = total[count + first : count + first + size]
    for out, first in ((gain, idw + 2), (shift, idw + 3)):
        row = [total[place : place + 1] for place in (first, count + first)]
        put_row(out, jnp.concatenate(row, axis=1))
    put_row(bias_q, mine[2 * count : 2 * count + 1])
    put_row(bias_v, mine[2 * count + 1 : 2 * count + 2])


def per_device(
    features, lap_vectors, node_counts, edge_counts, endpoints, w_ident, type_table,
    gain_one, shift_one, w_query, w_key, w_value, bias_query, bias_value, w_out, bias_out,
    gain_two, shift_two, w_up, bias_up, w_down, bias_down, cotangent,
):
    dp_count = lax.axis_size("dp")
    dp_index = lax.axis_index("dp")
    mp_index = lax.axis_index("mp")
    block = INNER * OUTER
    rest_count = dp_count // block
    def swap(part):
        return lax.ppermute(part, "mp", [(0, 1), (1, 0)])

    def inner_move(part, step):
        return lax.ppermute(part, "dp", [(s, s ^ step) for s in range(dp_count)])

    def outer_move(part, step):
        return lax.ppermute(part, "dp", [(s, s ^ (step * INNER)) for s in range(dp_count)])

    rows_all, dim = features.shape
    rows = rows_all // 2
    mols = rows // SEQ
    width = w_query.shape[1]
    heads = width // HDIM
    lapk = lap_vectors.shape[1]
    idw = w_ident.shape[0]

    def pinned(part):
        return pltpu.with_memory_space_constraint(part, pltpu.HBM)

    def lanes(part):
        return pinned(part.reshape(-1, LANES))

    nodes, edges = pinned(node_counts), pinned(edge_counts)
    count_scratch = pltpu.SMEM(node_counts.shape, jnp.int32)
    wide_scratch = pltpu.VMEM((dim // LANES, LANES), BF16)
    half_scratch = pltpu.VMEM((width // LANES, LANES), BF16)
    embed_args = (
        pinned(features), pinned(lap_vectors.T), pinned(endpoints.T), nodes,
        pinned(w_ident), pinned(type_table), lanes(gain_one), lanes(shift_one),
    )
    embed_scratch = [
        pltpu.VMEM((rows, dim), BF16),
        pltpu.VMEM((lapk, rows), BF16),
        pltpu.VMEM((2, rows), jnp.int32),
        count_scratch,
        pltpu.VMEM((idw, dim), BF16),
        pltpu.VMEM((2, dim), BF16),
        wide_scratch,
        wide_scratch,
    ]

    wq_got, wk_got, wv_got = swap(w_query), swap(w_key), swap(w_value)
    bq_got, bv_got, bu_got = swap(bias_query), swap(bias_value), swap(bias_up)
    wo_got, wu_got, wd_got = swap(w_out), swap(w_up), swap(w_down)

    hidden, ident, normed, normed_t, q_own, k_own, v_own = call(
        embed_kernel,
        (
            *embed_args, lanes(bias_query), lanes(bias_value),
            pinned(w_query), pinned(w_key), pinned(w_value),
        ),
        [outside()] * 13,
        [
            ((rows, dim), F32),
            ((idw, rows), BF16),
            ((rows, dim), BF16),
            ((dim, rows), BF16),
            ((rows, width), BF16),
            ((rows, width), BF16),
            ((rows, width), BF16),
        ],
        scratch=embed_scratch
        + [half_scratch] * 2
        + [pltpu.VMEM((dim, width), BF16)] * 3
        + [pltpu.SemaphoreType.DMA((13,))],
    )
    sent_rows = dim + 2 * width + 3 * rows + 16
    (
        q_got, k_got, v_got, probs, kept_a, sent_a, middle, active, grad_middle, grad_branch,
    ) = call(
        forward_kernel,
        (
            hidden, normed, q_own, k_own, v_own, wq_got, wk_got, wv_got,
            w_out, wo_got, w_up, wu_got, w_down, wd_got,
            *(part.reshape(-1, LANES) for part in (bq_got, bv_got, bu_got)),
            nodes, edges, pinned(cotangent),
            lanes(bias_up), lanes(bias_out), lanes(gain_two), lanes(shift_two),
        ),
        [whole()] * 17 + [outside()] * 7,
        [
            ((rows, width), BF16),
            ((rows, width), BF16),
            ((rows, width), BF16),
            ((mols, heads, SEQ, 2 * SEQ), BF16),
            ((sent_rows, width), BF16),
            ((sent_rows, width), BF16),
            ((rows, dim), F32),
            ((rows, dim), BF16),
            ((rows, dim), F32),
            ((rows, dim), BF16),
        ],
        scratch=[
            count_scratch,
            count_scratch,
            pltpu.VMEM((rows, dim), BF16),
            half_scratch,
            wide_scratch,
            wide_scratch,
            wide_scratch,
            pltpu.SemaphoreType.DMA((7,)),
            pltpu.VMEM((width, SEQ), F32),
            pltpu.VMEM((rows, dim), BF16),
            pltpu.VMEM((rows, dim), F32),
            pltpu.VMEM((rows, dim), BF16),
            pltpu.VMEM((rows, dim), F32),
            pltpu.VMEM((rows, dim), BF16),
        ],
        limit=30,
    )
    got_a = swap(sent_a)
    ga_own, ga_got = call(
        branch_kernel,
        (grad_branch, w_out, wo_got, nodes, edges),
        [whole()] * 3 + [outside()] * 2,
        [((rows, width), BF16), ((rows, width), BF16)],
        scratch=[count_scratch, count_scratch, pltpu.SemaphoreType.DMA((2,))],
    )

    unit = dim // block
    chunk = 3 * unit
    small_a, small_b = 16, 80

    def rest_sum(part):
        if rest_count == 1:
            return part
        groups = [[r * block + s for r in range(rest_count)] for s in range(block)]
        return lax.psum(part.astype(F32), "dp", axis_index_groups=groups).astype(part.dtype)

    pair = 2 * chunk

    def after(part, *others):
        return lax.optimization_barrier((part, *others))[0]

    def plane_all(parts, others=(), micros=0):
        got = [after(inner_move(parts[step], step), *others) for step in range(1, INNER)]
        return call(
            plane_all_kernel,
            (parts[0], *got),
            [whole()] * INNER,
            [
                ((chunk, width), BF16),
                ((parts[0].shape[0] - (OUTER - 1) * chunk, width), BF16),
                ((chunk, width), BF16),
                ((chunk, width), BF16),
            ],
            micros=micros,
        )

    def plane_step(parts, extra, micros=0):
        first, first_sent, second, second_sent = parts
        first_got, second_got = inner_move(first_sent, 1), inner_move(second_sent, 2)
        small_rows = extra[0].shape[0]
        return call(
            plane_sum_kernel,
            (first, first_got, second, second_got, *extra),
            [whole()] * 6,
            [((pair + small_rows, width), BF16)] * 2 + [((pair, width), BF16)] * 2,
            micros=micros,
        )

    def plane_turn(parts, others=(), micros=0):
        first, first_sent, second, second_sent = parts
        first_got = after(inner_move(first_sent, 2), *others)
        second_got = after(inner_move(second_sent, 1), *others)
        return call(
            line_cut_kernel,
            (first, first_got, second, second_got),
            [whole()] * 4,
            [
                ((chunk, width), BF16),
                ((first.shape[0] - chunk, width), BF16),
                ((chunk, width), BF16),
                ((chunk, width), BF16),
            ],
            micros=micros,
        )

    def line_step(parts, others=(), micros=0):
        got = [after(outer_move(parts[turn], turn), *others) for turn in range(1, OUTER)]
        mine, both = call(
            line_sum_kernel,
            (parts[0], parts[1], *got),
            [whole()] * 5,
            [((chunk, width), BF16), (parts[1].shape, BF16)],
            micros=micros,
        )
        if rest_count > 1:
            both = rest_sum(both)
            mine = both[:chunk]
        return mine, both

    def line_back(mine, both, others=(), micros=0):
        sent = (mine, both, mine)
        got = [after(outer_move(sent[turn - 1], turn), *others) for turn in range(1, OUTER)]
        small_rows = both.shape[0] - chunk
        return call(
            line_join_kernel,
            (both, *got),
            [whole()] * OUTER,
            [
                ((OUTER * chunk + small_rows, width), BF16),
                ((OUTER * chunk, width), BF16),
                ((small_rows, width), F32),
            ],
            micros=micros,
        )

    def plane_back(lines):
        return inner_move(lines[0], 1), inner_move(lines[1], 2)

    def plane_back_turn(side_x, side_y):
        return inner_move(side_y[:pair], 1), inner_move(side_x[pair : 2 * pair], 2)

    def placed(planes, split_second, micros=0):
        tall, flat = ((dim, width), F32), ((width, dim), F32)
        return call(
            lambda *refs: place_kernel(split_second, *refs),
            planes,
            [whole()] * len(planes),
            [tall, flat, flat] if split_second else [tall] * 3,
            micros=micros,
        )

    def attend_back(m, query_rows):
        return call(
            lambda *refs: attend_back_kernel(m, *refs),
            (query_rows, k_own, v_own, ga_own, q_got, k_got, v_got, ga_got, probs),
            [whole()] * 9,
            [((3 * SEQ, width), BF16)] * 2,
            scratch=[
                pltpu.VMEM((2, width, SEQ), F32),
                pltpu.VMEM((2, SEQ, width), F32),
                pltpu.VMEM((2, SEQ, width), F32),
            ],
        )

    backs = [attend_back(0, q_own)]
    kept_a = after(kept_a, backs[0][0])
    parts_a = call(
        ffn_grads_kernel,
        (kept_a, got_a, pinned(cotangent), nodes, edges),
        [whole()] * 2 + [outside()] * 3,
        [((OUTER * chunk + small_a, width), BF16)] * INNER,
        scratch=[
            pltpu.VMEM((rows_all, dim), BF16),
            count_scratch,
            count_scratch,
            pltpu.SemaphoreType.DMA((3,)),
            pltpu.VMEM((dim, width), BF16),
            pltpu.VMEM((4, width, width), BF16),
            pltpu.VMEM((rows_all, dim), BF16),
        ],
    )
    for m in range(1, mols):
        backs.append(attend_back(m, after(q_own, parts_a[0], backs[-1][0])))
    kept_b = [back[0] for back in backs]
    sent_b = [back[1] for back in backs]
    got_b = [swap(sent) for sent in sent_b]
    normed_t_got = call(
        partner_kernel,
        (*embed_args[:4], pinned(after(w_ident, kept_b[-1])), *embed_args[5:]),
        [outside()] * 8,
        [((dim, rows), BF16)],
        scratch=embed_scratch + [pltpu.SemaphoreType.DMA((8,))],
    )[0]
    parts_b = call(
        qkv_grads_kernel,
        (normed_t, normed_t_got, *kept_b, *got_b),
        [whole()] * (2 + 2 * mols),
        [((INNER * chunk, width), BF16)] * 4 + [((small_b, width), F32)],
        scratch=[
            pltpu.VMEM((3, dim, width), BF16),
            pltpu.VMEM((dim, 2 * rows), BF16),
            pltpu.VMEM((2 * rows, width), BF16),
        ],
    )
    grad_middle = after(grad_middle, parts_b[0])
    grad_features, small_own = call(
        embed_back_kernel,
        (
            *kept_b, *sent_b, w_query, w_key, w_value, wq_got, wk_got, wv_got, ident,
            grad_middle, embed_args[0], nodes, *embed_args[4:7],
        ),
        [whole()] * (8 + 2 * mols) + [outside()] * 5,
        [((rows, dim), F32), ((small_b, width), F32)],
        scratch=[
            pltpu.VMEM((rows, dim), BF16),
            count_scratch,
            pltpu.VMEM((idw, dim), BF16),
            pltpu.VMEM((2, dim), BF16),
            wide_scratch,
            pltpu.SemaphoreType.DMA((5,)),
            pltpu.VMEM((rows, dim), F32),
            pltpu.VMEM((idw + 8, dim), F32),
            pltpu.VMEM((rows, width), BF16),
        ],
        micros=0,
    )
    steps_b = plane_step(parts_b[:4], (small_own, parts_b[4]), micros=0)
    turned_a = plane_all(parts_a, others=(small_own,), micros=5)
    line_a = line_step(turned_a, others=steps_b, micros=3)
    turned_b = plane_turn(steps_b, others=line_a[:1], micros=0)
    lines_a = line_back(*line_a, others=turned_b, micros=3)
    line_b = line_step(turned_b, micros=8)
    planes_a = [lines_a[1]] + [inner_move(lines_a[1], step) for step in range(1, INNER)]
    wide, half = ((dim // LANES, LANES), F32), ((width // LANES, LANES), F32)
    lines_b = line_back(*line_b, others=planes_a[1:], micros=0)
    result = call(
        result_kernel,
        (middle, active, w_down, wd_got, lanes(after(bias_down, lines_b[1]))),
        [whole()] * 5,
        [((rows, dim), BF16)],
    )[0]
    sums_a = call(
        finish_first_kernel, (lines_a[2], swap(after(lines_a[2], lines_b[1]))), [whole()] * 2, [wide] * 4 + [half]
    )
    sides_b = plane_back(lines_b)
    far_b = plane_back_turn(*sides_b)
    planes_b = (lines_b[1], sides_b[0], sides_b[1], *far_b)
    extra = sides_b[0][OUTER * chunk :]
    own_b = lines_b[2] + extra.astype(F32)
    sums_b = call(
        finish_second_kernel,
        (lines_b[2], extra, swap(own_b)),
        [whole()] * 3,
        [((idw, dim), F32), ((2, dim), F32), wide, wide, half, half],
    )
    grad_w_up, grad_w_out, grad_w_down = placed(planes_a, True, micros=0)
    grad_w_query, grad_w_key, grad_w_value = placed(planes_b, False)
    return (
        result,
        grad_features,
        sums_b[0],
        sums_b[1],
        sums_b[2].reshape(-1),
        sums_b[3].reshape(-1),
        grad_w_query,
        grad_w_key,
        grad_w_value,
        sums_b[4].reshape(-1),
        sums_b[5].reshape(-1),
        grad_w_out,
        sums_a[0].reshape(-1),
        sums_a[1].reshape(-1),
        sums_a[2].reshape(-1),
        grad_w_up,
        sums_a[4].reshape(-1),
        grad_w_down,
        sums_a[3].reshape(-1),
    )


def solution(mesh):
    token, split = P("dp", None), P(("dp", "mp"), None)
    columns, lines, cut, copy = P(None, "mp"), P("mp", None), P("mp"), P()
    return jax.shard_map(
        per_device,
        mesh=mesh,
        in_specs=(
            token, token, P("dp"), P("dp"), token, copy, copy, copy, copy, columns, columns,
            columns, cut, cut, lines, copy, copy, copy, columns, cut, lines, copy, token,
        ),
        out_specs=(
            split, split, copy, copy, copy, copy, columns, columns, columns, cut, cut, lines,
            copy, copy, copy, columns, cut, lines, copy,
        ),
        check_vma=False,
    )
```

```python
import math

import jax
import jax.numpy as jnp
from jax import lax
from jax.experimental import pallas as pl
from jax.experimental.pallas import tpu as pltpu
from jax.sharding import PartitionSpec as P

HDIM = 24
SEQ = 128
LANES = 128
INNER = 4
OUTER = 4
EPSILON = 1e-05
SCALE = 1.0 / math.sqrt(HDIM)
F32, BF16 = jnp.float32, jnp.bfloat16
MIB = 1024 * 1024


def dot(left, right):
    return jnp.dot(left, right, preferred_element_type=F32)


def dot_nt(left, right):
    return lax.dot_general(left, right, (((1,), (1,)), ((), ())), preferred_element_type=F32)


def dot_tn(left, right):
    return lax.dot_general(left, right, (((0,), (0,)), ((), ())), preferred_element_type=F32)


def norm_parts(hidden):
    average = jnp.mean(hidden, axis=-1, keepdims=True)
    centred = hidden - average
    inverse = lax.rsqrt(jnp.mean(centred * centred, axis=-1, keepdims=True) + EPSILON)
    return centred * inverse, inverse


def norm_back(unit, inverse, grad_hat):
    return inverse * (
        grad_hat
        - jnp.mean(grad_hat, axis=-1, keepdims=True)
        - unit * jnp.mean(grad_hat * unit, axis=-1, keepdims=True)
    )


def row_sum(block):
    return jnp.sum(block, axis=0, keepdims=True)


def positions(length):
    return lax.broadcasted_iota(jnp.int32, (length, 1), 0)


def whole():
    return pl.BlockSpec(memory_space=pltpu.VMEM)


def outside():
    return pl.BlockSpec(memory_space=pltpu.HBM)


def places():
    index = lax.axis_index("dp")
    return lax.axis_index("mp"), index % INNER, index // INNER % OUTER


def copy_in(sources, targets, sems):
    copies = [
        pltpu.make_async_copy(source, target, sems.at[place])
        for place, (source, target) in enumerate(zip(sources, targets))
    ]
    for copy in copies:
        copy.start()
    return copies


def row_of(ref):
    block = ref[...].astype(F32)
    return jnp.concatenate([block[r : r + 1, :] for r in range(block.shape[0])], axis=1)


def put_row(ref, row):
    for r in range(ref.shape[0]):
        ref[r : r + 1, :] = row[:, r * LANES : (r + 1) * LANES]


def call(kernel, args, specs, outs, scratch=(), micros=0, limit=24):
    return pl.pallas_call(
        kernel,
        out_shape=[jax.ShapeDtypeStruct(shape, kind) for shape, kind in outs],
        in_specs=specs,
        out_specs=[whole() for _ in outs],
        scratch_shapes=list(scratch),
        compiler_params=pltpu.CompilerParams(vmem_limit_bytes=limit * MIB),
        cost_estimate=pl.CostEstimate(
            flops=micros * 1_000_000_000, bytes_accessed=0, transcendentals=0
        ),
    )(*args)


def head_windows(width):
    windows = []
    for pair in range(width // (2 * HDIM)):
        low = pair * 2 * HDIM // LANES * LANES
        high = -(-(pair + 1) * 2 * HDIM // LANES) * LANES
        windows.append((low, high))
    return windows


def split_heads(block, pair, window):
    low, high = window
    part = block[:, low:high]
    column = low + lax.broadcasted_iota(jnp.int32, (16, high - low), 1)
    sides = []
    for head in (2 * pair, 2 * pair + 1):
        inside = (column >= head * HDIM) & (column < (head + 1) * HDIM)
        mask = jnp.where(inside, 1.0, 0.0).astype(BF16)
        sides.append(part * jnp.concatenate([mask] * (block.shape[0] // 16), axis=0))
    return jnp.concatenate(sides, axis=0)


def embed_rows(feats, lap, ends, w_ident, types, gain, shift, at, count):
    table = lap[:, at]
    slot = lax.broadcasted_iota(jnp.int32, (SEQ, SEQ), 0)
    picked = []
    for end in (0, 1):
        pick = jnp.where(ends[end : end + 1, at] == slot, 1.0, 0.0).astype(BF16)
        picked.append(dot(table, pick))
    ident = jnp.concatenate(picked, axis=0).astype(BF16)
    hidden = feats[at, :].astype(F32) + dot_tn(ident, w_ident[...])
    kinds = types[...].astype(F32)
    hidden = hidden + jnp.where(positions(SEQ) >= count, kinds[1:2, :], kinds[0:1, :])
    unit, _ = norm_parts(hidden)
    return hidden, ident, (unit * gain + shift).astype(BF16)


def embed_kernel(
    feats_in, lap_in, ends_in, nodes_in, w_ident_in, types_in, gain_in, shift_in,
    bias_q_in, bias_v_in, wq_in, wk_in, wv_in,
    hidden_out, ident_out, normed_out, normed_t_out, q_out, k_out, v_out,
    feats, lap, ends, nodes, w_ident, types, gain_rows, shift_rows, bias_q, bias_v,
    w_q, w_k, w_v, sems,
):
    rows, dim = feats.shape
    mols = rows // SEQ
    core = places()[0]
    own_rows = pl.ds(pl.multiple_of(core * rows, SEQ), rows)
    copies = copy_in(
        (
            feats_in.at[own_rows, :], lap_in.at[:, own_rows], ends_in.at[:, own_rows], nodes_in,
            w_ident_in, types_in, gain_in, shift_in, bias_q_in, bias_v_in, wq_in, wk_in, wv_in,
        ),
        (
            feats, lap, ends, nodes, w_ident, types, gain_rows, shift_rows, bias_q, bias_v,
            w_q, w_k, w_v,
        ),
        sems,
    )
    for copy in copies[:10]:
        copy.wait()
    gain, shift = row_of(gain_rows), row_of(shift_rows)

    def molecule(m, carry):
        at = pl.ds(pl.multiple_of(m * SEQ, SEQ), SEQ)
        count = nodes[core * mols + m]
        hidden, ident, normed = embed_rows(
            feats, lap, ends, w_ident, types, gain, shift, at, count
        )
        ident_out[:, at] = ident
        hidden_out[at, :] = hidden
        normed_out[at, :] = normed
        normed_t_out[:, at] = normed.T
        return carry

    lax.fori_loop(0, mols, molecule, 0)
    normed = normed_out[...]
    copies[10].wait()
    q_out[...] = (dot(normed, w_q[...]) + row_of(bias_q)).astype(BF16)
    copies[11].wait()
    k_out[...] = dot(normed, w_k[...]).astype(BF16)
    copies[12].wait()
    v_out[...] = (dot(normed, w_v[...]) + row_of(bias_v)).astype(BF16)


def forward_kernel(
    hidden, normed, q_own, k_own, v_own, w_q, w_k, w_v, wo_own, wo, wu_own, wu, wd_own, wd,
    bias_q, bias_v, bias_u,
    nodes_in, edges_in, cots_in, bias_u_own_in, bias_o_in, gain_in, shift_in,
    q_out, k_out, v_out, probs_out, keep_out, send_out, middle, active, gm_out, grad_branch,
    nodes, edges, cots, bias_u_own, bias_o, gain_rows, shift_rows, sems,
    mixed, attended, unit, normed_two, slope, grad_ffn,
):
    rows, dim = hidden.shape
    width = q_own.shape[1]
    mols = rows // SEQ
    pairs = width // (2 * HDIM)
    windows = head_windows(width)
    core = places()[0]
    copies = copy_in(
        (
            nodes_in, edges_in, cots_in.at[pl.ds(pl.multiple_of(core * rows, SEQ), rows), :],
            bias_u_own_in, bias_o_in, gain_in, shift_in,
        ),
        (nodes, edges, cots, bias_u_own, bias_o, gain_rows, shift_rows),
        sems,
    )

    q_out[...] = (dot(normed[...], w_q[...]) + row_of(bias_q)).astype(BF16)
    k_out[...] = dot(normed[...], w_k[...]).astype(BF16)
    v_out[...] = (dot(normed[...], w_v[...]) + row_of(bias_v)).astype(BF16)

    for copy in copies:
        copy.wait()
    gain, shift, bias_out = row_of(gain_rows), row_of(shift_rows), row_of(bias_o)

    def attend(m, carry):
        at = pl.ds(pl.multiple_of(m * SEQ, SEQ), SEQ)
        place = core * mols + m
        count = nodes[place] + edges[place]
        key_keep = positions(SEQ) < count
        query_keep = lax.broadcasted_iota(jnp.int32, (1, SEQ), 1) < count
        sides = ((q_own, k_own, v_own, keep_out), (q_out, k_out, v_out, send_out))
        for side, (q_ref, k_ref, v_ref, part_out) in enumerate(sides):
            queries, key_rows = q_ref[at, :], k_ref[at, :]
            values_t = v_ref[at, :].T
            for pair in range(pairs):
                low, high = windows[pair]
                both = split_heads(queries, pair, windows[pair])
                scores = dot_nt(key_rows[:, low:high], both) * SCALE
                scores = jnp.where(key_keep, scores, -1e30)
                top = jnp.max(scores, axis=0, keepdims=True)
                raised = jnp.exp(scores - top)
                total = row_sum(raised)
                probs = (raised * (1.0 / total)).astype(BF16)
                probs_out[m, side * pairs + pair] = probs
                first = pair * 2 * HDIM
                out = dot(values_t[first : first + 2 * HDIM], probs)
                mixed[first : first + HDIM, :] = out[:HDIM, :SEQ]
                mixed[first + HDIM : first + 2 * HDIM, :] = out[HDIM:, SEQ:]
            kept = jnp.where(query_keep, mixed[...], 0.0).astype(BF16)
            part_out[dim : dim + width, at] = kept
            attended[at, side * width : (side + 1) * width] = kept.T
        return carry

    lax.fori_loop(0, mols, attend, 0)
    middle[...] = (
        hidden[...] + dot(attended[:, :width], wo_own[...]) + dot(attended[:, width:], wo[...])
    )

    def second_norm(m, carry):
        at = pl.ds(pl.multiple_of(m * SEQ, SEQ), SEQ)
        place = core * mols + m
        keep = positions(SEQ) < nodes[place] + edges[place]
        total = middle[at, :] + bias_out
        middle[at, :] = total
        unit_rows, _ = norm_parts(total)
        unit[at, :] = unit_rows
        rows_two = (unit_rows * gain + shift).astype(BF16)
        normed_two[at, :] = rows_two
        turned = rows_two.T
        keep_out[:dim, at] = turned
        send_out[:dim, at] = turned
        grad_ffn[at, :] = jnp.where(keep, cots[at, :].astype(F32), 0.0).astype(BF16)
        return carry

    lax.fori_loop(0, mols, second_norm, 0)

    for side, (w_ref, b_ref, part_out) in enumerate(
        ((wu_own, bias_u_own, keep_out), (wu, bias_u, send_out))
    ):
        columns = slice(side * width, (side + 1) * width)
        slope[:, columns] = dot(normed_two[...], w_ref[...]) + row_of(b_ref)

        def activate(m, carry):
            at = pl.ds(pl.multiple_of(m * SEQ, SEQ), SEQ)
            before = slope[at, columns]
            phi = 0.5 * (1.0 + lax.erf(before * math.sqrt(0.5)))
            out = (before * phi).astype(BF16)
            slope[at, columns] = phi + before * jnp.exp(before * before * -0.5) * (
                1.0 / math.sqrt(2.0 * math.pi)
            )
            active[at, columns] = out
            part_out[dim + width : dim + 2 * width, at] = out.T
            return carry

        lax.fori_loop(0, mols, activate, 0)

    place_b = dim + 2 * width
    for side, (w_ref, part_out) in enumerate(((wd_own, keep_out), (wd, send_out))):
        columns = slice(side * width, (side + 1) * width)
        grad_before = slope[:, columns] * dot_nt(grad_ffn[...], w_ref[...])
        part_out[place_b : place_b + rows, :] = grad_before.astype(BF16)

    back = pl.ds(place_b, rows)
    gm_out[...] = dot_nt(keep_out[back, :], wu_own[...]) + dot_nt(send_out[back, :], wu[...])

    def second_back(m, sums):
        at = pl.ds(pl.multiple_of(m * SEQ, SEQ), SEQ)
        place = core * mols + m
        keep = positions(SEQ) < nodes[place] + edges[place]
        grad_normed = gm_out[at, :]
        unit_rows = unit[at, :]
        _, inverse = norm_parts(middle[at, :])
        grad_result = jnp.where(keep, cots[at, :].astype(F32), 0.0)
        grad = grad_result + norm_back(unit_rows, inverse, grad_normed * gain)
        gm_out[at, :] = grad
        grad_branch[at, :] = grad.astype(BF16)
        return (
            sums[0] + row_sum(grad),
            sums[1] + row_sum(grad_normed * unit_rows),
            sums[2] + row_sum(grad_normed),
            sums[3] + row_sum(grad_result),
        )

    nothing = jnp.zeros((1, dim), F32)
    sums = lax.fori_loop(0, mols, second_back, (nothing,) * 4)
    place_m = place_b + rows
    for part_out in (keep_out, send_out):
        part_out[place_m : place_m + rows, :] = grad_branch[:, :width]
        part_out[place_m + rows : place_m + 2 * rows, :] = grad_branch[:, width:]
    small = jnp.concatenate(list(sums) + [nothing] * 12, axis=0)
    left, right = small[:, :width], small[:, width:]
    place_s = place_m + 2 * rows
    keep_out[place_s:, :] = jnp.where(core == 0, left, right).astype(BF16)
    send_out[place_s:, :] = jnp.where(core == 0, right, left).astype(BF16)


def result_kernel(middle, active, wd_own, wd, bias, result_out):
    width = wd.shape[0]
    result_out[...] = (
        middle[...]
        + dot(active[:, :width], wd_own[...])
        + dot(active[:, width:], wd[...])
        + row_of(bias)
    ).astype(BF16)


def branch_kernel(
    grad_branch, wo_own, wo, nodes_in, edges_in, ga_own_out, ga_out, nodes, edges, sems
):
    mols = grad_branch.shape[0] // SEQ
    core = places()[0]
    copies = copy_in((nodes_in, edges_in), (nodes, edges), sems)
    products = [dot_nt(grad_branch[...], weight[...]) for weight in (wo_own, wo)]
    for copy in copies:
        copy.wait()
    for ref, product in zip((ga_own_out, ga_out), products):
        for m in range(mols):
            place = core * mols + m
            keep = positions(SEQ) < nodes[place] + edges[place]
            at = slice(m * SEQ, (m + 1) * SEQ)
            ref[at, :] = jnp.where(keep, product[at], 0.0).astype(BF16)


def attend_back_kernel(
    m, q_own, k_own, v_own, ga_own, q_got, k_got, v_got, ga_got, probs_all,
    keep_out, send_out, dq_t, dk, dv,
):
    width = q_own.shape[1]
    pairs = width // (2 * HDIM)
    windows = head_windows(width)
    at = slice(m * SEQ, (m + 1) * SEQ)
    sides = (
        (q_own, k_own, v_own, ga_own, keep_out),
        (q_got, k_got, v_got, ga_got, send_out),
    )
    for side, (q_ref, k_ref, v_ref, g_ref, part_out) in enumerate(sides):
        queries, key_rows, values, grads = q_ref[at, :], k_ref[at, :], v_ref[at, :], g_ref[at, :]
        keys_t = key_rows.T
        dk[side] = jnp.zeros_like(dk[side])
        dv[side] = jnp.zeros_like(dv[side])
        for pair in range(pairs):
            low, high = windows[pair]
            both_q = split_heads(queries, pair, windows[pair])
            both_g = split_heads(grads, pair, windows[pair])
            probs_low = probs_all[m, side * pairs + pair]
            probs = probs_low.astype(F32)
            grad_probs = dot_nt(values[:, low:high], both_g)
            inner = row_sum(probs * grad_probs)
            grad_scores = (probs * (grad_probs - inner)).astype(BF16)
            dv[side, :, low:high] += dot(probs_low, both_g)
            dk[side, :, low:high] += dot(grad_scores, both_q)
            first = pair * 2 * HDIM
            out = dot(keys_t[first : first + 2 * HDIM], grad_scores)
            dq_t[side, first : first + HDIM, :] = out[:HDIM, :SEQ]
            dq_t[side, first + HDIM : first + 2 * HDIM, :] = out[HDIM:, SEQ:]
        part_out[:SEQ, :] = (dq_t[side] * SCALE).astype(BF16).T
        part_out[SEQ : 2 * SEQ, :] = (dk[side] * SCALE).astype(BF16)
        part_out[2 * SEQ :, :] = dv[side].astype(BF16)


def embed_back_kernel(*refs):
    mols = (len(refs) - 25) // 2
    grads_own, grads = refs[:mols], refs[mols : 2 * mols]
    (
        wq_own, wk_own, wv_own, w_q, w_k, w_v, ident, grad_middle,
        feats_in, nodes_in, w_ident_in, types_in, gain_in,
        features_out, keep_out, send_out,
        feats, nodes, w_ident, types, gain_rows, sems, grad_normed, small, stacked,
    ) = refs[2 * mols :]
    core = places()[0]
    rows = feats.shape[0]
    copies = copy_in(
        (
            feats_in.at[pl.ds(pl.multiple_of(core * rows, SEQ), rows), :], nodes_in,
            w_ident_in, types_in, gain_in,
        ),
        (feats, nodes, w_ident, types, gain_rows),
        sems,
    )
    rows, dim = feats.shape
    width = wq_own.shape[1]
    idw = ident.shape[0]
    total = None
    for part, weights in ((grads_own, (wq_own, wk_own, wv_own)), (grads, (w_q, w_k, w_v))):
        for place, weight in enumerate(weights):
            for m in range(mols):
                stacked[m * SEQ : (m + 1) * SEQ, :] = part[m][place * SEQ : (place + 1) * SEQ, :]
            term = dot_nt(stacked[...], weight[...])
            total = term if total is None else total + term
    grad_normed[...] = total
    small[...] = jnp.zeros_like(small)
    for copy in copies:
        copy.wait()
    gain = row_of(gain_rows)
    kinds = types[...].astype(F32)

    def molecule(m, carry):
        at = pl.ds(pl.multiple_of(m * SEQ, SEQ), SEQ)
        is_edge = positions(SEQ) >= nodes[core * mols + m]
        hidden = feats[at, :].astype(F32) + dot_tn(ident[:, at], w_ident[...])
        hidden = hidden + jnp.where(is_edge, kinds[1:2, :], kinds[0:1, :])
        unit, inverse = norm_parts(hidden)
        grad_rows = grad_normed[at, :]
        grad = grad_middle[at, :] + norm_back(unit, inverse, grad_rows * gain)
        features_out[at, :] = grad
        high = grad.astype(BF16)
        rest = (grad - high.astype(F32)).astype(BF16)
        picked = ident[:, at]
        small[:idw, :] += dot(picked, high) + dot(picked, rest)
        edge_rows = jnp.where(is_edge, grad, 0.0)
        small[idw : idw + 1, :] += row_sum(grad - edge_rows)
        small[idw + 1 : idw + 2, :] += row_sum(edge_rows)
        small[idw + 2 : idw + 3, :] += row_sum(grad_rows * unit)
        small[idw + 3 : idw + 4, :] += row_sum(grad_rows)
        return carry

    lax.fori_loop(0, mols, molecule, 0)
    left, right = small[:, :width], small[:, width:]
    keep_out[...] = jnp.where(core == 0, left, right)
    send_out[...] = jnp.where(core == 0, right, left).astype(BF16)


def deal_direct(unit, outs, block_at, small):
    _, inner, outer = places()
    for step, out in enumerate(outs):
        for turn in range(OUTER):
            start = turn * 3 * unit
            for place in range(3):
                out[start + place * unit : start + (place + 1) * unit, :] = block_at(
                    inner ^ step, outer ^ turn, place
                )
        out[OUTER * 3 * unit :, :] = small


def deal(unit, outs, block_at):
    _, inner, outer = places()
    first_kept, first_sent, second_kept, second_sent = outs
    for step in range(INNER):
        for turn in range(OUTER):
            if turn < 2:
                out, slot = (first_sent if step % 2 else first_kept), step // 2
            else:
                out, slot = (second_sent if step // 2 else second_kept), step % 2
            start = (slot * 2 + turn % 2) * 3 * unit
            for place in range(3):
                out[start + place * unit : start + (place + 1) * unit, :] = block_at(
                    inner ^ step, outer ^ turn, place
                )


def ffn_grads_kernel(kept, got, cots_in, nodes_in, edges_in, *rest):
    outs, (cots, nodes, edges, sems, tall, flat, grad_ffn) = rest[:4], rest[4:]
    copies = copy_in((nodes_in, edges_in, cots_in), (nodes, edges, cots), sems)
    rows_all, dim = cots.shape
    rows, width = rows_all // 2, kept.shape[1]
    mols = rows // SEQ
    core = places()[0]
    own_rows = pl.ds(pl.multiple_of(core * rows, SEQ), rows)
    other_rows = pl.ds(pl.multiple_of((1 - core) * rows, SEQ), rows)
    place_b = dim + 2 * width
    place_m = place_b + rows
    place_s = place_m + 2 * rows
    back = slice(place_b, place_m)
    tall[...] = (dot(kept[:dim, :], kept[back, :]) + dot(got[:dim, :], got[back, :])).astype(BF16)
    turned = slice(dim, dim + width)
    for half in (0, 1):
        mid = slice(place_m + half * rows, place_m + (half + 1) * rows)
        flat[half] = (
            dot(kept[turned, :], kept[mid, :]) + dot(got[turned, :], got[mid, :])
        ).astype(BF16)
    for copy in copies:
        copy.wait()
    for m in range(2 * mols):
        keep = positions(SEQ) < nodes[m] + edges[m]
        at = slice(m * SEQ, (m + 1) * SEQ)
        grad_ffn[at, :] = jnp.where(keep, cots[at, :].astype(F32), 0.0).astype(BF16)
    turned = slice(dim + width, dim + 2 * width)
    for half in (0, 1):
        columns = slice(half * width, (half + 1) * width)
        product = dot(kept[turned, :], grad_ffn[own_rows, columns])
        product = product + dot(got[turned, :], grad_ffn[other_rows, columns])
        flat[2 + half] = product.astype(BF16)
    bias = row_sum(kept[back, :].astype(F32)) + row_sum(got[back, :].astype(F32))
    small = kept[place_s:, :].astype(F32) + got[place_s:, :].astype(F32)
    spot = lax.broadcasted_iota(jnp.int32, small.shape, 0)
    small = jnp.where(spot == 4, bias, small).astype(BF16)
    unit = dim // (INNER * OUTER)

    def block_at(dest, z, place):
        if place == 0:
            return tall[pl.ds(pl.multiple_of((dest * OUTER + z) * unit, 16), unit), :]
        row = pl.multiple_of((dest * (OUTER // 2) + z // 2) * unit, 16)
        return flat[2 * (place - 1) + z % 2, pl.ds(row, unit), :]

    deal_direct(unit, outs, block_at, small)


def qkv_grads_kernel(normed_t, normed_t_got, *refs):
    mols = normed_t.shape[1] // SEQ
    kept, got = refs[:mols], refs[mols : 2 * mols]
    outs, small_out = refs[2 * mols : 2 * mols + 4], refs[2 * mols + 4]
    tall, normed, stacked = refs[2 * mols + 5 :]
    dim, rows = normed_t.shape
    unit = dim // (INNER * OUTER)
    normed[:, :rows] = normed_t[...]
    normed[:, rows:] = normed_t_got[...]
    spot = lax.broadcasted_iota(jnp.int32, small_out.shape, 0)
    small = jnp.zeros(small_out.shape, F32)
    for place in range(3):
        for m, part in enumerate(kept + got):
            stacked[m * SEQ : (m + 1) * SEQ, :] = part[place * SEQ : (place + 1) * SEQ, :]
        tall[place] = dot(normed[...], stacked[...]).astype(BF16)
        if place != 1:
            small = jnp.where(spot == 36 + place // 2, row_sum(stacked[...].astype(F32)), small)
    small_out[...] = small

    def block_at(dest, z, place):
        return tall[place, pl.ds(pl.multiple_of((dest * OUTER + z) * unit, 16), unit), :]

    deal(unit, outs, block_at)


def add(first, second):
    return (first.astype(F32) + second.astype(F32)).astype(BF16)


def plane_all_kernel(first, second, third, fourth, own, near, middle):
    chunk = own.shape[0]
    total = first[...].astype(F32) + second[...].astype(F32)
    total = (total + third[...].astype(F32) + fourth[...].astype(F32)).astype(BF16)
    own[...] = total[:chunk]
    near[:chunk, :] = total[chunk : 2 * chunk]
    near[chunk:, :] = total[3 * chunk :]
    middle[...] = total[2 * chunk : 3 * chunk]


def plane_sum_kernel(
    first, first_got, second, second_got, small_kept, small_got, small_more,
    first_kept, first_sent, second_kept, second_sent,
):
    pair = second_kept.shape[0]
    total = add(first[...], first_got[...])
    first_kept[:pair, :] = total[:pair]
    first_sent[:pair, :] = total[pair:]
    small = (small_kept[...] + small_got[...].astype(F32) + small_more[...]).astype(BF16)
    first_kept[pair:, :] = small
    first_sent[pair:, :] = small
    total = add(second[...], second_got[...])
    second_kept[...] = total[:pair]
    second_sent[...] = total[pair:]


def line_cut_kernel(first, first_got, second, second_got, own, near, middle):
    chunk = own.shape[0]
    total = add(first[...], first_got[...])
    own[...] = total[:chunk]
    near[:chunk, :] = total[chunk : 2 * chunk]
    near[2 * chunk :, :] = total[2 * chunk :]
    total = add(second[...], second_got[...])
    middle[...] = total[:chunk]
    near[chunk : 2 * chunk, :] = total[chunk:]


def line_near_kernel(own, near, middle, got, out, far):
    chunk = own.shape[0]
    out[...] = add(own[...], got[:chunk, :])
    far[:chunk, :] = add(middle[...], got[chunk : 2 * chunk, :])
    far[chunk:, :] = add(near[2 * chunk :, :], got[2 * chunk :, :])


def line_far_kernel(own, far, got, out, small_out):
    chunk = own.shape[0]
    out[...] = add(own[...], got[:chunk, :])
    small_out[...] = far[chunk:, :].astype(F32) + got[chunk:, :].astype(F32)


def join_kernel(*refs):
    outs = [ref for ref in refs if ref.shape[0] > refs[0].shape[0]]
    start = 0
    for part in refs[: len(refs) - len(outs)]:
        stop = start + part.shape[0]
        for out in outs:
            if stop <= out.shape[0]:
                out[start:stop, :] = part[...].astype(BF16)
        start = stop


def place_kernel(split_second, *refs):
    outs, parts = refs[-3:], refs[:-3]
    own = parts[0]
    _, inner, outer = places()
    unit = own.shape[0] // (3 * OUTER)
    width = own.shape[1]
    for step in range(INNER):
        for slot, turn in enumerate((0, 2, 1, 3)):
            ref, start = parts[step], slot * 3 * unit
            if len(parts) == 5 and step == 3 and slot >= 2:
                ref, start = parts[4], (slot - 2) * 3 * unit
            dest, z = inner ^ step, outer ^ turn
            tall = pl.ds(pl.multiple_of((dest * OUTER + z) * unit, 16), unit)
            flat = pl.ds(pl.multiple_of((dest * (OUTER // 2) + z // 2) * unit, 16), unit)
            columns = pl.ds(pl.multiple_of(z % 2 * width, LANES), width)
            for place in range(3):
                part = ref[start + place * unit : start + (place + 1) * unit, :].astype(F32)
                if split_second and place > 0:
                    outs[place][flat, columns] = part
                else:
                    outs[place][tall, :] = part


def finish_first_kernel(small, got, bias_out, gain, shift, bias_down, bias_up):
    core = places()[0]
    for place, ref in enumerate((bias_out, gain, shift, bias_down)):
        mine, other = small[place : place + 1, :], got[place : place + 1, :]
        left = jnp.where(core == 0, mine, other)
        put_row(ref, jnp.concatenate([left, jnp.where(core == 0, other, mine)], axis=1))
    put_row(bias_up, small[4:5, :])


def finish_second_kernel(small, extra, got, w_ident, types, gain, shift, bias_q, bias_v):
    idw = w_ident.shape[0]
    core = places()[0]
    mine, other = small[...] + extra[...].astype(F32), got[...]
    left = jnp.where(core == 0, mine, other)
    total = jnp.concatenate([left, jnp.where(core == 0, other, mine)], axis=1)
    w_ident[...] = total[:idw]
    types[...] = total[idw : idw + 2]
    put_row(gain, total[idw + 2 : idw + 3])
    put_row(shift, total[idw + 3 : idw + 4])
    put_row(bias_q, mine[idw + 4 : idw + 5])
    put_row(bias_v, mine[idw + 5 : idw + 6])


def per_device(
    features, lap_vectors, node_counts, edge_counts, endpoints, w_ident, type_table,
    gain_one, shift_one, w_query, w_key, w_value, bias_query, bias_value, w_out, bias_out,
    gain_two, shift_two, w_up, bias_up, w_down, bias_down, cotangent,
):
    dp_count = lax.axis_size("dp")
    dp_index = lax.axis_index("dp")
    mp_index = lax.axis_index("mp")
    block = INNER * OUTER
    rest_count = dp_count // block
    def swap(part):
        return lax.ppermute(part, "mp", [(0, 1), (1, 0)])

    def inner_move(part, step):
        return lax.ppermute(part, "dp", [(s, s ^ step) for s in range(dp_count)])

    def outer_move(part, step):
        return lax.ppermute(part, "dp", [(s, s ^ (step * INNER)) for s in range(dp_count)])

    rows_all, dim = features.shape
    rows = rows_all // 2
    mols = rows // SEQ
    width = w_query.shape[1]
    heads = width // HDIM
    lapk = lap_vectors.shape[1]
    idw = w_ident.shape[0]

    def pinned(part):
        return pltpu.with_memory_space_constraint(part, pltpu.HBM)

    def lanes(part):
        return pinned(part.reshape(-1, LANES))

    nodes, edges = pinned(node_counts), pinned(edge_counts)
    count_scratch = pltpu.SMEM(node_counts.shape, jnp.int32)
    wide_scratch = pltpu.VMEM((dim // LANES, LANES), BF16)
    half_scratch = pltpu.VMEM((width // LANES, LANES), BF16)
    embed_args = (
        pinned(features), pinned(lap_vectors.T), pinned(endpoints.T), nodes,
        pinned(w_ident), pinned(type_table), lanes(gain_one), lanes(shift_one),
    )
    embed_scratch = [
        pltpu.VMEM((rows, dim), BF16),
        pltpu.VMEM((lapk, rows), BF16),
        pltpu.VMEM((2, rows), jnp.int32),
        count_scratch,
        pltpu.VMEM((idw, dim), BF16),
        pltpu.VMEM((2, dim), BF16),
        wide_scratch,
        wide_scratch,
    ]

    wq_got, wk_got, wv_got = swap(w_query), swap(w_key), swap(w_value)
    bq_got, bv_got, bu_got = swap(bias_query), swap(bias_value), swap(bias_up)
    wo_got, wu_got, wd_got = swap(w_out), swap(w_up), swap(w_down)

    hidden, ident, normed, normed_t, q_own, k_own, v_own = call(
        embed_kernel,
        (
            *embed_args, lanes(bias_query), lanes(bias_value),
            pinned(w_query), pinned(w_key), pinned(w_value),
        ),
        [outside()] * 13,
        [
            ((rows, dim), F32),
            ((idw, rows), BF16),
            ((rows, dim), BF16),
            ((dim, rows), BF16),
            ((rows, width), BF16),
            ((rows, width), BF16),
            ((rows, width), BF16),
        ],
        scratch=embed_scratch
        + [half_scratch] * 2
        + [pltpu.VMEM((dim, width), BF16)] * 3
        + [pltpu.SemaphoreType.DMA((13,))],
    )
    sent_rows = dim + 2 * width + 3 * rows + 16
    (
        q_got, k_got, v_got, probs, kept_a, sent_a, middle, active, grad_middle, grad_branch,
    ) = call(
        forward_kernel,
        (
            hidden, normed, q_own, k_own, v_own, wq_got, wk_got, wv_got,
            w_out, wo_got, w_up, wu_got, w_down, wd_got,
            *(part.reshape(-1, LANES) for part in (bq_got, bv_got, bu_got)),
            nodes, edges, pinned(cotangent),
            lanes(bias_up), lanes(bias_out), lanes(gain_two), lanes(shift_two),
        ),
        [whole()] * 17 + [outside()] * 7,
        [
            ((rows, width), BF16),
            ((rows, width), BF16),
            ((rows, width), BF16),
            ((mols, heads, SEQ, 2 * SEQ), BF16),
            ((sent_rows, width), BF16),
            ((sent_rows, width), BF16),
            ((rows, dim), F32),
            ((rows, dim), BF16),
            ((rows, dim), F32),
            ((rows, dim), BF16),
        ],
        scratch=[
            count_scratch,
            count_scratch,
            pltpu.VMEM((rows, dim), BF16),
            half_scratch,
            wide_scratch,
            wide_scratch,
            wide_scratch,
            pltpu.SemaphoreType.DMA((7,)),
            pltpu.VMEM((width, SEQ), F32),
            pltpu.VMEM((rows, dim), BF16),
            pltpu.VMEM((rows, dim), F32),
            pltpu.VMEM((rows, dim), BF16),
            pltpu.VMEM((rows, dim), F32),
            pltpu.VMEM((rows, dim), BF16),
        ],
        limit=30,
    )
    got_a = swap(sent_a)
    ga_own, ga_got = call(
        branch_kernel,
        (grad_branch, w_out, wo_got, nodes, edges),
        [whole()] * 3 + [outside()] * 2,
        [((rows, width), BF16), ((rows, width), BF16)],
        scratch=[count_scratch, count_scratch, pltpu.SemaphoreType.DMA((2,))],
    )

    unit = dim // block
    chunk = 3 * unit
    small_a, small_b = 16, 48

    def rest_sum(part):
        if rest_count == 1:
            return part
        groups = [[r * block + s for r in range(rest_count)] for s in range(block)]
        return lax.psum(part.astype(F32), "dp", axis_index_groups=groups).astype(part.dtype)

    pair = 2 * chunk

    def after(part, *others):
        return lax.optimization_barrier((part, *others))[0]

    def line_shapes(small_rows):
        return [
            ((chunk, width), BF16), ((2 * chunk + small_rows, width), BF16), ((chunk, width), BF16),
        ]

    def plane_all(parts, others=(), micros=0):
        got = [after(inner_move(parts[step], step), *others) for step in range(1, INNER)]
        return call(
            plane_all_kernel,
            (parts[0], *got),
            [whole()] * INNER,
            line_shapes(parts[0].shape[0] - OUTER * chunk),
            micros=micros,
        )

    def plane_step(parts, extra, micros=0):
        first, first_sent, second, second_sent = parts
        first_got, second_got = inner_move(first_sent, 1), inner_move(second_sent, 2)
        small_rows = extra[0].shape[0]
        return call(
            plane_sum_kernel,
            (first, first_got, second, second_got, *extra),
            [whole()] * 7,
            [((pair + small_rows, width), BF16)] * 2 + [((pair, width), BF16)] * 2,
            micros=micros,
        )

    def plane_turn(parts, others=(), micros=0):
        first, first_sent, second, second_sent = parts
        first_got = after(inner_move(first_sent, 2), *others)
        second_got = after(inner_move(second_sent, 1), *others)
        return call(
            line_cut_kernel,
            (first, first_got, second, second_got),
            [whole()] * 4,
            line_shapes(first.shape[0] - pair),
            micros=micros,
        )

    def line_near(parts, others=(), micros=0):
        got = after(outer_move(parts[1], 1), *others)
        return call(
            line_near_kernel,
            (*parts, got),
            [whole()] * 4,
            [((chunk, width), BF16), ((parts[1].shape[0] - chunk, width), BF16)],
            micros=micros,
        )

    def line_far(parts, others=(), micros=0):
        got = after(outer_move(parts[1], 2), *others)
        mine, small = call(
            line_far_kernel,
            (*parts, got),
            [whole()] * 3,
            [((chunk, width), BF16), ((parts[1].shape[0] - chunk, width), F32)],
            micros=micros,
        )
        return rest_sum(mine), rest_sum(small)

    def line_back(mine, step, others=(), extra=(), micros=0):
        got = after(outer_move(mine, step), *others)
        size = 2 * mine.shape[0]
        more = sum(part.shape[0] for part in extra)
        return call(
            join_kernel,
            (mine, got, *extra),
            [whole()] * (2 + len(extra)),
            [((size + more, width), BF16)] * len(extra) + [((size, width), BF16)],
            micros=micros,
        )

    def plane_back(lines):
        return inner_move(lines[0], 1), inner_move(lines[1], 2)

    def plane_back_turn(side_x, side_y):
        return inner_move(side_y[:pair], 1), inner_move(side_x[pair : 2 * pair], 2)

    def placed(planes, split_second, micros=0):
        tall, flat = ((dim, width), F32), ((width, dim), F32)
        return call(
            lambda *refs: place_kernel(split_second, *refs),
            planes,
            [whole()] * len(planes),
            [tall, flat, flat] if split_second else [tall] * 3,
            micros=micros,
        )

    def attend_back(m, query_rows):
        return call(
            lambda *refs: attend_back_kernel(m, *refs),
            (query_rows, k_own, v_own, ga_own, q_got, k_got, v_got, ga_got, probs),
            [whole()] * 9,
            [((3 * SEQ, width), BF16)] * 2,
            scratch=[
                pltpu.VMEM((2, width, SEQ), F32),
                pltpu.VMEM((2, SEQ, width), F32),
                pltpu.VMEM((2, SEQ, width), F32),
            ],
        )

    backs = [attend_back(0, q_own)]
    kept_a = after(kept_a, backs[0][0])
    parts_a = call(
        ffn_grads_kernel,
        (kept_a, got_a, pinned(cotangent), nodes, edges),
        [whole()] * 2 + [outside()] * 3,
        [((OUTER * chunk + small_a, width), BF16)] * INNER,
        scratch=[
            pltpu.VMEM((rows_all, dim), BF16),
            count_scratch,
            count_scratch,
            pltpu.SemaphoreType.DMA((3,)),
            pltpu.VMEM((dim, width), BF16),
            pltpu.VMEM((4, width, width), BF16),
            pltpu.VMEM((rows_all, dim), BF16),
        ],
    )
    normed_t_got = swap(after(normed_t, parts_a[0]))
    for m in range(1, mols):
        gates = (parts_a[0], backs[-1][0]) + ((normed_t_got,) if m == mols - 1 else ())
        backs.append(attend_back(m, after(q_own, *gates)))
    kept_b = [back[0] for back in backs]
    sent_b = [back[1] for back in backs]
    got_b = [swap(sent) for sent in sent_b]
    parts_b = call(
        qkv_grads_kernel,
        (normed_t, normed_t_got, *kept_b, *got_b),
        [whole()] * (2 + 2 * mols),
        [((INNER * chunk, width), BF16)] * 4 + [((small_b, width), F32)],
        scratch=[
            pltpu.VMEM((3, dim, width), BF16),
            pltpu.VMEM((dim, 2 * rows), BF16),
            pltpu.VMEM((2 * rows, width), BF16),
        ],
    )
    grad_middle = after(grad_middle, parts_b[0])
    grad_features, small_kept, small_sent = call(
        embed_back_kernel,
        (
            *kept_b, *sent_b, w_query, w_key, w_value, wq_got, wk_got, wv_got, ident,
            grad_middle, embed_args[0], nodes, *embed_args[4:7],
        ),
        [whole()] * (8 + 2 * mols) + [outside()] * 5,
        [((rows, dim), F32), ((small_b, width), F32), ((small_b, width), BF16)],
        scratch=[
            pltpu.VMEM((rows, dim), BF16),
            count_scratch,
            pltpu.VMEM((idw, dim), BF16),
            pltpu.VMEM((2, dim), BF16),
            wide_scratch,
            pltpu.SemaphoreType.DMA((5,)),
            pltpu.VMEM((rows, dim), F32),
            pltpu.VMEM((small_b, dim), F32),
            pltpu.VMEM((rows, width), BF16),
        ],
        micros=0,
    )
    small_got = swap(small_sent)
    steps_b = plane_step(parts_b[:4], (small_kept, small_got, parts_b[4]))
    turned_a = plane_all(parts_a, others=(small_kept,), micros=2)
    near_a = line_near(turned_a, others=steps_b, micros=3)
    turned_b = plane_turn(steps_b, others=near_a[:1])
    line_a = line_far(near_a, micros=3)
    near_b = line_near(turned_b, others=line_a[:1])
    half_a = line_back(line_a[0], 2)[0]
    line_b = line_far(near_b, others=(half_a,))
    lines_a = line_back(half_a, 1)[0]
    half_b = line_back(line_b[0], 2, others=(lines_a,), micros=3)[0]
    sides_a = plane_back((lines_a, lines_a))
    far_a = plane_back_turn(*sides_a)
    planes_a = (lines_a, *sides_a, *far_a)
    lines_b = line_back(half_b, 1, others=far_a, extra=(line_b[1],))
    result = call(
        result_kernel,
        (middle, active, w_down, wd_got, lanes(after(bias_down, lines_b[1]))),
        [whole()] * 5,
        [((rows, dim), BF16)],
    )[0]
    wide, half = ((dim // LANES, LANES), F32), ((width // LANES, LANES), F32)
    sums_a = call(
        finish_first_kernel,
        (line_a[1], swap(after(line_a[1], lines_b[1]))),
        [whole()] * 2,
        [wide] * 4 + [half],
    )
    grad_w_up, grad_w_out, grad_w_down = placed(planes_a, True)
    sides_b = plane_back(lines_b)
    sides_b, _ = lax.optimization_barrier((sides_b, (result, sums_a, grad_w_up)))
    far_b = plane_back_turn(*sides_b)
    planes_b = (lines_b[1], sides_b[0], sides_b[1], *far_b)
    extra = sides_b[0][OUTER * chunk :]
    own_b = line_b[1] + extra.astype(F32)
    sums_b = call(
        finish_second_kernel,
        (line_b[1], extra, swap(own_b)),
        [whole()] * 3,
        [((idw, dim), F32), ((2, dim), F32), wide, wide, half, half],
    )
    grad_w_query, grad_w_key, grad_w_value = placed(planes_b, False)
    return (
        result,
        grad_features,
        sums_b[0],
        sums_b[1],
        sums_b[2].reshape(-1),
        sums_b[3].reshape(-1),
        grad_w_query,
        grad_w_key,
        grad_w_value,
        sums_b[4].reshape(-1),
        sums_b[5].reshape(-1),
        grad_w_out,
        sums_a[0].reshape(-1),
        sums_a[1].reshape(-1),
        sums_a[2].reshape(-1),
        grad_w_up,
        sums_a[4].reshape(-1),
        grad_w_down,
        sums_a[3].reshape(-1),
    )


def solution(mesh):
    token, split = P("dp", None), P(("dp", "mp"), None)
    columns, lines, cut, copy = P(None, "mp"), P("mp", None), P("mp"), P()
    return jax.shard_map(
        per_device,
        mesh=mesh,
        in_specs=(
            token, token, P("dp"), P("dp"), token, copy, copy, copy, copy, columns, columns,
            columns, cut, cut, lines, copy, copy, copy, columns, cut, lines, copy, token,
        ),
        out_specs=(
            split, split, copy, copy, copy, copy, columns, columns, columns, cut, cut, lines,
            copy, copy, copy, columns, cut, lines, copy,
        ),
        check_vma=False,
    )
```

```python
import math

import jax
import jax.numpy as jnp
from jax import lax
from jax.experimental import pallas as pl
from jax.experimental.pallas import tpu as pltpu
from jax.sharding import PartitionSpec as P

HDIM = 24
SEQ = 128
LANES = 128
INNER = 4
OUTER = 4
EPSILON = 1e-05
SCALE = 1.0 / math.sqrt(HDIM)
F32, BF16 = jnp.float32, jnp.bfloat16
MIB = 1024 * 1024


def dot(left, right):
    return jnp.dot(left, right, preferred_element_type=F32)


def dot_nt(left, right):
    return lax.dot_general(left, right, (((1,), (1,)), ((), ())), preferred_element_type=F32)


def dot_tn(left, right):
    return lax.dot_general(left, right, (((0,), (0,)), ((), ())), preferred_element_type=F32)


def norm_parts(hidden):
    average = jnp.mean(hidden, axis=-1, keepdims=True)
    centred = hidden - average
    inverse = lax.rsqrt(jnp.mean(centred * centred, axis=-1, keepdims=True) + EPSILON)
    return centred * inverse, inverse


def norm_back(unit, inverse, grad_hat):
    return inverse * (
        grad_hat
        - jnp.mean(grad_hat, axis=-1, keepdims=True)
        - unit * jnp.mean(grad_hat * unit, axis=-1, keepdims=True)
    )


def row_sum(block):
    return jnp.sum(block, axis=0, keepdims=True)


def positions(length):
    return lax.broadcasted_iota(jnp.int32, (length, 1), 0)


def whole():
    return pl.BlockSpec(memory_space=pltpu.VMEM)


def outside():
    return pl.BlockSpec(memory_space=pltpu.HBM)


def places():
    index = lax.axis_index("dp")
    return lax.axis_index("mp"), index % INNER, index // INNER % OUTER


def copy_in(sources, targets, sems):
    copies = [
        pltpu.make_async_copy(source, target, sems.at[place])
        for place, (source, target) in enumerate(zip(sources, targets))
    ]
    for copy in copies:
        copy.start()
    return copies


def row_of(ref):
    block = ref[...].astype(F32)
    return jnp.concatenate([block[r : r + 1, :] for r in range(block.shape[0])], axis=1)


def put_row(ref, row):
    for r in range(ref.shape[0]):
        ref[r : r + 1, :] = row[:, r * LANES : (r + 1) * LANES]


def call(kernel, args, specs, outs, scratch=(), micros=0, limit=24):
    return pl.pallas_call(
        kernel,
        out_shape=[jax.ShapeDtypeStruct(shape, kind) for shape, kind in outs],
        in_specs=specs,
        out_specs=[whole() for _ in outs],
        scratch_shapes=list(scratch),
        compiler_params=pltpu.CompilerParams(vmem_limit_bytes=limit * MIB),
        cost_estimate=pl.CostEstimate(
            flops=micros * 1_000_000_000, bytes_accessed=0, transcendentals=0
        ),
    )(*args)


def head_windows(width):
    windows = []
    for pair in range(width // (2 * HDIM)):
        low = pair * 2 * HDIM // LANES * LANES
        high = -(-(pair + 1) * 2 * HDIM // LANES) * LANES
        windows.append((low, high))
    return windows


def split_heads(block, pair, window):
    low, high = window
    part = block[:, low:high]
    column = low + lax.broadcasted_iota(jnp.int32, (16, high - low), 1)
    sides = []
    for head in (2 * pair, 2 * pair + 1):
        inside = (column >= head * HDIM) & (column < (head + 1) * HDIM)
        mask = jnp.where(inside, 1.0, 0.0).astype(BF16)
        sides.append(part * jnp.concatenate([mask] * (block.shape[0] // 16), axis=0))
    return jnp.concatenate(sides, axis=0)


def embed_rows(feats, lap, ends, w_ident, types, gain, shift, at, count):
    table = lap[:, at]
    slot = lax.broadcasted_iota(jnp.int32, (SEQ, SEQ), 0)
    picked = []
    for end in (0, 1):
        pick = jnp.where(ends[end : end + 1, at] == slot, 1.0, 0.0).astype(BF16)
        picked.append(dot(table, pick))
    ident = jnp.concatenate(picked, axis=0).astype(BF16)
    hidden = feats[at, :].astype(F32) + dot_tn(ident, w_ident[...])
    kinds = types[...].astype(F32)
    hidden = hidden + jnp.where(positions(SEQ) >= count, kinds[1:2, :], kinds[0:1, :])
    unit, _ = norm_parts(hidden)
    return hidden, ident, (unit * gain + shift).astype(BF16)


def embed_kernel(
    feats_in, lap_in, ends_in, nodes_in, w_ident_in, types_in, gain_in, shift_in,
    bias_q_in, bias_v_in, wq_in, wk_in, wv_in,
    hidden_out, ident_out, normed_out, normed_t_out, q_out, k_out, v_out,
    feats, lap, ends, nodes, w_ident, types, gain_rows, shift_rows, bias_q, bias_v,
    w_q, w_k, w_v, sems,
):
    rows, dim = feats.shape
    mols = rows // SEQ
    core = places()[0]
    own_rows = pl.ds(pl.multiple_of(core * rows, SEQ), rows)
    copies = copy_in(
        (
            feats_in.at[own_rows, :], lap_in.at[:, own_rows], ends_in.at[:, own_rows], nodes_in,
            w_ident_in, types_in, gain_in, shift_in, bias_q_in, bias_v_in, wq_in, wk_in, wv_in,
        ),
        (
            feats, lap, ends, nodes, w_ident, types, gain_rows, shift_rows, bias_q, bias_v,
            w_q, w_k, w_v,
        ),
        sems,
    )
    for copy in copies[:10]:
        copy.wait()
    gain, shift = row_of(gain_rows), row_of(shift_rows)

    def molecule(m, carry):
        at = pl.ds(pl.multiple_of(m * SEQ, SEQ), SEQ)
        count = nodes[core * mols + m]
        hidden, ident, normed = embed_rows(
            feats, lap, ends, w_ident, types, gain, shift, at, count
        )
        ident_out[:, at] = ident
        hidden_out[at, :] = hidden
        normed_out[at, :] = normed
        normed_t_out[:, at] = normed.T
        return carry

    lax.fori_loop(0, mols, molecule, 0)
    normed = normed_out[...]
    copies[10].wait()
    q_out[...] = (dot(normed, w_q[...]) + row_of(bias_q)).astype(BF16)
    copies[11].wait()
    k_out[...] = dot(normed, w_k[...]).astype(BF16)
    copies[12].wait()
    v_out[...] = (dot(normed, w_v[...]) + row_of(bias_v)).astype(BF16)


def forward_kernel(
    hidden, normed, q_own, k_own, v_own, w_q, w_k, w_v, wo_own, wo, wu_own, wu, wd_own, wd,
    bias_q, bias_v, bias_u,
    nodes_in, edges_in, cots_in, bias_u_own_in, bias_o_in, gain_in, shift_in,
    q_out, k_out, v_out, probs_out, keep_out, send_out, middle, active, gm_out, grad_branch,
    nodes, edges, cots, bias_u_own, bias_o, gain_rows, shift_rows, sems,
    mixed, attended, unit, normed_two, slope, grad_ffn,
):
    rows, dim = hidden.shape
    width = q_own.shape[1]
    mols = rows // SEQ
    pairs = width // (2 * HDIM)
    windows = head_windows(width)
    core = places()[0]
    copies = copy_in(
        (
            nodes_in, edges_in, cots_in.at[pl.ds(pl.multiple_of(core * rows, SEQ), rows), :],
            bias_u_own_in, bias_o_in, gain_in, shift_in,
        ),
        (nodes, edges, cots, bias_u_own, bias_o, gain_rows, shift_rows),
        sems,
    )

    q_out[...] = (dot(normed[...], w_q[...]) + row_of(bias_q)).astype(BF16)
    k_out[...] = dot(normed[...], w_k[...]).astype(BF16)
    v_out[...] = (dot(normed[...], w_v[...]) + row_of(bias_v)).astype(BF16)

    for copy in copies:
        copy.wait()
    gain, shift, bias_out = row_of(gain_rows), row_of(shift_rows), row_of(bias_o)

    def attend(m, carry):
        at = pl.ds(pl.multiple_of(m * SEQ, SEQ), SEQ)
        place = core * mols + m
        count = nodes[place] + edges[place]
        key_keep = positions(SEQ) < count
        query_keep = lax.broadcasted_iota(jnp.int32, (1, SEQ), 1) < count
        sides = ((q_own, k_own, v_own, keep_out), (q_out, k_out, v_out, send_out))
        for side, (q_ref, k_ref, v_ref, part_out) in enumerate(sides):
            queries, key_rows = q_ref[at, :], k_ref[at, :]
            values_t = v_ref[at, :].T
            for pair in range(pairs):
                low, high = windows[pair]
                both = split_heads(queries, pair, windows[pair])
                scores = dot_nt(key_rows[:, low:high], both) * SCALE
                scores = jnp.where(key_keep, scores, -1e30)
                top = jnp.max(scores, axis=0, keepdims=True)
                raised = jnp.exp(scores - top)
                total = row_sum(raised)
                probs = (raised * (1.0 / total)).astype(BF16)
                probs_out[m, side * pairs + pair] = probs
                first = pair * 2 * HDIM
                out = dot(values_t[first : first + 2 * HDIM], probs)
                mixed[first : first + HDIM, :] = out[:HDIM, :SEQ]
                mixed[first + HDIM : first + 2 * HDIM, :] = out[HDIM:, SEQ:]
            kept = jnp.where(query_keep, mixed[...], 0.0).astype(BF16)
            part_out[dim : dim + width, at] = kept
            attended[at, side * width : (side + 1) * width] = kept.T
        return carry

    lax.fori_loop(0, mols, attend, 0)
    middle[...] = (
        hidden[...] + dot(attended[:, :width], wo_own[...]) + dot(attended[:, width:], wo[...])
    )

    def second_norm(m, carry):
        at = pl.ds(pl.multiple_of(m * SEQ, SEQ), SEQ)
        place = core * mols + m
        keep = positions(SEQ) < nodes[place] + edges[place]
        total = middle[at, :] + bias_out
        middle[at, :] = total
        unit_rows, _ = norm_parts(total)
        unit[at, :] = unit_rows
        rows_two = (unit_rows * gain + shift).astype(BF16)
        normed_two[at, :] = rows_two
        turned = rows_two.T
        keep_out[:dim, at] = turned
        send_out[:dim, at] = turned
        grad_ffn[at, :] = jnp.where(keep, cots[at, :].astype(F32), 0.0).astype(BF16)
        return carry

    lax.fori_loop(0, mols, second_norm, 0)

    for side, (w_ref, b_ref, part_out) in enumerate(
        ((wu_own, bias_u_own, keep_out), (wu, bias_u, send_out))
    ):
        columns = slice(side * width, (side + 1) * width)
        slope[:, columns] = dot(normed_two[...], w_ref[...]) + row_of(b_ref)

        def activate(m, carry):
            at = pl.ds(pl.multiple_of(m * SEQ, SEQ), SEQ)
            before = slope[at, columns]
            phi = 0.5 * (1.0 + lax.erf(before * math.sqrt(0.5)))
            out = (before * phi).astype(BF16)
            slope[at, columns] = phi + before * jnp.exp(before * before * -0.5) * (
                1.0 / math.sqrt(2.0 * math.pi)
            )
            active[at, columns] = out
            part_out[dim + width : dim + 2 * width, at] = out.T
            return carry

        lax.fori_loop(0, mols, activate, 0)

    place_b = dim + 2 * width
    for side, (w_ref, part_out) in enumerate(((wd_own, keep_out), (wd, send_out))):
        columns = slice(side * width, (side + 1) * width)
        grad_before = slope[:, columns] * dot_nt(grad_ffn[...], w_ref[...])
        part_out[place_b : place_b + rows, :] = grad_before.astype(BF16)

    back = pl.ds(place_b, rows)
    gm_out[...] = dot_nt(keep_out[back, :], wu_own[...]) + dot_nt(send_out[back, :], wu[...])

    def second_back(m, sums):
        at = pl.ds(pl.multiple_of(m * SEQ, SEQ), SEQ)
        place = core * mols + m
        keep = positions(SEQ) < nodes[place] + edges[place]
        grad_normed = gm_out[at, :]
        unit_rows = unit[at, :]
        _, inverse = norm_parts(middle[at, :])
        grad_result = jnp.where(keep, cots[at, :].astype(F32), 0.0)
        grad = grad_result + norm_back(unit_rows, inverse, grad_normed * gain)
        gm_out[at, :] = grad
        grad_branch[at, :] = grad.astype(BF16)
        return (
            sums[0] + row_sum(grad),
            sums[1] + row_sum(grad_normed * unit_rows),
            sums[2] + row_sum(grad_normed),
            sums[3] + row_sum(grad_result),
        )

    nothing = jnp.zeros((1, dim), F32)
    sums = lax.fori_loop(0, mols, second_back, (nothing,) * 4)
    place_m = place_b + rows
    for part_out in (keep_out, send_out):
        part_out[place_m : place_m + rows, :] = grad_branch[:, :width]
        part_out[place_m + rows : place_m + 2 * rows, :] = grad_branch[:, width:]
    small = jnp.concatenate(list(sums) + [nothing] * 12, axis=0)
    left, right = small[:, :width], small[:, width:]
    place_s = place_m + 2 * rows
    keep_out[place_s:, :] = jnp.where(core == 0, left, right).astype(BF16)
    send_out[place_s:, :] = jnp.where(core == 0, right, left).astype(BF16)


def result_kernel(middle, active, wd_own, wd, bias, result_out):
    width = wd.shape[0]
    result_out[...] = (
        middle[...]
        + dot(active[:, :width], wd_own[...])
        + dot(active[:, width:], wd[...])
        + row_of(bias)
    ).astype(BF16)


def branch_kernel(
    grad_branch, wo_own, wo, nodes_in, edges_in, ga_own_out, ga_out, nodes, edges, sems
):
    mols = grad_branch.shape[0] // SEQ
    core = places()[0]
    copies = copy_in((nodes_in, edges_in), (nodes, edges), sems)
    products = [dot_nt(grad_branch[...], weight[...]) for weight in (wo_own, wo)]
    for copy in copies:
        copy.wait()
    for ref, product in zip((ga_own_out, ga_out), products):
        for m in range(mols):
            place = core * mols + m
            keep = positions(SEQ) < nodes[place] + edges[place]
            at = slice(m * SEQ, (m + 1) * SEQ)
            ref[at, :] = jnp.where(keep, product[at], 0.0).astype(BF16)


def attend_back_kernel(
    m, q_own, k_own, v_own, ga_own, q_got, k_got, v_got, ga_got, probs_all,
    keep_out, send_out, dq_t, dk, dv,
):
    width = q_own.shape[1]
    pairs = width // (2 * HDIM)
    windows = head_windows(width)
    at = slice(m * SEQ, (m + 1) * SEQ)
    sides = (
        (q_own, k_own, v_own, ga_own, keep_out),
        (q_got, k_got, v_got, ga_got, send_out),
    )
    for side, (q_ref, k_ref, v_ref, g_ref, part_out) in enumerate(sides):
        queries, key_rows, values, grads = q_ref[at, :], k_ref[at, :], v_ref[at, :], g_ref[at, :]
        keys_t = key_rows.T
        dk[side] = jnp.zeros_like(dk[side])
        dv[side] = jnp.zeros_like(dv[side])
        for pair in range(pairs):
            low, high = windows[pair]
            both_q = split_heads(queries, pair, windows[pair])
            both_g = split_heads(grads, pair, windows[pair])
            probs_low = probs_all[m, side * pairs + pair]
            probs = probs_low.astype(F32)
            grad_probs = dot_nt(values[:, low:high], both_g)
            inner = row_sum(probs * grad_probs)
            grad_scores = (probs * (grad_probs - inner)).astype(BF16)
            dv[side, :, low:high] += dot(probs_low, both_g)
            dk[side, :, low:high] += dot(grad_scores, both_q)
            first = pair * 2 * HDIM
            out = dot(keys_t[first : first + 2 * HDIM], grad_scores)
            dq_t[side, first : first + HDIM, :] = out[:HDIM, :SEQ]
            dq_t[side, first + HDIM : first + 2 * HDIM, :] = out[HDIM:, SEQ:]
        part_out[:SEQ, :] = (dq_t[side] * SCALE).astype(BF16).T
        part_out[SEQ : 2 * SEQ, :] = (dk[side] * SCALE).astype(BF16)
        part_out[2 * SEQ :, :] = dv[side].astype(BF16)


def embed_back_kernel(*refs):
    mols = (len(refs) - 25) // 2
    grads_own, grads = refs[:mols], refs[mols : 2 * mols]
    (
        wq_own, wk_own, wv_own, w_q, w_k, w_v, ident, grad_middle,
        feats_in, nodes_in, w_ident_in, types_in, gain_in,
        features_out, keep_out, send_out,
        feats, nodes, w_ident, types, gain_rows, sems, grad_normed, small, stacked,
    ) = refs[2 * mols :]
    core = places()[0]
    rows = feats.shape[0]
    copies = copy_in(
        (
            feats_in.at[pl.ds(pl.multiple_of(core * rows, SEQ), rows), :], nodes_in,
            w_ident_in, types_in, gain_in,
        ),
        (feats, nodes, w_ident, types, gain_rows),
        sems,
    )
    rows, dim = feats.shape
    width = wq_own.shape[1]
    idw = ident.shape[0]
    total = None
    for part, weights in ((grads_own, (wq_own, wk_own, wv_own)), (grads, (w_q, w_k, w_v))):
        for place, weight in enumerate(weights):
            for m in range(mols):
                stacked[m * SEQ : (m + 1) * SEQ, :] = part[m][place * SEQ : (place + 1) * SEQ, :]
            term = dot_nt(stacked[...], weight[...])
            total = term if total is None else total + term
    grad_normed[...] = total
    small[...] = jnp.zeros_like(small)
    for copy in copies:
        copy.wait()
    gain = row_of(gain_rows)
    kinds = types[...].astype(F32)

    def molecule(m, carry):
        at = pl.ds(pl.multiple_of(m * SEQ, SEQ), SEQ)
        is_edge = positions(SEQ) >= nodes[core * mols + m]
        hidden = feats[at, :].astype(F32) + dot_tn(ident[:, at], w_ident[...])
        hidden = hidden + jnp.where(is_edge, kinds[1:2, :], kinds[0:1, :])
        unit, inverse = norm_parts(hidden)
        grad_rows = grad_normed[at, :]
        grad = grad_middle[at, :] + norm_back(unit, inverse, grad_rows * gain)
        features_out[at, :] = grad
        high = grad.astype(BF16)
        rest = (grad - high.astype(F32)).astype(BF16)
        picked = ident[:, at]
        small[:idw, :] += dot(picked, high) + dot(picked, rest)
        edge_rows = jnp.where(is_edge, grad, 0.0)
        small[idw : idw + 1, :] += row_sum(grad - edge_rows)
        small[idw + 1 : idw + 2, :] += row_sum(edge_rows)
        small[idw + 2 : idw + 3, :] += row_sum(grad_rows * unit)
        small[idw + 3 : idw + 4, :] += row_sum(grad_rows)
        return carry

    lax.fori_loop(0, mols, molecule, 0)
    left, right = small[:, :width], small[:, width:]
    keep_out[...] = jnp.where(core == 0, left, right)
    send_out[...] = jnp.where(core == 0, right, left).astype(BF16)


def deal(unit, outs, block_at, small=None):
    _, inner, outer = places()
    first_kept, first_sent, second_kept, second_sent = outs
    for step in range(INNER):
        for turn in range(OUTER):
            if turn < 2:
                out, slot = (first_sent if step % 2 else first_kept), step // 2
            else:
                out, slot = (second_sent if step // 2 else second_kept), step % 2
            start = (slot * 2 + turn % 2) * 3 * unit
            for place in range(3):
                out[start + place * unit : start + (place + 1) * unit, :] = block_at(
                    inner ^ step, outer ^ turn, place
                )
    if small is not None:
        for out in (first_kept, first_sent):
            out[INNER * 3 * unit :, :] = small


def ffn_grads_kernel(kept, got, cots_in, nodes_in, edges_in, *rest):
    outs, (cots, nodes, edges, sems, tall, flat, grad_ffn) = rest[:4], rest[4:]
    copies = copy_in((nodes_in, edges_in, cots_in), (nodes, edges, cots), sems)
    rows_all, dim = cots.shape
    rows, width = rows_all // 2, kept.shape[1]
    mols = rows // SEQ
    core = places()[0]
    own_rows = pl.ds(pl.multiple_of(core * rows, SEQ), rows)
    other_rows = pl.ds(pl.multiple_of((1 - core) * rows, SEQ), rows)
    place_b = dim + 2 * width
    place_m = place_b + rows
    place_s = place_m + 2 * rows
    back = slice(place_b, place_m)
    tall[...] = (dot(kept[:dim, :], kept[back, :]) + dot(got[:dim, :], got[back, :])).astype(BF16)
    turned = slice(dim, dim + width)
    for half in (0, 1):
        mid = slice(place_m + half * rows, place_m + (half + 1) * rows)
        flat[half] = (
            dot(kept[turned, :], kept[mid, :]) + dot(got[turned, :], got[mid, :])
        ).astype(BF16)
    for copy in copies:
        copy.wait()
    for m in range(2 * mols):
        keep = positions(SEQ) < nodes[m] + edges[m]
        at = slice(m * SEQ, (m + 1) * SEQ)
        grad_ffn[at, :] = jnp.where(keep, cots[at, :].astype(F32), 0.0).astype(BF16)
    turned = slice(dim + width, dim + 2 * width)
    for half in (0, 1):
        columns = slice(half * width, (half + 1) * width)
        product = dot(kept[turned, :], grad_ffn[own_rows, columns])
        product = product + dot(got[turned, :], grad_ffn[other_rows, columns])
        flat[2 + half] = product.astype(BF16)
    bias = row_sum(kept[back, :].astype(F32)) + row_sum(got[back, :].astype(F32))
    small = kept[place_s:, :].astype(F32) + got[place_s:, :].astype(F32)
    spot = lax.broadcasted_iota(jnp.int32, small.shape, 0)
    small = jnp.where(spot == 4, bias, small).astype(BF16)
    unit = dim // (INNER * OUTER)

    def block_at(dest, z, place):
        if place == 0:
            return tall[pl.ds(pl.multiple_of((dest * OUTER + z) * unit, 16), unit), :]
        row = pl.multiple_of((dest * (OUTER // 2) + z // 2) * unit, 16)
        return flat[2 * (place - 1) + z % 2, pl.ds(row, unit), :]

    deal(unit, outs, block_at, small)


def qkv_grads_kernel(normed_t, normed_t_got, *refs):
    mols = normed_t.shape[1] // SEQ
    kept, got = refs[:mols], refs[mols : 2 * mols]
    outs, small_out = refs[2 * mols : 2 * mols + 4], refs[2 * mols + 4]
    tall, normed, stacked = refs[2 * mols + 5 :]
    dim, rows = normed_t.shape
    unit = dim // (INNER * OUTER)
    normed[:, :rows] = normed_t[...]
    normed[:, rows:] = normed_t_got[...]
    spot = lax.broadcasted_iota(jnp.int32, small_out.shape, 0)
    small = jnp.zeros(small_out.shape, F32)
    for place in range(3):
        for m, part in enumerate(kept + got):
            stacked[m * SEQ : (m + 1) * SEQ, :] = part[place * SEQ : (place + 1) * SEQ, :]
        tall[place] = dot(normed[...], stacked[...]).astype(BF16)
        if place != 1:
            small = jnp.where(spot == 36 + place // 2, row_sum(stacked[...].astype(F32)), small)
    small_out[...] = small

    def block_at(dest, z, place):
        return tall[place, pl.ds(pl.multiple_of((dest * OUTER + z) * unit, 16), unit), :]

    deal(unit, outs, block_at)


def add(first, second):
    return (first.astype(F32) + second.astype(F32)).astype(BF16)


def plane_sum_kernel(first, first_got, second, second_got, *refs):
    late, (first_kept, first_sent, second_kept, second_sent) = refs[:-4], refs[-4:]
    pair = second_kept.shape[0]
    total = add(first[...], first_got[...])
    first_kept[:pair, :] = total[:pair]
    first_sent[:pair, :] = total[pair : 2 * pair]
    if late:
        small = (late[0][...] + late[1][...].astype(F32) + late[2][...]).astype(BF16)
    else:
        small = total[2 * pair :]
    first_kept[pair:, :] = small
    first_sent[pair:, :] = small
    total = add(second[...], second_got[...])
    second_kept[...] = total[:pair]
    second_sent[...] = total[pair:]


def line_cut_kernel(first, first_got, second, second_got, own, near, middle, far):
    chunk = own.shape[0]
    total = add(first[...], first_got[...])
    own[...] = total[:chunk]
    near[...] = total[chunk:]
    total = add(second[...], second_got[...])
    middle[...] = total[:chunk]
    far[...] = total[chunk:]


def line_sum_kernel(own, near, near_got, middle_got, far_got, out, out_small):
    chunk = own.shape[0]
    total = own[...].astype(F32) + near_got[:chunk, :].astype(F32)
    total = total + middle_got[...].astype(F32) + far_got[...].astype(F32)
    out[...] = total.astype(BF16)
    out_small[:chunk, :] = total.astype(BF16)
    out_small[chunk:, :] = add(near[chunk:, :], near_got[chunk:, :])


def line_join_kernel(own, near, middle, far, line_x, line_y, small_out):
    chunk = near.shape[0]
    small = own[chunk:, :].astype(F32) + middle[chunk:, :].astype(F32)
    small_out[...] = small
    for out in (line_x, line_y):
        for turn, part in enumerate((own, near, middle, far)):
            out[turn * chunk : (turn + 1) * chunk, :] = part[:chunk, :]
    line_x[OUTER * chunk :, :] = small.astype(BF16)


def place_kernel(split_second, *refs):
    outs, parts = refs[-3:], refs[:-3]
    own = parts[0]
    _, inner, outer = places()
    unit = own.shape[0] // (3 * OUTER)
    width = own.shape[1]
    for step in range(INNER):
        for turn in range(OUTER):
            ref, start = parts[step], turn * 3 * unit
            if step == 3 and turn >= 2:
                ref, start = parts[4], (turn - 2) * 3 * unit
            dest, z = inner ^ step, outer ^ turn
            tall = pl.ds(pl.multiple_of((dest * OUTER + z) * unit, 16), unit)
            flat = pl.ds(pl.multiple_of((dest * (OUTER // 2) + z // 2) * unit, 16), unit)
            columns = pl.ds(pl.multiple_of(z % 2 * width, LANES), width)
            for place in range(3):
                part = ref[start + place * unit : start + (place + 1) * unit, :].astype(F32)
                if split_second and place > 0:
                    outs[place][flat, columns] = part
                else:
                    outs[place][tall, :] = part


def finish_first_kernel(small, got, bias_out, gain, shift, bias_down, bias_up):
    core = places()[0]
    for place, ref in enumerate((bias_out, gain, shift, bias_down)):
        mine, other = small[place : place + 1, :], got[place : place + 1, :]
        left = jnp.where(core == 0, mine, other)
        put_row(ref, jnp.concatenate([left, jnp.where(core == 0, other, mine)], axis=1))
    put_row(bias_up, small[4:5, :])


def finish_second_kernel(small, extra, got, w_ident, types, gain, shift, bias_q, bias_v):
    idw = w_ident.shape[0]
    core = places()[0]
    mine, other = small[...] + extra[...].astype(F32), got[...]
    left = jnp.where(core == 0, mine, other)
    total = jnp.concatenate([left, jnp.where(core == 0, other, mine)], axis=1)
    w_ident[...] = total[:idw]
    types[...] = total[idw : idw + 2]
    put_row(gain, total[idw + 2 : idw + 3])
    put_row(shift, total[idw + 3 : idw + 4])
    put_row(bias_q, mine[idw + 4 : idw + 5])
    put_row(bias_v, mine[idw + 5 : idw + 6])


def per_device(
    features, lap_vectors, node_counts, edge_counts, endpoints, w_ident, type_table,
    gain_one, shift_one, w_query, w_key, w_value, bias_query, bias_value, w_out, bias_out,
    gain_two, shift_two, w_up, bias_up, w_down, bias_down, cotangent,
):
    dp_count = lax.axis_size("dp")
    dp_index = lax.axis_index("dp")
    mp_index = lax.axis_index("mp")
    block = INNER * OUTER
    rest_count = dp_count // block
    def swap(part):
        return lax.ppermute(part, "mp", [(0, 1), (1, 0)])

    def inner_move(part, step):
        return lax.ppermute(part, "dp", [(s, s ^ step) for s in range(dp_count)])

    def outer_move(part, step):
        return lax.ppermute(part, "dp", [(s, s ^ (step * INNER)) for s in range(dp_count)])

    rows_all, dim = features.shape
    rows = rows_all // 2
    mols = rows // SEQ
    width = w_query.shape[1]
    heads = width // HDIM
    lapk = lap_vectors.shape[1]
    idw = w_ident.shape[0]

    def pinned(part):
        return pltpu.with_memory_space_constraint(part, pltpu.HBM)

    def lanes(part):
        return pinned(part.reshape(-1, LANES))

    nodes, edges = pinned(node_counts), pinned(edge_counts)
    count_scratch = pltpu.SMEM(node_counts.shape, jnp.int32)
    wide_scratch = pltpu.VMEM((dim // LANES, LANES), BF16)
    half_scratch = pltpu.VMEM((width // LANES, LANES), BF16)
    embed_args = (
        pinned(features), pinned(lap_vectors.T), pinned(endpoints.T), nodes,
        pinned(w_ident), pinned(type_table), lanes(gain_one), lanes(shift_one),
    )
    embed_scratch = [
        pltpu.VMEM((rows, dim), BF16),
        pltpu.VMEM((lapk, rows), BF16),
        pltpu.VMEM((2, rows), jnp.int32),
        count_scratch,
        pltpu.VMEM((idw, dim), BF16),
        pltpu.VMEM((2, dim), BF16),
        wide_scratch,
        wide_scratch,
    ]

    wq_got, wk_got, wv_got = swap(w_query), swap(w_key), swap(w_value)
    bq_got, bv_got, bu_got = swap(bias_query), swap(bias_value), swap(bias_up)
    wo_got, wu_got, wd_got = swap(w_out), swap(w_up), swap(w_down)

    hidden, ident, normed, normed_t, q_own, k_own, v_own = call(
        embed_kernel,
        (
            *embed_args, lanes(bias_query), lanes(bias_value),
            pinned(w_query), pinned(w_key), pinned(w_value),
        ),
        [outside()] * 13,
        [
            ((rows, dim), F32),
            ((idw, rows), BF16),
            ((rows, dim), BF16),
            ((dim, rows), BF16),
            ((rows, width), BF16),
            ((rows, width), BF16),
            ((rows, width), BF16),
        ],
        scratch=embed_scratch
        + [half_scratch] * 2
        + [pltpu.VMEM((dim, width), BF16)] * 3
        + [pltpu.SemaphoreType.DMA((13,))],
    )
    sent_rows = dim + 2 * width + 3 * rows + 16
    (
        q_got, k_got, v_got, probs, kept_a, sent_a, middle, active, grad_middle, grad_branch,
    ) = call(
        forward_kernel,
        (
            hidden, normed, q_own, k_own, v_own, wq_got, wk_got, wv_got,
            w_out, wo_got, w_up, wu_got, w_down, wd_got,
            *(part.reshape(-1, LANES) for part in (bq_got, bv_got, bu_got)),
            nodes, edges, pinned(cotangent),
            lanes(bias_up), lanes(bias_out), lanes(gain_two), lanes(shift_two),
        ),
        [whole()] * 17 + [outside()] * 7,
        [
            ((rows, width), BF16),
            ((rows, width), BF16),
            ((rows, width), BF16),
            ((mols, heads, SEQ, 2 * SEQ), BF16),
            ((sent_rows, width), BF16),
            ((sent_rows, width), BF16),
            ((rows, dim), F32),
            ((rows, dim), BF16),
            ((rows, dim), F32),
            ((rows, dim), BF16),
        ],
        scratch=[
            count_scratch,
            count_scratch,
            pltpu.VMEM((rows, dim), BF16),
            half_scratch,
            wide_scratch,
            wide_scratch,
            wide_scratch,
            pltpu.SemaphoreType.DMA((7,)),
            pltpu.VMEM((width, SEQ), F32),
            pltpu.VMEM((rows, dim), BF16),
            pltpu.VMEM((rows, dim), F32),
            pltpu.VMEM((rows, dim), BF16),
            pltpu.VMEM((rows, dim), F32),
            pltpu.VMEM((rows, dim), BF16),
        ],
        limit=30,
    )
    got_a = swap(sent_a)
    ga_own, ga_got = call(
        branch_kernel,
        (grad_branch, w_out, wo_got, nodes, edges),
        [whole()] * 3 + [outside()] * 2,
        [((rows, width), BF16), ((rows, width), BF16)],
        scratch=[count_scratch, count_scratch, pltpu.SemaphoreType.DMA((2,))],
    )

    unit = dim // block
    chunk = 3 * unit
    small_a, small_b = 16, 48

    def rest_sum(part):
        if rest_count == 1:
            return part
        groups = [[r * block + s for r in range(rest_count)] for s in range(block)]
        return lax.psum(part.astype(F32), "dp", axis_index_groups=groups).astype(part.dtype)

    pair = 2 * chunk

    def after(part, *others):
        return lax.optimization_barrier((part, *others))[0]

    def plane_step(parts, small_rows, late=(), others=(), micros=0):
        first, first_sent, second, second_sent = parts
        first_got = after(inner_move(first_sent, 1), *others)
        second_got = after(inner_move(second_sent, 2), *others)
        return call(
            plane_sum_kernel,
            (first, first_got, second, second_got, *late),
            [whole()] * (4 + len(late)),
            [((pair + small_rows, width), BF16)] * 2 + [((pair, width), BF16)] * 2,
            micros=micros,
        )

    def plane_turn(parts, others=(), micros=0):
        first, first_sent, second, second_sent = parts
        first_got = after(inner_move(first_sent, 2), *others)
        second_got = after(inner_move(second_sent, 1), *others)
        return call(
            line_cut_kernel,
            (first, first_got, second, second_got),
            [whole()] * 4,
            [
                ((chunk, width), BF16),
                ((first.shape[0] - chunk, width), BF16),
                ((chunk, width), BF16),
                ((chunk, width), BF16),
            ],
            micros=micros,
        )

    def line_step(parts, others=(), micros=0):
        got = [after(outer_move(parts[turn], turn), *others) for turn in range(1, OUTER)]
        mine, both = call(
            line_sum_kernel,
            (parts[0], parts[1], *got),
            [whole()] * 5,
            [((chunk, width), BF16), (parts[1].shape, BF16)],
            micros=micros,
        )
        if rest_count > 1:
            both = rest_sum(both)
            mine = both[:chunk]
        return mine, both

    def line_back(mine, both, others=(), micros=0):
        sent = (mine, both, mine)
        got = [after(outer_move(sent[turn - 1], turn), *others) for turn in range(1, OUTER)]
        small_rows = both.shape[0] - chunk
        return call(
            line_join_kernel,
            (both, *got),
            [whole()] * OUTER,
            [
                ((OUTER * chunk + small_rows, width), BF16),
                ((OUTER * chunk, width), BF16),
                ((small_rows, width), F32),
            ],
            micros=micros,
        )

    def plane_back(lines):
        return inner_move(lines[0], 1), inner_move(lines[1], 2)

    def plane_back_turn(side_x, side_y):
        return inner_move(side_y[:pair], 1), inner_move(side_x[pair : 2 * pair], 2)

    def placed(planes, split_second, micros=0):
        tall, flat = ((dim, width), F32), ((width, dim), F32)
        return call(
            lambda *refs: place_kernel(split_second, *refs),
            planes,
            [whole()] * len(planes),
            [tall, flat, flat] if split_second else [tall] * 3,
            micros=micros,
        )

    def attend_back(m, query_rows):
        return call(
            lambda *refs: attend_back_kernel(m, *refs),
            (query_rows, k_own, v_own, ga_own, q_got, k_got, v_got, ga_got, probs),
            [whole()] * 9,
            [((3 * SEQ, width), BF16)] * 2,
            scratch=[
                pltpu.VMEM((2, width, SEQ), F32),
                pltpu.VMEM((2, SEQ, width), F32),
                pltpu.VMEM((2, SEQ, width), F32),
            ],
        )

    backs = [attend_back(0, q_own)]
    kept_a = after(kept_a, backs[0][0])
    parts_a = call(
        ffn_grads_kernel,
        (kept_a, got_a, pinned(cotangent), nodes, edges),
        [whole()] * 2 + [outside()] * 3,
        [((INNER * chunk + small_a, width), BF16)] * 2 + [((INNER * chunk, width), BF16)] * 2,
        scratch=[
            pltpu.VMEM((rows_all, dim), BF16),
            count_scratch,
            count_scratch,
            pltpu.SemaphoreType.DMA((3,)),
            pltpu.VMEM((dim, width), BF16),
            pltpu.VMEM((4, width, width), BF16),
            pltpu.VMEM((rows_all, dim), BF16),
        ],
    )
    normed_t_got = swap(after(normed_t, parts_a[0]))
    for m in range(1, mols):
        gates = (parts_a[0], backs[-1][0]) + ((normed_t_got,) if m == mols - 1 else ())
        backs.append(attend_back(m, after(q_own, *gates)))
    kept_b = [back[0] for back in backs]
    sent_b = [back[1] for back in backs]
    got_b = [swap(sent) for sent in sent_b]
    steps_a = plane_step(parts_a, small_a, others=(kept_b[-1],))
    normed_t = after(normed_t, *steps_a)
    parts_b = call(
        qkv_grads_kernel,
        (normed_t, normed_t_got, *kept_b, *got_b),
        [whole()] * (2 + 2 * mols),
        [((INNER * chunk, width), BF16)] * 4 + [((small_b, width), F32)],
        scratch=[
            pltpu.VMEM((3, dim, width), BF16),
            pltpu.VMEM((dim, 2 * rows), BF16),
            pltpu.VMEM((2 * rows, width), BF16),
        ],
    )
    turned_a = plane_turn(steps_a, others=(parts_b[0],), micros=3)
    grad_middle = after(grad_middle, parts_b[0], *turned_a)
    grad_features, small_kept, small_sent = call(
        embed_back_kernel,
        (
            *kept_b, *sent_b, w_query, w_key, w_value, wq_got, wk_got, wv_got, ident,
            grad_middle, embed_args[0], nodes, *embed_args[4:7],
        ),
        [whole()] * (8 + 2 * mols) + [outside()] * 5,
        [((rows, dim), F32), ((small_b, width), F32), ((small_b, width), BF16)],
        scratch=[
            pltpu.VMEM((rows, dim), BF16),
            count_scratch,
            pltpu.VMEM((idw, dim), BF16),
            pltpu.VMEM((2, dim), BF16),
            wide_scratch,
            pltpu.SemaphoreType.DMA((5,)),
            pltpu.VMEM((rows, dim), F32),
            pltpu.VMEM((small_b, dim), F32),
            pltpu.VMEM((rows, width), BF16),
        ],
        micros=0,
    )
    small_got = swap(small_sent)
    steps_b = plane_step(parts_b[:4], small_b, late=(small_kept, small_got, parts_b[4]))
    line_a = line_step(turned_a, others=steps_b, micros=3)
    turned_b = plane_turn(steps_b, others=line_a[:1])
    lines_a = line_back(*line_a, others=turned_b, micros=3)
    line_b = line_step(turned_b, micros=12)
    sides_a = plane_back((lines_a[1], lines_a[1]))
    far_a = plane_back_turn(*sides_a)
    planes_a = (lines_a[1], *sides_a, *far_a)
    lines_b = line_back(*line_b, micros=2)
    result = call(
        result_kernel,
        (middle, active, w_down, wd_got, lanes(after(bias_down, lines_b[1]))),
        [whole()] * 5,
        [((rows, dim), BF16)],
    )[0]
    wide, half = ((dim // LANES, LANES), F32), ((width // LANES, LANES), F32)
    sums_a = call(
        finish_first_kernel,
        (lines_a[2], swap(after(lines_a[2], lines_b[1]))),
        [whole()] * 2,
        [wide] * 4 + [half],
    )
    grad_w_up, grad_w_out, grad_w_down = placed(planes_a, True, micros=10)
    sides_b = plane_back(lines_b)
    sides_b, _ = lax.optimization_barrier((sides_b, (result, sums_a, grad_w_up)))
    far_b = plane_back_turn(*sides_b)
    planes_b = (lines_b[1], sides_b[0], sides_b[1], *far_b)
    extra = sides_b[0][OUTER * chunk :]
    own_b = lines_b[2] + extra.astype(F32)
    sums_b = call(
        finish_second_kernel,
        (lines_b[2], extra, swap(own_b)),
        [whole()] * 3,
        [((idw, dim), F32), ((2, dim), F32), wide, wide, half, half],
    )
    grad_w_query, grad_w_key, grad_w_value = placed(planes_b, False)
    return (
        result,
        grad_features,
        sums_b[0],
        sums_b[1],
        sums_b[2].reshape(-1),
        sums_b[3].reshape(-1),
        grad_w_query,
        grad_w_key,
        grad_w_value,
        sums_b[4].reshape(-1),
        sums_b[5].reshape(-1),
        grad_w_out,
        sums_a[0].reshape(-1),
        sums_a[1].reshape(-1),
        sums_a[2].reshape(-1),
        grad_w_up,
        sums_a[4].reshape(-1),
        grad_w_down,
        sums_a[3].reshape(-1),
    )


def solution(mesh):
    token, split = P("dp", None), P(("dp", "mp"), None)
    columns, lines, cut, copy = P(None, "mp"), P("mp", None), P("mp"), P()
    return jax.shard_map(
        per_device,
        mesh=mesh,
        in_specs=(
            token, token, P("dp"), P("dp"), token, copy, copy, copy, copy, columns, columns,
            columns, cut, cut, lines, copy, copy, copy, columns, cut, lines, copy, token,
        ),
        out_specs=(
            split, split, copy, copy, copy, copy, columns, columns, columns, cut, cut, lines,
            copy, copy, copy, columns, cut, lines, copy,
        ),
        check_vma=False,
    )
```

```python
import math

import jax
import jax.numpy as jnp
from jax import lax
from jax.experimental import pallas as pl
from jax.experimental.pallas import tpu as pltpu
from jax.sharding import PartitionSpec as P

HDIM = 24
SEQ = 128
LANES = 128
INNER = 4
OUTER = 4
EPSILON = 1e-05
SCALE = 1.0 / math.sqrt(HDIM)
LOG2_SCALE = SCALE * math.log2(math.e)
F32, BF16 = jnp.float32, jnp.bfloat16
MIB = 1024 * 1024


def dot(left, right):
    return jnp.dot(left, right, preferred_element_type=F32)


def dot_nt(left, right):
    return lax.dot_general(left, right, (((1,), (1,)), ((), ())), preferred_element_type=F32)


def dot_tn(left, right):
    return lax.dot_general(left, right, (((0,), (0,)), ((), ())), preferred_element_type=F32)


def norm_parts(hidden):
    average = jnp.mean(hidden, axis=-1, keepdims=True)
    centred = hidden - average
    inverse = lax.rsqrt(jnp.mean(centred * centred, axis=-1, keepdims=True) + EPSILON)
    return centred * inverse, inverse


def norm_back(unit, inverse, grad_hat):
    return inverse * (
        grad_hat
        - jnp.mean(grad_hat, axis=-1, keepdims=True)
        - unit * jnp.mean(grad_hat * unit, axis=-1, keepdims=True)
    )


def row_sum(block):
    return jnp.sum(block, axis=0, keepdims=True)


def positions(length):
    return lax.broadcasted_iota(jnp.int32, (length, 1), 0)


def whole():
    return pl.BlockSpec(memory_space=pltpu.VMEM)


def outside():
    return pl.BlockSpec(memory_space=pltpu.HBM)


def places():
    index = lax.axis_index("dp")
    return lax.axis_index("mp"), index % INNER, index // INNER % OUTER


def copy_in(sources, targets, sems):
    copies = [
        pltpu.make_async_copy(source, target, sems.at[place])
        for place, (source, target) in enumerate(zip(sources, targets))
    ]
    for copy in copies:
        copy.start()
    return copies


def row_of(ref):
    block = ref[...].astype(F32)
    return jnp.concatenate([block[r : r + 1, :] for r in range(block.shape[0])], axis=1)


def put_row(ref, row):
    for r in range(ref.shape[0]):
        ref[r : r + 1, :] = row[:, r * LANES : (r + 1) * LANES]


def call(kernel, args, specs, outs, scratch=(), micros=0, limit=24):
    return pl.pallas_call(
        kernel,
        out_shape=[jax.ShapeDtypeStruct(shape, kind) for shape, kind in outs],
        in_specs=specs,
        out_specs=[whole() for _ in outs],
        scratch_shapes=list(scratch),
        compiler_params=pltpu.CompilerParams(vmem_limit_bytes=limit * MIB),
        cost_estimate=pl.CostEstimate(
            flops=micros * 1_000_000_000, bytes_accessed=0, transcendentals=0
        ),
    )(*args)


def head_windows(width):
    windows = []
    for pair in range(width // (2 * HDIM)):
        low = pair * 2 * HDIM // LANES * LANES
        high = -(-(pair + 1) * 2 * HDIM // LANES) * LANES
        windows.append((low, high))
    return windows


def split_heads(block, pair, window):
    low, high = window
    part = block[:, low:high]
    column = low + lax.broadcasted_iota(jnp.int32, (16, high - low), 1)
    sides = []
    for head in (2 * pair, 2 * pair + 1):
        inside = (column >= head * HDIM) & (column < (head + 1) * HDIM)
        mask = jnp.where(inside, 1.0, 0.0).astype(BF16)
        sides.append(part * jnp.concatenate([mask] * (block.shape[0] // 16), axis=0))
    return jnp.concatenate(sides, axis=0)


def embed_rows(feats, lap, ends, w_ident, types, gain, shift, at, count):
    table = lap[:, at]
    slot = lax.broadcasted_iota(jnp.int32, (SEQ, SEQ), 0)
    picked = []
    for end in (0, 1):
        pick = jnp.where(ends[end : end + 1, at] == slot, 1.0, 0.0).astype(BF16)
        picked.append(dot(table, pick))
    ident = jnp.concatenate(picked, axis=0).astype(BF16)
    hidden = feats[at, :].astype(F32) + dot_tn(ident, w_ident[...])
    kinds = types[...].astype(F32)
    hidden = hidden + jnp.where(positions(SEQ) >= count, kinds[1:2, :], kinds[0:1, :])
    unit, _ = norm_parts(hidden)
    return hidden, ident, (unit * gain + shift).astype(BF16)


def embed_kernel(
    feats_in, lap_in, ends_in, nodes_in, w_ident_in, types_in, gain_in, shift_in,
    bias_q_in, bias_v_in, wq_in, wk_in, wv_in,
    hidden_out, ident_out, normed_out, normed_t_out, q_out, k_out, v_out,
    feats, lap, ends, nodes, w_ident, types, gain_rows, shift_rows, bias_q, bias_v,
    w_q, w_k, w_v, sems,
):
    rows, dim = feats.shape
    mols = rows // SEQ
    core = places()[0]
    own_rows = pl.ds(pl.multiple_of(core * rows, SEQ), rows)
    copies = copy_in(
        (
            feats_in.at[own_rows, :], lap_in.at[:, own_rows], ends_in.at[:, own_rows], nodes_in,
            w_ident_in, types_in, gain_in, shift_in, bias_q_in, bias_v_in, wq_in, wk_in, wv_in,
        ),
        (
            feats, lap, ends, nodes, w_ident, types, gain_rows, shift_rows, bias_q, bias_v,
            w_q, w_k, w_v,
        ),
        sems,
    )
    for copy in copies[:10]:
        copy.wait()
    gain, shift = row_of(gain_rows), row_of(shift_rows)

    def molecule(m):
        at = slice(m * SEQ, (m + 1) * SEQ)
        count = nodes[core * mols + m]
        hidden, ident, normed = embed_rows(
            feats, lap, ends, w_ident, types, gain, shift, at, count
        )
        ident_out[:, at] = ident
        hidden_out[at, :] = hidden
        normed_out[at, :] = normed
        normed_t_out[:, at] = normed.T

    for m in range(mols):
        molecule(m)
    normed = normed_out[...]
    copies[10].wait()
    q_out[...] = (dot(normed, w_q[...]) + row_of(bias_q)).astype(BF16)
    copies[11].wait()
    k_out[...] = dot(normed, w_k[...]).astype(BF16)
    copies[12].wait()
    v_out[...] = (dot(normed, w_v[...]) + row_of(bias_v)).astype(BF16)


def forward_kernel(
    hidden, normed, q_own, k_own, v_own, w_q, w_k, w_v, wo_own, wo, wu_own, wu, wd_own, wd,
    bias_q, bias_v, bias_u,
    nodes_in, edges_in, cots_in, bias_u_own_in, bias_o_in, gain_in, shift_in,
    q_out, k_out, v_out, probs_out, keep_out, send_out, middle, active, gm_out, grad_branch,
    nodes, edges, cots, bias_u_own, bias_o, gain_rows, shift_rows, sems,
    mixed, attended, unit, normed_two, slope, grad_ffn,
):
    rows, dim = hidden.shape
    width = q_own.shape[1]
    mols = rows // SEQ
    pairs = width // (2 * HDIM)
    windows = head_windows(width)
    core = places()[0]
    copies = copy_in(
        (
            nodes_in, edges_in, cots_in.at[pl.ds(pl.multiple_of(core * rows, SEQ), rows), :],
            bias_u_own_in, bias_o_in, gain_in, shift_in,
        ),
        (nodes, edges, cots, bias_u_own, bias_o, gain_rows, shift_rows),
        sems,
    )

    q_out[...] = (dot(normed[...], w_q[...]) + row_of(bias_q)).astype(BF16)
    k_out[...] = dot(normed[...], w_k[...]).astype(BF16)
    v_out[...] = (dot(normed[...], w_v[...]) + row_of(bias_v)).astype(BF16)

    for copy in copies:
        copy.wait()
    gain, shift, bias_out = row_of(gain_rows), row_of(shift_rows), row_of(bias_o)

    def attend(m, carry):
        at = pl.ds(pl.multiple_of(m * SEQ, SEQ), SEQ)
        place = core * mols + m
        count = nodes[place] + edges[place]
        key_keep = positions(SEQ) < count
        query_keep = lax.broadcasted_iota(jnp.int32, (1, SEQ), 1) < count
        sides = ((q_own, k_own, v_own, keep_out), (q_out, k_out, v_out, send_out))
        for side, (q_ref, k_ref, v_ref, part_out) in enumerate(sides):
            queries, key_rows = q_ref[at, :], k_ref[at, :]
            values_t = v_ref[at, :].T
            for pair in range(pairs):
                low, high = windows[pair]
                both = split_heads(queries, pair, windows[pair])
                scores = dot_nt(key_rows[:, low:high], both)
                scores = jnp.where(key_keep, scores, -1e30)
                top = jnp.max(scores, axis=0, keepdims=True)
                raised = jnp.exp2((scores - top) * LOG2_SCALE)
                total = row_sum(raised)
                probs = (raised * (1.0 / total)).astype(BF16)
                probs_out[m, side * pairs + pair] = probs
                first = pair * 2 * HDIM
                out = dot(values_t[first : first + 2 * HDIM], probs)
                mixed[side, first : first + HDIM, :] = out[:HDIM, :SEQ]
                mixed[side, first + HDIM : first + 2 * HDIM, :] = out[HDIM:, SEQ:]
            kept = jnp.where(query_keep, mixed[side], 0.0).astype(BF16)
            part_out[dim : dim + width, at] = kept
            attended[at, side * width : (side + 1) * width] = kept.T
        return carry

    lax.fori_loop(0, mols, attend, 0)
    middle[...] = (
        hidden[...] + dot(attended[:, :width], wo_own[...]) + dot(attended[:, width:], wo[...])
    )

    for m in range(mols):
        at = slice(m * SEQ, (m + 1) * SEQ)
        place = core * mols + m
        keep = positions(SEQ) < nodes[place] + edges[place]
        total = middle[at, :] + bias_out
        middle[at, :] = total
        unit_rows, _ = norm_parts(total)
        unit[at, :] = unit_rows
        rows_two = (unit_rows * gain + shift).astype(BF16)
        normed_two[at, :] = rows_two
        turned = rows_two.T
        keep_out[:dim, at] = turned
        send_out[:dim, at] = turned
        grad_ffn[at, :] = jnp.where(keep, cots[at, :].astype(F32), 0.0).astype(BF16)

    for side, (w_ref, b_ref, part_out) in enumerate(
        ((wu_own, bias_u_own, keep_out), (wu, bias_u, send_out))
    ):
        columns = slice(side * width, (side + 1) * width)
        slope[:, columns] = dot(normed_two[...], w_ref[...]) + row_of(b_ref)

        for m in range(mols):
            at = slice(m * SEQ, (m + 1) * SEQ)
            before = slope[at, columns]
            phi = 0.5 * (1.0 + lax.erf(before * math.sqrt(0.5)))
            out = (before * phi).astype(BF16)
            slope[at, columns] = phi + before * jnp.exp(before * before * -0.5) * (
                1.0 / math.sqrt(2.0 * math.pi)
            )
            active[at, columns] = out
            part_out[dim + width : dim + 2 * width, at] = out.T

    place_b = dim + 2 * width
    for side, (w_ref, part_out) in enumerate(((wd_own, keep_out), (wd, send_out))):
        columns = slice(side * width, (side + 1) * width)
        grad_before = slope[:, columns] * dot_nt(grad_ffn[...], w_ref[...])
        part_out[place_b : place_b + rows, :] = grad_before.astype(BF16)

    back = pl.ds(place_b, rows)
    gm_out[...] = dot_nt(keep_out[back, :], wu_own[...]) + dot_nt(send_out[back, :], wu[...])

    nothing = jnp.zeros((1, dim), F32)
    sums = (nothing,) * 4
    for m in range(mols):
        at = slice(m * SEQ, (m + 1) * SEQ)
        place = core * mols + m
        keep = positions(SEQ) < nodes[place] + edges[place]
        grad_normed = gm_out[at, :]
        unit_rows = unit[at, :]
        _, inverse = norm_parts(middle[at, :])
        grad_result = jnp.where(keep, cots[at, :].astype(F32), 0.0)
        grad = grad_result + norm_back(unit_rows, inverse, grad_normed * gain)
        gm_out[at, :] = grad
        grad_branch[at, :] = grad.astype(BF16)
        sums = (
            sums[0] + row_sum(grad),
            sums[1] + row_sum(grad_normed * unit_rows),
            sums[2] + row_sum(grad_normed),
            sums[3] + row_sum(grad_result),
        )

    place_m = place_b + rows
    for part_out in (keep_out, send_out):
        part_out[place_m : place_m + rows, :] = grad_branch[:, :width]
        part_out[place_m + rows : place_m + 2 * rows, :] = grad_branch[:, width:]
    small = jnp.concatenate(list(sums) + [nothing] * 12, axis=0)
    left, right = small[:, :width], small[:, width:]
    place_s = place_m + 2 * rows
    keep_out[place_s:, :] = jnp.where(core == 0, left, right).astype(BF16)
    send_out[place_s:, :] = jnp.where(core == 0, right, left).astype(BF16)


def result_kernel(middle, active, wd_own, wd, bias, result_out):
    width = wd.shape[0]
    result_out[...] = (
        middle[...]
        + dot(active[:, :width], wd_own[...])
        + dot(active[:, width:], wd[...])
        + row_of(bias)
    ).astype(BF16)


def branch_kernel(
    grad_branch, wo_own, wo, nodes_in, edges_in, ga_own_out, ga_out, nodes, edges, sems
):
    mols = grad_branch.shape[0] // SEQ
    core = places()[0]
    copies = copy_in((nodes_in, edges_in), (nodes, edges), sems)
    products = [dot_nt(grad_branch[...], weight[...]) for weight in (wo_own, wo)]
    for copy in copies:
        copy.wait()
    for ref, product in zip((ga_own_out, ga_out), products):
        for m in range(mols):
            place = core * mols + m
            keep = positions(SEQ) < nodes[place] + edges[place]
            at = slice(m * SEQ, (m + 1) * SEQ)
            ref[at, :] = jnp.where(keep, product[at], 0.0).astype(BF16)


def attend_back_kernel(
    m, q_own, k_own, v_own, ga_own, q_got, k_got, v_got, ga_got, probs_all,
    keep_out, send_out, dq_t, dk, dv, slopes,
):
    width = q_own.shape[1]
    pairs = width // (2 * HDIM)
    windows = head_windows(width)
    at = slice(m * SEQ, (m + 1) * SEQ)
    sides = (
        (q_own, k_own, v_own, ga_own, keep_out),
        (q_got, k_got, v_got, ga_got, send_out),
    )

    def score_back(side, pair):
        low, high = windows[pair]
        both_g = split_heads(sides[side][3][at, :], pair, windows[pair])
        probs_low = probs_all[m, side * pairs + pair]
        probs = probs_low.astype(F32)
        grad_probs = dot_nt(sides[side][2][at, low:high], both_g)
        inner = row_sum(probs * grad_probs)
        slopes[side, pair] = (probs * (grad_probs - inner)).astype(BF16)
        dv[side, :, low:high] += dot(probs_low, both_g)

    def rows_back(side, pair, keys_t):
        low, high = windows[pair]
        grad_scores = slopes[side, pair]
        both_q = split_heads(sides[side][0][at, :], pair, windows[pair])
        dk[side, :, low:high] += dot(grad_scores, both_q)
        first = pair * 2 * HDIM
        out = dot(keys_t[first : first + 2 * HDIM], grad_scores)
        dq_t[side, first : first + HDIM, :] = out[:HDIM, :SEQ]
        dq_t[side, first + HDIM : first + 2 * HDIM, :] = out[HDIM:, SEQ:]

    def finish(side):
        part_out = sides[side][4]
        part_out[:SEQ, :] = (dq_t[side] * SCALE).astype(BF16).T
        part_out[SEQ : 2 * SEQ, :] = (dk[side] * SCALE).astype(BF16)
        part_out[2 * SEQ :, :] = dv[side].astype(BF16)

    dk[...] = jnp.zeros_like(dk)
    dv[...] = jnp.zeros_like(dv)
    keys_t = [side[1][at, :].T for side in sides]
    for pair in range(pairs):
        score_back(0, pair)
    for pair in range(pairs):
        rows_back(0, pair, keys_t[0])
        score_back(1, pair)
    finish(0)
    for pair in range(pairs):
        rows_back(1, pair, keys_t[1])
    finish(1)


def embed_back_kernel(*refs):
    mols = (len(refs) - 25) // 2
    grads_own, grads = refs[:mols], refs[mols : 2 * mols]
    (
        wq_own, wk_own, wv_own, w_q, w_k, w_v, ident, grad_middle,
        feats_in, nodes_in, w_ident_in, types_in, gain_in,
        features_out, keep_out, send_out,
        feats, nodes, w_ident, types, gain_rows, sems, grad_normed, small, stacked,
    ) = refs[2 * mols :]
    core = places()[0]
    rows = feats.shape[0]
    copies = copy_in(
        (
            feats_in.at[pl.ds(pl.multiple_of(core * rows, SEQ), rows), :], nodes_in,
            w_ident_in, types_in, gain_in,
        ),
        (feats, nodes, w_ident, types, gain_rows),
        sems,
    )
    rows, dim = feats.shape
    width = wq_own.shape[1]
    idw = ident.shape[0]
    total = None
    for part, weights in ((grads_own, (wq_own, wk_own, wv_own)), (grads, (w_q, w_k, w_v))):
        for place, weight in enumerate(weights):
            for m in range(mols):
                stacked[m * SEQ : (m + 1) * SEQ, :] = part[m][place * SEQ : (place + 1) * SEQ, :]
            term = dot_nt(stacked[...], weight[...])
            total = term if total is None else total + term
    grad_normed[...] = total
    small[...] = jnp.zeros_like(small)
    for copy in copies:
        copy.wait()
    gain = row_of(gain_rows)
    kinds = types[...].astype(F32)

    def molecule(m, carry):
        at = pl.ds(pl.multiple_of(m * SEQ, SEQ), SEQ)
        is_edge = positions(SEQ) >= nodes[core * mols + m]
        hidden = feats[at, :].astype(F32) + dot_tn(ident[:, at], w_ident[...])
        hidden = hidden + jnp.where(is_edge, kinds[1:2, :], kinds[0:1, :])
        unit, inverse = norm_parts(hidden)
        grad_rows = grad_normed[at, :]
        grad = grad_middle[at, :] + norm_back(unit, inverse, grad_rows * gain)
        features_out[at, :] = grad
        high = grad.astype(BF16)
        rest = (grad - high.astype(F32)).astype(BF16)
        picked = ident[:, at]
        small[:idw, :] += dot(picked, high) + dot(picked, rest)
        edge_rows = jnp.where(is_edge, grad, 0.0)
        small[idw : idw + 1, :] += row_sum(grad - edge_rows)
        small[idw + 1 : idw + 2, :] += row_sum(edge_rows)
        small[idw + 2 : idw + 3, :] += row_sum(grad_rows * unit)
        small[idw + 3 : idw + 4, :] += row_sum(grad_rows)
        return carry

    lax.fori_loop(0, mols, molecule, 0)
    left, right = small[:, :width], small[:, width:]
    keep_out[...] = jnp.where(core == 0, left, right)
    send_out[...] = jnp.where(core == 0, right, left).astype(BF16)


def deal(unit, outs, block_at, small=None):
    _, inner, outer = places()
    first_kept, first_sent, second_kept, second_sent = outs
    for step in range(INNER):
        for turn in range(OUTER):
            if turn < 2:
                out, slot = (first_sent if step % 2 else first_kept), step // 2
            else:
                out, slot = (second_sent if step // 2 else second_kept), step % 2
            start = (slot * 2 + turn % 2) * 3 * unit
            for place in range(3):
                out[start + place * unit : start + (place + 1) * unit, :] = block_at(
                    inner ^ step, outer ^ turn, place
                )
    if small is not None:
        for out in (first_kept, first_sent):
            out[INNER * 3 * unit :, :] = small


def ffn_grads_kernel(kept, got, cots_in, nodes_in, edges_in, *rest):
    outs, (cots, nodes, edges, sems, tall, flat, grad_ffn) = rest[:4], rest[4:]
    copies = copy_in((nodes_in, edges_in, cots_in), (nodes, edges, cots), sems)
    rows_all, dim = cots.shape
    rows, width = rows_all // 2, kept.shape[1]
    mols = rows // SEQ
    core = places()[0]
    own_rows = pl.ds(pl.multiple_of(core * rows, SEQ), rows)
    other_rows = pl.ds(pl.multiple_of((1 - core) * rows, SEQ), rows)
    place_b = dim + 2 * width
    place_m = place_b + rows
    place_s = place_m + 2 * rows
    back = slice(place_b, place_m)
    tall[...] = (dot(kept[:dim, :], kept[back, :]) + dot(got[:dim, :], got[back, :])).astype(BF16)
    turned = slice(dim, dim + width)
    for half in (0, 1):
        mid = slice(place_m + half * rows, place_m + (half + 1) * rows)
        flat[half] = (
            dot(kept[turned, :], kept[mid, :]) + dot(got[turned, :], got[mid, :])
        ).astype(BF16)
    for copy in copies:
        copy.wait()
    for m in range(2 * mols):
        keep = positions(SEQ) < nodes[m] + edges[m]
        at = slice(m * SEQ, (m + 1) * SEQ)
        grad_ffn[at, :] = jnp.where(keep, cots[at, :].astype(F32), 0.0).astype(BF16)
    turned = slice(dim + width, dim + 2 * width)
    for half in (0, 1):
        columns = slice(half * width, (half + 1) * width)
        product = dot(kept[turned, :], grad_ffn[own_rows, columns])
        product = product + dot(got[turned, :], grad_ffn[other_rows, columns])
        flat[2 + half] = product.astype(BF16)
    bias = row_sum(kept[back, :].astype(F32)) + row_sum(got[back, :].astype(F32))
    small = kept[place_s:, :].astype(F32) + got[place_s:, :].astype(F32)
    spot = lax.broadcasted_iota(jnp.int32, small.shape, 0)
    small = jnp.where(spot == 4, bias, small).astype(BF16)
    unit = dim // (INNER * OUTER)

    def block_at(dest, z, place):
        if place == 0:
            return tall[pl.ds(pl.multiple_of((dest * OUTER + z) * unit, 16), unit), :]
        row = pl.multiple_of((dest * (OUTER // 2) + z // 2) * unit, 16)
        return flat[2 * (place - 1) + z % 2, pl.ds(row, unit), :]

    deal(unit, outs, block_at, small)


def qkv_grads_kernel(normed_t, normed_t_got, *refs):
    mols = normed_t.shape[1] // SEQ
    kept, got = refs[:mols], refs[mols : 2 * mols]
    outs, small_out = refs[2 * mols : 2 * mols + 4], refs[2 * mols + 4]
    tall, normed, stacked = refs[2 * mols + 5 :]
    dim, rows = normed_t.shape
    unit = dim // (INNER * OUTER)
    normed[:, :rows] = normed_t[...]
    normed[:, rows:] = normed_t_got[...]
    spot = lax.broadcasted_iota(jnp.int32, small_out.shape, 0)
    small = jnp.zeros(small_out.shape, F32)
    for place in range(3):
        for m, part in enumerate(kept + got):
            stacked[m * SEQ : (m + 1) * SEQ, :] = part[place * SEQ : (place + 1) * SEQ, :]
        tall[place] = dot(normed[...], stacked[...]).astype(BF16)
        if place != 1:
            small = jnp.where(spot == 36 + place // 2, row_sum(stacked[...].astype(F32)), small)
    small_out[...] = small

    def block_at(dest, z, place):
        return tall[place, pl.ds(pl.multiple_of((dest * OUTER + z) * unit, 16), unit), :]

    deal(unit, outs, block_at)


def add(first, second):
    return (first.astype(F32) + second.astype(F32)).astype(BF16)


def plane_sum_kernel(first, first_got, second, second_got, *refs):
    late, (first_kept, first_sent, second_kept, second_sent) = refs[:-4], refs[-4:]
    pair = second_kept.shape[0]
    total = add(first[...], first_got[...])
    first_kept[:pair, :] = total[:pair]
    first_sent[:pair, :] = total[pair : 2 * pair]
    if late:
        small = (late[0][...] + late[1][...].astype(F32) + late[2][...]).astype(BF16)
    else:
        small = total[2 * pair :]
    first_kept[pair:, :] = small
    first_sent[pair:, :] = small
    total = add(second[...], second_got[...])
    second_kept[...] = total[:pair]
    second_sent[...] = total[pair:]


def line_cut_kernel(first, first_got, second, second_got, own, near, middle, far):
    chunk = own.shape[0]
    total = add(first[...], first_got[...])
    own[...] = total[:chunk]
    near[...] = total[chunk:]
    total = add(second[...], second_got[...])
    middle[...] = total[:chunk]
    far[...] = total[chunk:]


def line_sum_kernel(own, near, near_got, middle_got, far_got, out, out_small):
    chunk = own.shape[0]
    total = own[...].astype(F32) + near_got[:chunk, :].astype(F32)
    total = total + middle_got[...].astype(F32) + far_got[...].astype(F32)
    out[...] = total.astype(BF16)
    out_small[:chunk, :] = total.astype(BF16)
    out_small[chunk:, :] = add(near[chunk:, :], near_got[chunk:, :])


def line_join_kernel(own, near, middle, far, line_x, line_y, small_out):
    chunk = near.shape[0]
    small = own[chunk:, :].astype(F32) + middle[chunk:, :].astype(F32)
    small_out[...] = small
    for out in (line_x, line_y):
        for turn, part in enumerate((own, near, middle, far)):
            out[turn * chunk : (turn + 1) * chunk, :] = part[:chunk, :]
    line_x[OUTER * chunk :, :] = small.astype(BF16)


def place_kernel(split_second, *refs):
    outs, parts = refs[-3:], refs[:-3]
    own = parts[0]
    _, inner, outer = places()
    unit = own.shape[0] // (3 * OUTER)
    width = own.shape[1]
    for step in range(INNER):
        for turn in range(OUTER):
            ref, start = parts[step], turn * 3 * unit
            if step == 3 and turn >= 2:
                ref, start = parts[4], (turn - 2) * 3 * unit
            dest, z = inner ^ step, outer ^ turn
            tall = pl.ds(pl.multiple_of((dest * OUTER + z) * unit, 16), unit)
            flat = pl.ds(pl.multiple_of((dest * (OUTER // 2) + z // 2) * unit, 16), unit)
            columns = pl.ds(pl.multiple_of(z % 2 * width, LANES), width)
            for place in range(3):
                part = ref[start + place * unit : start + (place + 1) * unit, :].astype(F32)
                if split_second and place > 0:
                    outs[place][flat, columns] = part
                else:
                    outs[place][tall, :] = part


def finish_first_kernel(small, got, bias_out, gain, shift, bias_down, bias_up):
    core = places()[0]
    for place, ref in enumerate((bias_out, gain, shift, bias_down)):
        mine, other = small[place : place + 1, :], got[place : place + 1, :]
        left = jnp.where(core == 0, mine, other)
        put_row(ref, jnp.concatenate([left, jnp.where(core == 0, other, mine)], axis=1))
    put_row(bias_up, small[4:5, :])


def finish_second_kernel(small, extra, got, w_ident, types, gain, shift, bias_q, bias_v):
    idw = w_ident.shape[0]
    core = places()[0]
    mine, other = small[...] + extra[...].astype(F32), got[...]
    left = jnp.where(core == 0, mine, other)
    total = jnp.concatenate([left, jnp.where(core == 0, other, mine)], axis=1)
    w_ident[...] = total[:idw]
    types[...] = total[idw : idw + 2]
    put_row(gain, total[idw + 2 : idw + 3])
    put_row(shift, total[idw + 3 : idw + 4])
    put_row(bias_q, mine[idw + 4 : idw + 5])
    put_row(bias_v, mine[idw + 5 : idw + 6])


def per_device(
    features, lap_vectors, node_counts, edge_counts, endpoints, w_ident, type_table,
    gain_one, shift_one, w_query, w_key, w_value, bias_query, bias_value, w_out, bias_out,
    gain_two, shift_two, w_up, bias_up, w_down, bias_down, cotangent,
):
    dp_count = lax.axis_size("dp")
    dp_index = lax.axis_index("dp")
    mp_index = lax.axis_index("mp")
    block = INNER * OUTER
    rest_count = dp_count // block
    def swap(part):
        return lax.ppermute(part, "mp", [(0, 1), (1, 0)])

    def inner_move(part, step):
        return lax.ppermute(part, "dp", [(s, s ^ step) for s in range(dp_count)])

    def outer_move(part, step):
        return lax.ppermute(part, "dp", [(s, s ^ (step * INNER)) for s in range(dp_count)])

    rows_all, dim = features.shape
    rows = rows_all // 2
    mols = rows // SEQ
    width = w_query.shape[1]
    heads = width // HDIM
    lapk = lap_vectors.shape[1]
    idw = w_ident.shape[0]

    def pinned(part):
        return pltpu.with_memory_space_constraint(part, pltpu.HBM)

    def lanes(part):
        return pinned(part.reshape(-1, LANES))

    nodes, edges = pinned(node_counts), pinned(edge_counts)
    count_scratch = pltpu.SMEM(node_counts.shape, jnp.int32)
    wide_scratch = pltpu.VMEM((dim // LANES, LANES), BF16)
    half_scratch = pltpu.VMEM((width // LANES, LANES), BF16)
    embed_args = (
        pinned(features), pinned(lap_vectors.T), pinned(endpoints.T), nodes,
        pinned(w_ident), pinned(type_table), lanes(gain_one), lanes(shift_one),
    )
    embed_scratch = [
        pltpu.VMEM((rows, dim), BF16),
        pltpu.VMEM((lapk, rows), BF16),
        pltpu.VMEM((2, rows), jnp.int32),
        count_scratch,
        pltpu.VMEM((idw, dim), BF16),
        pltpu.VMEM((2, dim), BF16),
        wide_scratch,
        wide_scratch,
    ]

    wq_got, wk_got, wv_got = swap(w_query), swap(w_key), swap(w_value)
    bq_got, bv_got, bu_got = swap(bias_query), swap(bias_value), swap(bias_up)
    wo_got, wu_got, wd_got = swap(w_out), swap(w_up), swap(w_down)

    hidden, ident, normed, normed_t, q_own, k_own, v_own = call(
        embed_kernel,
        (
            *embed_args, lanes(bias_query), lanes(bias_value),
            pinned(w_query), pinned(w_key), pinned(w_value),
        ),
        [outside()] * 13,
        [
            ((rows, dim), F32),
            ((idw, rows), BF16),
            ((rows, dim), BF16),
            ((dim, rows), BF16),
            ((rows, width), BF16),
            ((rows, width), BF16),
            ((rows, width), BF16),
        ],
        scratch=embed_scratch
        + [half_scratch] * 2
        + [pltpu.VMEM((dim, width), BF16)] * 3
        + [pltpu.SemaphoreType.DMA((13,))],
    )
    sent_rows = dim + 2 * width + 3 * rows + 16
    (
        q_got, k_got, v_got, probs, kept_a, sent_a, middle, active, grad_middle, grad_branch,
    ) = call(
        forward_kernel,
        (
            hidden, normed, q_own, k_own, v_own, wq_got, wk_got, wv_got,
            w_out, wo_got, w_up, wu_got, w_down, wd_got,
            *(part.reshape(-1, LANES) for part in (bq_got, bv_got, bu_got)),
            nodes, edges, pinned(cotangent),
            lanes(bias_up), lanes(bias_out), lanes(gain_two), lanes(shift_two),
        ),
        [whole()] * 17 + [outside()] * 7,
        [
            ((rows, width), BF16),
            ((rows, width), BF16),
            ((rows, width), BF16),
            ((mols, heads, SEQ, 2 * SEQ), BF16),
            ((sent_rows, width), BF16),
            ((sent_rows, width), BF16),
            ((rows, dim), F32),
            ((rows, dim), BF16),
            ((rows, dim), F32),
            ((rows, dim), BF16),
        ],
        scratch=[
            count_scratch,
            count_scratch,
            pltpu.VMEM((rows, dim), BF16),
            half_scratch,
            wide_scratch,
            wide_scratch,
            wide_scratch,
            pltpu.SemaphoreType.DMA((7,)),
            pltpu.VMEM((2, width, SEQ), F32),
            pltpu.VMEM((rows, dim), BF16),
            pltpu.VMEM((rows, dim), F32),
            pltpu.VMEM((rows, dim), BF16),
            pltpu.VMEM((rows, dim), F32),
            pltpu.VMEM((rows, dim), BF16),
        ],
        limit=30,
    )
    got_a = swap(sent_a)
    ga_own, ga_got = call(
        branch_kernel,
        (grad_branch, w_out, wo_got, nodes, edges),
        [whole()] * 3 + [outside()] * 2,
        [((rows, width), BF16), ((rows, width), BF16)],
        scratch=[count_scratch, count_scratch, pltpu.SemaphoreType.DMA((2,))],
    )

    unit = dim // block
    chunk = 3 * unit
    small_a, small_b = 16, 48

    def rest_sum(part):
        if rest_count == 1:
            return part
        groups = [[r * block + s for r in range(rest_count)] for s in range(block)]
        return lax.psum(part.astype(F32), "dp", axis_index_groups=groups).astype(part.dtype)

    pair = 2 * chunk

    def after(part, *others):
        return lax.optimization_barrier((part, *others))[0]

    def plane_step(parts, small_rows, late=(), others=(), micros=0):
        first, first_sent, second, second_sent = parts
        first_got = after(inner_move(first_sent, 1), *others)
        second_got = after(inner_move(second_sent, 2), *others)
        return call(
            plane_sum_kernel,
            (first, first_got, second, second_got, *late),
            [whole()] * (4 + len(late)),
            [((pair + small_rows, width), BF16)] * 2 + [((pair, width), BF16)] * 2,
            micros=micros,
        )

    def plane_turn(parts, others=(), micros=0):
        first, first_sent, second, second_sent = parts
        first_got = after(inner_move(first_sent, 2), *others)
        second_got = after(inner_move(second_sent, 1), *others)
        return call(
            line_cut_kernel,
            (first, first_got, second, second_got),
            [whole()] * 4,
            [
                ((chunk, width), BF16),
                ((first.shape[0] - chunk, width), BF16),
                ((chunk, width), BF16),
                ((chunk, width), BF16),
            ],
            micros=micros,
        )

    def line_step(parts, others=(), micros=0):
        got = [after(outer_move(parts[turn], turn), *others) for turn in range(1, OUTER)]
        mine, both = call(
            line_sum_kernel,
            (parts[0], parts[1], *got),
            [whole()] * 5,
            [((chunk, width), BF16), (parts[1].shape, BF16)],
            micros=micros,
        )
        if rest_count > 1:
            both = rest_sum(both)
            mine = both[:chunk]
        return mine, both

    def line_back(mine, both, others=(), micros=0):
        sent = (mine, both, mine)
        got = [after(outer_move(sent[turn - 1], turn), *others) for turn in range(1, OUTER)]
        small_rows = both.shape[0] - chunk
        return call(
            line_join_kernel,
            (both, *got),
            [whole()] * OUTER,
            [
                ((OUTER * chunk + small_rows, width), BF16),
                ((OUTER * chunk, width), BF16),
                ((small_rows, width), F32),
            ],
            micros=micros,
        )

    def plane_back(lines):
        return inner_move(lines[0], 1), inner_move(lines[1], 2)

    def plane_back_turn(side_x, side_y):
        return inner_move(side_y[:pair], 1), inner_move(side_x[pair : 2 * pair], 2)

    def placed(planes, split_second, micros=0):
        tall, flat = ((dim, width), F32), ((width, dim), F32)
        return call(
            lambda *refs: place_kernel(split_second, *refs),
            planes,
            [whole()] * len(planes),
            [tall, flat, flat] if split_second else [tall] * 3,
            micros=micros,
        )

    def attend_back(m, query_rows):
        return call(
            lambda *refs: attend_back_kernel(m, *refs),
            (query_rows, k_own, v_own, ga_own, q_got, k_got, v_got, ga_got, probs),
            [whole()] * 9,
            [((3 * SEQ, width), BF16)] * 2,
            scratch=[
                pltpu.VMEM((2, width, SEQ), F32),
                pltpu.VMEM((2, SEQ, width), F32),
                pltpu.VMEM((2, SEQ, width), F32),
                pltpu.VMEM((2, heads // 2, SEQ, 2 * SEQ), BF16),
            ],
        )

    backs = [attend_back(0, q_own)]
    kept_a = after(kept_a, backs[0][0])
    parts_a = call(
        ffn_grads_kernel,
        (kept_a, got_a, pinned(cotangent), nodes, edges),
        [whole()] * 2 + [outside()] * 3,
        [((INNER * chunk + small_a, width), BF16)] * 2 + [((INNER * chunk, width), BF16)] * 2,
        scratch=[
            pltpu.VMEM((rows_all, dim), BF16),
            count_scratch,
            count_scratch,
            pltpu.SemaphoreType.DMA((3,)),
            pltpu.VMEM((dim, width), BF16),
            pltpu.VMEM((4, width, width), BF16),
            pltpu.VMEM((rows_all, dim), BF16),
        ],
    )
    normed_t_got = swap(after(normed_t, parts_a[0]))
    for m in range(1, mols):
        gates = (parts_a[0], backs[-1][0]) + ((normed_t_got,) if m == mols - 1 else ())
        backs.append(attend_back(m, after(q_own, *gates)))
    kept_b = [back[0] for back in backs]
    sent_b = [back[1] for back in backs]
    got_b = [swap(sent) for sent in sent_b]
    steps_a = plane_step(parts_a, small_a, others=(kept_b[-1],))
    normed_t = after(normed_t, *steps_a)
    parts_b = call(
        qkv_grads_kernel,
        (normed_t, normed_t_got, *kept_b, *got_b),
        [whole()] * (2 + 2 * mols),
        [((INNER * chunk, width), BF16)] * 4 + [((small_b, width), F32)],
        scratch=[
            pltpu.VMEM((3, dim, width), BF16),
            pltpu.VMEM((dim, 2 * rows), BF16),
            pltpu.VMEM((2 * rows, width), BF16),
        ],
    )
    turned_a = plane_turn(steps_a, others=(parts_b[0],), micros=3)
    grad_middle = after(grad_middle, parts_b[0], *turned_a)
    grad_features, small_kept, small_sent = call(
        embed_back_kernel,
        (
            *kept_b, *sent_b, w_query, w_key, w_value, wq_got, wk_got, wv_got, ident,
            grad_middle, embed_args[0], nodes, *embed_args[4:7],
        ),
        [whole()] * (8 + 2 * mols) + [outside()] * 5,
        [((rows, dim), F32), ((small_b, width), F32), ((small_b, width), BF16)],
        scratch=[
            pltpu.VMEM((rows, dim), BF16),
            count_scratch,
            pltpu.VMEM((idw, dim), BF16),
            pltpu.VMEM((2, dim), BF16),
            wide_scratch,
            pltpu.SemaphoreType.DMA((5,)),
            pltpu.VMEM((rows, dim), F32),
            pltpu.VMEM((small_b, dim), F32),
            pltpu.VMEM((rows, width), BF16),
        ],
        micros=0,
    )
    small_got = swap(small_sent)
    steps_b = plane_step(parts_b[:4], small_b, late=(small_kept, small_got, parts_b[4]))
    line_a = line_step(turned_a, others=steps_b, micros=3)
    turned_b = plane_turn(steps_b, others=line_a[:1])
    lines_a = line_back(*line_a, others=turned_b, micros=3)
    line_b = line_step(turned_b, micros=12)
    sides_a = plane_back((lines_a[1], lines_a[1]))
    far_a = plane_back_turn(*sides_a)
    planes_a = (lines_a[1], *sides_a, *far_a)
    lines_b = line_back(*line_b, micros=2)
    result = call(
        result_kernel,
        (middle, active, w_down, wd_got, lanes(after(bias_down, lines_b[1]))),
        [whole()] * 5,
        [((rows, dim), BF16)],
    )[0]
    wide, half = ((dim // LANES, LANES), F32), ((width // LANES, LANES), F32)
    sums_a = call(
        finish_first_kernel,
        (lines_a[2], swap(after(lines_a[2], lines_b[1]))),
        [whole()] * 2,
        [wide] * 4 + [half],
    )
    grad_w_up, grad_w_out, grad_w_down = placed(planes_a, True, micros=10)
    sides_b = plane_back(lines_b)
    sides_b, _ = lax.optimization_barrier((sides_b, (result, sums_a, grad_w_up)))
    far_b = plane_back_turn(*sides_b)
    planes_b = (lines_b[1], sides_b[0], sides_b[1], *far_b)
    extra = sides_b[0][OUTER * chunk :]
    own_b = lines_b[2] + extra.astype(F32)
    sums_b = call(
        finish_second_kernel,
        (lines_b[2], extra, swap(own_b)),
        [whole()] * 3,
        [((idw, dim), F32), ((2, dim), F32), wide, wide, half, half],
    )
    grad_w_query, grad_w_key, grad_w_value = placed(planes_b, False)
    return (
        result,
        grad_features,
        sums_b[0],
        sums_b[1],
        sums_b[2].reshape(-1),
        sums_b[3].reshape(-1),
        grad_w_query,
        grad_w_key,
        grad_w_value,
        sums_b[4].reshape(-1),
        sums_b[5].reshape(-1),
        grad_w_out,
        sums_a[0].reshape(-1),
        sums_a[1].reshape(-1),
        sums_a[2].reshape(-1),
        grad_w_up,
        sums_a[4].reshape(-1),
        grad_w_down,
        sums_a[3].reshape(-1),
    )


def solution(mesh):
    token, split = P("dp", None), P(("dp", "mp"), None)
    columns, lines, cut, copy = P(None, "mp"), P("mp", None), P("mp"), P()
    return jax.shard_map(
        per_device,
        mesh=mesh,
        in_specs=(
            token, token, P("dp"), P("dp"), token, copy, copy, copy, copy, columns, columns,
            columns, cut, cut, lines, copy, copy, copy, columns, cut, lines, copy, token,
        ),
        out_specs=(
            split, split, copy, copy, copy, copy, columns, columns, columns, cut, cut, lines,
            copy, copy, copy, columns, cut, lines, copy,
        ),
        check_vma=False,
    )
```

```python
import math

import jax
import jax.numpy as jnp
from jax import lax
from jax.experimental import pallas as pl
from jax.experimental.pallas import tpu as pltpu
from jax.sharding import PartitionSpec as P

HDIM = 24
SEQ = 128
LANES = 128
INNER = 4
OUTER = 4
EPSILON = 1e-05
SCALE = 1.0 / math.sqrt(HDIM)
LOG2_SCALE = SCALE * math.log2(math.e)
F32, BF16 = jnp.float32, jnp.bfloat16
MIB = 1024 * 1024


def dot(left, right):
    return jnp.dot(left, right, preferred_element_type=F32)


def dot_nt(left, right):
    return lax.dot_general(left, right, (((1,), (1,)), ((), ())), preferred_element_type=F32)


def dot_tn(left, right):
    return lax.dot_general(left, right, (((0,), (0,)), ((), ())), preferred_element_type=F32)


def norm_parts(hidden):
    average = jnp.mean(hidden, axis=-1, keepdims=True)
    centred = hidden - average
    inverse = lax.rsqrt(jnp.mean(centred * centred, axis=-1, keepdims=True) + EPSILON)
    return centred * inverse, inverse


def norm_back(unit, inverse, grad_hat):
    return inverse * (
        grad_hat
        - jnp.mean(grad_hat, axis=-1, keepdims=True)
        - unit * jnp.mean(grad_hat * unit, axis=-1, keepdims=True)
    )


def row_sum(block):
    return jnp.sum(block, axis=0, keepdims=True)


def positions(length):
    return lax.broadcasted_iota(jnp.int32, (length, 1), 0)


def whole():
    return pl.BlockSpec(memory_space=pltpu.VMEM)


def outside():
    return pl.BlockSpec(memory_space=pltpu.HBM)


def places():
    index = lax.axis_index("dp")
    return lax.axis_index("mp"), index % INNER, index // INNER % OUTER


def copy_in(sources, targets, sems):
    copies = [
        pltpu.make_async_copy(source, target, sems.at[place])
        for place, (source, target) in enumerate(zip(sources, targets))
    ]
    for copy in copies:
        copy.start()
    return copies


def row_of(ref):
    block = ref[...].astype(F32)
    return jnp.concatenate([block[r : r + 1, :] for r in range(block.shape[0])], axis=1)


def put_row(ref, row):
    for r in range(ref.shape[0]):
        ref[r : r + 1, :] = row[:, r * LANES : (r + 1) * LANES]


def call(kernel, args, specs, outs, scratch=(), micros=0, limit=24):
    return pl.pallas_call(
        kernel,
        out_shape=[jax.ShapeDtypeStruct(shape, kind) for shape, kind in outs],
        in_specs=specs,
        out_specs=[whole() for _ in outs],
        scratch_shapes=list(scratch),
        compiler_params=pltpu.CompilerParams(vmem_limit_bytes=limit * MIB),
        cost_estimate=pl.CostEstimate(
            flops=micros * 1_000_000_000, bytes_accessed=0, transcendentals=0
        ),
    )(*args)


def head_windows(width):
    windows = []
    for pair in range(width // (2 * HDIM)):
        low = pair * 2 * HDIM // LANES * LANES
        high = -(-(pair + 1) * 2 * HDIM // LANES) * LANES
        windows.append((low, high))
    return windows


def split_heads(block, pair, window):
    low, high = window
    part = block[:, low:high]
    column = low + lax.broadcasted_iota(jnp.int32, (16, high - low), 1)
    sides = []
    for head in (2 * pair, 2 * pair + 1):
        inside = (column >= head * HDIM) & (column < (head + 1) * HDIM)
        mask = jnp.where(inside, 1.0, 0.0).astype(BF16)
        sides.append(part * jnp.concatenate([mask] * (block.shape[0] // 16), axis=0))
    return jnp.concatenate(sides, axis=0)


def embed_rows(feats, lap, ends, w_ident, types, gain, shift, at, count):
    table = lap[:, at]
    slot = lax.broadcasted_iota(jnp.int32, (SEQ, SEQ), 0)
    picked = []
    for end in (0, 1):
        pick = jnp.where(ends[end : end + 1, at] == slot, 1.0, 0.0).astype(BF16)
        picked.append(dot(table, pick))
    ident = jnp.concatenate(picked, axis=0).astype(BF16)
    hidden = feats[at, :].astype(F32) + dot_tn(ident, w_ident[...])
    kinds = types[...].astype(F32)
    hidden = hidden + jnp.where(positions(SEQ) >= count, kinds[1:2, :], kinds[0:1, :])
    unit, _ = norm_parts(hidden)
    return hidden, ident, (unit * gain + shift).astype(BF16)


def embed_kernel(
    feats_in, lap_in, ends_in, nodes_in, w_ident_in, types_in, gain_in, shift_in,
    bias_q_in, bias_v_in, wq_in, wk_in, wv_in,
    hidden_out, ident_out, normed_out, normed_t_out, q_out, k_out, v_out,
    feats, lap, ends, nodes, w_ident, types, gain_rows, shift_rows, bias_q, bias_v,
    w_q, w_k, w_v, sems,
):
    rows, dim = feats.shape
    mols = rows // SEQ
    core = places()[0]
    own_rows = pl.ds(pl.multiple_of(core * rows, SEQ), rows)
    copies = copy_in(
        (
            feats_in.at[own_rows, :], lap_in.at[:, own_rows], ends_in.at[:, own_rows], nodes_in,
            w_ident_in, types_in, gain_in, shift_in, bias_q_in, bias_v_in, wq_in, wk_in, wv_in,
        ),
        (
            feats, lap, ends, nodes, w_ident, types, gain_rows, shift_rows, bias_q, bias_v,
            w_q, w_k, w_v,
        ),
        sems,
    )
    for copy in copies[:10]:
        copy.wait()
    gain, shift = row_of(gain_rows), row_of(shift_rows)

    def molecule(m):
        at = slice(m * SEQ, (m + 1) * SEQ)
        count = nodes[core * mols + m]
        hidden, ident, normed = embed_rows(
            feats, lap, ends, w_ident, types, gain, shift, at, count
        )
        ident_out[:, at] = ident
        hidden_out[at, :] = hidden
        normed_out[at, :] = normed
        normed_t_out[:, at] = normed.T

    for m in range(mols):
        molecule(m)
    normed = normed_out[...]
    copies[10].wait()
    q_out[...] = (dot(normed, w_q[...]) + row_of(bias_q)).astype(BF16)
    copies[11].wait()
    k_out[...] = dot(normed, w_k[...]).astype(BF16)
    copies[12].wait()
    v_out[...] = (dot(normed, w_v[...]) + row_of(bias_v)).astype(BF16)


def forward_kernel(
    hidden, normed, q_own, k_own, v_own, w_q, w_k, w_v, wo_own, wo, wu_own, wu, wd_own, wd,
    bias_q, bias_v, bias_u,
    nodes_in, edges_in, cots_in, bias_u_own_in, bias_o_in, gain_in, shift_in,
    q_out, k_out, v_out, probs_out, keep_out, send_out, middle, active, gm_out, grad_branch,
    nodes, edges, cots, bias_u_own, bias_o, gain_rows, shift_rows, sems,
    mixed, attended, unit, normed_two, slope, grad_ffn,
):
    rows, dim = hidden.shape
    width = q_own.shape[1]
    mols = rows // SEQ
    pairs = width // (2 * HDIM)
    windows = head_windows(width)
    core = places()[0]
    copies = copy_in(
        (
            nodes_in, edges_in, cots_in.at[pl.ds(pl.multiple_of(core * rows, SEQ), rows), :],
            bias_u_own_in, bias_o_in, gain_in, shift_in,
        ),
        (nodes, edges, cots, bias_u_own, bias_o, gain_rows, shift_rows),
        sems,
    )

    q_out[...] = (dot(normed[...], w_q[...]) + row_of(bias_q)).astype(BF16)
    k_out[...] = dot(normed[...], w_k[...]).astype(BF16)
    v_out[...] = (dot(normed[...], w_v[...]) + row_of(bias_v)).astype(BF16)

    for copy in copies:
        copy.wait()
    gain, shift, bias_out = row_of(gain_rows), row_of(shift_rows), row_of(bias_o)

    sides = ((q_own, k_own, v_own, keep_out), (q_out, k_out, v_out, send_out))
    units = [(m, side) for m in range(mols) for side in (0, 1)]

    def weigh(unit, pair):
        m, side = unit
        at = slice(m * SEQ, (m + 1) * SEQ)
        place = core * mols + m
        key_keep = positions(SEQ) < nodes[place] + edges[place]
        low, high = windows[pair]
        both = split_heads(sides[side][0][at, :], pair, windows[pair])
        scores = dot_nt(sides[side][1][at, low:high], both)
        scores = jnp.where(key_keep, scores, -1e30)
        top = jnp.max(scores, axis=0, keepdims=True)
        raised = jnp.exp2((scores - top) * LOG2_SCALE)
        probs_out[m, side * pairs + pair] = (raised * (1.0 / row_sum(raised))).astype(BF16)

    def mix(unit, pair, values_t):
        m, side = unit
        first = pair * 2 * HDIM
        out = dot(values_t[first : first + 2 * HDIM], probs_out[m, side * pairs + pair])
        mixed[side, first : first + HDIM, :] = out[:HDIM, :SEQ]
        mixed[side, first + HDIM : first + 2 * HDIM, :] = out[HDIM:, SEQ:]

    def keep_mixed(unit):
        m, side = unit
        at = slice(m * SEQ, (m + 1) * SEQ)
        place = core * mols + m
        query_keep = lax.broadcasted_iota(jnp.int32, (1, SEQ), 1) < nodes[place] + edges[place]
        kept = jnp.where(query_keep, mixed[side], 0.0).astype(BF16)
        sides[side][3][dim : dim + width, at] = kept
        attended[at, side * width : (side + 1) * width] = kept.T

    for pair in range(pairs):
        weigh(units[0], pair)
    for step, task in enumerate(units):
        values_t = sides[task[1]][2][task[0] * SEQ : (task[0] + 1) * SEQ, :].T
        for pair in range(pairs):
            mix(task, pair, values_t)
            if step + 1 < len(units):
                weigh(units[step + 1], pair)
        keep_mixed(task)
    middle[...] = (
        hidden[...] + dot(attended[:, :width], wo_own[...]) + dot(attended[:, width:], wo[...])
    )

    for m in range(mols):
        at = slice(m * SEQ, (m + 1) * SEQ)
        place = core * mols + m
        keep = positions(SEQ) < nodes[place] + edges[place]
        total = middle[at, :] + bias_out
        middle[at, :] = total
        unit_rows, _ = norm_parts(total)
        unit[at, :] = unit_rows
        rows_two = (unit_rows * gain + shift).astype(BF16)
        normed_two[at, :] = rows_two
        turned = rows_two.T
        keep_out[:dim, at] = turned
        send_out[:dim, at] = turned
        grad_ffn[at, :] = jnp.where(keep, cots[at, :].astype(F32), 0.0).astype(BF16)

    for side, (w_ref, b_ref, part_out) in enumerate(
        ((wu_own, bias_u_own, keep_out), (wu, bias_u, send_out))
    ):
        columns = slice(side * width, (side + 1) * width)
        slope[:, columns] = dot(normed_two[...], w_ref[...]) + row_of(b_ref)

        for m in range(mols):
            at = slice(m * SEQ, (m + 1) * SEQ)
            before = slope[at, columns]
            phi = 0.5 * (1.0 + lax.erf(before * math.sqrt(0.5)))
            out = (before * phi).astype(BF16)
            slope[at, columns] = phi + before * jnp.exp(before * before * -0.5) * (
                1.0 / math.sqrt(2.0 * math.pi)
            )
            active[at, columns] = out
            part_out[dim + width : dim + 2 * width, at] = out.T

    place_b = dim + 2 * width
    for side, (w_ref, part_out) in enumerate(((wd_own, keep_out), (wd, send_out))):
        columns = slice(side * width, (side + 1) * width)
        grad_before = slope[:, columns] * dot_nt(grad_ffn[...], w_ref[...])
        part_out[place_b : place_b + rows, :] = grad_before.astype(BF16)

    back = pl.ds(place_b, rows)
    gm_out[...] = dot_nt(keep_out[back, :], wu_own[...]) + dot_nt(send_out[back, :], wu[...])

    nothing = jnp.zeros((1, dim), F32)
    sums = (nothing,) * 4
    for m in range(mols):
        at = slice(m * SEQ, (m + 1) * SEQ)
        place = core * mols + m
        keep = positions(SEQ) < nodes[place] + edges[place]
        grad_normed = gm_out[at, :]
        unit_rows = unit[at, :]
        _, inverse = norm_parts(middle[at, :])
        grad_result = jnp.where(keep, cots[at, :].astype(F32), 0.0)
        grad = grad_result + norm_back(unit_rows, inverse, grad_normed * gain)
        gm_out[at, :] = grad
        grad_branch[at, :] = grad.astype(BF16)
        sums = (
            sums[0] + row_sum(grad),
            sums[1] + row_sum(grad_normed * unit_rows),
            sums[2] + row_sum(grad_normed),
            sums[3] + row_sum(grad_result),
        )

    place_m = place_b + rows
    for part_out in (keep_out, send_out):
        part_out[place_m : place_m + rows, :] = grad_branch[:, :width]
        part_out[place_m + rows : place_m + 2 * rows, :] = grad_branch[:, width:]
    small = jnp.concatenate(list(sums) + [nothing] * 12, axis=0)
    left, right = small[:, :width], small[:, width:]
    place_s = place_m + 2 * rows
    keep_out[place_s:, :] = jnp.where(core == 0, left, right).astype(BF16)
    send_out[place_s:, :] = jnp.where(core == 0, right, left).astype(BF16)


def result_kernel(middle, active, wd_own, wd, bias, result_out):
    width = wd.shape[0]
    result_out[...] = (
        middle[...]
        + dot(active[:, :width], wd_own[...])
        + dot(active[:, width:], wd[...])
        + row_of(bias)
    ).astype(BF16)


def branch_kernel(
    grad_branch, wo_own, wo, nodes_in, edges_in, ga_own_out, ga_out, nodes, edges, sems
):
    mols = grad_branch.shape[0] // SEQ
    core = places()[0]
    copies = copy_in((nodes_in, edges_in), (nodes, edges), sems)
    products = [dot_nt(grad_branch[...], weight[...]) for weight in (wo_own, wo)]
    for copy in copies:
        copy.wait()
    for ref, product in zip((ga_own_out, ga_out), products):
        for m in range(mols):
            place = core * mols + m
            keep = positions(SEQ) < nodes[place] + edges[place]
            at = slice(m * SEQ, (m + 1) * SEQ)
            ref[at, :] = jnp.where(keep, product[at], 0.0).astype(BF16)


def attend_back_kernel(
    m, q_own, k_own, v_own, ga_own, q_got, k_got, v_got, ga_got, probs_all,
    keep_out, send_out, dq_t, dk, dv, slopes,
):
    width = q_own.shape[1]
    pairs = width // (2 * HDIM)
    windows = head_windows(width)
    at = slice(m * SEQ, (m + 1) * SEQ)
    sides = (
        (q_own, k_own, v_own, ga_own, keep_out),
        (q_got, k_got, v_got, ga_got, send_out),
    )

    def score_back(side, pair):
        low, high = windows[pair]
        both_g = split_heads(sides[side][3][at, :], pair, windows[pair])
        probs_low = probs_all[m, side * pairs + pair]
        probs = probs_low.astype(F32)
        grad_probs = dot_nt(sides[side][2][at, low:high], both_g)
        inner = row_sum(probs * grad_probs)
        slopes[side, pair] = (probs * (grad_probs - inner)).astype(BF16)
        dv[side, :, low:high] += dot(probs_low, both_g)

    def rows_back(side, pair, keys_t):
        low, high = windows[pair]
        grad_scores = slopes[side, pair]
        both_q = split_heads(sides[side][0][at, :], pair, windows[pair])
        dk[side, :, low:high] += dot(grad_scores, both_q)
        first = pair * 2 * HDIM
        out = dot(keys_t[first : first + 2 * HDIM], grad_scores)
        dq_t[side, first : first + HDIM, :] = out[:HDIM, :SEQ]
        dq_t[side, first + HDIM : first + 2 * HDIM, :] = out[HDIM:, SEQ:]

    def finish(side):
        part_out = sides[side][4]
        part_out[:SEQ, :] = (dq_t[side] * SCALE).astype(BF16).T
        part_out[SEQ : 2 * SEQ, :] = (dk[side] * SCALE).astype(BF16)
        part_out[2 * SEQ :, :] = dv[side].astype(BF16)

    dk[...] = jnp.zeros_like(dk)
    dv[...] = jnp.zeros_like(dv)
    keys_t = [side[1][at, :].T for side in sides]
    for pair in range(pairs):
        score_back(0, pair)
    for pair in range(pairs):
        rows_back(0, pair, keys_t[0])
        score_back(1, pair)
    finish(0)
    for pair in range(pairs):
        rows_back(1, pair, keys_t[1])
    finish(1)


def embed_back_kernel(*refs):
    mols = (len(refs) - 25) // 2
    grads_own, grads = refs[:mols], refs[mols : 2 * mols]
    (
        wq_own, wk_own, wv_own, w_q, w_k, w_v, ident, grad_middle,
        feats_in, nodes_in, w_ident_in, types_in, gain_in,
        features_out, keep_out, send_out,
        feats, nodes, w_ident, types, gain_rows, sems, grad_normed, small, stacked,
    ) = refs[2 * mols :]
    core = places()[0]
    rows = feats.shape[0]
    copies = copy_in(
        (
            feats_in.at[pl.ds(pl.multiple_of(core * rows, SEQ), rows), :], nodes_in,
            w_ident_in, types_in, gain_in,
        ),
        (feats, nodes, w_ident, types, gain_rows),
        sems,
    )
    rows, dim = feats.shape
    width = wq_own.shape[1]
    idw = ident.shape[0]
    total = None
    for part, weights in ((grads_own, (wq_own, wk_own, wv_own)), (grads, (w_q, w_k, w_v))):
        for place, weight in enumerate(weights):
            for m in range(mols):
                stacked[m * SEQ : (m + 1) * SEQ, :] = part[m][place * SEQ : (place + 1) * SEQ, :]
            term = dot_nt(stacked[...], weight[...])
            total = term if total is None else total + term
    grad_normed[...] = total
    small[...] = jnp.zeros_like(small)
    for copy in copies:
        copy.wait()
    gain = row_of(gain_rows)
    kinds = types[...].astype(F32)

    def molecule(m, carry):
        at = pl.ds(pl.multiple_of(m * SEQ, SEQ), SEQ)
        is_edge = positions(SEQ) >= nodes[core * mols + m]
        hidden = feats[at, :].astype(F32) + dot_tn(ident[:, at], w_ident[...])
        hidden = hidden + jnp.where(is_edge, kinds[1:2, :], kinds[0:1, :])
        unit, inverse = norm_parts(hidden)
        grad_rows = grad_normed[at, :]
        grad = grad_middle[at, :] + norm_back(unit, inverse, grad_rows * gain)
        features_out[at, :] = grad
        high = grad.astype(BF16)
        rest = (grad - high.astype(F32)).astype(BF16)
        picked = ident[:, at]
        small[:idw, :] += dot(picked, high) + dot(picked, rest)
        edge_rows = jnp.where(is_edge, grad, 0.0)
        small[idw : idw + 1, :] += row_sum(grad - edge_rows)
        small[idw + 1 : idw + 2, :] += row_sum(edge_rows)
        small[idw + 2 : idw + 3, :] += row_sum(grad_rows * unit)
        small[idw + 3 : idw + 4, :] += row_sum(grad_rows)
        return carry

    lax.fori_loop(0, mols, molecule, 0)
    left, right = small[:, :width], small[:, width:]
    keep_out[...] = jnp.where(core == 0, left, right)
    send_out[...] = jnp.where(core == 0, right, left).astype(BF16)


def deal(unit, outs, block_at, small=None):
    _, inner, outer = places()
    first_kept, first_sent, second_kept, second_sent = outs
    for step in range(INNER):
        for turn in range(OUTER):
            if turn < 2:
                out, slot = (first_sent if step % 2 else first_kept), step // 2
            else:
                out, slot = (second_sent if step // 2 else second_kept), step % 2
            start = (slot * 2 + turn % 2) * 3 * unit
            for place in range(3):
                out[start + place * unit : start + (place + 1) * unit, :] = block_at(
                    inner ^ step, outer ^ turn, place
                )
    if small is not None:
        for out in (first_kept, first_sent):
            out[INNER * 3 * unit :, :] = small


def ffn_grads_kernel(kept, got, cots_in, nodes_in, edges_in, *rest):
    outs, (cots, nodes, edges, sems, tall, flat, grad_ffn) = rest[:4], rest[4:]
    copies = copy_in((nodes_in, edges_in, cots_in), (nodes, edges, cots), sems)
    rows_all, dim = cots.shape
    rows, width = rows_all // 2, kept.shape[1]
    mols = rows // SEQ
    core = places()[0]
    own_rows = pl.ds(pl.multiple_of(core * rows, SEQ), rows)
    other_rows = pl.ds(pl.multiple_of((1 - core) * rows, SEQ), rows)
    place_b = dim + 2 * width
    place_m = place_b + rows
    place_s = place_m + 2 * rows
    back = slice(place_b, place_m)
    tall[...] = (dot(kept[:dim, :], kept[back, :]) + dot(got[:dim, :], got[back, :])).astype(BF16)
    turned = slice(dim, dim + width)
    for half in (0, 1):
        mid = slice(place_m + half * rows, place_m + (half + 1) * rows)
        flat[half] = (
            dot(kept[turned, :], kept[mid, :]) + dot(got[turned, :], got[mid, :])
        ).astype(BF16)
    for copy in copies:
        copy.wait()
    for m in range(2 * mols):
        keep = positions(SEQ) < nodes[m] + edges[m]
        at = slice(m * SEQ, (m + 1) * SEQ)
        grad_ffn[at, :] = jnp.where(keep, cots[at, :].astype(F32), 0.0).astype(BF16)
    turned = slice(dim + width, dim + 2 * width)
    for half in (0, 1):
        columns = slice(half * width, (half + 1) * width)
        product = dot(kept[turned, :], grad_ffn[own_rows, columns])
        product = product + dot(got[turned, :], grad_ffn[other_rows, columns])
        flat[2 + half] = product.astype(BF16)
    bias = row_sum(kept[back, :].astype(F32)) + row_sum(got[back, :].astype(F32))
    small = kept[place_s:, :].astype(F32) + got[place_s:, :].astype(F32)
    spot = lax.broadcasted_iota(jnp.int32, small.shape, 0)
    small = jnp.where(spot == 4, bias, small).astype(BF16)
    unit = dim // (INNER * OUTER)

    def block_at(dest, z, place):
        if place == 0:
            return tall[pl.ds(pl.multiple_of((dest * OUTER + z) * unit, 16), unit), :]
        row = pl.multiple_of((dest * (OUTER // 2) + z // 2) * unit, 16)
        return flat[2 * (place - 1) + z % 2, pl.ds(row, unit), :]

    deal(unit, outs, block_at, small)


def qkv_grads_kernel(normed_t, normed_t_got, *refs):
    mols = normed_t.shape[1] // SEQ
    kept, got = refs[:mols], refs[mols : 2 * mols]
    outs, small_out = refs[2 * mols : 2 * mols + 4], refs[2 * mols + 4]
    tall, normed, stacked = refs[2 * mols + 5 :]
    dim, rows = normed_t.shape
    unit = dim // (INNER * OUTER)
    normed[:, :rows] = normed_t[...]
    normed[:, rows:] = normed_t_got[...]
    spot = lax.broadcasted_iota(jnp.int32, small_out.shape, 0)
    small = jnp.zeros(small_out.shape, F32)
    for place in range(3):
        for m, part in enumerate(kept + got):
            stacked[m * SEQ : (m + 1) * SEQ, :] = part[place * SEQ : (place + 1) * SEQ, :]
        tall[place] = dot(normed[...], stacked[...]).astype(BF16)
        if place != 1:
            small = jnp.where(spot == 36 + place // 2, row_sum(stacked[...].astype(F32)), small)
    small_out[...] = small

    def block_at(dest, z, place):
        return tall[place, pl.ds(pl.multiple_of((dest * OUTER + z) * unit, 16), unit), :]

    deal(unit, outs, block_at)


def add(first, second):
    return (first.astype(F32) + second.astype(F32)).astype(BF16)


def plane_sum_kernel(first, first_got, second, second_got, *refs):
    late, (first_kept, first_sent, second_kept, second_sent) = refs[:-4], refs[-4:]
    pair = second_kept.shape[0]
    total = add(first[...], first_got[...])
    first_kept[:pair, :] = total[:pair]
    first_sent[:pair, :] = total[pair : 2 * pair]
    if late:
        small = (late[0][...] + late[1][...].astype(F32) + late[2][...]).astype(BF16)
    else:
        small = total[2 * pair :]
    first_kept[pair:, :] = small
    first_sent[pair:, :] = small
    total = add(second[...], second_got[...])
    second_kept[...] = total[:pair]
    second_sent[...] = total[pair:]


def line_cut_kernel(first, first_got, second, second_got, own, near, middle, far):
    chunk = own.shape[0]
    total = add(first[...], first_got[...])
    own[...] = total[:chunk]
    near[...] = total[chunk:]
    total = add(second[...], second_got[...])
    middle[...] = total[:chunk]
    far[...] = total[chunk:]


def line_sum_kernel(own, near, near_got, middle_got, far_got, out, out_small):
    chunk = own.shape[0]
    total = own[...].astype(F32) + near_got[:chunk, :].astype(F32)
    total = total + middle_got[...].astype(F32) + far_got[...].astype(F32)
    out[...] = total.astype(BF16)
    out_small[:chunk, :] = total.astype(BF16)
    out_small[chunk:, :] = add(near[chunk:, :], near_got[chunk:, :])


def line_join_kernel(own, near, middle, far, line_x, line_y, small_out):
    chunk = near.shape[0]
    small = own[chunk:, :].astype(F32) + middle[chunk:, :].astype(F32)
    small_out[...] = small
    for out in (line_x, line_y):
        for turn, part in enumerate((own, near, middle, far)):
            out[turn * chunk : (turn + 1) * chunk, :] = part[:chunk, :]
    line_x[OUTER * chunk :, :] = small.astype(BF16)


def place_kernel(split_second, *refs):
    outs, parts = refs[-3:], refs[:-3]
    own = parts[0]
    _, inner, outer = places()
    unit = own.shape[0] // (3 * OUTER)
    width = own.shape[1]
    for step in range(INNER):
        for turn in range(OUTER):
            ref, start = parts[step], turn * 3 * unit
            if step == 3 and turn >= 2:
                ref, start = parts[4], (turn - 2) * 3 * unit
            dest, z = inner ^ step, outer ^ turn
            tall = pl.ds(pl.multiple_of((dest * OUTER + z) * unit, 16), unit)
            flat = pl.ds(pl.multiple_of((dest * (OUTER // 2) + z // 2) * unit, 16), unit)
            columns = pl.ds(pl.multiple_of(z % 2 * width, LANES), width)
            for place in range(3):
                part = ref[start + place * unit : start + (place + 1) * unit, :].astype(F32)
                if split_second and place > 0:
                    outs[place][flat, columns] = part
                else:
                    outs[place][tall, :] = part


def finish_first_kernel(small, got, bias_out, gain, shift, bias_down, bias_up):
    core = places()[0]
    for place, ref in enumerate((bias_out, gain, shift, bias_down)):
        mine, other = small[place : place + 1, :], got[place : place + 1, :]
        left = jnp.where(core == 0, mine, other)
        put_row(ref, jnp.concatenate([left, jnp.where(core == 0, other, mine)], axis=1))
    put_row(bias_up, small[4:5, :])


def finish_second_kernel(small, extra, got, w_ident, types, gain, shift, bias_q, bias_v):
    idw = w_ident.shape[0]
    core = places()[0]
    mine, other = small[...] + extra[...].astype(F32), got[...]
    left = jnp.where(core == 0, mine, other)
    total = jnp.concatenate([left, jnp.where(core == 0, other, mine)], axis=1)
    w_ident[...] = total[:idw]
    types[...] = total[idw : idw + 2]
    put_row(gain, total[idw + 2 : idw + 3])
    put_row(shift, total[idw + 3 : idw + 4])
    put_row(bias_q, mine[idw + 4 : idw + 5])
    put_row(bias_v, mine[idw + 5 : idw + 6])


def per_device(
    features, lap_vectors, node_counts, edge_counts, endpoints, w_ident, type_table,
    gain_one, shift_one, w_query, w_key, w_value, bias_query, bias_value, w_out, bias_out,
    gain_two, shift_two, w_up, bias_up, w_down, bias_down, cotangent,
):
    dp_count = lax.axis_size("dp")
    dp_index = lax.axis_index("dp")
    mp_index = lax.axis_index("mp")
    block = INNER * OUTER
    rest_count = dp_count // block
    def swap(part):
        return lax.ppermute(part, "mp", [(0, 1), (1, 0)])

    def inner_move(part, step):
        return lax.ppermute(part, "dp", [(s, s ^ step) for s in range(dp_count)])

    def outer_move(part, step):
        return lax.ppermute(part, "dp", [(s, s ^ (step * INNER)) for s in range(dp_count)])

    rows_all, dim = features.shape
    rows = rows_all // 2
    mols = rows // SEQ
    width = w_query.shape[1]
    heads = width // HDIM
    lapk = lap_vectors.shape[1]
    idw = w_ident.shape[0]

    def pinned(part):
        return pltpu.with_memory_space_constraint(part, pltpu.HBM)

    def lanes(part):
        return pinned(part.reshape(-1, LANES))

    nodes, edges = pinned(node_counts), pinned(edge_counts)
    count_scratch = pltpu.SMEM(node_counts.shape, jnp.int32)
    wide_scratch = pltpu.VMEM((dim // LANES, LANES), BF16)
    half_scratch = pltpu.VMEM((width // LANES, LANES), BF16)
    embed_args = (
        pinned(features), pinned(lap_vectors.T), pinned(endpoints.T), nodes,
        pinned(w_ident), pinned(type_table), lanes(gain_one), lanes(shift_one),
    )
    embed_scratch = [
        pltpu.VMEM((rows, dim), BF16),
        pltpu.VMEM((lapk, rows), BF16),
        pltpu.VMEM((2, rows), jnp.int32),
        count_scratch,
        pltpu.VMEM((idw, dim), BF16),
        pltpu.VMEM((2, dim), BF16),
        wide_scratch,
        wide_scratch,
    ]

    wq_got, wk_got, wv_got = swap(w_query), swap(w_key), swap(w_value)
    bq_got, bv_got, bu_got = swap(bias_query), swap(bias_value), swap(bias_up)
    wo_got, wu_got, wd_got = swap(w_out), swap(w_up), swap(w_down)

    hidden, ident, normed, normed_t, q_own, k_own, v_own = call(
        embed_kernel,
        (
            *embed_args, lanes(bias_query), lanes(bias_value),
            pinned(w_query), pinned(w_key), pinned(w_value),
        ),
        [outside()] * 13,
        [
            ((rows, dim), F32),
            ((idw, rows), BF16),
            ((rows, dim), BF16),
            ((dim, rows), BF16),
            ((rows, width), BF16),
            ((rows, width), BF16),
            ((rows, width), BF16),
        ],
        scratch=embed_scratch
        + [half_scratch] * 2
        + [pltpu.VMEM((dim, width), BF16)] * 3
        + [pltpu.SemaphoreType.DMA((13,))],
    )
    sent_rows = dim + 2 * width + 3 * rows + 16
    (
        q_got, k_got, v_got, probs, kept_a, sent_a, middle, active, grad_middle, grad_branch,
    ) = call(
        forward_kernel,
        (
            hidden, normed, q_own, k_own, v_own, wq_got, wk_got, wv_got,
            w_out, wo_got, w_up, wu_got, w_down, wd_got,
            *(part.reshape(-1, LANES) for part in (bq_got, bv_got, bu_got)),
            nodes, edges, pinned(cotangent),
            lanes(bias_up), lanes(bias_out), lanes(gain_two), lanes(shift_two),
        ),
        [whole()] * 17 + [outside()] * 7,
        [
            ((rows, width), BF16),
            ((rows, width), BF16),
            ((rows, width), BF16),
            ((mols, heads, SEQ, 2 * SEQ), BF16),
            ((sent_rows, width), BF16),
            ((sent_rows, width), BF16),
            ((rows, dim), F32),
            ((rows, dim), BF16),
            ((rows, dim), F32),
            ((rows, dim), BF16),
        ],
        scratch=[
            count_scratch,
            count_scratch,
            pltpu.VMEM((rows, dim), BF16),
            half_scratch,
            wide_scratch,
            wide_scratch,
            wide_scratch,
            pltpu.SemaphoreType.DMA((7,)),
            pltpu.VMEM((2, width, SEQ), F32),
            pltpu.VMEM((rows, dim), BF16),
            pltpu.VMEM((rows, dim), F32),
            pltpu.VMEM((rows, dim), BF16),
            pltpu.VMEM((rows, dim), F32),
            pltpu.VMEM((rows, dim), BF16),
        ],
        limit=30,
    )
    got_a = swap(sent_a)
    ga_own, ga_got = call(
        branch_kernel,
        (grad_branch, w_out, wo_got, nodes, edges),
        [whole()] * 3 + [outside()] * 2,
        [((rows, width), BF16), ((rows, width), BF16)],
        scratch=[count_scratch, count_scratch, pltpu.SemaphoreType.DMA((2,))],
    )

    unit = dim // block
    chunk = 3 * unit
    small_a, small_b = 16, 48

    def rest_sum(part):
        if rest_count == 1:
            return part
        groups = [[r * block + s for r in range(rest_count)] for s in range(block)]
        return lax.psum(part.astype(F32), "dp", axis_index_groups=groups).astype(part.dtype)

    pair = 2 * chunk

    def after(part, *others):
        return lax.optimization_barrier((part, *others))[0]

    def plane_step(parts, small_rows, late=(), others=(), micros=0):
        first, first_sent, second, second_sent = parts
        first_got = after(inner_move(first_sent, 1), *others)
        second_got = after(inner_move(second_sent, 2), *others)
        return call(
            plane_sum_kernel,
            (first, first_got, second, second_got, *late),
            [whole()] * (4 + len(late)),
            [((pair + small_rows, width), BF16)] * 2 + [((pair, width), BF16)] * 2,
            micros=micros,
        )

    def plane_turn(parts, others=(), micros=0):
        first, first_sent, second, second_sent = parts
        first_got = after(inner_move(first_sent, 2), *others)
        second_got = after(inner_move(second_sent, 1), *others)
        return call(
            line_cut_kernel,
            (first, first_got, second, second_got),
            [whole()] * 4,
            [
                ((chunk, width), BF16),
                ((first.shape[0] - chunk, width), BF16),
                ((chunk, width), BF16),
                ((chunk, width), BF16),
            ],
            micros=micros,
        )

    def line_step(parts, others=(), micros=0):
        got = [after(outer_move(parts[turn], turn), *others) for turn in range(1, OUTER)]
        mine, both = call(
            line_sum_kernel,
            (parts[0], parts[1], *got),
            [whole()] * 5,
            [((chunk, width), BF16), (parts[1].shape, BF16)],
            micros=micros,
        )
        if rest_count > 1:
            both = rest_sum(both)
            mine = both[:chunk]
        return mine, both

    def line_back(mine, both, others=(), micros=0):
        sent = (mine, both, mine)
        got = [after(outer_move(sent[turn - 1], turn), *others) for turn in range(1, OUTER)]
        small_rows = both.shape[0] - chunk
        return call(
            line_join_kernel,
            (both, *got),
            [whole()] * OUTER,
            [
                ((OUTER * chunk + small_rows, width), BF16),
                ((OUTER * chunk, width), BF16),
                ((small_rows, width), F32),
            ],
            micros=micros,
        )

    def plane_back(lines):
        return inner_move(lines[0], 1), inner_move(lines[1], 2)

    def plane_back_turn(side_x, side_y):
        return inner_move(side_y[:pair], 1), inner_move(side_x[pair : 2 * pair], 2)

    def placed(planes, split_second, micros=0):
        tall, flat = ((dim, width), F32), ((width, dim), F32)
        return call(
            lambda *refs: place_kernel(split_second, *refs),
            planes,
            [whole()] * len(planes),
            [tall, flat, flat] if split_second else [tall] * 3,
            micros=micros,
        )

    def attend_back(m, query_rows):
        return call(
            lambda *refs: attend_back_kernel(m, *refs),
            (query_rows, k_own, v_own, ga_own, q_got, k_got, v_got, ga_got, probs),
            [whole()] * 9,
            [((3 * SEQ, width), BF16)] * 2,
            scratch=[
                pltpu.VMEM((2, width, SEQ), F32),
                pltpu.VMEM((2, SEQ, width), F32),
                pltpu.VMEM((2, SEQ, width), F32),
                pltpu.VMEM((2, heads // 2, SEQ, 2 * SEQ), BF16),
            ],
        )

    backs = [attend_back(0, q_own)]
    kept_a = after(kept_a, backs[0][0])
    parts_a = call(
        ffn_grads_kernel,
        (kept_a, got_a, pinned(cotangent), nodes, edges),
        [whole()] * 2 + [outside()] * 3,
        [((INNER * chunk + small_a, width), BF16)] * 2 + [((INNER * chunk, width), BF16)] * 2,
        scratch=[
            pltpu.VMEM((rows_all, dim), BF16),
            count_scratch,
            count_scratch,
            pltpu.SemaphoreType.DMA((3,)),
            pltpu.VMEM((dim, width), BF16),
            pltpu.VMEM((4, width, width), BF16),
            pltpu.VMEM((rows_all, dim), BF16),
        ],
    )
    normed_t_got = swap(after(normed_t, parts_a[0]))
    for m in range(1, mols):
        gates = (parts_a[0], backs[-1][0]) + ((normed_t_got,) if m == mols - 1 else ())
        backs.append(attend_back(m, after(q_own, *gates)))
    kept_b = [back[0] for back in backs]
    sent_b = [back[1] for back in backs]
    got_b = [swap(sent) for sent in sent_b]
    parts_b = call(
        qkv_grads_kernel,
        (normed_t, normed_t_got, *kept_b, *got_b),
        [whole()] * (2 + 2 * mols),
        [((INNER * chunk, width), BF16)] * 4 + [((small_b, width), F32)],
        scratch=[
            pltpu.VMEM((3, dim, width), BF16),
            pltpu.VMEM((dim, 2 * rows), BF16),
            pltpu.VMEM((2 * rows, width), BF16),
        ],
    )
    steps_a = plane_step(parts_a, small_a, others=(parts_b[0],), micros=0)
    grad_middle = after(grad_middle, parts_b[0], *steps_a)
    grad_features, small_kept, small_sent = call(
        embed_back_kernel,
        (
            *kept_b, *sent_b, w_query, w_key, w_value, wq_got, wk_got, wv_got, ident,
            grad_middle, embed_args[0], nodes, *embed_args[4:7],
        ),
        [whole()] * (8 + 2 * mols) + [outside()] * 5,
        [((rows, dim), F32), ((small_b, width), F32), ((small_b, width), BF16)],
        scratch=[
            pltpu.VMEM((rows, dim), BF16),
            count_scratch,
            pltpu.VMEM((idw, dim), BF16),
            pltpu.VMEM((2, dim), BF16),
            wide_scratch,
            pltpu.SemaphoreType.DMA((5,)),
            pltpu.VMEM((rows, dim), F32),
            pltpu.VMEM((small_b, dim), F32),
            pltpu.VMEM((rows, width), BF16),
        ],
        micros=0,
    )
    small_got = swap(small_sent)
    turned_a = plane_turn(steps_a, others=(small_kept,), micros=3)
    steps_b = plane_step(parts_b[:4], small_b, late=(small_kept, small_got, parts_b[4]))
    line_a = line_step(turned_a, others=steps_b, micros=3)
    turned_b = plane_turn(steps_b, others=line_a[:1])
    lines_a = line_back(*line_a, others=turned_b, micros=3)
    line_b = line_step(turned_b, micros=12)
    sides_a = plane_back((lines_a[1], lines_a[1]))
    far_a = plane_back_turn(*sides_a)
    planes_a = (lines_a[1], *sides_a, *far_a)
    lines_b = line_back(*line_b, micros=2)
    result = call(
        result_kernel,
        (middle, active, w_down, wd_got, lanes(after(bias_down, lines_b[1]))),
        [whole()] * 5,
        [((rows, dim), BF16)],
    )[0]
    wide, half = ((dim // LANES, LANES), F32), ((width // LANES, LANES), F32)
    sums_a = call(
        finish_first_kernel,
        (lines_a[2], swap(after(lines_a[2], lines_b[1]))),
        [whole()] * 2,
        [wide] * 4 + [half],
    )
    grad_w_up, grad_w_out, grad_w_down = placed(planes_a, True, micros=10)
    sides_b = plane_back(lines_b)
    sides_b, _ = lax.optimization_barrier((sides_b, (result, sums_a, grad_w_up)))
    far_b = plane_back_turn(*sides_b)
    planes_b = (lines_b[1], sides_b[0], sides_b[1], *far_b)
    extra = sides_b[0][OUTER * chunk :]
    own_b = lines_b[2] + extra.astype(F32)
    sums_b = call(
        finish_second_kernel,
        (lines_b[2], extra, swap(own_b)),
        [whole()] * 3,
        [((idw, dim), F32), ((2, dim), F32), wide, wide, half, half],
    )
    grad_w_query, grad_w_key, grad_w_value = placed(planes_b, False)
    return (
        result,
        grad_features,
        sums_b[0],
        sums_b[1],
        sums_b[2].reshape(-1),
        sums_b[3].reshape(-1),
        grad_w_query,
        grad_w_key,
        grad_w_value,
        sums_b[4].reshape(-1),
        sums_b[5].reshape(-1),
        grad_w_out,
        sums_a[0].reshape(-1),
        sums_a[1].reshape(-1),
        sums_a[2].reshape(-1),
        grad_w_up,
        sums_a[4].reshape(-1),
        grad_w_down,
        sums_a[3].reshape(-1),
    )


def solution(mesh):
    token, split = P("dp", None), P(("dp", "mp"), None)
    columns, lines, cut, copy = P(None, "mp"), P("mp", None), P("mp"), P()
    return jax.shard_map(
        per_device,
        mesh=mesh,
        in_specs=(
            token, token, P("dp"), P("dp"), token, copy, copy, copy, copy, columns, columns,
            columns, cut, cut, lines, copy, copy, copy, columns, cut, lines, copy, token,
        ),
        out_specs=(
            split, split, copy, copy, copy, copy, columns, columns, columns, cut, cut, lines,
            copy, copy, copy, columns, cut, lines, copy,
        ),
        check_vma=False,
    )
```

```python
import math

import jax
import jax.numpy as jnp
from jax import lax
from jax.experimental import pallas as pl
from jax.experimental.pallas import tpu as pltpu
from jax.sharding import PartitionSpec as P

HDIM = 24
SEQ = 128
LANES = 128
INNER = 4
OUTER = 4
EPSILON = 1e-05
SCALE = 1.0 / math.sqrt(HDIM)
LOG2_SCALE = SCALE * math.log2(math.e)
F32, BF16 = jnp.float32, jnp.bfloat16
MIB = 1024 * 1024


def dot(left, right):
    return jnp.dot(left, right, preferred_element_type=F32)


def dot_nt(left, right):
    return lax.dot_general(left, right, (((1,), (1,)), ((), ())), preferred_element_type=F32)


def dot_tn(left, right):
    return lax.dot_general(left, right, (((0,), (0,)), ((), ())), preferred_element_type=F32)


def norm_parts(hidden):
    average = jnp.mean(hidden, axis=-1, keepdims=True)
    centred = hidden - average
    inverse = lax.rsqrt(jnp.mean(centred * centred, axis=-1, keepdims=True) + EPSILON)
    return centred * inverse, inverse


def norm_back(unit, inverse, grad_hat):
    return inverse * (
        grad_hat
        - jnp.mean(grad_hat, axis=-1, keepdims=True)
        - unit * jnp.mean(grad_hat * unit, axis=-1, keepdims=True)
    )


def row_sum(block):
    return jnp.sum(block, axis=0, keepdims=True)


def positions(length):
    return lax.broadcasted_iota(jnp.int32, (length, 1), 0)


def whole():
    return pl.BlockSpec(memory_space=pltpu.VMEM)


def outside():
    return pl.BlockSpec(memory_space=pltpu.HBM)


def places():
    index = lax.axis_index("dp")
    return lax.axis_index("mp"), index % INNER, index // INNER % OUTER


def copy_in(sources, targets, sems):
    copies = [
        pltpu.make_async_copy(source, target, sems.at[place])
        for place, (source, target) in enumerate(zip(sources, targets))
    ]
    for copy in copies:
        copy.start()
    return copies


def row_of(ref):
    block = ref[...].astype(F32)
    return jnp.concatenate([block[r : r + 1, :] for r in range(block.shape[0])], axis=1)


def put_row(ref, row):
    for r in range(ref.shape[0]):
        ref[r : r + 1, :] = row[:, r * LANES : (r + 1) * LANES]


def call(kernel, args, specs, outs, scratch=(), micros=0, limit=24):
    return pl.pallas_call(
        kernel,
        out_shape=[jax.ShapeDtypeStruct(shape, kind) for shape, kind in outs],
        in_specs=specs,
        out_specs=[whole() for _ in outs],
        scratch_shapes=list(scratch),
        compiler_params=pltpu.CompilerParams(vmem_limit_bytes=limit * MIB),
        cost_estimate=pl.CostEstimate(
            flops=micros * 1_000_000_000, bytes_accessed=0, transcendentals=0
        ),
    )(*args)


def head_windows(width):
    windows = []
    for pair in range(width // (2 * HDIM)):
        low = pair * 2 * HDIM // LANES * LANES
        high = -(-(pair + 1) * 2 * HDIM // LANES) * LANES
        windows.append((low, high))
    return windows


def split_heads(block, pair, window):
    low, high = window
    part = block[:, low:high]
    column = low + lax.broadcasted_iota(jnp.int32, (16, high - low), 1)
    sides = []
    for head in (2 * pair, 2 * pair + 1):
        inside = (column >= head * HDIM) & (column < (head + 1) * HDIM)
        mask = jnp.where(inside, 1.0, 0.0).astype(BF16)
        sides.append(part * jnp.concatenate([mask] * (block.shape[0] // 16), axis=0))
    return jnp.concatenate(sides, axis=0)


def embed_rows(feats, lap, ends, w_ident, types, gain, shift, at, count):
    table = lap[:, at]
    slot = lax.broadcasted_iota(jnp.int32, (SEQ, SEQ), 0)
    picked = []
    for end in (0, 1):
        pick = jnp.where(ends[end : end + 1, at] == slot, 1.0, 0.0).astype(BF16)
        picked.append(dot(table, pick))
    ident = jnp.concatenate(picked, axis=0).astype(BF16)
    hidden = feats[at, :].astype(F32) + dot_tn(ident, w_ident[...])
    kinds = types[...].astype(F32)
    hidden = hidden + jnp.where(positions(SEQ) >= count, kinds[1:2, :], kinds[0:1, :])
    unit, _ = norm_parts(hidden)
    return hidden, ident, (unit * gain + shift).astype(BF16)


def embed_kernel(
    feats_in, lap_in, ends_in, nodes_in, w_ident_in, types_in, gain_in, shift_in,
    bias_q_in, bias_v_in, wq_in, wk_in, wv_in,
    hidden_out, ident_out, normed_out, normed_t_out, q_out, k_out, v_out,
    feats, lap, ends, nodes, w_ident, types, gain_rows, shift_rows, bias_q, bias_v,
    w_q, w_k, w_v, sems,
):
    rows, dim = feats.shape
    mols = rows // SEQ
    core = places()[0]
    own_rows = pl.ds(pl.multiple_of(core * rows, SEQ), rows)
    copies = copy_in(
        (
            feats_in.at[own_rows, :], lap_in.at[:, own_rows], ends_in.at[:, own_rows], nodes_in,
            w_ident_in, types_in, gain_in, shift_in, bias_q_in, bias_v_in, wq_in, wk_in, wv_in,
        ),
        (
            feats, lap, ends, nodes, w_ident, types, gain_rows, shift_rows, bias_q, bias_v,
            w_q, w_k, w_v,
        ),
        sems,
    )
    for copy in copies[:10]:
        copy.wait()
    gain, shift = row_of(gain_rows), row_of(shift_rows)

    def molecule(m):
        at = slice(m * SEQ, (m + 1) * SEQ)
        count = nodes[core * mols + m]
        hidden, ident, normed = embed_rows(
            feats, lap, ends, w_ident, types, gain, shift, at, count
        )
        ident_out[:, at] = ident
        hidden_out[at, :] = hidden
        normed_out[at, :] = normed
        normed_t_out[:, at] = normed.T

    for m in range(mols):
        molecule(m)
    normed = normed_out[...]
    copies[10].wait()
    q_out[...] = (dot(normed, w_q[...]) + row_of(bias_q)).astype(BF16)
    copies[11].wait()
    k_out[...] = dot(normed, w_k[...]).astype(BF16)
    copies[12].wait()
    v_out[...] = (dot(normed, w_v[...]) + row_of(bias_v)).astype(BF16)


def forward_kernel(
    hidden, normed, q_own, k_own, v_own, w_q, w_k, w_v, wo_own, wo, wu_own, wu,
    bias_q, bias_v, bias_u,
    nodes_in, edges_in, bias_u_own_in, bias_o_in, gain_in, shift_in,
    q_out, k_out, v_out, probs_out, keep_out, send_out, middle, active, slope,
    nodes, edges, bias_u_own, bias_o, gain_rows, shift_rows, sems,
    mixed, attended, normed_two,
):
    rows, dim = hidden.shape
    width = q_own.shape[1]
    mols = rows // SEQ
    pairs = width // (2 * HDIM)
    windows = head_windows(width)
    core = places()[0]
    copies = copy_in(
        (nodes_in, edges_in, bias_u_own_in, bias_o_in, gain_in, shift_in),
        (nodes, edges, bias_u_own, bias_o, gain_rows, shift_rows),
        sems,
    )

    q_out[...] = (dot(normed[...], w_q[...]) + row_of(bias_q)).astype(BF16)
    k_out[...] = dot(normed[...], w_k[...]).astype(BF16)
    v_out[...] = (dot(normed[...], w_v[...]) + row_of(bias_v)).astype(BF16)

    for copy in copies:
        copy.wait()
    gain, shift, bias_out = row_of(gain_rows), row_of(shift_rows), row_of(bias_o)

    sides = ((q_own, k_own, v_own, keep_out), (q_out, k_out, v_out, send_out))
    units = [(m, side) for m in range(mols) for side in (0, 1)]

    def weigh(unit, pair):
        m, side = unit
        at = slice(m * SEQ, (m + 1) * SEQ)
        place = core * mols + m
        key_keep = positions(SEQ) < nodes[place] + edges[place]
        low, high = windows[pair]
        both = split_heads(sides[side][0][at, :], pair, windows[pair])
        scores = dot_nt(sides[side][1][at, low:high], both)
        scores = jnp.where(key_keep, scores, -1e30)
        top = jnp.max(scores, axis=0, keepdims=True)
        raised = jnp.exp2((scores - top) * LOG2_SCALE)
        probs_out[m, side * pairs + pair] = (raised * (1.0 / row_sum(raised))).astype(BF16)

    def mix(unit, pair, values_t):
        m, side = unit
        first = pair * 2 * HDIM
        out = dot(values_t[first : first + 2 * HDIM], probs_out[m, side * pairs + pair])
        mixed[side, first : first + HDIM, :] = out[:HDIM, :SEQ]
        mixed[side, first + HDIM : first + 2 * HDIM, :] = out[HDIM:, SEQ:]

    def keep_mixed(unit):
        m, side = unit
        at = slice(m * SEQ, (m + 1) * SEQ)
        place = core * mols + m
        query_keep = lax.broadcasted_iota(jnp.int32, (1, SEQ), 1) < nodes[place] + edges[place]
        kept = jnp.where(query_keep, mixed[side], 0.0).astype(BF16)
        sides[side][3][dim : dim + width, at] = kept
        attended[at, side * width : (side + 1) * width] = kept.T

    for pair in range(pairs):
        weigh(units[0], pair)
    for step, task in enumerate(units):
        values_t = sides[task[1]][2][task[0] * SEQ : (task[0] + 1) * SEQ, :].T
        for pair in range(pairs):
            mix(task, pair, values_t)
            if step + 1 < len(units):
                weigh(units[step + 1], pair)
        keep_mixed(task)
    middle[...] = (
        hidden[...] + dot(attended[:, :width], wo_own[...]) + dot(attended[:, width:], wo[...])
    )

    for m in range(mols):
        at = slice(m * SEQ, (m + 1) * SEQ)
        total = middle[at, :] + bias_out
        middle[at, :] = total
        unit_rows, _ = norm_parts(total)
        rows_two = (unit_rows * gain + shift).astype(BF16)
        normed_two[at, :] = rows_two
        turned = rows_two.T
        keep_out[:dim, at] = turned
        send_out[:dim, at] = turned

    for side, (w_ref, b_ref, part_out) in enumerate(
        ((wu_own, bias_u_own, keep_out), (wu, bias_u, send_out))
    ):
        columns = slice(side * width, (side + 1) * width)
        slope[:, columns] = dot(normed_two[...], w_ref[...]) + row_of(b_ref)

        for m in range(mols):
            at = slice(m * SEQ, (m + 1) * SEQ)
            before = slope[at, columns]
            phi = 0.5 * (1.0 + lax.erf(before * math.sqrt(0.5)))
            out = (before * phi).astype(BF16)
            slope[at, columns] = phi + before * jnp.exp(before * before * -0.5) * (
                1.0 / math.sqrt(2.0 * math.pi)
            )
            active[at, columns] = out
            part_out[dim + width : dim + 2 * width, at] = out.T


def ffn_back_kernel(
    middle, slope, wu_own, wu, wd_own, wd, nodes_in, edges_in, cots_in, gain_in,
    keep_out, send_out, gm_out, grad_branch,
    nodes, edges, cots, gain_rows, sems, grad_ffn,
):
    rows, dim = middle.shape
    width = wd.shape[0]
    mols = rows // SEQ
    core = places()[0]
    own_rows = pl.ds(pl.multiple_of(core * rows, SEQ), rows)
    copies = copy_in(
        (nodes_in, edges_in, cots_in.at[own_rows, :], gain_in),
        (nodes, edges, cots, gain_rows),
        sems,
    )
    for copy in copies:
        copy.wait()
    gain = row_of(gain_rows)
    for m in range(mols):
        at = slice(m * SEQ, (m + 1) * SEQ)
        place = core * mols + m
        keep = positions(SEQ) < nodes[place] + edges[place]
        grad_ffn[at, :] = jnp.where(keep, cots[at, :].astype(F32), 0.0).astype(BF16)
    place_b = 0
    for side, (w_ref, part_out) in enumerate(((wd_own, keep_out), (wd, send_out))):
        columns = slice(side * width, (side + 1) * width)
        grad_before = slope[:, columns] * dot_nt(grad_ffn[...], w_ref[...])
        part_out[place_b : place_b + rows, :] = grad_before.astype(BF16)

    back = pl.ds(place_b, rows)
    gm_out[...] = dot_nt(keep_out[back, :], wu_own[...]) + dot_nt(send_out[back, :], wu[...])

    nothing = jnp.zeros((1, dim), F32)
    sums = (nothing,) * 4
    for m in range(mols):
        at = slice(m * SEQ, (m + 1) * SEQ)
        place = core * mols + m
        keep = positions(SEQ) < nodes[place] + edges[place]
        grad_normed = gm_out[at, :]
        unit_rows, inverse = norm_parts(middle[at, :])
        grad_result = jnp.where(keep, cots[at, :].astype(F32), 0.0)
        grad = grad_result + norm_back(unit_rows, inverse, grad_normed * gain)
        gm_out[at, :] = grad
        grad_branch[at, :] = grad.astype(BF16)
        sums = (
            sums[0] + row_sum(grad),
            sums[1] + row_sum(grad_normed * unit_rows),
            sums[2] + row_sum(grad_normed),
            sums[3] + row_sum(grad_result),
        )

    place_m = place_b + rows
    for part_out in (keep_out, send_out):
        part_out[place_m : place_m + rows, :] = grad_branch[:, :width]
        part_out[place_m + rows : place_m + 2 * rows, :] = grad_branch[:, width:]
    small = jnp.concatenate(list(sums) + [nothing] * 12, axis=0)
    left, right = small[:, :width], small[:, width:]
    place_s = place_m + 2 * rows
    keep_out[place_s:, :] = jnp.where(core == 0, left, right).astype(BF16)
    send_out[place_s:, :] = jnp.where(core == 0, right, left).astype(BF16)


def result_kernel(middle, active, wd_own, wd, bias, result_out):
    width = wd.shape[0]
    result_out[...] = (
        middle[...]
        + dot(active[:, :width], wd_own[...])
        + dot(active[:, width:], wd[...])
        + row_of(bias)
    ).astype(BF16)


def branch_kernel(
    grad_branch, wo_own, wo, nodes_in, edges_in, ga_own_out, ga_out, nodes, edges, sems
):
    mols = grad_branch.shape[0] // SEQ
    core = places()[0]
    copies = copy_in((nodes_in, edges_in), (nodes, edges), sems)
    products = [dot_nt(grad_branch[...], weight[...]) for weight in (wo_own, wo)]
    for copy in copies:
        copy.wait()
    for ref, product in zip((ga_own_out, ga_out), products):
        for m in range(mols):
            place = core * mols + m
            keep = positions(SEQ) < nodes[place] + edges[place]
            at = slice(m * SEQ, (m + 1) * SEQ)
            ref[at, :] = jnp.where(keep, product[at], 0.0).astype(BF16)


def attend_back_kernel(
    q_own, k_own, v_own, ga_own, q_got, k_got, v_got, ga_got, probs_all,
    keep_out, send_out, dq_t, dk, dv, slopes,
):
    rows, width = q_own.shape
    pairs = width // (2 * HDIM)
    windows = head_windows(width)
    sides = (
        (q_own, k_own, v_own, ga_own, keep_out),
        (q_got, k_got, v_got, ga_got, send_out),
    )
    units = [(m, side) for m in range(rows // SEQ) for side in (0, 1)]

    def score_back(unit, pair):
        m, side = unit
        at = slice(m * SEQ, (m + 1) * SEQ)
        low, high = windows[pair]
        both_g = split_heads(sides[side][3][at, :], pair, windows[pair])
        probs_low = probs_all[m, side * pairs + pair]
        probs = probs_low.astype(F32)
        grad_probs = dot_nt(sides[side][2][at, low:high], both_g)
        inner = row_sum(probs * grad_probs)
        slopes[side, pair] = (probs * (grad_probs - inner)).astype(BF16)
        dv[side, :, low:high] += dot(probs_low, both_g)

    def rows_back(unit, pair, keys_t):
        m, side = unit
        low, high = windows[pair]
        grad_scores = slopes[side, pair]
        both_q = split_heads(sides[side][0][m * SEQ : (m + 1) * SEQ, :], pair, windows[pair])
        dk[side, :, low:high] += dot(grad_scores, both_q)
        first = pair * 2 * HDIM
        out = dot(keys_t[first : first + 2 * HDIM], grad_scores)
        dq_t[side, first : first + HDIM, :] = out[:HDIM, :SEQ]
        dq_t[side, first + HDIM : first + 2 * HDIM, :] = out[HDIM:, SEQ:]

    def begin(unit):
        dk[unit[1]] = jnp.zeros_like(dk[unit[1]])
        dv[unit[1]] = jnp.zeros_like(dv[unit[1]])

    def finish(unit):
        m, side = unit
        part_out = sides[side][4]
        base = m * SEQ
        part_out[base : base + SEQ, :] = (dq_t[side] * SCALE).astype(BF16).T
        part_out[rows + base : rows + base + SEQ, :] = (dk[side] * SCALE).astype(BF16)
        part_out[2 * rows + base : 2 * rows + base + SEQ, :] = dv[side].astype(BF16)

    begin(units[0])
    for pair in range(pairs):
        score_back(units[0], pair)
    for step, unit in enumerate(units):
        keys_t = sides[unit[1]][1][unit[0] * SEQ : (unit[0] + 1) * SEQ, :].T
        if step + 1 < len(units):
            begin(units[step + 1])
        for pair in range(pairs):
            rows_back(unit, pair, keys_t)
            if step + 1 < len(units):
                score_back(units[step + 1], pair)
        finish(unit)


def embed_back_kernel(*refs):
    (
        grads_own, grads,
        wq_own, wk_own, wv_own, w_q, w_k, w_v, ident, grad_middle,
        feats_in, nodes_in, w_ident_in, types_in, gain_in,
        features_out, keep_out, send_out,
        feats, nodes, w_ident, types, gain_rows, sems, grad_normed, small,
    ) = refs
    core = places()[0]
    rows = feats.shape[0]
    copies = copy_in(
        (
            feats_in.at[pl.ds(pl.multiple_of(core * rows, SEQ), rows), :], nodes_in,
            w_ident_in, types_in, gain_in,
        ),
        (feats, nodes, w_ident, types, gain_rows),
        sems,
    )
    rows, dim = feats.shape
    width = wq_own.shape[1]
    idw = ident.shape[0]
    total = None
    for part, weights in ((grads_own, (wq_own, wk_own, wv_own)), (grads, (w_q, w_k, w_v))):
        for place, weight in enumerate(weights):
            term = dot_nt(part[place * rows : (place + 1) * rows, :], weight[...])
            total = term if total is None else total + term
    grad_normed[...] = total
    mols = rows // SEQ
    small[...] = jnp.zeros_like(small)
    for copy in copies:
        copy.wait()
    gain = row_of(gain_rows)
    kinds = types[...].astype(F32)

    def molecule(m, carry):
        at = pl.ds(pl.multiple_of(m * SEQ, SEQ), SEQ)
        is_edge = positions(SEQ) >= nodes[core * mols + m]
        hidden = feats[at, :].astype(F32) + dot_tn(ident[:, at], w_ident[...])
        hidden = hidden + jnp.where(is_edge, kinds[1:2, :], kinds[0:1, :])
        unit, inverse = norm_parts(hidden)
        grad_rows = grad_normed[at, :]
        grad = grad_middle[at, :] + norm_back(unit, inverse, grad_rows * gain)
        features_out[at, :] = grad
        high = grad.astype(BF16)
        rest = (grad - high.astype(F32)).astype(BF16)
        picked = ident[:, at]
        small[:idw, :] += dot(picked, high) + dot(picked, rest)
        edge_rows = jnp.where(is_edge, grad, 0.0)
        small[idw : idw + 1, :] += row_sum(grad - edge_rows)
        small[idw + 1 : idw + 2, :] += row_sum(edge_rows)
        small[idw + 2 : idw + 3, :] += row_sum(grad_rows * unit)
        small[idw + 3 : idw + 4, :] += row_sum(grad_rows)
        return carry

    lax.fori_loop(0, mols, molecule, 0)
    left, right = small[:, :width], small[:, width:]
    keep_out[...] = jnp.where(core == 0, left, right)
    send_out[...] = jnp.where(core == 0, right, left).astype(BF16)


def deal(unit, places_in, outs, block_at, small=None):
    _, inner, outer = places()
    first_kept, first_sent, second_kept, second_sent = outs
    for step in range(INNER):
        for turn in range(OUTER):
            if turn < 2:
                out, slot = (first_sent if step % 2 else first_kept), step // 2
            else:
                out, slot = (second_sent if step // 2 else second_kept), step % 2
            start = (slot * 2 + turn % 2) * places_in * unit
            for place in range(places_in):
                out[start + place * unit : start + (place + 1) * unit, :] = block_at(
                    inner ^ step, outer ^ turn, place
                )
    if small is not None:
        for out in (first_kept, first_sent):
            out[INNER * places_in * unit :, :] = small


def flat_block(flat, unit, dest, z):
    row = pl.multiple_of((dest * (OUTER // 2) + z // 2) * unit, 16)
    return flat[z % 2, pl.ds(row, unit), :]


def down_grads_kernel(kept, got, cots_in, nodes_in, edges_in, *rest):
    outs, (cots, nodes, edges, sems, flat, grad_ffn) = rest[:4], rest[4:]
    copies = copy_in((nodes_in, edges_in, cots_in), (nodes, edges, cots), sems)
    for copy in copies:
        copy.wait()
    rows_all, dim = cots.shape
    rows, width = rows_all // 2, kept.shape[1]
    core = places()[0]
    for m in range(rows_all // SEQ):
        keep = positions(SEQ) < nodes[m] + edges[m]
        at = slice(m * SEQ, (m + 1) * SEQ)
        grad_ffn[at, :] = jnp.where(keep, cots[at, :].astype(F32), 0.0).astype(BF16)
    own_rows = pl.ds(pl.multiple_of(core * rows, SEQ), rows)
    other_rows = pl.ds(pl.multiple_of((1 - core) * rows, SEQ), rows)
    turned = slice(dim + width, dim + 2 * width)
    for half in (0, 1):
        columns = slice(half * width, (half + 1) * width)
        product = dot(kept[turned, :], grad_ffn[own_rows, columns])
        product = product + dot(got[turned, :], grad_ffn[other_rows, columns])
        flat[half] = product.astype(BF16)
    unit = dim // (INNER * OUTER)
    deal(unit, 1, outs, lambda dest, z, place: flat_block(flat, unit, dest, z))


def ffn_grads_kernel(kept, got, kept_back, got_back, *rest):
    outs, (tall, flat) = rest[:4], rest[4:]
    rows, width = kept.shape[1], kept.shape[1]
    dim = kept.shape[0] - 2 * width
    back, place_s = slice(0, rows), 3 * rows
    tall[...] = (
        dot(kept[:dim, :], kept_back[back, :]) + dot(got[:dim, :], got_back[back, :])
    ).astype(BF16)
    turned = slice(dim, dim + width)
    for half in (0, 1):
        mid = slice((1 + half) * rows, (2 + half) * rows)
        flat[half] = (
            dot(kept[turned, :], kept_back[mid, :]) + dot(got[turned, :], got_back[mid, :])
        ).astype(BF16)
    bias = row_sum(kept_back[back, :].astype(F32)) + row_sum(got_back[back, :].astype(F32))
    small = kept_back[place_s:, :].astype(F32) + got_back[place_s:, :].astype(F32)
    spot = lax.broadcasted_iota(jnp.int32, small.shape, 0)
    small = jnp.where(spot == 4, bias, small).astype(BF16)
    unit = dim // (INNER * OUTER)

    def block_at(dest, z, place):
        if place == 0:
            return tall[pl.ds(pl.multiple_of((dest * OUTER + z) * unit, 16), unit), :]
        return flat_block(flat, unit, dest, z)

    deal(unit, 2, outs, block_at, small)


def qkv_grads_kernel(normed_t, normed_t_got, kept, got, *refs):
    outs, small_out, (tall, normed, stacked) = refs[:4], refs[4], refs[5:]
    dim, rows = normed_t.shape
    unit = dim // (INNER * OUTER)
    normed[:, :rows] = normed_t[...]
    normed[:, rows:] = normed_t_got[...]
    spot = lax.broadcasted_iota(jnp.int32, small_out.shape, 0)
    small = jnp.zeros(small_out.shape, F32)
    for place in range(3):
        part = slice(place * rows, (place + 1) * rows)
        stacked[:rows, :] = kept[part, :]
        stacked[rows:, :] = got[part, :]
        tall[place] = dot(normed[...], stacked[...]).astype(BF16)
        if place != 1:
            small = jnp.where(spot == 36 + place // 2, row_sum(stacked[...].astype(F32)), small)
    small_out[...] = small

    def block_at(dest, z, place):
        return tall[place, pl.ds(pl.multiple_of((dest * OUTER + z) * unit, 16), unit), :]

    deal(unit, 3, outs, block_at)


def add(first, second):
    return (first.astype(F32) + second.astype(F32)).astype(BF16)


def plane_sum_kernel(first, first_got, second, second_got, *refs):
    late, (first_kept, first_sent, second_kept, second_sent) = refs[:-4], refs[-4:]
    pair = second_kept.shape[0]
    total = add(first[...], first_got[...])
    first_kept[:pair, :] = total[:pair]
    first_sent[:pair, :] = total[pair : 2 * pair]
    if late:
        small = (late[0][...] + late[1][...].astype(F32) + late[2][...]).astype(BF16)
    else:
        small = total[2 * pair :]
    first_kept[pair:, :] = small
    first_sent[pair:, :] = small
    total = add(second[...], second_got[...])
    second_kept[...] = total[:pair]
    second_sent[...] = total[pair:]


def plane_join_kernel(first, first_got, second, second_got, *refs):
    ahead, outs = refs[:4], refs[4:]
    unit = ahead[0].shape[0] // 4
    small = add(first[8 * unit :, :], first_got[8 * unit :, :])
    for place, (left, right, more, more_got) in enumerate(
        ((first, first_got, *ahead[:2]), (second, second_got, *ahead[2:]))
    ):
        total = add(left[: 8 * unit, :], right[: 8 * unit, :])
        late = add(more[...], more_got[...])
        for block in range(4):
            out = outs[2 * place + block // 2]
            start = block % 2 * 3 * unit
            out[start : start + 2 * unit, :] = total[2 * block * unit : 2 * (block + 1) * unit]
            out[start + 2 * unit : start + 3 * unit, :] = late[block * unit : (block + 1) * unit]
    for out in outs[:2]:
        out[6 * unit :, :] = small


def line_cut_kernel(first, first_got, second, second_got, own, near, middle, far):
    chunk = own.shape[0]
    total = add(first[...], first_got[...])
    own[...] = total[:chunk]
    near[...] = total[chunk:]
    total = add(second[...], second_got[...])
    middle[...] = total[:chunk]
    far[...] = total[chunk:]


def line_sum_kernel(own, near, near_got, middle_got, far_got, out, out_small):
    chunk = own.shape[0]
    total = own[...].astype(F32) + near_got[:chunk, :].astype(F32)
    total = total + middle_got[...].astype(F32) + far_got[...].astype(F32)
    out[...] = total.astype(BF16)
    out_small[:chunk, :] = total.astype(BF16)
    out_small[chunk:, :] = add(near[chunk:, :], near_got[chunk:, :])


def line_join_kernel(own, near, middle, far, line_x, line_y, small_out):
    chunk = near.shape[0]
    small = own[chunk:, :].astype(F32) + middle[chunk:, :].astype(F32)
    small_out[...] = small
    for out in (line_x, line_y):
        for turn, part in enumerate((own, near, middle, far)):
            out[turn * chunk : (turn + 1) * chunk, :] = part[:chunk, :]
    line_x[OUTER * chunk :, :] = small.astype(BF16)


def place_kernel(split_second, *refs):
    outs, parts = refs[-3:], refs[:-3]
    own = parts[0]
    _, inner, outer = places()
    unit = own.shape[0] // (3 * OUTER)
    width = own.shape[1]
    for step in range(INNER):
        for turn in range(OUTER):
            ref, start = parts[step], turn * 3 * unit
            if step == 3 and turn >= 2:
                ref, start = parts[4], (turn - 2) * 3 * unit
            dest, z = inner ^ step, outer ^ turn
            tall = pl.ds(pl.multiple_of((dest * OUTER + z) * unit, 16), unit)
            flat = pl.ds(pl.multiple_of((dest * (OUTER // 2) + z // 2) * unit, 16), unit)
            columns = pl.ds(pl.multiple_of(z % 2 * width, LANES), width)
            for place in range(3):
                part = ref[start + place * unit : start + (place + 1) * unit, :].astype(F32)
                if split_second and place > 0:
                    outs[place][flat, columns] = part
                else:
                    outs[place][tall, :] = part


def finish_first_kernel(small, got, bias_out, gain, shift, bias_down, bias_up):
    core = places()[0]
    for place, ref in enumerate((bias_out, gain, shift, bias_down)):
        mine, other = small[place : place + 1, :], got[place : place + 1, :]
        left = jnp.where(core == 0, mine, other)
        put_row(ref, jnp.concatenate([left, jnp.where(core == 0, other, mine)], axis=1))
    put_row(bias_up, small[4:5, :])


def finish_second_kernel(small, extra, got, w_ident, types, gain, shift, bias_q, bias_v):
    idw = w_ident.shape[0]
    core = places()[0]
    mine, other = small[...] + extra[...].astype(F32), got[...]
    left = jnp.where(core == 0, mine, other)
    total = jnp.concatenate([left, jnp.where(core == 0, other, mine)], axis=1)
    w_ident[...] = total[:idw]
    types[...] = total[idw : idw + 2]
    put_row(gain, total[idw + 2 : idw + 3])
    put_row(shift, total[idw + 3 : idw + 4])
    put_row(bias_q, mine[idw + 4 : idw + 5])
    put_row(bias_v, mine[idw + 5 : idw + 6])


def per_device(
    features, lap_vectors, node_counts, edge_counts, endpoints, w_ident, type_table,
    gain_one, shift_one, w_query, w_key, w_value, bias_query, bias_value, w_out, bias_out,
    gain_two, shift_two, w_up, bias_up, w_down, bias_down, cotangent,
):
    dp_count = lax.axis_size("dp")
    dp_index = lax.axis_index("dp")
    mp_index = lax.axis_index("mp")
    block = INNER * OUTER
    rest_count = dp_count // block
    def swap(part):
        return lax.ppermute(part, "mp", [(0, 1), (1, 0)])

    def inner_move(part, step):
        return lax.ppermute(part, "dp", [(s, s ^ step) for s in range(dp_count)])

    def outer_move(part, step):
        return lax.ppermute(part, "dp", [(s, s ^ (step * INNER)) for s in range(dp_count)])

    rows_all, dim = features.shape
    rows = rows_all // 2
    mols = rows // SEQ
    width = w_query.shape[1]
    heads = width // HDIM
    lapk = lap_vectors.shape[1]
    idw = w_ident.shape[0]

    def pinned(part):
        return pltpu.with_memory_space_constraint(part, pltpu.HBM)

    def lanes(part):
        return pinned(part.reshape(-1, LANES))

    nodes, edges = pinned(node_counts), pinned(edge_counts)
    count_scratch = pltpu.SMEM(node_counts.shape, jnp.int32)
    wide_scratch = pltpu.VMEM((dim // LANES, LANES), BF16)
    half_scratch = pltpu.VMEM((width // LANES, LANES), BF16)
    embed_args = (
        pinned(features), pinned(lap_vectors.T), pinned(endpoints.T), nodes,
        pinned(w_ident), pinned(type_table), lanes(gain_one), lanes(shift_one),
    )
    embed_scratch = [
        pltpu.VMEM((rows, dim), BF16),
        pltpu.VMEM((lapk, rows), BF16),
        pltpu.VMEM((2, rows), jnp.int32),
        count_scratch,
        pltpu.VMEM((idw, dim), BF16),
        pltpu.VMEM((2, dim), BF16),
        wide_scratch,
        wide_scratch,
    ]

    wq_got, wk_got, wv_got = swap(w_query), swap(w_key), swap(w_value)
    bq_got, bv_got, bu_got = swap(bias_query), swap(bias_value), swap(bias_up)
    wo_got, wu_got, wd_got = swap(w_out), swap(w_up), swap(w_down)

    hidden, ident, normed, normed_t, q_own, k_own, v_own = call(
        embed_kernel,
        (
            *embed_args, lanes(bias_query), lanes(bias_value),
            pinned(w_query), pinned(w_key), pinned(w_value),
        ),
        [outside()] * 13,
        [
            ((rows, dim), F32),
            ((idw, rows), BF16),
            ((rows, dim), BF16),
            ((dim, rows), BF16),
            ((rows, width), BF16),
            ((rows, width), BF16),
            ((rows, width), BF16),
        ],
        scratch=embed_scratch
        + [half_scratch] * 2
        + [pltpu.VMEM((dim, width), BF16)] * 3
        + [pltpu.SemaphoreType.DMA((13,))],
    )
    ahead_rows, back_rows = dim + 2 * width, 3 * rows + 16
    q_got, k_got, v_got, probs, kept_a, sent_a, middle, active, slope = call(
        forward_kernel,
        (
            hidden, normed, q_own, k_own, v_own, wq_got, wk_got, wv_got,
            w_out, wo_got, w_up, wu_got,
            *(part.reshape(-1, LANES) for part in (bq_got, bv_got, bu_got)),
            nodes, edges,
            lanes(bias_up), lanes(bias_out), lanes(gain_two), lanes(shift_two),
        ),
        [whole()] * 15 + [outside()] * 6,
        [
            ((rows, width), BF16),
            ((rows, width), BF16),
            ((rows, width), BF16),
            ((mols, heads, SEQ, 2 * SEQ), BF16),
            ((ahead_rows, width), BF16),
            ((ahead_rows, width), BF16),
            ((rows, dim), F32),
            ((rows, dim), BF16),
            ((rows, dim), F32),
        ],
        scratch=[
            count_scratch,
            count_scratch,
            half_scratch,
            wide_scratch,
            wide_scratch,
            wide_scratch,
            pltpu.SemaphoreType.DMA((6,)),
            pltpu.VMEM((2, width, SEQ), F32),
            pltpu.VMEM((rows, dim), BF16),
            pltpu.VMEM((rows, dim), BF16),
        ],
        limit=30,
    )
    got_a = swap(sent_a)
    kept_back, sent_back, grad_middle, grad_branch = call(
        ffn_back_kernel,
        (
            middle, slope, w_up, wu_got, w_down, wd_got,
            nodes, edges, pinned(cotangent), lanes(gain_two),
        ),
        [whole()] * 6 + [outside()] * 4,
        [
            ((back_rows, width), BF16),
            ((back_rows, width), BF16),
            ((rows, dim), F32),
            ((rows, dim), BF16),
        ],
        scratch=[
            count_scratch,
            count_scratch,
            pltpu.VMEM((rows, dim), BF16),
            wide_scratch,
            pltpu.SemaphoreType.DMA((4,)),
            pltpu.VMEM((rows, dim), BF16),
        ],
    )
    got_back = swap(sent_back)

    unit = dim // block
    chunk = 3 * unit
    small_a, small_b = 16, 48

    def rest_sum(part):
        if rest_count == 1:
            return part
        groups = [[r * block + s for r in range(rest_count)] for s in range(block)]
        return lax.psum(part.astype(F32), "dp", axis_index_groups=groups).astype(part.dtype)

    pair = 2 * chunk

    def after(part, *others):
        return lax.optimization_barrier((part, *others))[0]

    def plane_step(parts, small_rows, late=(), others=(), micros=0):
        first, first_sent, second, second_sent = parts
        first_got = after(inner_move(first_sent, 1), *others)
        second_got = after(inner_move(second_sent, 2), *others)
        return call(
            plane_sum_kernel,
            (first, first_got, second, second_got, *late),
            [whole()] * (4 + len(late)),
            [((pair + small_rows, width), BF16)] * 2 + [((pair, width), BF16)] * 2,
            micros=micros,
        )

    def plane_turn(parts, others=(), micros=0):
        first, first_sent, second, second_sent = parts
        first_got = after(inner_move(first_sent, 2), *others)
        second_got = after(inner_move(second_sent, 1), *others)
        return call(
            line_cut_kernel,
            (first, first_got, second, second_got),
            [whole()] * 4,
            [
                ((chunk, width), BF16),
                ((first.shape[0] - chunk, width), BF16),
                ((chunk, width), BF16),
                ((chunk, width), BF16),
            ],
            micros=micros,
        )

    def line_step(parts, others=(), micros=0):
        got = [after(outer_move(parts[turn], turn), *others) for turn in range(1, OUTER)]
        mine, both = call(
            line_sum_kernel,
            (parts[0], parts[1], *got),
            [whole()] * 5,
            [((chunk, width), BF16), (parts[1].shape, BF16)],
            micros=micros,
        )
        if rest_count > 1:
            both = rest_sum(both)
            mine = both[:chunk]
        return mine, both

    def line_back(mine, both, others=(), micros=0):
        sent = (mine, both, mine)
        got = [after(outer_move(sent[turn - 1], turn), *others) for turn in range(1, OUTER)]
        small_rows = both.shape[0] - chunk
        return call(
            line_join_kernel,
            (both, *got),
            [whole()] * OUTER,
            [
                ((OUTER * chunk + small_rows, width), BF16),
                ((OUTER * chunk, width), BF16),
                ((small_rows, width), F32),
            ],
            micros=micros,
        )

    def plane_back(lines):
        return inner_move(lines[0], 1), inner_move(lines[1], 2)

    def plane_back_turn(side_x, side_y):
        return inner_move(side_y[:pair], 1), inner_move(side_x[pair : 2 * pair], 2)

    def placed(planes, split_second, micros=0):
        tall, flat = ((dim, width), F32), ((width, dim), F32)
        return call(
            lambda *refs: place_kernel(split_second, *refs),
            planes,
            [whole()] * len(planes),
            [tall, flat, flat] if split_second else [tall] * 3,
            micros=micros,
        )

    parts_down = call(
        down_grads_kernel,
        (after(kept_a, grad_branch), got_a, pinned(cotangent), nodes, edges),
        [whole()] * 2 + [outside()] * 3,
        [((INNER * unit, width), BF16)] * 4,
        scratch=[
            pltpu.VMEM((rows_all, dim), BF16),
            count_scratch,
            count_scratch,
            pltpu.SemaphoreType.DMA((3,)),
            pltpu.VMEM((2, width, width), BF16),
            pltpu.VMEM((rows_all, dim), BF16),
        ],
    )
    parts_a = call(
        ffn_grads_kernel,
        (after(kept_a, parts_down[0]), got_a, kept_back, got_back),
        [whole()] * 4,
        [((2 * INNER * unit + small_a, width), BF16)] * 2 + [((2 * INNER * unit, width), BF16)] * 2,
        scratch=[pltpu.VMEM((dim, width), BF16), pltpu.VMEM((2, width, width), BF16)],
    )
    ahead = [
        after(inner_move(parts_down[1], 1), parts_a[0]),
        after(inner_move(parts_down[3], 2), parts_a[0]),
    ]
    ga_own, ga_got = call(
        branch_kernel,
        (after(grad_branch, parts_a[0], *ahead), w_out, wo_got, nodes, edges),
        [whole()] * 3 + [outside()] * 2,
        [((rows, width), BF16), ((rows, width), BF16)],
        scratch=[count_scratch, count_scratch, pltpu.SemaphoreType.DMA((2,))],
    )

    kept_b, sent_b = call(
        attend_back_kernel,
        (q_own, k_own, v_own, ga_own, q_got, k_got, v_got, ga_got, probs),
        [whole()] * 9,
        [((3 * rows, width), BF16)] * 2,
        scratch=[
            pltpu.VMEM((2, width, SEQ), F32),
            pltpu.VMEM((2, SEQ, width), F32),
            pltpu.VMEM((2, SEQ, width), F32),
            pltpu.VMEM((2, heads // 2, SEQ, 2 * SEQ), BF16),
        ],
    )
    normed_t_got = swap(after(normed_t, parts_a[0]))
    got_b = swap(sent_b)
    moved = [after(inner_move(parts_a[1], 1), kept_b), after(inner_move(parts_a[3], 2), kept_b)]
    moved = moved + ahead
    steps_a = call(
        plane_join_kernel,
        (
            parts_a[0], moved[0], parts_a[2], moved[1],
            parts_down[0], moved[2], parts_down[2], moved[3],
        ),
        [whole()] * 8,
        [((pair + small_a, width), BF16)] * 2 + [((pair, width), BF16)] * 2,
        micros=6,
    )
    normed_t = after(normed_t, *steps_a)
    parts_b = call(
        qkv_grads_kernel,
        (normed_t, normed_t_got, kept_b, got_b),
        [whole()] * 4,
        [((INNER * chunk, width), BF16)] * 4 + [((small_b, width), F32)],
        scratch=[
            pltpu.VMEM((3, dim, width), BF16),
            pltpu.VMEM((dim, 2 * rows), BF16),
            pltpu.VMEM((2 * rows, width), BF16),
        ],
    )
    grad_middle = after(grad_middle, parts_b[0], *steps_a)
    grad_features, small_kept, small_sent = call(
        embed_back_kernel,
        (
            kept_b, sent_b, w_query, w_key, w_value, wq_got, wk_got, wv_got, ident,
            grad_middle, embed_args[0], nodes, *embed_args[4:7],
        ),
        [whole()] * 10 + [outside()] * 5,
        [((rows, dim), F32), ((small_b, width), F32), ((small_b, width), BF16)],
        scratch=[
            pltpu.VMEM((rows, dim), BF16),
            count_scratch,
            pltpu.VMEM((idw, dim), BF16),
            pltpu.VMEM((2, dim), BF16),
            wide_scratch,
            pltpu.SemaphoreType.DMA((5,)),
            pltpu.VMEM((rows, dim), F32),
            pltpu.VMEM((small_b, dim), F32),
        ],
        micros=0,
    )
    small_got = swap(small_sent)
    turned_a = plane_turn(steps_a, others=(small_kept,), micros=3)
    steps_b = plane_step(parts_b[:4], small_b, late=(small_kept, small_got, parts_b[4]))
    line_a = line_step(turned_a, others=steps_b, micros=3)
    turned_b = plane_turn(steps_b, others=line_a[:1])
    lines_a = line_back(*line_a, others=turned_b, micros=3)
    line_b = line_step(turned_b, micros=12)
    sides_a = plane_back((lines_a[1], lines_a[1]))
    far_a = plane_back_turn(*sides_a)
    planes_a = (lines_a[1], *sides_a, *far_a)
    lines_b = line_back(*line_b, micros=2)
    result = call(
        result_kernel,
        (middle, active, w_down, wd_got, lanes(after(bias_down, lines_b[1]))),
        [whole()] * 5,
        [((rows, dim), BF16)],
    )[0]
    wide, half = ((dim // LANES, LANES), F32), ((width // LANES, LANES), F32)
    sums_a = call(
        finish_first_kernel,
        (lines_a[2], swap(after(lines_a[2], lines_b[1]))),
        [whole()] * 2,
        [wide] * 4 + [half],
    )
    grad_w_up, grad_w_out, grad_w_down = placed(planes_a, True, micros=10)
    sides_b = plane_back(lines_b)
    sides_b, _ = lax.optimization_barrier((sides_b, (result, sums_a, grad_w_up)))
    far_b = plane_back_turn(*sides_b)
    planes_b = (lines_b[1], sides_b[0], sides_b[1], *far_b)
    extra = sides_b[0][OUTER * chunk :]
    own_b = lines_b[2] + extra.astype(F32)
    sums_b = call(
        finish_second_kernel,
        (lines_b[2], extra, swap(own_b)),
        [whole()] * 3,
        [((idw, dim), F32), ((2, dim), F32), wide, wide, half, half],
    )
    grad_w_query, grad_w_key, grad_w_value = placed(planes_b, False)
    return (
        result,
        grad_features,
        sums_b[0],
        sums_b[1],
        sums_b[2].reshape(-1),
        sums_b[3].reshape(-1),
        grad_w_query,
        grad_w_key,
        grad_w_value,
        sums_b[4].reshape(-1),
        sums_b[5].reshape(-1),
        grad_w_out,
        sums_a[0].reshape(-1),
        sums_a[1].reshape(-1),
        sums_a[2].reshape(-1),
        grad_w_up,
        sums_a[4].reshape(-1),
        grad_w_down,
        sums_a[3].reshape(-1),
    )


def solution(mesh):
    token, split = P("dp", None), P(("dp", "mp"), None)
    columns, lines, cut, copy = P(None, "mp"), P("mp", None), P("mp"), P()
    return jax.shard_map(
        per_device,
        mesh=mesh,
        in_specs=(
            token, token, P("dp"), P("dp"), token, copy, copy, copy, copy, columns, columns,
            columns, cut, cut, lines, copy, copy, copy, columns, cut, lines, copy, token,
        ),
        out_specs=(
            split, split, copy, copy, copy, copy, columns, columns, columns, cut, cut, lines,
            copy, copy, copy, columns, cut, lines, copy,
        ),
        check_vma=False,
    )
```

```python
import math

import jax
import jax.numpy as jnp
from jax import lax
from jax.experimental import pallas as pl
from jax.experimental.pallas import tpu as pltpu
from jax.sharding import PartitionSpec as P

HDIM = 24
SEQ = 128
LANES = 128
INNER = 4
OUTER = 4
EPSILON = 1e-05
SCALE = 1.0 / math.sqrt(HDIM)
LOG2_SCALE = SCALE * math.log2(math.e)
F32, BF16 = jnp.float32, jnp.bfloat16
MIB = 1024 * 1024


def dot(left, right):
    return jnp.dot(left, right, preferred_element_type=F32)


def dot_nt(left, right):
    return lax.dot_general(left, right, (((1,), (1,)), ((), ())), preferred_element_type=F32)


def dot_tn(left, right):
    return lax.dot_general(left, right, (((0,), (0,)), ((), ())), preferred_element_type=F32)


def norm_parts(hidden):
    average = jnp.mean(hidden, axis=-1, keepdims=True)
    centred = hidden - average
    inverse = lax.rsqrt(jnp.mean(centred * centred, axis=-1, keepdims=True) + EPSILON)
    return centred * inverse, inverse


def norm_back(unit, inverse, grad_hat):
    return inverse * (
        grad_hat
        - jnp.mean(grad_hat, axis=-1, keepdims=True)
        - unit * jnp.mean(grad_hat * unit, axis=-1, keepdims=True)
    )


def row_sum(block):
    return jnp.sum(block, axis=0, keepdims=True)


def positions(length):
    return lax.broadcasted_iota(jnp.int32, (length, 1), 0)


def whole():
    return pl.BlockSpec(memory_space=pltpu.VMEM)


def outside():
    return pl.BlockSpec(memory_space=pltpu.HBM)


def places():
    index = lax.axis_index("dp")
    return lax.axis_index("mp"), index % INNER, index // INNER % OUTER


def copy_in(sources, targets, sems):
    copies = [
        pltpu.make_async_copy(source, target, sems.at[place])
        for place, (source, target) in enumerate(zip(sources, targets))
    ]
    for copy in copies:
        copy.start()
    return copies


def row_of(ref):
    block = ref[...].astype(F32)
    return jnp.concatenate([block[r : r + 1, :] for r in range(block.shape[0])], axis=1)


def put_row(ref, row):
    for r in range(ref.shape[0]):
        ref[r : r + 1, :] = row[:, r * LANES : (r + 1) * LANES]


def call(kernel, args, specs, outs, scratch=(), micros=0, limit=24):
    return pl.pallas_call(
        kernel,
        out_shape=[jax.ShapeDtypeStruct(shape, kind) for shape, kind in outs],
        in_specs=specs,
        out_specs=[whole() for _ in outs],
        scratch_shapes=list(scratch),
        compiler_params=pltpu.CompilerParams(vmem_limit_bytes=limit * MIB),
        cost_estimate=pl.CostEstimate(
            flops=micros * 1_000_000_000, bytes_accessed=0, transcendentals=0
        ),
    )(*args)


def head_windows(width):
    windows = []
    for pair in range(width // (2 * HDIM)):
        low = pair * 2 * HDIM // LANES * LANES
        high = -(-(pair + 1) * 2 * HDIM // LANES) * LANES
        windows.append((low, high))
    return windows


def split_heads(block, pair, window):
    low, high = window
    part = block[:, low:high]
    column = low + lax.broadcasted_iota(jnp.int32, (16, high - low), 1)
    sides = []
    for head in (2 * pair, 2 * pair + 1):
        inside = (column >= head * HDIM) & (column < (head + 1) * HDIM)
        mask = jnp.where(inside, 1.0, 0.0).astype(BF16)
        sides.append(part * jnp.concatenate([mask] * (block.shape[0] // 16), axis=0))
    return jnp.concatenate(sides, axis=0)


def embed_rows(feats, lap, ends, w_ident, types, gain, shift, at, count):
    table = lap[:, at]
    slot = lax.broadcasted_iota(jnp.int32, (SEQ, SEQ), 0)
    picked = []
    for end in (0, 1):
        pick = jnp.where(ends[end : end + 1, at] == slot, 1.0, 0.0).astype(BF16)
        picked.append(dot(table, pick))
    ident = jnp.concatenate(picked, axis=0).astype(BF16)
    hidden = feats[at, :].astype(F32) + dot_tn(ident, w_ident[...])
    kinds = types[...].astype(F32)
    hidden = hidden + jnp.where(positions(SEQ) >= count, kinds[1:2, :], kinds[0:1, :])
    unit, _ = norm_parts(hidden)
    return hidden, ident, (unit * gain + shift).astype(BF16)


def embed_kernel(
    feats_in, lap_in, ends_in, nodes_in, w_ident_in, types_in, gain_in, shift_in,
    bias_q_in, bias_v_in, wq_in, wk_in, wv_in, edges_in,
    hidden_out, ident_out, normed_out, normed_t_out, q_out, k_out, v_out, keep_out,
    feats, lap, ends, nodes, w_ident, types, gain_rows, shift_rows, bias_q, bias_v,
    w_q, w_k, w_v, edges, sems,
):
    rows, dim = feats.shape
    mols = rows // SEQ
    core = places()[0]
    own_rows = pl.ds(pl.multiple_of(core * rows, SEQ), rows)
    copies = copy_in(
        (
            feats_in.at[own_rows, :], lap_in.at[:, own_rows], ends_in.at[:, own_rows], nodes_in,
            w_ident_in, types_in, gain_in, shift_in, bias_q_in, bias_v_in, wq_in, wk_in, wv_in,
            edges_in,
        ),
        (
            feats, lap, ends, nodes, w_ident, types, gain_rows, shift_rows, bias_q, bias_v,
            w_q, w_k, w_v, edges,
        ),
        sems,
    )
    for copy in copies[:10]:
        copy.wait()
    gain, shift = row_of(gain_rows), row_of(shift_rows)

    def molecule(m):
        at = slice(m * SEQ, (m + 1) * SEQ)
        count = nodes[core * mols + m]
        hidden, ident, normed = embed_rows(
            feats, lap, ends, w_ident, types, gain, shift, at, count
        )
        ident_out[:, at] = ident
        hidden_out[at, :] = hidden
        normed_out[at, :] = normed
        normed_t_out[:, at] = normed.T

    for m in range(mols):
        molecule(m)
    normed = normed_out[...]
    copies[10].wait()
    q_out[...] = (dot(normed, w_q[...]) + row_of(bias_q)).astype(BF16)
    copies[11].wait()
    k_out[...] = dot(normed, w_k[...]).astype(BF16)
    copies[12].wait()
    v_out[...] = (dot(normed, w_v[...]) + row_of(bias_v)).astype(BF16)
    copies[13].wait()
    for m in range(2 * mols):
        inside = lax.broadcasted_iota(jnp.int32, (SEQ, LANES), 0) < nodes[m] + edges[m]
        keep_out[m * SEQ : (m + 1) * SEQ, :] = jnp.where(inside, 1.0, 0.0)


def forward_kernel(
    hidden, normed, q_own, k_own, v_own, w_q, w_k, w_v, wo_own, wo, wu_own, wu,
    bias_q, bias_v, bias_u,
    nodes_in, edges_in, bias_u_own_in, bias_o_in, gain_in, shift_in,
    q_out, k_out, v_out, probs_out, keep_out, send_out, middle, active, slope,
    nodes, edges, bias_u_own, bias_o, gain_rows, shift_rows, sems,
    mixed, attended, normed_two,
):
    rows, dim = hidden.shape
    width = q_own.shape[1]
    mols = rows // SEQ
    pairs = width // (2 * HDIM)
    windows = head_windows(width)
    core = places()[0]
    copies = copy_in(
        (nodes_in, edges_in, bias_u_own_in, bias_o_in, gain_in, shift_in),
        (nodes, edges, bias_u_own, bias_o, gain_rows, shift_rows),
        sems,
    )

    q_out[...] = (dot(normed[...], w_q[...]) + row_of(bias_q)).astype(BF16)
    k_out[...] = dot(normed[...], w_k[...]).astype(BF16)
    v_out[...] = (dot(normed[...], w_v[...]) + row_of(bias_v)).astype(BF16)

    for copy in copies:
        copy.wait()
    gain, shift, bias_out = row_of(gain_rows), row_of(shift_rows), row_of(bias_o)

    sides = ((q_own, k_own, v_own, keep_out), (q_out, k_out, v_out, send_out))
    units = [(m, side) for m in range(mols) for side in (0, 1)]

    def weigh(unit, pair):
        m, side = unit
        at = slice(m * SEQ, (m + 1) * SEQ)
        place = core * mols + m
        key_keep = positions(SEQ) < nodes[place] + edges[place]
        low, high = windows[pair]
        both = split_heads(sides[side][0][at, :], pair, windows[pair])
        scores = dot_nt(sides[side][1][at, low:high], both)
        scores = jnp.where(key_keep, scores, -1e30)
        top = jnp.max(scores, axis=0, keepdims=True)
        raised = jnp.exp2((scores - top) * LOG2_SCALE)
        probs_out[m, side * pairs + pair] = (raised * (1.0 / row_sum(raised))).astype(BF16)

    def mix(unit, pair, values_t):
        m, side = unit
        first = pair * 2 * HDIM
        out = dot(values_t[first : first + 2 * HDIM], probs_out[m, side * pairs + pair])
        mixed[side, first : first + HDIM, :] = out[:HDIM, :SEQ]
        mixed[side, first + HDIM : first + 2 * HDIM, :] = out[HDIM:, SEQ:]

    def keep_mixed(unit):
        m, side = unit
        at = slice(m * SEQ, (m + 1) * SEQ)
        place = core * mols + m
        query_keep = lax.broadcasted_iota(jnp.int32, (1, SEQ), 1) < nodes[place] + edges[place]
        kept = jnp.where(query_keep, mixed[side], 0.0).astype(BF16)
        sides[side][3][dim : dim + width, at] = kept
        attended[at, side * width : (side + 1) * width] = kept.T

    for pair in range(pairs):
        weigh(units[0], pair)
    for step, task in enumerate(units):
        values_t = sides[task[1]][2][task[0] * SEQ : (task[0] + 1) * SEQ, :].T
        for pair in range(pairs):
            mix(task, pair, values_t)
            if step + 1 < len(units):
                weigh(units[step + 1], pair)
        keep_mixed(task)
    middle[...] = (
        hidden[...] + dot(attended[:, :width], wo_own[...]) + dot(attended[:, width:], wo[...])
    )

    for m in range(mols):
        at = slice(m * SEQ, (m + 1) * SEQ)
        total = middle[at, :] + bias_out
        middle[at, :] = total
        unit_rows, _ = norm_parts(total)
        rows_two = (unit_rows * gain + shift).astype(BF16)
        normed_two[at, :] = rows_two
        turned = rows_two.T
        keep_out[:dim, at] = turned
        send_out[:dim, at] = turned

    for side, (w_ref, b_ref, part_out) in enumerate(
        ((wu_own, bias_u_own, keep_out), (wu, bias_u, send_out))
    ):
        columns = slice(side * width, (side + 1) * width)
        slope[:, columns] = dot(normed_two[...], w_ref[...]) + row_of(b_ref)

        for m in range(mols):
            at = slice(m * SEQ, (m + 1) * SEQ)
            before = slope[at, columns]
            phi = 0.5 * (1.0 + lax.erf(before * math.sqrt(0.5)))
            out = (before * phi).astype(BF16)
            slope[at, columns] = phi + before * jnp.exp(before * before * -0.5) * (
                1.0 / math.sqrt(2.0 * math.pi)
            )
            active[at, columns] = out
            part_out[dim + width : dim + 2 * width, at] = out.T


def ffn_back_kernel(
    middle, slope, wu_own, wu, wd_own, wd, keep_rows, cots, gain_in,
    keep_out, send_out, gm_out, grad_branch,
    gain_rows, sems, grad_ffn,
):
    rows, dim = middle.shape
    width = wd.shape[0]
    mols = rows // SEQ
    core = places()[0]
    copies = copy_in((gain_in,), (gain_rows,), sems)

    def own_cots(m):
        at = pl.ds(pl.multiple_of(core * rows + m * SEQ, SEQ), SEQ)
        return jnp.where(keep_rows[at, 0:1] > 0.5, cots[at, :].astype(F32), 0.0)

    for m in range(mols):
        at = slice(m * SEQ, (m + 1) * SEQ)
        grad_ffn[at, :] = own_cots(m).astype(BF16)
    place_b = 0
    for side, (w_ref, part_out) in enumerate(((wd_own, keep_out), (wd, send_out))):
        columns = slice(side * width, (side + 1) * width)
        grad_before = slope[:, columns] * dot_nt(grad_ffn[...], w_ref[...])
        part_out[place_b : place_b + rows, :] = grad_before.astype(BF16)

    back = pl.ds(place_b, rows)
    gm_out[...] = dot_nt(keep_out[back, :], wu_own[...]) + dot_nt(send_out[back, :], wu[...])

    copies[0].wait()
    gain = row_of(gain_rows)
    nothing = jnp.zeros((1, dim), F32)
    sums = (nothing,) * 4
    for m in range(mols):
        at = slice(m * SEQ, (m + 1) * SEQ)
        grad_normed = gm_out[at, :]
        unit_rows, inverse = norm_parts(middle[at, :])
        grad_result = own_cots(m)
        grad = grad_result + norm_back(unit_rows, inverse, grad_normed * gain)
        gm_out[at, :] = grad
        grad_branch[at, :] = grad.astype(BF16)
        sums = (
            sums[0] + row_sum(grad),
            sums[1] + row_sum(grad_normed * unit_rows),
            sums[2] + row_sum(grad_normed),
            sums[3] + row_sum(grad_result),
        )

    place_m = place_b + rows
    for part_out in (keep_out, send_out):
        part_out[place_m : place_m + rows, :] = grad_branch[:, :width]
        part_out[place_m + rows : place_m + 2 * rows, :] = grad_branch[:, width:]
    small = jnp.concatenate(list(sums) + [nothing] * 12, axis=0)
    left, right = small[:, :width], small[:, width:]
    place_s = place_m + 2 * rows
    keep_out[place_s:, :] = jnp.where(core == 0, left, right).astype(BF16)
    send_out[place_s:, :] = jnp.where(core == 0, right, left).astype(BF16)


def result_kernel(middle, active, wd_own, wd, bias, result_out):
    width = wd.shape[0]
    result_out[...] = (
        middle[...]
        + dot(active[:, :width], wd_own[...])
        + dot(active[:, width:], wd[...])
        + row_of(bias)
    ).astype(BF16)


def branch_kernel(grad_branch, wo_own, wo, keep_rows, ga_own_out, ga_out):
    rows = grad_branch.shape[0]
    own_rows = pl.ds(pl.multiple_of(places()[0] * rows, SEQ), rows)
    keep = keep_rows[own_rows, 0:1] > 0.5
    for ref, weight in ((ga_own_out, wo_own), (ga_out, wo)):
        ref[...] = jnp.where(keep, dot_nt(grad_branch[...], weight[...]), 0.0).astype(BF16)


def attend_back_kernel(
    q_own, k_own, v_own, ga_own, q_got, k_got, v_got, ga_got, probs_all,
    keep_out, send_out, dq_t, dk, dv, slopes,
):
    rows, width = q_own.shape
    pairs = width // (2 * HDIM)
    windows = head_windows(width)
    sides = (
        (q_own, k_own, v_own, ga_own, keep_out),
        (q_got, k_got, v_got, ga_got, send_out),
    )
    units = [(m, side) for m in range(rows // SEQ) for side in (0, 1)]

    def score_back(unit, pair):
        m, side = unit
        at = slice(m * SEQ, (m + 1) * SEQ)
        low, high = windows[pair]
        both_g = split_heads(sides[side][3][at, :], pair, windows[pair])
        probs_low = probs_all[m, side * pairs + pair]
        probs = probs_low.astype(F32)
        grad_probs = dot_nt(sides[side][2][at, low:high], both_g)
        inner = row_sum(probs * grad_probs)
        slopes[side, pair] = (probs * (grad_probs - inner)).astype(BF16)
        dv[side, :, low:high] += dot(probs_low, both_g)

    def rows_back(unit, pair, keys_t):
        m, side = unit
        low, high = windows[pair]
        grad_scores = slopes[side, pair]
        both_q = split_heads(sides[side][0][m * SEQ : (m + 1) * SEQ, :], pair, windows[pair])
        dk[side, :, low:high] += dot(grad_scores, both_q)
        first = pair * 2 * HDIM
        out = dot(keys_t[first : first + 2 * HDIM], grad_scores)
        dq_t[side, first : first + HDIM, :] = out[:HDIM, :SEQ]
        dq_t[side, first + HDIM : first + 2 * HDIM, :] = out[HDIM:, SEQ:]

    def begin(unit):
        dk[unit[1]] = jnp.zeros_like(dk[unit[1]])
        dv[unit[1]] = jnp.zeros_like(dv[unit[1]])

    def finish(unit):
        m, side = unit
        part_out = sides[side][4]
        base = m * SEQ
        part_out[base : base + SEQ, :] = (dq_t[side] * SCALE).astype(BF16).T
        part_out[rows + base : rows + base + SEQ, :] = (dk[side] * SCALE).astype(BF16)
        part_out[2 * rows + base : 2 * rows + base + SEQ, :] = dv[side].astype(BF16)

    begin(units[0])
    for pair in range(pairs):
        score_back(units[0], pair)
    for step, unit in enumerate(units):
        keys_t = sides[unit[1]][1][unit[0] * SEQ : (unit[0] + 1) * SEQ, :].T
        if step + 1 < len(units):
            begin(units[step + 1])
        for pair in range(pairs):
            rows_back(unit, pair, keys_t)
            if step + 1 < len(units):
                score_back(units[step + 1], pair)
        finish(unit)


def embed_back_kernel(*refs):
    (
        grads_own, grads,
        wq_own, wk_own, wv_own, w_q, w_k, w_v, ident, grad_middle,
        feats_in, nodes_in, w_ident_in, types_in, gain_in,
        features_out, keep_out, send_out,
        feats, nodes, w_ident, types, gain_rows, sems, grad_normed, small,
    ) = refs
    core = places()[0]
    rows = feats.shape[0]
    copies = copy_in(
        (
            feats_in.at[pl.ds(pl.multiple_of(core * rows, SEQ), rows), :], nodes_in,
            w_ident_in, types_in, gain_in,
        ),
        (feats, nodes, w_ident, types, gain_rows),
        sems,
    )
    rows, dim = feats.shape
    width = wq_own.shape[1]
    idw = ident.shape[0]
    total = None
    for part, weights in ((grads_own, (wq_own, wk_own, wv_own)), (grads, (w_q, w_k, w_v))):
        for place, weight in enumerate(weights):
            term = dot_nt(part[place * rows : (place + 1) * rows, :], weight[...])
            total = term if total is None else total + term
    grad_normed[...] = total
    mols = rows // SEQ
    small[...] = jnp.zeros_like(small)
    for copy in copies:
        copy.wait()
    gain = row_of(gain_rows)
    kinds = types[...].astype(F32)

    def molecule(m, carry):
        at = pl.ds(pl.multiple_of(m * SEQ, SEQ), SEQ)
        is_edge = positions(SEQ) >= nodes[core * mols + m]
        hidden = feats[at, :].astype(F32) + dot_tn(ident[:, at], w_ident[...])
        hidden = hidden + jnp.where(is_edge, kinds[1:2, :], kinds[0:1, :])
        unit, inverse = norm_parts(hidden)
        grad_rows = grad_normed[at, :]
        grad = grad_middle[at, :] + norm_back(unit, inverse, grad_rows * gain)
        features_out[at, :] = grad
        high = grad.astype(BF16)
        rest = (grad - high.astype(F32)).astype(BF16)
        picked = ident[:, at]
        small[:idw, :] += dot(picked, high) + dot(picked, rest)
        edge_rows = jnp.where(is_edge, grad, 0.0)
        small[idw : idw + 1, :] += row_sum(grad - edge_rows)
        small[idw + 1 : idw + 2, :] += row_sum(edge_rows)
        small[idw + 2 : idw + 3, :] += row_sum(grad_rows * unit)
        small[idw + 3 : idw + 4, :] += row_sum(grad_rows)
        return carry

    lax.fori_loop(0, mols, molecule, 0)
    left, right = small[:, :width], small[:, width:]
    keep_out[...] = jnp.where(core == 0, left, right)
    send_out[...] = jnp.where(core == 0, right, left).astype(BF16)


def deal(unit, places_in, outs, block_at, small=None):
    _, inner, outer = places()
    first_kept, first_sent, second_kept, second_sent = outs
    for step in range(INNER):
        for turn in range(OUTER):
            if turn < 2:
                out, slot = (first_sent if step % 2 else first_kept), step // 2
            else:
                out, slot = (second_sent if step // 2 else second_kept), step % 2
            start = (slot * 2 + turn % 2) * places_in * unit
            for place in range(places_in):
                out[start + place * unit : start + (place + 1) * unit, :] = block_at(
                    inner ^ step, outer ^ turn, place
                )
    if small is not None:
        for out in (first_kept, first_sent):
            out[INNER * places_in * unit :, :] = small


def flat_block(flat, unit, dest, z):
    row = pl.multiple_of((dest * (OUTER // 2) + z // 2) * unit, 16)
    return flat[z % 2, pl.ds(row, unit), :]


def down_grads_kernel(kept, got, cots, keep_rows, *rest):
    outs, (flat, grad_ffn) = rest[:4], rest[4:]
    rows_all, dim = cots.shape
    rows, width = rows_all // 2, kept.shape[1]
    core = places()[0]
    for m in range(rows_all // SEQ):
        at = slice(m * SEQ, (m + 1) * SEQ)
        grad_ffn[at, :] = jnp.where(keep_rows[at, 0:1] > 0.5, cots[at, :].astype(F32), 0.0).astype(BF16)
    own_rows = pl.ds(pl.multiple_of(core * rows, SEQ), rows)
    other_rows = pl.ds(pl.multiple_of((1 - core) * rows, SEQ), rows)
    turned = slice(dim + width, dim + 2 * width)
    for half in (0, 1):
        columns = slice(half * width, (half + 1) * width)
        product = dot(kept[turned, :], grad_ffn[own_rows, columns])
        product = product + dot(got[turned, :], grad_ffn[other_rows, columns])
        flat[half] = product.astype(BF16)
    unit = dim // (INNER * OUTER)
    deal(unit, 1, outs, lambda dest, z, place: flat_block(flat, unit, dest, z))


def ffn_grads_kernel(kept, got, kept_back, got_back, *rest):
    outs, (tall, flat) = rest[:4], rest[4:]
    rows, width = kept.shape[1], kept.shape[1]
    dim = kept.shape[0] - 2 * width
    back, place_s = slice(0, rows), 3 * rows
    tall[...] = (
        dot(kept[:dim, :], kept_back[back, :]) + dot(got[:dim, :], got_back[back, :])
    ).astype(BF16)
    turned = slice(dim, dim + width)
    for half in (0, 1):
        mid = slice((1 + half) * rows, (2 + half) * rows)
        flat[half] = (
            dot(kept[turned, :], kept_back[mid, :]) + dot(got[turned, :], got_back[mid, :])
        ).astype(BF16)
    bias = row_sum(kept_back[back, :].astype(F32)) + row_sum(got_back[back, :].astype(F32))
    small = kept_back[place_s:, :].astype(F32) + got_back[place_s:, :].astype(F32)
    spot = lax.broadcasted_iota(jnp.int32, small.shape, 0)
    small = jnp.where(spot == 4, bias, small).astype(BF16)
    unit = dim // (INNER * OUTER)

    def block_at(dest, z, place):
        if place == 0:
            return tall[pl.ds(pl.multiple_of((dest * OUTER + z) * unit, 16), unit), :]
        return flat_block(flat, unit, dest, z)

    deal(unit, 2, outs, block_at, small)


def qkv_grads_kernel(normed_t, normed_t_got, kept, got, *refs):
    outs, small_out, (tall, normed, stacked) = refs[:4], refs[4], refs[5:]
    dim, rows = normed_t.shape
    unit = dim // (INNER * OUTER)
    normed[:, :rows] = normed_t[...]
    normed[:, rows:] = normed_t_got[...]
    spot = lax.broadcasted_iota(jnp.int32, small_out.shape, 0)
    small = jnp.zeros(small_out.shape, F32)
    for place in range(3):
        part = slice(place * rows, (place + 1) * rows)
        stacked[:rows, :] = kept[part, :]
        stacked[rows:, :] = got[part, :]
        tall[place] = dot(normed[...], stacked[...]).astype(BF16)
        if place != 1:
            small = jnp.where(spot == 36 + place // 2, row_sum(stacked[...].astype(F32)), small)
    small_out[...] = small

    def block_at(dest, z, place):
        return tall[place, pl.ds(pl.multiple_of((dest * OUTER + z) * unit, 16), unit), :]

    deal(unit, 3, outs, block_at)


def add(first, second):
    return (first.astype(F32) + second.astype(F32)).astype(BF16)


def plane_sum_kernel(first, first_got, second, second_got, *refs):
    late, (first_kept, first_sent, second_kept, second_sent) = refs[:-4], refs[-4:]
    pair = second_kept.shape[0]
    total = add(first[...], first_got[...])
    first_kept[:pair, :] = total[:pair]
    first_sent[:pair, :] = total[pair : 2 * pair]
    if late:
        small = (late[0][...] + late[1][...].astype(F32) + late[2][...]).astype(BF16)
    else:
        small = total[2 * pair :]
    first_kept[pair:, :] = small
    first_sent[pair:, :] = small
    total = add(second[...], second_got[...])
    second_kept[...] = total[:pair]
    second_sent[...] = total[pair:]


def plane_join_kernel(first, first_got, second, second_got, *refs):
    ahead, outs = refs[:4], refs[4:]
    unit = ahead[0].shape[0] // 4
    small = add(first[8 * unit :, :], first_got[8 * unit :, :])
    for place, (left, right, more, more_got) in enumerate(
        ((first, first_got, *ahead[:2]), (second, second_got, *ahead[2:]))
    ):
        total = add(left[: 8 * unit, :], right[: 8 * unit, :])
        late = add(more[...], more_got[...])
        for block in range(4):
            out = outs[2 * place + block // 2]
            start = block % 2 * 3 * unit
            out[start : start + 2 * unit, :] = total[2 * block * unit : 2 * (block + 1) * unit]
            out[start + 2 * unit : start + 3 * unit, :] = late[block * unit : (block + 1) * unit]
    for out in outs[:2]:
        out[6 * unit :, :] = small


def line_cut_kernel(first, first_got, second, second_got, own, near, middle, far):
    chunk = own.shape[0]
    total = add(first[...], first_got[...])
    own[...] = total[:chunk]
    near[...] = total[chunk:]
    total = add(second[...], second_got[...])
    middle[...] = total[:chunk]
    far[...] = total[chunk:]


def line_sum_kernel(own, near, near_got, middle_got, far_got, out, out_small):
    chunk = own.shape[0]
    total = own[...].astype(F32) + near_got[:chunk, :].astype(F32)
    total = total + middle_got[...].astype(F32) + far_got[...].astype(F32)
    out[...] = total.astype(BF16)
    out_small[:chunk, :] = total.astype(BF16)
    out_small[chunk:, :] = add(near[chunk:, :], near_got[chunk:, :])


def line_join_kernel(own, near, middle, far, line_x, line_y, small_out):
    chunk = near.shape[0]
    small = own[chunk:, :].astype(F32) + middle[chunk:, :].astype(F32)
    small_out[...] = small
    for out in (line_x, line_y):
        for turn, part in enumerate((own, near, middle, far)):
            out[turn * chunk : (turn + 1) * chunk, :] = part[:chunk, :]
    line_x[OUTER * chunk :, :] = small.astype(BF16)


def place_kernel(split_second, *refs):
    outs, parts = refs[-3:], refs[:-3]
    own = parts[0]
    _, inner, outer = places()
    unit = own.shape[0] // (3 * OUTER)
    width = own.shape[1]
    for step in range(INNER):
        for turn in range(OUTER):
            ref, start = parts[step], turn * 3 * unit
            if step == 3 and turn >= 2:
                ref, start = parts[4], (turn - 2) * 3 * unit
            dest, z = inner ^ step, outer ^ turn
            tall = pl.ds(pl.multiple_of((dest * OUTER + z) * unit, 16), unit)
            flat = pl.ds(pl.multiple_of((dest * (OUTER // 2) + z // 2) * unit, 16), unit)
            columns = pl.ds(pl.multiple_of(z % 2 * width, LANES), width)
            for place in range(3):
                part = ref[start + place * unit : start + (place + 1) * unit, :].astype(F32)
                if split_second and place > 0:
                    outs[place][flat, columns] = part
                else:
                    outs[place][tall, :] = part


def finish_first_kernel(small, got, bias_out, gain, shift, bias_down, bias_up):
    core = places()[0]
    for place, ref in enumerate((bias_out, gain, shift, bias_down)):
        mine, other = small[place : place + 1, :], got[place : place + 1, :]
        left = jnp.where(core == 0, mine, other)
        put_row(ref, jnp.concatenate([left, jnp.where(core == 0, other, mine)], axis=1))
    put_row(bias_up, small[4:5, :])


def finish_second_kernel(small, extra, got, w_ident, types, gain, shift, bias_q, bias_v):
    idw = w_ident.shape[0]
    core = places()[0]
    mine, other = small[...] + extra[...].astype(F32), got[...]
    left = jnp.where(core == 0, mine, other)
    total = jnp.concatenate([left, jnp.where(core == 0, other, mine)], axis=1)
    w_ident[...] = total[:idw]
    types[...] = total[idw : idw + 2]
    put_row(gain, total[idw + 2 : idw + 3])
    put_row(shift, total[idw + 3 : idw + 4])
    put_row(bias_q, mine[idw + 4 : idw + 5])
    put_row(bias_v, mine[idw + 5 : idw + 6])


def per_device(
    features, lap_vectors, node_counts, edge_counts, endpoints, w_ident, type_table,
    gain_one, shift_one, w_query, w_key, w_value, bias_query, bias_value, w_out, bias_out,
    gain_two, shift_two, w_up, bias_up, w_down, bias_down, cotangent,
):
    dp_count = lax.axis_size("dp")
    dp_index = lax.axis_index("dp")
    mp_index = lax.axis_index("mp")
    block = INNER * OUTER
    rest_count = dp_count // block
    def swap(part):
        return lax.ppermute(part, "mp", [(0, 1), (1, 0)])

    def inner_move(part, step):
        return lax.ppermute(part, "dp", [(s, s ^ step) for s in range(dp_count)])

    def outer_move(part, step):
        return lax.ppermute(part, "dp", [(s, s ^ (step * INNER)) for s in range(dp_count)])

    rows_all, dim = features.shape
    rows = rows_all // 2
    mols = rows // SEQ
    width = w_query.shape[1]
    heads = width // HDIM
    lapk = lap_vectors.shape[1]
    idw = w_ident.shape[0]

    def pinned(part):
        return pltpu.with_memory_space_constraint(part, pltpu.HBM)

    def lanes(part):
        return pinned(part.reshape(-1, LANES))

    nodes, edges = pinned(node_counts), pinned(edge_counts)
    count_scratch = pltpu.SMEM(node_counts.shape, jnp.int32)
    wide_scratch = pltpu.VMEM((dim // LANES, LANES), BF16)
    half_scratch = pltpu.VMEM((width // LANES, LANES), BF16)
    embed_args = (
        pinned(features), pinned(lap_vectors.T), pinned(endpoints.T), nodes,
        pinned(w_ident), pinned(type_table), lanes(gain_one), lanes(shift_one),
    )
    embed_scratch = [
        pltpu.VMEM((rows, dim), BF16),
        pltpu.VMEM((lapk, rows), BF16),
        pltpu.VMEM((2, rows), jnp.int32),
        count_scratch,
        pltpu.VMEM((idw, dim), BF16),
        pltpu.VMEM((2, dim), BF16),
        wide_scratch,
        wide_scratch,
    ]

    wq_got, wk_got, wv_got = swap(w_query), swap(w_key), swap(w_value)
    bq_got, bv_got, bu_got = swap(bias_query), swap(bias_value), swap(bias_up)
    wo_got, wu_got, wd_got = swap(w_out), swap(w_up), swap(w_down)

    hidden, ident, normed, normed_t, q_own, k_own, v_own, keep_rows = call(
        embed_kernel,
        (
            *embed_args, lanes(bias_query), lanes(bias_value),
            pinned(w_query), pinned(w_key), pinned(w_value), edges,
        ),
        [outside()] * 14,
        [
            ((rows, dim), F32),
            ((idw, rows), BF16),
            ((rows, dim), BF16),
            ((dim, rows), BF16),
            ((rows, width), BF16),
            ((rows, width), BF16),
            ((rows, width), BF16),
            ((rows_all, LANES), F32),
        ],
        scratch=embed_scratch
        + [half_scratch] * 2
        + [pltpu.VMEM((dim, width), BF16)] * 3
        + [count_scratch, pltpu.SemaphoreType.DMA((14,))],
    )
    ahead_rows, back_rows = dim + 2 * width, 3 * rows + 16
    q_got, k_got, v_got, probs, kept_a, sent_a, middle, active, slope = call(
        forward_kernel,
        (
            hidden, normed, q_own, k_own, v_own, wq_got, wk_got, wv_got,
            w_out, wo_got, w_up, wu_got,
            *(part.reshape(-1, LANES) for part in (bq_got, bv_got, bu_got)),
            nodes, edges,
            lanes(bias_up), lanes(bias_out), lanes(gain_two), lanes(shift_two),
        ),
        [whole()] * 15 + [outside()] * 6,
        [
            ((rows, width), BF16),
            ((rows, width), BF16),
            ((rows, width), BF16),
            ((mols, heads, SEQ, 2 * SEQ), BF16),
            ((ahead_rows, width), BF16),
            ((ahead_rows, width), BF16),
            ((rows, dim), F32),
            ((rows, dim), BF16),
            ((rows, dim), F32),
        ],
        scratch=[
            count_scratch,
            count_scratch,
            half_scratch,
            wide_scratch,
            wide_scratch,
            wide_scratch,
            pltpu.SemaphoreType.DMA((6,)),
            pltpu.VMEM((2, width, SEQ), F32),
            pltpu.VMEM((rows, dim), BF16),
            pltpu.VMEM((rows, dim), BF16),
        ],
        limit=30,
    )
    got_a = swap(sent_a)
    kept_back, sent_back, grad_middle, grad_branch = call(
        ffn_back_kernel,
        (
            middle, slope, w_up, wu_got, w_down, wd_got, keep_rows, cotangent,
            lanes(gain_two),
        ),
        [whole()] * 8 + [outside()],
        [
            ((back_rows, width), BF16),
            ((back_rows, width), BF16),
            ((rows, dim), F32),
            ((rows, dim), BF16),
        ],
        scratch=[wide_scratch, pltpu.SemaphoreType.DMA((1,)), pltpu.VMEM((rows, dim), BF16)],
    )
    got_back = swap(sent_back)

    unit = dim // block
    chunk = 3 * unit
    small_a, small_b = 16, 48

    def rest_sum(part):
        if rest_count == 1:
            return part
        groups = [[r * block + s for r in range(rest_count)] for s in range(block)]
        return lax.psum(part.astype(F32), "dp", axis_index_groups=groups).astype(part.dtype)

    pair = 2 * chunk

    def after(part, *others):
        return lax.optimization_barrier((part, *others))[0]

    def plane_step(parts, small_rows, late=(), others=(), micros=0):
        first, first_sent, second, second_sent = parts
        first_got = after(inner_move(first_sent, 1), *others)
        second_got = after(inner_move(second_sent, 2), *others)
        return call(
            plane_sum_kernel,
            (first, first_got, second, second_got, *late),
            [whole()] * (4 + len(late)),
            [((pair + small_rows, width), BF16)] * 2 + [((pair, width), BF16)] * 2,
            micros=micros,
        )

    def plane_turn(parts, others=(), micros=0):
        first, first_sent, second, second_sent = parts
        first_got = after(inner_move(first_sent, 2), *others)
        second_got = after(inner_move(second_sent, 1), *others)
        return call(
            line_cut_kernel,
            (first, first_got, second, second_got),
            [whole()] * 4,
            [
                ((chunk, width), BF16),
                ((first.shape[0] - chunk, width), BF16),
                ((chunk, width), BF16),
                ((chunk, width), BF16),
            ],
            micros=micros,
        )

    def line_step(parts, others=(), micros=0):
        got = [after(outer_move(parts[turn], turn), *others) for turn in range(1, OUTER)]
        mine, both = call(
            line_sum_kernel,
            (parts[0], parts[1], *got),
            [whole()] * 5,
            [((chunk, width), BF16), (parts[1].shape, BF16)],
            micros=micros,
        )
        if rest_count > 1:
            both = rest_sum(both)
            mine = both[:chunk]
        return mine, both

    def line_back(mine, both, others=(), micros=0):
        sent = (mine, both, mine)
        got = [after(outer_move(sent[turn - 1], turn), *others) for turn in range(1, OUTER)]
        small_rows = both.shape[0] - chunk
        return call(
            line_join_kernel,
            (both, *got),
            [whole()] * OUTER,
            [
                ((OUTER * chunk + small_rows, width), BF16),
                ((OUTER * chunk, width), BF16),
                ((small_rows, width), F32),
            ],
            micros=micros,
        )

    def plane_back(lines):
        return inner_move(lines[0], 1), inner_move(lines[1], 2)

    def plane_back_turn(side_x, side_y):
        return inner_move(side_y[:pair], 1), inner_move(side_x[pair : 2 * pair], 2)

    def placed(planes, split_second, micros=0):
        tall, flat = ((dim, width), F32), ((width, dim), F32)
        return call(
            lambda *refs: place_kernel(split_second, *refs),
            planes,
            [whole()] * len(planes),
            [tall, flat, flat] if split_second else [tall] * 3,
            micros=micros,
        )

    parts_down = call(
        down_grads_kernel,
        (after(kept_a, grad_branch), got_a, cotangent, keep_rows),
        [whole()] * 4,
        [((INNER * unit, width), BF16)] * 4,
        scratch=[pltpu.VMEM((2, width, width), BF16), pltpu.VMEM((rows_all, dim), BF16)],
    )
    parts_a = call(
        ffn_grads_kernel,
        (after(kept_a, parts_down[0]), got_a, kept_back, got_back),
        [whole()] * 4,
        [((2 * INNER * unit + small_a, width), BF16)] * 2 + [((2 * INNER * unit, width), BF16)] * 2,
        scratch=[pltpu.VMEM((dim, width), BF16), pltpu.VMEM((2, width, width), BF16)],
    )
    ahead = [
        after(inner_move(parts_down[1], 1), parts_a[0]),
        after(inner_move(parts_down[3], 2), parts_a[0]),
    ]
    ga_own, ga_got = call(
        branch_kernel,
        (after(grad_branch, parts_a[0], *ahead), w_out, wo_got, keep_rows),
        [whole()] * 4,
        [((rows, width), BF16), ((rows, width), BF16)],
    )

    kept_b, sent_b = call(
        attend_back_kernel,
        (q_own, k_own, v_own, ga_own, q_got, k_got, v_got, ga_got, probs),
        [whole()] * 9,
        [((3 * rows, width), BF16)] * 2,
        scratch=[
            pltpu.VMEM((2, width, SEQ), F32),
            pltpu.VMEM((2, SEQ, width), F32),
            pltpu.VMEM((2, SEQ, width), F32),
            pltpu.VMEM((2, heads // 2, SEQ, 2 * SEQ), BF16),
        ],
    )
    normed_t_got = swap(after(normed_t, parts_a[0]))
    got_b = swap(sent_b)
    moved = [after(inner_move(parts_a[1], 1), kept_b), after(inner_move(parts_a[3], 2), kept_b)]
    moved = moved + ahead
    steps_a = call(
        plane_join_kernel,
        (
            parts_a[0], moved[0], parts_a[2], moved[1],
            parts_down[0], moved[2], parts_down[2], moved[3],
        ),
        [whole()] * 8,
        [((pair + small_a, width), BF16)] * 2 + [((pair, width), BF16)] * 2,
        micros=6,
    )
    normed_t = after(normed_t, *steps_a)
    parts_b = call(
        qkv_grads_kernel,
        (normed_t, normed_t_got, kept_b, got_b),
        [whole()] * 4,
        [((INNER * chunk, width), BF16)] * 4 + [((small_b, width), F32)],
        scratch=[
            pltpu.VMEM((3, dim, width), BF16),
            pltpu.VMEM((dim, 2 * rows), BF16),
            pltpu.VMEM((2 * rows, width), BF16),
        ],
    )
    turned_a = plane_turn(steps_a, others=(parts_b[0],), micros=3)
    grad_middle = after(grad_middle, parts_b[0], *turned_a)
    grad_features, small_kept, small_sent = call(
        embed_back_kernel,
        (
            kept_b, sent_b, w_query, w_key, w_value, wq_got, wk_got, wv_got, ident,
            grad_middle, embed_args[0], nodes, *embed_args[4:7],
        ),
        [whole()] * 10 + [outside()] * 5,
        [((rows, dim), F32), ((small_b, width), F32), ((small_b, width), BF16)],
        scratch=[
            pltpu.VMEM((rows, dim), BF16),
            count_scratch,
            pltpu.VMEM((idw, dim), BF16),
            pltpu.VMEM((2, dim), BF16),
            wide_scratch,
            pltpu.SemaphoreType.DMA((5,)),
            pltpu.VMEM((rows, dim), F32),
            pltpu.VMEM((small_b, dim), F32),
        ],
        micros=0,
    )
    small_got = swap(small_sent)
    steps_b = plane_step(parts_b[:4], small_b, late=(small_kept, small_got, parts_b[4]))
    line_a = line_step(turned_a, others=steps_b, micros=3)
    turned_b = plane_turn(steps_b, others=line_a[:1])
    lines_a = line_back(*line_a, others=turned_b, micros=1)
    line_b = line_step(turned_b, micros=12)
    sides_a = plane_back((lines_a[1], lines_a[1]))
    far_a = plane_back_turn(*sides_a)
    planes_a = (lines_a[1], *sides_a, *far_a)
    lines_b = line_back(*line_b, micros=2)
    result = call(
        result_kernel,
        (middle, active, w_down, wd_got, lanes(after(bias_down, lines_b[1]))),
        [whole()] * 5,
        [((rows, dim), BF16)],
    )[0]
    wide, half = ((dim // LANES, LANES), F32), ((width // LANES, LANES), F32)
    sums_a = call(
        finish_first_kernel,
        (lines_a[2], swap(after(lines_a[2], lines_b[1]))),
        [whole()] * 2,
        [wide] * 4 + [half],
    )
    grad_w_up, grad_w_out, grad_w_down = placed(planes_a, True, micros=10)
    sides_b = plane_back(lines_b)
    sides_b, _ = lax.optimization_barrier((sides_b, (result, sums_a, grad_w_up)))
    far_b = plane_back_turn(*sides_b)
    planes_b = (lines_b[1], sides_b[0], sides_b[1], *far_b)
    extra = sides_b[0][OUTER * chunk :]
    own_b = lines_b[2] + extra.astype(F32)
    sums_b = call(
        finish_second_kernel,
        (lines_b[2], extra, swap(own_b)),
        [whole()] * 3,
        [((idw, dim), F32), ((2, dim), F32), wide, wide, half, half],
    )
    grad_w_query, grad_w_key, grad_w_value = placed(planes_b, False)
    return (
        result,
        grad_features,
        sums_b[0],
        sums_b[1],
        sums_b[2].reshape(-1),
        sums_b[3].reshape(-1),
        grad_w_query,
        grad_w_key,
        grad_w_value,
        sums_b[4].reshape(-1),
        sums_b[5].reshape(-1),
        grad_w_out,
        sums_a[0].reshape(-1),
        sums_a[1].reshape(-1),
        sums_a[2].reshape(-1),
        grad_w_up,
        sums_a[4].reshape(-1),
        grad_w_down,
        sums_a[3].reshape(-1),
    )


def solution(mesh):
    token, split = P("dp", None), P(("dp", "mp"), None)
    columns, lines, cut, copy = P(None, "mp"), P("mp", None), P("mp"), P()
    return jax.shard_map(
        per_device,
        mesh=mesh,
        in_specs=(
            token, token, P("dp"), P("dp"), token, copy, copy, copy, copy, columns, columns,
            columns, cut, cut, lines, copy, copy, copy, columns, cut, lines, copy, token,
        ),
        out_specs=(
            split, split, copy, copy, copy, copy, columns, columns, columns, cut, cut, lines,
            copy, copy, copy, columns, cut, lines, copy,
        ),
        check_vma=False,
    )
```

```python
import math

import jax
import jax.numpy as jnp
from jax import lax
from jax.experimental import pallas as pl
from jax.experimental.pallas import tpu as pltpu
from jax.sharding import PartitionSpec as P

HDIM = 24
SEQ = 128
LANES = 128
INNER = 4
OUTER = 4
EPSILON = 1e-05
SCALE = 1.0 / math.sqrt(HDIM)
LOG2_SCALE = SCALE * math.log2(math.e)
F32, BF16 = jnp.float32, jnp.bfloat16
MIB = 1024 * 1024


def dot(left, right):
    return jnp.dot(left, right, preferred_element_type=F32)


def dot_nt(left, right):
    return lax.dot_general(left, right, (((1,), (1,)), ((), ())), preferred_element_type=F32)


def dot_tn(left, right):
    return lax.dot_general(left, right, (((0,), (0,)), ((), ())), preferred_element_type=F32)


def norm_parts(hidden):
    average = jnp.mean(hidden, axis=-1, keepdims=True)
    centred = hidden - average
    inverse = lax.rsqrt(jnp.mean(centred * centred, axis=-1, keepdims=True) + EPSILON)
    return centred * inverse, inverse


def norm_back(unit, inverse, grad_hat):
    return inverse * (
        grad_hat
        - jnp.mean(grad_hat, axis=-1, keepdims=True)
        - unit * jnp.mean(grad_hat * unit, axis=-1, keepdims=True)
    )


def row_sum(block):
    return jnp.sum(block, axis=0, keepdims=True)


def positions(length):
    return lax.broadcasted_iota(jnp.int32, (length, 1), 0)


def whole():
    return pl.BlockSpec(memory_space=pltpu.VMEM)


def outside():
    return pl.BlockSpec(memory_space=pltpu.HBM)


def places():
    index = lax.axis_index("dp")
    return lax.axis_index("mp"), index % INNER, index // INNER % OUTER


def copy_in(sources, targets, sems):
    copies = [
        pltpu.make_async_copy(source, target, sems.at[place])
        for place, (source, target) in enumerate(zip(sources, targets))
    ]
    for copy in copies:
        copy.start()
    return copies


def row_of(ref):
    block = ref[...].astype(F32)
    return jnp.concatenate([block[r : r + 1, :] for r in range(block.shape[0])], axis=1)


def put_row(ref, row):
    for r in range(ref.shape[0]):
        ref[r : r + 1, :] = row[:, r * LANES : (r + 1) * LANES]


def call(kernel, args, specs, outs, scratch=(), micros=0, limit=24):
    return pl.pallas_call(
        kernel,
        out_shape=[jax.ShapeDtypeStruct(shape, kind) for shape, kind in outs],
        in_specs=specs,
        out_specs=[whole() for _ in outs],
        scratch_shapes=list(scratch),
        compiler_params=pltpu.CompilerParams(vmem_limit_bytes=limit * MIB),
        cost_estimate=pl.CostEstimate(
            flops=micros * 1_000_000_000, bytes_accessed=0, transcendentals=0
        ),
    )(*args)


def head_windows(width):
    windows = []
    for pair in range(width // (2 * HDIM)):
        low = pair * 2 * HDIM // LANES * LANES
        high = -(-(pair + 1) * 2 * HDIM // LANES) * LANES
        windows.append((low, high))
    return windows


def split_heads(block, pair, window):
    low, high = window
    part = block[:, low:high]
    column = low + lax.broadcasted_iota(jnp.int32, (16, high - low), 1)
    sides = []
    for head in (2 * pair, 2 * pair + 1):
        inside = (column >= head * HDIM) & (column < (head + 1) * HDIM)
        mask = jnp.where(inside, 1.0, 0.0).astype(BF16)
        sides.append(part * jnp.concatenate([mask] * (block.shape[0] // 16), axis=0))
    return jnp.concatenate(sides, axis=0)


def embed_rows(feats, lap, ends, w_ident, types, gain, shift, at, count):
    table = lap[:, at]
    slot = lax.broadcasted_iota(jnp.int32, (SEQ, SEQ), 0)
    picked = []
    for end in (0, 1):
        pick = jnp.where(ends[end : end + 1, at] == slot, 1.0, 0.0).astype(BF16)
        picked.append(dot(table, pick))
    ident = jnp.concatenate(picked, axis=0).astype(BF16)
    hidden = feats[at, :].astype(F32) + dot_tn(ident, w_ident[...])
    kinds = types[...].astype(F32)
    hidden = hidden + jnp.where(positions(SEQ) >= count, kinds[1:2, :], kinds[0:1, :])
    unit, _ = norm_parts(hidden)
    return hidden, ident, (unit * gain + shift).astype(BF16)


def embed_kernel(
    feats_in, lap_in, ends_in, nodes_in, w_ident_in, types_in, gain_in, shift_in,
    bias_q_in, bias_v_in, wq_in, wk_in, wv_in, edges_in,
    hidden_out, ident_out, normed_out, normed_t_out, q_out, k_out, v_out, keep_out,
    feats, lap, ends, nodes, w_ident, types, gain_rows, shift_rows, bias_q, bias_v,
    w_q, w_k, w_v, edges, sems,
):
    rows, dim = feats.shape
    mols = rows // SEQ
    core = places()[0]
    own_rows = pl.ds(pl.multiple_of(core * rows, SEQ), rows)
    copies = copy_in(
        (
            feats_in.at[own_rows, :], lap_in.at[:, own_rows], ends_in.at[:, own_rows], nodes_in,
            w_ident_in, types_in, gain_in, shift_in, bias_q_in, bias_v_in, wq_in, wk_in, wv_in,
            edges_in,
        ),
        (
            feats, lap, ends, nodes, w_ident, types, gain_rows, shift_rows, bias_q, bias_v,
            w_q, w_k, w_v, edges,
        ),
        sems,
    )
    for copy in copies[:10]:
        copy.wait()
    gain, shift = row_of(gain_rows), row_of(shift_rows)

    def molecule(m):
        at = slice(m * SEQ, (m + 1) * SEQ)
        count = nodes[core * mols + m]
        hidden, ident, normed = embed_rows(
            feats, lap, ends, w_ident, types, gain, shift, at, count
        )
        ident_out[:, at] = ident
        hidden_out[at, :] = hidden
        normed_out[at, :] = normed
        normed_t_out[:, at] = normed.T

    for m in range(mols):
        molecule(m)
    normed = normed_out[...]
    copies[10].wait()
    q_out[...] = (dot(normed, w_q[...]) + row_of(bias_q)).astype(BF16)
    copies[11].wait()
    k_out[...] = dot(normed, w_k[...]).astype(BF16)
    copies[12].wait()
    v_out[...] = (dot(normed, w_v[...]) + row_of(bias_v)).astype(BF16)
    copies[13].wait()
    for m in range(2 * mols):
        inside = lax.broadcasted_iota(jnp.int32, (SEQ, LANES), 0) < nodes[m] + edges[m]
        keep_out[m * SEQ : (m + 1) * SEQ, :] = jnp.where(inside, 1.0, 0.0)


def forward_kernel(
    hidden, normed, q_own, k_own, v_own, w_q, w_k, w_v, wo_own, wo, wu_own, wu,
    bias_q, bias_v, bias_u,
    nodes_in, edges_in, bias_u_own_in, bias_o_in, gain_in, shift_in,
    q_out, k_out, v_out, probs_out, keep_out, send_out, middle, active, slope,
    nodes, edges, bias_u_own, bias_o, gain_rows, shift_rows, sems,
    mixed, attended, normed_two,
):
    rows, dim = hidden.shape
    width = q_own.shape[1]
    mols = rows // SEQ
    pairs = width // (2 * HDIM)
    windows = head_windows(width)
    core = places()[0]
    copies = copy_in(
        (nodes_in, edges_in, bias_u_own_in, bias_o_in, gain_in, shift_in),
        (nodes, edges, bias_u_own, bias_o, gain_rows, shift_rows),
        sems,
    )

    q_out[...] = (dot(normed[...], w_q[...]) + row_of(bias_q)).astype(BF16)
    k_out[...] = dot(normed[...], w_k[...]).astype(BF16)
    v_out[...] = (dot(normed[...], w_v[...]) + row_of(bias_v)).astype(BF16)

    for copy in copies:
        copy.wait()
    gain, shift, bias_out = row_of(gain_rows), row_of(shift_rows), row_of(bias_o)

    sides = ((q_own, k_own, v_own, keep_out), (q_out, k_out, v_out, send_out))
    units = [(m, side) for m in range(mols) for side in (0, 1)]

    def weigh(unit, pair):
        m, side = unit
        at = slice(m * SEQ, (m + 1) * SEQ)
        place = core * mols + m
        key_keep = positions(SEQ) < nodes[place] + edges[place]
        low, high = windows[pair]
        both = split_heads(sides[side][0][at, :], pair, windows[pair])
        scores = dot_nt(sides[side][1][at, low:high], both)
        scores = jnp.where(key_keep, scores, -1e30)
        top = jnp.max(scores, axis=0, keepdims=True)
        raised = jnp.exp2((scores - top) * LOG2_SCALE)
        probs_out[m, side * pairs + pair] = (raised * (1.0 / row_sum(raised))).astype(BF16)

    def mix(unit, pair, values_t):
        m, side = unit
        first = pair * 2 * HDIM
        out = dot(values_t[first : first + 2 * HDIM], probs_out[m, side * pairs + pair])
        mixed[side, first : first + HDIM, :] = out[:HDIM, :SEQ]
        mixed[side, first + HDIM : first + 2 * HDIM, :] = out[HDIM:, SEQ:]

    def keep_mixed(unit):
        m, side = unit
        at = slice(m * SEQ, (m + 1) * SEQ)
        place = core * mols + m
        query_keep = lax.broadcasted_iota(jnp.int32, (1, SEQ), 1) < nodes[place] + edges[place]
        kept = jnp.where(query_keep, mixed[side], 0.0).astype(BF16)
        sides[side][3][dim : dim + width, at] = kept
        attended[at, side * width : (side + 1) * width] = kept.T

    for pair in range(pairs):
        weigh(units[0], pair)
    for step, task in enumerate(units):
        values_t = sides[task[1]][2][task[0] * SEQ : (task[0] + 1) * SEQ, :].T
        for pair in range(pairs):
            mix(task, pair, values_t)
            if step + 1 < len(units):
                weigh(units[step + 1], pair)
        keep_mixed(task)
    middle[...] = (
        hidden[...] + dot(attended[:, :width], wo_own[...]) + dot(attended[:, width:], wo[...])
    )

    for m in range(mols):
        at = slice(m * SEQ, (m + 1) * SEQ)
        total = middle[at, :] + bias_out
        middle[at, :] = total
        unit_rows, _ = norm_parts(total)
        rows_two = (unit_rows * gain + shift).astype(BF16)
        normed_two[at, :] = rows_two
        turned = rows_two.T
        keep_out[:dim, at] = turned
        send_out[:dim, at] = turned

    for side, (w_ref, b_ref, part_out) in enumerate(
        ((wu_own, bias_u_own, keep_out), (wu, bias_u, send_out))
    ):
        columns = slice(side * width, (side + 1) * width)
        slope[:, columns] = dot(normed_two[...], w_ref[...]) + row_of(b_ref)

        for m in range(mols):
            at = slice(m * SEQ, (m + 1) * SEQ)
            before = slope[at, columns]
            phi = 0.5 * (1.0 + lax.erf(before * math.sqrt(0.5)))
            out = (before * phi).astype(BF16)
            slope[at, columns] = phi + before * jnp.exp(before * before * -0.5) * (
                1.0 / math.sqrt(2.0 * math.pi)
            )
            active[at, columns] = out
            part_out[dim + width : dim + 2 * width, at] = out.T


def ffn_back_kernel(
    middle, slope, wu_own, wu, wd_own, wd, keep_rows, cots, gain_in,
    keep_out, send_out, gm_out, grad_branch,
    gain_rows, sems, grad_ffn,
):
    rows, dim = middle.shape
    width = wd.shape[0]
    mols = rows // SEQ
    core = places()[0]
    copies = copy_in((gain_in,), (gain_rows,), sems)

    def own_cots(m):
        at = pl.ds(pl.multiple_of(core * rows + m * SEQ, SEQ), SEQ)
        return jnp.where(keep_rows[at, 0:1] > 0.5, cots[at, :].astype(F32), 0.0)

    for m in range(mols):
        at = slice(m * SEQ, (m + 1) * SEQ)
        grad_ffn[at, :] = own_cots(m).astype(BF16)
    place_b = 0
    for side, (w_ref, part_out) in enumerate(((wd_own, keep_out), (wd, send_out))):
        columns = slice(side * width, (side + 1) * width)
        grad_before = slope[:, columns] * dot_nt(grad_ffn[...], w_ref[...])
        part_out[place_b : place_b + rows, :] = grad_before.astype(BF16)

    back = pl.ds(place_b, rows)
    gm_out[...] = dot_nt(keep_out[back, :], wu_own[...]) + dot_nt(send_out[back, :], wu[...])

    copies[0].wait()
    gain = row_of(gain_rows)
    nothing = jnp.zeros((1, dim), F32)
    sums = (nothing,) * 4
    for m in range(mols):
        at = slice(m * SEQ, (m + 1) * SEQ)
        grad_normed = gm_out[at, :]
        unit_rows, inverse = norm_parts(middle[at, :])
        grad_result = own_cots(m)
        grad = grad_result + norm_back(unit_rows, inverse, grad_normed * gain)
        gm_out[at, :] = grad
        grad_branch[at, :] = grad.astype(BF16)
        sums = (
            sums[0] + row_sum(grad),
            sums[1] + row_sum(grad_normed * unit_rows),
            sums[2] + row_sum(grad_normed),
            sums[3] + row_sum(grad_result),
        )

    place_m = place_b + rows
    for part_out in (keep_out, send_out):
        part_out[place_m : place_m + rows, :] = grad_branch[:, :width]
        part_out[place_m + rows : place_m + 2 * rows, :] = grad_branch[:, width:]
    small = jnp.concatenate(list(sums) + [nothing] * 12, axis=0)
    left, right = small[:, :width], small[:, width:]
    place_s = place_m + 2 * rows
    keep_out[place_s:, :] = jnp.where(core == 0, left, right).astype(BF16)
    send_out[place_s:, :] = jnp.where(core == 0, right, left).astype(BF16)


def result_kernel(middle, active, wd_own, wd, bias, result_out):
    width = wd.shape[0]
    result_out[...] = (
        middle[...]
        + dot(active[:, :width], wd_own[...])
        + dot(active[:, width:], wd[...])
        + row_of(bias)
    ).astype(BF16)


def branch_kernel(grad_branch, wo_own, wo, keep_rows, ga_own_out, ga_out):
    rows = grad_branch.shape[0]
    own_rows = pl.ds(pl.multiple_of(places()[0] * rows, SEQ), rows)
    keep = keep_rows[own_rows, 0:1] > 0.5
    for ref, weight in ((ga_own_out, wo_own), (ga_out, wo)):
        ref[...] = jnp.where(keep, dot_nt(grad_branch[...], weight[...]), 0.0).astype(BF16)


def attend_back_kernel(
    q_own, k_own, v_own, ga_own, q_got, k_got, v_got, ga_got, probs_all,
    keep_out, send_out, dq_t, dk, dv, slopes,
):
    rows, width = q_own.shape
    pairs = width // (2 * HDIM)
    windows = head_windows(width)
    sides = (
        (q_own, k_own, v_own, ga_own, keep_out),
        (q_got, k_got, v_got, ga_got, send_out),
    )
    units = [(m, side) for m in range(rows // SEQ) for side in (0, 1)]

    def score_back(unit, pair):
        m, side = unit
        at = slice(m * SEQ, (m + 1) * SEQ)
        low, high = windows[pair]
        both_g = split_heads(sides[side][3][at, :], pair, windows[pair])
        probs_low = probs_all[m, side * pairs + pair]
        probs = probs_low.astype(F32)
        grad_probs = dot_nt(sides[side][2][at, low:high], both_g)
        inner = row_sum(probs * grad_probs)
        slopes[side, pair] = (probs * (grad_probs - inner)).astype(BF16)
        dv[side, :, low:high] += dot(probs_low, both_g)

    def rows_back(unit, pair, keys_t):
        m, side = unit
        low, high = windows[pair]
        grad_scores = slopes[side, pair]
        both_q = split_heads(sides[side][0][m * SEQ : (m + 1) * SEQ, :], pair, windows[pair])
        dk[side, :, low:high] += dot(grad_scores, both_q)
        first = pair * 2 * HDIM
        out = dot(keys_t[first : first + 2 * HDIM], grad_scores)
        dq_t[side, first : first + HDIM, :] = out[:HDIM, :SEQ]
        dq_t[side, first + HDIM : first + 2 * HDIM, :] = out[HDIM:, SEQ:]

    def begin(unit):
        dk[unit[1]] = jnp.zeros_like(dk[unit[1]])
        dv[unit[1]] = jnp.zeros_like(dv[unit[1]])

    def finish(unit):
        m, side = unit
        part_out = sides[side][4]
        base = m * SEQ
        part_out[base : base + SEQ, :] = (dq_t[side] * SCALE).astype(BF16).T
        part_out[rows + base : rows + base + SEQ, :] = (dk[side] * SCALE).astype(BF16)
        part_out[2 * rows + base : 2 * rows + base + SEQ, :] = dv[side].astype(BF16)

    begin(units[0])
    for pair in range(pairs):
        score_back(units[0], pair)
    for step, unit in enumerate(units):
        keys_t = sides[unit[1]][1][unit[0] * SEQ : (unit[0] + 1) * SEQ, :].T
        if step + 1 < len(units):
            begin(units[step + 1])
        for pair in range(pairs):
            rows_back(unit, pair, keys_t)
            if step + 1 < len(units):
                score_back(units[step + 1], pair)
        finish(unit)


def embed_back_kernel(*refs):
    (
        grads_own, grads,
        wq_own, wk_own, wv_own, w_q, w_k, w_v, ident, grad_middle,
        feats_in, nodes_in, w_ident_in, types_in, gain_in,
        features_out, keep_out, send_out,
        feats, nodes, w_ident, types, gain_rows, sems, grad_normed, small,
    ) = refs
    core = places()[0]
    rows = feats.shape[0]
    copies = copy_in(
        (
            feats_in.at[pl.ds(pl.multiple_of(core * rows, SEQ), rows), :], nodes_in,
            w_ident_in, types_in, gain_in,
        ),
        (feats, nodes, w_ident, types, gain_rows),
        sems,
    )
    rows, dim = feats.shape
    width = wq_own.shape[1]
    idw = ident.shape[0]
    total = None
    for part, weights in ((grads_own, (wq_own, wk_own, wv_own)), (grads, (w_q, w_k, w_v))):
        for place, weight in enumerate(weights):
            term = dot_nt(part[place * rows : (place + 1) * rows, :], weight[...])
            total = term if total is None else total + term
    grad_normed[...] = total
    mols = rows // SEQ
    small[...] = jnp.zeros_like(small)
    for copy in copies:
        copy.wait()
    gain = row_of(gain_rows)
    kinds = types[...].astype(F32)

    def molecule(m, carry):
        at = pl.ds(pl.multiple_of(m * SEQ, SEQ), SEQ)
        is_edge = positions(SEQ) >= nodes[core * mols + m]
        hidden = feats[at, :].astype(F32) + dot_tn(ident[:, at], w_ident[...])
        hidden = hidden + jnp.where(is_edge, kinds[1:2, :], kinds[0:1, :])
        unit, inverse = norm_parts(hidden)
        grad_rows = grad_normed[at, :]
        grad = grad_middle[at, :] + norm_back(unit, inverse, grad_rows * gain)
        features_out[at, :] = grad
        high = grad.astype(BF16)
        rest = (grad - high.astype(F32)).astype(BF16)
        picked = ident[:, at]
        small[:idw, :] += dot(picked, high) + dot(picked, rest)
        edge_rows = jnp.where(is_edge, grad, 0.0)
        small[idw : idw + 1, :] += row_sum(grad - edge_rows)
        small[idw + 1 : idw + 2, :] += row_sum(edge_rows)
        small[idw + 2 : idw + 3, :] += row_sum(grad_rows * unit)
        small[idw + 3 : idw + 4, :] += row_sum(grad_rows)
        return carry

    lax.fori_loop(0, mols, molecule, 0)
    left, right = small[:, :width], small[:, width:]
    keep_out[...] = jnp.where(core == 0, left, right)
    send_out[...] = jnp.where(core == 0, right, left).astype(BF16)


def deal(unit, places_in, outs, block_at, small=None):
    _, inner, outer = places()
    first_kept, first_sent, second_kept, second_sent = outs
    for step in range(INNER):
        for turn in range(OUTER):
            if turn < 2:
                out, slot = (first_sent if step % 2 else first_kept), step // 2
            else:
                out, slot = (second_sent if step // 2 else second_kept), step % 2
            start = (slot * 2 + turn % 2) * places_in * unit
            for place in range(places_in):
                out[start + place * unit : start + (place + 1) * unit, :] = block_at(
                    inner ^ step, outer ^ turn, place
                )
    if small is not None:
        for out in (first_kept, first_sent):
            out[INNER * places_in * unit :, :] = small


def flat_block(flat, unit, dest, z):
    row = pl.multiple_of((dest * (OUTER // 2) + z // 2) * unit, 16)
    return flat[z % 2, pl.ds(row, unit), :]


def down_grads_kernel(kept, got, cots, keep_rows, *rest):
    outs, (flat, grad_ffn) = rest[:4], rest[4:]
    rows_all, dim = cots.shape
    rows, width = rows_all // 2, kept.shape[1]
    core = places()[0]
    for m in range(rows_all // SEQ):
        at = slice(m * SEQ, (m + 1) * SEQ)
        grad_ffn[at, :] = jnp.where(keep_rows[at, 0:1] > 0.5, cots[at, :].astype(F32), 0.0).astype(BF16)
    own_rows = pl.ds(pl.multiple_of(core * rows, SEQ), rows)
    other_rows = pl.ds(pl.multiple_of((1 - core) * rows, SEQ), rows)
    turned = slice(dim + width, dim + 2 * width)
    for half in (0, 1):
        columns = slice(half * width, (half + 1) * width)
        product = dot(kept[turned, :], grad_ffn[own_rows, columns])
        product = product + dot(got[turned, :], grad_ffn[other_rows, columns])
        flat[half] = product.astype(BF16)
    unit = dim // (INNER * OUTER)
    deal(unit, 1, outs, lambda dest, z, place: flat_block(flat, unit, dest, z))


def ffn_grads_kernel(kept, got, kept_back, got_back, *rest):
    outs, (tall, flat) = rest[:4], rest[4:]
    rows, width = kept.shape[1], kept.shape[1]
    dim = kept.shape[0] - 2 * width
    back, place_s = slice(0, rows), 3 * rows
    tall[...] = (
        dot(kept[:dim, :], kept_back[back, :]) + dot(got[:dim, :], got_back[back, :])
    ).astype(BF16)
    turned = slice(dim, dim + width)
    for half in (0, 1):
        mid = slice((1 + half) * rows, (2 + half) * rows)
        flat[half] = (
            dot(kept[turned, :], kept_back[mid, :]) + dot(got[turned, :], got_back[mid, :])
        ).astype(BF16)
    bias = row_sum(kept_back[back, :].astype(F32)) + row_sum(got_back[back, :].astype(F32))
    small = kept_back[place_s:, :].astype(F32) + got_back[place_s:, :].astype(F32)
    spot = lax.broadcasted_iota(jnp.int32, small.shape, 0)
    small = jnp.where(spot == 4, bias, small).astype(BF16)
    unit = dim // (INNER * OUTER)

    def block_at(dest, z, place):
        if place == 0:
            return tall[pl.ds(pl.multiple_of((dest * OUTER + z) * unit, 16), unit), :]
        return flat_block(flat, unit, dest, z)

    deal(unit, 2, outs, block_at, small)


def qkv_grads_kernel(normed_t, normed_t_got, kept, got, *refs):
    outs, small_out, (tall, normed, stacked) = refs[:4], refs[4], refs[5:]
    dim, rows = normed_t.shape
    unit = dim // (INNER * OUTER)
    normed[:, :rows] = normed_t[...]
    normed[:, rows:] = normed_t_got[...]
    spot = lax.broadcasted_iota(jnp.int32, small_out.shape, 0)
    small = jnp.zeros(small_out.shape, F32)
    for place in range(3):
        part = slice(place * rows, (place + 1) * rows)
        stacked[:rows, :] = kept[part, :]
        stacked[rows:, :] = got[part, :]
        tall[place] = dot(normed[...], stacked[...]).astype(BF16)
        if place != 1:
            small = jnp.where(spot == 36 + place // 2, row_sum(stacked[...].astype(F32)), small)
    small_out[...] = small

    def block_at(dest, z, place):
        return tall[place, pl.ds(pl.multiple_of((dest * OUTER + z) * unit, 16), unit), :]

    deal(unit, 3, outs, block_at)


def add(first, second):
    return (first.astype(F32) + second.astype(F32)).astype(BF16)


def plane_sum_kernel(first, first_got, second, second_got, *refs):
    late, (first_kept, first_sent, second_kept, second_sent) = refs[:-4], refs[-4:]
    pair = second_kept.shape[0]
    total = add(first[...], first_got[...])
    first_kept[:pair, :] = total[:pair]
    first_sent[:pair, :] = total[pair : 2 * pair]
    if late:
        small = (late[0][...] + late[1][...].astype(F32) + late[2][...]).astype(BF16)
    else:
        small = total[2 * pair :]
    first_kept[pair:, :] = small
    first_sent[pair:, :] = small
    total = add(second[...], second_got[...])
    second_kept[...] = total[:pair]
    second_sent[...] = total[pair:]


def plane_join_kernel(first, first_got, second, second_got, *refs):
    ahead, outs = refs[:4], refs[4:]
    unit = ahead[0].shape[0] // 4
    small = add(first[8 * unit :, :], first_got[8 * unit :, :])
    for place, (left, right, more, more_got) in enumerate(
        ((first, first_got, *ahead[:2]), (second, second_got, *ahead[2:]))
    ):
        total = add(left[: 8 * unit, :], right[: 8 * unit, :])
        late = add(more[...], more_got[...])
        for block in range(4):
            out = outs[2 * place + block // 2]
            start = block % 2 * 3 * unit
            out[start : start + 2 * unit, :] = total[2 * block * unit : 2 * (block + 1) * unit]
            out[start + 2 * unit : start + 3 * unit, :] = late[block * unit : (block + 1) * unit]
    for out in outs[:2]:
        out[6 * unit :, :] = small


def line_cut_kernel(first, first_got, second, second_got, own, near, middle, far):
    chunk = own.shape[0]
    total = add(first[...], first_got[...])
    own[...] = total[:chunk]
    near[...] = total[chunk:]
    total = add(second[...], second_got[...])
    middle[...] = total[:chunk]
    far[...] = total[chunk:]


def line_sum_kernel(own, near, near_got, middle_got, far_got, out, out_small):
    chunk = own.shape[0]
    total = own[...].astype(F32) + near_got[:chunk, :].astype(F32)
    total = total + middle_got[...].astype(F32) + far_got[...].astype(F32)
    out[...] = total.astype(BF16)
    out_small[:chunk, :] = total.astype(BF16)
    out_small[chunk:, :] = add(near[chunk:, :], near_got[chunk:, :])


def line_half_kernel(own, got, out, small_out):
    chunk = out.shape[0] // 2
    out[:chunk, :] = own[:chunk, :]
    out[chunk:, :] = got[:chunk, :]
    small_out[...] = own[chunk:, :].astype(F32) + got[chunk:, :].astype(F32)


def line_whole_kernel(first, second, out):
    out[: first.shape[0], :] = first[...]
    out[first.shape[0] :, :] = second[...]


def line_join_kernel(own, near, middle, far, line_x, line_y, small_out):
    chunk = near.shape[0]
    small = own[chunk:, :].astype(F32) + middle[chunk:, :].astype(F32)
    small_out[...] = small
    for out in (line_x, line_y):
        for turn, part in enumerate((own, near, middle, far)):
            out[turn * chunk : (turn + 1) * chunk, :] = part[:chunk, :]
    line_x[OUTER * chunk :, :] = small.astype(BF16)


def place_kernel(split_second, turns, *refs):
    outs, parts = refs[-3:], refs[:-3]
    own = parts[0]
    _, inner, outer = places()
    unit = own.shape[0] // (3 * OUTER)
    width = own.shape[1]
    for step in range(INNER):
        for slot, turn in enumerate(turns):
            ref, start = parts[step], slot * 3 * unit
            if step == 3 and slot >= 2:
                ref, start = parts[4], (slot - 2) * 3 * unit
            dest, z = inner ^ step, outer ^ turn
            tall = pl.ds(pl.multiple_of((dest * OUTER + z) * unit, 16), unit)
            flat = pl.ds(pl.multiple_of((dest * (OUTER // 2) + z // 2) * unit, 16), unit)
            columns = pl.ds(pl.multiple_of(z % 2 * width, LANES), width)
            for place in range(3):
                part = ref[start + place * unit : start + (place + 1) * unit, :].astype(F32)
                if split_second and place > 0:
                    outs[place][flat, columns] = part
                else:
                    outs[place][tall, :] = part


def finish_first_kernel(small, got, bias_out, gain, shift, bias_down, bias_up):
    core = places()[0]
    for place, ref in enumerate((bias_out, gain, shift, bias_down)):
        mine, other = small[place : place + 1, :], got[place : place + 1, :]
        left = jnp.where(core == 0, mine, other)
        put_row(ref, jnp.concatenate([left, jnp.where(core == 0, other, mine)], axis=1))
    put_row(bias_up, small[4:5, :])


def finish_second_kernel(small, extra, got, w_ident, types, gain, shift, bias_q, bias_v):
    idw = w_ident.shape[0]
    core = places()[0]
    mine, other = small[...] + extra[...].astype(F32), got[...]
    left = jnp.where(core == 0, mine, other)
    total = jnp.concatenate([left, jnp.where(core == 0, other, mine)], axis=1)
    w_ident[...] = total[:idw]
    types[...] = total[idw : idw + 2]
    put_row(gain, total[idw + 2 : idw + 3])
    put_row(shift, total[idw + 3 : idw + 4])
    put_row(bias_q, mine[idw + 4 : idw + 5])
    put_row(bias_v, mine[idw + 5 : idw + 6])


def per_device(
    features, lap_vectors, node_counts, edge_counts, endpoints, w_ident, type_table,
    gain_one, shift_one, w_query, w_key, w_value, bias_query, bias_value, w_out, bias_out,
    gain_two, shift_two, w_up, bias_up, w_down, bias_down, cotangent,
):
    dp_count = lax.axis_size("dp")
    dp_index = lax.axis_index("dp")
    mp_index = lax.axis_index("mp")
    block = INNER * OUTER
    rest_count = dp_count // block
    def swap(part):
        return lax.ppermute(part, "mp", [(0, 1), (1, 0)])

    def inner_move(part, step):
        return lax.ppermute(part, "dp", [(s, s ^ step) for s in range(dp_count)])

    def outer_move(part, step):
        return lax.ppermute(part, "dp", [(s, s ^ (step * INNER)) for s in range(dp_count)])

    rows_all, dim = features.shape
    rows = rows_all // 2
    mols = rows // SEQ
    width = w_query.shape[1]
    heads = width // HDIM
    lapk = lap_vectors.shape[1]
    idw = w_ident.shape[0]

    def pinned(part):
        return pltpu.with_memory_space_constraint(part, pltpu.HBM)

    def lanes(part):
        return pinned(part.reshape(-1, LANES))

    nodes, edges = pinned(node_counts), pinned(edge_counts)
    count_scratch = pltpu.SMEM(node_counts.shape, jnp.int32)
    wide_scratch = pltpu.VMEM((dim // LANES, LANES), BF16)
    half_scratch = pltpu.VMEM((width // LANES, LANES), BF16)
    embed_args = (
        pinned(features), pinned(lap_vectors.T), pinned(endpoints.T), nodes,
        pinned(w_ident), pinned(type_table), lanes(gain_one), lanes(shift_one),
    )
    embed_scratch = [
        pltpu.VMEM((rows, dim), BF16),
        pltpu.VMEM((lapk, rows), BF16),
        pltpu.VMEM((2, rows), jnp.int32),
        count_scratch,
        pltpu.VMEM((idw, dim), BF16),
        pltpu.VMEM((2, dim), BF16),
        wide_scratch,
        wide_scratch,
    ]

    wq_got, wk_got, wv_got = swap(w_query), swap(w_key), swap(w_value)
    bq_got, bv_got, bu_got = swap(bias_query), swap(bias_value), swap(bias_up)
    wo_got, wu_got, wd_got = swap(w_out), swap(w_up), swap(w_down)

    hidden, ident, normed, normed_t, q_own, k_own, v_own, keep_rows = call(
        embed_kernel,
        (
            *embed_args, lanes(bias_query), lanes(bias_value),
            pinned(w_query), pinned(w_key), pinned(w_value), edges,
        ),
        [outside()] * 14,
        [
            ((rows, dim), F32),
            ((idw, rows), BF16),
            ((rows, dim), BF16),
            ((dim, rows), BF16),
            ((rows, width), BF16),
            ((rows, width), BF16),
            ((rows, width), BF16),
            ((rows_all, LANES), F32),
        ],
        scratch=embed_scratch
        + [half_scratch] * 2
        + [pltpu.VMEM((dim, width), BF16)] * 3
        + [count_scratch, pltpu.SemaphoreType.DMA((14,))],
    )
    ahead_rows, back_rows = dim + 2 * width, 3 * rows + 16
    q_got, k_got, v_got, probs, kept_a, sent_a, middle, active, slope = call(
        forward_kernel,
        (
            hidden, normed, q_own, k_own, v_own, wq_got, wk_got, wv_got,
            w_out, wo_got, w_up, wu_got,
            *(part.reshape(-1, LANES) for part in (bq_got, bv_got, bu_got)),
            nodes, edges,
            lanes(bias_up), lanes(bias_out), lanes(gain_two), lanes(shift_two),
        ),
        [whole()] * 15 + [outside()] * 6,
        [
            ((rows, width), BF16),
            ((rows, width), BF16),
            ((rows, width), BF16),
            ((mols, heads, SEQ, 2 * SEQ), BF16),
            ((ahead_rows, width), BF16),
            ((ahead_rows, width), BF16),
            ((rows, dim), F32),
            ((rows, dim), BF16),
            ((rows, dim), F32),
        ],
        scratch=[
            count_scratch,
            count_scratch,
            half_scratch,
            wide_scratch,
            wide_scratch,
            wide_scratch,
            pltpu.SemaphoreType.DMA((6,)),
            pltpu.VMEM((2, width, SEQ), F32),
            pltpu.VMEM((rows, dim), BF16),
            pltpu.VMEM((rows, dim), BF16),
        ],
        limit=30,
    )
    got_a = swap(sent_a)
    kept_back, sent_back, grad_middle, grad_branch = call(
        ffn_back_kernel,
        (
            middle, slope, w_up, wu_got, w_down, wd_got, keep_rows, cotangent,
            lanes(gain_two),
        ),
        [whole()] * 8 + [outside()],
        [
            ((back_rows, width), BF16),
            ((back_rows, width), BF16),
            ((rows, dim), F32),
            ((rows, dim), BF16),
        ],
        scratch=[wide_scratch, pltpu.SemaphoreType.DMA((1,)), pltpu.VMEM((rows, dim), BF16)],
    )
    got_back = swap(sent_back)

    unit = dim // block
    chunk = 3 * unit
    small_a, small_b = 16, 48

    def rest_sum(part):
        if rest_count == 1:
            return part
        groups = [[r * block + s for r in range(rest_count)] for s in range(block)]
        return lax.psum(part.astype(F32), "dp", axis_index_groups=groups).astype(part.dtype)

    pair = 2 * chunk

    def after(part, *others):
        return lax.optimization_barrier((part, *others))[0]

    def plane_step(parts, small_rows, late=(), others=(), micros=0):
        first, first_sent, second, second_sent = parts
        first_got = after(inner_move(first_sent, 1), *others)
        second_got = after(inner_move(second_sent, 2), *others)
        return call(
            plane_sum_kernel,
            (first, first_got, second, second_got, *late),
            [whole()] * (4 + len(late)),
            [((pair + small_rows, width), BF16)] * 2 + [((pair, width), BF16)] * 2,
            micros=micros,
        )

    def plane_turn(parts, others=(), micros=0):
        first, first_sent, second, second_sent = parts
        first_got = after(inner_move(first_sent, 2), *others)
        second_got = after(inner_move(second_sent, 1), *others)
        return call(
            line_cut_kernel,
            (first, first_got, second, second_got),
            [whole()] * 4,
            [
                ((chunk, width), BF16),
                ((first.shape[0] - chunk, width), BF16),
                ((chunk, width), BF16),
                ((chunk, width), BF16),
            ],
            micros=micros,
        )

    def line_step(parts, others=(), micros=0):
        got = [after(outer_move(parts[turn], turn), *others) for turn in range(1, OUTER)]
        mine, both = call(
            line_sum_kernel,
            (parts[0], parts[1], *got),
            [whole()] * 5,
            [((chunk, width), BF16), (parts[1].shape, BF16)],
            micros=micros,
        )
        if rest_count > 1:
            both = rest_sum(both)
            mine = both[:chunk]
        return mine, both

    def line_back(mine, both, others=(), micros=0):
        sent = (mine, both, mine)
        got = [after(outer_move(sent[turn - 1], turn), *others) for turn in range(1, OUTER)]
        small_rows = both.shape[0] - chunk
        return call(
            line_join_kernel,
            (both, *got),
            [whole()] * OUTER,
            [
                ((OUTER * chunk + small_rows, width), BF16),
                ((OUTER * chunk, width), BF16),
                ((small_rows, width), F32),
            ],
            micros=micros,
        )

    def line_back_pairs(both, others=(), half_micros=0, micros=0):
        got = after(outer_move(both, 2), *others)
        half, small = call(
            line_half_kernel,
            (both, got),
            [whole()] * 2,
            [((2 * chunk, width), BF16), ((both.shape[0] - chunk, width), F32)],
            micros=half_micros,
        )
        line = call(
            line_whole_kernel,
            (half, outer_move(half, 1)),
            [whole()] * 2,
            [((OUTER * chunk, width), BF16)],
            micros=micros,
        )[0]
        return line, small

    def plane_back(lines):
        return inner_move(lines[0], 1), inner_move(lines[1], 2)

    def plane_back_turn(side_x, side_y):
        return inner_move(side_y[:pair], 1), inner_move(side_x[pair : 2 * pair], 2)

    def placed(planes, split_second, turns, micros=0):
        tall, flat = ((dim, width), F32), ((width, dim), F32)
        return call(
            lambda *refs: place_kernel(split_second, turns, *refs),
            planes,
            [whole()] * len(planes),
            [tall, flat, flat] if split_second else [tall] * 3,
            micros=micros,
        )

    parts_down = call(
        down_grads_kernel,
        (after(kept_a, grad_branch), got_a, cotangent, keep_rows),
        [whole()] * 4,
        [((INNER * unit, width), BF16)] * 4,
        scratch=[pltpu.VMEM((2, width, width), BF16), pltpu.VMEM((rows_all, dim), BF16)],
    )
    parts_a = call(
        ffn_grads_kernel,
        (after(kept_a, parts_down[0]), got_a, kept_back, got_back),
        [whole()] * 4,
        [((2 * INNER * unit + small_a, width), BF16)] * 2 + [((2 * INNER * unit, width), BF16)] * 2,
        scratch=[pltpu.VMEM((dim, width), BF16), pltpu.VMEM((2, width, width), BF16)],
    )
    ahead = [
        after(inner_move(parts_down[1], 1), parts_a[0]),
        after(inner_move(parts_down[3], 2), parts_a[0]),
    ]
    ga_own, ga_got = call(
        branch_kernel,
        (after(grad_branch, parts_a[0], *ahead), w_out, wo_got, keep_rows),
        [whole()] * 4,
        [((rows, width), BF16), ((rows, width), BF16)],
    )

    kept_b, sent_b = call(
        attend_back_kernel,
        (q_own, k_own, v_own, ga_own, q_got, k_got, v_got, ga_got, probs),
        [whole()] * 9,
        [((3 * rows, width), BF16)] * 2,
        scratch=[
            pltpu.VMEM((2, width, SEQ), F32),
            pltpu.VMEM((2, SEQ, width), F32),
            pltpu.VMEM((2, SEQ, width), F32),
            pltpu.VMEM((2, heads // 2, SEQ, 2 * SEQ), BF16),
        ],
    )
    normed_t_got = swap(after(normed_t, parts_a[0]))
    got_b = swap(sent_b)
    moved = [after(inner_move(parts_a[1], 1), kept_b), after(inner_move(parts_a[3], 2), kept_b)]
    moved = moved + ahead
    steps_a = call(
        plane_join_kernel,
        (
            parts_a[0], moved[0], parts_a[2], moved[1],
            parts_down[0], moved[2], parts_down[2], moved[3],
        ),
        [whole()] * 8,
        [((pair + small_a, width), BF16)] * 2 + [((pair, width), BF16)] * 2,
        micros=6,
    )
    normed_t = after(normed_t, *steps_a)
    parts_b = call(
        qkv_grads_kernel,
        (normed_t, normed_t_got, kept_b, got_b),
        [whole()] * 4,
        [((INNER * chunk, width), BF16)] * 4 + [((small_b, width), F32)],
        scratch=[
            pltpu.VMEM((3, dim, width), BF16),
            pltpu.VMEM((dim, 2 * rows), BF16),
            pltpu.VMEM((2 * rows, width), BF16),
        ],
    )
    turned_a = plane_turn(steps_a, others=(parts_b[0],), micros=3)
    grad_middle = after(grad_middle, parts_b[0], *turned_a)
    grad_features, small_kept, small_sent = call(
        embed_back_kernel,
        (
            kept_b, sent_b, w_query, w_key, w_value, wq_got, wk_got, wv_got, ident,
            grad_middle, embed_args[0], nodes, *embed_args[4:7],
        ),
        [whole()] * 10 + [outside()] * 5,
        [((rows, dim), F32), ((small_b, width), F32), ((small_b, width), BF16)],
        scratch=[
            pltpu.VMEM((rows, dim), BF16),
            count_scratch,
            pltpu.VMEM((idw, dim), BF16),
            pltpu.VMEM((2, dim), BF16),
            wide_scratch,
            pltpu.SemaphoreType.DMA((5,)),
            pltpu.VMEM((rows, dim), F32),
            pltpu.VMEM((small_b, dim), F32),
        ],
        micros=0,
    )
    small_got = swap(small_sent)
    steps_b = plane_step(parts_b[:4], small_b, late=(small_kept, small_got, parts_b[4]))
    line_a = line_step(turned_a, others=steps_b, micros=3)
    turned_b = plane_turn(steps_b, others=line_a[:1], micros=0)
    line_all_a, small_sum_a = line_back_pairs(line_a[1], others=turned_b, half_micros=1, micros=5)
    line_b = line_step(turned_b, others=(line_all_a,), micros=12)
    sides_a = plane_back((line_all_a, line_all_a))
    far_a = plane_back_turn(*sides_a)
    planes_a = (line_all_a, *sides_a, *far_a)
    lines_b = line_back(*line_b, micros=2)
    result = call(
        result_kernel,
        (middle, active, w_down, wd_got, lanes(after(bias_down, lines_b[1]))),
        [whole()] * 5,
        [((rows, dim), BF16)],
    )[0]
    wide, half = ((dim // LANES, LANES), F32), ((width // LANES, LANES), F32)
    sums_a = call(
        finish_first_kernel,
        (small_sum_a, swap(after(small_sum_a, lines_b[1]))),
        [whole()] * 2,
        [wide] * 4 + [half],
    )
    grad_w_up, grad_w_out, grad_w_down = placed(planes_a, True, (0, 2, 1, 3), micros=10)
    sides_b = plane_back(lines_b)
    sides_b, _ = lax.optimization_barrier((sides_b, (result, sums_a, grad_w_up)))
    far_b = plane_back_turn(*sides_b)
    planes_b = (lines_b[1], sides_b[0], sides_b[1], *far_b)
    extra = sides_b[0][OUTER * chunk :]
    own_b = lines_b[2] + extra.astype(F32)
    sums_b = call(
        finish_second_kernel,
        (lines_b[2], extra, swap(own_b)),
        [whole()] * 3,
        [((idw, dim), F32), ((2, dim), F32), wide, wide, half, half],
    )
    grad_w_query, grad_w_key, grad_w_value = placed(planes_b, False, (0, 1, 2, 3))
    return (
        result,
        grad_features,
        sums_b[0],
        sums_b[1],
        sums_b[2].reshape(-1),
        sums_b[3].reshape(-1),
        grad_w_query,
        grad_w_key,
        grad_w_value,
        sums_b[4].reshape(-1),
        sums_b[5].reshape(-1),
        grad_w_out,
        sums_a[0].reshape(-1),
        sums_a[1].reshape(-1),
        sums_a[2].reshape(-1),
        grad_w_up,
        sums_a[4].reshape(-1),
        grad_w_down,
        sums_a[3].reshape(-1),
    )


def solution(mesh):
    token, split = P("dp", None), P(("dp", "mp"), None)
    columns, lines, cut, copy = P(None, "mp"), P("mp", None), P("mp"), P()
    return jax.shard_map(
        per_device,
        mesh=mesh,
        in_specs=(
            token, token, P("dp"), P("dp"), token, copy, copy, copy, copy, columns, columns,
            columns, cut, cut, lines, copy, copy, copy, columns, cut, lines, copy, token,
        ),
        out_specs=(
            split, split, copy, copy, copy, copy, columns, columns, columns, cut, cut, lines,
            copy, copy, copy, columns, cut, lines, copy,
        ),
        check_vma=False,
    )
```

```python
import math

import jax
import jax.numpy as jnp
from jax import lax
from jax.experimental import pallas as pl
from jax.experimental.pallas import tpu as pltpu
from jax.sharding import PartitionSpec as P

HDIM = 24
SEQ = 128
LANES = 128
INNER = 4
OUTER = 4
EPSILON = 1e-05
SCALE = 1.0 / math.sqrt(HDIM)
LOG2_SCALE = SCALE * math.log2(math.e)
F32, BF16 = jnp.float32, jnp.bfloat16
MIB = 1024 * 1024


def dot(left, right):
    return jnp.dot(left, right, preferred_element_type=F32)


def dot_nt(left, right):
    return lax.dot_general(left, right, (((1,), (1,)), ((), ())), preferred_element_type=F32)


def dot_tn(left, right):
    return lax.dot_general(left, right, (((0,), (0,)), ((), ())), preferred_element_type=F32)


def norm_parts(hidden):
    average = jnp.mean(hidden, axis=-1, keepdims=True)
    centred = hidden - average
    inverse = lax.rsqrt(jnp.mean(centred * centred, axis=-1, keepdims=True) + EPSILON)
    return centred * inverse, inverse


def norm_back(unit, inverse, grad_hat):
    return inverse * (
        grad_hat
        - jnp.mean(grad_hat, axis=-1, keepdims=True)
        - unit * jnp.mean(grad_hat * unit, axis=-1, keepdims=True)
    )


def row_sum(block):
    return jnp.sum(block, axis=0, keepdims=True)


def positions(length):
    return lax.broadcasted_iota(jnp.int32, (length, 1), 0)


def whole():
    return pl.BlockSpec(memory_space=pltpu.VMEM)


def outside():
    return pl.BlockSpec(memory_space=pltpu.HBM)


def places():
    index = lax.axis_index("dp")
    return lax.axis_index("mp"), index % INNER, index // INNER % OUTER


def copy_in(sources, targets, sems):
    copies = [
        pltpu.make_async_copy(source, target, sems.at[place])
        for place, (source, target) in enumerate(zip(sources, targets))
    ]
    for copy in copies:
        copy.start()
    return copies


def row_of(ref):
    block = ref[...].astype(F32)
    return jnp.concatenate([block[r : r + 1, :] for r in range(block.shape[0])], axis=1)


def put_row(ref, row):
    for r in range(ref.shape[0]):
        ref[r : r + 1, :] = row[:, r * LANES : (r + 1) * LANES]


def call(kernel, args, specs, outs, scratch=(), micros=0, limit=24, in_place=None):
    return pl.pallas_call(
        kernel,
        out_shape=[jax.ShapeDtypeStruct(shape, kind) for shape, kind in outs],
        in_specs=specs,
        out_specs=[outside() if in_place else whole() for _ in outs],
        input_output_aliases=in_place or {},
        scratch_shapes=list(scratch),
        compiler_params=pltpu.CompilerParams(vmem_limit_bytes=limit * MIB),
        cost_estimate=pl.CostEstimate(
            flops=micros * 1_000_000_000, bytes_accessed=0, transcendentals=0
        ),
    )(*args)


def head_windows(width):
    windows = []
    for pair in range(width // (2 * HDIM)):
        low = pair * 2 * HDIM // LANES * LANES
        high = -(-(pair + 1) * 2 * HDIM // LANES) * LANES
        windows.append((low, high))
    return windows


def split_heads(block, pair, window):
    low, high = window
    part = block[:, low:high]
    column = low + lax.broadcasted_iota(jnp.int32, (16, high - low), 1)
    sides = []
    for head in (2 * pair, 2 * pair + 1):
        inside = (column >= head * HDIM) & (column < (head + 1) * HDIM)
        mask = jnp.where(inside, 1.0, 0.0).astype(BF16)
        sides.append(part * jnp.concatenate([mask] * (block.shape[0] // 16), axis=0))
    return jnp.concatenate(sides, axis=0)


def embed_rows(feats, lap, ends, w_ident, types, gain, shift, at, count):
    table = lap[:, at]
    slot = lax.broadcasted_iota(jnp.int32, (SEQ, SEQ), 0)
    picked = []
    for end in (0, 1):
        pick = jnp.where(ends[end : end + 1, at] == slot, 1.0, 0.0).astype(BF16)
        picked.append(dot(table, pick))
    ident = jnp.concatenate(picked, axis=0).astype(BF16)
    hidden = feats[at, :].astype(F32) + dot_tn(ident, w_ident[...])
    kinds = types[...].astype(F32)
    hidden = hidden + jnp.where(positions(SEQ) >= count, kinds[1:2, :], kinds[0:1, :])
    unit, _ = norm_parts(hidden)
    return hidden, ident, (unit * gain + shift).astype(BF16)


def embed_kernel(
    feats_in, lap_in, ends_in, nodes_in, w_ident_in, types_in, gain_in, shift_in,
    bias_q_in, bias_v_in, wq_in, wk_in, wv_in, edges_in,
    hidden_out, ident_out, normed_out, normed_t_out, q_out, k_out, v_out, keep_out,
    feats, lap, ends, nodes, w_ident, types, gain_rows, shift_rows, bias_q, bias_v,
    w_q, w_k, w_v, edges, sems,
):
    rows, dim = feats.shape
    mols = rows // SEQ
    core = places()[0]
    own_rows = pl.ds(pl.multiple_of(core * rows, SEQ), rows)
    copies = copy_in(
        (
            feats_in.at[own_rows, :], lap_in.at[:, own_rows], ends_in.at[:, own_rows], nodes_in,
            w_ident_in, types_in, gain_in, shift_in, bias_q_in, bias_v_in, wq_in, wk_in, wv_in,
            edges_in,
        ),
        (
            feats, lap, ends, nodes, w_ident, types, gain_rows, shift_rows, bias_q, bias_v,
            w_q, w_k, w_v, edges,
        ),
        sems,
    )
    for copy in copies[:10]:
        copy.wait()
    gain, shift = row_of(gain_rows), row_of(shift_rows)

    def molecule(m):
        at = slice(m * SEQ, (m + 1) * SEQ)
        count = nodes[core * mols + m]
        hidden, ident, normed = embed_rows(
            feats, lap, ends, w_ident, types, gain, shift, at, count
        )
        ident_out[:, at] = ident
        hidden_out[at, :] = hidden
        normed_out[at, :] = normed
        normed_t_out[:, at] = normed.T

    for m in range(mols):
        molecule(m)
    normed = normed_out[...]
    copies[10].wait()
    q_out[...] = (dot(normed, w_q[...]) + row_of(bias_q)).astype(BF16)
    copies[11].wait()
    k_out[...] = dot(normed, w_k[...]).astype(BF16)
    copies[12].wait()
    v_out[...] = (dot(normed, w_v[...]) + row_of(bias_v)).astype(BF16)
    copies[13].wait()
    for m in range(2 * mols):
        inside = lax.broadcasted_iota(jnp.int32, (SEQ, LANES), 0) < nodes[m] + edges[m]
        keep_out[m * SEQ : (m + 1) * SEQ, :] = jnp.where(inside, 1.0, 0.0)


def forward_kernel(
    hidden, normed, q_own, k_own, v_own, w_q, w_k, w_v, wo_own, wo, wu_own, wu,
    bias_q, bias_v, bias_u,
    nodes_in, edges_in, bias_u_own_in, bias_o_in, gain_in, shift_in,
    q_out, k_out, v_out, probs_out, keep_out, send_out, middle, active, slope,
    nodes, edges, bias_u_own, bias_o, gain_rows, shift_rows, sems,
    mixed, attended, normed_two,
):
    rows, dim = hidden.shape
    width = q_own.shape[1]
    mols = rows // SEQ
    pairs = width // (2 * HDIM)
    windows = head_windows(width)
    core = places()[0]
    copies = copy_in(
        (nodes_in, edges_in, bias_u_own_in, bias_o_in, gain_in, shift_in),
        (nodes, edges, bias_u_own, bias_o, gain_rows, shift_rows),
        sems,
    )

    q_out[...] = (dot(normed[...], w_q[...]) + row_of(bias_q)).astype(BF16)
    k_out[...] = dot(normed[...], w_k[...]).astype(BF16)
    v_out[...] = (dot(normed[...], w_v[...]) + row_of(bias_v)).astype(BF16)

    for copy in copies:
        copy.wait()
    gain, shift, bias_out = row_of(gain_rows), row_of(shift_rows), row_of(bias_o)

    sides = ((q_own, k_own, v_own, keep_out), (q_out, k_out, v_out, send_out))
    units = [(m, side) for m in range(mols) for side in (0, 1)]

    def weigh(unit, pair):
        m, side = unit
        at = slice(m * SEQ, (m + 1) * SEQ)
        place = core * mols + m
        key_keep = positions(SEQ) < nodes[place] + edges[place]
        low, high = windows[pair]
        both = split_heads(sides[side][0][at, :], pair, windows[pair])
        scores = dot_nt(sides[side][1][at, low:high], both)
        scores = jnp.where(key_keep, scores, -1e30)
        top = jnp.max(scores, axis=0, keepdims=True)
        raised = jnp.exp2((scores - top) * LOG2_SCALE)
        probs_out[m, side * pairs + pair] = (raised * (1.0 / row_sum(raised))).astype(BF16)

    def mix(unit, pair, values_t):
        m, side = unit
        first = pair * 2 * HDIM
        out = dot(values_t[first : first + 2 * HDIM], probs_out[m, side * pairs + pair])
        mixed[side, first : first + HDIM, :] = out[:HDIM, :SEQ]
        mixed[side, first + HDIM : first + 2 * HDIM, :] = out[HDIM:, SEQ:]

    def keep_mixed(unit):
        m, side = unit
        at = slice(m * SEQ, (m + 1) * SEQ)
        place = core * mols + m
        query_keep = lax.broadcasted_iota(jnp.int32, (1, SEQ), 1) < nodes[place] + edges[place]
        kept = jnp.where(query_keep, mixed[side], 0.0).astype(BF16)
        sides[side][3][dim : dim + width, at] = kept
        attended[at, side * width : (side + 1) * width] = kept.T

    for pair in range(pairs):
        weigh(units[0], pair)
    for step, task in enumerate(units):
        values_t = sides[task[1]][2][task[0] * SEQ : (task[0] + 1) * SEQ, :].T
        for pair in range(pairs):
            mix(task, pair, values_t)
            if step + 1 < len(units):
                weigh(units[step + 1], pair)
        keep_mixed(task)
    middle[...] = (
        hidden[...] + dot(attended[:, :width], wo_own[...]) + dot(attended[:, width:], wo[...])
    )

    for m in range(mols):
        at = slice(m * SEQ, (m + 1) * SEQ)
        total = middle[at, :] + bias_out
        middle[at, :] = total
        unit_rows, _ = norm_parts(total)
        rows_two = (unit_rows * gain + shift).astype(BF16)
        normed_two[at, :] = rows_two
        turned = rows_two.T
        keep_out[:dim, at] = turned
        send_out[:dim, at] = turned

    for side, (w_ref, b_ref, part_out) in enumerate(
        ((wu_own, bias_u_own, keep_out), (wu, bias_u, send_out))
    ):
        columns = slice(side * width, (side + 1) * width)
        slope[:, columns] = dot(normed_two[...], w_ref[...]) + row_of(b_ref)

        for m in range(mols):
            at = slice(m * SEQ, (m + 1) * SEQ)
            before = slope[at, columns]
            phi = 0.5 * (1.0 + lax.erf(before * math.sqrt(0.5)))
            out = (before * phi).astype(BF16)
            slope[at, columns] = phi + before * jnp.exp(before * before * -0.5) * (
                1.0 / math.sqrt(2.0 * math.pi)
            )
            active[at, columns] = out
            part_out[dim + width : dim + 2 * width, at] = out.T


def ffn_back_kernel(
    middle, slope, wu_own, wu, wd_own, wd, keep_rows, cots, gain_in,
    keep_out, send_out, gm_out, grad_branch,
    gain_rows, sems, grad_ffn,
):
    rows, dim = middle.shape
    width = wd.shape[0]
    mols = rows // SEQ
    core = places()[0]
    copies = copy_in((gain_in,), (gain_rows,), sems)

    def own_cots(m):
        at = pl.ds(pl.multiple_of(core * rows + m * SEQ, SEQ), SEQ)
        return jnp.where(keep_rows[at, 0:1] > 0.5, cots[at, :].astype(F32), 0.0)

    for m in range(mols):
        at = slice(m * SEQ, (m + 1) * SEQ)
        grad_ffn[at, :] = own_cots(m).astype(BF16)
    place_b = 0
    for side, (w_ref, part_out) in enumerate(((wd_own, keep_out), (wd, send_out))):
        columns = slice(side * width, (side + 1) * width)
        grad_before = slope[:, columns] * dot_nt(grad_ffn[...], w_ref[...])
        part_out[place_b : place_b + rows, :] = grad_before.astype(BF16)

    back = pl.ds(place_b, rows)
    gm_out[...] = dot_nt(keep_out[back, :], wu_own[...]) + dot_nt(send_out[back, :], wu[...])

    copies[0].wait()
    gain = row_of(gain_rows)
    nothing = jnp.zeros((1, dim), F32)
    sums = (nothing,) * 4
    for m in range(mols):
        at = slice(m * SEQ, (m + 1) * SEQ)
        grad_normed = gm_out[at, :]
        unit_rows, inverse = norm_parts(middle[at, :])
        grad_result = own_cots(m)
        grad = grad_result + norm_back(unit_rows, inverse, grad_normed * gain)
        gm_out[at, :] = grad
        grad_branch[at, :] = grad.astype(BF16)
        sums = (
            sums[0] + row_sum(grad),
            sums[1] + row_sum(grad_normed * unit_rows),
            sums[2] + row_sum(grad_normed),
            sums[3] + row_sum(grad_result),
        )

    place_m = place_b + rows
    for part_out in (keep_out, send_out):
        part_out[place_m : place_m + rows, :] = grad_branch[:, :width]
        part_out[place_m + rows : place_m + 2 * rows, :] = grad_branch[:, width:]
    small = jnp.concatenate(list(sums) + [nothing] * 12, axis=0)
    left, right = small[:, :width], small[:, width:]
    place_s = place_m + 2 * rows
    keep_out[place_s:, :] = jnp.where(core == 0, left, right).astype(BF16)
    send_out[place_s:, :] = jnp.where(core == 0, right, left).astype(BF16)


def result_kernel(middle, active, wd_own, wd, bias, result_out):
    width = wd.shape[0]
    result_out[...] = (
        middle[...]
        + dot(active[:, :width], wd_own[...])
        + dot(active[:, width:], wd[...])
        + row_of(bias)
    ).astype(BF16)


def branch_kernel(grad_branch, wo_own, wo, keep_rows, ga_own_out, ga_out):
    rows = grad_branch.shape[0]
    own_rows = pl.ds(pl.multiple_of(places()[0] * rows, SEQ), rows)
    keep = keep_rows[own_rows, 0:1] > 0.5
    for ref, weight in ((ga_own_out, wo_own), (ga_out, wo)):
        ref[...] = jnp.where(keep, dot_nt(grad_branch[...], weight[...]), 0.0).astype(BF16)


def attend_back_kernel(
    q_own, k_own, v_own, ga_own, q_got, k_got, v_got, ga_got, probs_all,
    keep_out, send_out, dq_t, dk, dv, slopes,
):
    rows, width = q_own.shape
    pairs = width // (2 * HDIM)
    windows = head_windows(width)
    sides = (
        (q_own, k_own, v_own, ga_own, keep_out),
        (q_got, k_got, v_got, ga_got, send_out),
    )
    units = [(m, side) for m in range(rows // SEQ) for side in (0, 1)]

    def score_back(unit, pair):
        m, side = unit
        at = slice(m * SEQ, (m + 1) * SEQ)
        low, high = windows[pair]
        both_g = split_heads(sides[side][3][at, :], pair, windows[pair])
        probs_low = probs_all[m, side * pairs + pair]
        probs = probs_low.astype(F32)
        grad_probs = dot_nt(sides[side][2][at, low:high], both_g)
        inner = row_sum(probs * grad_probs)
        slopes[side, pair] = (probs * (grad_probs - inner)).astype(BF16)
        dv[side, :, low:high] += dot(probs_low, both_g)

    def rows_back(unit, pair, keys_t):
        m, side = unit
        low, high = windows[pair]
        grad_scores = slopes[side, pair]
        both_q = split_heads(sides[side][0][m * SEQ : (m + 1) * SEQ, :], pair, windows[pair])
        dk[side, :, low:high] += dot(grad_scores, both_q)
        first = pair * 2 * HDIM
        out = dot(keys_t[first : first + 2 * HDIM], grad_scores)
        dq_t[side, first : first + HDIM, :] = out[:HDIM, :SEQ]
        dq_t[side, first + HDIM : first + 2 * HDIM, :] = out[HDIM:, SEQ:]

    def begin(unit):
        dk[unit[1]] = jnp.zeros_like(dk[unit[1]])
        dv[unit[1]] = jnp.zeros_like(dv[unit[1]])

    def finish(unit):
        m, side = unit
        part_out = sides[side][4]
        base = m * SEQ
        part_out[base : base + SEQ, :] = (dq_t[side] * SCALE).astype(BF16).T
        part_out[rows + base : rows + base + SEQ, :] = (dk[side] * SCALE).astype(BF16)
        part_out[2 * rows + base : 2 * rows + base + SEQ, :] = dv[side].astype(BF16)

    begin(units[0])
    for pair in range(pairs):
        score_back(units[0], pair)
    for step, unit in enumerate(units):
        keys_t = sides[unit[1]][1][unit[0] * SEQ : (unit[0] + 1) * SEQ, :].T
        if step + 1 < len(units):
            begin(units[step + 1])
        for pair in range(pairs):
            rows_back(unit, pair, keys_t)
            if step + 1 < len(units):
                score_back(units[step + 1], pair)
        finish(unit)


def embed_back_kernel(*refs):
    (
        grads_own, grads,
        wq_own, wk_own, wv_own, w_q, w_k, w_v, ident, grad_middle,
        feats_in, nodes_in, w_ident_in, types_in, gain_in,
        features_out, keep_out, send_out,
        feats, nodes, w_ident, types, gain_rows, sems, grad_normed, small,
    ) = refs
    core = places()[0]
    rows = feats.shape[0]
    copies = copy_in(
        (
            feats_in.at[pl.ds(pl.multiple_of(core * rows, SEQ), rows), :], nodes_in,
            w_ident_in, types_in, gain_in,
        ),
        (feats, nodes, w_ident, types, gain_rows),
        sems,
    )
    rows, dim = feats.shape
    width = wq_own.shape[1]
    idw = ident.shape[0]
    total = None
    for part, weights in ((grads_own, (wq_own, wk_own, wv_own)), (grads, (w_q, w_k, w_v))):
        for place, weight in enumerate(weights):
            term = dot_nt(part[place * rows : (place + 1) * rows, :], weight[...])
            total = term if total is None else total + term
    grad_normed[...] = total
    mols = rows // SEQ
    small[...] = jnp.zeros_like(small)
    for copy in copies:
        copy.wait()
    gain = row_of(gain_rows)
    kinds = types[...].astype(F32)

    def molecule(m, carry):
        at = pl.ds(pl.multiple_of(m * SEQ, SEQ), SEQ)
        is_edge = positions(SEQ) >= nodes[core * mols + m]
        hidden = feats[at, :].astype(F32) + dot_tn(ident[:, at], w_ident[...])
        hidden = hidden + jnp.where(is_edge, kinds[1:2, :], kinds[0:1, :])
        unit, inverse = norm_parts(hidden)
        grad_rows = grad_normed[at, :]
        grad = grad_middle[at, :] + norm_back(unit, inverse, grad_rows * gain)
        features_out[at, :] = grad
        high = grad.astype(BF16)
        rest = (grad - high.astype(F32)).astype(BF16)
        picked = ident[:, at]
        small[:idw, :] += dot(picked, high) + dot(picked, rest)
        edge_rows = jnp.where(is_edge, grad, 0.0)
        small[idw : idw + 1, :] += row_sum(grad - edge_rows)
        small[idw + 1 : idw + 2, :] += row_sum(edge_rows)
        small[idw + 2 : idw + 3, :] += row_sum(grad_rows * unit)
        small[idw + 3 : idw + 4, :] += row_sum(grad_rows)
        return carry

    lax.fori_loop(0, mols, molecule, 0)
    left, right = small[:, :width], small[:, width:]
    keep_out[...] = jnp.where(core == 0, left, right)
    send_out[...] = jnp.where(core == 0, right, left).astype(BF16)


def deal(unit, places_in, outs, block_at, small=None):
    _, inner, outer = places()
    first_kept, first_sent, second_kept, second_sent = outs
    for step in range(INNER):
        for turn in range(OUTER):
            if turn < 2:
                out, slot = (first_sent if step % 2 else first_kept), step // 2
            else:
                out, slot = (second_sent if step // 2 else second_kept), step % 2
            start = (slot * 2 + turn % 2) * places_in * unit
            for place in range(places_in):
                out[start + place * unit : start + (place + 1) * unit, :] = block_at(
                    inner ^ step, outer ^ turn, place
                )
    if small is not None:
        for out in (first_kept, first_sent):
            out[INNER * places_in * unit :, :] = small


def flat_block(flat, unit, dest, z):
    row = pl.multiple_of((dest * (OUTER // 2) + z // 2) * unit, 16)
    return flat[z % 2, pl.ds(row, unit), :]


def down_grads_kernel(kept, got, cots, keep_rows, *rest):
    outs, (flat, grad_ffn) = rest[:4], rest[4:]
    rows_all, dim = cots.shape
    rows, width = rows_all // 2, kept.shape[1]
    core = places()[0]
    for m in range(rows_all // SEQ):
        at = slice(m * SEQ, (m + 1) * SEQ)
        grad_ffn[at, :] = jnp.where(keep_rows[at, 0:1] > 0.5, cots[at, :].astype(F32), 0.0).astype(BF16)
    own_rows = pl.ds(pl.multiple_of(core * rows, SEQ), rows)
    other_rows = pl.ds(pl.multiple_of((1 - core) * rows, SEQ), rows)
    turned = slice(dim + width, dim + 2 * width)
    for half in (0, 1):
        columns = slice(half * width, (half + 1) * width)
        product = dot(kept[turned, :], grad_ffn[own_rows, columns])
        product = product + dot(got[turned, :], grad_ffn[other_rows, columns])
        flat[half] = product.astype(BF16)
    unit = dim // (INNER * OUTER)
    deal(unit, 1, outs, lambda dest, z, place: flat_block(flat, unit, dest, z))


def ffn_grads_kernel(kept, got, kept_back, got_back, *rest):
    outs, (tall, flat) = rest[:4], rest[4:]
    rows, width = kept.shape[1], kept.shape[1]
    dim = kept.shape[0] - 2 * width
    back, place_s = slice(0, rows), 3 * rows
    tall[...] = (
        dot(kept[:dim, :], kept_back[back, :]) + dot(got[:dim, :], got_back[back, :])
    ).astype(BF16)
    turned = slice(dim, dim + width)
    for half in (0, 1):
        mid = slice((1 + half) * rows, (2 + half) * rows)
        flat[half] = (
            dot(kept[turned, :], kept_back[mid, :]) + dot(got[turned, :], got_back[mid, :])
        ).astype(BF16)
    bias = row_sum(kept_back[back, :].astype(F32)) + row_sum(got_back[back, :].astype(F32))
    small = kept_back[place_s:, :].astype(F32) + got_back[place_s:, :].astype(F32)
    spot = lax.broadcasted_iota(jnp.int32, small.shape, 0)
    small = jnp.where(spot == 4, bias, small).astype(BF16)
    unit = dim // (INNER * OUTER)

    def block_at(dest, z, place):
        if place == 0:
            return tall[pl.ds(pl.multiple_of((dest * OUTER + z) * unit, 16), unit), :]
        return flat_block(flat, unit, dest, z)

    deal(unit, 2, outs, block_at, small)


def qkv_grads_kernel(normed_t, normed_t_got, kept, got, *refs):
    outs, small_out, (tall, normed, stacked) = refs[:4], refs[4], refs[5:]
    dim, rows = normed_t.shape
    unit = dim // (INNER * OUTER)
    normed[:, :rows] = normed_t[...]
    normed[:, rows:] = normed_t_got[...]
    spot = lax.broadcasted_iota(jnp.int32, small_out.shape, 0)
    small = jnp.zeros(small_out.shape, F32)
    for place in range(3):
        part = slice(place * rows, (place + 1) * rows)
        stacked[:rows, :] = kept[part, :]
        stacked[rows:, :] = got[part, :]
        tall[place] = dot(normed[...], stacked[...]).astype(BF16)
        if place != 1:
            small = jnp.where(spot == 36 + place // 2, row_sum(stacked[...].astype(F32)), small)
    small_out[...] = small

    def block_at(dest, z, place):
        return tall[place, pl.ds(pl.multiple_of((dest * OUTER + z) * unit, 16), unit), :]

    deal(unit, 3, outs, block_at)


def add(first, second):
    return (first.astype(F32) + second.astype(F32)).astype(BF16)


def plane_sum_kernel(first, first_got, second, second_got, *refs):
    late, (first_kept, first_sent, second_kept, second_sent) = refs[:-4], refs[-4:]
    pair = second_kept.shape[0]
    total = add(first[...], first_got[...])
    first_kept[:pair, :] = total[:pair]
    first_sent[:pair, :] = total[pair : 2 * pair]
    if late:
        small = (late[0][...] + late[1][...].astype(F32) + late[2][...]).astype(BF16)
    else:
        small = total[2 * pair :]
    first_kept[pair:, :] = small
    first_sent[pair:, :] = small
    total = add(second[...], second_got[...])
    second_kept[...] = total[:pair]
    second_sent[...] = total[pair:]


def plane_join_kernel(first, first_got, second, second_got, *refs):
    ahead, outs = refs[:4], refs[4:]
    unit = ahead[0].shape[0] // 4
    small = add(first[8 * unit :, :], first_got[8 * unit :, :])
    for place, (left, right, more, more_got) in enumerate(
        ((first, first_got, *ahead[:2]), (second, second_got, *ahead[2:]))
    ):
        total = add(left[: 8 * unit, :], right[: 8 * unit, :])
        late = add(more[...], more_got[...])
        for block in range(4):
            out = outs[2 * place + block // 2]
            start = block % 2 * 3 * unit
            out[start : start + 2 * unit, :] = total[2 * block * unit : 2 * (block + 1) * unit]
            out[start + 2 * unit : start + 3 * unit, :] = late[block * unit : (block + 1) * unit]
    for out in outs[:2]:
        out[6 * unit :, :] = small


def line_cut_kernel(first, first_got, second, second_got, own, near, middle, far):
    chunk = own.shape[0]
    total = add(first[...], first_got[...])
    own[...] = total[:chunk]
    near[...] = total[chunk:]
    total = add(second[...], second_got[...])
    middle[...] = total[:chunk]
    far[...] = total[chunk:]


def line_sum_kernel(own, near, near_got, middle_got, far_got, out, out_small):
    chunk = own.shape[0]
    total = own[...].astype(F32) + near_got[:chunk, :].astype(F32)
    total = total + middle_got[...].astype(F32) + far_got[...].astype(F32)
    out[...] = total.astype(BF16)
    out_small[:chunk, :] = total.astype(BF16)
    out_small[chunk:, :] = add(near[chunk:, :], near_got[chunk:, :])


def line_half_kernel(own, got, out, small_out):
    chunk = out.shape[0] // 2
    out[:chunk, :] = own[:chunk, :]
    out[chunk:, :] = got[:chunk, :]
    small_out[...] = own[chunk:, :].astype(F32) + got[chunk:, :].astype(F32)


def line_whole_kernel(first, second, out):
    out[: first.shape[0], :] = first[...]
    out[first.shape[0] :, :] = second[...]


def line_join_kernel(own, near, middle, far, line_x, line_y, small_out):
    chunk = near.shape[0]
    small = own[chunk:, :].astype(F32) + middle[chunk:, :].astype(F32)
    small_out[...] = small
    for out in (line_x, line_y):
        for turn, part in enumerate((own, near, middle, far)):
            out[turn * chunk : (turn + 1) * chunk, :] = part[:chunk, :]
    line_x[OUTER * chunk :, :] = small.astype(BF16)


def place_kernel(split_second, turns, *refs):
    outs, parts = refs[-3:], refs[:-3]
    own = parts[0]
    steps = min(len(parts), INNER)
    _, inner, outer = places()
    unit = own.shape[0] // (3 * OUTER)
    width = own.shape[1]
    for step in range(steps):
        for slot, turn in enumerate(turns):
            ref, start = parts[step], slot * 3 * unit
            if step == 3 and slot >= 2:
                ref, start = parts[4], (slot - 2) * 3 * unit
            dest, z = inner ^ step, outer ^ turn
            tall = pl.ds(pl.multiple_of((dest * OUTER + z) * unit, 16), unit)
            flat = pl.ds(pl.multiple_of((dest * (OUTER // 2) + z // 2) * unit, 16), unit)
            columns = pl.ds(pl.multiple_of(z % 2 * width, LANES), width)
            for place in range(3):
                part = ref[start + place * unit : start + (place + 1) * unit, :].astype(F32)
                if split_second and place > 0:
                    outs[place][flat, columns] = part
                else:
                    outs[place][tall, :] = part


def corner_kernel(first, second, *refs):
    outs, blocks, sems = refs[3:6], refs[6], refs[7]
    _, inner, outer = places()
    unit = first.shape[0] // 6
    size = OUTER * unit
    for turn in range(OUTER):
        ref, start = (first, turn * 3 * unit) if turn < 2 else (second, (turn - 2) * 3 * unit)
        at = pl.ds(pl.multiple_of((outer ^ turn) * unit, 16), unit)
        for place in range(3):
            rows = slice(start + place * unit, start + (place + 1) * unit)
            blocks[place, at, :] = ref[rows, :].astype(F32)
    at = pl.ds(pl.multiple_of((inner ^ 3) * size, 64), size)
    copies = copy_in(
        [blocks.at[place] for place in range(3)], [out.at[at, :] for out in outs], sems
    )
    for copy in copies:
        copy.wait()


def finish_first_kernel(small, got, bias_out, gain, shift, bias_down, bias_up):
    core = places()[0]
    for place, ref in enumerate((bias_out, gain, shift, bias_down)):
        mine, other = small[place : place + 1, :], got[place : place + 1, :]
        left = jnp.where(core == 0, mine, other)
        put_row(ref, jnp.concatenate([left, jnp.where(core == 0, other, mine)], axis=1))
    put_row(bias_up, small[4:5, :])


def finish_second_kernel(small, extra, got, w_ident, types, gain, shift, bias_q, bias_v):
    idw = w_ident.shape[0]
    core = places()[0]
    mine, other = small[...] + extra[...].astype(F32), got[...]
    left = jnp.where(core == 0, mine, other)
    total = jnp.concatenate([left, jnp.where(core == 0, other, mine)], axis=1)
    w_ident[...] = total[:idw]
    types[...] = total[idw : idw + 2]
    put_row(gain, total[idw + 2 : idw + 3])
    put_row(shift, total[idw + 3 : idw + 4])
    put_row(bias_q, mine[idw + 4 : idw + 5])
    put_row(bias_v, mine[idw + 5 : idw + 6])


def per_device(
    features, lap_vectors, node_counts, edge_counts, endpoints, w_ident, type_table,
    gain_one, shift_one, w_query, w_key, w_value, bias_query, bias_value, w_out, bias_out,
    gain_two, shift_two, w_up, bias_up, w_down, bias_down, cotangent,
):
    dp_count = lax.axis_size("dp")
    dp_index = lax.axis_index("dp")
    mp_index = lax.axis_index("mp")
    block = INNER * OUTER
    rest_count = dp_count // block
    def swap(part):
        return lax.ppermute(part, "mp", [(0, 1), (1, 0)])

    def inner_move(part, step):
        return lax.ppermute(part, "dp", [(s, s ^ step) for s in range(dp_count)])

    def outer_move(part, step):
        return lax.ppermute(part, "dp", [(s, s ^ (step * INNER)) for s in range(dp_count)])

    rows_all, dim = features.shape
    rows = rows_all // 2
    mols = rows // SEQ
    width = w_query.shape[1]
    heads = width // HDIM
    lapk = lap_vectors.shape[1]
    idw = w_ident.shape[0]

    def pinned(part):
        return pltpu.with_memory_space_constraint(part, pltpu.HBM)

    def lanes(part):
        return pinned(part.reshape(-1, LANES))

    nodes, edges = pinned(node_counts), pinned(edge_counts)
    count_scratch = pltpu.SMEM(node_counts.shape, jnp.int32)
    wide_scratch = pltpu.VMEM((dim // LANES, LANES), BF16)
    half_scratch = pltpu.VMEM((width // LANES, LANES), BF16)
    embed_args = (
        pinned(features), pinned(lap_vectors.T), pinned(endpoints.T), nodes,
        pinned(w_ident), pinned(type_table), lanes(gain_one), lanes(shift_one),
    )
    embed_scratch = [
        pltpu.VMEM((rows, dim), BF16),
        pltpu.VMEM((lapk, rows), BF16),
        pltpu.VMEM((2, rows), jnp.int32),
        count_scratch,
        pltpu.VMEM((idw, dim), BF16),
        pltpu.VMEM((2, dim), BF16),
        wide_scratch,
        wide_scratch,
    ]

    wq_got, wk_got, wv_got = swap(w_query), swap(w_key), swap(w_value)
    bq_got, bv_got, bu_got = swap(bias_query), swap(bias_value), swap(bias_up)
    wo_got, wu_got, wd_got = swap(w_out), swap(w_up), swap(w_down)

    hidden, ident, normed, normed_t, q_own, k_own, v_own, keep_rows = call(
        embed_kernel,
        (
            *embed_args, lanes(bias_query), lanes(bias_value),
            pinned(w_query), pinned(w_key), pinned(w_value), edges,
        ),
        [outside()] * 14,
        [
            ((rows, dim), F32),
            ((idw, rows), BF16),
            ((rows, dim), BF16),
            ((dim, rows), BF16),
            ((rows, width), BF16),
            ((rows, width), BF16),
            ((rows, width), BF16),
            ((rows_all, LANES), F32),
        ],
        scratch=embed_scratch
        + [half_scratch] * 2
        + [pltpu.VMEM((dim, width), BF16)] * 3
        + [count_scratch, pltpu.SemaphoreType.DMA((14,))],
    )
    ahead_rows, back_rows = dim + 2 * width, 3 * rows + 16
    q_got, k_got, v_got, probs, kept_a, sent_a, middle, active, slope = call(
        forward_kernel,
        (
            hidden, normed, q_own, k_own, v_own, wq_got, wk_got, wv_got,
            w_out, wo_got, w_up, wu_got,
            *(part.reshape(-1, LANES) for part in (bq_got, bv_got, bu_got)),
            nodes, edges,
            lanes(bias_up), lanes(bias_out), lanes(gain_two), lanes(shift_two),
        ),
        [whole()] * 15 + [outside()] * 6,
        [
            ((rows, width), BF16),
            ((rows, width), BF16),
            ((rows, width), BF16),
            ((mols, heads, SEQ, 2 * SEQ), BF16),
            ((ahead_rows, width), BF16),
            ((ahead_rows, width), BF16),
            ((rows, dim), F32),
            ((rows, dim), BF16),
            ((rows, dim), F32),
        ],
        scratch=[
            count_scratch,
            count_scratch,
            half_scratch,
            wide_scratch,
            wide_scratch,
            wide_scratch,
            pltpu.SemaphoreType.DMA((6,)),
            pltpu.VMEM((2, width, SEQ), F32),
            pltpu.VMEM((rows, dim), BF16),
            pltpu.VMEM((rows, dim), BF16),
        ],
        limit=30,
    )
    got_a = swap(sent_a)
    kept_back, sent_back, grad_middle, grad_branch = call(
        ffn_back_kernel,
        (
            middle, slope, w_up, wu_got, w_down, wd_got, keep_rows, cotangent,
            lanes(gain_two),
        ),
        [whole()] * 8 + [outside()],
        [
            ((back_rows, width), BF16),
            ((back_rows, width), BF16),
            ((rows, dim), F32),
            ((rows, dim), BF16),
        ],
        scratch=[wide_scratch, pltpu.SemaphoreType.DMA((1,)), pltpu.VMEM((rows, dim), BF16)],
    )
    got_back = swap(sent_back)

    unit = dim // block
    chunk = 3 * unit
    small_a, small_b = 16, 48

    def rest_sum(part):
        if rest_count == 1:
            return part
        groups = [[r * block + s for r in range(rest_count)] for s in range(block)]
        return lax.psum(part.astype(F32), "dp", axis_index_groups=groups).astype(part.dtype)

    pair = 2 * chunk

    def after(part, *others):
        return lax.optimization_barrier((part, *others))[0]

    def plane_step(parts, small_rows, late=(), others=(), micros=0):
        first, first_sent, second, second_sent = parts
        first_got = after(inner_move(first_sent, 1), *others)
        second_got = after(inner_move(second_sent, 2), *others)
        return call(
            plane_sum_kernel,
            (first, first_got, second, second_got, *late),
            [whole()] * (4 + len(late)),
            [((pair + small_rows, width), BF16)] * 2 + [((pair, width), BF16)] * 2,
            micros=micros,
        )

    def plane_turn(parts, others=(), micros=0):
        first, first_sent, second, second_sent = parts
        first_got = after(inner_move(first_sent, 2), *others)
        second_got = after(inner_move(second_sent, 1), *others)
        return call(
            line_cut_kernel,
            (first, first_got, second, second_got),
            [whole()] * 4,
            [
                ((chunk, width), BF16),
                ((first.shape[0] - chunk, width), BF16),
                ((chunk, width), BF16),
                ((chunk, width), BF16),
            ],
            micros=micros,
        )

    def line_step(parts, others=(), micros=0):
        got = [after(outer_move(parts[turn], turn), *others) for turn in range(1, OUTER)]
        mine, both = call(
            line_sum_kernel,
            (parts[0], parts[1], *got),
            [whole()] * 5,
            [((chunk, width), BF16), (parts[1].shape, BF16)],
            micros=micros,
        )
        if rest_count > 1:
            both = rest_sum(both)
            mine = both[:chunk]
        return mine, both

    def line_back(mine, both, others=(), micros=0):
        sent = (mine, both, mine)
        got = [after(outer_move(sent[turn - 1], turn), *others) for turn in range(1, OUTER)]
        small_rows = both.shape[0] - chunk
        return call(
            line_join_kernel,
            (both, *got),
            [whole()] * OUTER,
            [
                ((OUTER * chunk + small_rows, width), BF16),
                ((OUTER * chunk, width), BF16),
                ((small_rows, width), F32),
            ],
            micros=micros,
        )

    def line_back_pairs(both, others=(), later=(), half_micros=0, micros=0):
        got = after(outer_move(both, 2), *others)
        half, small = call(
            line_half_kernel,
            (both, got),
            [whole()] * 2,
            [((2 * chunk, width), BF16), ((both.shape[0] - chunk, width), F32)],
            micros=half_micros,
        )
        line = call(
            line_whole_kernel,
            (half, after(outer_move(half, 1), *later)),
            [whole()] * 2,
            [((OUTER * chunk, width), BF16)],
            micros=micros,
        )[0]
        return line, small

    def plane_back(lines):
        return inner_move(lines[0], 1), inner_move(lines[1], 2)

    def plane_back_turn(side_x, side_y):
        return inner_move(side_y[:pair], 1), inner_move(side_x[pair : 2 * pair], 2)

    def placed(planes, split_second, turns, micros=0):
        tall, flat = ((dim, width), F32), ((width, dim), F32)
        return call(
            lambda *refs: place_kernel(split_second, turns, *refs),
            planes,
            [whole()] * len(planes),
            [tall, flat, flat] if split_second else [tall] * 3,
            micros=micros,
        )

    parts_down = call(
        down_grads_kernel,
        (after(kept_a, grad_branch), got_a, cotangent, keep_rows),
        [whole()] * 4,
        [((INNER * unit, width), BF16)] * 4,
        scratch=[pltpu.VMEM((2, width, width), BF16), pltpu.VMEM((rows_all, dim), BF16)],
    )
    parts_a = call(
        ffn_grads_kernel,
        (after(kept_a, parts_down[0]), got_a, kept_back, got_back),
        [whole()] * 4,
        [((2 * INNER * unit + small_a, width), BF16)] * 2 + [((2 * INNER * unit, width), BF16)] * 2,
        scratch=[pltpu.VMEM((dim, width), BF16), pltpu.VMEM((2, width, width), BF16)],
    )
    ahead = [
        after(inner_move(parts_down[1], 1), parts_a[0]),
        after(inner_move(parts_down[3], 2), parts_a[0]),
    ]
    ga_own, ga_got = call(
        branch_kernel,
        (after(grad_branch, parts_a[0], *ahead), w_out, wo_got, keep_rows),
        [whole()] * 4,
        [((rows, width), BF16), ((rows, width), BF16)],
    )

    kept_b, sent_b = call(
        attend_back_kernel,
        (q_own, k_own, v_own, ga_own, q_got, k_got, v_got, ga_got, probs),
        [whole()] * 9,
        [((3 * rows, width), BF16)] * 2,
        scratch=[
            pltpu.VMEM((2, width, SEQ), F32),
            pltpu.VMEM((2, SEQ, width), F32),
            pltpu.VMEM((2, SEQ, width), F32),
            pltpu.VMEM((2, heads // 2, SEQ, 2 * SEQ), BF16),
        ],
    )
    normed_t_got = swap(after(normed_t, parts_a[0]))
    got_b = swap(sent_b)
    moved = [after(inner_move(parts_a[1], 1), kept_b), after(inner_move(parts_a[3], 2), kept_b)]
    moved = moved + ahead
    steps_a = call(
        plane_join_kernel,
        (
            parts_a[0], moved[0], parts_a[2], moved[1],
            parts_down[0], moved[2], parts_down[2], moved[3],
        ),
        [whole()] * 8,
        [((pair + small_a, width), BF16)] * 2 + [((pair, width), BF16)] * 2,
        micros=6,
    )
    normed_t = after(normed_t, *steps_a)
    parts_b = call(
        qkv_grads_kernel,
        (normed_t, normed_t_got, kept_b, got_b),
        [whole()] * 4,
        [((INNER * chunk, width), BF16)] * 4 + [((small_b, width), F32)],
        scratch=[
            pltpu.VMEM((3, dim, width), BF16),
            pltpu.VMEM((dim, 2 * rows), BF16),
            pltpu.VMEM((2 * rows, width), BF16),
        ],
    )
    turned_a = plane_turn(steps_a, others=(parts_b[0],), micros=3)
    grad_middle = after(grad_middle, parts_b[0], *turned_a)
    grad_features, small_kept, small_sent = call(
        embed_back_kernel,
        (
            kept_b, sent_b, w_query, w_key, w_value, wq_got, wk_got, wv_got, ident,
            grad_middle, embed_args[0], nodes, *embed_args[4:7],
        ),
        [whole()] * 10 + [outside()] * 5,
        [((rows, dim), F32), ((small_b, width), F32), ((small_b, width), BF16)],
        scratch=[
            pltpu.VMEM((rows, dim), BF16),
            count_scratch,
            pltpu.VMEM((idw, dim), BF16),
            pltpu.VMEM((2, dim), BF16),
            wide_scratch,
            pltpu.SemaphoreType.DMA((5,)),
            pltpu.VMEM((rows, dim), F32),
            pltpu.VMEM((small_b, dim), F32),
        ],
        micros=0,
    )
    small_got = swap(small_sent)
    steps_b = plane_step(parts_b[:4], small_b, late=(small_kept, small_got, parts_b[4]))
    line_a = line_step(turned_a, others=steps_b, micros=3)
    turned_b = plane_turn(steps_b, others=line_a[:1], micros=0)
    line_b = line_step(turned_b, micros=12)
    line_all_a, small_sum_a = line_back_pairs(
        line_a[1], others=turned_b, later=line_b, half_micros=1, micros=5
    )
    sides_a = plane_back((line_all_a, line_all_a))
    far_a = plane_back_turn(*sides_a)
    planes_a = (line_all_a, *sides_a, *far_a)
    lines_b = line_back(*line_b, micros=2)
    result = call(
        result_kernel,
        (middle, active, w_down, wd_got, lanes(after(bias_down, lines_b[1]))),
        [whole()] * 5,
        [((rows, dim), BF16)],
    )[0]
    wide, half = ((dim // LANES, LANES), F32), ((width // LANES, LANES), F32)
    sums_a = call(
        finish_first_kernel,
        (small_sum_a, swap(after(small_sum_a, lines_b[1]))),
        [whole()] * 2,
        [wide] * 4 + [half],
    )
    grad_w_up, grad_w_out, grad_w_down = placed(planes_a, True, (0, 2, 1, 3), micros=10)
    sides_b = plane_back(lines_b)
    sides_b, _ = lax.optimization_barrier((sides_b, (result, sums_a, grad_w_up)))
    near_b = placed((lines_b[1], sides_b[0], sides_b[1]), False, (0, 1, 2, 3))
    far_b = plane_back_turn(*sides_b)
    far_b, near_b = lax.optimization_barrier((far_b, near_b))
    extra = sides_b[0][OUTER * chunk :]
    own_b = lines_b[2] + extra.astype(F32)
    sums_b = call(
        finish_second_kernel,
        (lines_b[2], extra, swap(own_b)),
        [whole()] * 3,
        [((idw, dim), F32), ((2, dim), F32), wide, wide, half, half],
    )
    grad_w_query, grad_w_key, grad_w_value = call(
        corner_kernel,
        (*far_b, *near_b),
        [whole()] * 2 + [outside()] * 3,
        [((dim, width), F32)] * 3,
        scratch=[
            pltpu.VMEM((3, dim // INNER, width), F32),
            pltpu.SemaphoreType.DMA((3,)),
        ],
        in_place={2: 0, 3: 1, 4: 2},
    )
    return (
        result,
        grad_features,
        sums_b[0],
        sums_b[1],
        sums_b[2].reshape(-1),
        sums_b[3].reshape(-1),
        grad_w_query,
        grad_w_key,
        grad_w_value,
        sums_b[4].reshape(-1),
        sums_b[5].reshape(-1),
        grad_w_out,
        sums_a[0].reshape(-1),
        sums_a[1].reshape(-1),
        sums_a[2].reshape(-1),
        grad_w_up,
        sums_a[4].reshape(-1),
        grad_w_down,
        sums_a[3].reshape(-1),
    )


def solution(mesh):
    token, split = P("dp", None), P(("dp", "mp"), None)
    columns, lines, cut, copy = P(None, "mp"), P("mp", None), P("mp"), P()
    return jax.shard_map(
        per_device,
        mesh=mesh,
        in_specs=(
            token, token, P("dp"), P("dp"), token, copy, copy, copy, copy, columns, columns,
            columns, cut, cut, lines, copy, copy, copy, columns, cut, lines, copy, token,
        ),
        out_specs=(
            split, split, copy, copy, copy, copy, columns, columns, columns, cut, cut, lines,
            copy, copy, copy, columns, cut, lines, copy,
        ),
        check_vma=False,
    )
```

```python
import math

import jax
import jax.numpy as jnp
from jax import lax
from jax.experimental import pallas as pl
from jax.experimental.pallas import tpu as pltpu
from jax.sharding import PartitionSpec as P

HDIM = 24
SEQ = 128
LANES = 128
INNER = 4
OUTER = 4
EPSILON = 1e-05
SCALE = 1.0 / math.sqrt(HDIM)
LOG2_SCALE = SCALE * math.log2(math.e)
F32, BF16 = jnp.float32, jnp.bfloat16
MIB = 1024 * 1024


def dot(left, right):
    return jnp.dot(left, right, preferred_element_type=F32)


def dot_nt(left, right):
    return lax.dot_general(left, right, (((1,), (1,)), ((), ())), preferred_element_type=F32)


def dot_tn(left, right):
    return lax.dot_general(left, right, (((0,), (0,)), ((), ())), preferred_element_type=F32)


def norm_parts(hidden):
    average = jnp.mean(hidden, axis=-1, keepdims=True)
    centred = hidden - average
    inverse = lax.rsqrt(jnp.mean(centred * centred, axis=-1, keepdims=True) + EPSILON)
    return centred * inverse, inverse


def norm_back(unit, inverse, grad_hat):
    return inverse * (
        grad_hat
        - jnp.mean(grad_hat, axis=-1, keepdims=True)
        - unit * jnp.mean(grad_hat * unit, axis=-1, keepdims=True)
    )


def row_sum(block):
    return jnp.sum(block, axis=0, keepdims=True)


def positions(length):
    return lax.broadcasted_iota(jnp.int32, (length, 1), 0)


def whole():
    return pl.BlockSpec(memory_space=pltpu.VMEM)


def outside():
    return pl.BlockSpec(memory_space=pltpu.HBM)


def places():
    index = lax.axis_index("dp")
    return lax.axis_index("mp"), index % INNER, index // INNER % OUTER


def copy_in(sources, targets, sems):
    copies = [
        pltpu.make_async_copy(source, target, sems.at[place])
        for place, (source, target) in enumerate(zip(sources, targets))
    ]
    for copy in copies:
        copy.start()
    return copies


def row_of(ref):
    block = ref[...].astype(F32)
    return jnp.concatenate([block[r : r + 1, :] for r in range(block.shape[0])], axis=1)


def put_row(ref, row):
    for r in range(ref.shape[0]):
        ref[r : r + 1, :] = row[:, r * LANES : (r + 1) * LANES]


def call(kernel, args, specs, outs, scratch=(), micros=0, limit=24, in_place=None):
    return pl.pallas_call(
        kernel,
        out_shape=[jax.ShapeDtypeStruct(shape, kind) for shape, kind in outs],
        in_specs=specs,
        out_specs=[outside() if in_place else whole() for _ in outs],
        input_output_aliases=in_place or {},
        scratch_shapes=list(scratch),
        compiler_params=pltpu.CompilerParams(vmem_limit_bytes=limit * MIB),
        cost_estimate=pl.CostEstimate(
            flops=micros * 1_000_000_000, bytes_accessed=0, transcendentals=0
        ),
    )(*args)


def head_windows(width):
    windows = []
    for pair in range(width // (2 * HDIM)):
        low = pair * 2 * HDIM // LANES * LANES
        high = -(-(pair + 1) * 2 * HDIM // LANES) * LANES
        windows.append((low, high))
    return windows


def split_heads(block, pair, window):
    low, high = window
    part = block[:, low:high]
    column = low + lax.broadcasted_iota(jnp.int32, (16, high - low), 1)
    sides = []
    for head in (2 * pair, 2 * pair + 1):
        inside = (column >= head * HDIM) & (column < (head + 1) * HDIM)
        mask = jnp.where(inside, 1.0, 0.0).astype(BF16)
        sides.append(part * jnp.concatenate([mask] * (block.shape[0] // 16), axis=0))
    return jnp.concatenate(sides, axis=0)


def embed_rows(feats, lap, ends, w_ident, types, gain, shift, at, count):
    table = lap[:, at]
    slot = lax.broadcasted_iota(jnp.int32, (SEQ, SEQ), 0)
    picked = []
    for end in (0, 1):
        pick = jnp.where(ends[end : end + 1, at] == slot, 1.0, 0.0).astype(BF16)
        picked.append(dot(table, pick))
    ident = jnp.concatenate(picked, axis=0).astype(BF16)
    hidden = feats[at, :].astype(F32) + dot_tn(ident, w_ident[...])
    kinds = types[...].astype(F32)
    hidden = hidden + jnp.where(positions(SEQ) >= count, kinds[1:2, :], kinds[0:1, :])
    unit, _ = norm_parts(hidden)
    return hidden, ident, (unit * gain + shift).astype(BF16)


def embed_kernel(
    feats_in, lap_in, ends_in, nodes_in, w_ident_in, types_in, gain_in, shift_in,
    bias_q_in, bias_v_in, wq_in, wk_in, wv_in, edges_in,
    hidden_out, ident_out, normed_out, normed_t_out, q_out, k_out, v_out, keep_out,
    feats, lap, ends, nodes, w_ident, types, gain_rows, shift_rows, bias_q, bias_v,
    w_q, w_k, w_v, edges, sems,
):
    rows, dim = feats.shape
    mols = rows // SEQ
    core = places()[0]
    own_rows = pl.ds(pl.multiple_of(core * rows, SEQ), rows)
    copies = copy_in(
        (
            feats_in.at[own_rows, :], lap_in.at[:, own_rows], ends_in.at[:, own_rows], nodes_in,
            w_ident_in, types_in, gain_in, shift_in, bias_q_in, bias_v_in, wq_in, wk_in, wv_in,
            edges_in,
        ),
        (
            feats, lap, ends, nodes, w_ident, types, gain_rows, shift_rows, bias_q, bias_v,
            w_q, w_k, w_v, edges,
        ),
        sems,
    )
    for copy in copies[:10]:
        copy.wait()
    gain, shift = row_of(gain_rows), row_of(shift_rows)

    def molecule(m):
        at = slice(m * SEQ, (m + 1) * SEQ)
        count = nodes[core * mols + m]
        hidden, ident, normed = embed_rows(
            feats, lap, ends, w_ident, types, gain, shift, at, count
        )
        ident_out[:, at] = ident
        hidden_out[at, :] = hidden
        normed_out[at, :] = normed
        normed_t_out[:, at] = normed.T

    for m in range(mols):
        molecule(m)
    normed = normed_out[...]
    copies[10].wait()
    q_out[...] = (dot(normed, w_q[...]) + row_of(bias_q)).astype(BF16)
    copies[11].wait()
    k_out[...] = dot(normed, w_k[...]).astype(BF16)
    copies[12].wait()
    v_out[...] = (dot(normed, w_v[...]) + row_of(bias_v)).astype(BF16)
    copies[13].wait()
    for m in range(2 * mols):
        inside = lax.broadcasted_iota(jnp.int32, (SEQ, LANES), 0) < nodes[m] + edges[m]
        keep_out[m * SEQ : (m + 1) * SEQ, :] = jnp.where(inside, 1.0, 0.0)


def forward_kernel(
    hidden, normed, q_own, k_own, v_own, w_q, w_k, w_v, wo_own, wo, wu_own, wu,
    bias_q, bias_v, bias_u,
    nodes_in, edges_in, bias_u_own_in, bias_o_in, gain_in, shift_in,
    q_out, k_out, v_out, probs_out, keep_out, send_out, middle, active, slope,
    nodes, edges, bias_u_own, bias_o, gain_rows, shift_rows, sems,
    mixed, attended, normed_two,
):
    rows, dim = hidden.shape
    width = q_own.shape[1]
    mols = rows // SEQ
    pairs = width // (2 * HDIM)
    windows = head_windows(width)
    core = places()[0]
    copies = copy_in(
        (nodes_in, edges_in, bias_u_own_in, bias_o_in, gain_in, shift_in),
        (nodes, edges, bias_u_own, bias_o, gain_rows, shift_rows),
        sems,
    )

    for copy in copies:
        copy.wait()
    gain, shift, bias_out = row_of(gain_rows), row_of(shift_rows), row_of(bias_o)

    sides = ((q_own, k_own, v_own, keep_out), (q_out, k_out, v_out, send_out))
    units = [(m, side) for side in (0, 1) for m in range(mols)]

    def weigh(unit, pair):
        m, side = unit
        at = slice(m * SEQ, (m + 1) * SEQ)
        place = core * mols + m
        key_keep = positions(SEQ) < nodes[place] + edges[place]
        low, high = windows[pair]
        both = split_heads(sides[side][0][at, :], pair, windows[pair])
        scores = dot_nt(sides[side][1][at, low:high], both)
        scores = jnp.where(key_keep, scores, -1e30)
        top = jnp.max(scores, axis=0, keepdims=True)
        raised = jnp.exp2((scores - top) * LOG2_SCALE)
        probs_out[m, side * pairs + pair] = (raised * (1.0 / row_sum(raised))).astype(BF16)

    def mix(step, pair, values_t):
        m, side = units[step]
        first = pair * 2 * HDIM
        out = dot(values_t[first : first + 2 * HDIM], probs_out[m, side * pairs + pair])
        mixed[step % 2, first : first + HDIM, :] = out[:HDIM, :SEQ]
        mixed[step % 2, first + HDIM : first + 2 * HDIM, :] = out[HDIM:, SEQ:]

    def keep_mixed(step):
        m, side = units[step]
        at = slice(m * SEQ, (m + 1) * SEQ)
        place = core * mols + m
        query_keep = lax.broadcasted_iota(jnp.int32, (1, SEQ), 1) < nodes[place] + edges[place]
        kept = jnp.where(query_keep, mixed[step % 2], 0.0).astype(BF16)
        sides[side][3][dim : dim + width, at] = kept
        attended[at, side * width : (side + 1) * width] = kept.T

    partner = ((q_out, w_q, bias_q), (k_out, w_k, None), (v_out, w_v, bias_v))
    for pair in range(pairs):
        weigh(units[0], pair)
        if pair % 2 == 0 and pair // 2 < len(partner):
            out, weight, bias = partner[pair // 2]
            rows_of = dot(normed[...], weight[...])
            out[...] = (rows_of if bias is None else rows_of + row_of(bias)).astype(BF16)
    for step, task in enumerate(units):
        values_t = sides[task[1]][2][task[0] * SEQ : (task[0] + 1) * SEQ, :].T
        for pair in range(pairs):
            mix(step, pair, values_t)
            if step + 1 < len(units):
                weigh(units[step + 1], pair)
        keep_mixed(step)
    middle[...] = (
        hidden[...] + dot(attended[:, :width], wo_own[...]) + dot(attended[:, width:], wo[...])
    )

    for m in range(mols):
        at = slice(m * SEQ, (m + 1) * SEQ)
        total = middle[at, :] + bias_out
        middle[at, :] = total
        unit_rows, _ = norm_parts(total)
        rows_two = (unit_rows * gain + shift).astype(BF16)
        normed_two[at, :] = rows_two
        turned = rows_two.T
        keep_out[:dim, at] = turned
        send_out[:dim, at] = turned

    for side, (w_ref, b_ref, part_out) in enumerate(
        ((wu_own, bias_u_own, keep_out), (wu, bias_u, send_out))
    ):
        columns = slice(side * width, (side + 1) * width)
        slope[:, columns] = dot(normed_two[...], w_ref[...]) + row_of(b_ref)

        for m in range(mols):
            at = slice(m * SEQ, (m + 1) * SEQ)
            before = slope[at, columns]
            phi = 0.5 * (1.0 + lax.erf(before * math.sqrt(0.5)))
            out = (before * phi).astype(BF16)
            slope[at, columns] = phi + before * jnp.exp(before * before * -0.5) * (
                1.0 / math.sqrt(2.0 * math.pi)
            )
            active[at, columns] = out
            part_out[dim + width : dim + 2 * width, at] = out.T


def ffn_back_kernel(
    middle, slope, wu_own, wu, wd_own, wd, keep_rows, cots, gain_in,
    keep_out, send_out, gm_out, grad_branch,
    gain_rows, sems, grad_ffn,
):
    rows, dim = middle.shape
    width = wd.shape[0]
    mols = rows // SEQ
    core = places()[0]
    copies = copy_in((gain_in,), (gain_rows,), sems)

    def own_cots(m):
        at = pl.ds(pl.multiple_of(core * rows + m * SEQ, SEQ), SEQ)
        return jnp.where(keep_rows[at, 0:1] > 0.5, cots[at, :].astype(F32), 0.0)

    for m in range(mols):
        at = slice(m * SEQ, (m + 1) * SEQ)
        grad_ffn[at, :] = own_cots(m).astype(BF16)
    place_b = 0
    for side, (w_ref, part_out) in enumerate(((wd_own, keep_out), (wd, send_out))):
        columns = slice(side * width, (side + 1) * width)
        grad_before = slope[:, columns] * dot_nt(grad_ffn[...], w_ref[...])
        part_out[place_b : place_b + rows, :] = grad_before.astype(BF16)

    back = pl.ds(place_b, rows)
    gm_out[...] = dot_nt(keep_out[back, :], wu_own[...]) + dot_nt(send_out[back, :], wu[...])

    copies[0].wait()
    gain = row_of(gain_rows)
    nothing = jnp.zeros((1, dim), F32)
    sums = (nothing,) * 4
    for m in range(mols):
        at = slice(m * SEQ, (m + 1) * SEQ)
        grad_normed = gm_out[at, :]
        unit_rows, inverse = norm_parts(middle[at, :])
        grad_result = own_cots(m)
        grad = grad_result + norm_back(unit_rows, inverse, grad_normed * gain)
        gm_out[at, :] = grad
        grad_branch[at, :] = grad.astype(BF16)
        sums = (
            sums[0] + row_sum(grad),
            sums[1] + row_sum(grad_normed * unit_rows),
            sums[2] + row_sum(grad_normed),
            sums[3] + row_sum(grad_result),
        )

    place_m = place_b + rows
    for part_out in (keep_out, send_out):
        part_out[place_m : place_m + rows, :] = grad_branch[:, :width]
        part_out[place_m + rows : place_m + 2 * rows, :] = grad_branch[:, width:]
    small = jnp.concatenate(list(sums) + [nothing] * 12, axis=0)
    left, right = small[:, :width], small[:, width:]
    place_s = place_m + 2 * rows
    keep_out[place_s:, :] = jnp.where(core == 0, left, right).astype(BF16)
    send_out[place_s:, :] = jnp.where(core == 0, right, left).astype(BF16)


def result_kernel(middle, active, wd_own, wd, bias, result_out):
    width = wd.shape[0]
    result_out[...] = (
        middle[...]
        + dot(active[:, :width], wd_own[...])
        + dot(active[:, width:], wd[...])
        + row_of(bias)
    ).astype(BF16)


def branch_kernel(grad_branch, wo_own, wo, keep_rows, ga_own_out, ga_out):
    rows = grad_branch.shape[0]
    own_rows = pl.ds(pl.multiple_of(places()[0] * rows, SEQ), rows)
    keep = keep_rows[own_rows, 0:1] > 0.5
    for ref, weight in ((ga_own_out, wo_own), (ga_out, wo)):
        ref[...] = jnp.where(keep, dot_nt(grad_branch[...], weight[...]), 0.0).astype(BF16)


def attend_back_kernel(
    q_own, k_own, v_own, ga_own, q_got, k_got, v_got, ga_got, probs_all,
    keep_out, send_out, dq_t, dk, dv, slopes,
):
    rows, width = q_own.shape
    pairs = width // (2 * HDIM)
    windows = head_windows(width)
    sides = (
        (q_own, k_own, v_own, ga_own, keep_out),
        (q_got, k_got, v_got, ga_got, send_out),
    )
    units = [(m, side) for m in range(rows // SEQ) for side in (0, 1)]

    def score_back(unit, pair):
        m, side = unit
        at = slice(m * SEQ, (m + 1) * SEQ)
        low, high = windows[pair]
        both_g = split_heads(sides[side][3][at, :], pair, windows[pair])
        probs_low = probs_all[m, side * pairs + pair]
        probs = probs_low.astype(F32)
        grad_probs = dot_nt(sides[side][2][at, low:high], both_g)
        inner = row_sum(probs * grad_probs)
        slopes[side, pair] = (probs * (grad_probs - inner)).astype(BF16)
        dv[side, :, low:high] += dot(probs_low, both_g)

    def rows_back(unit, pair, keys_t):
        m, side = unit
        low, high = windows[pair]
        grad_scores = slopes[side, pair]
        both_q = split_heads(sides[side][0][m * SEQ : (m + 1) * SEQ, :], pair, windows[pair])
        dk[side, :, low:high] += dot(grad_scores, both_q)
        first = pair * 2 * HDIM
        out = dot(keys_t[first : first + 2 * HDIM], grad_scores)
        dq_t[side, first : first + HDIM, :] = out[:HDIM, :SEQ]
        dq_t[side, first + HDIM : first + 2 * HDIM, :] = out[HDIM:, SEQ:]

    def begin(unit):
        dk[unit[1]] = jnp.zeros_like(dk[unit[1]])
        dv[unit[1]] = jnp.zeros_like(dv[unit[1]])

    def finish(unit):
        m, side = unit
        part_out = sides[side][4]
        base = m * SEQ
        part_out[base : base + SEQ, :] = (dq_t[side] * SCALE).astype(BF16).T
        part_out[rows + base : rows + base + SEQ, :] = (dk[side] * SCALE).astype(BF16)
        part_out[2 * rows + base : 2 * rows + base + SEQ, :] = dv[side].astype(BF16)

    begin(units[0])
    for pair in range(pairs):
        score_back(units[0], pair)
    for step, unit in enumerate(units):
        keys_t = sides[unit[1]][1][unit[0] * SEQ : (unit[0] + 1) * SEQ, :].T
        if step + 1 < len(units):
            begin(units[step + 1])
        for pair in range(pairs):
            rows_back(unit, pair, keys_t)
            if step + 1 < len(units):
                score_back(units[step + 1], pair)
        finish(unit)


def embed_back_kernel(*refs):
    (
        grads_own, grads,
        wq_own, wk_own, wv_own, w_q, w_k, w_v, ident, grad_middle,
        feats_in, nodes_in, w_ident_in, types_in, gain_in,
        features_out, keep_out, send_out,
        feats, nodes, w_ident, types, gain_rows, sems, grad_normed, small,
    ) = refs
    core = places()[0]
    rows = feats.shape[0]
    copies = copy_in(
        (
            feats_in.at[pl.ds(pl.multiple_of(core * rows, SEQ), rows), :], nodes_in,
            w_ident_in, types_in, gain_in,
        ),
        (feats, nodes, w_ident, types, gain_rows),
        sems,
    )
    rows, dim = feats.shape
    width = wq_own.shape[1]
    idw = ident.shape[0]
    total = None
    for part, weights in ((grads_own, (wq_own, wk_own, wv_own)), (grads, (w_q, w_k, w_v))):
        for place, weight in enumerate(weights):
            term = dot_nt(part[place * rows : (place + 1) * rows, :], weight[...])
            total = term if total is None else total + term
    grad_normed[...] = total
    mols = rows // SEQ
    small[...] = jnp.zeros_like(small)
    for copy in copies:
        copy.wait()
    gain = row_of(gain_rows)
    kinds = types[...].astype(F32)

    def molecule(m, carry):
        at = pl.ds(pl.multiple_of(m * SEQ, SEQ), SEQ)
        is_edge = positions(SEQ) >= nodes[core * mols + m]
        hidden = feats[at, :].astype(F32) + dot_tn(ident[:, at], w_ident[...])
        hidden = hidden + jnp.where(is_edge, kinds[1:2, :], kinds[0:1, :])
        unit, inverse = norm_parts(hidden)
        grad_rows = grad_normed[at, :]
        grad = grad_middle[at, :] + norm_back(unit, inverse, grad_rows * gain)
        features_out[at, :] = grad
        high = grad.astype(BF16)
        rest = (grad - high.astype(F32)).astype(BF16)
        picked = ident[:, at]
        small[:idw, :] += dot(picked, high) + dot(picked, rest)
        edge_rows = jnp.where(is_edge, grad, 0.0)
        small[idw : idw + 1, :] += row_sum(grad - edge_rows)
        small[idw + 1 : idw + 2, :] += row_sum(edge_rows)
        small[idw + 2 : idw + 3, :] += row_sum(grad_rows * unit)
        small[idw + 3 : idw + 4, :] += row_sum(grad_rows)
        return carry

    lax.fori_loop(0, mols, molecule, 0)
    left, right = small[:, :width], small[:, width:]
    keep_out[...] = jnp.where(core == 0, left, right)
    send_out[...] = jnp.where(core == 0, right, left).astype(BF16)


def deal(unit, places_in, outs, block_at, small=None):
    _, inner, outer = places()
    first_kept, first_sent, second_kept, second_sent = outs
    for step in range(INNER):
        for turn in range(OUTER):
            if turn < 2:
                out, slot = (first_sent if step % 2 else first_kept), step // 2
            else:
                out, slot = (second_sent if step // 2 else second_kept), step % 2
            start = (slot * 2 + turn % 2) * places_in * unit
            for place in range(places_in):
                out[start + place * unit : start + (place + 1) * unit, :] = block_at(
                    inner ^ step, outer ^ turn, place
                )
    if small is not None:
        for out in (first_kept, first_sent):
            out[INNER * places_in * unit :, :] = small


def flat_block(flat, unit, dest, z):
    row = pl.multiple_of((dest * (OUTER // 2) + z // 2) * unit, 16)
    return flat[z % 2, pl.ds(row, unit), :]


def down_grads_kernel(kept, got, cots, keep_rows, *rest):
    outs, (flat, grad_ffn) = rest[:4], rest[4:]
    rows_all, dim = cots.shape
    rows, width = rows_all // 2, kept.shape[1]
    core = places()[0]
    for m in range(rows_all // SEQ):
        at = slice(m * SEQ, (m + 1) * SEQ)
        grad_ffn[at, :] = jnp.where(keep_rows[at, 0:1] > 0.5, cots[at, :].astype(F32), 0.0).astype(BF16)
    own_rows = pl.ds(pl.multiple_of(core * rows, SEQ), rows)
    other_rows = pl.ds(pl.multiple_of((1 - core) * rows, SEQ), rows)
    turned = slice(dim + width, dim + 2 * width)
    for half in (0, 1):
        columns = slice(half * width, (half + 1) * width)
        product = dot(kept[turned, :], grad_ffn[own_rows, columns])
        product = product + dot(got[turned, :], grad_ffn[other_rows, columns])
        flat[half] = product.astype(BF16)
    unit = dim // (INNER * OUTER)
    deal(unit, 1, outs, lambda dest, z, place: flat_block(flat, unit, dest, z))


def ffn_grads_kernel(kept, got, kept_back, got_back, *rest):
    outs, (tall, flat) = rest[:4], rest[4:]
    rows, width = kept.shape[1], kept.shape[1]
    dim = kept.shape[0] - 2 * width
    back, place_s = slice(0, rows), 3 * rows
    tall[...] = (
        dot(kept[:dim, :], kept_back[back, :]) + dot(got[:dim, :], got_back[back, :])
    ).astype(BF16)
    turned = slice(dim, dim + width)
    for half in (0, 1):
        mid = slice((1 + half) * rows, (2 + half) * rows)
        flat[half] = (
            dot(kept[turned, :], kept_back[mid, :]) + dot(got[turned, :], got_back[mid, :])
        ).astype(BF16)
    bias = row_sum(kept_back[back, :].astype(F32)) + row_sum(got_back[back, :].astype(F32))
    small = kept_back[place_s:, :].astype(F32) + got_back[place_s:, :].astype(F32)
    spot = lax.broadcasted_iota(jnp.int32, small.shape, 0)
    small = jnp.where(spot == 4, bias, small).astype(BF16)
    unit = dim // (INNER * OUTER)

    def block_at(dest, z, place):
        if place == 0:
            return tall[pl.ds(pl.multiple_of((dest * OUTER + z) * unit, 16), unit), :]
        return flat_block(flat, unit, dest, z)

    deal(unit, 2, outs, block_at, small)


def qkv_grads_kernel(normed_t, normed_t_got, kept, got, *refs):
    outs, small_out, (tall, normed, stacked) = refs[:4], refs[4], refs[5:]
    dim, rows = normed_t.shape
    unit = dim // (INNER * OUTER)
    normed[:, :rows] = normed_t[...]
    normed[:, rows:] = normed_t_got[...]
    spot = lax.broadcasted_iota(jnp.int32, small_out.shape, 0)
    small = jnp.zeros(small_out.shape, F32)
    for place in range(3):
        part = slice(place * rows, (place + 1) * rows)
        stacked[:rows, :] = kept[part, :]
        stacked[rows:, :] = got[part, :]
        tall[place] = dot(normed[...], stacked[...]).astype(BF16)
        if place != 1:
            small = jnp.where(spot == 36 + place // 2, row_sum(stacked[...].astype(F32)), small)
    small_out[...] = small

    def block_at(dest, z, place):
        return tall[place, pl.ds(pl.multiple_of((dest * OUTER + z) * unit, 16), unit), :]

    deal(unit, 3, outs, block_at)


def add(first, second):
    return (first.astype(F32) + second.astype(F32)).astype(BF16)


def plane_sum_kernel(first, first_got, second, second_got, *refs):
    late, (first_kept, first_sent, second_kept, second_sent) = refs[:-4], refs[-4:]
    pair = second_kept.shape[0]
    total = add(first[...], first_got[...])
    first_kept[:pair, :] = total[:pair]
    first_sent[:pair, :] = total[pair : 2 * pair]
    if late:
        small = (late[0][...] + late[1][...].astype(F32) + late[2][...]).astype(BF16)
    else:
        small = total[2 * pair :]
    first_kept[pair:, :] = small
    first_sent[pair:, :] = small
    total = add(second[...], second_got[...])
    second_kept[...] = total[:pair]
    second_sent[...] = total[pair:]


def plane_join_kernel(first, first_got, second, second_got, *refs):
    ahead, outs = refs[:4], refs[4:]
    unit = ahead[0].shape[0] // 4
    small = add(first[8 * unit :, :], first_got[8 * unit :, :])
    for place, (left, right, more, more_got) in enumerate(
        ((first, first_got, *ahead[:2]), (second, second_got, *ahead[2:]))
    ):
        total = add(left[: 8 * unit, :], right[: 8 * unit, :])
        late = add(more[...], more_got[...])
        for block in range(4):
            out = outs[2 * place + block // 2]
            start = block % 2 * 3 * unit
            out[start : start + 2 * unit, :] = total[2 * block * unit : 2 * (block + 1) * unit]
            out[start + 2 * unit : start + 3 * unit, :] = late[block * unit : (block + 1) * unit]
    for out in outs[:2]:
        out[6 * unit :, :] = small


def line_cut_kernel(first, first_got, second, second_got, own, near, middle, far):
    chunk = own.shape[0]
    total = add(first[...], first_got[...])
    own[...] = total[:chunk]
    near[...] = total[chunk:]
    total = add(second[...], second_got[...])
    middle[...] = total[:chunk]
    far[...] = total[chunk:]


def line_sum_kernel(own, near, near_got, middle_got, far_got, out, out_small):
    chunk = own.shape[0]
    total = own[...].astype(F32) + near_got[:chunk, :].astype(F32)
    total = total + middle_got[...].astype(F32) + far_got[...].astype(F32)
    out[...] = total.astype(BF16)
    out_small[:chunk, :] = total.astype(BF16)
    out_small[chunk:, :] = add(near[chunk:, :], near_got[chunk:, :])


def line_half_kernel(own, got, out, small_out):
    chunk = out.shape[0] // 2
    out[:chunk, :] = own[:chunk, :]
    out[chunk:, :] = got[:chunk, :]
    small_out[...] = own[chunk:, :].astype(F32) + got[chunk:, :].astype(F32)


def line_whole_kernel(first, second, out):
    out[: first.shape[0], :] = first[...]
    out[first.shape[0] :, :] = second[...]


def line_join_kernel(own, near, middle, far, line_x, line_y, small_out):
    chunk = near.shape[0]
    small = own[chunk:, :].astype(F32) + middle[chunk:, :].astype(F32)
    small_out[...] = small
    for out in (line_x, line_y):
        for turn, part in enumerate((own, near, middle, far)):
            out[turn * chunk : (turn + 1) * chunk, :] = part[:chunk, :]
    line_x[OUTER * chunk :, :] = small.astype(BF16)


def place_kernel(split_second, turns, *refs):
    outs, parts = refs[-3:], refs[:-3]
    own = parts[0]
    steps = min(len(parts), INNER)
    _, inner, outer = places()
    unit = own.shape[0] // (3 * OUTER)
    width = own.shape[1]
    for step in range(steps):
        for slot, turn in enumerate(turns):
            ref, start = parts[step], slot * 3 * unit
            if step == 3 and slot >= 2:
                ref, start = parts[4], (slot - 2) * 3 * unit
            dest, z = inner ^ step, outer ^ turn
            tall = pl.ds(pl.multiple_of((dest * OUTER + z) * unit, 16), unit)
            flat = pl.ds(pl.multiple_of((dest * (OUTER // 2) + z // 2) * unit, 16), unit)
            columns = pl.ds(pl.multiple_of(z % 2 * width, LANES), width)
            for place in range(3):
                part = ref[start + place * unit : start + (place + 1) * unit, :].astype(F32)
                if split_second and place > 0:
                    outs[place][flat, columns] = part
                else:
                    outs[place][tall, :] = part


def corner_kernel(first, second, *refs):
    outs, blocks, sems = refs[3:6], refs[6], refs[7]
    _, inner, outer = places()
    unit = first.shape[0] // 6
    size = OUTER * unit
    for turn in range(OUTER):
        ref, start = (first, turn * 3 * unit) if turn < 2 else (second, (turn - 2) * 3 * unit)
        at = pl.ds(pl.multiple_of((outer ^ turn) * unit, 16), unit)
        for place in range(3):
            rows = slice(start + place * unit, start + (place + 1) * unit)
            blocks[place, at, :] = ref[rows, :].astype(F32)
    at = pl.ds(pl.multiple_of((inner ^ 3) * size, 64), size)
    copies = copy_in(
        [blocks.at[place] for place in range(3)], [out.at[at, :] for out in outs], sems
    )
    for copy in copies:
        copy.wait()


def finish_first_kernel(small, got, bias_out, gain, shift, bias_down, bias_up):
    core = places()[0]
    for place, ref in enumerate((bias_out, gain, shift, bias_down)):
        mine, other = small[place : place + 1, :], got[place : place + 1, :]
        left = jnp.where(core == 0, mine, other)
        put_row(ref, jnp.concatenate([left, jnp.where(core == 0, other, mine)], axis=1))
    put_row(bias_up, small[4:5, :])


def finish_second_kernel(small, extra, got, w_ident, types, gain, shift, bias_q, bias_v):
    idw = w_ident.shape[0]
    core = places()[0]
    mine, other = small[...] + extra[...].astype(F32), got[...]
    left = jnp.where(core == 0, mine, other)
    total = jnp.concatenate([left, jnp.where(core == 0, other, mine)], axis=1)
    w_ident[...] = total[:idw]
    types[...] = total[idw : idw + 2]
    put_row(gain, total[idw + 2 : idw + 3])
    put_row(shift, total[idw + 3 : idw + 4])
    put_row(bias_q, mine[idw + 4 : idw + 5])
    put_row(bias_v, mine[idw + 5 : idw + 6])


def per_device(
    features, lap_vectors, node_counts, edge_counts, endpoints, w_ident, type_table,
    gain_one, shift_one, w_query, w_key, w_value, bias_query, bias_value, w_out, bias_out,
    gain_two, shift_two, w_up, bias_up, w_down, bias_down, cotangent,
):
    dp_count = lax.axis_size("dp")
    dp_index = lax.axis_index("dp")
    mp_index = lax.axis_index("mp")
    block = INNER * OUTER
    rest_count = dp_count // block
    def swap(part):
        return lax.ppermute(part, "mp", [(0, 1), (1, 0)])

    def inner_move(part, step):
        return lax.ppermute(part, "dp", [(s, s ^ step) for s in range(dp_count)])

    def outer_move(part, step):
        return lax.ppermute(part, "dp", [(s, s ^ (step * INNER)) for s in range(dp_count)])

    rows_all, dim = features.shape
    rows = rows_all // 2
    mols = rows // SEQ
    width = w_query.shape[1]
    heads = width // HDIM
    lapk = lap_vectors.shape[1]
    idw = w_ident.shape[0]

    def pinned(part):
        return pltpu.with_memory_space_constraint(part, pltpu.HBM)

    def lanes(part):
        return pinned(part.reshape(-1, LANES))

    nodes, edges = pinned(node_counts), pinned(edge_counts)
    count_scratch = pltpu.SMEM(node_counts.shape, jnp.int32)
    wide_scratch = pltpu.VMEM((dim // LANES, LANES), BF16)
    half_scratch = pltpu.VMEM((width // LANES, LANES), BF16)
    def after(part, *others):
        return lax.optimization_barrier((part, *others))[0]

    bq_got, bv_got, bu_got = swap(bias_query), swap(bias_value), swap(bias_up)
    embed_args = (
        pinned(features), pinned(lap_vectors.T), pinned(endpoints.T), nodes,
        pinned(w_ident), pinned(type_table), lanes(gain_one), lanes(shift_one),
    )
    embed_scratch = [
        pltpu.VMEM((rows, dim), BF16),
        pltpu.VMEM((lapk, rows), BF16),
        pltpu.VMEM((2, rows), jnp.int32),
        count_scratch,
        pltpu.VMEM((idw, dim), BF16),
        pltpu.VMEM((2, dim), BF16),
        wide_scratch,
        wide_scratch,
    ]

    wq_got, wk_got, wv_got = swap(w_query), swap(w_key), swap(w_value)
    wo_got, wu_got = swap(w_out), swap(w_up)

    hidden, ident, normed, normed_t, q_own, k_own, v_own, keep_rows = call(
        embed_kernel,
        (
            *embed_args, lanes(bias_query), lanes(bias_value),
            pinned(w_query), pinned(w_key), pinned(w_value), edges,
        ),
        [outside()] * 14,
        [
            ((rows, dim), F32),
            ((idw, rows), BF16),
            ((rows, dim), BF16),
            ((dim, rows), BF16),
            ((rows, width), BF16),
            ((rows, width), BF16),
            ((rows, width), BF16),
            ((rows_all, LANES), F32),
        ],
        scratch=embed_scratch
        + [half_scratch] * 2
        + [pltpu.VMEM((dim, width), BF16)] * 3
        + [count_scratch, pltpu.SemaphoreType.DMA((14,))],
    )
    wd_got = swap(after(w_down, normed))
    ahead_rows, back_rows = dim + 2 * width, 3 * rows + 16
    q_got, k_got, v_got, probs, kept_a, sent_a, middle, active, slope = call(
        forward_kernel,
        (
            hidden, normed, q_own, k_own, v_own, wq_got, wk_got, wv_got,
            w_out, wo_got, w_up, wu_got,
            *(part.reshape(-1, LANES) for part in (bq_got, bv_got, bu_got)),
            nodes, edges,
            lanes(bias_up), lanes(bias_out), lanes(gain_two), lanes(shift_two),
        ),
        [whole()] * 15 + [outside()] * 6,
        [
            ((rows, width), BF16),
            ((rows, width), BF16),
            ((rows, width), BF16),
            ((mols, heads, SEQ, 2 * SEQ), BF16),
            ((ahead_rows, width), BF16),
            ((ahead_rows, width), BF16),
            ((rows, dim), F32),
            ((rows, dim), BF16),
            ((rows, dim), F32),
        ],
        scratch=[
            count_scratch,
            count_scratch,
            half_scratch,
            wide_scratch,
            wide_scratch,
            wide_scratch,
            pltpu.SemaphoreType.DMA((6,)),
            pltpu.VMEM((2, width, SEQ), F32),
            pltpu.VMEM((rows, dim), BF16),
            pltpu.VMEM((rows, dim), BF16),
        ],
        limit=30,
    )
    got_a = swap(sent_a)
    kept_back, sent_back, grad_middle, grad_branch = call(
        ffn_back_kernel,
        (
            middle, slope, w_up, wu_got, w_down, wd_got, keep_rows, cotangent,
            lanes(gain_two),
        ),
        [whole()] * 8 + [outside()],
        [
            ((back_rows, width), BF16),
            ((back_rows, width), BF16),
            ((rows, dim), F32),
            ((rows, dim), BF16),
        ],
        scratch=[wide_scratch, pltpu.SemaphoreType.DMA((1,)), pltpu.VMEM((rows, dim), BF16)],
    )
    got_back = swap(sent_back)

    unit = dim // block
    chunk = 3 * unit
    small_a, small_b = 16, 48

    def rest_sum(part):
        if rest_count == 1:
            return part
        groups = [[r * block + s for r in range(rest_count)] for s in range(block)]
        return lax.psum(part.astype(F32), "dp", axis_index_groups=groups).astype(part.dtype)

    pair = 2 * chunk

    def plane_step(parts, small_rows, late=(), others=(), micros=0):
        first, first_sent, second, second_sent = parts
        first_got = after(inner_move(first_sent, 1), *others)
        second_got = after(inner_move(second_sent, 2), *others)
        return call(
            plane_sum_kernel,
            (first, first_got, second, second_got, *late),
            [whole()] * (4 + len(late)),
            [((pair + small_rows, width), BF16)] * 2 + [((pair, width), BF16)] * 2,
            micros=micros,
        )

    def plane_turn(parts, others=(), micros=0):
        first, first_sent, second, second_sent = parts
        first_got = after(inner_move(first_sent, 2), *others)
        second_got = after(inner_move(second_sent, 1), *others)
        return call(
            line_cut_kernel,
            (first, first_got, second, second_got),
            [whole()] * 4,
            [
                ((chunk, width), BF16),
                ((first.shape[0] - chunk, width), BF16),
                ((chunk, width), BF16),
                ((chunk, width), BF16),
            ],
            micros=micros,
        )

    def line_step(parts, others=(), micros=0):
        got = [after(outer_move(parts[turn], turn), *others) for turn in range(1, OUTER)]
        mine, both = call(
            line_sum_kernel,
            (parts[0], parts[1], *got),
            [whole()] * 5,
            [((chunk, width), BF16), (parts[1].shape, BF16)],
            micros=micros,
        )
        if rest_count > 1:
            both = rest_sum(both)
            mine = both[:chunk]
        return mine, both

    def line_back(mine, both, others=(), micros=0):
        sent = (mine, both, mine)
        got = [after(outer_move(sent[turn - 1], turn), *others) for turn in range(1, OUTER)]
        small_rows = both.shape[0] - chunk
        return call(
            line_join_kernel,
            (both, *got),
            [whole()] * OUTER,
            [
                ((OUTER * chunk + small_rows, width), BF16),
                ((OUTER * chunk, width), BF16),
                ((small_rows, width), F32),
            ],
            micros=micros,
        )

    def line_back_pairs(both, others=(), half_micros=0, micros=0):
        got = after(outer_move(both, 2), *others)
        half, small = call(
            line_half_kernel,
            (both, got),
            [whole()] * 2,
            [((2 * chunk, width), BF16), ((both.shape[0] - chunk, width), F32)],
            micros=half_micros,
        )
        line = call(
            line_whole_kernel,
            (half, outer_move(half, 1)),
            [whole()] * 2,
            [((OUTER * chunk, width), BF16)],
            micros=micros,
        )[0]
        return line, small

    def plane_back(lines):
        return inner_move(lines[0], 1), inner_move(lines[1], 2)

    def plane_back_turn(side_x, side_y):
        return inner_move(side_y[:pair], 1), inner_move(side_x[pair : 2 * pair], 2)

    def placed(planes, split_second, turns, micros=0):
        tall, flat = ((dim, width), F32), ((width, dim), F32)
        return call(
            lambda *refs: place_kernel(split_second, turns, *refs),
            planes,
            [whole()] * len(planes),
            [tall, flat, flat] if split_second else [tall] * 3,
            micros=micros,
        )

    parts_down = call(
        down_grads_kernel,
        (after(kept_a, grad_branch), got_a, cotangent, keep_rows),
        [whole()] * 4,
        [((INNER * unit, width), BF16)] * 4,
        scratch=[pltpu.VMEM((2, width, width), BF16), pltpu.VMEM((rows_all, dim), BF16)],
    )
    parts_a = call(
        ffn_grads_kernel,
        (after(kept_a, parts_down[0]), got_a, kept_back, got_back),
        [whole()] * 4,
        [((2 * INNER * unit + small_a, width), BF16)] * 2 + [((2 * INNER * unit, width), BF16)] * 2,
        scratch=[pltpu.VMEM((dim, width), BF16), pltpu.VMEM((2, width, width), BF16)],
    )
    ahead = [
        after(inner_move(parts_down[1], 1), parts_a[0]),
        after(inner_move(parts_down[3], 2), parts_a[0]),
    ]
    ga_own, ga_got = call(
        branch_kernel,
        (after(grad_branch, parts_a[0], *ahead), w_out, wo_got, keep_rows),
        [whole()] * 4,
        [((rows, width), BF16), ((rows, width), BF16)],
    )

    kept_b, sent_b = call(
        attend_back_kernel,
        (q_own, k_own, v_own, ga_own, q_got, k_got, v_got, ga_got, probs),
        [whole()] * 9,
        [((3 * rows, width), BF16)] * 2,
        scratch=[
            pltpu.VMEM((2, width, SEQ), F32),
            pltpu.VMEM((2, SEQ, width), F32),
            pltpu.VMEM((2, SEQ, width), F32),
            pltpu.VMEM((2, heads // 2, SEQ, 2 * SEQ), BF16),
        ],
    )
    normed_t_got = swap(after(normed_t, parts_a[0]))
    got_b = swap(sent_b)
    moved = [after(inner_move(parts_a[1], 1), kept_b), after(inner_move(parts_a[3], 2), kept_b)]
    moved = moved + ahead
    steps_a = call(
        plane_join_kernel,
        (
            parts_a[0], moved[0], parts_a[2], moved[1],
            parts_down[0], moved[2], parts_down[2], moved[3],
        ),
        [whole()] * 8,
        [((pair + small_a, width), BF16)] * 2 + [((pair, width), BF16)] * 2,
        micros=6,
    )
    normed_t = after(normed_t, *steps_a)
    parts_b = call(
        qkv_grads_kernel,
        (normed_t, normed_t_got, kept_b, got_b),
        [whole()] * 4,
        [((INNER * chunk, width), BF16)] * 4 + [((small_b, width), F32)],
        scratch=[
            pltpu.VMEM((3, dim, width), BF16),
            pltpu.VMEM((dim, 2 * rows), BF16),
            pltpu.VMEM((2 * rows, width), BF16),
        ],
    )
    turned_a = plane_turn(steps_a, others=(parts_b[0],), micros=3)
    grad_middle = after(grad_middle, parts_b[0], *turned_a)
    grad_features, small_kept, small_sent = call(
        embed_back_kernel,
        (
            kept_b, sent_b, w_query, w_key, w_value, wq_got, wk_got, wv_got, ident,
            grad_middle, embed_args[0], nodes, *embed_args[4:7],
        ),
        [whole()] * 10 + [outside()] * 5,
        [((rows, dim), F32), ((small_b, width), F32), ((small_b, width), BF16)],
        scratch=[
            pltpu.VMEM((rows, dim), BF16),
            count_scratch,
            pltpu.VMEM((idw, dim), BF16),
            pltpu.VMEM((2, dim), BF16),
            wide_scratch,
            pltpu.SemaphoreType.DMA((5,)),
            pltpu.VMEM((rows, dim), F32),
            pltpu.VMEM((small_b, dim), F32),
        ],
        micros=0,
    )
    small_got = swap(small_sent)
    steps_b = plane_step(parts_b[:4], small_b, late=(small_kept, small_got, parts_b[4]))
    line_a = line_step(turned_a, others=steps_b, micros=3)
    turned_b = plane_turn(steps_b, others=line_a[:1], micros=0)
    line_all_a, small_sum_a = line_back_pairs(line_a[1], others=turned_b, half_micros=1, micros=5)
    line_b = line_step(turned_b, others=(line_all_a,), micros=12)
    sides_a = plane_back((line_all_a, line_all_a))
    far_a = plane_back_turn(*sides_a)
    planes_a = (line_all_a, *sides_a, *far_a)
    lines_b = line_back(*line_b, micros=2)
    result = call(
        result_kernel,
        (middle, active, w_down, wd_got, lanes(after(bias_down, lines_b[1]))),
        [whole()] * 5,
        [((rows, dim), BF16)],
    )[0]
    wide, half = ((dim // LANES, LANES), F32), ((width // LANES, LANES), F32)
    sums_a = call(
        finish_first_kernel,
        (small_sum_a, swap(after(small_sum_a, lines_b[1]))),
        [whole()] * 2,
        [wide] * 4 + [half],
    )
    grad_w_up, grad_w_out, grad_w_down = placed(planes_a, True, (0, 2, 1, 3), micros=10)
    sides_b = plane_back(lines_b)
    sides_b, _ = lax.optimization_barrier((sides_b, (result, sums_a, grad_w_up)))
    near_b = placed((lines_b[1], sides_b[0], sides_b[1]), False, (0, 1, 2, 3))
    far_b = plane_back_turn(*sides_b)
    far_b, near_b = lax.optimization_barrier((far_b, near_b))
    extra = sides_b[0][OUTER * chunk :]
    own_b = lines_b[2] + extra.astype(F32)
    sums_b = call(
        finish_second_kernel,
        (lines_b[2], extra, swap(own_b)),
        [whole()] * 3,
        [((idw, dim), F32), ((2, dim), F32), wide, wide, half, half],
    )
    grad_w_query, grad_w_key, grad_w_value = call(
        corner_kernel,
        (*far_b, *near_b),
        [whole()] * 2 + [outside()] * 3,
        [((dim, width), F32)] * 3,
        scratch=[
            pltpu.VMEM((3, dim // INNER, width), F32),
            pltpu.SemaphoreType.DMA((3,)),
        ],
        in_place={2: 0, 3: 1, 4: 2},
    )
    return (
        result,
        grad_features,
        sums_b[0],
        sums_b[1],
        sums_b[2].reshape(-1),
        sums_b[3].reshape(-1),
        grad_w_query,
        grad_w_key,
        grad_w_value,
        sums_b[4].reshape(-1),
        sums_b[5].reshape(-1),
        grad_w_out,
        sums_a[0].reshape(-1),
        sums_a[1].reshape(-1),
        sums_a[2].reshape(-1),
        grad_w_up,
        sums_a[4].reshape(-1),
        grad_w_down,
        sums_a[3].reshape(-1),
    )


def solution(mesh):
    token, split = P("dp", None), P(("dp", "mp"), None)
    columns, lines, cut, copy = P(None, "mp"), P("mp", None), P("mp"), P()
    return jax.shard_map(
        per_device,
        mesh=mesh,
        in_specs=(
            token, token, P("dp"), P("dp"), token, copy, copy, copy, copy, columns, columns,
            columns, cut, cut, lines, copy, copy, copy, columns, cut, lines, copy, token,
        ),
        out_specs=(
            split, split, copy, copy, copy, copy, columns, columns, columns, cut, cut, lines,
            copy, copy, copy, columns, cut, lines, copy,
        ),
        check_vma=False,
    )
```

```python
import math

import jax
import jax.numpy as jnp
from jax import lax
from jax.experimental import pallas as pl
from jax.experimental.pallas import tpu as pltpu
from jax.sharding import PartitionSpec as P

HDIM = 24
SEQ = 128
LANES = 128
INNER = 4
OUTER = 4
EPSILON = 1e-05
SCALE = 1.0 / math.sqrt(HDIM)
LOG2_SCALE = SCALE * math.log2(math.e)
F32, BF16 = jnp.float32, jnp.bfloat16
MIB = 1024 * 1024


def dot(left, right):
    return jnp.dot(left, right, preferred_element_type=F32)


def dot_nt(left, right):
    return lax.dot_general(left, right, (((1,), (1,)), ((), ())), preferred_element_type=F32)


def dot_tn(left, right):
    return lax.dot_general(left, right, (((0,), (0,)), ((), ())), preferred_element_type=F32)


def norm_parts(hidden):
    average = jnp.mean(hidden, axis=-1, keepdims=True)
    centred = hidden - average
    inverse = lax.rsqrt(jnp.mean(centred * centred, axis=-1, keepdims=True) + EPSILON)
    return centred * inverse, inverse


def norm_back(unit, inverse, grad_hat):
    return inverse * (
        grad_hat
        - jnp.mean(grad_hat, axis=-1, keepdims=True)
        - unit * jnp.mean(grad_hat * unit, axis=-1, keepdims=True)
    )


def row_sum(block):
    return jnp.sum(block, axis=0, keepdims=True)


def positions(length):
    return lax.broadcasted_iota(jnp.int32, (length, 1), 0)


def whole():
    return pl.BlockSpec(memory_space=pltpu.VMEM)


def outside():
    return pl.BlockSpec(memory_space=pltpu.HBM)


def places():
    index = lax.axis_index("dp")
    return lax.axis_index("mp"), index % INNER, index // INNER % OUTER


def copy_in(sources, targets, sems):
    copies = [
        pltpu.make_async_copy(source, target, sems.at[place])
        for place, (source, target) in enumerate(zip(sources, targets))
    ]
    for copy in copies:
        copy.start()
    return copies


def row_of(ref):
    block = ref[...].astype(F32)
    return jnp.concatenate([block[r : r + 1, :] for r in range(block.shape[0])], axis=1)


def put_row(ref, row):
    for r in range(ref.shape[0]):
        ref[r : r + 1, :] = row[:, r * LANES : (r + 1) * LANES]


def call(kernel, args, specs, outs, scratch=(), micros=0, limit=24, in_place=None):
    return pl.pallas_call(
        kernel,
        out_shape=[jax.ShapeDtypeStruct(shape, kind) for shape, kind in outs],
        in_specs=specs,
        out_specs=[outside() if in_place else whole() for _ in outs],
        input_output_aliases=in_place or {},
        scratch_shapes=list(scratch),
        compiler_params=pltpu.CompilerParams(vmem_limit_bytes=limit * MIB),
        cost_estimate=pl.CostEstimate(
            flops=micros * 1_000_000_000, bytes_accessed=0, transcendentals=0
        ),
    )(*args)


def head_windows(width):
    windows = []
    for pair in range(width // (2 * HDIM)):
        low = pair * 2 * HDIM // LANES * LANES
        high = -(-(pair + 1) * 2 * HDIM // LANES) * LANES
        windows.append((low, high))
    return windows


def split_heads(block, pair, window):
    low, high = window
    part = block[:, low:high]
    column = low + lax.broadcasted_iota(jnp.int32, (16, high - low), 1)
    sides = []
    for head in (2 * pair, 2 * pair + 1):
        inside = (column >= head * HDIM) & (column < (head + 1) * HDIM)
        mask = jnp.where(inside, 1.0, 0.0).astype(BF16)
        sides.append(part * jnp.concatenate([mask] * (block.shape[0] // 16), axis=0))
    return jnp.concatenate(sides, axis=0)


def embed_rows(feats, lap, ends, w_ident, types, gain, shift, at, count):
    table = lap[:, at]
    slot = lax.broadcasted_iota(jnp.int32, (SEQ, SEQ), 0)
    picked = []
    for end in (0, 1):
        pick = jnp.where(ends[end : end + 1, at] == slot, 1.0, 0.0).astype(BF16)
        picked.append(dot(table, pick))
    ident = jnp.concatenate(picked, axis=0).astype(BF16)
    hidden = feats[at, :].astype(F32) + dot_tn(ident, w_ident[...])
    kinds = types[...].astype(F32)
    hidden = hidden + jnp.where(positions(SEQ) >= count, kinds[1:2, :], kinds[0:1, :])
    unit, _ = norm_parts(hidden)
    return hidden, ident, (unit * gain + shift).astype(BF16)


def embed_kernel(
    feats_in, lap_in, ends_in, nodes_in, w_ident_in, types_in, gain_in, shift_in,
    bias_q_in, bias_v_in, wq_in, wk_in, wv_in, edges_in,
    hidden_out, ident_out, normed_out, normed_t_out, q_out, k_out, v_out, keep_out,
    feats, lap, ends, nodes, w_ident, types, gain_rows, shift_rows, bias_q, bias_v,
    w_q, w_k, w_v, edges, sems,
):
    rows, dim = feats.shape
    mols = rows // SEQ
    core = places()[0]
    own_rows = pl.ds(pl.multiple_of(core * rows, SEQ), rows)
    copies = copy_in(
        (
            feats_in.at[own_rows, :], lap_in.at[:, own_rows], ends_in.at[:, own_rows], nodes_in,
            w_ident_in, types_in, gain_in, shift_in, bias_q_in, bias_v_in, wq_in, wk_in, wv_in,
            edges_in,
        ),
        (
            feats, lap, ends, nodes, w_ident, types, gain_rows, shift_rows, bias_q, bias_v,
            w_q, w_k, w_v, edges,
        ),
        sems,
    )
    for copy in copies[:10]:
        copy.wait()
    gain, shift = row_of(gain_rows), row_of(shift_rows)

    def molecule(m):
        at = slice(m * SEQ, (m + 1) * SEQ)
        count = nodes[core * mols + m]
        hidden, ident, normed = embed_rows(
            feats, lap, ends, w_ident, types, gain, shift, at, count
        )
        ident_out[:, at] = ident
        hidden_out[at, :] = hidden
        normed_out[at, :] = normed
        normed_t_out[:, at] = normed.T

    for m in range(mols):
        molecule(m)
    normed = normed_out[...]
    copies[10].wait()
    q_out[...] = (dot(normed, w_q[...]) + row_of(bias_q)).astype(BF16)
    copies[11].wait()
    k_out[...] = dot(normed, w_k[...]).astype(BF16)
    copies[12].wait()
    v_out[...] = (dot(normed, w_v[...]) + row_of(bias_v)).astype(BF16)
    copies[13].wait()
    for m in range(2 * mols):
        inside = lax.broadcasted_iota(jnp.int32, (SEQ, LANES), 0) < nodes[m] + edges[m]
        keep_out[m * SEQ : (m + 1) * SEQ, :] = jnp.where(inside, 1.0, 0.0)


def forward_kernel(
    hidden, normed, q_own, k_own, v_own, w_q, w_k, w_v, wo_own, wo, wu_own, wu,
    bias_q, bias_v, bias_u,
    nodes_in, edges_in, bias_u_own_in, bias_o_in, gain_in, shift_in,
    q_out, k_out, v_out, probs_out, keep_out, send_out, middle, active, slope,
    nodes, edges, bias_u_own, bias_o, gain_rows, shift_rows, sems,
    mixed, attended, normed_two,
):
    rows, dim = hidden.shape
    width = q_own.shape[1]
    mols = rows // SEQ
    pairs = width // (2 * HDIM)
    windows = head_windows(width)
    core = places()[0]
    copies = copy_in(
        (nodes_in, edges_in, bias_u_own_in, bias_o_in, gain_in, shift_in),
        (nodes, edges, bias_u_own, bias_o, gain_rows, shift_rows),
        sems,
    )

    for copy in copies:
        copy.wait()
    gain, shift, bias_out = row_of(gain_rows), row_of(shift_rows), row_of(bias_o)

    sides = ((q_own, k_own, v_own, keep_out), (q_out, k_out, v_out, send_out))
    units = [(m, side) for side in (0, 1) for m in range(mols)]

    def weigh(unit, pair):
        m, side = unit
        at = slice(m * SEQ, (m + 1) * SEQ)
        place = core * mols + m
        key_keep = positions(SEQ) < nodes[place] + edges[place]
        low, high = windows[pair]
        both = split_heads(sides[side][0][at, :], pair, windows[pair])
        scores = dot_nt(sides[side][1][at, low:high], both)
        scores = jnp.where(key_keep, scores, -1e30)
        top = jnp.max(scores, axis=0, keepdims=True)
        raised = jnp.exp2((scores - top) * LOG2_SCALE)
        probs_out[m, side * pairs + pair] = (raised * (1.0 / row_sum(raised))).astype(BF16)

    def mix(step, pair, values_t):
        m, side = units[step]
        first = pair * 2 * HDIM
        out = dot(values_t[first : first + 2 * HDIM], probs_out[m, side * pairs + pair])
        mixed[step % 2, first : first + HDIM, :] = out[:HDIM, :SEQ]
        mixed[step % 2, first + HDIM : first + 2 * HDIM, :] = out[HDIM:, SEQ:]

    def keep_mixed(step):
        m, side = units[step]
        at = slice(m * SEQ, (m + 1) * SEQ)
        place = core * mols + m
        query_keep = lax.broadcasted_iota(jnp.int32, (1, SEQ), 1) < nodes[place] + edges[place]
        kept = jnp.where(query_keep, mixed[step % 2], 0.0).astype(BF16)
        sides[side][3][dim : dim + width, at] = kept
        attended[at, side * width : (side + 1) * width] = kept.T

    partner = ((q_out, w_q, bias_q), (k_out, w_k, None), (v_out, w_v, bias_v))
    for pair in range(pairs):
        weigh(units[0], pair)
        if pair % 2 == 0 and pair // 2 < len(partner):
            out, weight, bias = partner[pair // 2]
            rows_of = dot(normed[...], weight[...])
            out[...] = (rows_of if bias is None else rows_of + row_of(bias)).astype(BF16)
    for step, task in enumerate(units):
        values_t = sides[task[1]][2][task[0] * SEQ : (task[0] + 1) * SEQ, :].T
        for pair in range(pairs):
            mix(step, pair, values_t)
            if step + 1 < len(units):
                weigh(units[step + 1], pair)
        keep_mixed(step)
    middle[...] = (
        hidden[...] + dot(attended[:, :width], wo_own[...]) + dot(attended[:, width:], wo[...])
    )

    for m in range(mols):
        at = slice(m * SEQ, (m + 1) * SEQ)
        total = middle[at, :] + bias_out
        middle[at, :] = total
        unit_rows, _ = norm_parts(total)
        rows_two = (unit_rows * gain + shift).astype(BF16)
        normed_two[at, :] = rows_two
        turned = rows_two.T
        keep_out[:dim, at] = turned
        send_out[:dim, at] = turned

    for side, (w_ref, b_ref, part_out) in enumerate(
        ((wu_own, bias_u_own, keep_out), (wu, bias_u, send_out))
    ):
        columns = slice(side * width, (side + 1) * width)
        slope[:, columns] = dot(normed_two[...], w_ref[...]) + row_of(b_ref)

        for m in range(mols):
            at = slice(m * SEQ, (m + 1) * SEQ)
            before = slope[at, columns]
            phi = 0.5 * (1.0 + lax.erf(before * math.sqrt(0.5)))
            out = (before * phi).astype(BF16)
            slope[at, columns] = phi + before * jnp.exp(before * before * -0.5) * (
                1.0 / math.sqrt(2.0 * math.pi)
            )
            active[at, columns] = out
            part_out[dim + width : dim + 2 * width, at] = out.T


def ffn_back_kernel(
    middle, slope, wu_own, wu, wd_own, wd, keep_rows, cots, gain_in,
    keep_out, send_out, gm_out, grad_branch,
    gain_rows, sems, grad_ffn,
):
    rows, dim = middle.shape
    width = wd.shape[0]
    mols = rows // SEQ
    core = places()[0]
    copies = copy_in((gain_in,), (gain_rows,), sems)

    def own_cots(m):
        at = pl.ds(pl.multiple_of(core * rows + m * SEQ, SEQ), SEQ)
        return jnp.where(keep_rows[at, 0:1] > 0.5, cots[at, :].astype(F32), 0.0)

    for m in range(mols):
        at = slice(m * SEQ, (m + 1) * SEQ)
        grad_ffn[at, :] = own_cots(m).astype(BF16)
    place_b = 0
    for side, (w_ref, part_out) in enumerate(((wd_own, keep_out), (wd, send_out))):
        columns = slice(side * width, (side + 1) * width)
        grad_before = slope[:, columns] * dot_nt(grad_ffn[...], w_ref[...])
        part_out[place_b : place_b + rows, :] = grad_before.astype(BF16)

    back = pl.ds(place_b, rows)
    gm_out[...] = dot_nt(keep_out[back, :], wu_own[...]) + dot_nt(send_out[back, :], wu[...])

    copies[0].wait()
    gain = row_of(gain_rows)
    nothing = jnp.zeros((1, dim), F32)
    sums = (nothing,) * 4
    for m in range(mols):
        at = slice(m * SEQ, (m + 1) * SEQ)
        grad_normed = gm_out[at, :]
        unit_rows, inverse = norm_parts(middle[at, :])
        grad_result = own_cots(m)
        grad = grad_result + norm_back(unit_rows, inverse, grad_normed * gain)
        gm_out[at, :] = grad
        grad_branch[at, :] = grad.astype(BF16)
        sums = (
            sums[0] + row_sum(grad),
            sums[1] + row_sum(grad_normed * unit_rows),
            sums[2] + row_sum(grad_normed),
            sums[3] + row_sum(grad_result),
        )

    place_m = place_b + rows
    for part_out in (keep_out, send_out):
        part_out[place_m : place_m + rows, :] = grad_branch[:, :width]
        part_out[place_m + rows : place_m + 2 * rows, :] = grad_branch[:, width:]
    small = jnp.concatenate(list(sums) + [nothing] * 12, axis=0)
    left, right = small[:, :width], small[:, width:]
    place_s = place_m + 2 * rows
    keep_out[place_s:, :] = jnp.where(core == 0, left, right).astype(BF16)
    send_out[place_s:, :] = jnp.where(core == 0, right, left).astype(BF16)


def result_kernel(middle, active, wd_own, wd, bias, result_out):
    width = wd.shape[0]
    result_out[...] = (
        middle[...]
        + dot(active[:, :width], wd_own[...])
        + dot(active[:, width:], wd[...])
        + row_of(bias)
    ).astype(BF16)


def branch_kernel(grad_branch, wo_own, wo, keep_rows, ga_own_out, ga_out):
    rows = grad_branch.shape[0]
    own_rows = pl.ds(pl.multiple_of(places()[0] * rows, SEQ), rows)
    keep = keep_rows[own_rows, 0:1] > 0.5
    for ref, weight in ((ga_own_out, wo_own), (ga_out, wo)):
        ref[...] = jnp.where(keep, dot_nt(grad_branch[...], weight[...]), 0.0).astype(BF16)


def attend_back_kernel(
    q_own, k_own, v_own, ga_own, q_got, k_got, v_got, ga_got, probs_all,
    keep_out, send_out, dq_t, dk, dv, slopes,
):
    rows, width = q_own.shape
    pairs = width // (2 * HDIM)
    windows = head_windows(width)
    sides = (
        (q_own, k_own, v_own, ga_own, keep_out),
        (q_got, k_got, v_got, ga_got, send_out),
    )
    units = [(m, side) for m in range(rows // SEQ) for side in (0, 1)]

    def score_back(unit, pair):
        m, side = unit
        at = slice(m * SEQ, (m + 1) * SEQ)
        low, high = windows[pair]
        both_g = split_heads(sides[side][3][at, :], pair, windows[pair])
        probs_low = probs_all[m, side * pairs + pair]
        probs = probs_low.astype(F32)
        grad_probs = dot_nt(sides[side][2][at, low:high], both_g)
        inner = row_sum(probs * grad_probs)
        slopes[side, pair] = (probs * (grad_probs - inner)).astype(BF16)
        dv[side, :, low:high] += dot(probs_low, both_g)

    def rows_back(unit, pair, keys_t):
        m, side = unit
        low, high = windows[pair]
        grad_scores = slopes[side, pair]
        both_q = split_heads(sides[side][0][m * SEQ : (m + 1) * SEQ, :], pair, windows[pair])
        dk[side, :, low:high] += dot(grad_scores, both_q)
        first = pair * 2 * HDIM
        out = dot(keys_t[first : first + 2 * HDIM], grad_scores)
        dq_t[side, first : first + HDIM, :] = out[:HDIM, :SEQ]
        dq_t[side, first + HDIM : first + 2 * HDIM, :] = out[HDIM:, SEQ:]

    def begin(unit):
        dk[unit[1]] = jnp.zeros_like(dk[unit[1]])
        dv[unit[1]] = jnp.zeros_like(dv[unit[1]])

    def finish(unit):
        m, side = unit
        part_out = sides[side][4]
        base = m * SEQ
        part_out[base : base + SEQ, :] = (dq_t[side] * SCALE).astype(BF16).T
        part_out[rows + base : rows + base + SEQ, :] = (dk[side] * SCALE).astype(BF16)
        part_out[2 * rows + base : 2 * rows + base + SEQ, :] = dv[side].astype(BF16)

    begin(units[0])
    for pair in range(pairs):
        score_back(units[0], pair)
    for step, unit in enumerate(units):
        keys_t = sides[unit[1]][1][unit[0] * SEQ : (unit[0] + 1) * SEQ, :].T
        if step + 1 < len(units):
            begin(units[step + 1])
        for pair in range(pairs):
            rows_back(unit, pair, keys_t)
            if step + 1 < len(units):
                score_back(units[step + 1], pair)
        finish(unit)


def embed_back_kernel(*refs):
    (
        grads_own, grads,
        wq_own, wk_own, wv_own, w_q, w_k, w_v, ident, grad_middle,
        feats_in, nodes_in, w_ident_in, types_in, gain_in,
        features_out, keep_out, send_out,
        feats, nodes, w_ident, types, gain_rows, sems, grad_normed, small,
    ) = refs
    core = places()[0]
    rows = feats.shape[0]
    copies = copy_in(
        (
            feats_in.at[pl.ds(pl.multiple_of(core * rows, SEQ), rows), :], nodes_in,
            w_ident_in, types_in, gain_in,
        ),
        (feats, nodes, w_ident, types, gain_rows),
        sems,
    )
    rows, dim = feats.shape
    width = wq_own.shape[1]
    idw = ident.shape[0]
    total = None
    for part, weights in ((grads_own, (wq_own, wk_own, wv_own)), (grads, (w_q, w_k, w_v))):
        for place, weight in enumerate(weights):
            term = dot_nt(part[place * rows : (place + 1) * rows, :], weight[...])
            total = term if total is None else total + term
    grad_normed[...] = total
    mols = rows // SEQ
    small[...] = jnp.zeros_like(small)
    for copy in copies:
        copy.wait()
    gain = row_of(gain_rows)
    kinds = types[...].astype(F32)

    def molecule(m, carry):
        at = pl.ds(pl.multiple_of(m * SEQ, SEQ), SEQ)
        is_edge = positions(SEQ) >= nodes[core * mols + m]
        hidden = feats[at, :].astype(F32) + dot_tn(ident[:, at], w_ident[...])
        hidden = hidden + jnp.where(is_edge, kinds[1:2, :], kinds[0:1, :])
        unit, inverse = norm_parts(hidden)
        grad_rows = grad_normed[at, :]
        grad = grad_middle[at, :] + norm_back(unit, inverse, grad_rows * gain)
        features_out[at, :] = grad
        high = grad.astype(BF16)
        rest = (grad - high.astype(F32)).astype(BF16)
        picked = ident[:, at]
        small[:idw, :] += dot(picked, high) + dot(picked, rest)
        edge_rows = jnp.where(is_edge, grad, 0.0)
        small[idw : idw + 1, :] += row_sum(grad - edge_rows)
        small[idw + 1 : idw + 2, :] += row_sum(edge_rows)
        small[idw + 2 : idw + 3, :] += row_sum(grad_rows * unit)
        small[idw + 3 : idw + 4, :] += row_sum(grad_rows)
        return carry

    lax.fori_loop(0, mols, molecule, 0)
    left, right = small[:, :width], small[:, width:]
    keep_out[...] = jnp.where(core == 0, left, right)
    send_out[...] = jnp.where(core == 0, right, left).astype(BF16)


def deal(unit, places_in, outs, block_at, small=None):
    _, inner, outer = places()
    first_kept, first_sent, second_kept, second_sent = outs
    for step in range(INNER):
        for turn in range(OUTER):
            if turn < 2:
                out, slot = (first_sent if step % 2 else first_kept), step // 2
            else:
                out, slot = (second_sent if step // 2 else second_kept), step % 2
            start = (slot * 2 + turn % 2) * places_in * unit
            for place in range(places_in):
                out[start + place * unit : start + (place + 1) * unit, :] = block_at(
                    inner ^ step, outer ^ turn, place
                )
    if small is not None:
        for out in (first_kept, first_sent):
            out[INNER * places_in * unit :, :] = small


def flat_block(flat, unit, dest, z):
    row = pl.multiple_of((dest * (OUTER // 2) + z // 2) * unit, 16)
    return flat[z % 2, pl.ds(row, unit), :]


def down_grads_kernel(kept, got, cots, keep_rows, *rest):
    outs, (flat, grad_ffn) = rest[:4], rest[4:]
    rows_all, dim = cots.shape
    rows, width = rows_all // 2, kept.shape[1]
    core = places()[0]
    for m in range(rows_all // SEQ):
        at = slice(m * SEQ, (m + 1) * SEQ)
        grad_ffn[at, :] = jnp.where(keep_rows[at, 0:1] > 0.5, cots[at, :].astype(F32), 0.0).astype(BF16)
    own_rows = pl.ds(pl.multiple_of(core * rows, SEQ), rows)
    other_rows = pl.ds(pl.multiple_of((1 - core) * rows, SEQ), rows)
    turned = slice(dim + width, dim + 2 * width)
    for half in (0, 1):
        columns = slice(half * width, (half + 1) * width)
        product = dot(kept[turned, :], grad_ffn[own_rows, columns])
        product = product + dot(got[turned, :], grad_ffn[other_rows, columns])
        flat[half] = product.astype(BF16)
    unit = dim // (INNER * OUTER)
    deal(unit, 1, outs, lambda dest, z, place: flat_block(flat, unit, dest, z))


def ffn_grads_kernel(kept, got, kept_back, got_back, *rest):
    outs, (tall, flat) = rest[:4], rest[4:]
    rows, width = kept.shape[1], kept.shape[1]
    dim = kept.shape[0] - 2 * width
    back, place_s = slice(0, rows), 3 * rows
    tall[...] = (
        dot(kept[:dim, :], kept_back[back, :]) + dot(got[:dim, :], got_back[back, :])
    ).astype(BF16)
    turned = slice(dim, dim + width)
    for half in (0, 1):
        mid = slice((1 + half) * rows, (2 + half) * rows)
        flat[half] = (
            dot(kept[turned, :], kept_back[mid, :]) + dot(got[turned, :], got_back[mid, :])
        ).astype(BF16)
    bias = row_sum(kept_back[back, :].astype(F32)) + row_sum(got_back[back, :].astype(F32))
    small = kept_back[place_s:, :].astype(F32) + got_back[place_s:, :].astype(F32)
    spot = lax.broadcasted_iota(jnp.int32, small.shape, 0)
    small = jnp.where(spot == 4, bias, small).astype(BF16)
    unit = dim // (INNER * OUTER)

    def block_at(dest, z, place):
        if place == 0:
            return tall[pl.ds(pl.multiple_of((dest * OUTER + z) * unit, 16), unit), :]
        return flat_block(flat, unit, dest, z)

    deal(unit, 2, outs, block_at, small)


def qkv_grads_kernel(normed_t, normed_t_got, kept, got, *refs):
    outs, small_out, (tall, normed, stacked) = refs[:4], refs[4], refs[5:]
    dim, rows = normed_t.shape
    unit = dim // (INNER * OUTER)
    normed[:, :rows] = normed_t[...]
    normed[:, rows:] = normed_t_got[...]
    spot = lax.broadcasted_iota(jnp.int32, small_out.shape, 0)
    small = jnp.zeros(small_out.shape, F32)
    for place in range(3):
        part = slice(place * rows, (place + 1) * rows)
        stacked[:rows, :] = kept[part, :]
        stacked[rows:, :] = got[part, :]
        tall[place] = dot(normed[...], stacked[...]).astype(BF16)
        if place != 1:
            small = jnp.where(spot == 36 + place // 2, row_sum(stacked[...].astype(F32)), small)
    small_out[...] = small

    def block_at(dest, z, place):
        return tall[place, pl.ds(pl.multiple_of((dest * OUTER + z) * unit, 16), unit), :]

    deal(unit, 3, outs, block_at)


def add(first, second):
    return (first.astype(F32) + second.astype(F32)).astype(BF16)


def plane_sum_kernel(first, first_got, second, second_got, *refs):
    late, (first_kept, first_sent, second_kept, second_sent) = refs[:-4], refs[-4:]
    pair = second_kept.shape[0]
    total = add(first[...], first_got[...])
    first_kept[:pair, :] = total[:pair]
    first_sent[:pair, :] = total[pair : 2 * pair]
    if late:
        small = (late[0][...] + late[1][...].astype(F32) + late[2][...]).astype(BF16)
    else:
        small = total[2 * pair :]
    first_kept[pair:, :] = small
    first_sent[pair:, :] = small
    total = add(second[...], second_got[...])
    second_kept[...] = total[:pair]
    second_sent[...] = total[pair:]


def plane_join_kernel(first, first_got, second, second_got, *refs):
    ahead, outs = refs[:4], refs[4:]
    unit = ahead[0].shape[0] // 4
    small = add(first[8 * unit :, :], first_got[8 * unit :, :])
    for place, (left, right, more, more_got) in enumerate(
        ((first, first_got, *ahead[:2]), (second, second_got, *ahead[2:]))
    ):
        total = add(left[: 8 * unit, :], right[: 8 * unit, :])
        late = add(more[...], more_got[...])
        for block in range(4):
            out = outs[2 * place + block // 2]
            start = block % 2 * 3 * unit
            out[start : start + 2 * unit, :] = total[2 * block * unit : 2 * (block + 1) * unit]
            out[start + 2 * unit : start + 3 * unit, :] = late[block * unit : (block + 1) * unit]
    for out in outs[:2]:
        out[6 * unit :, :] = small


def line_cut_kernel(first, first_got, second, second_got, own, near, middle, far):
    chunk = own.shape[0]
    total = add(first[...], first_got[...])
    own[...] = total[:chunk]
    near[...] = total[chunk:]
    total = add(second[...], second_got[...])
    middle[...] = total[:chunk]
    far[...] = total[chunk:]


def line_sum_kernel(own, near, near_got, middle_got, far_got, out, out_small):
    chunk = own.shape[0]
    total = own[...].astype(F32) + near_got[:chunk, :].astype(F32)
    total = total + middle_got[...].astype(F32) + far_got[...].astype(F32)
    out[...] = total.astype(BF16)
    out_small[:chunk, :] = total.astype(BF16)
    out_small[chunk:, :] = add(near[chunk:, :], near_got[chunk:, :])


def line_join_kernel(own, near, middle, far, line_x, line_y, small_out):
    chunk = near.shape[0]
    small = own[chunk:, :].astype(F32) + middle[chunk:, :].astype(F32)
    small_out[...] = small
    for out in (line_x, line_y):
        for turn, part in enumerate((own, near, middle, far)):
            out[turn * chunk : (turn + 1) * chunk, :] = part[:chunk, :]
    line_x[OUTER * chunk :, :] = small.astype(BF16)


def place_kernel(split_second, *refs):
    outs, parts = refs[-3:], refs[:-3]
    own = parts[0]
    steps = min(len(parts), INNER)
    _, inner, outer = places()
    unit = own.shape[0] // (3 * OUTER)
    width = own.shape[1]
    for step in range(steps):
        for turn in range(OUTER):
            ref, start = parts[step], turn * 3 * unit
            if step == 3 and turn >= 2:
                ref, start = parts[4], (turn - 2) * 3 * unit
            dest, z = inner ^ step, outer ^ turn
            tall = pl.ds(pl.multiple_of((dest * OUTER + z) * unit, 16), unit)
            flat = pl.ds(pl.multiple_of((dest * (OUTER // 2) + z // 2) * unit, 16), unit)
            columns = pl.ds(pl.multiple_of(z % 2 * width, LANES), width)
            for place in range(3):
                part = ref[start + place * unit : start + (place + 1) * unit, :].astype(F32)
                if split_second and place > 0:
                    outs[place][flat, columns] = part
                else:
                    outs[place][tall, :] = part


def corner_kernel(first, second, *refs):
    outs, blocks, sems = refs[3:6], refs[6], refs[7]
    _, inner, outer = places()
    unit = first.shape[0] // 6
    size = OUTER * unit
    for turn in range(OUTER):
        ref, start = (first, turn * 3 * unit) if turn < 2 else (second, (turn - 2) * 3 * unit)
        at = pl.ds(pl.multiple_of((outer ^ turn) * unit, 16), unit)
        for place in range(3):
            rows = slice(start + place * unit, start + (place + 1) * unit)
            blocks[place, at, :] = ref[rows, :].astype(F32)
    at = pl.ds(pl.multiple_of((inner ^ 3) * size, 64), size)
    copies = copy_in(
        [blocks.at[place] for place in range(3)], [out.at[at, :] for out in outs], sems
    )
    for copy in copies:
        copy.wait()


def finish_first_kernel(small, got, bias_out, gain, shift, bias_down, bias_up):
    core = places()[0]
    for place, ref in enumerate((bias_out, gain, shift, bias_down)):
        mine, other = small[place : place + 1, :], got[place : place + 1, :]
        left = jnp.where(core == 0, mine, other)
        put_row(ref, jnp.concatenate([left, jnp.where(core == 0, other, mine)], axis=1))
    put_row(bias_up, small[4:5, :])


def finish_second_kernel(small, extra, got, w_ident, types, gain, shift, bias_q, bias_v):
    idw = w_ident.shape[0]
    core = places()[0]
    mine, other = small[...] + extra[...].astype(F32), got[...]
    left = jnp.where(core == 0, mine, other)
    total = jnp.concatenate([left, jnp.where(core == 0, other, mine)], axis=1)
    w_ident[...] = total[:idw]
    types[...] = total[idw : idw + 2]
    put_row(gain, total[idw + 2 : idw + 3])
    put_row(shift, total[idw + 3 : idw + 4])
    put_row(bias_q, mine[idw + 4 : idw + 5])
    put_row(bias_v, mine[idw + 5 : idw + 6])


def per_device(
    features, lap_vectors, node_counts, edge_counts, endpoints, w_ident, type_table,
    gain_one, shift_one, w_query, w_key, w_value, bias_query, bias_value, w_out, bias_out,
    gain_two, shift_two, w_up, bias_up, w_down, bias_down, cotangent,
):
    dp_count = lax.axis_size("dp")
    dp_index = lax.axis_index("dp")
    mp_index = lax.axis_index("mp")
    block = INNER * OUTER
    rest_count = dp_count // block
    def swap(part):
        return lax.ppermute(part, "mp", [(0, 1), (1, 0)])

    def inner_move(part, step):
        return lax.ppermute(part, "dp", [(s, s ^ step) for s in range(dp_count)])

    def outer_move(part, step):
        return lax.ppermute(part, "dp", [(s, s ^ (step * INNER)) for s in range(dp_count)])

    rows_all, dim = features.shape
    rows = rows_all // 2
    mols = rows // SEQ
    width = w_query.shape[1]
    heads = width // HDIM
    lapk = lap_vectors.shape[1]
    idw = w_ident.shape[0]

    def pinned(part):
        return pltpu.with_memory_space_constraint(part, pltpu.HBM)

    def lanes(part):
        return pinned(part.reshape(-1, LANES))

    nodes, edges = pinned(node_counts), pinned(edge_counts)
    count_scratch = pltpu.SMEM(node_counts.shape, jnp.int32)
    wide_scratch = pltpu.VMEM((dim // LANES, LANES), BF16)
    half_scratch = pltpu.VMEM((width // LANES, LANES), BF16)
    def after(part, *others):
        return lax.optimization_barrier((part, *others))[0]

    embed_args = (
        pinned(features), pinned(lap_vectors.T), pinned(endpoints.T), nodes,
        pinned(w_ident), pinned(type_table), lanes(gain_one), lanes(shift_one),
    )
    embed_scratch = [
        pltpu.VMEM((rows, dim), BF16),
        pltpu.VMEM((lapk, rows), BF16),
        pltpu.VMEM((2, rows), jnp.int32),
        count_scratch,
        pltpu.VMEM((idw, dim), BF16),
        pltpu.VMEM((2, dim), BF16),
        wide_scratch,
        wide_scratch,
    ]

    wq_got, wk_got, wv_got = swap(w_query), swap(w_key), swap(w_value)
    bq_got, bv_got, bu_got = swap(bias_query), swap(bias_value), swap(bias_up)
    wo_got, wu_got = swap(w_out), swap(w_up)

    hidden, ident, normed, normed_t, q_own, k_own, v_own, keep_rows = call(
        embed_kernel,
        (
            *embed_args, lanes(bias_query), lanes(bias_value),
            pinned(w_query), pinned(w_key), pinned(w_value), edges,
        ),
        [outside()] * 14,
        [
            ((rows, dim), F32),
            ((idw, rows), BF16),
            ((rows, dim), BF16),
            ((dim, rows), BF16),
            ((rows, width), BF16),
            ((rows, width), BF16),
            ((rows, width), BF16),
            ((rows_all, LANES), F32),
        ],
        scratch=embed_scratch
        + [half_scratch] * 2
        + [pltpu.VMEM((dim, width), BF16)] * 3
        + [count_scratch, pltpu.SemaphoreType.DMA((14,))],
    )
    wd_got = swap(after(w_down, normed))
    ahead_rows, back_rows = dim + 2 * width, 3 * rows + 16
    q_got, k_got, v_got, probs, kept_a, sent_a, middle, active, slope = call(
        forward_kernel,
        (
            hidden, normed, q_own, k_own, v_own, wq_got, wk_got, wv_got,
            w_out, wo_got, w_up, wu_got,
            *(part.reshape(-1, LANES) for part in (bq_got, bv_got, bu_got)),
            nodes, edges,
            lanes(bias_up), lanes(bias_out), lanes(gain_two), lanes(shift_two),
        ),
        [whole()] * 15 + [outside()] * 6,
        [
            ((rows, width), BF16),
            ((rows, width), BF16),
            ((rows, width), BF16),
            ((mols, heads, SEQ, 2 * SEQ), BF16),
            ((ahead_rows, width), BF16),
            ((ahead_rows, width), BF16),
            ((rows, dim), F32),
            ((rows, dim), BF16),
            ((rows, dim), F32),
        ],
        scratch=[
            count_scratch,
            count_scratch,
            half_scratch,
            wide_scratch,
            wide_scratch,
            wide_scratch,
            pltpu.SemaphoreType.DMA((6,)),
            pltpu.VMEM((2, width, SEQ), F32),
            pltpu.VMEM((rows, dim), BF16),
            pltpu.VMEM((rows, dim), BF16),
        ],
        limit=30,
    )
    got_a = swap(sent_a)
    kept_back, sent_back, grad_middle, grad_branch = call(
        ffn_back_kernel,
        (
            middle, slope, w_up, wu_got, w_down, wd_got, keep_rows, cotangent,
            lanes(gain_two),
        ),
        [whole()] * 8 + [outside()],
        [
            ((back_rows, width), BF16),
            ((back_rows, width), BF16),
            ((rows, dim), F32),
            ((rows, dim), BF16),
        ],
        scratch=[wide_scratch, pltpu.SemaphoreType.DMA((1,)), pltpu.VMEM((rows, dim), BF16)],
    )
    got_back = swap(sent_back)

    unit = dim // block
    chunk = 3 * unit
    small_a, small_b = 16, 48

    def rest_sum(part):
        if rest_count == 1:
            return part
        groups = [[r * block + s for r in range(rest_count)] for s in range(block)]
        return lax.psum(part.astype(F32), "dp", axis_index_groups=groups).astype(part.dtype)

    pair = 2 * chunk

    def plane_step(parts, small_rows, late=(), others=(), micros=0):
        first, first_sent, second, second_sent = parts
        first_got = after(inner_move(first_sent, 1), *others)
        second_got = after(inner_move(second_sent, 2), *others)
        return call(
            plane_sum_kernel,
            (first, first_got, second, second_got, *late),
            [whole()] * (4 + len(late)),
            [((pair + small_rows, width), BF16)] * 2 + [((pair, width), BF16)] * 2,
            micros=micros,
        )

    def plane_turn(parts, others=(), micros=0):
        first, first_sent, second, second_sent = parts
        first_got = after(inner_move(first_sent, 2), *others)
        second_got = after(inner_move(second_sent, 1), *others)
        return call(
            line_cut_kernel,
            (first, first_got, second, second_got),
            [whole()] * 4,
            [
                ((chunk, width), BF16),
                ((first.shape[0] - chunk, width), BF16),
                ((chunk, width), BF16),
                ((chunk, width), BF16),
            ],
            micros=micros,
        )

    def line_step(parts, others=(), micros=0):
        got = [after(outer_move(parts[turn], turn), *others) for turn in range(1, OUTER)]
        mine, both = call(
            line_sum_kernel,
            (parts[0], parts[1], *got),
            [whole()] * 5,
            [((chunk, width), BF16), (parts[1].shape, BF16)],
            micros=micros,
        )
        if rest_count > 1:
            both = rest_sum(both)
            mine = both[:chunk]
        return mine, both

    def line_back(mine, both, others=(), micros=0):
        sent = (mine, both, mine)
        got = [after(outer_move(sent[turn - 1], turn), *others) for turn in range(1, OUTER)]
        small_rows = both.shape[0] - chunk
        return call(
            line_join_kernel,
            (both, *got),
            [whole()] * OUTER,
            [
                ((OUTER * chunk + small_rows, width), BF16),
                ((OUTER * chunk, width), BF16),
                ((small_rows, width), F32),
            ],
            micros=micros,
        )

    def plane_back(lines):
        return inner_move(lines[0], 1), inner_move(lines[1], 2)

    def plane_back_turn(side_x, side_y):
        return inner_move(side_y[:pair], 1), inner_move(side_x[pair : 2 * pair], 2)

    def placed(planes, split_second, micros=0):
        tall, flat = ((dim, width), F32), ((width, dim), F32)
        return call(
            lambda *refs: place_kernel(split_second, *refs),
            planes,
            [whole()] * len(planes),
            [tall, flat, flat] if split_second else [tall] * 3,
            micros=micros,
        )

    parts_down = call(
        down_grads_kernel,
        (after(kept_a, grad_branch), got_a, cotangent, keep_rows),
        [whole()] * 4,
        [((INNER * unit, width), BF16)] * 4,
        scratch=[pltpu.VMEM((2, width, width), BF16), pltpu.VMEM((rows_all, dim), BF16)],
    )
    parts_a = call(
        ffn_grads_kernel,
        (after(kept_a, parts_down[0]), got_a, kept_back, got_back),
        [whole()] * 4,
        [((2 * INNER * unit + small_a, width), BF16)] * 2 + [((2 * INNER * unit, width), BF16)] * 2,
        scratch=[pltpu.VMEM((dim, width), BF16), pltpu.VMEM((2, width, width), BF16)],
    )
    ahead = [
        after(inner_move(parts_down[1], 1), parts_a[0]),
        after(inner_move(parts_down[3], 2), parts_a[0]),
    ]
    ga_own, ga_got = call(
        branch_kernel,
        (after(grad_branch, parts_a[0], *ahead), w_out, wo_got, keep_rows),
        [whole()] * 4,
        [((rows, width), BF16), ((rows, width), BF16)],
    )

    kept_b, sent_b = call(
        attend_back_kernel,
        (q_own, k_own, v_own, ga_own, q_got, k_got, v_got, ga_got, probs),
        [whole()] * 9,
        [((3 * rows, width), BF16)] * 2,
        scratch=[
            pltpu.VMEM((2, width, SEQ), F32),
            pltpu.VMEM((2, SEQ, width), F32),
            pltpu.VMEM((2, SEQ, width), F32),
            pltpu.VMEM((2, heads // 2, SEQ, 2 * SEQ), BF16),
        ],
    )
    normed_t_got = swap(after(normed_t, parts_a[0]))
    got_b = swap(sent_b)
    moved = [after(inner_move(parts_a[1], 1), kept_b), after(inner_move(parts_a[3], 2), kept_b)]
    moved = moved + ahead
    steps_a = call(
        plane_join_kernel,
        (
            parts_a[0], moved[0], parts_a[2], moved[1],
            parts_down[0], moved[2], parts_down[2], moved[3],
        ),
        [whole()] * 8,
        [((pair + small_a, width), BF16)] * 2 + [((pair, width), BF16)] * 2,
        micros=6,
    )
    normed_t = after(normed_t, *steps_a)
    parts_b = call(
        qkv_grads_kernel,
        (normed_t, normed_t_got, kept_b, got_b),
        [whole()] * 4,
        [((INNER * chunk, width), BF16)] * 4 + [((small_b, width), F32)],
        scratch=[
            pltpu.VMEM((3, dim, width), BF16),
            pltpu.VMEM((dim, 2 * rows), BF16),
            pltpu.VMEM((2 * rows, width), BF16),
        ],
    )
    turned_a = plane_turn(steps_a, others=(parts_b[0],), micros=3)
    grad_middle = after(grad_middle, parts_b[0], *turned_a)
    grad_features, small_kept, small_sent = call(
        embed_back_kernel,
        (
            kept_b, sent_b, w_query, w_key, w_value, wq_got, wk_got, wv_got, ident,
            grad_middle, embed_args[0], nodes, *embed_args[4:7],
        ),
        [whole()] * 10 + [outside()] * 5,
        [((rows, dim), F32), ((small_b, width), F32), ((small_b, width), BF16)],
        scratch=[
            pltpu.VMEM((rows, dim), BF16),
            count_scratch,
            pltpu.VMEM((idw, dim), BF16),
            pltpu.VMEM((2, dim), BF16),
            wide_scratch,
            pltpu.SemaphoreType.DMA((5,)),
            pltpu.VMEM((rows, dim), F32),
            pltpu.VMEM((small_b, dim), F32),
        ],
        micros=0,
    )
    small_got = swap(small_sent)
    steps_b = plane_step(parts_b[:4], small_b, late=(small_kept, small_got, parts_b[4]))
    line_a = line_step(turned_a, others=steps_b, micros=3)
    turned_b = plane_turn(steps_b, others=line_a[:1])
    lines_a = line_back(*line_a, others=turned_b, micros=1)
    line_b = line_step(turned_b, micros=12)
    sides_a = plane_back((lines_a[1], lines_a[1]))
    far_a = plane_back_turn(*sides_a)
    planes_a = (lines_a[1], *sides_a, *far_a)
    lines_b = line_back(*line_b, micros=2)
    result = call(
        result_kernel,
        (middle, active, w_down, wd_got, lanes(after(bias_down, lines_b[1]))),
        [whole()] * 5,
        [((rows, dim), BF16)],
    )[0]
    wide, half = ((dim // LANES, LANES), F32), ((width // LANES, LANES), F32)
    sums_a = call(
        finish_first_kernel,
        (lines_a[2], swap(after(lines_a[2], lines_b[1]))),
        [whole()] * 2,
        [wide] * 4 + [half],
    )
    grad_w_up, grad_w_out, grad_w_down = placed(planes_a, True, micros=10)
    sides_b = plane_back(lines_b)
    sides_b, _ = lax.optimization_barrier((sides_b, (result, sums_a, grad_w_up)))
    near_b = placed((lines_b[1], sides_b[0], sides_b[1]), False)
    far_b = plane_back_turn(*sides_b)
    far_b, near_b = lax.optimization_barrier((far_b, near_b))
    extra = sides_b[0][OUTER * chunk :]
    own_b = lines_b[2] + extra.astype(F32)
    sums_b = call(
        finish_second_kernel,
        (lines_b[2], extra, swap(own_b)),
        [whole()] * 3,
        [((idw, dim), F32), ((2, dim), F32), wide, wide, half, half],
    )
    grad_w_query, grad_w_key, grad_w_value = call(
        corner_kernel,
        (*far_b, *near_b),
        [whole()] * 2 + [outside()] * 3,
        [((dim, width), F32)] * 3,
        scratch=[
            pltpu.VMEM((3, dim // INNER, width), F32),
            pltpu.SemaphoreType.DMA((3,)),
        ],
        in_place={2: 0, 3: 1, 4: 2},
    )
    return (
        result,
        grad_features,
        sums_b[0],
        sums_b[1],
        sums_b[2].reshape(-1),
        sums_b[3].reshape(-1),
        grad_w_query,
        grad_w_key,
        grad_w_value,
        sums_b[4].reshape(-1),
        sums_b[5].reshape(-1),
        grad_w_out,
        sums_a[0].reshape(-1),
        sums_a[1].reshape(-1),
        sums_a[2].reshape(-1),
        grad_w_up,
        sums_a[4].reshape(-1),
        grad_w_down,
        sums_a[3].reshape(-1),
    )


def solution(mesh):
    token, split = P("dp", None), P(("dp", "mp"), None)
    columns, lines, cut, copy = P(None, "mp"), P("mp", None), P("mp"), P()
    return jax.shard_map(
        per_device,
        mesh=mesh,
        in_specs=(
            token, token, P("dp"), P("dp"), token, copy, copy, copy, copy, columns, columns,
            columns, cut, cut, lines, copy, copy, copy, columns, cut, lines, copy, token,
        ),
        out_specs=(
            split, split, copy, copy, copy, copy, columns, columns, columns, cut, cut, lines,
            copy, copy, copy, columns, cut, lines, copy,
        ),
        check_vma=False,
    )
```

```python
import math

import jax
import jax.numpy as jnp
from jax import lax
from jax.experimental import pallas as pl
from jax.experimental.pallas import tpu as pltpu
from jax.sharding import PartitionSpec as P

HDIM = 24
SEQ = 128
LANES = 128
INNER = 4
OUTER = 4
EPSILON = 1e-05
SCALE = 1.0 / math.sqrt(HDIM)
LOG2_SCALE = SCALE * math.log2(math.e)
F32, BF16 = jnp.float32, jnp.bfloat16
MIB = 1024 * 1024


def dot(left, right):
    return jnp.dot(left, right, preferred_element_type=F32)


def dot_nt(left, right):
    return lax.dot_general(left, right, (((1,), (1,)), ((), ())), preferred_element_type=F32)


def dot_tn(left, right):
    return lax.dot_general(left, right, (((0,), (0,)), ((), ())), preferred_element_type=F32)


def norm_parts(hidden):
    average = jnp.mean(hidden, axis=-1, keepdims=True)
    centred = hidden - average
    inverse = lax.rsqrt(jnp.mean(centred * centred, axis=-1, keepdims=True) + EPSILON)
    return centred * inverse, inverse


def norm_back(unit, inverse, grad_hat):
    return inverse * (
        grad_hat
        - jnp.mean(grad_hat, axis=-1, keepdims=True)
        - unit * jnp.mean(grad_hat * unit, axis=-1, keepdims=True)
    )


def row_sum(block):
    return jnp.sum(block, axis=0, keepdims=True)


def positions(length):
    return lax.broadcasted_iota(jnp.int32, (length, 1), 0)


def whole():
    return pl.BlockSpec(memory_space=pltpu.VMEM)


def outside():
    return pl.BlockSpec(memory_space=pltpu.HBM)


def places():
    index = lax.axis_index("dp")
    return lax.axis_index("mp"), index % INNER, index // INNER % OUTER


def copy_in(sources, targets, sems):
    copies = [
        pltpu.make_async_copy(source, target, sems.at[place])
        for place, (source, target) in enumerate(zip(sources, targets))
    ]
    for copy in copies:
        copy.start()
    return copies


def row_of(ref):
    block = ref[...].astype(F32)
    return jnp.concatenate([block[r : r + 1, :] for r in range(block.shape[0])], axis=1)


def put_row(ref, row):
    for r in range(ref.shape[0]):
        ref[r : r + 1, :] = row[:, r * LANES : (r + 1) * LANES]


def call(kernel, args, specs, outs, scratch=(), micros=0, limit=24, in_place=None):
    return pl.pallas_call(
        kernel,
        out_shape=[jax.ShapeDtypeStruct(shape, kind) for shape, kind in outs],
        in_specs=specs,
        out_specs=[outside() if in_place else whole() for _ in outs],
        input_output_aliases=in_place or {},
        scratch_shapes=list(scratch),
        compiler_params=pltpu.CompilerParams(vmem_limit_bytes=limit * MIB),
        cost_estimate=pl.CostEstimate(
            flops=micros * 1_000_000_000, bytes_accessed=0, transcendentals=0
        ),
    )(*args)


def head_windows(width):
    windows = []
    for pair in range(width // (2 * HDIM)):
        low = pair * 2 * HDIM // LANES * LANES
        high = -(-(pair + 1) * 2 * HDIM // LANES) * LANES
        windows.append((low, high))
    return windows


def head_masks(windows):
    masks = []
    for pair, (low, high) in enumerate(windows):
        column = low + lax.broadcasted_iota(jnp.int32, (16, high - low), 1)
        masks.append(
            [
                jnp.where(
                    (column >= head * HDIM) & (column < (head + 1) * HDIM), 1.0, 0.0
                ).astype(BF16)
                for head in (2 * pair, 2 * pair + 1)
            ]
        )
    return masks


def split_heads(block, masks, window):
    part = block[:, window[0] : window[1]]
    tiles = block.shape[0] // 16
    return jnp.concatenate(
        [part * jnp.concatenate([mask] * tiles, axis=0) for mask in masks], axis=0
    )


def embed_rows(feats, lap, ends, w_ident, types, gain, shift, at, count):
    table = lap[:, at]
    slot = lax.broadcasted_iota(jnp.int32, (SEQ, SEQ), 0)
    picked = []
    for end in (0, 1):
        pick = jnp.where(ends[end : end + 1, at] == slot, 1.0, 0.0).astype(BF16)
        picked.append(dot(table, pick))
    ident = jnp.concatenate(picked, axis=0).astype(BF16)
    hidden = feats[at, :].astype(F32) + dot_tn(ident, w_ident[...])
    kinds = types[...].astype(F32)
    hidden = hidden + jnp.where(positions(SEQ) >= count, kinds[1:2, :], kinds[0:1, :])
    unit, _ = norm_parts(hidden)
    return hidden, ident, (unit * gain + shift).astype(BF16)


def embed_kernel(
    feats_in, lap_in, ends_in, nodes_in, w_ident_in, types_in, gain_in, shift_in,
    bias_q_in, bias_v_in, wq_in, wk_in, wv_in, edges_in,
    hidden_out, ident_out, normed_out, normed_t_out, q_out, k_out, v_out, keep_out,
    feats, lap, ends, nodes, w_ident, types, gain_rows, shift_rows, bias_q, bias_v,
    w_q, w_k, w_v, edges, sems,
):
    rows, dim = feats.shape
    mols = rows // SEQ
    core = places()[0]
    own_rows = pl.ds(pl.multiple_of(core * rows, SEQ), rows)
    copies = copy_in(
        (
            feats_in.at[own_rows, :], lap_in.at[:, own_rows], ends_in.at[:, own_rows], nodes_in,
            w_ident_in, types_in, gain_in, shift_in, bias_q_in, bias_v_in, wq_in, wk_in, wv_in,
            edges_in,
        ),
        (
            feats, lap, ends, nodes, w_ident, types, gain_rows, shift_rows, bias_q, bias_v,
            w_q, w_k, w_v, edges,
        ),
        sems,
    )
    for copy in copies[:10]:
        copy.wait()
    gain, shift = row_of(gain_rows), row_of(shift_rows)

    def molecule(m):
        at = slice(m * SEQ, (m + 1) * SEQ)
        count = nodes[core * mols + m]
        hidden, ident, normed = embed_rows(
            feats, lap, ends, w_ident, types, gain, shift, at, count
        )
        ident_out[:, at] = ident
        hidden_out[at, :] = hidden
        normed_out[at, :] = normed
        normed_t_out[:, at] = normed.T

    for m in range(mols):
        molecule(m)
    normed = normed_out[...]
    copies[10].wait()
    q_out[...] = (dot(normed, w_q[...]) + row_of(bias_q)).astype(BF16)
    copies[11].wait()
    k_out[...] = dot(normed, w_k[...]).astype(BF16)
    copies[12].wait()
    v_out[...] = (dot(normed, w_v[...]) + row_of(bias_v)).astype(BF16)
    copies[13].wait()
    for m in range(2 * mols):
        inside = lax.broadcasted_iota(jnp.int32, (SEQ, LANES), 0) < nodes[m] + edges[m]
        keep_out[m * SEQ : (m + 1) * SEQ, :] = jnp.where(inside, 1.0, 0.0)


def forward_kernel(
    hidden, normed, q_own, k_own, v_own, w_q, w_k, w_v, wo_own, wo, wu_own, wu,
    bias_q, bias_v, bias_u,
    nodes_in, edges_in, bias_u_own_in, bias_o_in, gain_in, shift_in,
    q_out, k_out, v_out, probs_out, keep_out, send_out, middle, active, slope,
    nodes, edges, bias_u_own, bias_o, gain_rows, shift_rows, sems,
    mixed, attended, normed_two,
):
    rows, dim = hidden.shape
    width = q_own.shape[1]
    mols = rows // SEQ
    pairs = width // (2 * HDIM)
    windows = head_windows(width)
    masks = head_masks(windows)
    core = places()[0]
    copies = copy_in(
        (nodes_in, edges_in, bias_u_own_in, bias_o_in, gain_in, shift_in),
        (nodes, edges, bias_u_own, bias_o, gain_rows, shift_rows),
        sems,
    )

    for copy in copies:
        copy.wait()
    gain, shift, bias_out = row_of(gain_rows), row_of(shift_rows), row_of(bias_o)

    sides = ((q_own, k_own, v_own, keep_out), (q_out, k_out, v_out, send_out))
    units = [(m, side) for side in (0, 1) for m in range(mols)]

    def weigh(unit, pair):
        m, side = unit
        at = slice(m * SEQ, (m + 1) * SEQ)
        place = core * mols + m
        key_keep = positions(SEQ) < nodes[place] + edges[place]
        low, high = windows[pair]
        both = split_heads(sides[side][0][at, :], masks[pair], windows[pair])
        scores = dot_nt(sides[side][1][at, low:high], both)
        scores = jnp.where(key_keep, scores, -1e30)
        top = jnp.max(scores, axis=0, keepdims=True)
        raised = jnp.exp2((scores - top) * LOG2_SCALE)
        probs_out[m, side * pairs + pair] = (raised * (1.0 / row_sum(raised))).astype(BF16)

    def mix(step, pair, values_t):
        m, side = units[step]
        first = pair * 2 * HDIM
        out = dot(values_t[first : first + 2 * HDIM], probs_out[m, side * pairs + pair])
        mixed[step % 2, first : first + HDIM, :] = out[:HDIM, :SEQ]
        mixed[step % 2, first + HDIM : first + 2 * HDIM, :] = out[HDIM:, SEQ:]

    def keep_mixed(step):
        m, side = units[step]
        at = slice(m * SEQ, (m + 1) * SEQ)
        place = core * mols + m
        query_keep = lax.broadcasted_iota(jnp.int32, (1, SEQ), 1) < nodes[place] + edges[place]
        kept = jnp.where(query_keep, mixed[step % 2], 0.0).astype(BF16)
        sides[side][3][dim : dim + width, at] = kept
        attended[at, side * width : (side + 1) * width] = kept.T

    partner = ((q_out, w_q, bias_q), (k_out, w_k, None), (v_out, w_v, bias_v))
    for pair in range(pairs):
        weigh(units[0], pair)
        if pair % 2 == 0 and pair // 2 < len(partner):
            out, weight, bias = partner[pair // 2]
            rows_of = dot(normed[...], weight[...])
            out[...] = (rows_of if bias is None else rows_of + row_of(bias)).astype(BF16)
    for step, task in enumerate(units):
        values_t = sides[task[1]][2][task[0] * SEQ : (task[0] + 1) * SEQ, :].T
        for pair in range(pairs):
            mix(step, pair, values_t)
            if step + 1 < len(units):
                weigh(units[step + 1], pair)
        keep_mixed(step)
    middle[...] = (
        hidden[...] + dot(attended[:, :width], wo_own[...]) + dot(attended[:, width:], wo[...])
    )

    for m in range(mols):
        at = slice(m * SEQ, (m + 1) * SEQ)
        total = middle[at, :] + bias_out
        middle[at, :] = total
        unit_rows, _ = norm_parts(total)
        rows_two = (unit_rows * gain + shift).astype(BF16)
        normed_two[at, :] = rows_two
        turned = rows_two.T
        keep_out[:dim, at] = turned
        send_out[:dim, at] = turned

    for side, (w_ref, b_ref, part_out) in enumerate(
        ((wu_own, bias_u_own, keep_out), (wu, bias_u, send_out))
    ):
        columns = slice(side * width, (side + 1) * width)
        slope[:, columns] = dot(normed_two[...], w_ref[...]) + row_of(b_ref)

        for m in range(mols):
            at = slice(m * SEQ, (m + 1) * SEQ)
            before = slope[at, columns]
            phi = 0.5 * (1.0 + lax.erf(before * math.sqrt(0.5)))
            out = (before * phi).astype(BF16)
            slope[at, columns] = phi + before * jnp.exp(before * before * -0.5) * (
                1.0 / math.sqrt(2.0 * math.pi)
            )
            active[at, columns] = out
            part_out[dim + width : dim + 2 * width, at] = out.T


def ffn_back_kernel(
    middle, slope, wu_own, wu, wd_own, wd, keep_rows, cots, gain_in,
    keep_out, send_out, gm_out, grad_branch,
    gain_rows, sems, grad_ffn,
):
    rows, dim = middle.shape
    width = wd.shape[0]
    mols = rows // SEQ
    core = places()[0]
    copies = copy_in((gain_in,), (gain_rows,), sems)

    def own_cots(m):
        at = pl.ds(pl.multiple_of(core * rows + m * SEQ, SEQ), SEQ)
        return jnp.where(keep_rows[at, 0:1] > 0.5, cots[at, :].astype(F32), 0.0)

    for m in range(mols):
        at = slice(m * SEQ, (m + 1) * SEQ)
        grad_ffn[at, :] = own_cots(m).astype(BF16)
    place_b = 0
    for side, (w_ref, part_out) in enumerate(((wd_own, keep_out), (wd, send_out))):
        columns = slice(side * width, (side + 1) * width)
        grad_before = slope[:, columns] * dot_nt(grad_ffn[...], w_ref[...])
        part_out[place_b : place_b + rows, :] = grad_before.astype(BF16)

    back = pl.ds(place_b, rows)
    gm_out[...] = dot_nt(keep_out[back, :], wu_own[...]) + dot_nt(send_out[back, :], wu[...])

    copies[0].wait()
    gain = row_of(gain_rows)
    nothing = jnp.zeros((1, dim), F32)
    sums = (nothing,) * 4
    for m in range(mols):
        at = slice(m * SEQ, (m + 1) * SEQ)
        grad_normed = gm_out[at, :]
        unit_rows, inverse = norm_parts(middle[at, :])
        grad_result = own_cots(m)
        grad = grad_result + norm_back(unit_rows, inverse, grad_normed * gain)
        gm_out[at, :] = grad
        grad_branch[at, :] = grad.astype(BF16)
        sums = (
            sums[0] + row_sum(grad),
            sums[1] + row_sum(grad_normed * unit_rows),
            sums[2] + row_sum(grad_normed),
            sums[3] + row_sum(grad_result),
        )

    place_m = place_b + rows
    for part_out in (keep_out, send_out):
        part_out[place_m : place_m + rows, :] = grad_branch[:, :width]
        part_out[place_m + rows : place_m + 2 * rows, :] = grad_branch[:, width:]
    small = jnp.concatenate(list(sums) + [nothing] * 12, axis=0)
    left, right = small[:, :width], small[:, width:]
    place_s = place_m + 2 * rows
    keep_out[place_s:, :] = jnp.where(core == 0, left, right).astype(BF16)
    send_out[place_s:, :] = jnp.where(core == 0, right, left).astype(BF16)


def result_kernel(middle, active, wd_own, wd, bias, result_out):
    width = wd.shape[0]
    result_out[...] = (
        middle[...]
        + dot(active[:, :width], wd_own[...])
        + dot(active[:, width:], wd[...])
        + row_of(bias)
    ).astype(BF16)


def branch_kernel(grad_branch, wo_own, wo, keep_rows, ga_own_out, ga_out):
    rows = grad_branch.shape[0]
    own_rows = pl.ds(pl.multiple_of(places()[0] * rows, SEQ), rows)
    keep = keep_rows[own_rows, 0:1] > 0.5
    for ref, weight in ((ga_own_out, wo_own), (ga_out, wo)):
        ref[...] = jnp.where(keep, dot_nt(grad_branch[...], weight[...]), 0.0).astype(BF16)


def attend_back_kernel(
    q_own, k_own, v_own, ga_own, q_got, k_got, v_got, ga_got, probs_all,
    keep_out, send_out, dq_t, dk, dv, slopes,
):
    rows, width = q_own.shape
    pairs = width // (2 * HDIM)
    windows = head_windows(width)
    masks = head_masks(windows)
    sides = (
        (q_own, k_own, v_own, ga_own, keep_out),
        (q_got, k_got, v_got, ga_got, send_out),
    )
    units = [(m, side) for m in range(rows // SEQ) for side in (0, 1)]

    def score_back(unit, pair):
        m, side = unit
        at = slice(m * SEQ, (m + 1) * SEQ)
        low, high = windows[pair]
        both_g = split_heads(sides[side][3][at, :], masks[pair], windows[pair])
        probs_low = probs_all[m, side * pairs + pair]
        probs = probs_low.astype(F32)
        grad_probs = dot_nt(sides[side][2][at, low:high], both_g)
        inner = row_sum(probs * grad_probs)
        slopes[side, pair] = (probs * (grad_probs - inner)).astype(BF16)
        dv[side, :, low:high] += dot(probs_low, both_g)

    def rows_back(unit, pair, keys_t):
        m, side = unit
        low, high = windows[pair]
        grad_scores = slopes[side, pair]
        both_q = split_heads(sides[side][0][m * SEQ : (m + 1) * SEQ, :], masks[pair], windows[pair])
        dk[side, :, low:high] += dot(grad_scores, both_q)
        first = pair * 2 * HDIM
        out = dot(keys_t[first : first + 2 * HDIM], grad_scores)
        dq_t[side, first : first + HDIM, :] = out[:HDIM, :SEQ]
        dq_t[side, first + HDIM : first + 2 * HDIM, :] = out[HDIM:, SEQ:]

    def begin(unit):
        dk[unit[1]] = jnp.zeros_like(dk[unit[1]])
        dv[unit[1]] = jnp.zeros_like(dv[unit[1]])

    def finish(unit):
        m, side = unit
        part_out = sides[side][4]
        base = m * SEQ
        part_out[base : base + SEQ, :] = (dq_t[side] * SCALE).astype(BF16).T
        part_out[rows + base : rows + base + SEQ, :] = (dk[side] * SCALE).astype(BF16)
        part_out[2 * rows + base : 2 * rows + base + SEQ, :] = dv[side].astype(BF16)

    begin(units[0])
    for pair in range(pairs):
        score_back(units[0], pair)
    for step, unit in enumerate(units):
        keys_t = sides[unit[1]][1][unit[0] * SEQ : (unit[0] + 1) * SEQ, :].T
        if step + 1 < len(units):
            begin(units[step + 1])
        for pair in range(pairs):
            rows_back(unit, pair, keys_t)
            if step + 1 < len(units):
                score_back(units[step + 1], pair)
        finish(unit)


def embed_back_kernel(*refs):
    (
        grads_own, grads,
        wq_own, wk_own, wv_own, w_q, w_k, w_v, ident, grad_middle,
        feats_in, nodes_in, w_ident_in, types_in, gain_in,
        features_out, keep_out, send_out,
        feats, nodes, w_ident, types, gain_rows, sems, grad_normed, small,
    ) = refs
    core = places()[0]
    rows = feats.shape[0]
    copies = copy_in(
        (
            feats_in.at[pl.ds(pl.multiple_of(core * rows, SEQ), rows), :], nodes_in,
            w_ident_in, types_in, gain_in,
        ),
        (feats, nodes, w_ident, types, gain_rows),
        sems,
    )
    rows, dim = feats.shape
    width = wq_own.shape[1]
    idw = ident.shape[0]
    total = None
    for part, weights in ((grads_own, (wq_own, wk_own, wv_own)), (grads, (w_q, w_k, w_v))):
        for place, weight in enumerate(weights):
            term = dot_nt(part[place * rows : (place + 1) * rows, :], weight[...])
            total = term if total is None else total + term
    grad_normed[...] = total
    mols = rows // SEQ
    small[...] = jnp.zeros_like(small)
    for copy in copies:
        copy.wait()
    gain = row_of(gain_rows)
    kinds = types[...].astype(F32)

    def molecule(m, carry):
        at = pl.ds(pl.multiple_of(m * SEQ, SEQ), SEQ)
        is_edge = positions(SEQ) >= nodes[core * mols + m]
        hidden = feats[at, :].astype(F32) + dot_tn(ident[:, at], w_ident[...])
        hidden = hidden + jnp.where(is_edge, kinds[1:2, :], kinds[0:1, :])
        unit, inverse = norm_parts(hidden)
        grad_rows = grad_normed[at, :]
        grad = grad_middle[at, :] + norm_back(unit, inverse, grad_rows * gain)
        features_out[at, :] = grad
        high = grad.astype(BF16)
        rest = (grad - high.astype(F32)).astype(BF16)
        picked = ident[:, at]
        small[:idw, :] += dot(picked, high) + dot(picked, rest)
        edge_rows = jnp.where(is_edge, grad, 0.0)
        small[idw : idw + 1, :] += row_sum(grad - edge_rows)
        small[idw + 1 : idw + 2, :] += row_sum(edge_rows)
        small[idw + 2 : idw + 3, :] += row_sum(grad_rows * unit)
        small[idw + 3 : idw + 4, :] += row_sum(grad_rows)
        return carry

    lax.fori_loop(0, mols, molecule, 0)
    left, right = small[:, :width], small[:, width:]
    keep_out[...] = jnp.where(core == 0, left, right)
    send_out[...] = jnp.where(core == 0, right, left).astype(BF16)


def deal(unit, places_in, outs, block_at, small=None):
    _, inner, outer = places()
    first_kept, first_sent, second_kept, second_sent = outs
    for step in range(INNER):
        for turn in range(OUTER):
            if turn < 2:
                out, slot = (first_sent if step % 2 else first_kept), step // 2
            else:
                out, slot = (second_sent if step // 2 else second_kept), step % 2
            start = (slot * 2 + turn % 2) * places_in * unit
            for place in range(places_in):
                out[start + place * unit : start + (place + 1) * unit, :] = block_at(
                    inner ^ step, outer ^ turn, place
                )
    if small is not None:
        for out in (first_kept, first_sent):
            out[INNER * places_in * unit :, :] = small


def flat_block(flat, unit, dest, z):
    row = pl.multiple_of((dest * (OUTER // 2) + z // 2) * unit, 16)
    return flat[z % 2, pl.ds(row, unit), :]


def down_grads_kernel(kept, got, cots, keep_rows, *rest):
    outs, (flat, grad_ffn) = rest[:4], rest[4:]
    rows_all, dim = cots.shape
    rows, width = rows_all // 2, kept.shape[1]
    core = places()[0]
    for m in range(rows_all // SEQ):
        at = slice(m * SEQ, (m + 1) * SEQ)
        grad_ffn[at, :] = jnp.where(keep_rows[at, 0:1] > 0.5, cots[at, :].astype(F32), 0.0).astype(BF16)
    own_rows = pl.ds(pl.multiple_of(core * rows, SEQ), rows)
    other_rows = pl.ds(pl.multiple_of((1 - core) * rows, SEQ), rows)
    turned = slice(dim + width, dim + 2 * width)
    for half in (0, 1):
        columns = slice(half * width, (half + 1) * width)
        product = dot(kept[turned, :], grad_ffn[own_rows, columns])
        product = product + dot(got[turned, :], grad_ffn[other_rows, columns])
        flat[half] = product.astype(BF16)
    unit = dim // (INNER * OUTER)
    deal(unit, 1, outs, lambda dest, z, place: flat_block(flat, unit, dest, z))


def ffn_grads_kernel(kept, got, kept_back, got_back, *rest):
    outs, (tall, flat) = rest[:4], rest[4:]
    rows, width = kept.shape[1], kept.shape[1]
    dim = kept.shape[0] - 2 * width
    back, place_s = slice(0, rows), 3 * rows
    tall[...] = (
        dot(kept[:dim, :], kept_back[back, :]) + dot(got[:dim, :], got_back[back, :])
    ).astype(BF16)
    turned = slice(dim, dim + width)
    for half in (0, 1):
        mid = slice((1 + half) * rows, (2 + half) * rows)
        flat[half] = (
            dot(kept[turned, :], kept_back[mid, :]) + dot(got[turned, :], got_back[mid, :])
        ).astype(BF16)
    bias = row_sum(kept_back[back, :].astype(F32)) + row_sum(got_back[back, :].astype(F32))
    small = kept_back[place_s:, :].astype(F32) + got_back[place_s:, :].astype(F32)
    spot = lax.broadcasted_iota(jnp.int32, small.shape, 0)
    small = jnp.where(spot == 4, bias, small).astype(BF16)
    unit = dim // (INNER * OUTER)

    def block_at(dest, z, place):
        if place == 0:
            return tall[pl.ds(pl.multiple_of((dest * OUTER + z) * unit, 16), unit), :]
        return flat_block(flat, unit, dest, z)

    deal(unit, 2, outs, block_at, small)


def qkv_grads_kernel(normed_t, normed_t_got, kept, got, *refs):
    outs, small_out, (tall, normed, stacked) = refs[:4], refs[4], refs[5:]
    dim, rows = normed_t.shape
    unit = dim // (INNER * OUTER)
    normed[:, :rows] = normed_t[...]
    normed[:, rows:] = normed_t_got[...]
    spot = lax.broadcasted_iota(jnp.int32, small_out.shape, 0)
    small = jnp.zeros(small_out.shape, F32)
    for place in range(3):
        part = slice(place * rows, (place + 1) * rows)
        stacked[:rows, :] = kept[part, :]
        stacked[rows:, :] = got[part, :]
        tall[place] = dot(normed[...], stacked[...]).astype(BF16)
        if place != 1:
            small = jnp.where(spot == 36 + place // 2, row_sum(stacked[...].astype(F32)), small)
    small_out[...] = small

    def block_at(dest, z, place):
        return tall[place, pl.ds(pl.multiple_of((dest * OUTER + z) * unit, 16), unit), :]

    deal(unit, 3, outs, block_at)


def add(first, second):
    return (first.astype(F32) + second.astype(F32)).astype(BF16)


def plane_sum_kernel(first, first_got, second, second_got, *refs):
    late, (first_kept, first_sent, second_kept, second_sent) = refs[:-4], refs[-4:]
    pair = second_kept.shape[0]
    total = add(first[...], first_got[...])
    first_kept[:pair, :] = total[:pair]
    first_sent[:pair, :] = total[pair : 2 * pair]
    if late:
        small = (late[0][...] + late[1][...].astype(F32) + late[2][...]).astype(BF16)
    else:
        small = total[2 * pair :]
    first_kept[pair:, :] = small
    first_sent[pair:, :] = small
    total = add(second[...], second_got[...])
    second_kept[...] = total[:pair]
    second_sent[...] = total[pair:]


def plane_join_kernel(first, first_got, second, second_got, *refs):
    ahead, outs = refs[:4], refs[4:]
    unit = ahead[0].shape[0] // 4
    small = add(first[8 * unit :, :], first_got[8 * unit :, :])
    for place, (left, right, more, more_got) in enumerate(
        ((first, first_got, *ahead[:2]), (second, second_got, *ahead[2:]))
    ):
        total = add(left[: 8 * unit, :], right[: 8 * unit, :])
        late = add(more[...], more_got[...])
        for block in range(4):
            out = outs[2 * place + block // 2]
            start = block % 2 * 3 * unit
            out[start : start + 2 * unit, :] = total[2 * block * unit : 2 * (block + 1) * unit]
            out[start + 2 * unit : start + 3 * unit, :] = late[block * unit : (block + 1) * unit]
    for out in outs[:2]:
        out[6 * unit :, :] = small


def line_cut_kernel(first, first_got, second, second_got, own, near, middle, far):
    chunk = own.shape[0]
    total = add(first[...], first_got[...])
    own[...] = total[:chunk]
    near[...] = total[chunk:]
    total = add(second[...], second_got[...])
    middle[...] = total[:chunk]
    far[...] = total[chunk:]


def line_sum_kernel(own, near, near_got, middle_got, far_got, out, out_small):
    chunk = own.shape[0]
    total = own[...].astype(F32) + near_got[:chunk, :].astype(F32)
    total = total + middle_got[...].astype(F32) + far_got[...].astype(F32)
    out[...] = total.astype(BF16)
    out_small[:chunk, :] = total.astype(BF16)
    out_small[chunk:, :] = add(near[chunk:, :], near_got[chunk:, :])


def line_join_kernel(own, near, middle, far, line_x, line_y, small_out):
    chunk = near.shape[0]
    small = own[chunk:, :].astype(F32) + middle[chunk:, :].astype(F32)
    small_out[...] = small
    for out in (line_x, line_y):
        for turn, part in enumerate((own, near, middle, far)):
            out[turn * chunk : (turn + 1) * chunk, :] = part[:chunk, :]
    line_x[OUTER * chunk :, :] = small.astype(BF16)


def place_kernel(split_second, *refs):
    outs, parts = refs[-3:], refs[:-3]
    own = parts[0]
    steps = min(len(parts), INNER)
    _, inner, outer = places()
    unit = own.shape[0] // (3 * OUTER)
    width = own.shape[1]
    for step in range(steps):
        for turn in range(OUTER):
            ref, start = parts[step], turn * 3 * unit
            if step == 3 and turn >= 2:
                ref, start = parts[4], (turn - 2) * 3 * unit
            dest, z = inner ^ step, outer ^ turn
            tall = pl.ds(pl.multiple_of((dest * OUTER + z) * unit, 16), unit)
            flat = pl.ds(pl.multiple_of((dest * (OUTER // 2) + z // 2) * unit, 16), unit)
            columns = pl.ds(pl.multiple_of(z % 2 * width, LANES), width)
            for place in range(3):
                part = ref[start + place * unit : start + (place + 1) * unit, :].astype(F32)
                if split_second and place > 0:
                    outs[place][flat, columns] = part
                else:
                    outs[place][tall, :] = part


def corner_kernel(first, second, *refs):
    outs, blocks, sems = refs[3:6], refs[6], refs[7]
    _, inner, outer = places()
    unit = first.shape[0] // 6
    size = OUTER * unit
    for turn in range(OUTER):
        ref, start = (first, turn * 3 * unit) if turn < 2 else (second, (turn - 2) * 3 * unit)
        at = pl.ds(pl.multiple_of((outer ^ turn) * unit, 16), unit)
        for place in range(3):
            rows = slice(start + place * unit, start + (place + 1) * unit)
            blocks[place, at, :] = ref[rows, :].astype(F32)
    at = pl.ds(pl.multiple_of((inner ^ 3) * size, 64), size)
    copies = copy_in(
        [blocks.at[place] for place in range(3)], [out.at[at, :] for out in outs], sems
    )
    for copy in copies:
        copy.wait()


def finish_first_kernel(small, got, bias_out, gain, shift, bias_down, bias_up):
    core = places()[0]
    for place, ref in enumerate((bias_out, gain, shift, bias_down)):
        mine, other = small[place : place + 1, :], got[place : place + 1, :]
        left = jnp.where(core == 0, mine, other)
        put_row(ref, jnp.concatenate([left, jnp.where(core == 0, other, mine)], axis=1))
    put_row(bias_up, small[4:5, :])


def finish_second_kernel(small, extra, got, w_ident, types, gain, shift, bias_q, bias_v):
    idw = w_ident.shape[0]
    core = places()[0]
    mine, other = small[...] + extra[...].astype(F32), got[...]
    left = jnp.where(core == 0, mine, other)
    total = jnp.concatenate([left, jnp.where(core == 0, other, mine)], axis=1)
    w_ident[...] = total[:idw]
    types[...] = total[idw : idw + 2]
    put_row(gain, total[idw + 2 : idw + 3])
    put_row(shift, total[idw + 3 : idw + 4])
    put_row(bias_q, mine[idw + 4 : idw + 5])
    put_row(bias_v, mine[idw + 5 : idw + 6])


def per_device(
    features, lap_vectors, node_counts, edge_counts, endpoints, w_ident, type_table,
    gain_one, shift_one, w_query, w_key, w_value, bias_query, bias_value, w_out, bias_out,
    gain_two, shift_two, w_up, bias_up, w_down, bias_down, cotangent,
):
    dp_count = lax.axis_size("dp")
    dp_index = lax.axis_index("dp")
    mp_index = lax.axis_index("mp")
    block = INNER * OUTER
    rest_count = dp_count // block
    def swap(part):
        return lax.ppermute(part, "mp", [(0, 1), (1, 0)])

    def inner_move(part, step):
        return lax.ppermute(part, "dp", [(s, s ^ step) for s in range(dp_count)])

    def outer_move(part, step):
        return lax.ppermute(part, "dp", [(s, s ^ (step * INNER)) for s in range(dp_count)])

    rows_all, dim = features.shape
    rows = rows_all // 2
    mols = rows // SEQ
    width = w_query.shape[1]
    heads = width // HDIM
    lapk = lap_vectors.shape[1]
    idw = w_ident.shape[0]

    def pinned(part):
        return pltpu.with_memory_space_constraint(part, pltpu.HBM)

    def lanes(part):
        return pinned(part.reshape(-1, LANES))

    nodes, edges = pinned(node_counts), pinned(edge_counts)
    count_scratch = pltpu.SMEM(node_counts.shape, jnp.int32)
    wide_scratch = pltpu.VMEM((dim // LANES, LANES), BF16)
    half_scratch = pltpu.VMEM((width // LANES, LANES), BF16)
    def after(part, *others):
        return lax.optimization_barrier((part, *others))[0]

    embed_args = (
        pinned(features), pinned(lap_vectors.T), pinned(endpoints.T), nodes,
        pinned(w_ident), pinned(type_table), lanes(gain_one), lanes(shift_one),
    )
    embed_scratch = [
        pltpu.VMEM((rows, dim), BF16),
        pltpu.VMEM((lapk, rows), BF16),
        pltpu.VMEM((2, rows), jnp.int32),
        count_scratch,
        pltpu.VMEM((idw, dim), BF16),
        pltpu.VMEM((2, dim), BF16),
        wide_scratch,
        wide_scratch,
    ]

    wq_got, wk_got, wv_got = swap(w_query), swap(w_key), swap(w_value)
    bq_got, bv_got, bu_got = swap(bias_query), swap(bias_value), swap(bias_up)
    wo_got, wu_got = swap(w_out), swap(w_up)

    hidden, ident, normed, normed_t, q_own, k_own, v_own, keep_rows = call(
        embed_kernel,
        (
            *embed_args, lanes(bias_query), lanes(bias_value),
            pinned(w_query), pinned(w_key), pinned(w_value), edges,
        ),
        [outside()] * 14,
        [
            ((rows, dim), F32),
            ((idw, rows), BF16),
            ((rows, dim), BF16),
            ((dim, rows), BF16),
            ((rows, width), BF16),
            ((rows, width), BF16),
            ((rows, width), BF16),
            ((rows_all, LANES), F32),
        ],
        scratch=embed_scratch
        + [half_scratch] * 2
        + [pltpu.VMEM((dim, width), BF16)] * 3
        + [count_scratch, pltpu.SemaphoreType.DMA((14,))],
    )
    wd_got = swap(after(w_down, normed))
    ahead_rows, back_rows = dim + 2 * width, 3 * rows + 16
    q_got, k_got, v_got, probs, kept_a, sent_a, middle, active, slope = call(
        forward_kernel,
        (
            hidden, normed, q_own, k_own, v_own, wq_got, wk_got, wv_got,
            w_out, wo_got, w_up, wu_got,
            *(part.reshape(-1, LANES) for part in (bq_got, bv_got, bu_got)),
            nodes, edges,
            lanes(bias_up), lanes(bias_out), lanes(gain_two), lanes(shift_two),
        ),
        [whole()] * 15 + [outside()] * 6,
        [
            ((rows, width), BF16),
            ((rows, width), BF16),
            ((rows, width), BF16),
            ((mols, heads, SEQ, 2 * SEQ), BF16),
            ((ahead_rows, width), BF16),
            ((ahead_rows, width), BF16),
            ((rows, dim), F32),
            ((rows, dim), BF16),
            ((rows, dim), F32),
        ],
        scratch=[
            count_scratch,
            count_scratch,
            half_scratch,
            wide_scratch,
            wide_scratch,
            wide_scratch,
            pltpu.SemaphoreType.DMA((6,)),
            pltpu.VMEM((2, width, SEQ), F32),
            pltpu.VMEM((rows, dim), BF16),
            pltpu.VMEM((rows, dim), BF16),
        ],
        limit=30,
    )
    got_a = swap(sent_a)
    kept_back, sent_back, grad_middle, grad_branch = call(
        ffn_back_kernel,
        (
            middle, slope, w_up, wu_got, w_down, wd_got, keep_rows, cotangent,
            lanes(gain_two),
        ),
        [whole()] * 8 + [outside()],
        [
            ((back_rows, width), BF16),
            ((back_rows, width), BF16),
            ((rows, dim), F32),
            ((rows, dim), BF16),
        ],
        scratch=[wide_scratch, pltpu.SemaphoreType.DMA((1,)), pltpu.VMEM((rows, dim), BF16)],
    )
    got_back = swap(sent_back)

    unit = dim // block
    chunk = 3 * unit
    small_a, small_b = 16, 48

    def rest_sum(part):
        if rest_count == 1:
            return part
        groups = [[r * block + s for r in range(rest_count)] for s in range(block)]
        return lax.psum(part.astype(F32), "dp", axis_index_groups=groups).astype(part.dtype)

    pair = 2 * chunk

    def plane_step(parts, small_rows, late=(), others=(), micros=0):
        first, first_sent, second, second_sent = parts
        first_got = after(inner_move(first_sent, 1), *others)
        second_got = after(inner_move(second_sent, 2), *others)
        return call(
            plane_sum_kernel,
            (first, first_got, second, second_got, *late),
            [whole()] * (4 + len(late)),
            [((pair + small_rows, width), BF16)] * 2 + [((pair, width), BF16)] * 2,
            micros=micros,
        )

    def plane_turn(parts, others=(), micros=0):
        first, first_sent, second, second_sent = parts
        first_got = after(inner_move(first_sent, 2), *others)
        second_got = after(inner_move(second_sent, 1), *others)
        return call(
            line_cut_kernel,
            (first, first_got, second, second_got),
            [whole()] * 4,
            [
                ((chunk, width), BF16),
                ((first.shape[0] - chunk, width), BF16),
                ((chunk, width), BF16),
                ((chunk, width), BF16),
            ],
            micros=micros,
        )

    def line_step(parts, others=(), micros=0):
        got = [after(outer_move(parts[turn], turn), *others) for turn in range(1, OUTER)]
        mine, both = call(
            line_sum_kernel,
            (parts[0], parts[1], *got),
            [whole()] * 5,
            [((chunk, width), BF16), (parts[1].shape, BF16)],
            micros=micros,
        )
        if rest_count > 1:
            both = rest_sum(both)
            mine = both[:chunk]
        return mine, both

    def line_back(mine, both, others=(), micros=0):
        sent = (mine, both, mine)
        got = [after(outer_move(sent[turn - 1], turn), *others) for turn in range(1, OUTER)]
        small_rows = both.shape[0] - chunk
        return call(
            line_join_kernel,
            (both, *got),
            [whole()] * OUTER,
            [
                ((OUTER * chunk + small_rows, width), BF16),
                ((OUTER * chunk, width), BF16),
                ((small_rows, width), F32),
            ],
            micros=micros,
        )

    def plane_back(lines):
        return inner_move(lines[0], 1), inner_move(lines[1], 2)

    def plane_back_turn(side_x, side_y):
        return inner_move(side_y[:pair], 1), inner_move(side_x[pair : 2 * pair], 2)

    def placed(planes, split_second, micros=0):
        tall, flat = ((dim, width), F32), ((width, dim), F32)
        return call(
            lambda *refs: place_kernel(split_second, *refs),
            planes,
            [whole()] * len(planes),
            [tall, flat, flat] if split_second else [tall] * 3,
            micros=micros,
        )

    parts_down = call(
        down_grads_kernel,
        (after(kept_a, grad_branch), got_a, cotangent, keep_rows),
        [whole()] * 4,
        [((INNER * unit, width), BF16)] * 4,
        scratch=[pltpu.VMEM((2, width, width), BF16), pltpu.VMEM((rows_all, dim), BF16)],
    )
    parts_a = call(
        ffn_grads_kernel,
        (after(kept_a, parts_down[0]), got_a, kept_back, got_back),
        [whole()] * 4,
        [((2 * INNER * unit + small_a, width), BF16)] * 2 + [((2 * INNER * unit, width), BF16)] * 2,
        scratch=[pltpu.VMEM((dim, width), BF16), pltpu.VMEM((2, width, width), BF16)],
    )
    ahead = [
        after(inner_move(parts_down[1], 1), parts_a[0]),
        after(inner_move(parts_down[3], 2), parts_a[0]),
    ]
    ga_own, ga_got = call(
        branch_kernel,
        (after(grad_branch, parts_a[0], *ahead), w_out, wo_got, keep_rows),
        [whole()] * 4,
        [((rows, width), BF16), ((rows, width), BF16)],
    )

    kept_b, sent_b = call(
        attend_back_kernel,
        (q_own, k_own, v_own, ga_own, q_got, k_got, v_got, ga_got, probs),
        [whole()] * 9,
        [((3 * rows, width), BF16)] * 2,
        scratch=[
            pltpu.VMEM((2, width, SEQ), F32),
            pltpu.VMEM((2, SEQ, width), F32),
            pltpu.VMEM((2, SEQ, width), F32),
            pltpu.VMEM((2, heads // 2, SEQ, 2 * SEQ), BF16),
        ],
    )
    normed_t_got = swap(after(normed_t, parts_a[0]))
    got_b = swap(sent_b)
    moved = [after(inner_move(parts_a[1], 1), kept_b), after(inner_move(parts_a[3], 2), kept_b)]
    moved = moved + ahead
    steps_a = call(
        plane_join_kernel,
        (
            parts_a[0], moved[0], parts_a[2], moved[1],
            parts_down[0], moved[2], parts_down[2], moved[3],
        ),
        [whole()] * 8,
        [((pair + small_a, width), BF16)] * 2 + [((pair, width), BF16)] * 2,
        micros=6,
    )
    normed_t = after(normed_t, *steps_a)
    parts_b = call(
        qkv_grads_kernel,
        (normed_t, normed_t_got, kept_b, got_b),
        [whole()] * 4,
        [((INNER * chunk, width), BF16)] * 4 + [((small_b, width), F32)],
        scratch=[
            pltpu.VMEM((3, dim, width), BF16),
            pltpu.VMEM((dim, 2 * rows), BF16),
            pltpu.VMEM((2 * rows, width), BF16),
        ],
    )
    turned_a = plane_turn(steps_a, others=(parts_b[0],), micros=3)
    grad_middle = after(grad_middle, parts_b[0], *turned_a)
    grad_features, small_kept, small_sent = call(
        embed_back_kernel,
        (
            kept_b, sent_b, w_query, w_key, w_value, wq_got, wk_got, wv_got, ident,
            grad_middle, embed_args[0], nodes, *embed_args[4:7],
        ),
        [whole()] * 10 + [outside()] * 5,
        [((rows, dim), F32), ((small_b, width), F32), ((small_b, width), BF16)],
        scratch=[
            pltpu.VMEM((rows, dim), BF16),
            count_scratch,
            pltpu.VMEM((idw, dim), BF16),
            pltpu.VMEM((2, dim), BF16),
            wide_scratch,
            pltpu.SemaphoreType.DMA((5,)),
            pltpu.VMEM((rows, dim), F32),
            pltpu.VMEM((small_b, dim), F32),
        ],
        micros=0,
    )
    small_got = swap(small_sent)
    steps_b = plane_step(parts_b[:4], small_b, late=(small_kept, small_got, parts_b[4]))
    line_a = line_step(turned_a, others=steps_b, micros=3)
    turned_b = plane_turn(steps_b, others=line_a[:1])
    lines_a = line_back(*line_a, others=turned_b, micros=1)
    line_b = line_step(turned_b, micros=12)
    sides_a = plane_back((lines_a[1], lines_a[1]))
    far_a = plane_back_turn(*sides_a)
    planes_a = (lines_a[1], *sides_a, *far_a)
    lines_b = line_back(*line_b, micros=2)
    result = call(
        result_kernel,
        (middle, active, w_down, wd_got, lanes(after(bias_down, lines_b[1]))),
        [whole()] * 5,
        [((rows, dim), BF16)],
    )[0]
    wide, half = ((dim // LANES, LANES), F32), ((width // LANES, LANES), F32)
    sums_a = call(
        finish_first_kernel,
        (lines_a[2], swap(after(lines_a[2], lines_b[1]))),
        [whole()] * 2,
        [wide] * 4 + [half],
    )
    grad_w_up, grad_w_out, grad_w_down = placed(planes_a, True, micros=10)
    sides_b = plane_back(lines_b)
    sides_b, _ = lax.optimization_barrier((sides_b, (result, sums_a, grad_w_up)))
    near_b = placed((lines_b[1], sides_b[0], sides_b[1]), False)
    far_b = plane_back_turn(*sides_b)
    far_b, near_b = lax.optimization_barrier((far_b, near_b))
    extra = sides_b[0][OUTER * chunk :]
    own_b = lines_b[2] + extra.astype(F32)
    sums_b = call(
        finish_second_kernel,
        (lines_b[2], extra, swap(own_b)),
        [whole()] * 3,
        [((idw, dim), F32), ((2, dim), F32), wide, wide, half, half],
    )
    grad_w_query, grad_w_key, grad_w_value = call(
        corner_kernel,
        (*far_b, *near_b),
        [whole()] * 2 + [outside()] * 3,
        [((dim, width), F32)] * 3,
        scratch=[
            pltpu.VMEM((3, dim // INNER, width), F32),
            pltpu.SemaphoreType.DMA((3,)),
        ],
        in_place={2: 0, 3: 1, 4: 2},
    )
    return (
        result,
        grad_features,
        sums_b[0],
        sums_b[1],
        sums_b[2].reshape(-1),
        sums_b[3].reshape(-1),
        grad_w_query,
        grad_w_key,
        grad_w_value,
        sums_b[4].reshape(-1),
        sums_b[5].reshape(-1),
        grad_w_out,
        sums_a[0].reshape(-1),
        sums_a[1].reshape(-1),
        sums_a[2].reshape(-1),
        grad_w_up,
        sums_a[4].reshape(-1),
        grad_w_down,
        sums_a[3].reshape(-1),
    )


def solution(mesh):
    token, split = P("dp", None), P(("dp", "mp"), None)
    columns, lines, cut, copy = P(None, "mp"), P("mp", None), P("mp"), P()
    return jax.shard_map(
        per_device,
        mesh=mesh,
        in_specs=(
            token, token, P("dp"), P("dp"), token, copy, copy, copy, copy, columns, columns,
            columns, cut, cut, lines, copy, copy, copy, columns, cut, lines, copy, token,
        ),
        out_specs=(
            split, split, copy, copy, copy, copy, columns, columns, columns, cut, cut, lines,
            copy, copy, copy, columns, cut, lines, copy,
        ),
        check_vma=False,
    )
```

```python
import math

import jax
import jax.numpy as jnp
from jax import lax
from jax.experimental import pallas as pl
from jax.experimental.pallas import tpu as pltpu
from jax.sharding import PartitionSpec as P

HDIM = 24
SEQ = 128
LANES = 128
INNER = 4
OUTER = 4
EPSILON = 1e-05
SCALE = 1.0 / math.sqrt(HDIM)
LOG2_SCALE = SCALE * math.log2(math.e)
F32, BF16 = jnp.float32, jnp.bfloat16
MIB = 1024 * 1024


def dot(left, right):
    return jnp.dot(left, right, preferred_element_type=F32)


def dot_nt(left, right):
    return lax.dot_general(left, right, (((1,), (1,)), ((), ())), preferred_element_type=F32)


def dot_tn(left, right):
    return lax.dot_general(left, right, (((0,), (0,)), ((), ())), preferred_element_type=F32)


def norm_parts(hidden):
    average = jnp.mean(hidden, axis=-1, keepdims=True)
    centred = hidden - average
    inverse = lax.rsqrt(jnp.mean(centred * centred, axis=-1, keepdims=True) + EPSILON)
    return centred * inverse, inverse


def norm_back(unit, inverse, grad_hat):
    return inverse * (
        grad_hat
        - jnp.mean(grad_hat, axis=-1, keepdims=True)
        - unit * jnp.mean(grad_hat * unit, axis=-1, keepdims=True)
    )


def row_sum(block):
    return jnp.sum(block, axis=0, keepdims=True)


def positions(length):
    return lax.broadcasted_iota(jnp.int32, (length, 1), 0)


def whole():
    return pl.BlockSpec(memory_space=pltpu.VMEM)


def outside():
    return pl.BlockSpec(memory_space=pltpu.HBM)


def places():
    index = lax.axis_index("dp")
    return lax.axis_index("mp"), index % INNER, index // INNER % OUTER


def copy_in(sources, targets, sems):
    copies = [
        pltpu.make_async_copy(source, target, sems.at[place])
        for place, (source, target) in enumerate(zip(sources, targets))
    ]
    for copy in copies:
        copy.start()
    return copies


def row_of(ref):
    block = ref[...].astype(F32)
    return jnp.concatenate([block[r : r + 1, :] for r in range(block.shape[0])], axis=1)


def put_row(ref, row):
    for r in range(ref.shape[0]):
        ref[r : r + 1, :] = row[:, r * LANES : (r + 1) * LANES]


def call(kernel, args, specs, outs, scratch=(), micros=0, limit=24, in_place=None):
    return pl.pallas_call(
        kernel,
        out_shape=[jax.ShapeDtypeStruct(shape, kind) for shape, kind in outs],
        in_specs=specs,
        out_specs=[outside() if in_place else whole() for _ in outs],
        input_output_aliases=in_place or {},
        scratch_shapes=list(scratch),
        compiler_params=pltpu.CompilerParams(vmem_limit_bytes=limit * MIB),
        cost_estimate=pl.CostEstimate(
            flops=micros * 1_000_000_000, bytes_accessed=0, transcendentals=0
        ),
    )(*args)


def head_windows(width):
    windows = []
    for pair in range(width // (2 * HDIM)):
        low = pair * 2 * HDIM // LANES * LANES
        high = -(-(pair + 1) * 2 * HDIM // LANES) * LANES
        windows.append((low, high))
    return windows


def head_masks(windows):
    masks = []
    for pair, (low, high) in enumerate(windows):
        column = low + lax.broadcasted_iota(jnp.int32, (16, high - low), 1)
        masks.append(
            [
                jnp.where(
                    (column >= head * HDIM) & (column < (head + 1) * HDIM), 1.0, 0.0
                ).astype(BF16)
                for head in (2 * pair, 2 * pair + 1)
            ]
        )
    return masks


def split_heads(block, masks, window):
    part = block[:, window[0] : window[1]]
    tiles = block.shape[0] // 16
    return jnp.concatenate(
        [part * jnp.concatenate([mask] * tiles, axis=0) for mask in masks], axis=0
    )


def embed_rows(feats, lap, ends, w_ident, types, gain, shift, at, count):
    table = lap[:, at]
    slot = lax.broadcasted_iota(jnp.int32, (SEQ, SEQ), 0)
    picked = []
    for end in (0, 1):
        pick = jnp.where(ends[end : end + 1, at] == slot, 1.0, 0.0).astype(BF16)
        picked.append(dot(table, pick))
    ident = jnp.concatenate(picked, axis=0).astype(BF16)
    hidden = feats[at, :].astype(F32) + dot_tn(ident, w_ident[...])
    kinds = types[...].astype(F32)
    hidden = hidden + jnp.where(positions(SEQ) >= count, kinds[1:2, :], kinds[0:1, :])
    unit, _ = norm_parts(hidden)
    return hidden, ident, (unit * gain + shift).astype(BF16)


def embed_kernel(
    feats_in, lap_in, ends_in, nodes_in, w_ident_in, types_in, gain_in, shift_in,
    bias_q_in, bias_v_in, wq_in, wk_in, wv_in, edges_in,
    hidden_out, ident_out, normed_out, normed_t_out, q_out, k_out, v_out, keep_out,
    feats, lap, ends, nodes, w_ident, types, gain_rows, shift_rows, bias_q, bias_v,
    w_q, w_k, w_v, edges, sems,
):
    rows, dim = feats.shape
    mols = rows // SEQ
    core = places()[0]
    own_rows = pl.ds(pl.multiple_of(core * rows, SEQ), rows)
    parts = [pl.ds(pl.multiple_of(core * rows + m * SEQ, SEQ), SEQ) for m in range(mols)]
    copies = copy_in(
        (
            feats_in.at[parts[0], :], lap_in.at[:, own_rows], ends_in.at[:, own_rows], nodes_in,
            w_ident_in, types_in, gain_in, shift_in, bias_q_in, bias_v_in, wq_in, wk_in, wv_in,
            edges_in, *(feats_in.at[part, :] for part in parts[1:]),
        ),
        (
            feats.at[pl.ds(0, SEQ), :], lap, ends, nodes, w_ident, types, gain_rows, shift_rows, bias_q, bias_v,
            w_q, w_k, w_v, edges,
            *(feats.at[pl.ds(m * SEQ, SEQ), :] for m in range(1, mols)),
        ),
        sems,
    )
    for copy in copies[:10]:
        copy.wait()
    gain, shift = row_of(gain_rows), row_of(shift_rows)

    def molecule(m):
        if m > 0:
            copies[13 + m].wait()
        at = slice(m * SEQ, (m + 1) * SEQ)
        count = nodes[core * mols + m]
        hidden, ident, normed = embed_rows(
            feats, lap, ends, w_ident, types, gain, shift, at, count
        )
        ident_out[:, at] = ident
        hidden_out[at, :] = hidden
        normed_out[at, :] = normed
        normed_t_out[:, at] = normed.T

    for m in range(mols):
        molecule(m)
    normed = normed_out[...]
    copies[10].wait()
    q_out[...] = (dot(normed, w_q[...]) + row_of(bias_q)).astype(BF16)
    copies[11].wait()
    k_out[...] = dot(normed, w_k[...]).astype(BF16)
    copies[12].wait()
    v_out[...] = (dot(normed, w_v[...]) + row_of(bias_v)).astype(BF16)
    copies[13].wait()
    for m in range(2 * mols):
        inside = lax.broadcasted_iota(jnp.int32, (SEQ, LANES), 0) < nodes[m] + edges[m]
        keep_out[m * SEQ : (m + 1) * SEQ, :] = jnp.where(inside, 1.0, 0.0)


def forward_kernel(
    hidden, normed, q_own, k_own, v_own, w_q, w_k, w_v, wo_own, wo, wu_own, wu,
    bias_q, bias_v, bias_u,
    nodes_in, edges_in, bias_u_own_in, bias_o_in, gain_in, shift_in,
    q_out, k_out, v_out, probs_out, keep_out, send_out, middle, active, slope,
    nodes, edges, bias_u_own, bias_o, gain_rows, shift_rows, sems,
    mixed, attended, normed_two,
):
    rows, dim = hidden.shape
    width = q_own.shape[1]
    mols = rows // SEQ
    pairs = width // (2 * HDIM)
    windows = head_windows(width)
    masks = head_masks(windows)
    core = places()[0]
    copies = copy_in(
        (nodes_in, edges_in, bias_u_own_in, bias_o_in, gain_in, shift_in),
        (nodes, edges, bias_u_own, bias_o, gain_rows, shift_rows),
        sems,
    )

    for copy in copies:
        copy.wait()
    gain, shift, bias_out = row_of(gain_rows), row_of(shift_rows), row_of(bias_o)

    sides = ((q_own, k_own, v_own, keep_out), (q_out, k_out, v_out, send_out))
    units = [(m, side) for side in (0, 1) for m in range(mols)]

    def weigh(unit, pair):
        m, side = unit
        at = slice(m * SEQ, (m + 1) * SEQ)
        place = core * mols + m
        key_keep = positions(SEQ) < nodes[place] + edges[place]
        low, high = windows[pair]
        both = split_heads(sides[side][0][at, :], masks[pair], windows[pair])
        scores = dot_nt(sides[side][1][at, low:high], both)
        scores = jnp.where(key_keep, scores, -1e30)
        top = jnp.max(scores, axis=0, keepdims=True)
        raised = jnp.exp2((scores - top) * LOG2_SCALE)
        probs_out[m, side * pairs + pair] = (raised * (1.0 / row_sum(raised))).astype(BF16)

    def mix(step, pair, values_t):
        m, side = units[step]
        first = pair * 2 * HDIM
        out = dot(values_t[first : first + 2 * HDIM], probs_out[m, side * pairs + pair])
        mixed[step % 2, first : first + HDIM, :] = out[:HDIM, :SEQ]
        mixed[step % 2, first + HDIM : first + 2 * HDIM, :] = out[HDIM:, SEQ:]

    def keep_mixed(step):
        m, side = units[step]
        at = slice(m * SEQ, (m + 1) * SEQ)
        place = core * mols + m
        query_keep = lax.broadcasted_iota(jnp.int32, (1, SEQ), 1) < nodes[place] + edges[place]
        kept = jnp.where(query_keep, mixed[step % 2], 0.0).astype(BF16)
        sides[side][3][dim : dim + width, at] = kept
        attended[at, side * width : (side + 1) * width] = kept.T

    partner = ((q_out, w_q, bias_q), (k_out, w_k, None), (v_out, w_v, bias_v))
    for pair in range(pairs):
        weigh(units[0], pair)
        if pair % 2 == 0 and pair // 2 < len(partner):
            out, weight, bias = partner[pair // 2]
            rows_of = dot(normed[...], weight[...])
            out[...] = (rows_of if bias is None else rows_of + row_of(bias)).astype(BF16)
    for step, task in enumerate(units):
        values_t = sides[task[1]][2][task[0] * SEQ : (task[0] + 1) * SEQ, :].T
        for pair in range(pairs):
            mix(step, pair, values_t)
            if step + 1 < len(units):
                weigh(units[step + 1], pair)
        keep_mixed(step)
    middle[...] = (
        hidden[...] + dot(attended[:, :width], wo_own[...]) + dot(attended[:, width:], wo[...])
    )

    for m in range(mols):
        at = slice(m * SEQ, (m + 1) * SEQ)
        total = middle[at, :] + bias_out
        middle[at, :] = total
        unit_rows, _ = norm_parts(total)
        rows_two = (unit_rows * gain + shift).astype(BF16)
        normed_two[at, :] = rows_two
        turned = rows_two.T
        keep_out[:dim, at] = turned
        send_out[:dim, at] = turned

    for side, (w_ref, b_ref, part_out) in enumerate(
        ((wu_own, bias_u_own, keep_out), (wu, bias_u, send_out))
    ):
        columns = slice(side * width, (side + 1) * width)
        slope[:, columns] = dot(normed_two[...], w_ref[...]) + row_of(b_ref)

        for m in range(mols):
            at = slice(m * SEQ, (m + 1) * SEQ)
            before = slope[at, columns]
            phi = 0.5 * (1.0 + lax.erf(before * math.sqrt(0.5)))
            out = (before * phi).astype(BF16)
            slope[at, columns] = phi + before * jnp.exp(before * before * -0.5) * (
                1.0 / math.sqrt(2.0 * math.pi)
            )
            active[at, columns] = out
            part_out[dim + width : dim + 2 * width, at] = out.T


def ffn_back_kernel(
    middle, slope, wu_own, wu, wd_own, wd, keep_rows, cots, gain_in,
    keep_out, send_out, gm_out, grad_branch,
    gain_rows, sems, grad_ffn,
):
    rows, dim = middle.shape
    width = wd.shape[0]
    mols = rows // SEQ
    core = places()[0]
    copies = copy_in((gain_in,), (gain_rows,), sems)

    def own_cots(m):
        at = pl.ds(pl.multiple_of(core * rows + m * SEQ, SEQ), SEQ)
        return jnp.where(keep_rows[at, 0:1] > 0.5, cots[at, :].astype(F32), 0.0)

    for m in range(mols):
        at = slice(m * SEQ, (m + 1) * SEQ)
        grad_ffn[at, :] = own_cots(m).astype(BF16)
    place_b = 0
    for side, (w_ref, part_out) in enumerate(((wd_own, keep_out), (wd, send_out))):
        columns = slice(side * width, (side + 1) * width)
        grad_before = slope[:, columns] * dot_nt(grad_ffn[...], w_ref[...])
        part_out[place_b : place_b + rows, :] = grad_before.astype(BF16)

    back = pl.ds(place_b, rows)
    gm_out[...] = dot_nt(keep_out[back, :], wu_own[...]) + dot_nt(send_out[back, :], wu[...])

    copies[0].wait()
    gain = row_of(gain_rows)
    nothing = jnp.zeros((1, dim), F32)
    sums = (nothing,) * 4
    for m in range(mols):
        at = slice(m * SEQ, (m + 1) * SEQ)
        grad_normed = gm_out[at, :]
        unit_rows, inverse = norm_parts(middle[at, :])
        grad_result = own_cots(m)
        grad = grad_result + norm_back(unit_rows, inverse, grad_normed * gain)
        gm_out[at, :] = grad
        grad_branch[at, :] = grad.astype(BF16)
        sums = (
            sums[0] + row_sum(grad),
            sums[1] + row_sum(grad_normed * unit_rows),
            sums[2] + row_sum(grad_normed),
            sums[3] + row_sum(grad_result),
        )

    place_m = place_b + rows
    for part_out in (keep_out, send_out):
        part_out[place_m : place_m + rows, :] = grad_branch[:, :width]
        part_out[place_m + rows : place_m + 2 * rows, :] = grad_branch[:, width:]
    small = jnp.concatenate(list(sums) + [nothing] * 12, axis=0)
    left, right = small[:, :width], small[:, width:]
    place_s = place_m + 2 * rows
    keep_out[place_s:, :] = jnp.where(core == 0, left, right).astype(BF16)
    send_out[place_s:, :] = jnp.where(core == 0, right, left).astype(BF16)


def result_kernel(middle, active, wd_own, wd, bias, result_out):
    width = wd.shape[0]
    result_out[...] = (
        middle[...]
        + dot(active[:, :width], wd_own[...])
        + dot(active[:, width:], wd[...])
        + row_of(bias)
    ).astype(BF16)


def branch_kernel(grad_branch, wo_own, wo, keep_rows, ga_own_out, ga_out):
    rows = grad_branch.shape[0]
    own_rows = pl.ds(pl.multiple_of(places()[0] * rows, SEQ), rows)
    keep = keep_rows[own_rows, 0:1] > 0.5
    for ref, weight in ((ga_own_out, wo_own), (ga_out, wo)):
        ref[...] = jnp.where(keep, dot_nt(grad_branch[...], weight[...]), 0.0).astype(BF16)


def attend_back_kernel(
    q_own, k_own, v_own, ga_own, q_got, k_got, v_got, ga_got, probs_all,
    keep_out, send_out, dq_t, dk, dv, slopes,
):
    rows, width = q_own.shape
    pairs = width // (2 * HDIM)
    windows = head_windows(width)
    masks = head_masks(windows)
    sides = (
        (q_own, k_own, v_own, ga_own, keep_out),
        (q_got, k_got, v_got, ga_got, send_out),
    )
    units = [(m, side) for m in range(rows // SEQ) for side in (0, 1)]

    def score_back(unit, pair):
        m, side = unit
        at = slice(m * SEQ, (m + 1) * SEQ)
        low, high = windows[pair]
        both_g = split_heads(sides[side][3][at, :], masks[pair], windows[pair])
        probs_low = probs_all[m, side * pairs + pair]
        probs = probs_low.astype(F32)
        grad_probs = dot_nt(sides[side][2][at, low:high], both_g)
        inner = row_sum(probs * grad_probs)
        slopes[side, pair] = (probs * (grad_probs - inner)).astype(BF16)
        dv[side, :, low:high] += dot(probs_low, both_g)

    def rows_back(unit, pair, keys_t):
        m, side = unit
        low, high = windows[pair]
        grad_scores = slopes[side, pair]
        both_q = split_heads(sides[side][0][m * SEQ : (m + 1) * SEQ, :], masks[pair], windows[pair])
        dk[side, :, low:high] += dot(grad_scores, both_q)
        first = pair * 2 * HDIM
        out = dot(keys_t[first : first + 2 * HDIM], grad_scores)
        dq_t[side, first : first + HDIM, :] = out[:HDIM, :SEQ]
        dq_t[side, first + HDIM : first + 2 * HDIM, :] = out[HDIM:, SEQ:]

    def begin(unit):
        dk[unit[1]] = jnp.zeros_like(dk[unit[1]])
        dv[unit[1]] = jnp.zeros_like(dv[unit[1]])

    def finish(unit):
        m, side = unit
        part_out = sides[side][4]
        base = m * SEQ
        part_out[base : base + SEQ, :] = (dq_t[side] * SCALE).astype(BF16).T
        part_out[rows + base : rows + base + SEQ, :] = (dk[side] * SCALE).astype(BF16)
        part_out[2 * rows + base : 2 * rows + base + SEQ, :] = dv[side].astype(BF16)

    begin(units[0])
    for pair in range(pairs):
        score_back(units[0], pair)
    for step, unit in enumerate(units):
        keys_t = sides[unit[1]][1][unit[0] * SEQ : (unit[0] + 1) * SEQ, :].T
        if step + 1 < len(units):
            begin(units[step + 1])
        for pair in range(pairs):
            rows_back(unit, pair, keys_t)
            if step + 1 < len(units):
                score_back(units[step + 1], pair)
        finish(unit)


def embed_back_kernel(*refs):
    (
        grads_own, grads,
        wq_own, wk_own, wv_own, w_q, w_k, w_v, ident, grad_middle,
        feats_in, nodes_in, w_ident_in, types_in, gain_in,
        features_out, keep_out, send_out,
        feats, nodes, w_ident, types, gain_rows, sems, grad_normed, small,
    ) = refs
    core = places()[0]
    rows = feats.shape[0]
    copies = copy_in(
        (
            feats_in.at[pl.ds(pl.multiple_of(core * rows, SEQ), rows), :], nodes_in,
            w_ident_in, types_in, gain_in,
        ),
        (feats, nodes, w_ident, types, gain_rows),
        sems,
    )
    rows, dim = feats.shape
    width = wq_own.shape[1]
    idw = ident.shape[0]
    total = None
    for part, weights in ((grads_own, (wq_own, wk_own, wv_own)), (grads, (w_q, w_k, w_v))):
        for place, weight in enumerate(weights):
            term = dot_nt(part[place * rows : (place + 1) * rows, :], weight[...])
            total = term if total is None else total + term
    grad_normed[...] = total
    mols = rows // SEQ
    small[...] = jnp.zeros_like(small)
    for copy in copies:
        copy.wait()
    gain = row_of(gain_rows)
    kinds = types[...].astype(F32)

    def molecule(m, carry):
        at = pl.ds(pl.multiple_of(m * SEQ, SEQ), SEQ)
        is_edge = positions(SEQ) >= nodes[core * mols + m]
        hidden = feats[at, :].astype(F32) + dot_tn(ident[:, at], w_ident[...])
        hidden = hidden + jnp.where(is_edge, kinds[1:2, :], kinds[0:1, :])
        unit, inverse = norm_parts(hidden)
        grad_rows = grad_normed[at, :]
        grad = grad_middle[at, :] + norm_back(unit, inverse, grad_rows * gain)
        features_out[at, :] = grad
        high = grad.astype(BF16)
        rest = (grad - high.astype(F32)).astype(BF16)
        picked = ident[:, at]
        small[:idw, :] += dot(picked, high) + dot(picked, rest)
        edge_rows = jnp.where(is_edge, grad, 0.0)
        small[idw : idw + 1, :] += row_sum(grad - edge_rows)
        small[idw + 1 : idw + 2, :] += row_sum(edge_rows)
        small[idw + 2 : idw + 3, :] += row_sum(grad_rows * unit)
        small[idw + 3 : idw + 4, :] += row_sum(grad_rows)
        return carry

    lax.fori_loop(0, mols, molecule, 0)
    left, right = small[:, :width], small[:, width:]
    keep_out[...] = jnp.where(core == 0, left, right)
    send_out[...] = jnp.where(core == 0, right, left).astype(BF16)


def deal(unit, places_in, outs, block_at, small=None):
    _, inner, outer = places()
    first_kept, first_sent, second_kept, second_sent = outs
    for step in range(INNER):
        for turn in range(OUTER):
            if turn < 2:
                out, slot = (first_sent if step % 2 else first_kept), step // 2
            else:
                out, slot = (second_sent if step // 2 else second_kept), step % 2
            start = (slot * 2 + turn % 2) * places_in * unit
            for place in range(places_in):
                out[start + place * unit : start + (place + 1) * unit, :] = block_at(
                    inner ^ step, outer ^ turn, place
                )
    if small is not None:
        for out in (first_kept, first_sent):
            out[INNER * places_in * unit :, :] = small


def flat_block(flat, unit, dest, z):
    row = pl.multiple_of((dest * (OUTER // 2) + z // 2) * unit, 16)
    return flat[z % 2, pl.ds(row, unit), :]


def down_grads_kernel(kept, got, cots, keep_rows, *rest):
    outs, (flat, grad_ffn) = rest[:4], rest[4:]
    rows_all, dim = cots.shape
    rows, width = rows_all // 2, kept.shape[1]
    core = places()[0]
    for m in range(rows_all // SEQ):
        at = slice(m * SEQ, (m + 1) * SEQ)
        grad_ffn[at, :] = jnp.where(keep_rows[at, 0:1] > 0.5, cots[at, :].astype(F32), 0.0).astype(BF16)
    own_rows = pl.ds(pl.multiple_of(core * rows, SEQ), rows)
    other_rows = pl.ds(pl.multiple_of((1 - core) * rows, SEQ), rows)
    turned = slice(dim + width, dim + 2 * width)
    for half in (0, 1):
        columns = slice(half * width, (half + 1) * width)
        product = dot(kept[turned, :], grad_ffn[own_rows, columns])
        product = product + dot(got[turned, :], grad_ffn[other_rows, columns])
        flat[half] = product.astype(BF16)
    unit = dim // (INNER * OUTER)
    deal(unit, 1, outs, lambda dest, z, place: flat_block(flat, unit, dest, z))


def ffn_grads_kernel(kept, got, kept_back, got_back, *rest):
    outs, (tall, flat) = rest[:4], rest[4:]
    rows, width = kept.shape[1], kept.shape[1]
    dim = kept.shape[0] - 2 * width
    back, place_s = slice(0, rows), 3 * rows
    tall[...] = (
        dot(kept[:dim, :], kept_back[back, :]) + dot(got[:dim, :], got_back[back, :])
    ).astype(BF16)
    turned = slice(dim, dim + width)
    for half in (0, 1):
        mid = slice((1 + half) * rows, (2 + half) * rows)
        flat[half] = (
            dot(kept[turned, :], kept_back[mid, :]) + dot(got[turned, :], got_back[mid, :])
        ).astype(BF16)
    bias = row_sum(kept_back[back, :].astype(F32)) + row_sum(got_back[back, :].astype(F32))
    small = kept_back[place_s:, :].astype(F32) + got_back[place_s:, :].astype(F32)
    spot = lax.broadcasted_iota(jnp.int32, small.shape, 0)
    small = jnp.where(spot == 4, bias, small).astype(BF16)
    unit = dim // (INNER * OUTER)

    def block_at(dest, z, place):
        if place == 0:
            return tall[pl.ds(pl.multiple_of((dest * OUTER + z) * unit, 16), unit), :]
        return flat_block(flat, unit, dest, z)

    deal(unit, 2, outs, block_at, small)


def qkv_grads_kernel(normed_t, normed_t_got, kept, got, *refs):
    outs, small_out, (tall, normed, stacked) = refs[:4], refs[4], refs[5:]
    dim, rows = normed_t.shape
    unit = dim // (INNER * OUTER)
    normed[:, :rows] = normed_t[...]
    normed[:, rows:] = normed_t_got[...]
    spot = lax.broadcasted_iota(jnp.int32, small_out.shape, 0)
    small = jnp.zeros(small_out.shape, F32)
    for place in range(3):
        part = slice(place * rows, (place + 1) * rows)
        stacked[:rows, :] = kept[part, :]
        stacked[rows:, :] = got[part, :]
        tall[place] = dot(normed[...], stacked[...]).astype(BF16)
        if place != 1:
            small = jnp.where(spot == 36 + place // 2, row_sum(stacked[...].astype(F32)), small)
    small_out[...] = small

    def block_at(dest, z, place):
        return tall[place, pl.ds(pl.multiple_of((dest * OUTER + z) * unit, 16), unit), :]

    deal(unit, 3, outs, block_at)


def add(first, second):
    return (first.astype(F32) + second.astype(F32)).astype(BF16)


def plane_sum_kernel(first, first_got, second, second_got, *refs):
    late, (first_kept, first_sent, second_kept, second_sent) = refs[:-4], refs[-4:]
    pair = second_kept.shape[0]
    total = add(first[...], first_got[...])
    first_kept[:pair, :] = total[:pair]
    first_sent[:pair, :] = total[pair : 2 * pair]
    if late:
        small = (late[0][...] + late[1][...].astype(F32) + late[2][...]).astype(BF16)
    else:
        small = total[2 * pair :]
    first_kept[pair:, :] = small
    first_sent[pair:, :] = small
    total = add(second[...], second_got[...])
    second_kept[...] = total[:pair]
    second_sent[...] = total[pair:]


def plane_join_kernel(first, first_got, second, second_got, *refs):
    ahead, outs = refs[:4], refs[4:]
    unit = ahead[0].shape[0] // 4
    small = add(first[8 * unit :, :], first_got[8 * unit :, :])
    for place, (left, right, more, more_got) in enumerate(
        ((first, first_got, *ahead[:2]), (second, second_got, *ahead[2:]))
    ):
        total = add(left[: 8 * unit, :], right[: 8 * unit, :])
        late = add(more[...], more_got[...])
        for block in range(4):
            out = outs[2 * place + block // 2]
            start = block % 2 * 3 * unit
            out[start : start + 2 * unit, :] = total[2 * block * unit : 2 * (block + 1) * unit]
            out[start + 2 * unit : start + 3 * unit, :] = late[block * unit : (block + 1) * unit]
    for out in outs[:2]:
        out[6 * unit :, :] = small


def line_cut_kernel(first, first_got, second, second_got, own, near, middle, far):
    chunk = own.shape[0]
    total = add(first[...], first_got[...])
    own[...] = total[:chunk]
    near[...] = total[chunk:]
    total = add(second[...], second_got[...])
    middle[...] = total[:chunk]
    far[...] = total[chunk:]


def line_sum_kernel(own, near, near_got, middle_got, far_got, out, out_small):
    chunk = own.shape[0]
    total = own[...].astype(F32) + near_got[:chunk, :].astype(F32)
    total = total + middle_got[...].astype(F32) + far_got[...].astype(F32)
    out[...] = total.astype(BF16)
    out_small[:chunk, :] = total.astype(BF16)
    out_small[chunk:, :] = add(near[chunk:, :], near_got[chunk:, :])


def line_join_kernel(own, near, middle, far, line_x, line_y, small_out):
    chunk = near.shape[0]
    small = own[chunk:, :].astype(F32) + middle[chunk:, :].astype(F32)
    small_out[...] = small
    for out in (line_x, line_y):
        for turn, part in enumerate((own, near, middle, far)):
            out[turn * chunk : (turn + 1) * chunk, :] = part[:chunk, :]
    line_x[OUTER * chunk :, :] = small.astype(BF16)


def place_kernel(split_second, *refs):
    outs, parts = refs[-3:], refs[:-3]
    own = parts[0]
    steps = min(len(parts), INNER)
    _, inner, outer = places()
    unit = own.shape[0] // (3 * OUTER)
    width = own.shape[1]
    for step in range(steps):
        for turn in range(OUTER):
            ref, start = parts[step], turn * 3 * unit
            if step == 3 and turn >= 2:
                ref, start = parts[4], (turn - 2) * 3 * unit
            dest, z = inner ^ step, outer ^ turn
            tall = pl.ds(pl.multiple_of((dest * OUTER + z) * unit, 16), unit)
            flat = pl.ds(pl.multiple_of((dest * (OUTER // 2) + z // 2) * unit, 16), unit)
            columns = pl.ds(pl.multiple_of(z % 2 * width, LANES), width)
            for place in range(3):
                part = ref[start + place * unit : start + (place + 1) * unit, :].astype(F32)
                if split_second and place > 0:
                    outs[place][flat, columns] = part
                else:
                    outs[place][tall, :] = part


def corner_kernel(first, second, *refs):
    outs, blocks, sems = refs[3:6], refs[6], refs[7]
    _, inner, outer = places()
    unit = first.shape[0] // 6
    size = OUTER * unit
    target = pl.ds(pl.multiple_of((inner ^ 3) * size, 64), size)
    copies = []
    for place in range(3):
        for turn in range(OUTER):
            ref, start = (first, turn * 3 * unit) if turn < 2 else (second, (turn - 2) * 3 * unit)
            at = pl.ds(pl.multiple_of((outer ^ turn) * unit, 16), unit)
            rows = slice(start + place * unit, start + (place + 1) * unit)
            blocks[place, at, :] = ref[rows, :].astype(F32)
        copies.append(
            pltpu.make_async_copy(blocks.at[place], outs[place].at[target, :], sems.at[place])
        )
        copies[-1].start()
    for copy in copies:
        copy.wait()


def finish_first_kernel(small, got, bias_out, gain, shift, bias_down, bias_up):
    core = places()[0]
    for place, ref in enumerate((bias_out, gain, shift, bias_down)):
        mine, other = small[place : place + 1, :], got[place : place + 1, :]
        left = jnp.where(core == 0, mine, other)
        put_row(ref, jnp.concatenate([left, jnp.where(core == 0, other, mine)], axis=1))
    put_row(bias_up, small[4:5, :])


def finish_second_kernel(small, extra, got, w_ident, types, gain, shift, bias_q, bias_v):
    idw = w_ident.shape[0]
    core = places()[0]
    mine, other = small[...] + extra[...].astype(F32), got[...]
    left = jnp.where(core == 0, mine, other)
    total = jnp.concatenate([left, jnp.where(core == 0, other, mine)], axis=1)
    w_ident[...] = total[:idw]
    types[...] = total[idw : idw + 2]
    put_row(gain, total[idw + 2 : idw + 3])
    put_row(shift, total[idw + 3 : idw + 4])
    put_row(bias_q, mine[idw + 4 : idw + 5])
    put_row(bias_v, mine[idw + 5 : idw + 6])


def per_device(
    features, lap_vectors, node_counts, edge_counts, endpoints, w_ident, type_table,
    gain_one, shift_one, w_query, w_key, w_value, bias_query, bias_value, w_out, bias_out,
    gain_two, shift_two, w_up, bias_up, w_down, bias_down, cotangent,
):
    dp_count = lax.axis_size("dp")
    dp_index = lax.axis_index("dp")
    mp_index = lax.axis_index("mp")
    block = INNER * OUTER
    rest_count = dp_count // block
    def swap(part):
        return lax.ppermute(part, "mp", [(0, 1), (1, 0)])

    def inner_move(part, step):
        return lax.ppermute(part, "dp", [(s, s ^ step) for s in range(dp_count)])

    def outer_move(part, step):
        return lax.ppermute(part, "dp", [(s, s ^ (step * INNER)) for s in range(dp_count)])

    rows_all, dim = features.shape
    rows = rows_all // 2
    mols = rows // SEQ
    width = w_query.shape[1]
    heads = width // HDIM
    lapk = lap_vectors.shape[1]
    idw = w_ident.shape[0]

    def pinned(part):
        return pltpu.with_memory_space_constraint(part, pltpu.HBM)

    def lanes(part):
        return pinned(part.reshape(-1, LANES))

    nodes, edges = pinned(node_counts), pinned(edge_counts)
    count_scratch = pltpu.SMEM(node_counts.shape, jnp.int32)
    wide_scratch = pltpu.VMEM((dim // LANES, LANES), BF16)
    half_scratch = pltpu.VMEM((width // LANES, LANES), BF16)
    def after(part, *others):
        return lax.optimization_barrier((part, *others))[0]

    embed_args = (
        pinned(features), pinned(lap_vectors.T), pinned(endpoints.T), nodes,
        pinned(w_ident), pinned(type_table), lanes(gain_one), lanes(shift_one),
    )
    embed_scratch = [
        pltpu.VMEM((rows, dim), BF16),
        pltpu.VMEM((lapk, rows), BF16),
        pltpu.VMEM((2, rows), jnp.int32),
        count_scratch,
        pltpu.VMEM((idw, dim), BF16),
        pltpu.VMEM((2, dim), BF16),
        wide_scratch,
        wide_scratch,
    ]

    wq_got, wk_got, wv_got = swap(w_query), swap(w_key), swap(w_value)
    bq_got, bv_got, bu_got = swap(bias_query), swap(bias_value), swap(bias_up)
    wo_got, wu_got = swap(w_out), swap(w_up)

    hidden, ident, normed, normed_t, q_own, k_own, v_own, keep_rows = call(
        embed_kernel,
        (
            *embed_args, lanes(bias_query), lanes(bias_value),
            pinned(w_query), pinned(w_key), pinned(w_value), edges,
        ),
        [outside()] * 14,
        [
            ((rows, dim), F32),
            ((idw, rows), BF16),
            ((rows, dim), BF16),
            ((dim, rows), BF16),
            ((rows, width), BF16),
            ((rows, width), BF16),
            ((rows, width), BF16),
            ((rows_all, LANES), F32),
        ],
        scratch=embed_scratch
        + [half_scratch] * 2
        + [pltpu.VMEM((dim, width), BF16)] * 3
        + [count_scratch, pltpu.SemaphoreType.DMA((13 + mols,))],
    )
    wd_got = swap(after(w_down, normed))
    ahead_rows, back_rows = dim + 2 * width, 3 * rows + 16
    q_got, k_got, v_got, probs, kept_a, sent_a, middle, active, slope = call(
        forward_kernel,
        (
            hidden, normed, q_own, k_own, v_own, wq_got, wk_got, wv_got,
            w_out, wo_got, w_up, wu_got,
            *(part.reshape(-1, LANES) for part in (bq_got, bv_got, bu_got)),
            nodes, edges,
            lanes(bias_up), lanes(bias_out), lanes(gain_two), lanes(shift_two),
        ),
        [whole()] * 15 + [outside()] * 6,
        [
            ((rows, width), BF16),
            ((rows, width), BF16),
            ((rows, width), BF16),
            ((mols, heads, SEQ, 2 * SEQ), BF16),
            ((ahead_rows, width), BF16),
            ((ahead_rows, width), BF16),
            ((rows, dim), F32),
            ((rows, dim), BF16),
            ((rows, dim), F32),
        ],
        scratch=[
            count_scratch,
            count_scratch,
            half_scratch,
            wide_scratch,
            wide_scratch,
            wide_scratch,
            pltpu.SemaphoreType.DMA((6,)),
            pltpu.VMEM((2, width, SEQ), F32),
            pltpu.VMEM((rows, dim), BF16),
            pltpu.VMEM((rows, dim), BF16),
        ],
        limit=30,
    )
    got_a = swap(sent_a)
    kept_back, sent_back, grad_middle, grad_branch = call(
        ffn_back_kernel,
        (
            middle, slope, w_up, wu_got, w_down, wd_got, keep_rows, cotangent,
            lanes(gain_two),
        ),
        [whole()] * 8 + [outside()],
        [
            ((back_rows, width), BF16),
            ((back_rows, width), BF16),
            ((rows, dim), F32),
            ((rows, dim), BF16),
        ],
        scratch=[wide_scratch, pltpu.SemaphoreType.DMA((1,)), pltpu.VMEM((rows, dim), BF16)],
    )
    got_back = swap(sent_back)

    unit = dim // block
    chunk = 3 * unit
    small_a, small_b = 16, 48

    def rest_sum(part):
        if rest_count == 1:
            return part
        groups = [[r * block + s for r in range(rest_count)] for s in range(block)]
        return lax.psum(part.astype(F32), "dp", axis_index_groups=groups).astype(part.dtype)

    pair = 2 * chunk

    def plane_step(parts, small_rows, late=(), others=(), micros=0):
        first, first_sent, second, second_sent = parts
        first_got = after(inner_move(first_sent, 1), *others)
        second_got = after(inner_move(second_sent, 2), *others)
        return call(
            plane_sum_kernel,
            (first, first_got, second, second_got, *late),
            [whole()] * (4 + len(late)),
            [((pair + small_rows, width), BF16)] * 2 + [((pair, width), BF16)] * 2,
            micros=micros,
        )

    def plane_turn(parts, others=(), micros=0):
        first, first_sent, second, second_sent = parts
        first_got = after(inner_move(first_sent, 2), *others)
        second_got = after(inner_move(second_sent, 1), *others)
        return call(
            line_cut_kernel,
            (first, first_got, second, second_got),
            [whole()] * 4,
            [
                ((chunk, width), BF16),
                ((first.shape[0] - chunk, width), BF16),
                ((chunk, width), BF16),
                ((chunk, width), BF16),
            ],
            micros=micros,
        )

    def line_step(parts, others=(), micros=0):
        got = [after(outer_move(parts[turn], turn), *others) for turn in range(1, OUTER)]
        mine, both = call(
            line_sum_kernel,
            (parts[0], parts[1], *got),
            [whole()] * 5,
            [((chunk, width), BF16), (parts[1].shape, BF16)],
            micros=micros,
        )
        if rest_count > 1:
            both = rest_sum(both)
            mine = both[:chunk]
        return mine, both

    def line_back(mine, both, others=(), micros=0):
        sent = (mine, both, mine)
        got = [after(outer_move(sent[turn - 1], turn), *others) for turn in range(1, OUTER)]
        small_rows = both.shape[0] - chunk
        return call(
            line_join_kernel,
            (both, *got),
            [whole()] * OUTER,
            [
                ((OUTER * chunk + small_rows, width), BF16),
                ((OUTER * chunk, width), BF16),
                ((small_rows, width), F32),
            ],
            micros=micros,
        )

    def plane_back(lines):
        return inner_move(lines[0], 1), inner_move(lines[1], 2)

    def plane_back_turn(side_x, side_y):
        return inner_move(side_y[:pair], 1), inner_move(side_x[pair : 2 * pair], 2)

    def placed(planes, split_second, micros=0):
        tall, flat = ((dim, width), F32), ((width, dim), F32)
        return call(
            lambda *refs: place_kernel(split_second, *refs),
            planes,
            [whole()] * len(planes),
            [tall, flat, flat] if split_second else [tall] * 3,
            micros=micros,
        )

    parts_down = call(
        down_grads_kernel,
        (after(kept_a, grad_branch), got_a, cotangent, keep_rows),
        [whole()] * 4,
        [((INNER * unit, width), BF16)] * 4,
        scratch=[pltpu.VMEM((2, width, width), BF16), pltpu.VMEM((rows_all, dim), BF16)],
    )
    parts_a = call(
        ffn_grads_kernel,
        (after(kept_a, parts_down[0]), got_a, kept_back, got_back),
        [whole()] * 4,
        [((2 * INNER * unit + small_a, width), BF16)] * 2 + [((2 * INNER * unit, width), BF16)] * 2,
        scratch=[pltpu.VMEM((dim, width), BF16), pltpu.VMEM((2, width, width), BF16)],
    )
    ahead = [
        after(inner_move(parts_down[1], 1), parts_a[0]),
        after(inner_move(parts_down[3], 2), parts_a[0]),
    ]
    ga_own, ga_got = call(
        branch_kernel,
        (after(grad_branch, parts_a[0], *ahead), w_out, wo_got, keep_rows),
        [whole()] * 4,
        [((rows, width), BF16), ((rows, width), BF16)],
    )

    kept_b, sent_b = call(
        attend_back_kernel,
        (q_own, k_own, v_own, ga_own, q_got, k_got, v_got, ga_got, probs),
        [whole()] * 9,
        [((3 * rows, width), BF16)] * 2,
        scratch=[
            pltpu.VMEM((2, width, SEQ), F32),
            pltpu.VMEM((2, SEQ, width), F32),
            pltpu.VMEM((2, SEQ, width), F32),
            pltpu.VMEM((2, heads // 2, SEQ, 2 * SEQ), BF16),
        ],
    )
    normed_t_got = swap(after(normed_t, parts_a[0]))
    got_b = swap(sent_b)
    moved = [after(inner_move(parts_a[1], 1), kept_b), after(inner_move(parts_a[3], 2), kept_b)]
    moved = moved + ahead
    steps_a = call(
        plane_join_kernel,
        (
            parts_a[0], moved[0], parts_a[2], moved[1],
            parts_down[0], moved[2], parts_down[2], moved[3],
        ),
        [whole()] * 8,
        [((pair + small_a, width), BF16)] * 2 + [((pair, width), BF16)] * 2,
        micros=6,
    )
    normed_t = after(normed_t, *steps_a)
    parts_b = call(
        qkv_grads_kernel,
        (normed_t, normed_t_got, kept_b, got_b),
        [whole()] * 4,
        [((INNER * chunk, width), BF16)] * 4 + [((small_b, width), F32)],
        scratch=[
            pltpu.VMEM((3, dim, width), BF16),
            pltpu.VMEM((dim, 2 * rows), BF16),
            pltpu.VMEM((2 * rows, width), BF16),
        ],
    )
    turned_a = plane_turn(steps_a, others=(parts_b[0],), micros=3)
    grad_middle = after(grad_middle, parts_b[0], *turned_a)
    grad_features, small_kept, small_sent = call(
        embed_back_kernel,
        (
            kept_b, sent_b, w_query, w_key, w_value, wq_got, wk_got, wv_got, ident,
            grad_middle, embed_args[0], nodes, *embed_args[4:7],
        ),
        [whole()] * 10 + [outside()] * 5,
        [((rows, dim), F32), ((small_b, width), F32), ((small_b, width), BF16)],
        scratch=[
            pltpu.VMEM((rows, dim), BF16),
            count_scratch,
            pltpu.VMEM((idw, dim), BF16),
            pltpu.VMEM((2, dim), BF16),
            wide_scratch,
            pltpu.SemaphoreType.DMA((5,)),
            pltpu.VMEM((rows, dim), F32),
            pltpu.VMEM((small_b, dim), F32),
        ],
        micros=0,
    )
    small_got = swap(small_sent)
    steps_b = plane_step(parts_b[:4], small_b, late=(small_kept, small_got, parts_b[4]))
    line_a = line_step(turned_a, others=steps_b, micros=3)
    turned_b = plane_turn(steps_b, others=line_a[:1])
    lines_a = line_back(*line_a, others=turned_b, micros=1)
    line_b = line_step(turned_b, micros=12)
    sides_a = plane_back((lines_a[1], lines_a[1]))
    far_a = plane_back_turn(*sides_a)
    planes_a = (lines_a[1], *sides_a, *far_a)
    lines_b = line_back(*line_b, micros=2)
    result = call(
        result_kernel,
        (middle, active, w_down, wd_got, lanes(after(bias_down, lines_b[1]))),
        [whole()] * 5,
        [((rows, dim), BF16)],
    )[0]
    wide, half = ((dim // LANES, LANES), F32), ((width // LANES, LANES), F32)
    sums_a = call(
        finish_first_kernel,
        (lines_a[2], swap(after(lines_a[2], lines_b[1]))),
        [whole()] * 2,
        [wide] * 4 + [half],
    )
    grad_w_up, grad_w_out, grad_w_down = placed(planes_a, True, micros=10)
    sides_b = plane_back(lines_b)
    sides_b, _ = lax.optimization_barrier((sides_b, (result, sums_a, grad_w_up)))
    near_b = placed((lines_b[1], sides_b[0], sides_b[1]), False)
    far_b = plane_back_turn(*sides_b)
    far_b, near_b = lax.optimization_barrier((far_b, near_b))
    extra = sides_b[0][OUTER * chunk :]
    own_b = lines_b[2] + extra.astype(F32)
    sums_b = call(
        finish_second_kernel,
        (lines_b[2], extra, swap(own_b)),
        [whole()] * 3,
        [((idw, dim), F32), ((2, dim), F32), wide, wide, half, half],
    )
    grad_w_query, grad_w_key, grad_w_value = call(
        corner_kernel,
        (*far_b, *near_b),
        [whole()] * 2 + [outside()] * 3,
        [((dim, width), F32)] * 3,
        scratch=[
            pltpu.VMEM((3, dim // INNER, width), F32),
            pltpu.SemaphoreType.DMA((3,)),
        ],
        in_place={2: 0, 3: 1, 4: 2},
    )
    return (
        result,
        grad_features,
        sums_b[0],
        sums_b[1],
        sums_b[2].reshape(-1),
        sums_b[3].reshape(-1),
        grad_w_query,
        grad_w_key,
        grad_w_value,
        sums_b[4].reshape(-1),
        sums_b[5].reshape(-1),
        grad_w_out,
        sums_a[0].reshape(-1),
        sums_a[1].reshape(-1),
        sums_a[2].reshape(-1),
        grad_w_up,
        sums_a[4].reshape(-1),
        grad_w_down,
        sums_a[3].reshape(-1),
    )


def solution(mesh):
    token, split = P("dp", None), P(("dp", "mp"), None)
    columns, lines, cut, copy = P(None, "mp"), P("mp", None), P("mp"), P()
    return jax.shard_map(
        per_device,
        mesh=mesh,
        in_specs=(
            token, token, P("dp"), P("dp"), token, copy, copy, copy, copy, columns, columns,
            columns, cut, cut, lines, copy, copy, copy, columns, cut, lines, copy, token,
        ),
        out_specs=(
            split, split, copy, copy, copy, copy, columns, columns, columns, cut, cut, lines,
            copy, copy, copy, columns, cut, lines, copy,
        ),
        check_vma=False,
    )
```
